32 devices in a mesh: dp: 4 (over y, x), expert: 8 (over z, core).
Axes of the slice: x: 2, y: 2, z: 4, core: 2. Of those that a mesh axis runs over, the one named last changes fastest.
Arguments:
- tokens: bfloat16 [16, 512, 1536], P('expert', 'dp'), may hold values from -6 to 6
- lengths: int32 [16], P('expert'), may hold values from 385 to 512, as said below
- routes: int32 [16, 512, 4], P('expert', 'dp'), may hold values from 0 to 7, all different within a row; in each aligned block of 128 rows (0 to 127, 128 to 255, ..., all dimensions but the last counted through in order) at most 96 rows name the same one
- prenorm: bfloat16 [1536], P(('dp', 'expert')), may hold values from 0.5 to 1.5
- w_query: bfloat16 [1536, 1536], P(('dp', 'expert')), may hold values from -0.15625 to 0.15625
- key_value_weight: bfloat16 [1536, 512], P(('dp', 'expert')), may hold values from -0.15625 to 0.15625
- w_output: bfloat16 [1536, 1536], P(('dp', 'expert')), may hold values from -1.25 to 1.25
- midnorm: bfloat16 [1536], P(('dp', 'expert')), may hold values from 0.5 to 1.5
- w_router: bfloat16 [1536, 8], P(('dp', 'expert')), may hold values from -0.078125 to 0.078125
- expert_in: bfloat16 [8, 1536, 1536], P('expert', 'dp'), may hold values from -0.15625 to 0.15625
- expert_out: bfloat16 [8, 768, 1536], P('expert', 'dp'), may hold values from -0.625 to 0.625
- cotangent: bfloat16 [16, 512, 1536], P('expert', 'dp'), may hold values from -6 to 6
Outputs:
- block_out: bfloat16 [16, 512, 1536], P('expert', 'dp')
- grad_tokens: float32 [16, 512, 1536], P('expert', 'dp')
- grad_prenorm: float32 [1536], P(('dp', 'expert'))
- grad_query: float32 [1536, 1536], P(('dp', 'expert'))
- key_value_weight_gradient: float32 [1536, 512], P(('dp', 'expert'))
- grad_output: float32 [1536, 1536], P(('dp', 'expert'))
- grad_midnorm: float32 [1536], P(('dp', 'expert'))
- grad_router: float32 [1536, 8], P(('dp', 'expert'))
- grad_expertin: float32 [8, 1536, 1536], P('expert', 'dp')
- grad_expertout: float32 [8, 768, 1536], P('expert', 'dp')
The draws below stay inside these ranges and needn't reach their ends.
Inputs may be any that keep to these rules, and one draw needn't show every extreme that they name: `lengths`: each sequence has from 385 to 512 live slots; one sequence has exactly 512 and one exactly 385. `routes`: each slot names 4 different experts; in each aligned block of 128 slots of a sequence (the slots of one device), no expert is named by more than 96 slots, and some expert reaches 96. Padded slots are routed too.
All inputs are finite; a program needn't handle non-finite values.
Results may differ from the reference program's by a relative error of at most 0.018.
Values may be sent and summed in bfloat16 or wider, within the bound.
A program may use at most 192 MiB of HBM per device.

```python
import math
import jax
import jax.numpy as jnp
import numpy as np
from jax import lax

MODEL_WIDTH = 1536
QUERY_HEADS = 12
KEY_VALUE_HEADS = 2
HEAD_SIZE = 128
FF = 768
TOP = 4
TOK_MB = 128
EXPERTS = 8
SLOTS = 512
SEQS = 16
CAP = 96


def draw_lengths(key, part):
    key = jax.random.fold_in(key, 11)
    first_key, second_key = jax.random.split(key)
    drawn = jax.random.randint(first_key, (SEQS,), 3 * TOK_MB + 1, SLOTS + 1, dtype=jnp.int32)
    order = jax.random.permutation(second_key, SEQS)
    drawn = drawn.at[order[0]].set(SLOTS)
    drawn = drawn.at[order[1]].set(3 * TOK_MB + 1)
    return drawn.astype(jnp.int32)


def shard_levels(rng, dims, shards, low, largest):
    gain = 1.0
    for dim, shards_of in shards:
        steps = jax.random.uniform(jax.random.fold_in(jax.random.fold_in(rng, 6), dim), (shards_of,), jnp.float32, low / len(shards), largest / len(shards))
        gain = gain * jnp.repeat(jnp.exp(steps), dims[dim] // shards_of).reshape((-1,) + (1,) * (len(dims) - 1 - dim))
    return gain


def routed_block(rng, own, number, rows, count, top, reach, lean):
    ranking = jax.random.permutation(rng, count)
    packed, usual = portions_of(count, rows * top, reach, lean, True), portions_of(count, rows * top, reach, lean, False)
    places = jnp.arange(count)

    def named(sizes, turn):
        used = int((sizes > 0).sum())
        fixed = max(1, used // 4)
        moved = fixed + (places - fixed + turn * (used - fixed)) % max(1, count - fixed)
        return jnp.zeros((count,), jnp.int32).at[ranking[jnp.where(places < fixed, places, moved)]].set(jnp.asarray(sizes, jnp.int32))

    sizes = jnp.where(number % 4 == 0, named(packed, number // 4), named(usual, number - number // 4 - 1))
    mixed = jax.random.permutation(jax.random.fold_in(own, 3), count)
    source_of, sink = mixed[0:count // 2 * 2:2], mixed[1:count // 2 * 2:2]
    slack = jnp.minimum(sizes[source_of] - 1, reach - sizes[sink]) // 2
    slack = jnp.where((source_of == ranking[0]) | (sink == ranking[0]) | (sizes[sink] == 0), 0, jnp.maximum(slack, 0))
    moved = jax.random.randint(jax.random.fold_in(own, 4), (count // 2,), 0, 1 << 20) % (slack + 1)
    sizes = sizes.at[source_of].add(-moved).at[sink].add(moved)
    labels = jnp.searchsorted(jnp.cumsum(sizes), jnp.arange(rows * top), side="right").astype(jnp.int32)
    table = labels.reshape(top, rows).T
    table = table[jax.random.permutation(jax.random.fold_in(own, 1), rows)]
    turn = jax.random.randint(jax.random.fold_in(own, 2), (rows, 1), 0, top)
    return jnp.take_along_axis(table, (jnp.arange(top)[None, :] + turn) % top, axis=1)


def portions_of(number_of, total, limit, slope, full):
    weights = [(1 << 20) // math.isqrt(standing ** slope) + 1 for standing in range(1, number_of + 1)]
    largest = limit if full else min(limit, max(-(-total // number_of), total * weights[0] // sum(weights)))
    least = 1 if total - largest >= number_of - 1 else 0
    holding, spare = [largest] + [least] * (number_of - 1), total - largest - least * (number_of - 1)
    while spare > 0:
        candidates = [i for i in range(1, number_of) if holding[i] < largest] or [i for i in range(1, number_of) if holding[i] < limit]
        whole, remaining = sum([weights[i] for i in candidates]), spare
        for i in candidates:
            extra = min(limit - holding[i], max(1, remaining * weights[i] // whole), spare)
            holding[i] = holding[i] + extra
            spare = spare - extra
    return np.array(holding)


def noise(rng, extent, deviation, reach, shards=(), kind=jnp.bfloat16):
    array = deviation * jax.random.normal(rng, extent, jnp.float32)
    if shards:
        array = array * shard_levels(rng, extent, shards, -0.22, 0.18)
    return jnp.clip(array, -reach, reach).astype(kind)


def setup_inputs(seed: int = 0) -> dict:
    arg_keys = jax.random.split(jax.random.key(seed), 13)
    tokens = noise(arg_keys[0], (SEQS, SLOTS, MODEL_WIDTH), 1.0, 6.0, ((0, 8), (1, 4)))
    lengths = draw_lengths(jax.random.fold_in(arg_keys[12], 71), 0)
    routes_keys = jax.random.split(jax.random.fold_in(arg_keys[2], 1), SEQS * SLOTS // TOK_MB)
    routes_turns = jax.random.permutation(jax.random.fold_in(arg_keys[2], 3), SEQS * SLOTS // TOK_MB)
    routes = jax.vmap(lambda own, number: routed_block(jax.random.fold_in(arg_keys[2], 2), own, number, TOK_MB, EXPERTS, TOP, CAP, 2))(routes_keys, routes_turns).reshape((SEQS, SLOTS, TOP))
    prenorm = jnp.clip(1.0 + 0.1 * jax.random.normal(arg_keys[3], (MODEL_WIDTH,), jnp.float32), 0.5, 1.5).astype(jnp.bfloat16)
    w_query = noise(arg_keys[4], (MODEL_WIDTH, QUERY_HEADS * HEAD_SIZE), MODEL_WIDTH ** -0.5, 0.15625, ((0, 32),))
    key_value_weight = noise(arg_keys[5], (MODEL_WIDTH, 2 * KEY_VALUE_HEADS * HEAD_SIZE), MODEL_WIDTH ** -0.5, 0.15625, ((0, 32),))
    w_output = noise(arg_keys[6], (QUERY_HEADS * HEAD_SIZE, MODEL_WIDTH), (QUERY_HEADS * HEAD_SIZE * 8 // SLOTS) ** -0.5, 1.25, ((0, 32),))
    midnorm = jnp.clip(1.0 + 0.1 * jax.random.normal(arg_keys[7], (MODEL_WIDTH,), jnp.float32), 0.5, 1.5).astype(jnp.bfloat16)
    w_router = noise(arg_keys[8], (MODEL_WIDTH, EXPERTS), (4 * MODEL_WIDTH) ** -0.5, 0.078125, ((0, 32),))
    expert_in = noise(arg_keys[9], (EXPERTS, MODEL_WIDTH, 2 * FF), MODEL_WIDTH ** -0.5, 0.15625, ((0, 8), (1, 4)))
    expert_out = noise(arg_keys[10], (EXPERTS, FF, MODEL_WIDTH), (FF // 8) ** -0.5, 0.625, ((0, 8), (1, 4)))
    cotangent = noise(arg_keys[11], (SEQS, SLOTS, MODEL_WIDTH), 1.0, 6.0, ((0, 8), (1, 4)))
    return {"tokens": tokens, "lengths": lengths, "routes": routes, "prenorm": prenorm, "w_query": w_query, "key_value_weight": key_value_weight, "w_output": w_output, "midnorm": midnorm, "w_router": w_router, "expert_in": expert_in, "expert_out": expert_out, "cotangent": cotangent}


@jax.custom_vjp
def reduced_precision(v):
    return lax.optimization_barrier(v.astype(jnp.bfloat16)).astype(jnp.float32)

@jax.custom_vjp
def reduced_backward(v):
    return v

def low_keep(v):
    return (reduced_precision(v), None)

def low_pass(kept, grad):
    return (grad,)

def back_keep(v):
    return (v, None)

def back_low(kept, grad):
    return (reduced_precision(grad),)
reduced_precision.defvjp(low_keep, low_pass)
reduced_backward.defvjp(back_keep, back_low)
epsilon = 1e-06
rope_base = 10000.0
highest = lax.Precision.HIGHEST

def matrix_product(left, right):
    return jnp.dot(left, right, precision=highest)

def rms_scaled(values):
    return values * lax.rsqrt(lax.optimization_barrier(jnp.mean(values * values, axis=-1, keepdims=True)) + epsilon)

def rope_tables(expert_slot_count):
    half_width = HEAD_SIZE // 2
    inv_freq = rope_base ** (-(jnp.arange(half_width, dtype=jnp.float32) * 2.0 / HEAD_SIZE))
    angles = jnp.arange(expert_slot_count, dtype=jnp.float32)[:, None] * inv_freq[None, :]
    return (jnp.cos(angles), jnp.sin(angles))

def apply_rotation(values, cosine_table, sine_table):
    half_width = values.shape[-1] // 2
    first_half = values[..., :half_width]
    second = values[..., half_width:]
    cos_rows = cosine_table[:, None, :]
    sin_rows = sine_table[:, None, :]
    return jnp.concatenate([first_half * cos_rows - second * sin_rows, second * cos_rows + first_half * sin_rows], axis=-1)

def slot_index(routes):
    token_rows = routes.shape[0]
    blocks = token_rows // TOK_MB
    flat_routes = routes.reshape(blocks, TOK_MB * TOP)
    onehot = (flat_routes[:, :, None] == jnp.arange(EXPERTS, dtype=jnp.int32)[None, None, :]).astype(jnp.int32)
    before = jnp.cumsum(onehot, axis=1) - onehot
    within = lax.optimization_barrier(jnp.sum(before * onehot, axis=-1)).astype(jnp.int32)
    block_base = jnp.arange(blocks, dtype=jnp.int32)[:, None] * EXPERTS
    return ((block_base + flat_routes) * CAP + within).reshape(token_rows, TOP).astype(jnp.int32)

def sequence(tokens, length, routes, prenorm, w_query, key_value_weight, w_output, midnorm, w_router, expert_in, expert_out):
    expert_slot_count = tokens.shape[0]
    positions = jnp.arange(expert_slot_count, dtype=jnp.int32)
    live_rows = positions < length
    allowed = (positions[None, :] <= positions[:, None]) & live_rows[None, :]
    normalized_input = reduced_precision(rms_scaled(tokens) * prenorm)
    query_matrix = reduced_backward(matrix_product(normalized_input, w_query)).reshape(expert_slot_count, QUERY_HEADS, HEAD_SIZE)
    key_value_rows = reduced_backward(matrix_product(normalized_input, key_value_weight)).reshape(expert_slot_count, 2, KEY_VALUE_HEADS, HEAD_SIZE)
    cosine_table, sine_table = rope_tables(expert_slot_count)
    query_matrix = reduced_precision(apply_rotation(query_matrix, cosine_table, sine_table)).reshape(expert_slot_count, KEY_VALUE_HEADS, QUERY_HEADS // KEY_VALUE_HEADS, HEAD_SIZE)
    key_rows = reduced_precision(apply_rotation(key_value_rows[:, 0], cosine_table, sine_table))
    values = reduced_precision(key_value_rows[:, 1])
    scores = reduced_backward(jnp.einsum('qhgd,khd->hgqk', query_matrix, key_rows, precision=highest) * HEAD_SIZE ** (-0.5))
    scores = jnp.where(allowed[None, None], scores, -1e+30)
    top_score = lax.optimization_barrier(jnp.max(scores, axis=-1, keepdims=True))
    weights = jnp.exp(scores - top_score)
    probs_low = reduced_precision(weights / lax.optimization_barrier(jnp.sum(weights, axis=-1, keepdims=True)))
    attended = jnp.einsum('hgqk,khd->qhgd', probs_low, values, precision=highest).reshape(expert_slot_count, QUERY_HEADS * HEAD_SIZE)
    attended = reduced_precision(reduced_backward(attended))
    mixed_rows = tokens + reduced_backward(matrix_product(attended, w_output))
    normed_two = reduced_precision(rms_scaled(mixed_rows) * midnorm)
    logits = matrix_product(normed_two, w_router)
    gate_values = jax.nn.softmax(jnp.take_along_axis(logits, routes, axis=1), axis=-1)
    copies = reduced_backward(jnp.broadcast_to(normed_two[:, None, :], (expert_slot_count, TOP, MODEL_WIDTH)))
    slot_idx = slot_index(routes)
    blocks = expert_slot_count // TOK_MB
    buffer = jnp.zeros((blocks * EXPERTS * CAP, MODEL_WIDTH), jnp.float32).at[slot_idx.reshape(-1)].add(copies.reshape(expert_slot_count * TOP, MODEL_WIDTH))
    buffer = buffer.reshape(blocks, EXPERTS, CAP, MODEL_WIDTH)
    gate_up = reduced_backward(jnp.einsum('becd,edf->becf', buffer, expert_in, precision=highest))
    hidden = reduced_precision(jax.nn.silu(gate_up[..., :FF]) * gate_up[..., FF:])
    result = jnp.einsum('becf,efd->becd', hidden, expert_out, precision=highest)
    result = reduced_precision(reduced_backward(result)).reshape(blocks * EXPERTS * CAP, MODEL_WIDTH)
    returned = result[slot_idx]
    expert_sum = lax.optimization_barrier(jnp.sum(gate_values[:, :, None] * returned, axis=1))
    return jnp.where(live_rows[:, None], mixed_rows + expert_sum, 0.0)

def reference(tokens, lengths, routes, prenorm, w_query, key_value_weight, w_output, midnorm, w_router, expert_in, expert_out, cotangent):
    params = tuple((weight.astype(jnp.float32) for weight in (prenorm, w_query, key_value_weight, w_output, midnorm, w_router, expert_in, expert_out)))
    checked = jax.checkpoint(sequence)

    def forward(inputs, weight_set):

        def advance(carried, element):
            return (carried, checked(element[0], element[1], element[2], *weight_set))
        return lax.scan(advance, jnp.zeros((), jnp.float32), (inputs, lengths, routes))[1]
    outputs, pullback = jax.vjp(forward, tokens.astype(jnp.float32), params)
    grad_in, weight_grads = pullback(cotangent.astype(jnp.float32))
    return (outputs.astype(jnp.bfloat16), grad_in, weight_grads[0], weight_grads[1], weight_grads[2], weight_grads[3], weight_grads[4], weight_grads[5], weight_grads[6], weight_grads[7])
```

```python
import jax
import jax.numpy as jnp
from jax import lax
from jax.experimental import pallas as pl
from jax.experimental.pallas import tpu as pltpu
from jax.sharding import PartitionSpec as P

QUERY_HEADS = 12
KEY_VALUE_HEADS = 2
HEAD_SIZE = 128
FF = 768
TOP = 4


epsilon = 1e-06
rope_base = 10000.0
highest = lax.Precision.HIGHEST


def rope_tables(positions):
    half_width = HEAD_SIZE // 2
    inv_freq = rope_base ** (-(jnp.arange(half_width, dtype=jnp.float32) * 2.0 / HEAD_SIZE))
    angles = positions.astype(jnp.float32)[:, None] * inv_freq[None, :]
    return (jnp.cos(angles), jnp.sin(angles))


def apply_rotation(values, cosine_table, sine_table):
    half_width = values.shape[-1] // 2
    first_half = values[..., :half_width]
    second = values[..., half_width:]
    cos_rows = cosine_table[:, None, :]
    sin_rows = sine_table[:, None, :]
    return jnp.concatenate(
        [first_half * cos_rows - second * sin_rows, second * cos_rows + first_half * sin_rows],
        axis=-1,
    )


def unrotate(values, cosine_table, sine_table):
    half_width = values.shape[-1] // 2
    first_half = values[..., :half_width]
    second = values[..., half_width:]
    cos_rows = cosine_table[:, None, :]
    sin_rows = sine_table[:, None, :]
    return jnp.concatenate(
        [first_half * cos_rows + second * sin_rows, second * cos_rows - first_half * sin_rows],
        axis=-1,
    )


def rms_parts(values):
    inverse = lax.rsqrt(jnp.mean(values * values, axis=-1, keepdims=True) + epsilon)
    return (values * inverse, inverse)


def norm_back(grad_normed, normalized_input, inverse, gain):
    scaled = grad_normed * gain
    return inverse * (
        scaled - normalized_input * jnp.mean(scaled * normalized_input, axis=-1, keepdims=True)
    )


def slot_index(route_rows, expert_count, capacity):
    flat_routes = route_rows.reshape(-1)
    onehot = (flat_routes[:, None] == jnp.arange(expert_count, dtype=jnp.int32)[None, :]).astype(
        jnp.int32
    )
    before = jnp.cumsum(onehot, axis=0) - onehot
    within = jnp.sum(before * onehot, axis=-1)
    return flat_routes * capacity + within


def masked_scores(query_matrix, key_rows, allowed):
    scores = jnp.einsum(
        "qhgd,khd->hgqk", query_matrix, key_rows, preferred_element_type=jnp.float32
    ) * HEAD_SIZE ** (-0.5)
    return jnp.where(allowed[None, None], scores, -1e30)


def local(
    tokens,
    lengths,
    routes,
    prenorm,
    w_query,
    key_value_weight,
    w_output,
    midnorm,
    w_router,
    expert_in,
    expert_out,
    cotangent,
):
    micro_count, token_rows, hidden_width = tokens.shape
    dp_size = lax.axis_size("dp")
    expert_size = lax.axis_size("expert")
    dp_rank = lax.axis_index("dp")
    local_experts = expert_in.shape[0]
    expert_count = local_experts * expert_size
    capacity = max(2, 3 * token_rows * TOP // (2 * expert_count))
    query_group_width = QUERY_HEADS // KEY_VALUE_HEADS
    expert_slot_total = token_rows * dp_size
    score_scale = HEAD_SIZE ** (-0.5)
    positions = dp_rank * token_rows + jnp.arange(token_rows, dtype=jnp.int32)
    key_pos = jnp.arange(expert_slot_total, dtype=jnp.int32)
    cosine_table, sine_table = rope_tables(positions)
    total_prenorm = jnp.zeros((hidden_width,), jnp.float32)
    total_query = jnp.zeros((hidden_width, QUERY_HEADS * HEAD_SIZE), jnp.float32)
    total_key_value = jnp.zeros((hidden_width, 2 * KEY_VALUE_HEADS * HEAD_SIZE), jnp.float32)
    total_output = jnp.zeros((QUERY_HEADS * HEAD_SIZE, hidden_width), jnp.float32)
    total_midnorm = jnp.zeros((hidden_width,), jnp.float32)
    total_router = jnp.zeros((hidden_width, expert_count), jnp.float32)
    total_upper = jnp.zeros((local_experts, hidden_width, 2 * FF), jnp.float32)
    total_down = jnp.zeros((local_experts, FF, hidden_width), jnp.float32)
    outputs_list = []
    grads_list = []
    for micro_step in range(micro_count):
        dense_all = (
            lax.all_gather(prenorm, ("dp", "expert"), axis=0, tiled=True),
            lax.all_gather(w_query, ("dp", "expert"), axis=0, tiled=True),
            lax.all_gather(key_value_weight, ("dp", "expert"), axis=0, tiled=True),
            lax.all_gather(w_output, ("dp", "expert"), axis=0, tiled=True),
            lax.all_gather(midnorm, ("dp", "expert"), axis=0, tiled=True),
            lax.all_gather(w_router, ("dp", "expert"), axis=0, tiled=True),
        )
        expert_all = (
            lax.all_gather(expert_in, "dp", axis=1, tiled=True),
            lax.all_gather(expert_out, "dp", axis=1, tiled=True),
        )
        gain_one = dense_all[0].astype(jnp.float32)
        query_all = dense_all[1]
        keyval_all = dense_all[2]
        output_all = dense_all[3]
        gain_two = dense_all[4].astype(jnp.float32)
        router_all = dense_all[5]
        gateup_all = expert_all[0]
        down_all = expert_all[1]
        input_rows = tokens[micro_step].astype(jnp.float32)
        length = lengths[micro_step]
        route_rows = routes[micro_step]
        live_rows = (positions < length)[:, None]
        normed_one, inverse_one = rms_parts(input_rows)
        normalized_input = (normed_one * gain_one).astype(jnp.bfloat16)
        query_pre = jnp.dot(
            normalized_input, query_all, preferred_element_type=jnp.float32
        ).reshape(token_rows, QUERY_HEADS, HEAD_SIZE)
        keyval_pre = jnp.dot(
            normalized_input, keyval_all, preferred_element_type=jnp.float32
        ).reshape(token_rows, 2, KEY_VALUE_HEADS, HEAD_SIZE)
        query_matrix = (
            apply_rotation(query_pre, cosine_table, sine_table)
            .astype(jnp.bfloat16)
            .reshape(token_rows, KEY_VALUE_HEADS, query_group_width, HEAD_SIZE)
        )
        local_key_rows = apply_rotation(keyval_pre[:, 0], cosine_table, sine_table).astype(
            jnp.bfloat16
        )
        local_value_rows = keyval_pre[:, 1].astype(jnp.bfloat16)
        packed_tokens = jnp.stack([local_key_rows, local_value_rows], axis=1).reshape(
            token_rows, 2 * KEY_VALUE_HEADS * HEAD_SIZE
        )
        gathered_rows = lax.all_gather(packed_tokens, "dp", axis=0, tiled=True).reshape(
            expert_slot_total, 2, KEY_VALUE_HEADS, HEAD_SIZE
        )
        key_rows = gathered_rows[:, 0]
        value_rows = gathered_rows[:, 1]
        allowed = (key_pos[None, :] <= positions[:, None]) & (key_pos[None, :] < length)
        scores = masked_scores(query_matrix, key_rows, allowed)
        top_score = jnp.max(scores, axis=-1, keepdims=True)
        weights = jnp.exp(scores - top_score)
        weight_total = jnp.sum(weights, axis=-1, keepdims=True)
        log_total = top_score + jnp.log(weight_total)
        probs_low = (weights / weight_total).astype(jnp.bfloat16)
        attended = jnp.einsum(
            "hgqk,khd->qhgd", probs_low, value_rows, preferred_element_type=jnp.float32
        )
        attended = attended.reshape(token_rows, QUERY_HEADS * HEAD_SIZE).astype(jnp.bfloat16)
        mixed_rows = input_rows + jnp.dot(attended, output_all, preferred_element_type=jnp.float32)
        normed_mid, inverse_two = rms_parts(mixed_rows)
        normed_two = (normed_mid * gain_two).astype(jnp.bfloat16)
        logits = jnp.dot(normed_two, router_all, preferred_element_type=jnp.float32)
        onehot = (
            route_rows[:, :, None] == jnp.arange(expert_count, dtype=jnp.int32)[None, None, :]
        ).astype(jnp.float32)
        chosen = jnp.sum(onehot * logits[:, None, :], axis=-1)
        gate_values = jax.nn.softmax(chosen, axis=-1)
        slot_idx = slot_index(route_rows, expert_count, capacity)
        send_rows = jnp.zeros((expert_count * capacity, hidden_width), jnp.bfloat16)
        send_rows = send_rows.at[slot_idx].set(jnp.repeat(normed_two, TOP, axis=0))
        received = lax.all_to_all(
            send_rows.reshape(expert_count, capacity, hidden_width),
            "expert",
            split_axis=0,
            concat_axis=0,
            tiled=True,
        )
        item_count = received.shape[1]
        grouped = received.reshape(expert_size, local_experts, item_count, hidden_width)
        gate_up = jnp.einsum(
            "slcd,ldf->slcf", grouped, gateup_all, preferred_element_type=jnp.float32
        )
        hidden = (jax.nn.silu(gate_up[..., :FF]) * gate_up[..., FF:]).astype(jnp.bfloat16)
        result = jnp.einsum(
            "slcf,lfd->slcd", hidden, down_all, preferred_element_type=jnp.float32
        ).astype(jnp.bfloat16)
        back_rows = lax.all_to_all(
            result.reshape(expert_count, item_count, hidden_width),
            "expert",
            split_axis=0,
            concat_axis=0,
            tiled=True,
        )
        back_rows, kept_rows, kept_gateup = (
            back_rows,
            received,
            gate_up.reshape(expert_count, item_count, 2 * FF),
        )
        returned = back_rows.reshape(expert_count * capacity, hidden_width)[slot_idx].reshape(
            token_rows, TOP, hidden_width
        )
        returned_wide = returned.astype(jnp.float32)
        expert_sum = jnp.sum(gate_values[:, :, None] * returned_wide, axis=1)
        final_rows = jnp.where(live_rows, mixed_rows + expert_sum, 0.0)
        outputs_list.append(final_rows.astype(jnp.bfloat16))
        grad_rows = jnp.where(live_rows, cotangent[micro_step].astype(jnp.float32), 0.0)
        grad_gate = jnp.sum(grad_rows[:, None, :] * returned_wide, axis=-1)
        grad_chosen = gate_values * (
            grad_gate - jnp.sum(gate_values * grad_gate, axis=-1, keepdims=True)
        )
        grad_logits = jnp.sum(onehot * grad_chosen[:, :, None], axis=1)
        router_term = jnp.dot(normed_two.astype(jnp.float32).T, grad_logits, precision=highest)
        grad_normtwo = jnp.dot(grad_logits, router_all.astype(jnp.float32).T, precision=highest)
        grad_result = (
            (gate_values[:, :, None] * grad_rows[:, None, :])
            .astype(jnp.bfloat16)
            .reshape(token_rows * TOP, hidden_width)
        )
        send_grads = (
            jnp.zeros((expert_count * capacity, hidden_width), jnp.bfloat16)
            .at[slot_idx]
            .set(grad_result)
        )
        recv_grads, again_rows = (
            lax.all_to_all(
                send_grads.reshape(expert_count, capacity, hidden_width),
                "expert",
                split_axis=0,
                concat_axis=0,
                tiled=True,
            ),
            lax.all_to_all(
                send_rows.reshape(expert_count, capacity, hidden_width),
                "expert",
                split_axis=0,
                concat_axis=0,
                tiled=True,
            ),
        )
        grouped_rows = again_rows.reshape(expert_size, local_experts, capacity, hidden_width)
        gate_up = jnp.einsum(
            "slcd,ldf->slcf", grouped_rows, gateup_all, preferred_element_type=jnp.float32
        )
        grouped_grads = recv_grads.reshape(expert_size, local_experts, capacity, hidden_width)
        gate_part = gate_up[..., :FF]
        up_part = gate_up[..., FF:]
        sigmoid_gate = jax.nn.sigmoid(gate_part)
        silu_gate = gate_part * sigmoid_gate
        hidden = (silu_gate * up_part).astype(jnp.bfloat16)
        grad_hidden = jnp.einsum(
            "slcd,lfd->slcf", grouped_grads, down_all, preferred_element_type=jnp.float32
        )
        down_term = jnp.einsum(
            "slcf,slcd->lfd", hidden, grouped_grads, preferred_element_type=jnp.float32
        )
        grad_gatepart = (
            grad_hidden * up_part * sigmoid_gate * (1.0 + gate_part * (1.0 - sigmoid_gate))
        )
        grad_gateup = jnp.concatenate([grad_gatepart, grad_hidden * silu_gate], axis=-1).astype(
            jnp.bfloat16
        )
        upper_term = jnp.einsum(
            "slcd,slcf->ldf", grouped_rows, grad_gateup, preferred_element_type=jnp.float32
        )
        grad_copies = jnp.einsum(
            "slcf,ldf->slcd", grad_gateup, gateup_all, preferred_element_type=jnp.float32
        ).astype(jnp.bfloat16)
        back_grads = lax.all_to_all(
            grad_copies.reshape(expert_count, capacity, hidden_width),
            "expert",
            split_axis=0,
            concat_axis=0,
            tiled=True,
        )
        copy_rows = back_grads.reshape(expert_count * capacity, hidden_width)[slot_idx].reshape(
            token_rows, TOP, hidden_width
        )
        grad_normtwo = grad_normtwo + jnp.sum(copy_rows.astype(jnp.float32), axis=1)
        midnorm_term = jnp.sum(grad_normtwo * normed_mid, axis=0)
        grad_mixed = grad_rows + norm_back(grad_normtwo, normed_mid, inverse_two, gain_two)
        grad_proj = grad_mixed.astype(jnp.bfloat16)
        output_term = jnp.dot(attended.T, grad_proj, preferred_element_type=jnp.float32)
        attention_gradient = jnp.dot(
            grad_proj, output_all.T, preferred_element_type=jnp.float32
        ).astype(jnp.bfloat16)
        attention_gradient = attention_gradient.reshape(
            token_rows, KEY_VALUE_HEADS, query_group_width, HEAD_SIZE
        )
        scores = masked_scores(query_matrix, key_rows, allowed)
        prob_rows = jnp.exp(scores - log_total)
        grad_probs = jnp.einsum(
            "qhgd,khd->hgqk", attention_gradient, value_rows, preferred_element_type=jnp.float32
        )
        row_delta = jnp.sum(prob_rows * grad_probs, axis=-1, keepdims=True)
        grad_scores = (prob_rows * (grad_probs - row_delta)).astype(jnp.bfloat16)
        prob_low = prob_rows.astype(jnp.bfloat16)
        grad_qrot = (
            jnp.einsum("hgqk,khd->qhgd", grad_scores, key_rows, preferred_element_type=jnp.float32)
            * score_scale
        )
        grad_keys = (
            jnp.einsum(
                "hgqk,qhgd->khd", grad_scores, query_matrix, preferred_element_type=jnp.float32
            )
            * score_scale
        )
        grad_vals = jnp.einsum(
            "hgqk,qhgd->khd", prob_low, attention_gradient, preferred_element_type=jnp.float32
        )
        own_keys = (
            lax.psum_scatter(
                jnp.stack([grad_keys, grad_vals], axis=1)
                .reshape(lax.axis_size("dp") * token_rows, 2 * KEY_VALUE_HEADS * HEAD_SIZE)
                .astype(jnp.bfloat16),
                "dp",
                scatter_dimension=0,
                tiled=True,
            )
            .astype(jnp.float32)
            .reshape(token_rows, 2, KEY_VALUE_HEADS, HEAD_SIZE)
        )
        grad_query = (
            unrotate(
                grad_qrot.reshape(token_rows, QUERY_HEADS, HEAD_SIZE), cosine_table, sine_table
            )
            .astype(jnp.bfloat16)
            .reshape(token_rows, QUERY_HEADS * HEAD_SIZE)
        )
        key_gradient = unrotate(own_keys[:, 0], cosine_table, sine_table).astype(jnp.bfloat16)
        value_gradient = own_keys[:, 1].astype(jnp.bfloat16)
        key_value_weight_gradient = jnp.stack([key_gradient, value_gradient], axis=1).reshape(
            token_rows, 2 * KEY_VALUE_HEADS * HEAD_SIZE
        )
        query_term = jnp.dot(normalized_input.T, grad_query, preferred_element_type=jnp.float32)
        keyval_term = jnp.dot(
            normalized_input.T, key_value_weight_gradient, preferred_element_type=jnp.float32
        )
        grad_normone = jnp.dot(grad_query, query_all.T, preferred_element_type=jnp.float32)
        grad_normone = grad_normone + jnp.dot(
            key_value_weight_gradient, keyval_all.T, preferred_element_type=jnp.float32
        )
        prenorm_term = jnp.sum(grad_normone * normed_one, axis=0)
        grads_list.append(grad_mixed + norm_back(grad_normone, normed_one, inverse_one, gain_one))
        total_prenorm = total_prenorm + prenorm_term
        total_query = total_query + query_term
        total_key_value = total_key_value + keyval_term
        total_output = total_output + output_term
        total_midnorm = total_midnorm + midnorm_term
        total_router = total_router + router_term
        total_upper = total_upper + upper_term
        total_down = total_down + down_term
    dense_grads = (
        lax.psum_scatter(total_prenorm, ("dp", "expert"), scatter_dimension=0, tiled=True),
        lax.psum_scatter(total_query, ("dp", "expert"), scatter_dimension=0, tiled=True),
        lax.psum_scatter(total_key_value, ("dp", "expert"), scatter_dimension=0, tiled=True),
        lax.psum_scatter(total_output, ("dp", "expert"), scatter_dimension=0, tiled=True),
        lax.psum_scatter(total_midnorm, ("dp", "expert"), scatter_dimension=0, tiled=True),
        lax.psum_scatter(total_router, ("dp", "expert"), scatter_dimension=0, tiled=True),
    )
    expert_grads = (
        lax.psum_scatter(
            total_upper.astype(jnp.bfloat16), "dp", scatter_dimension=1, tiled=True
        ).astype(jnp.float32),
        lax.psum_scatter(
            total_down.astype(jnp.bfloat16), "dp", scatter_dimension=1, tiled=True
        ).astype(jnp.float32),
    )
    return (
        jnp.stack(outputs_list),
        jnp.stack(grads_list),
        dense_grads[0],
        dense_grads[1],
        dense_grads[2],
        dense_grads[3],
        dense_grads[4],
        dense_grads[5],
        expert_grads[0],
        expert_grads[1],
    )


MESH = pl.DeviceIdType.MESH
CHUNK = 256
PIECE = 96


def remote(src, dst, send_sem, recv_sem, target):
    return pltpu.make_async_remote_copy(
        src_ref=src,
        dst_ref=dst,
        send_sem=send_sem,
        recv_sem=recv_sem,
        device_id=target,
        device_id_type=MESH,
    )


def place():
    d = lax.axis_index("dp")
    e = lax.axis_index("expert")
    z = lax.div(e, 2)
    c = lax.rem(e, 2)
    x = lax.rem(d, 2)
    y = lax.div(d, 2)
    return d, e, z, c, x, y


def expert_kernel(
    x_hbm,
    g_hbm,
    gt_hbm,
    win_hbm,
    wout_hbm,
    dx_out,
    dgt_out,
    outp_hbm,
    gin_hbm,
    gout_hbm,
    win,
    wout,
    xall,
    gall,
    gtall,
    dgu,
    hg,
    dxb,
    dgb,
    sibr,
    sibg,
    ro,
    rog,
    ri,
    rig,
    stage,
    own_sem,
    stage_sem,
    w_recv,
    w_send,
    ag_recv,
    ag_send,
    sib_recv,
    sib_send,
    red_recv,
    red_send,
):
    d, e, z, c, x, y = place()
    d_x = d + 1 - 2 * x
    d_y = d + 2 - 4 * y
    d_d = 3 - d
    hi = lax.div(z, 2)
    zz = z * hi + (3 - z) * (1 - hi)
    other = 1 - c
    to_x = (d_x, e)
    to_y = (d_y, e)
    to_sib = (d, 2 * z + other)
    to_up = (d, e + jnp.where(z < 3, 2, -2))
    to_down = (d, e + jnp.where(z > 0, -2, 2))
    e_in = e + 2 - 4 * hi
    e_out = e - 2 + 4 * hi
    to_in = (d, e_in)
    to_out = (d, jnp.where(zz == 2, e_out, e_in))
    mid = zz == 2
    end = zz == 3

    barrier = pltpu.get_barrier_semaphore()
    for target in (to_x, to_y, to_sib, to_in):
        pl.semaphore_signal(barrier, inc=1, device_id=target, device_id_type=MESH)

    @pl.when(mid)
    def _():
        pl.semaphore_signal(barrier, inc=1, device_id=to_out, device_id_type=MESH)

    pl.semaphore_wait(barrier, 7 - zz)

    gathered = ((x_hbm, xall), (gt_hbm, gtall), (g_hbm, gall))

    def part(a, ref, zp, lane, s):
        if a == 1:
            return ref.at[2 * zp + lane, s]
        return ref.at[pl.ds(pl.multiple_of((2 * zp + lane) * CHUNK + s * 128, 128), 128)]

    def own_part(a, ref, s):
        if a == 1:
            return ref.at[s]
        return ref.at[pl.ds(s * 128, 128)]

    def ag_copy(a, zp, s, way, src=None):
        ref = part(a, gathered[a][1], zp, c, s)
        return remote(
            ref if src is None else src,
            ref,
            ag_send.at[way, a, zp, s],
            ag_recv.at[a, zp, s],
            to_up if way == 0 else to_down,
        )

    def sib_copy(a, zp, s, src=None):
        ref = part(a, gathered[a][1], zp, c, s)
        return remote(
            ref if src is None else src,
            ref,
            sib_send.at[a, zp, s],
            sib_recv.at[a, zp, s],
            to_sib,
        )

    def piece(p, dd):
        if p < 4:
            return win.at[pl.ds(pl.multiple_of(dd * 384 + p * PIECE, 16), PIECE)]
        return wout.at[pl.ds(pl.multiple_of(dd * 192 + (p - 4) * PIECE, 16), PIECE)]

    def own_piece(p):
        if p < 4:
            return win_hbm.at[pl.ds(p * PIECE, PIECE)]
        return wout_hbm.at[pl.ds((p - 4) * PIECE, PIECE)]

    def w_copy(p, way, src_d, target, row, src=None):
        ref = piece(p, src_d)
        return remote(
            ref if src is None else src, ref, w_send.at[row, p], w_recv.at[row, p], target
        )

    for a in range(3):
        for s in range(2):
            src = own_part(a, gathered[a][0], s)

            @pl.when(z < 3)
            def _():
                ag_copy(a, z, s, 0, src).start()

            @pl.when(z > 0)
            def _():
                ag_copy(a, z, s, 1, src).start()

            sib_copy(a, z, s, src).start()
    for p in range(6):
        w_copy(p, 0, d, to_x, 0, own_piece(p)).start()
        w_copy(p, 0, d, to_y, 1, own_piece(p)).start()
    own_copies = [
        pltpu.make_async_copy(
            x_hbm, xall.at[pl.ds(pl.multiple_of(e * CHUNK, 128), CHUNK)], own_sem.at[0]
        ),
        pltpu.make_async_copy(
            g_hbm, gall.at[pl.ds(pl.multiple_of(e * CHUNK, 128), CHUNK)], own_sem.at[1]
        ),
        pltpu.make_async_copy(gt_hbm, gtall.at[e], own_sem.at[2]),
        pltpu.make_async_copy(
            win_hbm, win.at[pl.ds(pl.multiple_of(d * 384, 16), 384)], own_sem.at[3]
        ),
        pltpu.make_async_copy(
            wout_hbm, wout.at[pl.ds(pl.multiple_of(d * 192, 16), 192)], own_sem.at[4]
        ),
    ]
    for copy in own_copies:
        copy.start()

    def pass_on(a, k, s):
        @pl.when(z - k >= 0)
        def _():
            ag_copy(a, z - k, s, 0).wait_recv()

            @pl.when(z < 3)
            def _():
                ag_copy(a, z - k, s, 0).start()

            sib_copy(a, z - k, s).start()

        @pl.when(z + k <= 3)
        def _():
            ag_copy(a, z + k, s, 1).wait_recv()

            @pl.when(z > 0)
            def _():
                ag_copy(a, z + k, s, 1).start()

            sib_copy(a, z + k, s).start()

    for p in range(6):
        w_copy(p, 0, d_x, to_x, 0).wait_recv()
        if p % 2 == 0:
            w_copy(p, 0, d_x, to_y, 3).start()
        w_copy(p, 0, d_y, to_y, 1).wait_recv()
        if p % 2 == 1:
            w_copy(p, 0, d_y, to_x, 2).start()
        for a in range(2):
            pass_on(a, 1 + p // 2, p % 2)
    for p in range(6):
        if p % 2 == 0:
            w_copy(p, 0, d_d, to_y, 3).wait_recv()
        else:
            w_copy(p, 0, d_d, to_x, 2).wait_recv()
    for p in range(6):
        pass_on(2, 1 + p // 2, p % 2)
    for a in range(3):
        for zp in range(4):
            for s in range(2):
                ref = part(a, gathered[a][1], zp, other, s)
                remote(
                    ref, ref, sib_send.at[a, zp, s], sib_recv.at[a, zp, s], to_sib
                ).wait_recv()
    for copy in own_copies:
        copy.wait()

    eye = lax.broadcasted_iota(jnp.int32, (128, 128), 0) == lax.broadcasted_iota(
        jnp.int32, (128, 128), 1
    )
    mine = lax.broadcasted_iota(jnp.int32, (8, 128), 0) == e

    def order(i):
        v = jnp.where(i < 2, i, jnp.where(i == 2, 5 - zz, zz))
        return v * hi + (3 - v) * (1 - hi)

    def out_copy(i, zp):
        return pltpu.make_async_copy(
            stage.at[lax.rem(i, 2)],
            outp_hbm.at[pl.ds(pl.multiple_of(zp * 512, 512), 512)],
            stage_sem.at[lax.rem(i, 2)],
        )

    def lane_rows(i, lane):
        return pl.ds(pl.multiple_of(i * 512 + lane * CHUNK, CHUNK), CHUNK)

    def sib_sum_copies(i):
        return (
            remote(
                dxb.at[lane_rows(i, other)], sibr.at[i], red_send.at[0, i], red_recv.at[0, i], to_sib
            ),
            remote(dgb.at[i, other], sibg.at[i], red_send.at[1, i], red_recv.at[1, i], to_sib),
        )

    def hop_copies(i, target, dst, dstg, row):
        return (
            remote(
                dxb.at[lane_rows(i, c)], dst.at[i], red_send.at[2, i], red_recv.at[row, i], target
            ),
            remote(dgb.at[i, c], dstg.at[i], red_send.at[3, i], red_recv.at[row + 1, i], target),
        )

    def wait_from(ref, refg, slot, row):
        remote(ref.at[slot], ref.at[slot], red_send.at[2, slot], red_recv.at[row, slot], to_in).wait_recv()
        remote(refg.at[slot], refg.at[slot], red_send.at[3, slot], red_recv.at[row + 1, slot], to_in).wait_recv()

    def combine(i, incoming):
        total = dxb[lane_rows(i, c)].astype(jnp.float32) + sibr[i].astype(jnp.float32)
        totalg = dgb[i, c] + sibg[i]
        for ref, refg, slot in incoming:
            total = total + ref[slot].astype(jnp.float32)
            totalg = totalg + refg[slot]
        return total, totalg

    def combine_store(i, incoming):
        total, totalg = combine(i, incoming)
        dxb[lane_rows(i, c)] = total.astype(jnp.bfloat16)
        dgb[i, c] = totalg

    @pl.loop(0, 4)
    def _(i):
        zp = order(i)
        rows = pl.ds(pl.multiple_of(zp * 512, 512), 512)
        xc = xall[rows]
        gate = jnp.dot(xc, win[:, :FF], preferred_element_type=jnp.float32)
        up = jnp.dot(xc, win[:, FF:], preferred_element_type=jnp.float32)
        back = lax.dot_general(
            gall[rows], wout[...], (((1,), (1,)), ((), ())), preferred_element_type=jnp.float32
        )
        columns = []
        for lane in range(2):
            for s in range(2):
                row = jnp.sum(jnp.where(mine, gtall[2 * zp + lane, s], 0.0), axis=0, keepdims=True)
                columns.append(jnp.sum(jnp.where(eye, row, 0.0), axis=1, keepdims=True))
        weight = jnp.concatenate(columns, axis=0)
        sig = jax.nn.sigmoid(gate)
        silu = gate * sig
        hidden = (silu * up).astype(jnp.bfloat16).astype(jnp.float32)
        dgate = jnp.sum(hidden * back, axis=1, keepdims=True)
        for lane in range(2):
            for s in range(2):
                at = (2 * lane + s) * 128
                row = jnp.sum(jnp.where(eye, dgate[at : at + 128], 0.0), axis=0, keepdims=True)
                dgb[i, lane, s] = jnp.where(mine, row, 0.0)
        hg[rows] = (hidden * weight).astype(jnp.bfloat16)
        back = back * weight
        dgu[rows, :FF] = (back * up * (sig * (1.0 + gate * (1.0 - sig)))).astype(jnp.bfloat16)
        dgu[rows, FF:] = (back * silu).astype(jnp.bfloat16)
        dxb[pl.ds(pl.multiple_of(i * 512, 512), 512)] = lax.dot_general(
            dgu[rows], win[...], (((1,), (1,)), ((), ())), preferred_element_type=jnp.float32
        ).astype(jnp.bfloat16)
        for copy in sib_sum_copies(i):
            copy.start()

        @pl.when(i >= 2)
        def _():
            out_copy(i, zp).wait()

        stage[lax.rem(i, 2)] = jnp.dot(
            hg[rows], wout[...], preferred_element_type=jnp.float32
        ).astype(jnp.bfloat16)
        out_copy(i, zp).start()
        for copy in sib_sum_copies(i):
            copy.wait_recv()

        @pl.when(end & (i < 3))
        def _():
            combine_store(i, ())
            for copy in hop_copies(i, to_in, ro, rog, 2):
                copy.start()

        @pl.when(mid & (i == 2))
        def _():
            wait_from(ro, rog, 0, 2)
            combine_store(0, ((ro, rog, 0),))
            for copy in hop_copies(0, to_in, ri, rig, 4):
                copy.start()

    @pl.when(mid)
    def _():
        wait_from(ro, rog, 1, 2)
        combine_store(1, ((ro, rog, 1),))
        for copy in hop_copies(1, to_in, ri, rig, 4):
            copy.start()

    def grad_copy(k, target, at):
        return pltpu.make_async_copy(
            stage.at[k % 2, pl.ds(0, 384)], target.at[pl.ds(at, 384)], stage_sem.at[k % 2]
        )

    blocks = [(gout_hbm, 0), (gout_hbm, 384)] + [(gin_hbm, 384 * k) for k in range(4)]
    for k in range(2):
        out_copy(k, 0).wait()
    for k, (target, at) in enumerate(blocks):
        if k >= 2:
            grad_copy(k - 2, *blocks[k - 2]).wait()
        left = hg if k < 2 else xall
        right = gall if k < 2 else dgu
        stage[k % 2, :384] = lax.dot_general(
            left[:, at : at + 384],
            right[...],
            (((0,), (0,)), ((), ())),
            preferred_element_type=jnp.float32,
        ).astype(jnp.bfloat16)
        grad_copy(k, target, at).start()
        if k == 1:

            @pl.when(mid)
            def _():
                wait_from(ri, rig, 0, 4)
                combine_store(2, ((ri, rig, 0),))
                for copy in hop_copies(2, to_out, ri, rig, 4):
                    copy.start()

    for k in (4, 5):
        grad_copy(k, *blocks[k]).wait()

    @pl.when(mid)
    def _():
        wait_from(ro, rog, 2, 2)
        wait_from(ri, rig, 1, 4)
        total, totalg = combine(3, ((ro, rog, 2), (ri, rig, 1)))
        dx_out[...] = total
        dgt_out[...] = totalg

    @pl.when(end)
    def _():
        wait_from(ri, rig, 2, 4)
        total, totalg = combine(3, ((ri, rig, 2),))
        dx_out[...] = total
        dgt_out[...] = totalg

    for p in range(6):
        w_copy(p, 0, d, to_x, 0, own_piece(p)).wait_send()
        w_copy(p, 0, d, to_y, 1, own_piece(p)).wait_send()
        if p % 2 == 0:
            w_copy(p, 0, d_x, to_y, 3).wait_send()
        else:
            w_copy(p, 0, d_y, to_x, 2).wait_send()
    for a in range(3):
        for s in range(2):
            for zp in range(4):
                sib_copy(a, zp, s).wait_send()

                @pl.when((zp <= z) & (z < 3))
                def _():
                    ag_copy(a, zp, s, 0).wait_send()

                @pl.when((zp >= z) & (z > 0))
                def _():
                    ag_copy(a, zp, s, 1).wait_send()

    for i in range(4):
        for copy in sib_sum_copies(i):
            copy.wait_send()
        if i < 3:
            for copy in hop_copies(i, to_in, ro, rog, 2):
                copy.wait_send()


def expert_stage(rows, grads, gates_t, w_in, w_out):
    bf, f32 = jnp.bfloat16, jnp.float32
    shape = jax.ShapeDtypeStruct
    width = rows.shape[-1]
    hbm = pl.BlockSpec(memory_space=pltpu.HBM)
    vmem = pl.BlockSpec(memory_space=pltpu.VMEM)
    dma = pltpu.SemaphoreType.DMA
    return pl.pallas_call(
        expert_kernel,
        out_shape=(
            shape((CHUNK, width), f32),
            shape((2, 8, 128), f32),
            shape((8 * CHUNK, width), bf),
            shape((width, 2 * FF), bf),
            shape((FF, width), bf),
        ),
        in_specs=[hbm] * 5,
        out_specs=(vmem, vmem, hbm, hbm, hbm),
        scratch_shapes=[
            pltpu.VMEM((width, 2 * FF), bf),
            pltpu.VMEM((FF, width), bf),
            pltpu.VMEM((8 * CHUNK, width), bf),
            pltpu.VMEM((8 * CHUNK, width), bf),
            pltpu.VMEM((8, 2, 8, 128), f32),
            pltpu.VMEM((8 * CHUNK, 2 * FF), bf),
            pltpu.VMEM((8 * CHUNK, FF), bf),
            pltpu.VMEM((8 * CHUNK, width), bf),
            pltpu.VMEM((4, 2, 2, 8, 128), f32),
            pltpu.VMEM((4, CHUNK, width), bf),
            pltpu.VMEM((4, 2, 8, 128), f32),
            pltpu.VMEM((3, CHUNK, width), bf),
            pltpu.VMEM((3, 2, 8, 128), f32),
            pltpu.VMEM((3, CHUNK, width), bf),
            pltpu.VMEM((3, 2, 8, 128), f32),
            pltpu.VMEM((2, 512, width), bf),
            dma((5,)),
            dma((2,)),
            dma((4, 6)),
            dma((4, 6)),
            dma((3, 4, 2)),
            dma((2, 3, 4, 2)),
            dma((3, 4, 2)),
            dma((3, 4, 2)),
            dma((6, 4)),
            dma((4, 4)),
        ],
        compiler_params=pltpu.CompilerParams(
            collective_id=1, has_side_effects=True, vmem_limit_bytes=63 * 2**20
        ),
        name="expert_stage",
    )(rows, grads, gates_t, w_in, w_out)


def fast_local(
    tokens,
    lengths,
    routes,
    prenorm,
    w_query,
    key_value_weight,
    w_output,
    midnorm,
    w_router,
    expert_in,
    expert_out,
    cotangent,
):
    bf, f32 = jnp.bfloat16, jnp.float32
    seqs, token_rows, width = tokens.shape
    dp_size = lax.axis_size("dp")
    dp_rank = lax.axis_index("dp")
    expert_count = lax.axis_size("expert")
    group = QUERY_HEADS // KEY_VALUE_HEADS
    slots = token_rows * dp_size
    rows = seqs * token_rows
    scale = HEAD_SIZE ** (-0.5)
    both = ("dp", "expert")
    small = jnp.concatenate(
        [w_router, prenorm[:, None], midnorm[:, None], jnp.zeros((w_router.shape[0], 118), bf)], axis=1
    )
    packed = jnp.concatenate([w_query, key_value_weight, w_output, small], axis=1)
    packed = lax.all_gather(packed, both, axis=0, tiled=True)
    query_all = packed[:, :1536]
    keyval_all = packed[:, 1536:2048]
    output_all = packed[:, 2048:3584]
    router_all = packed[:, 3584:3592]
    gain_one = packed[:, 3592].astype(f32)
    gain_two = packed[:, 3593].astype(f32)

    positions = dp_rank * token_rows + jnp.arange(token_rows, dtype=jnp.int32)
    key_pos = jnp.arange(slots, dtype=jnp.int32)
    cosine_table, sine_table = rope_tables(positions)
    cosine_table = jnp.tile(cosine_table, (seqs, 1))
    sine_table = jnp.tile(sine_table, (seqs, 1))
    live = (positions[None, :] < lengths[:, None]).reshape(rows, 1)
    x = tokens.reshape(rows, width).astype(f32)
    g = jnp.where(live, cotangent.reshape(rows, width), 0)
    n1, inv1 = rms_parts(x)
    normed = (n1 * gain_one).astype(bf)
    q = jnp.dot(normed, query_all, preferred_element_type=f32).reshape(rows, QUERY_HEADS, HEAD_SIZE)
    kv = jnp.dot(normed, keyval_all, preferred_element_type=f32).reshape(
        rows, 2, KEY_VALUE_HEADS, HEAD_SIZE
    )
    q_rot = apply_rotation(q, cosine_table, sine_table).astype(bf)
    q_rot = q_rot.reshape(seqs, token_rows, KEY_VALUE_HEADS, group, HEAD_SIZE)
    k_rot = apply_rotation(kv[:, 0], cosine_table, sine_table).astype(bf)
    kv_own = jnp.stack([k_rot, kv[:, 1].astype(bf)], axis=1).reshape(seqs, token_rows, 512)
    kv_all = lax.all_gather(kv_own, "dp", axis=1, tiled=True).reshape(
        seqs, slots, 2, KEY_VALUE_HEADS, HEAD_SIZE
    )
    keys, values = kv_all[:, :, 0], kv_all[:, :, 1]
    allowed = (key_pos[None, None, :] <= positions[None, :, None]) & (
        key_pos[None, None, :] < lengths[:, None, None]
    )

    def score():
        out = jnp.einsum("sqhgd,skhd->shgqk", q_rot, keys, preferred_element_type=f32) * scale
        return jnp.where(allowed[:, None, None], out, -1e30)

    scores = score()
    top = jnp.max(scores, axis=-1, keepdims=True)
    weights = jnp.exp(scores - top)
    total = jnp.sum(weights, axis=-1, keepdims=True)
    lse = top + jnp.log(total)
    probs_low = (weights / total).astype(bf)
    attended = jnp.einsum("shgqk,skhd->sqhgd", probs_low, values, preferred_element_type=f32)
    attended = attended.reshape(rows, QUERY_HEADS * HEAD_SIZE).astype(bf)
    mixed = x + jnp.dot(attended, output_all, preferred_element_type=f32)
    n2, inv2 = rms_parts(mixed)
    normed2 = (n2 * gain_two).astype(bf)
    logits = jnp.dot(normed2, router_all, preferred_element_type=f32)
    chosen = jnp.any(
        routes.reshape(rows, TOP)[:, :, None] == jnp.arange(expert_count, dtype=jnp.int32), axis=1
    )
    gates = jax.nn.softmax(jnp.where(chosen, logits, -jnp.inf), axis=-1)
    gates_t = jnp.transpose(gates.reshape(seqs, token_rows, expert_count), (0, 2, 1))
    dx, dgate_t, outp, gin, gout = expert_stage(
        normed2, g, gates_t, expert_in[0], expert_out[0]
    )
    expert_sum = lax.psum_scatter(outp, "expert", scatter_dimension=0, tiled=True).astype(f32)
    block_out = jnp.where(live, mixed + expert_sum, 0.0).astype(bf)
    gf = g.astype(f32)
    dgate = jnp.transpose(dgate_t, (0, 2, 1)).reshape(rows, expert_count)
    dlogit = gates * (dgate - jnp.sum(gates * dgate, axis=-1, keepdims=True))
    g_router = jnp.dot(normed2.astype(f32).T, dlogit, precision=highest)
    dn2 = dx + jnp.dot(dlogit, router_all.astype(f32).T, precision=highest)
    g_mid = jnp.sum(dn2 * n2, axis=0)
    dmixed = gf + norm_back(dn2, n2, inv2, gain_two)
    dproj = dmixed.astype(bf)
    g_out = jnp.dot(attended.T, dproj, preferred_element_type=f32)
    datt = jnp.dot(dproj, output_all.T, preferred_element_type=f32).astype(bf)
    datt = datt.reshape(seqs, token_rows, KEY_VALUE_HEADS, group, HEAD_SIZE)
    probs = jnp.exp(score() - lse)
    dprobs = jnp.einsum("sqhgd,skhd->shgqk", datt, values, preferred_element_type=f32)
    delta = jnp.sum(probs * dprobs, axis=-1, keepdims=True)
    dscores = (probs * (dprobs - delta)).astype(bf)
    dq_rot = jnp.einsum("shgqk,skhd->sqhgd", dscores, keys, preferred_element_type=f32) * scale
    dk = jnp.einsum("shgqk,sqhgd->skhd", dscores, q_rot, preferred_element_type=f32) * scale
    dv = jnp.einsum(
        "shgqk,sqhgd->skhd", probs.astype(bf), datt, preferred_element_type=f32
    )
    dkv = jnp.stack([dk, dv], axis=2).reshape(seqs, slots, 512).astype(bf)
    own = lax.psum_scatter(dkv, "dp", scatter_dimension=1, tiled=True).astype(f32)
    own = own.reshape(rows, 2, KEY_VALUE_HEADS, HEAD_SIZE)
    dq = unrotate(dq_rot.reshape(rows, QUERY_HEADS, HEAD_SIZE), cosine_table, sine_table)
    dq = dq.astype(bf).reshape(rows, QUERY_HEADS * HEAD_SIZE)
    dk_own = unrotate(own[:, 0], cosine_table, sine_table).astype(bf)
    dkv_own = jnp.stack([dk_own, own[:, 1].astype(bf)], axis=1).reshape(rows, 512)
    g_query = jnp.dot(normed.T, dq, preferred_element_type=f32)
    g_kv = jnp.dot(normed.T, dkv_own, preferred_element_type=f32)
    dn1 = jnp.dot(dq, query_all.T, preferred_element_type=f32)
    dn1 = dn1 + jnp.dot(dkv_own, keyval_all.T, preferred_element_type=f32)
    g_pre = jnp.sum(dn1 * n1, axis=0)
    grad_tokens = dmixed + norm_back(dn1, n1, inv1, gain_one)
    dense = jnp.concatenate(
        [g_query, g_kv, g_out, g_router, g_pre[:, None], g_mid[:, None]], axis=1
    ).astype(bf)
    dense = lax.psum_scatter(dense, both, scatter_dimension=0, tiled=True).astype(f32)
    upper = lax.psum_scatter(gin, "dp", scatter_dimension=0, tiled=True).astype(f32)
    down = lax.psum_scatter(gout, "dp", scatter_dimension=0, tiled=True).astype(f32)
    return (
        block_out.reshape(seqs, token_rows, width),
        grad_tokens.reshape(seqs, token_rows, width),
        dense[:, 3592],
        dense[:, :1536],
        dense[:, 1536:2048],
        dense[:, 2048:3584],
        dense[:, 3593],
        dense[:, 3584:3592],
        upper[None],
        down[None],
    )


def solution(mesh):
    placed = (
        P("expert", "dp", None),
        P("expert"),
        P("expert", "dp", None),
        P(("dp", "expert")),
        P(("dp", "expert"), None),
        P(("dp", "expert"), None),
        P(("dp", "expert"), None),
        P(("dp", "expert")),
        P(("dp", "expert"), None),
        P("expert", "dp", None),
        P("expert", "dp", None),
        P("expert", "dp", None),
    )
    small = mesh.shape["dp"] == 4 and mesh.shape["expert"] == 8
    return jax.shard_map(
        fast_local if small else local,
        mesh=mesh,
        in_specs=placed,
        out_specs=(
            P("expert", "dp", None),
            P("expert", "dp", None),
            P(("dp", "expert")),
            P(("dp", "expert"), None),
            P(("dp", "expert"), None),
            P(("dp", "expert"), None),
            P(("dp", "expert")),
            P(("dp", "expert"), None),
            P("expert", "dp", None),
            P("expert", "dp", None),
        ),
        check_vma=False,
    )
```

```python
import jax
import jax.numpy as jnp
from jax import lax
from jax.experimental import pallas as pl
from jax.experimental.pallas import tpu as pltpu
from jax.sharding import PartitionSpec as P

QUERY_HEADS = 12
KEY_VALUE_HEADS = 2
HEAD_SIZE = 128
FF = 768
TOP = 4


epsilon = 1e-06
rope_base = 10000.0
highest = lax.Precision.HIGHEST


def rope_tables(positions):
    half_width = HEAD_SIZE // 2
    inv_freq = rope_base ** (-(jnp.arange(half_width, dtype=jnp.float32) * 2.0 / HEAD_SIZE))
    angles = positions.astype(jnp.float32)[:, None] * inv_freq[None, :]
    return (jnp.cos(angles), jnp.sin(angles))


def apply_rotation(values, cosine_table, sine_table):
    half_width = values.shape[-1] // 2
    first_half = values[..., :half_width]
    second = values[..., half_width:]
    cos_rows = cosine_table[:, None, :]
    sin_rows = sine_table[:, None, :]
    return jnp.concatenate(
        [first_half * cos_rows - second * sin_rows, second * cos_rows + first_half * sin_rows],
        axis=-1,
    )


def unrotate(values, cosine_table, sine_table):
    half_width = values.shape[-1] // 2
    first_half = values[..., :half_width]
    second = values[..., half_width:]
    cos_rows = cosine_table[:, None, :]
    sin_rows = sine_table[:, None, :]
    return jnp.concatenate(
        [first_half * cos_rows + second * sin_rows, second * cos_rows - first_half * sin_rows],
        axis=-1,
    )


def rms_parts(values):
    inverse = lax.rsqrt(jnp.mean(values * values, axis=-1, keepdims=True) + epsilon)
    return (values * inverse, inverse)


def norm_back(grad_normed, normalized_input, inverse, gain):
    scaled = grad_normed * gain
    return inverse * (
        scaled - normalized_input * jnp.mean(scaled * normalized_input, axis=-1, keepdims=True)
    )


def slot_index(route_rows, expert_count, capacity):
    flat_routes = route_rows.reshape(-1)
    onehot = (flat_routes[:, None] == jnp.arange(expert_count, dtype=jnp.int32)[None, :]).astype(
        jnp.int32
    )
    before = jnp.cumsum(onehot, axis=0) - onehot
    within = jnp.sum(before * onehot, axis=-1)
    return flat_routes * capacity + within


def masked_scores(query_matrix, key_rows, allowed):
    scores = jnp.einsum(
        "qhgd,khd->hgqk", query_matrix, key_rows, preferred_element_type=jnp.float32
    ) * HEAD_SIZE ** (-0.5)
    return jnp.where(allowed[None, None], scores, -1e30)


def local(
    tokens,
    lengths,
    routes,
    prenorm,
    w_query,
    key_value_weight,
    w_output,
    midnorm,
    w_router,
    expert_in,
    expert_out,
    cotangent,
):
    micro_count, token_rows, hidden_width = tokens.shape
    dp_size = lax.axis_size("dp")
    expert_size = lax.axis_size("expert")
    dp_rank = lax.axis_index("dp")
    local_experts = expert_in.shape[0]
    expert_count = local_experts * expert_size
    capacity = max(2, 3 * token_rows * TOP // (2 * expert_count))
    query_group_width = QUERY_HEADS // KEY_VALUE_HEADS
    expert_slot_total = token_rows * dp_size
    score_scale = HEAD_SIZE ** (-0.5)
    positions = dp_rank * token_rows + jnp.arange(token_rows, dtype=jnp.int32)
    key_pos = jnp.arange(expert_slot_total, dtype=jnp.int32)
    cosine_table, sine_table = rope_tables(positions)
    total_prenorm = jnp.zeros((hidden_width,), jnp.float32)
    total_query = jnp.zeros((hidden_width, QUERY_HEADS * HEAD_SIZE), jnp.float32)
    total_key_value = jnp.zeros((hidden_width, 2 * KEY_VALUE_HEADS * HEAD_SIZE), jnp.float32)
    total_output = jnp.zeros((QUERY_HEADS * HEAD_SIZE, hidden_width), jnp.float32)
    total_midnorm = jnp.zeros((hidden_width,), jnp.float32)
    total_router = jnp.zeros((hidden_width, expert_count), jnp.float32)
    total_upper = jnp.zeros((local_experts, hidden_width, 2 * FF), jnp.float32)
    total_down = jnp.zeros((local_experts, FF, hidden_width), jnp.float32)
    outputs_list = []
    grads_list = []
    for micro_step in range(micro_count):
        dense_all = (
            lax.all_gather(prenorm, ("dp", "expert"), axis=0, tiled=True),
            lax.all_gather(w_query, ("dp", "expert"), axis=0, tiled=True),
            lax.all_gather(key_value_weight, ("dp", "expert"), axis=0, tiled=True),
            lax.all_gather(w_output, ("dp", "expert"), axis=0, tiled=True),
            lax.all_gather(midnorm, ("dp", "expert"), axis=0, tiled=True),
            lax.all_gather(w_router, ("dp", "expert"), axis=0, tiled=True),
        )
        expert_all = (
            lax.all_gather(expert_in, "dp", axis=1, tiled=True),
            lax.all_gather(expert_out, "dp", axis=1, tiled=True),
        )
        gain_one = dense_all[0].astype(jnp.float32)
        query_all = dense_all[1]
        keyval_all = dense_all[2]
        output_all = dense_all[3]
        gain_two = dense_all[4].astype(jnp.float32)
        router_all = dense_all[5]
        gateup_all = expert_all[0]
        down_all = expert_all[1]
        input_rows = tokens[micro_step].astype(jnp.float32)
        length = lengths[micro_step]
        route_rows = routes[micro_step]
        live_rows = (positions < length)[:, None]
        normed_one, inverse_one = rms_parts(input_rows)
        normalized_input = (normed_one * gain_one).astype(jnp.bfloat16)
        query_pre = jnp.dot(
            normalized_input, query_all, preferred_element_type=jnp.float32
        ).reshape(token_rows, QUERY_HEADS, HEAD_SIZE)
        keyval_pre = jnp.dot(
            normalized_input, keyval_all, preferred_element_type=jnp.float32
        ).reshape(token_rows, 2, KEY_VALUE_HEADS, HEAD_SIZE)
        query_matrix = (
            apply_rotation(query_pre, cosine_table, sine_table)
            .astype(jnp.bfloat16)
            .reshape(token_rows, KEY_VALUE_HEADS, query_group_width, HEAD_SIZE)
        )
        local_key_rows = apply_rotation(keyval_pre[:, 0], cosine_table, sine_table).astype(
            jnp.bfloat16
        )
        local_value_rows = keyval_pre[:, 1].astype(jnp.bfloat16)
        packed_tokens = jnp.stack([local_key_rows, local_value_rows], axis=1).reshape(
            token_rows, 2 * KEY_VALUE_HEADS * HEAD_SIZE
        )
        gathered_rows = lax.all_gather(packed_tokens, "dp", axis=0, tiled=True).reshape(
            expert_slot_total, 2, KEY_VALUE_HEADS, HEAD_SIZE
        )
        key_rows = gathered_rows[:, 0]
        value_rows = gathered_rows[:, 1]
        allowed = (key_pos[None, :] <= positions[:, None]) & (key_pos[None, :] < length)
        scores = masked_scores(query_matrix, key_rows, allowed)
        top_score = jnp.max(scores, axis=-1, keepdims=True)
        weights = jnp.exp(scores - top_score)
        weight_total = jnp.sum(weights, axis=-1, keepdims=True)
        log_total = top_score + jnp.log(weight_total)
        probs_low = (weights / weight_total).astype(jnp.bfloat16)
        attended = jnp.einsum(
            "hgqk,khd->qhgd", probs_low, value_rows, preferred_element_type=jnp.float32
        )
        attended = attended.reshape(token_rows, QUERY_HEADS * HEAD_SIZE).astype(jnp.bfloat16)
        mixed_rows = input_rows + jnp.dot(attended, output_all, preferred_element_type=jnp.float32)
        normed_mid, inverse_two = rms_parts(mixed_rows)
        normed_two = (normed_mid * gain_two).astype(jnp.bfloat16)
        logits = jnp.dot(normed_two, router_all, preferred_element_type=jnp.float32)
        onehot = (
            route_rows[:, :, None] == jnp.arange(expert_count, dtype=jnp.int32)[None, None, :]
        ).astype(jnp.float32)
        chosen = jnp.sum(onehot * logits[:, None, :], axis=-1)
        gate_values = jax.nn.softmax(chosen, axis=-1)
        slot_idx = slot_index(route_rows, expert_count, capacity)
        send_rows = jnp.zeros((expert_count * capacity, hidden_width), jnp.bfloat16)
        send_rows = send_rows.at[slot_idx].set(jnp.repeat(normed_two, TOP, axis=0))
        received = lax.all_to_all(
            send_rows.reshape(expert_count, capacity, hidden_width),
            "expert",
            split_axis=0,
            concat_axis=0,
            tiled=True,
        )
        item_count = received.shape[1]
        grouped = received.reshape(expert_size, local_experts, item_count, hidden_width)
        gate_up = jnp.einsum(
            "slcd,ldf->slcf", grouped, gateup_all, preferred_element_type=jnp.float32
        )
        hidden = (jax.nn.silu(gate_up[..., :FF]) * gate_up[..., FF:]).astype(jnp.bfloat16)
        result = jnp.einsum(
            "slcf,lfd->slcd", hidden, down_all, preferred_element_type=jnp.float32
        ).astype(jnp.bfloat16)
        back_rows = lax.all_to_all(
            result.reshape(expert_count, item_count, hidden_width),
            "expert",
            split_axis=0,
            concat_axis=0,
            tiled=True,
        )
        back_rows, kept_rows, kept_gateup = (
            back_rows,
            received,
            gate_up.reshape(expert_count, item_count, 2 * FF),
        )
        returned = back_rows.reshape(expert_count * capacity, hidden_width)[slot_idx].reshape(
            token_rows, TOP, hidden_width
        )
        returned_wide = returned.astype(jnp.float32)
        expert_sum = jnp.sum(gate_values[:, :, None] * returned_wide, axis=1)
        final_rows = jnp.where(live_rows, mixed_rows + expert_sum, 0.0)
        outputs_list.append(final_rows.astype(jnp.bfloat16))
        grad_rows = jnp.where(live_rows, cotangent[micro_step].astype(jnp.float32), 0.0)
        grad_gate = jnp.sum(grad_rows[:, None, :] * returned_wide, axis=-1)
        grad_chosen = gate_values * (
            grad_gate - jnp.sum(gate_values * grad_gate, axis=-1, keepdims=True)
        )
        grad_logits = jnp.sum(onehot * grad_chosen[:, :, None], axis=1)
        router_term = jnp.dot(normed_two.astype(jnp.float32).T, grad_logits, precision=highest)
        grad_normtwo = jnp.dot(grad_logits, router_all.astype(jnp.float32).T, precision=highest)
        grad_result = (
            (gate_values[:, :, None] * grad_rows[:, None, :])
            .astype(jnp.bfloat16)
            .reshape(token_rows * TOP, hidden_width)
        )
        send_grads = (
            jnp.zeros((expert_count * capacity, hidden_width), jnp.bfloat16)
            .at[slot_idx]
            .set(grad_result)
        )
        recv_grads, again_rows = (
            lax.all_to_all(
                send_grads.reshape(expert_count, capacity, hidden_width),
                "expert",
                split_axis=0,
                concat_axis=0,
                tiled=True,
            ),
            lax.all_to_all(
                send_rows.reshape(expert_count, capacity, hidden_width),
                "expert",
                split_axis=0,
                concat_axis=0,
                tiled=True,
            ),
        )
        grouped_rows = again_rows.reshape(expert_size, local_experts, capacity, hidden_width)
        gate_up = jnp.einsum(
            "slcd,ldf->slcf", grouped_rows, gateup_all, preferred_element_type=jnp.float32
        )
        grouped_grads = recv_grads.reshape(expert_size, local_experts, capacity, hidden_width)
        gate_part = gate_up[..., :FF]
        up_part = gate_up[..., FF:]
        sigmoid_gate = jax.nn.sigmoid(gate_part)
        silu_gate = gate_part * sigmoid_gate
        hidden = (silu_gate * up_part).astype(jnp.bfloat16)
        grad_hidden = jnp.einsum(
            "slcd,lfd->slcf", grouped_grads, down_all, preferred_element_type=jnp.float32
        )
        down_term = jnp.einsum(
            "slcf,slcd->lfd", hidden, grouped_grads, preferred_element_type=jnp.float32
        )
        grad_gatepart = (
            grad_hidden * up_part * sigmoid_gate * (1.0 + gate_part * (1.0 - sigmoid_gate))
        )
        grad_gateup = jnp.concatenate([grad_gatepart, grad_hidden * silu_gate], axis=-1).astype(
            jnp.bfloat16
        )
        upper_term = jnp.einsum(
            "slcd,slcf->ldf", grouped_rows, grad_gateup, preferred_element_type=jnp.float32
        )
        grad_copies = jnp.einsum(
            "slcf,ldf->slcd", grad_gateup, gateup_all, preferred_element_type=jnp.float32
        ).astype(jnp.bfloat16)
        back_grads = lax.all_to_all(
            grad_copies.reshape(expert_count, capacity, hidden_width),
            "expert",
            split_axis=0,
            concat_axis=0,
            tiled=True,
        )
        copy_rows = back_grads.reshape(expert_count * capacity, hidden_width)[slot_idx].reshape(
            token_rows, TOP, hidden_width
        )
        grad_normtwo = grad_normtwo + jnp.sum(copy_rows.astype(jnp.float32), axis=1)
        midnorm_term = jnp.sum(grad_normtwo * normed_mid, axis=0)
        grad_mixed = grad_rows + norm_back(grad_normtwo, normed_mid, inverse_two, gain_two)
        grad_proj = grad_mixed.astype(jnp.bfloat16)
        output_term = jnp.dot(attended.T, grad_proj, preferred_element_type=jnp.float32)
        attention_gradient = jnp.dot(
            grad_proj, output_all.T, preferred_element_type=jnp.float32
        ).astype(jnp.bfloat16)
        attention_gradient = attention_gradient.reshape(
            token_rows, KEY_VALUE_HEADS, query_group_width, HEAD_SIZE
        )
        scores = masked_scores(query_matrix, key_rows, allowed)
        prob_rows = jnp.exp(scores - log_total)
        grad_probs = jnp.einsum(
            "qhgd,khd->hgqk", attention_gradient, value_rows, preferred_element_type=jnp.float32
        )
        row_delta = jnp.sum(prob_rows * grad_probs, axis=-1, keepdims=True)
        grad_scores = (prob_rows * (grad_probs - row_delta)).astype(jnp.bfloat16)
        prob_low = prob_rows.astype(jnp.bfloat16)
        grad_qrot = (
            jnp.einsum("hgqk,khd->qhgd", grad_scores, key_rows, preferred_element_type=jnp.float32)
            * score_scale
        )
        grad_keys = (
            jnp.einsum(
                "hgqk,qhgd->khd", grad_scores, query_matrix, preferred_element_type=jnp.float32
            )
            * score_scale
        )
        grad_vals = jnp.einsum(
            "hgqk,qhgd->khd", prob_low, attention_gradient, preferred_element_type=jnp.float32
        )
        own_keys = (
            lax.psum_scatter(
                jnp.stack([grad_keys, grad_vals], axis=1)
                .reshape(lax.axis_size("dp") * token_rows, 2 * KEY_VALUE_HEADS * HEAD_SIZE)
                .astype(jnp.bfloat16),
                "dp",
                scatter_dimension=0,
                tiled=True,
            )
            .astype(jnp.float32)
            .reshape(token_rows, 2, KEY_VALUE_HEADS, HEAD_SIZE)
        )
        grad_query = (
            unrotate(
                grad_qrot.reshape(token_rows, QUERY_HEADS, HEAD_SIZE), cosine_table, sine_table
            )
            .astype(jnp.bfloat16)
            .reshape(token_rows, QUERY_HEADS * HEAD_SIZE)
        )
        key_gradient = unrotate(own_keys[:, 0], cosine_table, sine_table).astype(jnp.bfloat16)
        value_gradient = own_keys[:, 1].astype(jnp.bfloat16)
        key_value_weight_gradient = jnp.stack([key_gradient, value_gradient], axis=1).reshape(
            token_rows, 2 * KEY_VALUE_HEADS * HEAD_SIZE
        )
        query_term = jnp.dot(normalized_input.T, grad_query, preferred_element_type=jnp.float32)
        keyval_term = jnp.dot(
            normalized_input.T, key_value_weight_gradient, preferred_element_type=jnp.float32
        )
        grad_normone = jnp.dot(grad_query, query_all.T, preferred_element_type=jnp.float32)
        grad_normone = grad_normone + jnp.dot(
            key_value_weight_gradient, keyval_all.T, preferred_element_type=jnp.float32
        )
        prenorm_term = jnp.sum(grad_normone * normed_one, axis=0)
        grads_list.append(grad_mixed + norm_back(grad_normone, normed_one, inverse_one, gain_one))
        total_prenorm = total_prenorm + prenorm_term
        total_query = total_query + query_term
        total_key_value = total_key_value + keyval_term
        total_output = total_output + output_term
        total_midnorm = total_midnorm + midnorm_term
        total_router = total_router + router_term
        total_upper = total_upper + upper_term
        total_down = total_down + down_term
    dense_grads = (
        lax.psum_scatter(total_prenorm, ("dp", "expert"), scatter_dimension=0, tiled=True),
        lax.psum_scatter(total_query, ("dp", "expert"), scatter_dimension=0, tiled=True),
        lax.psum_scatter(total_key_value, ("dp", "expert"), scatter_dimension=0, tiled=True),
        lax.psum_scatter(total_output, ("dp", "expert"), scatter_dimension=0, tiled=True),
        lax.psum_scatter(total_midnorm, ("dp", "expert"), scatter_dimension=0, tiled=True),
        lax.psum_scatter(total_router, ("dp", "expert"), scatter_dimension=0, tiled=True),
    )
    expert_grads = (
        lax.psum_scatter(
            total_upper.astype(jnp.bfloat16), "dp", scatter_dimension=1, tiled=True
        ).astype(jnp.float32),
        lax.psum_scatter(
            total_down.astype(jnp.bfloat16), "dp", scatter_dimension=1, tiled=True
        ).astype(jnp.float32),
    )
    return (
        jnp.stack(outputs_list),
        jnp.stack(grads_list),
        dense_grads[0],
        dense_grads[1],
        dense_grads[2],
        dense_grads[3],
        dense_grads[4],
        dense_grads[5],
        expert_grads[0],
        expert_grads[1],
    )


MESH = pl.DeviceIdType.MESH
CHUNK = 256
PIECE = 96


def remote(src, dst, send_sem, recv_sem, target):
    return pltpu.make_async_remote_copy(
        src_ref=src,
        dst_ref=dst,
        send_sem=send_sem,
        recv_sem=recv_sem,
        device_id=target,
        device_id_type=MESH,
    )


def place():
    d = lax.axis_index("dp")
    e = lax.axis_index("expert")
    z = lax.div(e, 2)
    c = lax.rem(e, 2)
    x = lax.rem(d, 2)
    y = lax.div(d, 2)
    return d, e, z, c, x, y


def expert_kernel(
    x_hbm,
    g_hbm,
    gt_hbm,
    win_hbm,
    wout_hbm,
    dx_out,
    dgt_out,
    outp_hbm,
    gin_hbm,
    gout_hbm,
    win,
    wout,
    xall,
    gall,
    gtall,
    dgu,
    hg,
    dxb,
    dgb,
    sibr,
    sibg,
    ro,
    rog,
    ri,
    rig,
    stage,
    own_sem,
    stage_sem,
    w_recv,
    w_send,
    ag_recv,
    ag_send,
    sib_recv,
    sib_send,
    red_recv,
    red_send,
):
    d, e, z, c, x, y = place()
    d_x = d + 1 - 2 * x
    d_y = d + 2 - 4 * y
    d_d = 3 - d
    hi = lax.div(z, 2)
    zz = z * hi + (3 - z) * (1 - hi)
    other = 1 - c
    to_x = (d_x, e)
    to_y = (d_y, e)
    to_sib = (d, 2 * z + other)
    to_up = (d, e + jnp.where(z < 3, 2, -2))
    to_down = (d, e + jnp.where(z > 0, -2, 2))
    e_in = e + 2 - 4 * hi
    e_out = e - 2 + 4 * hi
    to_in = (d, e_in)
    to_out = (d, jnp.where(zz == 2, e_out, e_in))
    mid = zz == 2
    end = zz == 3

    barrier = pltpu.get_barrier_semaphore()
    for target in (to_x, to_y, to_sib, to_in):
        pl.semaphore_signal(barrier, inc=1, device_id=target, device_id_type=MESH)

    @pl.when(mid)
    def _():
        pl.semaphore_signal(barrier, inc=1, device_id=to_out, device_id_type=MESH)

    pl.semaphore_wait(barrier, 7 - zz)

    gathered = ((x_hbm, xall), (gt_hbm, gtall))

    def part(a, ref, zp, lane, s):
        if a == 1:
            return ref.at[2 * zp + lane, s]
        return ref.at[pl.ds(pl.multiple_of((2 * zp + lane) * CHUNK + s * 128, 128), 128)]

    def own_part(a, ref, s):
        if a == 1:
            return ref.at[s]
        return ref.at[pl.ds(s * 128, 128)]

    def ag_copy(a, zp, s, way, src=None):
        ref = part(a, gathered[a][1], zp, c, s)
        return remote(
            ref if src is None else src,
            ref,
            ag_send.at[way, a, zp, s],
            ag_recv.at[a, zp, s],
            to_up if way == 0 else to_down,
        )

    def sib_copy(a, zp, s, src=None):
        ref = part(a, gathered[a][1], zp, c, s)
        return remote(
            ref if src is None else src,
            ref,
            sib_send.at[a, zp, s],
            sib_recv.at[a, zp, s],
            to_sib,
        )

    def piece(p, dd):
        if p < 4:
            return win.at[pl.ds(pl.multiple_of(dd * 384 + p * PIECE, 16), PIECE)]
        return wout.at[pl.ds(pl.multiple_of(dd * 192 + (p - 4) * PIECE, 16), PIECE)]

    def own_piece(p):
        if p < 4:
            return win_hbm.at[pl.ds(p * PIECE, PIECE)]
        return wout_hbm.at[pl.ds((p - 4) * PIECE, PIECE)]

    def w_copy(p, way, src_d, target, row, src=None):
        ref = piece(p, src_d)
        return remote(
            ref if src is None else src, ref, w_send.at[row, p], w_recv.at[row, p], target
        )

    for a in range(2):
        for s in range(2):
            src = own_part(a, gathered[a][0], s)

            @pl.when(z < 3)
            def _():
                ag_copy(a, z, s, 0, src).start()

            @pl.when(z > 0)
            def _():
                ag_copy(a, z, s, 1, src).start()

            sib_copy(a, z, s, src).start()
    for p in range(6):
        w_copy(p, 0, d, to_x, 0, own_piece(p)).start()
        w_copy(p, 0, d, to_y, 1, own_piece(p)).start()
    own_copies = [
        pltpu.make_async_copy(
            x_hbm, xall.at[pl.ds(pl.multiple_of(e * CHUNK, 128), CHUNK)], own_sem.at[0]
        ),
        pltpu.make_async_copy(g_hbm, gall, own_sem.at[1]),
        pltpu.make_async_copy(gt_hbm, gtall.at[e], own_sem.at[2]),
        pltpu.make_async_copy(
            win_hbm, win.at[pl.ds(pl.multiple_of(d * 384, 16), 384)], own_sem.at[3]
        ),
        pltpu.make_async_copy(
            wout_hbm, wout.at[pl.ds(pl.multiple_of(d * 192, 16), 192)], own_sem.at[4]
        ),
    ]
    for copy in own_copies:
        copy.start()

    def pass_on(a, k, s):
        @pl.when(z - k >= 0)
        def _():
            ag_copy(a, z - k, s, 0).wait_recv()

            @pl.when(z < 3)
            def _():
                ag_copy(a, z - k, s, 0).start()

            sib_copy(a, z - k, s).start()

        @pl.when(z + k <= 3)
        def _():
            ag_copy(a, z + k, s, 1).wait_recv()

            @pl.when(z > 0)
            def _():
                ag_copy(a, z + k, s, 1).start()

            sib_copy(a, z + k, s).start()

    for p in range(6):
        w_copy(p, 0, d_x, to_x, 0).wait_recv()
        if p % 2 == 0:
            w_copy(p, 0, d_x, to_y, 3).start()
        w_copy(p, 0, d_y, to_y, 1).wait_recv()
        if p % 2 == 1:
            w_copy(p, 0, d_y, to_x, 2).start()
        for a in range(2):
            pass_on(a, 1 + p // 2, p % 2)
    for p in range(6):
        if p % 2 == 0:
            w_copy(p, 0, d_d, to_y, 3).wait_recv()
        else:
            w_copy(p, 0, d_d, to_x, 2).wait_recv()
    for a in range(2):
        for zp in range(4):
            for s in range(2):
                ref = part(a, gathered[a][1], zp, other, s)
                remote(
                    ref, ref, sib_send.at[a, zp, s], sib_recv.at[a, zp, s], to_sib
                ).wait_recv()
    for copy in own_copies:
        copy.wait()

    eye = lax.broadcasted_iota(jnp.int32, (128, 128), 0) == lax.broadcasted_iota(
        jnp.int32, (128, 128), 1
    )
    mine = lax.broadcasted_iota(jnp.int32, (8, 128), 0) == e

    def order(i):
        v = jnp.where(i < 2, i, jnp.where(i == 2, 5 - zz, zz))
        return v * hi + (3 - v) * (1 - hi)

    def out_copy(i, zp):
        return pltpu.make_async_copy(
            stage.at[lax.rem(i, 2)],
            outp_hbm.at[pl.ds(pl.multiple_of(zp * 512, 512), 512)],
            stage_sem.at[lax.rem(i, 2)],
        )

    def lane_rows(i, lane):
        return pl.ds(pl.multiple_of(i * 512 + lane * CHUNK, CHUNK), CHUNK)

    def sib_sum_copies(i):
        return (
            remote(
                dxb.at[lane_rows(i, other)], sibr.at[i], red_send.at[0, i], red_recv.at[0, i], to_sib
            ),
            remote(dgb.at[i, other], sibg.at[i], red_send.at[1, i], red_recv.at[1, i], to_sib),
        )

    def hop_copies(i, target, dst, dstg, row):
        return (
            remote(
                dxb.at[lane_rows(i, c)], dst.at[i], red_send.at[2, i], red_recv.at[row, i], target
            ),
            remote(dgb.at[i, c], dstg.at[i], red_send.at[3, i], red_recv.at[row + 1, i], target),
        )

    def wait_from(ref, refg, slot, row):
        remote(ref.at[slot], ref.at[slot], red_send.at[2, slot], red_recv.at[row, slot], to_in).wait_recv()
        remote(refg.at[slot], refg.at[slot], red_send.at[3, slot], red_recv.at[row + 1, slot], to_in).wait_recv()

    def combine(i, incoming):
        total = dxb[lane_rows(i, c)].astype(jnp.float32) + sibr[i].astype(jnp.float32)
        totalg = dgb[i, c] + sibg[i]
        for ref, refg, slot in incoming:
            total = total + ref[slot].astype(jnp.float32)
            totalg = totalg + refg[slot]
        return total, totalg

    def combine_store(i, incoming):
        total, totalg = combine(i, incoming)
        dxb[lane_rows(i, c)] = total.astype(jnp.bfloat16)
        dgb[i, c] = totalg

    @pl.loop(0, 4)
    def _(i):
        zp = order(i)
        rows = pl.ds(pl.multiple_of(zp * 512, 512), 512)
        xc = xall[rows]
        gate = jnp.dot(xc, win[:, :FF], preferred_element_type=jnp.float32)
        up = jnp.dot(xc, win[:, FF:], preferred_element_type=jnp.float32)
        back = lax.dot_general(
            gall[rows], wout[...], (((1,), (1,)), ((), ())), preferred_element_type=jnp.float32
        )
        columns = []
        for lane in range(2):
            for s in range(2):
                row = jnp.sum(jnp.where(mine, gtall[2 * zp + lane, s], 0.0), axis=0, keepdims=True)
                columns.append(jnp.sum(jnp.where(eye, row, 0.0), axis=1, keepdims=True))
        weight = jnp.concatenate(columns, axis=0)
        sig = jax.nn.sigmoid(gate)
        silu = gate * sig
        hidden = (silu * up).astype(jnp.bfloat16).astype(jnp.float32)
        dgate = jnp.sum(hidden * back, axis=1, keepdims=True)
        for lane in range(2):
            for s in range(2):
                at = (2 * lane + s) * 128
                row = jnp.sum(jnp.where(eye, dgate[at : at + 128], 0.0), axis=0, keepdims=True)
                dgb[i, lane, s] = jnp.where(mine, row, 0.0)
        hg[rows] = (hidden * weight).astype(jnp.bfloat16)
        back = back * weight
        dgu[rows, :FF] = (back * up * (sig * (1.0 + gate * (1.0 - sig)))).astype(jnp.bfloat16)
        dgu[rows, FF:] = (back * silu).astype(jnp.bfloat16)
        dxb[pl.ds(pl.multiple_of(i * 512, 512), 512)] = lax.dot_general(
            dgu[rows], win[...], (((1,), (1,)), ((), ())), preferred_element_type=jnp.float32
        ).astype(jnp.bfloat16)
        for copy in sib_sum_copies(i):
            copy.start()

        @pl.when(i >= 2)
        def _():
            out_copy(i, zp).wait()

        stage[lax.rem(i, 2)] = jnp.dot(
            hg[rows], wout[...], preferred_element_type=jnp.float32
        ).astype(jnp.bfloat16)
        out_copy(i, zp).start()
        for copy in sib_sum_copies(i):
            copy.wait_recv()

        @pl.when(end & (i < 3))
        def _():
            combine_store(i, ())
            for copy in hop_copies(i, to_in, ro, rog, 2):
                copy.start()

        @pl.when(mid & (i == 2))
        def _():
            wait_from(ro, rog, 0, 2)
            combine_store(0, ((ro, rog, 0),))
            for copy in hop_copies(0, to_in, ri, rig, 4):
                copy.start()

    @pl.when(mid)
    def _():
        wait_from(ro, rog, 1, 2)
        combine_store(1, ((ro, rog, 1),))
        for copy in hop_copies(1, to_in, ri, rig, 4):
            copy.start()

    def grad_copy(k, target, at):
        return pltpu.make_async_copy(
            stage.at[k % 2, pl.ds(0, 384)], target.at[pl.ds(at, 384)], stage_sem.at[k % 2]
        )

    blocks = [(gout_hbm, 0), (gout_hbm, 384)] + [(gin_hbm, 384 * k) for k in range(4)]
    for k in range(2):
        out_copy(k, 0).wait()
    for k, (target, at) in enumerate(blocks):
        if k >= 2:
            grad_copy(k - 2, *blocks[k - 2]).wait()
        left = hg if k < 2 else xall
        right = gall if k < 2 else dgu
        stage[k % 2, :384] = lax.dot_general(
            left[:, at : at + 384],
            right[...],
            (((0,), (0,)), ((), ())),
            preferred_element_type=jnp.float32,
        ).astype(jnp.bfloat16)
        grad_copy(k, target, at).start()
        if k == 1:

            @pl.when(mid)
            def _():
                wait_from(ri, rig, 0, 4)
                combine_store(2, ((ri, rig, 0),))
                for copy in hop_copies(2, to_out, ri, rig, 4):
                    copy.start()

    for k in (4, 5):
        grad_copy(k, *blocks[k]).wait()

    @pl.when(mid)
    def _():
        wait_from(ro, rog, 2, 2)
        wait_from(ri, rig, 1, 4)
        total, totalg = combine(3, ((ro, rog, 2), (ri, rig, 1)))
        dx_out[...] = total
        dgt_out[...] = totalg

    @pl.when(end)
    def _():
        wait_from(ri, rig, 2, 4)
        total, totalg = combine(3, ((ri, rig, 2),))
        dx_out[...] = total
        dgt_out[...] = totalg

    for p in range(6):
        w_copy(p, 0, d, to_x, 0, own_piece(p)).wait_send()
        w_copy(p, 0, d, to_y, 1, own_piece(p)).wait_send()
        if p % 2 == 0:
            w_copy(p, 0, d_x, to_y, 3).wait_send()
        else:
            w_copy(p, 0, d_y, to_x, 2).wait_send()
    for a in range(2):
        for s in range(2):
            for zp in range(4):
                sib_copy(a, zp, s).wait_send()

                @pl.when((zp <= z) & (z < 3))
                def _():
                    ag_copy(a, zp, s, 0).wait_send()

                @pl.when((zp >= z) & (z > 0))
                def _():
                    ag_copy(a, zp, s, 1).wait_send()

    for i in range(4):
        for copy in sib_sum_copies(i):
            copy.wait_send()
        if i < 3:
            for copy in hop_copies(i, to_in, ro, rog, 2):
                copy.wait_send()


def expert_stage(rows, grads, gates_t, w_in, w_out):
    bf, f32 = jnp.bfloat16, jnp.float32
    shape = jax.ShapeDtypeStruct
    width = rows.shape[-1]
    hbm = pl.BlockSpec(memory_space=pltpu.HBM)
    vmem = pl.BlockSpec(memory_space=pltpu.VMEM)
    dma = pltpu.SemaphoreType.DMA
    return pl.pallas_call(
        expert_kernel,
        out_shape=(
            shape((CHUNK, width), f32),
            shape((2, 8, 128), f32),
            shape((8 * CHUNK, width), bf),
            shape((width, 2 * FF), bf),
            shape((FF, width), bf),
        ),
        in_specs=[hbm] * 5,
        out_specs=(vmem, vmem, hbm, hbm, hbm),
        scratch_shapes=[
            pltpu.VMEM((width, 2 * FF), bf),
            pltpu.VMEM((FF, width), bf),
            pltpu.VMEM((8 * CHUNK, width), bf),
            pltpu.VMEM((8 * CHUNK, width), bf),
            pltpu.VMEM((8, 2, 8, 128), f32),
            pltpu.VMEM((8 * CHUNK, 2 * FF), bf),
            pltpu.VMEM((8 * CHUNK, FF), bf),
            pltpu.VMEM((8 * CHUNK, width), bf),
            pltpu.VMEM((4, 2, 2, 8, 128), f32),
            pltpu.VMEM((4, CHUNK, width), bf),
            pltpu.VMEM((4, 2, 8, 128), f32),
            pltpu.VMEM((3, CHUNK, width), bf),
            pltpu.VMEM((3, 2, 8, 128), f32),
            pltpu.VMEM((3, CHUNK, width), bf),
            pltpu.VMEM((3, 2, 8, 128), f32),
            pltpu.VMEM((2, 512, width), bf),
            dma((5,)),
            dma((2,)),
            dma((4, 6)),
            dma((4, 6)),
            dma((2, 4, 2)),
            dma((2, 2, 4, 2)),
            dma((2, 4, 2)),
            dma((2, 4, 2)),
            dma((6, 4)),
            dma((4, 4)),
        ],
        compiler_params=pltpu.CompilerParams(
            collective_id=1, has_side_effects=True, vmem_limit_bytes=63 * 2**20
        ),
        name="expert_stage",
    )(rows, grads, gates_t, w_in, w_out)


def attention_kernel(
    tok_ref,
    wa_hbm,
    wb_hbm,
    g_hbm,
    cos_ref,
    sin_ref,
    lens_ref,
    routes_ref,
    wa_out,
    wb_out,
    gall,
    q_out,
    kv_out,
    att_out,
    mixed_out,
    normed_out,
    gates_out,
    wa,
    wb,
    qs,
    kvs,
    att,
    own_sem,
    z_recv,
    z_send,
    xy_recv,
    xy_send,
    sib_recv,
    sib_send,
    g_recv,
    g_send,
    gs_recv,
    gs_send,
    kv_recv,
    kv_send,
):
    bf, f32 = jnp.bfloat16, jnp.float32
    d, e, z, c, x, y = place()
    d_x = d + 1 - 2 * x
    d_y = d + 2 - 4 * y
    d_d = 3 - d
    other = 1 - c
    to_x = (d_x, e)
    to_y = (d_y, e)
    to_sib = (d, 2 * z + other)
    to_up = (d, e + jnp.where(z < 3, 2, -2))
    to_down = (d, e + jnp.where(z > 0, -2, 2))

    barrier = pltpu.get_barrier_semaphore()
    for target in (to_x, to_y, to_sib):
        pl.semaphore_signal(barrier, inc=1, device_id=target, device_id_type=MESH)

    @pl.when(z < 3)
    def _():
        pl.semaphore_signal(barrier, inc=1, device_id=to_up, device_id_type=MESH)

    @pl.when(z > 0)
    def _():
        pl.semaphore_signal(barrier, inc=1, device_id=to_down, device_id_type=MESH)

    pl.semaphore_wait(barrier, 5 - jnp.where((z == 0) | (z == 3), 1, 0))

    full = (wa, wb)
    shard = (wa_hbm, wb_hbm)

    def block(a, dd, zp, lane):
        at = pl.multiple_of((dd * 8 + 2 * zp + lane) * 48, 16)
        return full[a].at[pl.ds(at, 48)]

    def z_copy(a, zp, way, src=None):
        ref = block(a, d, zp, c)
        return remote(
            ref if src is None else src,
            ref,
            z_send.at[a, way, zp],
            z_recv.at[a, zp],
            to_up if way == 0 else to_down,
        )

    def xy_copy(a, dd, zp, row, target, src=None):
        ref = block(a, dd, zp, c)
        return remote(
            ref if src is None else src,
            ref,
            xy_send.at[a, row, zp],
            xy_recv.at[a, row, zp],
            target,
        )

    def s_copy(a, dd, zp, src=None, lane=None):
        ref = block(a, dd, zp, c if lane is None else lane)
        return remote(
            ref if src is None else src,
            ref,
            sib_send.at[a, dd, zp],
            sib_recv.at[a, dd, zp],
            to_sib,
        )

    def have(a, zp, src=None):
        xy_copy(a, d, zp, 0, to_x, src).start()
        xy_copy(a, d, zp, 1, to_y, src).start()
        s_copy(a, d, zp, src).start()

    def own_start(a):
        @pl.when(z < 3)
        def _():
            z_copy(a, z, 0, shard[a]).start()

        @pl.when(z > 0)
        def _():
            z_copy(a, z, 1, shard[a]).start()

        have(a, z, shard[a])

    def from_z(a, k):
        @pl.when(z - k >= 0)
        def _():
            z_copy(a, z - k, 0).wait_recv()

            @pl.when(z < 3)
            def _():
                z_copy(a, z - k, 0).start()

            have(a, z - k)

        @pl.when(z + k <= 3)
        def _():
            z_copy(a, z + k, 1).wait_recv()

            @pl.when(z > 0)
            def _():
                z_copy(a, z + k, 1).start()

            have(a, z + k)

    def from_xy_one(a, zp):
        xy_copy(a, d_x, zp, 0, to_x).wait_recv()

        @pl.when(lax.rem(zp, 2) == 0)
        def _():
            xy_copy(a, d_x, zp, 2, to_y).start()

        s_copy(a, d_x, zp).start()
        xy_copy(a, d_y, zp, 1, to_y).wait_recv()

        @pl.when(lax.rem(zp, 2) == 1)
        def _():
            xy_copy(a, d_y, zp, 2, to_x).start()

        s_copy(a, d_y, zp).start()

    def from_xy(a, k):
        @pl.when(z - k >= 0)
        def _():
            from_xy_one(a, z - k)

        if k > 0:

            @pl.when(z + k <= 3)
            def _():
                from_xy_one(a, z + k)

    def from_diag(a):
        for k in range(4):
            zp = lax.rem(z + k, 4)
            xy_copy(a, d_d, zp, 2, to_x).wait_recv()
            s_copy(a, d_d, zp).start()

    def from_sib(a):
        for dd in range(4):
            for zp in range(4):
                s_copy(a, dd, zp, lane=other).wait_recv()

    def drain(a):
        for zp in range(4):
            for dd in range(4):
                s_copy(a, dd, zp).wait_send()
            for row in range(3):
                xy_copy(a, d, zp, row, to_x).wait_send()

            @pl.when((zp <= z) & (z < 3))
            def _():
                z_copy(a, zp, 0).wait_send()

            @pl.when((zp >= z) & (z > 0))
            def _():
                z_copy(a, zp, 1).wait_send()

    def g_part(zp, lane, s):
        at = pl.multiple_of((2 * zp + lane) * CHUNK + s * 128, 128)
        return gall.at[pl.ds(at, 128)]

    def g_copy(zp, s, way, src=None):
        ref = g_part(zp, c, s)
        return remote(
            ref if src is None else src,
            ref,
            g_send.at[way, zp, s],
            g_recv.at[zp, s],
            to_up if way == 0 else to_down,
        )

    def gs_copy(zp, s, src=None, lane=None):
        ref = g_part(zp, c if lane is None else lane, s)
        return remote(
            ref if src is None else src, ref, gs_send.at[zp, s], gs_recv.at[zp, s], to_sib
        )

    def g_start():
        for s in range(2):
            src = g_hbm.at[pl.ds(s * 128, 128)]

            @pl.when(z < 3)
            def _():
                g_copy(z, s, 0, src).start()

            @pl.when(z > 0)
            def _():
                g_copy(z, s, 1, src).start()

            gs_copy(z, s, src).start()

    def g_pass(k, s):
        @pl.when(z - k >= 0)
        def _():
            g_copy(z - k, s, 0).wait_recv()

            @pl.when(z < 3)
            def _():
                g_copy(z - k, s, 0).start()

            gs_copy(z - k, s).start()

        @pl.when(z + k <= 3)
        def _():
            g_copy(z + k, s, 1).wait_recv()

            @pl.when(z > 0)
            def _():
                g_copy(z + k, s, 1).start()

            gs_copy(z + k, s).start()

    own = [
        pltpu.make_async_copy(shard[a], block(a, d, z, c), own_sem.at[a]) for a in range(2)
    ] + [
        pltpu.make_async_copy(
            g_hbm, gall.at[pl.ds(pl.multiple_of(e * CHUNK, CHUNK), CHUNK)], own_sem.at[2]
        )
    ]
    own_start(0)
    own_start(1)
    for copy in own:
        copy.start()
    g_start()
    tok = tok_ref[...].astype(f32)
    n1 = tok * lax.rsqrt(jnp.mean(tok * tok, axis=1, keepdims=True) + epsilon)
    for k in range(1, 4):
        from_z(0, k)
        from_xy(0, k - 1)
        from_z(1, k)
    from_xy(0, 3)
    from_diag(0)
    own[0].wait()
    from_sib(0)

    small = wa[:, 2048:]
    eye = (
        lax.broadcasted_iota(jnp.int32, (128, 128), 0)
        == lax.broadcasted_iota(jnp.int32, (128, 128), 1)
    ).astype(bf)
    small_t = lax.dot_general(eye, small, (((1,), (1,)), ((), ())), preferred_element_type=f32)
    normed = (n1 * small_t[8:9]).astype(bf)
    cos_rows = jnp.concatenate([cos_ref[...]] * 2, axis=0)
    sin_rows = jnp.concatenate([sin_ref[...]] * 2, axis=0)

    def rotate(v):
        return v * cos_rows + pltpu.roll(v, 64, 1) * sin_rows

    kv = jnp.dot(normed, wa[:, 1536:2048], preferred_element_type=f32)
    for h in range(2):
        kvs[d, :, h * 128 : (h + 1) * 128] = rotate(kv[:, h * 128 : (h + 1) * 128]).astype(bf)
    kvs[d, :, 256:] = kv[:, 256:].astype(bf)

    def kv_copy(dd, s, row, target):
        ref = kvs.at[dd, pl.ds(s * 128, 128)]
        return remote(ref, ref, kv_send.at[row, s], kv_recv.at[row, s], target)

    for s in range(2):
        kv_copy(d, s, 0, to_x).start()
        kv_copy(d, s, 1, to_y).start()
    from_xy(1, 0)
    q = jnp.dot(normed, wa[:, :1536], preferred_element_type=f32)
    for head in range(QUERY_HEADS):
        rot = rotate(q[:, head * 128 : (head + 1) * 128]).astype(bf)
        for s in range(2):
            at = (s * QUERY_HEADS + head) * 128
            qs[at : at + 128] = rot[s * 128 : (s + 1) * 128]
    g_pass(1, 0)
    kv_copy(d_x, 0, 0, to_x).wait_recv()
    kv_copy(d_x, 0, 2, to_y).start()
    kv_copy(d_y, 1, 1, to_y).wait_recv()
    kv_copy(d_y, 1, 2, to_x).start()
    kv_copy(d_y, 0, 1, to_y).wait_recv()
    kv_copy(d_x, 1, 0, to_x).wait_recv()
    for k in range(1, 4):
        from_xy(1, k)
    g_pass(1, 1)
    for s in range(2):
        kv_copy(d_d, s, 2, to_x).wait_recv()
    q_copy = pltpu.make_async_copy(qs, q_out, own_sem.at[3])
    kvo_copy = pltpu.make_async_copy(kvs, kv_out, own_sem.at[4])
    wa_copy = pltpu.make_async_copy(wa, wa_out, own_sem.at[5])
    for copy in (q_copy, kvo_copy, wa_copy):
        copy.start()

    query_pos = d * 128 + lax.broadcasted_iota(jnp.int32, (128, 512), 0)
    key_pos = lax.broadcasted_iota(jnp.int32, (128, 512), 1)

    @pl.loop(0, 4)
    def _(n):
        s = lax.div(n, 2)
        h = lax.rem(n, 2)
        lens = lens_ref[s][0:1, 0:1]
        allowed = (key_pos <= query_pos) & (key_pos < lens)
        ks = kvs[:, pl.ds(pl.multiple_of(s * 128, 128), 128), pl.ds(pl.multiple_of(h * 128, 128), 128)]
        vs = kvs[:, pl.ds(pl.multiple_of(s * 128, 128), 128), pl.ds(pl.multiple_of(256 + h * 128, 128), 128)]
        ks = ks.reshape(512, 128)
        vs = vs.reshape(512, 128)
        for half in range(2):
            qh = qs[pl.ds(pl.multiple_of(n * 768 + half * 384, 128), 384)]
            scores = lax.dot_general(qh, ks, (((1,), (1,)), ((), ())), preferred_element_type=f32)
            scores = scores.reshape(3, 128, 512) * HEAD_SIZE ** (-0.5)
            scores = jnp.where(allowed[None], scores, -1e30)
            top = jnp.max(scores, axis=-1, keepdims=True)
            weights = jnp.exp(scores - top)
            weights = weights * (1.0 / jnp.sum(weights, axis=-1, keepdims=True))
            out = jnp.dot(
                weights.astype(bf).reshape(384, 512), vs, preferred_element_type=f32
            ).astype(bf)
            for j in range(3):
                att[
                    pl.ds(pl.multiple_of(s * 128, 128), 128),
                    pl.ds(pl.multiple_of(h * 768 + (half * 3 + j) * 128, 128), 128),
                ] = out[j * 128 : (j + 1) * 128]

    g_pass(2, 0)
    from_diag(1)
    own[1].wait()
    from_sib(1)
    att_copy = pltpu.make_async_copy(att, att_out, own_sem.at[6])
    wb_copy = pltpu.make_async_copy(wb, wb_out, own_sem.at[7])
    att_copy.start()
    wb_copy.start()
    mixed = tok_ref[...].astype(f32) + jnp.dot(att[...], wb[...], preferred_element_type=f32)
    mixed_out[...] = mixed
    n2 = mixed * lax.rsqrt(jnp.mean(mixed * mixed, axis=1, keepdims=True) + epsilon)
    normed2 = (n2 * small_t[9:10]).astype(bf)
    normed_out[...] = normed2
    logits = jnp.dot(normed2, small, preferred_element_type=f32)
    lanes = lax.broadcasted_iota(jnp.int32, (CHUNK, 128), 1)
    chosen = lanes == routes_ref[:, 0:1]
    for t in range(1, TOP):
        chosen = chosen | (lanes == routes_ref[:, t : t + 1])
    logits = jnp.where(chosen, logits, -1e30)
    weights = jnp.where(chosen, jnp.exp(logits - jnp.max(logits, axis=1, keepdims=True)), 0.0)
    gates_out[...] = weights / jnp.sum(weights, axis=1, keepdims=True)

    g_pass(2, 1)
    g_pass(3, 0)
    g_pass(3, 1)
    for zp in range(4):
        for s in range(2):
            gs_copy(zp, s, lane=other).wait_recv()
    own[2].wait()
    for copy in (q_copy, kvo_copy, wa_copy, att_copy, wb_copy):
        copy.wait()
    drain(0)
    drain(1)
    for s in range(2):
        for row in range(3):
            kv_copy(d, s, row, to_x).wait_send()
        for zp in range(4):
            gs_copy(zp, s).wait_send()

            @pl.when((zp <= z) & (z < 3))
            def _():
                g_copy(zp, s, 0).wait_send()

            @pl.when((zp >= z) & (z > 0))
            def _():
                g_copy(zp, s, 1).wait_send()


def attention_stage(rows, w_a, w_b, grads, cos_rows, sin_rows, lens, routes):
    bf, f32 = jnp.bfloat16, jnp.float32
    shape = jax.ShapeDtypeStruct
    width = rows.shape[-1]
    wide = w_a.shape[-1]
    hbm = pl.BlockSpec(memory_space=pltpu.HBM)
    vmem = pl.BlockSpec(memory_space=pltpu.VMEM)
    dma = pltpu.SemaphoreType.DMA
    return pl.pallas_call(
        attention_kernel,
        out_shape=(
            shape((width, wide), bf),
            shape((width, width), bf),
            shape((8 * CHUNK, width), bf),
            shape((2 * QUERY_HEADS * 128, 128), bf),
            shape((4, CHUNK, 512), bf),
            shape((CHUNK, width), bf),
            shape((CHUNK, width), f32),
            shape((CHUNK, width), bf),
            shape((CHUNK, 128), f32),
        ),
        in_specs=[vmem, hbm, hbm, hbm, vmem, vmem, vmem, vmem],
        out_specs=(hbm, hbm, hbm, hbm, hbm, hbm, vmem, vmem, vmem),
        scratch_shapes=[
            pltpu.VMEM((width, wide), bf),
            pltpu.VMEM((width, width), bf),
            pltpu.VMEM((2 * QUERY_HEADS * 128, 128), bf),
            pltpu.VMEM((4, CHUNK, 512), bf),
            pltpu.VMEM((CHUNK, width), bf),
            dma((8,)),
            dma((2, 4)),
            dma((2, 2, 4)),
            dma((2, 3, 4)),
            dma((2, 3, 4)),
            dma((2, 4, 4)),
            dma((2, 4, 4)),
            dma((4, 2)),
            dma((2, 4, 2)),
            dma((4, 2)),
            dma((4, 2)),
            dma((3, 2)),
            dma((3, 2)),
        ],
        compiler_params=pltpu.CompilerParams(
            collective_id=2, has_side_effects=True, vmem_limit_bytes=60 * 2**20
        ),
        name="attention_stage",
    )(rows, w_a, w_b, grads, cos_rows, sin_rows, lens, routes)


def fast_local(
    tokens,
    lengths,
    routes,
    prenorm,
    w_query,
    key_value_weight,
    w_output,
    midnorm,
    w_router,
    expert_in,
    expert_out,
    cotangent,
):
    bf, f32 = jnp.bfloat16, jnp.float32
    seqs, token_rows, width = tokens.shape
    dp_size = lax.axis_size("dp")
    dp_rank = lax.axis_index("dp")
    expert_count = lax.axis_size("expert")
    group = QUERY_HEADS // KEY_VALUE_HEADS
    slots = token_rows * dp_size
    rows = seqs * token_rows
    scale = HEAD_SIZE ** (-0.5)
    both = ("dp", "expert")
    small = jnp.concatenate(
        [w_router, prenorm[:, None], midnorm[:, None], jnp.zeros((w_router.shape[0], 118), bf)], axis=1
    )
    shard_a = jnp.concatenate([w_query, key_value_weight, small], axis=1)
    positions = dp_rank * token_rows + jnp.arange(token_rows, dtype=jnp.int32)
    key_pos = jnp.arange(slots, dtype=jnp.int32)
    cosine_table, sine_table = rope_tables(positions)
    cos_rows = jnp.concatenate([cosine_table, cosine_table], axis=1)
    sin_rows = jnp.concatenate([-sine_table, sine_table], axis=1)
    live = (positions[None, :] < lengths[:, None]).reshape(rows, 1)
    x = tokens.reshape(rows, width)
    g = jnp.where(live, cotangent.reshape(rows, width), 0)
    lens = jnp.broadcast_to(lengths[:, None, None], (seqs, 8, 128))
    full_a, output_all, gall, q_rot, kv_all, attended, mixed, normed2, gates = attention_stage(
        x, shard_a, w_output, g, cos_rows, sin_rows, lens, routes.reshape(rows, TOP)
    )
    gates_t = jnp.transpose(gates[:, :8].reshape(seqs, token_rows, 8), (0, 2, 1))
    dx, dgate_t, outp, gin, gout = expert_stage(
        normed2, gall, gates_t, expert_in[0], expert_out[0]
    )
    gates = gates[:, :8]

    query_all = full_a[:, :1536]
    keyval_all = full_a[:, 1536:2048]
    router_all = full_a[:, 2048:2056]
    gain_one = full_a[:, 2056].astype(f32)
    gain_two = full_a[:, 2057].astype(f32)
    x = x.astype(f32)
    n1, inv1 = rms_parts(x)
    normed = (n1 * gain_one).astype(bf)
    n2, inv2 = rms_parts(mixed)
    q_rot = q_rot.reshape(seqs, KEY_VALUE_HEADS, group, token_rows, HEAD_SIZE)
    kv_all = kv_all.reshape(4, seqs, token_rows, 512).transpose(1, 0, 2, 3)
    kv_all = kv_all.reshape(seqs, slots, 2, KEY_VALUE_HEADS, HEAD_SIZE)
    keys, values = kv_all[:, :, 0], kv_all[:, :, 1]
    allowed = (key_pos[None, None, :] <= positions[None, :, None]) & (
        key_pos[None, None, :] < lengths[:, None, None]
    )
    cosine_table = jnp.tile(cosine_table, (seqs, 1))
    sine_table = jnp.tile(sine_table, (seqs, 1))
    scores = jnp.einsum("shgqd,skhd->shgqk", q_rot, keys, preferred_element_type=f32) * scale
    scores = jnp.where(allowed[:, None, None], scores, -1e30)

    expert_sum = lax.psum_scatter(outp, "expert", scatter_dimension=0, tiled=True).astype(f32)
    block_out = jnp.where(live, mixed + expert_sum, 0.0).astype(bf)
    gf = g.astype(f32)
    dgate = jnp.transpose(dgate_t, (0, 2, 1)).reshape(rows, expert_count)
    dlogit = gates * (dgate - jnp.sum(gates * dgate, axis=-1, keepdims=True))
    g_router = jnp.dot(normed2.astype(f32).T, dlogit, precision=highest)
    dn2 = dx + jnp.dot(dlogit, router_all.astype(f32).T, precision=highest)
    g_mid = jnp.sum(dn2 * n2, axis=0)
    dmixed = gf + norm_back(dn2, n2, inv2, gain_two)
    dproj = dmixed.astype(bf)
    g_out = jnp.dot(attended.T, dproj, preferred_element_type=f32)
    datt = jnp.dot(dproj, output_all.T, preferred_element_type=f32).astype(bf)
    datt = datt.reshape(seqs, token_rows, KEY_VALUE_HEADS, group, HEAD_SIZE)
    probs = jax.nn.softmax(scores, axis=-1)
    dprobs = jnp.einsum("sqhgd,skhd->shgqk", datt, values, preferred_element_type=f32)
    delta = jnp.sum(probs * dprobs, axis=-1, keepdims=True)
    dscores = (probs * (dprobs - delta)).astype(bf)
    dq_rot = jnp.einsum("shgqk,skhd->sqhgd", dscores, keys, preferred_element_type=f32) * scale
    dk = jnp.einsum("shgqk,shgqd->skhd", dscores, q_rot, preferred_element_type=f32) * scale
    dv = jnp.einsum("shgqk,sqhgd->skhd", probs.astype(bf), datt, preferred_element_type=f32)
    dkv = jnp.stack([dk, dv], axis=2).reshape(seqs, slots, 512).astype(bf)
    own = lax.psum_scatter(dkv, "dp", scatter_dimension=1, tiled=True).astype(f32)
    own = own.reshape(rows, 2, KEY_VALUE_HEADS, HEAD_SIZE)
    dq = unrotate(dq_rot.reshape(rows, QUERY_HEADS, HEAD_SIZE), cosine_table, sine_table)
    dq = dq.astype(bf).reshape(rows, QUERY_HEADS * HEAD_SIZE)
    dk_own = unrotate(own[:, 0], cosine_table, sine_table).astype(bf)
    dkv_own = jnp.stack([dk_own, own[:, 1].astype(bf)], axis=1).reshape(rows, 512)
    g_query = jnp.dot(normed.T, dq, preferred_element_type=f32)
    g_kv = jnp.dot(normed.T, dkv_own, preferred_element_type=f32)
    dn1 = jnp.dot(dq, query_all.T, preferred_element_type=f32)
    dn1 = dn1 + jnp.dot(dkv_own, keyval_all.T, preferred_element_type=f32)
    g_pre = jnp.sum(dn1 * n1, axis=0)
    grad_tokens = dmixed + norm_back(dn1, n1, inv1, gain_one)
    dense = jnp.concatenate(
        [g_query, g_kv, g_out, g_router, g_pre[:, None], g_mid[:, None]], axis=1
    ).astype(bf)
    dense = lax.psum_scatter(dense, both, scatter_dimension=0, tiled=True).astype(f32)
    upper = lax.psum_scatter(gin, "dp", scatter_dimension=0, tiled=True).astype(f32)
    down = lax.psum_scatter(gout, "dp", scatter_dimension=0, tiled=True).astype(f32)
    return (
        block_out.reshape(seqs, token_rows, width),
        grad_tokens.reshape(seqs, token_rows, width),
        dense[:, 3592],
        dense[:, :1536],
        dense[:, 1536:2048],
        dense[:, 2048:3584],
        dense[:, 3593],
        dense[:, 3584:3592],
        upper[None],
        down[None],
    )


def solution(mesh):
    placed = (
        P("expert", "dp", None),
        P("expert"),
        P("expert", "dp", None),
        P(("dp", "expert")),
        P(("dp", "expert"), None),
        P(("dp", "expert"), None),
        P(("dp", "expert"), None),
        P(("dp", "expert")),
        P(("dp", "expert"), None),
        P("expert", "dp", None),
        P("expert", "dp", None),
        P("expert", "dp", None),
    )
    fits = mesh.shape["dp"] == 4 and mesh.shape["expert"] == 8
    return jax.shard_map(
        fast_local if fits else local,
        mesh=mesh,
        in_specs=placed,
        out_specs=(
            P("expert", "dp", None),
            P("expert", "dp", None),
            P(("dp", "expert")),
            P(("dp", "expert"), None),
            P(("dp", "expert"), None),
            P(("dp", "expert"), None),
            P(("dp", "expert")),
            P(("dp", "expert"), None),
            P("expert", "dp", None),
            P("expert", "dp", None),
        ),
        check_vma=False,
    )
```

```python
import jax
import jax.numpy as jnp
from jax import lax
from jax.experimental import pallas as pl
from jax.experimental.pallas import tpu as pltpu
from jax.sharding import PartitionSpec as P

QUERY_HEADS = 12
KEY_VALUE_HEADS = 2
HEAD_SIZE = 128
FF = 768
TOP = 4


epsilon = 1e-06
rope_base = 10000.0
highest = lax.Precision.HIGHEST


def rope_tables(positions):
    half_width = HEAD_SIZE // 2
    inv_freq = rope_base ** (-(jnp.arange(half_width, dtype=jnp.float32) * 2.0 / HEAD_SIZE))
    angles = positions.astype(jnp.float32)[:, None] * inv_freq[None, :]
    return (jnp.cos(angles), jnp.sin(angles))


def apply_rotation(values, cosine_table, sine_table):
    half_width = values.shape[-1] // 2
    first_half = values[..., :half_width]
    second = values[..., half_width:]
    cos_rows = cosine_table[:, None, :]
    sin_rows = sine_table[:, None, :]
    return jnp.concatenate(
        [first_half * cos_rows - second * sin_rows, second * cos_rows + first_half * sin_rows],
        axis=-1,
    )


def unrotate(values, cosine_table, sine_table):
    half_width = values.shape[-1] // 2
    first_half = values[..., :half_width]
    second = values[..., half_width:]
    cos_rows = cosine_table[:, None, :]
    sin_rows = sine_table[:, None, :]
    return jnp.concatenate(
        [first_half * cos_rows + second * sin_rows, second * cos_rows - first_half * sin_rows],
        axis=-1,
    )


def rms_parts(values):
    inverse = lax.rsqrt(jnp.mean(values * values, axis=-1, keepdims=True) + epsilon)
    return (values * inverse, inverse)


def norm_back(grad_normed, normalized_input, inverse, gain):
    scaled = grad_normed * gain
    return inverse * (
        scaled - normalized_input * jnp.mean(scaled * normalized_input, axis=-1, keepdims=True)
    )


def slot_index(route_rows, expert_count, capacity):
    flat_routes = route_rows.reshape(-1)
    onehot = (flat_routes[:, None] == jnp.arange(expert_count, dtype=jnp.int32)[None, :]).astype(
        jnp.int32
    )
    before = jnp.cumsum(onehot, axis=0) - onehot
    within = jnp.sum(before * onehot, axis=-1)
    return flat_routes * capacity + within


def masked_scores(query_matrix, key_rows, allowed):
    scores = jnp.einsum(
        "qhgd,khd->hgqk", query_matrix, key_rows, preferred_element_type=jnp.float32
    ) * HEAD_SIZE ** (-0.5)
    return jnp.where(allowed[None, None], scores, -1e30)


def local(
    tokens,
    lengths,
    routes,
    prenorm,
    w_query,
    key_value_weight,
    w_output,
    midnorm,
    w_router,
    expert_in,
    expert_out,
    cotangent,
):
    micro_count, token_rows, hidden_width = tokens.shape
    dp_size = lax.axis_size("dp")
    expert_size = lax.axis_size("expert")
    dp_rank = lax.axis_index("dp")
    local_experts = expert_in.shape[0]
    expert_count = local_experts * expert_size
    capacity = max(2, 3 * token_rows * TOP // (2 * expert_count))
    query_group_width = QUERY_HEADS // KEY_VALUE_HEADS
    expert_slot_total = token_rows * dp_size
    score_scale = HEAD_SIZE ** (-0.5)
    positions = dp_rank * token_rows + jnp.arange(token_rows, dtype=jnp.int32)
    key_pos = jnp.arange(expert_slot_total, dtype=jnp.int32)
    cosine_table, sine_table = rope_tables(positions)
    total_prenorm = jnp.zeros((hidden_width,), jnp.float32)
    total_query = jnp.zeros((hidden_width, QUERY_HEADS * HEAD_SIZE), jnp.float32)
    total_key_value = jnp.zeros((hidden_width, 2 * KEY_VALUE_HEADS * HEAD_SIZE), jnp.float32)
    total_output = jnp.zeros((QUERY_HEADS * HEAD_SIZE, hidden_width), jnp.float32)
    total_midnorm = jnp.zeros((hidden_width,), jnp.float32)
    total_router = jnp.zeros((hidden_width, expert_count), jnp.float32)
    total_upper = jnp.zeros((local_experts, hidden_width, 2 * FF), jnp.float32)
    total_down = jnp.zeros((local_experts, FF, hidden_width), jnp.float32)
    outputs_list = []
    grads_list = []
    for micro_step in range(micro_count):
        dense_all = (
            lax.all_gather(prenorm, ("dp", "expert"), axis=0, tiled=True),
            lax.all_gather(w_query, ("dp", "expert"), axis=0, tiled=True),
            lax.all_gather(key_value_weight, ("dp", "expert"), axis=0, tiled=True),
            lax.all_gather(w_output, ("dp", "expert"), axis=0, tiled=True),
            lax.all_gather(midnorm, ("dp", "expert"), axis=0, tiled=True),
            lax.all_gather(w_router, ("dp", "expert"), axis=0, tiled=True),
        )
        expert_all = (
            lax.all_gather(expert_in, "dp", axis=1, tiled=True),
            lax.all_gather(expert_out, "dp", axis=1, tiled=True),
        )
        gain_one = dense_all[0].astype(jnp.float32)
        query_all = dense_all[1]
        keyval_all = dense_all[2]
        output_all = dense_all[3]
        gain_two = dense_all[4].astype(jnp.float32)
        router_all = dense_all[5]
        gateup_all = expert_all[0]
        down_all = expert_all[1]
        input_rows = tokens[micro_step].astype(jnp.float32)
        length = lengths[micro_step]
        route_rows = routes[micro_step]
        live_rows = (positions < length)[:, None]
        normed_one, inverse_one = rms_parts(input_rows)
        normalized_input = (normed_one * gain_one).astype(jnp.bfloat16)
        query_pre = jnp.dot(
            normalized_input, query_all, preferred_element_type=jnp.float32
        ).reshape(token_rows, QUERY_HEADS, HEAD_SIZE)
        keyval_pre = jnp.dot(
            normalized_input, keyval_all, preferred_element_type=jnp.float32
        ).reshape(token_rows, 2, KEY_VALUE_HEADS, HEAD_SIZE)
        query_matrix = (
            apply_rotation(query_pre, cosine_table, sine_table)
            .astype(jnp.bfloat16)
            .reshape(token_rows, KEY_VALUE_HEADS, query_group_width, HEAD_SIZE)
        )
        local_key_rows = apply_rotation(keyval_pre[:, 0], cosine_table, sine_table).astype(
            jnp.bfloat16
        )
        local_value_rows = keyval_pre[:, 1].astype(jnp.bfloat16)
        packed_tokens = jnp.stack([local_key_rows, local_value_rows], axis=1).reshape(
            token_rows, 2 * KEY_VALUE_HEADS * HEAD_SIZE
        )
        gathered_rows = lax.all_gather(packed_tokens, "dp", axis=0, tiled=True).reshape(
            expert_slot_total, 2, KEY_VALUE_HEADS, HEAD_SIZE
        )
        key_rows = gathered_rows[:, 0]
        value_rows = gathered_rows[:, 1]
        allowed = (key_pos[None, :] <= positions[:, None]) & (key_pos[None, :] < length)
        scores = masked_scores(query_matrix, key_rows, allowed)
        top_score = jnp.max(scores, axis=-1, keepdims=True)
        weights = jnp.exp(scores - top_score)
        weight_total = jnp.sum(weights, axis=-1, keepdims=True)
        log_total = top_score + jnp.log(weight_total)
        probs_low = (weights / weight_total).astype(jnp.bfloat16)
        attended = jnp.einsum(
            "hgqk,khd->qhgd", probs_low, value_rows, preferred_element_type=jnp.float32
        )
        attended = attended.reshape(token_rows, QUERY_HEADS * HEAD_SIZE).astype(jnp.bfloat16)
        mixed_rows = input_rows + jnp.dot(attended, output_all, preferred_element_type=jnp.float32)
        normed_mid, inverse_two = rms_parts(mixed_rows)
        normed_two = (normed_mid * gain_two).astype(jnp.bfloat16)
        logits = jnp.dot(normed_two, router_all, preferred_element_type=jnp.float32)
        onehot = (
            route_rows[:, :, None] == jnp.arange(expert_count, dtype=jnp.int32)[None, None, :]
        ).astype(jnp.float32)
        chosen = jnp.sum(onehot * logits[:, None, :], axis=-1)
        gate_values = jax.nn.softmax(chosen, axis=-1)
        slot_idx = slot_index(route_rows, expert_count, capacity)
        send_rows = jnp.zeros((expert_count * capacity, hidden_width), jnp.bfloat16)
        send_rows = send_rows.at[slot_idx].set(jnp.repeat(normed_two, TOP, axis=0))
        received = lax.all_to_all(
            send_rows.reshape(expert_count, capacity, hidden_width),
            "expert",
            split_axis=0,
            concat_axis=0,
            tiled=True,
        )
        item_count = received.shape[1]
        grouped = received.reshape(expert_size, local_experts, item_count, hidden_width)
        gate_up = jnp.einsum(
            "slcd,ldf->slcf", grouped, gateup_all, preferred_element_type=jnp.float32
        )
        hidden = (jax.nn.silu(gate_up[..., :FF]) * gate_up[..., FF:]).astype(jnp.bfloat16)
        result = jnp.einsum(
            "slcf,lfd->slcd", hidden, down_all, preferred_element_type=jnp.float32
        ).astype(jnp.bfloat16)
        back_rows = lax.all_to_all(
            result.reshape(expert_count, item_count, hidden_width),
            "expert",
            split_axis=0,
            concat_axis=0,
            tiled=True,
        )
        back_rows, kept_rows, kept_gateup = (
            back_rows,
            received,
            gate_up.reshape(expert_count, item_count, 2 * FF),
        )
        returned = back_rows.reshape(expert_count * capacity, hidden_width)[slot_idx].reshape(
            token_rows, TOP, hidden_width
        )
        returned_wide = returned.astype(jnp.float32)
        expert_sum = jnp.sum(gate_values[:, :, None] * returned_wide, axis=1)
        final_rows = jnp.where(live_rows, mixed_rows + expert_sum, 0.0)
        outputs_list.append(final_rows.astype(jnp.bfloat16))
        grad_rows = jnp.where(live_rows, cotangent[micro_step].astype(jnp.float32), 0.0)
        grad_gate = jnp.sum(grad_rows[:, None, :] * returned_wide, axis=-1)
        grad_chosen = gate_values * (
            grad_gate - jnp.sum(gate_values * grad_gate, axis=-1, keepdims=True)
        )
        grad_logits = jnp.sum(onehot * grad_chosen[:, :, None], axis=1)
        router_term = jnp.dot(normed_two.astype(jnp.float32).T, grad_logits, precision=highest)
        grad_normtwo = jnp.dot(grad_logits, router_all.astype(jnp.float32).T, precision=highest)
        grad_result = (
            (gate_values[:, :, None] * grad_rows[:, None, :])
            .astype(jnp.bfloat16)
            .reshape(token_rows * TOP, hidden_width)
        )
        send_grads = (
            jnp.zeros((expert_count * capacity, hidden_width), jnp.bfloat16)
            .at[slot_idx]
            .set(grad_result)
        )
        recv_grads, again_rows = (
            lax.all_to_all(
                send_grads.reshape(expert_count, capacity, hidden_width),
                "expert",
                split_axis=0,
                concat_axis=0,
                tiled=True,
            ),
            lax.all_to_all(
                send_rows.reshape(expert_count, capacity, hidden_width),
                "expert",
                split_axis=0,
                concat_axis=0,
                tiled=True,
            ),
        )
        grouped_rows = again_rows.reshape(expert_size, local_experts, capacity, hidden_width)
        gate_up = jnp.einsum(
            "slcd,ldf->slcf", grouped_rows, gateup_all, preferred_element_type=jnp.float32
        )
        grouped_grads = recv_grads.reshape(expert_size, local_experts, capacity, hidden_width)
        gate_part = gate_up[..., :FF]
        up_part = gate_up[..., FF:]
        sigmoid_gate = jax.nn.sigmoid(gate_part)
        silu_gate = gate_part * sigmoid_gate
        hidden = (silu_gate * up_part).astype(jnp.bfloat16)
        grad_hidden = jnp.einsum(
            "slcd,lfd->slcf", grouped_grads, down_all, preferred_element_type=jnp.float32
        )
        down_term = jnp.einsum(
            "slcf,slcd->lfd", hidden, grouped_grads, preferred_element_type=jnp.float32
        )
        grad_gatepart = (
            grad_hidden * up_part * sigmoid_gate * (1.0 + gate_part * (1.0 - sigmoid_gate))
        )
        grad_gateup = jnp.concatenate([grad_gatepart, grad_hidden * silu_gate], axis=-1).astype(
            jnp.bfloat16
        )
        upper_term = jnp.einsum(
            "slcd,slcf->ldf", grouped_rows, grad_gateup, preferred_element_type=jnp.float32
        )
        grad_copies = jnp.einsum(
            "slcf,ldf->slcd", grad_gateup, gateup_all, preferred_element_type=jnp.float32
        ).astype(jnp.bfloat16)
        back_grads = lax.all_to_all(
            grad_copies.reshape(expert_count, capacity, hidden_width),
            "expert",
            split_axis=0,
            concat_axis=0,
            tiled=True,
        )
        copy_rows = back_grads.reshape(expert_count * capacity, hidden_width)[slot_idx].reshape(
            token_rows, TOP, hidden_width
        )
        grad_normtwo = grad_normtwo + jnp.sum(copy_rows.astype(jnp.float32), axis=1)
        midnorm_term = jnp.sum(grad_normtwo * normed_mid, axis=0)
        grad_mixed = grad_rows + norm_back(grad_normtwo, normed_mid, inverse_two, gain_two)
        grad_proj = grad_mixed.astype(jnp.bfloat16)
        output_term = jnp.dot(attended.T, grad_proj, preferred_element_type=jnp.float32)
        attention_gradient = jnp.dot(
            grad_proj, output_all.T, preferred_element_type=jnp.float32
        ).astype(jnp.bfloat16)
        attention_gradient = attention_gradient.reshape(
            token_rows, KEY_VALUE_HEADS, query_group_width, HEAD_SIZE
        )
        scores = masked_scores(query_matrix, key_rows, allowed)
        prob_rows = jnp.exp(scores - log_total)
        grad_probs = jnp.einsum(
            "qhgd,khd->hgqk", attention_gradient, value_rows, preferred_element_type=jnp.float32
        )
        row_delta = jnp.sum(prob_rows * grad_probs, axis=-1, keepdims=True)
        grad_scores = (prob_rows * (grad_probs - row_delta)).astype(jnp.bfloat16)
        prob_low = prob_rows.astype(jnp.bfloat16)
        grad_qrot = (
            jnp.einsum("hgqk,khd->qhgd", grad_scores, key_rows, preferred_element_type=jnp.float32)
            * score_scale
        )
        grad_keys = (
            jnp.einsum(
                "hgqk,qhgd->khd", grad_scores, query_matrix, preferred_element_type=jnp.float32
            )
            * score_scale
        )
        grad_vals = jnp.einsum(
            "hgqk,qhgd->khd", prob_low, attention_gradient, preferred_element_type=jnp.float32
        )
        own_keys = (
            lax.psum_scatter(
                jnp.stack([grad_keys, grad_vals], axis=1)
                .reshape(lax.axis_size("dp") * token_rows, 2 * KEY_VALUE_HEADS * HEAD_SIZE)
                .astype(jnp.bfloat16),
                "dp",
                scatter_dimension=0,
                tiled=True,
            )
            .astype(jnp.float32)
            .reshape(token_rows, 2, KEY_VALUE_HEADS, HEAD_SIZE)
        )
        grad_query = (
            unrotate(
                grad_qrot.reshape(token_rows, QUERY_HEADS, HEAD_SIZE), cosine_table, sine_table
            )
            .astype(jnp.bfloat16)
            .reshape(token_rows, QUERY_HEADS * HEAD_SIZE)
        )
        key_gradient = unrotate(own_keys[:, 0], cosine_table, sine_table).astype(jnp.bfloat16)
        value_gradient = own_keys[:, 1].astype(jnp.bfloat16)
        key_value_weight_gradient = jnp.stack([key_gradient, value_gradient], axis=1).reshape(
            token_rows, 2 * KEY_VALUE_HEADS * HEAD_SIZE
        )
        query_term = jnp.dot(normalized_input.T, grad_query, preferred_element_type=jnp.float32)
        keyval_term = jnp.dot(
            normalized_input.T, key_value_weight_gradient, preferred_element_type=jnp.float32
        )
        grad_normone = jnp.dot(grad_query, query_all.T, preferred_element_type=jnp.float32)
        grad_normone = grad_normone + jnp.dot(
            key_value_weight_gradient, keyval_all.T, preferred_element_type=jnp.float32
        )
        prenorm_term = jnp.sum(grad_normone * normed_one, axis=0)
        grads_list.append(grad_mixed + norm_back(grad_normone, normed_one, inverse_one, gain_one))
        total_prenorm = total_prenorm + prenorm_term
        total_query = total_query + query_term
        total_key_value = total_key_value + keyval_term
        total_output = total_output + output_term
        total_midnorm = total_midnorm + midnorm_term
        total_router = total_router + router_term
        total_upper = total_upper + upper_term
        total_down = total_down + down_term
    dense_grads = (
        lax.psum_scatter(total_prenorm, ("dp", "expert"), scatter_dimension=0, tiled=True),
        lax.psum_scatter(total_query, ("dp", "expert"), scatter_dimension=0, tiled=True),
        lax.psum_scatter(total_key_value, ("dp", "expert"), scatter_dimension=0, tiled=True),
        lax.psum_scatter(total_output, ("dp", "expert"), scatter_dimension=0, tiled=True),
        lax.psum_scatter(total_midnorm, ("dp", "expert"), scatter_dimension=0, tiled=True),
        lax.psum_scatter(total_router, ("dp", "expert"), scatter_dimension=0, tiled=True),
    )
    expert_grads = (
        lax.psum_scatter(
            total_upper.astype(jnp.bfloat16), "dp", scatter_dimension=1, tiled=True
        ).astype(jnp.float32),
        lax.psum_scatter(
            total_down.astype(jnp.bfloat16), "dp", scatter_dimension=1, tiled=True
        ).astype(jnp.float32),
    )
    return (
        jnp.stack(outputs_list),
        jnp.stack(grads_list),
        dense_grads[0],
        dense_grads[1],
        dense_grads[2],
        dense_grads[3],
        dense_grads[4],
        dense_grads[5],
        expert_grads[0],
        expert_grads[1],
    )


MESH = pl.DeviceIdType.MESH
CHUNK = 256
PIECE = 96


def remote(src, dst, send_sem, recv_sem, target):
    return pltpu.make_async_remote_copy(
        src_ref=src,
        dst_ref=dst,
        send_sem=send_sem,
        recv_sem=recv_sem,
        device_id=target,
        device_id_type=MESH,
    )


def place():
    d = lax.axis_index("dp")
    e = lax.axis_index("expert")
    z = lax.div(e, 2)
    c = lax.rem(e, 2)
    x = lax.rem(d, 2)
    y = lax.div(d, 2)
    return d, e, z, c, x, y


def expert_kernel(
    x_hbm,
    g_hbm,
    gt_hbm,
    win_hbm,
    wout_hbm,
    dx_out,
    dgt_out,
    outp_hbm,
    gin_hbm,
    gout_hbm,
    win,
    wout,
    xall,
    gall,
    gtall,
    dgu,
    hg,
    dxb,
    dgb,
    sibr,
    sibg,
    ro,
    rog,
    ri,
    rig,
    stage,
    own_sem,
    stage_sem,
    w_recv,
    w_send,
    ag_recv,
    ag_send,
    sib_recv,
    sib_send,
    red_recv,
    red_send,
):
    d, e, z, c, x, y = place()
    d_x = d + 1 - 2 * x
    d_y = d + 2 - 4 * y
    d_d = 3 - d
    hi = lax.div(z, 2)
    zz = z * hi + (3 - z) * (1 - hi)
    other = 1 - c
    to_x = (d_x, e)
    to_y = (d_y, e)
    to_sib = (d, 2 * z + other)
    to_up = (d, e + jnp.where(z < 3, 2, -2))
    to_down = (d, e + jnp.where(z > 0, -2, 2))
    e_in = e + 2 - 4 * hi
    e_out = e - 2 + 4 * hi
    to_in = (d, e_in)
    to_out = (d, jnp.where(zz == 2, e_out, e_in))
    mid = zz == 2
    end = zz == 3

    barrier = pltpu.get_barrier_semaphore()
    for target in (to_x, to_y, to_sib, to_in):
        pl.semaphore_signal(barrier, inc=1, device_id=target, device_id_type=MESH)

    @pl.when(mid)
    def _():
        pl.semaphore_signal(barrier, inc=1, device_id=to_out, device_id_type=MESH)

    pl.semaphore_wait(barrier, 7 - zz)

    gathered = ((x_hbm, xall), (gt_hbm, gtall))

    def part(a, ref, zp, lane, s):
        if a == 1:
            return ref.at[2 * zp + lane, s]
        return ref.at[pl.ds(pl.multiple_of((2 * zp + lane) * CHUNK + s * 128, 128), 128)]

    def own_part(a, ref, s):
        if a == 1:
            return ref.at[s]
        return ref.at[pl.ds(s * 128, 128)]

    def ag_copy(a, zp, s, way, src=None):
        ref = part(a, gathered[a][1], zp, c, s)
        return remote(
            ref if src is None else src,
            ref,
            ag_send.at[way, a, zp, s],
            ag_recv.at[a, zp, s],
            to_up if way == 0 else to_down,
        )

    def sib_copy(a, zp, s, src=None):
        ref = part(a, gathered[a][1], zp, c, s)
        return remote(
            ref if src is None else src,
            ref,
            sib_send.at[a, zp, s],
            sib_recv.at[a, zp, s],
            to_sib,
        )

    def piece(p, dd):
        if p < 4:
            return win.at[pl.ds(pl.multiple_of(dd * 384 + p * PIECE, 16), PIECE)]
        return wout.at[pl.ds(pl.multiple_of(dd * 192 + (p - 4) * PIECE, 16), PIECE)]

    def own_piece(p):
        if p < 4:
            return win_hbm.at[pl.ds(p * PIECE, PIECE)]
        return wout_hbm.at[pl.ds((p - 4) * PIECE, PIECE)]

    def w_copy(p, way, src_d, target, row, src=None):
        ref = piece(p, src_d)
        return remote(
            ref if src is None else src, ref, w_send.at[row, p], w_recv.at[row, p], target
        )

    for a in range(2):
        for s in range(2):
            src = own_part(a, gathered[a][0], s)

            @pl.when(z < 3)
            def _():
                ag_copy(a, z, s, 0, src).start()

            @pl.when(z > 0)
            def _():
                ag_copy(a, z, s, 1, src).start()

            sib_copy(a, z, s, src).start()
    for p in range(6):
        w_copy(p, 0, d, to_x, 0, own_piece(p)).start()
        w_copy(p, 0, d, to_y, 1, own_piece(p)).start()
    own_copies = [
        pltpu.make_async_copy(
            x_hbm, xall.at[pl.ds(pl.multiple_of(e * CHUNK, 128), CHUNK)], own_sem.at[0]
        ),
        pltpu.make_async_copy(g_hbm, gall, own_sem.at[1]),
        pltpu.make_async_copy(gt_hbm, gtall.at[e], own_sem.at[2]),
        pltpu.make_async_copy(
            win_hbm, win.at[pl.ds(pl.multiple_of(d * 384, 16), 384)], own_sem.at[3]
        ),
        pltpu.make_async_copy(
            wout_hbm, wout.at[pl.ds(pl.multiple_of(d * 192, 16), 192)], own_sem.at[4]
        ),
    ]
    for copy in own_copies:
        copy.start()

    def pass_on(a, k, s):
        @pl.when(z - k >= 0)
        def _():
            ag_copy(a, z - k, s, 0).wait_recv()

            @pl.when(z < 3)
            def _():
                ag_copy(a, z - k, s, 0).start()

            sib_copy(a, z - k, s).start()

        @pl.when(z + k <= 3)
        def _():
            ag_copy(a, z + k, s, 1).wait_recv()

            @pl.when(z > 0)
            def _():
                ag_copy(a, z + k, s, 1).start()

            sib_copy(a, z + k, s).start()

    for p in range(6):
        w_copy(p, 0, d_x, to_x, 0).wait_recv()
        if p % 2 == 0:
            w_copy(p, 0, d_x, to_y, 3).start()
        w_copy(p, 0, d_y, to_y, 1).wait_recv()
        if p % 2 == 1:
            w_copy(p, 0, d_y, to_x, 2).start()
        for a in range(2):
            pass_on(a, 1 + p // 2, p % 2)
    for p in range(6):
        if p % 2 == 0:
            w_copy(p, 0, d_d, to_y, 3).wait_recv()
        else:
            w_copy(p, 0, d_d, to_x, 2).wait_recv()
    for a in range(2):
        for zp in range(4):
            for s in range(2):
                ref = part(a, gathered[a][1], zp, other, s)
                remote(
                    ref, ref, sib_send.at[a, zp, s], sib_recv.at[a, zp, s], to_sib
                ).wait_recv()
    for copy in own_copies:
        copy.wait()

    eye = lax.broadcasted_iota(jnp.int32, (128, 128), 0) == lax.broadcasted_iota(
        jnp.int32, (128, 128), 1
    )
    mine = lax.broadcasted_iota(jnp.int32, (8, 128), 0) == e

    def order(i):
        v = jnp.where(i < 2, i, jnp.where(i == 2, 5 - zz, zz))
        return v * hi + (3 - v) * (1 - hi)

    def out_copy(i, zp):
        return pltpu.make_async_copy(
            stage.at[lax.rem(i, 2)],
            outp_hbm.at[pl.ds(pl.multiple_of(zp * 512, 512), 512)],
            stage_sem.at[lax.rem(i, 2)],
        )

    def lane_rows(i, lane):
        return pl.ds(pl.multiple_of(i * 512 + lane * CHUNK, CHUNK), CHUNK)

    def sib_sum_copies(i):
        return (
            remote(
                dxb.at[lane_rows(i, other)], sibr.at[i], red_send.at[0, i], red_recv.at[0, i], to_sib
            ),
            remote(dgb.at[i, other], sibg.at[i], red_send.at[1, i], red_recv.at[1, i], to_sib),
        )

    def hop_copies(i, target, dst, dstg, row):
        return (
            remote(
                dxb.at[lane_rows(i, c)], dst.at[i], red_send.at[2, i], red_recv.at[row, i], target
            ),
            remote(dgb.at[i, c], dstg.at[i], red_send.at[3, i], red_recv.at[row + 1, i], target),
        )

    def wait_from(ref, refg, slot, row):
        remote(ref.at[slot], ref.at[slot], red_send.at[2, slot], red_recv.at[row, slot], to_in).wait_recv()
        remote(refg.at[slot], refg.at[slot], red_send.at[3, slot], red_recv.at[row + 1, slot], to_in).wait_recv()

    def combine(i, incoming):
        total = dxb[lane_rows(i, c)].astype(jnp.float32) + sibr[i].astype(jnp.float32)
        totalg = dgb[i, c] + sibg[i]
        for ref, refg, slot in incoming:
            total = total + ref[slot].astype(jnp.float32)
            totalg = totalg + refg[slot]
        return total, totalg

    def combine_store(i, incoming):
        total, totalg = combine(i, incoming)
        dxb[lane_rows(i, c)] = total.astype(jnp.bfloat16)
        dgb[i, c] = totalg

    @pl.loop(0, 4)
    def _(i):
        zp = order(i)
        rows = pl.ds(pl.multiple_of(zp * 512, 512), 512)
        xc = xall[rows]
        gate = jnp.dot(xc, win[:, :FF], preferred_element_type=jnp.float32)
        up = jnp.dot(xc, win[:, FF:], preferred_element_type=jnp.float32)
        back = lax.dot_general(
            gall[rows], wout[...], (((1,), (1,)), ((), ())), preferred_element_type=jnp.float32
        )
        columns = []
        for lane in range(2):
            for s in range(2):
                row = jnp.sum(jnp.where(mine, gtall[2 * zp + lane, s], 0.0), axis=0, keepdims=True)
                columns.append(jnp.sum(jnp.where(eye, row, 0.0), axis=1, keepdims=True))
        weight = jnp.concatenate(columns, axis=0)
        sig = jax.nn.sigmoid(gate)
        silu = gate * sig
        hidden = (silu * up).astype(jnp.bfloat16).astype(jnp.float32)
        dgate = jnp.sum(hidden * back, axis=1, keepdims=True)
        for lane in range(2):
            for s in range(2):
                at = (2 * lane + s) * 128
                row = jnp.sum(jnp.where(eye, dgate[at : at + 128], 0.0), axis=0, keepdims=True)
                dgb[i, lane, s] = jnp.where(mine, row, 0.0)
        hg[rows] = (hidden * weight).astype(jnp.bfloat16)
        back = back * weight
        dgu[rows, :FF] = (back * up * (sig * (1.0 + gate * (1.0 - sig)))).astype(jnp.bfloat16)
        dgu[rows, FF:] = (back * silu).astype(jnp.bfloat16)
        dxb[pl.ds(pl.multiple_of(i * 512, 512), 512)] = lax.dot_general(
            dgu[rows], win[...], (((1,), (1,)), ((), ())), preferred_element_type=jnp.float32
        ).astype(jnp.bfloat16)
        for copy in sib_sum_copies(i):
            copy.start()

        @pl.when(i >= 2)
        def _():
            out_copy(i, zp).wait()

        stage[lax.rem(i, 2)] = jnp.dot(
            hg[rows], wout[...], preferred_element_type=jnp.float32
        ).astype(jnp.bfloat16)
        out_copy(i, zp).start()
        for copy in sib_sum_copies(i):
            copy.wait_recv()

        @pl.when(end & (i < 3))
        def _():
            combine_store(i, ())
            for copy in hop_copies(i, to_in, ro, rog, 2):
                copy.start()

        @pl.when(mid & (i == 2))
        def _():
            wait_from(ro, rog, 0, 2)
            combine_store(0, ((ro, rog, 0),))
            for copy in hop_copies(0, to_in, ri, rig, 4):
                copy.start()

    @pl.when(mid)
    def _():
        wait_from(ro, rog, 1, 2)
        combine_store(1, ((ro, rog, 1),))
        for copy in hop_copies(1, to_in, ri, rig, 4):
            copy.start()

    def grad_copy(k, target, at):
        return pltpu.make_async_copy(
            stage.at[k % 2, pl.ds(0, 384)], target.at[pl.ds(at, 384)], stage_sem.at[k % 2]
        )

    blocks = [(gout_hbm, 0), (gout_hbm, 384)] + [(gin_hbm, 384 * k) for k in range(4)]
    for k in range(2):
        out_copy(k, 0).wait()
    for k, (target, at) in enumerate(blocks):
        if k >= 2:
            grad_copy(k - 2, *blocks[k - 2]).wait()
        left = hg if k < 2 else xall
        right = gall if k < 2 else dgu
        stage[k % 2, :384] = lax.dot_general(
            left[:, at : at + 384],
            right[...],
            (((0,), (0,)), ((), ())),
            preferred_element_type=jnp.float32,
        ).astype(jnp.bfloat16)
        grad_copy(k, target, at).start()
        if k == 1:

            @pl.when(mid)
            def _():
                wait_from(ri, rig, 0, 4)
                combine_store(2, ((ri, rig, 0),))
                for copy in hop_copies(2, to_out, ri, rig, 4):
                    copy.start()

    for k in (4, 5):
        grad_copy(k, *blocks[k]).wait()

    @pl.when(mid)
    def _():
        wait_from(ro, rog, 2, 2)
        wait_from(ri, rig, 1, 4)
        total, totalg = combine(3, ((ro, rog, 2), (ri, rig, 1)))
        dx_out[...] = total
        dgt_out[...] = totalg

    @pl.when(end)
    def _():
        wait_from(ri, rig, 2, 4)
        total, totalg = combine(3, ((ri, rig, 2),))
        dx_out[...] = total
        dgt_out[...] = totalg

    for p in range(6):
        w_copy(p, 0, d, to_x, 0, own_piece(p)).wait_send()
        w_copy(p, 0, d, to_y, 1, own_piece(p)).wait_send()
        if p % 2 == 0:
            w_copy(p, 0, d_x, to_y, 3).wait_send()
        else:
            w_copy(p, 0, d_y, to_x, 2).wait_send()
    for a in range(2):
        for s in range(2):
            for zp in range(4):
                sib_copy(a, zp, s).wait_send()

                @pl.when((zp <= z) & (z < 3))
                def _():
                    ag_copy(a, zp, s, 0).wait_send()

                @pl.when((zp >= z) & (z > 0))
                def _():
                    ag_copy(a, zp, s, 1).wait_send()

    for i in range(4):
        for copy in sib_sum_copies(i):
            copy.wait_send()
        if i < 3:
            for copy in hop_copies(i, to_in, ro, rog, 2):
                copy.wait_send()


def expert_stage(rows, grads, gates_t, w_in, w_out):
    bf, f32 = jnp.bfloat16, jnp.float32
    shape = jax.ShapeDtypeStruct
    width = rows.shape[-1]
    hbm = pl.BlockSpec(memory_space=pltpu.HBM)
    vmem = pl.BlockSpec(memory_space=pltpu.VMEM)
    dma = pltpu.SemaphoreType.DMA
    return pl.pallas_call(
        expert_kernel,
        out_shape=(
            shape((CHUNK, width), f32),
            shape((2, 8, 128), f32),
            shape((8 * CHUNK, width), bf),
            shape((width, 2 * FF), bf),
            shape((FF, width), bf),
        ),
        in_specs=[hbm] * 5,
        out_specs=(vmem, vmem, hbm, hbm, hbm),
        scratch_shapes=[
            pltpu.VMEM((width, 2 * FF), bf),
            pltpu.VMEM((FF, width), bf),
            pltpu.VMEM((8 * CHUNK, width), bf),
            pltpu.VMEM((8 * CHUNK, width), bf),
            pltpu.VMEM((8, 2, 8, 128), f32),
            pltpu.VMEM((8 * CHUNK, 2 * FF), bf),
            pltpu.VMEM((8 * CHUNK, FF), bf),
            pltpu.VMEM((8 * CHUNK, width), bf),
            pltpu.VMEM((4, 2, 2, 8, 128), f32),
            pltpu.VMEM((4, CHUNK, width), bf),
            pltpu.VMEM((4, 2, 8, 128), f32),
            pltpu.VMEM((3, CHUNK, width), bf),
            pltpu.VMEM((3, 2, 8, 128), f32),
            pltpu.VMEM((3, CHUNK, width), bf),
            pltpu.VMEM((3, 2, 8, 128), f32),
            pltpu.VMEM((2, 512, width), bf),
            dma((5,)),
            dma((2,)),
            dma((4, 6)),
            dma((4, 6)),
            dma((2, 4, 2)),
            dma((2, 2, 4, 2)),
            dma((2, 4, 2)),
            dma((2, 4, 2)),
            dma((6, 4)),
            dma((4, 4)),
        ],
        compiler_params=pltpu.CompilerParams(
            collective_id=1, has_side_effects=True, vmem_limit_bytes=63 * 2**20
        ),
        name="expert_stage",
    )(rows, grads, gates_t, w_in, w_out)


def attention_kernel(
    tok_ref,
    wa_hbm,
    wb_hbm,
    g_hbm,
    cos_ref,
    sin_ref,
    lens_ref,
    routes_ref,
    wa_out,
    wb_out,
    gall,
    q_out,
    kv_out,
    att_out,
    mixed_out,
    normed_out,
    gates_out,
    wa,
    wb,
    qs,
    kvs,
    att,
    own_sem,
    z_recv,
    z_send,
    xy_recv,
    xy_send,
    sib_recv,
    sib_send,
    g_recv,
    g_send,
    gs_recv,
    gs_send,
    kv_recv,
    kv_send,
):
    bf, f32 = jnp.bfloat16, jnp.float32
    d, e, z, c, x, y = place()
    d_x = d + 1 - 2 * x
    d_y = d + 2 - 4 * y
    d_d = 3 - d
    other = 1 - c
    to_x = (d_x, e)
    to_y = (d_y, e)
    to_sib = (d, 2 * z + other)
    to_up = (d, e + jnp.where(z < 3, 2, -2))
    to_down = (d, e + jnp.where(z > 0, -2, 2))

    barrier = pltpu.get_barrier_semaphore()
    for target in (to_x, to_y, to_sib):
        pl.semaphore_signal(barrier, inc=1, device_id=target, device_id_type=MESH)

    @pl.when(z < 3)
    def _():
        pl.semaphore_signal(barrier, inc=1, device_id=to_up, device_id_type=MESH)

    @pl.when(z > 0)
    def _():
        pl.semaphore_signal(barrier, inc=1, device_id=to_down, device_id_type=MESH)

    pl.semaphore_wait(barrier, 5 - jnp.where((z == 0) | (z == 3), 1, 0))

    full = (wa, wb)
    shard = (wa_hbm, wb_hbm)

    def block(a, dd, zp, lane):
        at = pl.multiple_of((dd * 8 + 2 * zp + lane) * 48, 16)
        return full[a].at[pl.ds(at, 48)]

    def z_copy(a, zp, way, src=None):
        ref = block(a, d, zp, c)
        return remote(
            ref if src is None else src,
            ref,
            z_send.at[a, way, zp],
            z_recv.at[a, zp],
            to_up if way == 0 else to_down,
        )

    def xy_copy(a, dd, zp, row, target, src=None):
        ref = block(a, dd, zp, c)
        return remote(
            ref if src is None else src,
            ref,
            xy_send.at[a, row, zp],
            xy_recv.at[a, row, zp],
            target,
        )

    def s_copy(a, dd, zp, src=None, lane=None):
        ref = block(a, dd, zp, c if lane is None else lane)
        return remote(
            ref if src is None else src,
            ref,
            sib_send.at[a, dd, zp],
            sib_recv.at[a, dd, zp],
            to_sib,
        )

    def have(a, zp, src=None):
        xy_copy(a, d, zp, 0, to_x, src).start()
        xy_copy(a, d, zp, 1, to_y, src).start()
        s_copy(a, d, zp, src).start()

    def own_start(a):
        @pl.when(z < 3)
        def _():
            z_copy(a, z, 0, shard[a]).start()

        @pl.when(z > 0)
        def _():
            z_copy(a, z, 1, shard[a]).start()

        have(a, z, shard[a])

    def from_z(a, k):
        @pl.when(z - k >= 0)
        def _():
            z_copy(a, z - k, 0).wait_recv()

            @pl.when(z < 3)
            def _():
                z_copy(a, z - k, 0).start()

            have(a, z - k)

        @pl.when(z + k <= 3)
        def _():
            z_copy(a, z + k, 1).wait_recv()

            @pl.when(z > 0)
            def _():
                z_copy(a, z + k, 1).start()

            have(a, z + k)

    def from_xy_one(a, zp):
        xy_copy(a, d_x, zp, 0, to_x).wait_recv()

        @pl.when(lax.rem(zp, 2) == 0)
        def _():
            xy_copy(a, d_x, zp, 2, to_y).start()

        s_copy(a, d_x, zp).start()
        xy_copy(a, d_y, zp, 1, to_y).wait_recv()

        @pl.when(lax.rem(zp, 2) == 1)
        def _():
            xy_copy(a, d_y, zp, 2, to_x).start()

        s_copy(a, d_y, zp).start()

    def from_xy(a, k):
        @pl.when(z - k >= 0)
        def _():
            from_xy_one(a, z - k)

        if k > 0:

            @pl.when(z + k <= 3)
            def _():
                from_xy_one(a, z + k)

    def from_diag(a):
        for k in range(4):
            zp = lax.rem(z + k, 4)
            xy_copy(a, d_d, zp, 2, to_x).wait_recv()
            s_copy(a, d_d, zp).start()

    def from_sib(a):
        for dd in range(4):
            for zp in range(4):
                s_copy(a, dd, zp, lane=other).wait_recv()

    def drain(a):
        for zp in range(4):
            for dd in range(4):
                s_copy(a, dd, zp).wait_send()
            for row in range(3):
                xy_copy(a, d, zp, row, to_x).wait_send()

            @pl.when((zp <= z) & (z < 3))
            def _():
                z_copy(a, zp, 0).wait_send()

            @pl.when((zp >= z) & (z > 0))
            def _():
                z_copy(a, zp, 1).wait_send()

    def g_part(zp, lane, s):
        at = pl.multiple_of((2 * zp + lane) * CHUNK + s * 128, 128)
        return gall.at[pl.ds(at, 128)]

    def g_copy(zp, s, way, src=None):
        ref = g_part(zp, c, s)
        return remote(
            ref if src is None else src,
            ref,
            g_send.at[way, zp, s],
            g_recv.at[zp, s],
            to_up if way == 0 else to_down,
        )

    def gs_copy(zp, s, src=None, lane=None):
        ref = g_part(zp, c if lane is None else lane, s)
        return remote(
            ref if src is None else src, ref, gs_send.at[zp, s], gs_recv.at[zp, s], to_sib
        )

    def g_start():
        for s in range(2):
            src = g_hbm.at[pl.ds(s * 128, 128)]

            @pl.when(z < 3)
            def _():
                g_copy(z, s, 0, src).start()

            @pl.when(z > 0)
            def _():
                g_copy(z, s, 1, src).start()

            gs_copy(z, s, src).start()

    def g_pass(k, s):
        @pl.when(z - k >= 0)
        def _():
            g_copy(z - k, s, 0).wait_recv()

            @pl.when(z < 3)
            def _():
                g_copy(z - k, s, 0).start()

            gs_copy(z - k, s).start()

        @pl.when(z + k <= 3)
        def _():
            g_copy(z + k, s, 1).wait_recv()

            @pl.when(z > 0)
            def _():
                g_copy(z + k, s, 1).start()

            gs_copy(z + k, s).start()

    own = [
        pltpu.make_async_copy(shard[a], block(a, d, z, c), own_sem.at[a]) for a in range(2)
    ] + [
        pltpu.make_async_copy(
            g_hbm, gall.at[pl.ds(pl.multiple_of(e * CHUNK, CHUNK), CHUNK)], own_sem.at[2]
        )
    ]
    own_start(0)
    own_start(1)
    for copy in own:
        copy.start()
    g_start()
    tok = tok_ref[...].astype(f32)
    n1 = tok * lax.rsqrt(jnp.mean(tok * tok, axis=1, keepdims=True) + epsilon)
    for k in range(1, 4):
        from_z(0, k)
        from_xy(0, k - 1)
        from_z(1, k)
    from_xy(0, 3)
    from_diag(0)
    own[0].wait()
    from_sib(0)

    small = wa[:, 2048:]
    eye = (
        lax.broadcasted_iota(jnp.int32, (128, 128), 0)
        == lax.broadcasted_iota(jnp.int32, (128, 128), 1)
    ).astype(bf)
    small_t = lax.dot_general(eye, small, (((1,), (1,)), ((), ())), preferred_element_type=f32)
    normed = (n1 * small_t[8:9]).astype(bf)
    cos_rows = jnp.concatenate([cos_ref[...]] * 2, axis=0)
    sin_rows = jnp.concatenate([sin_ref[...]] * 2, axis=0)

    def rotate(v):
        return v * cos_rows + pltpu.roll(v, 64, 1) * sin_rows

    kv = jnp.dot(normed, wa[:, 1536:2048], preferred_element_type=f32)
    for h in range(2):
        kvs[d, :, h * 128 : (h + 1) * 128] = rotate(kv[:, h * 128 : (h + 1) * 128]).astype(bf)
    kvs[d, :, 256:] = kv[:, 256:].astype(bf)

    def kv_copy(dd, s, row, target):
        ref = kvs.at[dd, pl.ds(s * 128, 128)]
        return remote(ref, ref, kv_send.at[row, s], kv_recv.at[row, s], target)

    for s in range(2):
        kv_copy(d, s, 0, to_x).start()
        kv_copy(d, s, 1, to_y).start()
    from_xy(1, 0)
    q = jnp.dot(normed, wa[:, :1536], preferred_element_type=f32)
    for head in range(QUERY_HEADS):
        rot = rotate(q[:, head * 128 : (head + 1) * 128]).astype(bf)
        for s in range(2):
            at = (s * QUERY_HEADS + head) * 128
            qs[at : at + 128] = rot[s * 128 : (s + 1) * 128]
    g_pass(1, 0)
    kv_copy(d_x, 0, 0, to_x).wait_recv()
    kv_copy(d_x, 0, 2, to_y).start()
    kv_copy(d_y, 1, 1, to_y).wait_recv()
    kv_copy(d_y, 1, 2, to_x).start()
    kv_copy(d_y, 0, 1, to_y).wait_recv()
    kv_copy(d_x, 1, 0, to_x).wait_recv()
    for k in range(1, 4):
        from_xy(1, k)
    g_pass(1, 1)
    for s in range(2):
        kv_copy(d_d, s, 2, to_x).wait_recv()
    q_copy = pltpu.make_async_copy(qs, q_out, own_sem.at[3])
    kvo_copy = pltpu.make_async_copy(kvs, kv_out, own_sem.at[4])
    wa_copy = pltpu.make_async_copy(wa, wa_out, own_sem.at[5])
    for copy in (q_copy, kvo_copy, wa_copy):
        copy.start()

    query_pos = d * 128 + lax.broadcasted_iota(jnp.int32, (128, 512), 0)
    key_pos = lax.broadcasted_iota(jnp.int32, (128, 512), 1)

    @pl.loop(0, 4)
    def _(n):
        s = lax.div(n, 2)
        h = lax.rem(n, 2)
        lens = lens_ref[s][0:1, 0:1]
        allowed = (key_pos <= query_pos) & (key_pos < lens)
        ks = kvs[:, pl.ds(pl.multiple_of(s * 128, 128), 128), pl.ds(pl.multiple_of(h * 128, 128), 128)]
        vs = kvs[:, pl.ds(pl.multiple_of(s * 128, 128), 128), pl.ds(pl.multiple_of(256 + h * 128, 128), 128)]
        ks = ks.reshape(512, 128)
        vs = vs.reshape(512, 128)
        for half in range(2):
            qh = qs[pl.ds(pl.multiple_of(n * 768 + half * 384, 128), 384)]
            scores = lax.dot_general(qh, ks, (((1,), (1,)), ((), ())), preferred_element_type=f32)
            scores = scores.reshape(3, 128, 512) * HEAD_SIZE ** (-0.5)
            scores = jnp.where(allowed[None], scores, -1e30)
            top = jnp.max(scores, axis=-1, keepdims=True)
            weights = jnp.exp(scores - top)
            weights = weights * (1.0 / jnp.sum(weights, axis=-1, keepdims=True))
            out = jnp.dot(
                weights.astype(bf).reshape(384, 512), vs, preferred_element_type=f32
            ).astype(bf)
            for j in range(3):
                att[
                    pl.ds(pl.multiple_of(s * 128, 128), 128),
                    pl.ds(pl.multiple_of(h * 768 + (half * 3 + j) * 128, 128), 128),
                ] = out[j * 128 : (j + 1) * 128]

    g_pass(2, 0)
    from_diag(1)
    own[1].wait()
    from_sib(1)
    att_copy = pltpu.make_async_copy(att, att_out, own_sem.at[6])
    wb_copy = pltpu.make_async_copy(wb, wb_out, own_sem.at[7])
    att_copy.start()
    wb_copy.start()
    mixed = tok_ref[...].astype(f32) + jnp.dot(att[...], wb[...], preferred_element_type=f32)
    mixed_out[...] = mixed
    n2 = mixed * lax.rsqrt(jnp.mean(mixed * mixed, axis=1, keepdims=True) + epsilon)
    normed2 = (n2 * small_t[9:10]).astype(bf)
    normed_out[...] = normed2
    logits = jnp.dot(normed2, small, preferred_element_type=f32)
    lanes = lax.broadcasted_iota(jnp.int32, (CHUNK, 128), 1)
    chosen = lanes == routes_ref[:, 0:1]
    for t in range(1, TOP):
        chosen = chosen | (lanes == routes_ref[:, t : t + 1])
    logits = jnp.where(chosen, logits, -1e30)
    weights = jnp.where(chosen, jnp.exp(logits - jnp.max(logits, axis=1, keepdims=True)), 0.0)
    gates_out[...] = weights / jnp.sum(weights, axis=1, keepdims=True)

    g_pass(2, 1)
    g_pass(3, 0)
    g_pass(3, 1)
    for zp in range(4):
        for s in range(2):
            gs_copy(zp, s, lane=other).wait_recv()
    own[2].wait()
    for copy in (q_copy, kvo_copy, wa_copy, att_copy, wb_copy):
        copy.wait()
    drain(0)
    drain(1)
    for s in range(2):
        for row in range(3):
            kv_copy(d, s, row, to_x).wait_send()
        for zp in range(4):
            gs_copy(zp, s).wait_send()

            @pl.when((zp <= z) & (z < 3))
            def _():
                g_copy(zp, s, 0).wait_send()

            @pl.when((zp >= z) & (z > 0))
            def _():
                g_copy(zp, s, 1).wait_send()


def attention_stage(rows, w_a, w_b, grads, cos_rows, sin_rows, lens, routes):
    bf, f32 = jnp.bfloat16, jnp.float32
    shape = jax.ShapeDtypeStruct
    width = rows.shape[-1]
    wide = w_a.shape[-1]
    hbm = pl.BlockSpec(memory_space=pltpu.HBM)
    vmem = pl.BlockSpec(memory_space=pltpu.VMEM)
    dma = pltpu.SemaphoreType.DMA
    return pl.pallas_call(
        attention_kernel,
        out_shape=(
            shape((width, wide), bf),
            shape((width, width), bf),
            shape((8 * CHUNK, width), bf),
            shape((2 * QUERY_HEADS * 128, 128), bf),
            shape((4, CHUNK, 512), bf),
            shape((CHUNK, width), bf),
            shape((CHUNK, width), f32),
            shape((CHUNK, width), bf),
            shape((CHUNK, 128), f32),
        ),
        in_specs=[vmem, hbm, hbm, hbm, vmem, vmem, vmem, vmem],
        out_specs=(hbm, hbm, hbm, hbm, hbm, hbm, vmem, vmem, vmem),
        scratch_shapes=[
            pltpu.VMEM((width, wide), bf),
            pltpu.VMEM((width, width), bf),
            pltpu.VMEM((2 * QUERY_HEADS * 128, 128), bf),
            pltpu.VMEM((4, CHUNK, 512), bf),
            pltpu.VMEM((CHUNK, width), bf),
            dma((8,)),
            dma((2, 4)),
            dma((2, 2, 4)),
            dma((2, 3, 4)),
            dma((2, 3, 4)),
            dma((2, 4, 4)),
            dma((2, 4, 4)),
            dma((4, 2)),
            dma((2, 4, 2)),
            dma((4, 2)),
            dma((4, 2)),
            dma((3, 2)),
            dma((3, 2)),
        ],
        compiler_params=pltpu.CompilerParams(
            collective_id=2, has_side_effects=True, vmem_limit_bytes=60 * 2**20
        ),
        name="attention_stage",
    )(rows, w_a, w_b, grads, cos_rows, sin_rows, lens, routes)


def backward_kernel(
    dx_ref,
    dgt_ref,
    gates_ref,
    mixed_ref,
    g_ref,
    tok_ref,
    q_ref,
    kv_ref,
    att_ref,
    cos_ref,
    sin_ref,
    lens_ref,
    live_ref,
    wa_hbm,
    wb_hbm,
    gin_hbm,
    gout_hbm,
    outp_hbm,
    block_out,
    dtok_out,
    ga_out,
    gb_out,
    ein_out,
    eout_out,
    osib,
    oro,
    ori,
    wide,
    small,
    ga,
    gb,
    sib_a,
    sib_b,
    ta,
    xa,
    ya,
    roa,
    ria,
    tb,
    xb,
    yb,
    rob,
    rib,
    te,
    xe,
    ye,
    le,
    old,
    oslot,
    dat,
    dkv,
    tk,
    xk,
    yk,
    load_sem,
    le_sem,
    old_sem,
    os_recv,
    os_send,
    ds_recv,
    ds_send,
    t_recv,
    x_recv,
    y_recv,
    t_send,
    d_send,
    s_send,
    ro_recv,
    ri_recv,
    hop_send,
):
    bf, f32 = jnp.bfloat16, jnp.float32
    d, e, z, c, x, y = place()
    d_x = d + 1 - 2 * x
    d_y = d + 2 - 4 * y
    d_d = 3 - d
    hi = lax.div(z, 2)
    zz = z * hi + (3 - z) * (1 - hi)
    other = 1 - c
    mid = zz == 2
    end = zz == 3
    to_x = (d_x, e)
    to_y = (d_y, e)
    to_sib = (d, 2 * z + other)
    e_in = e + 2 - 4 * hi
    to_in = (d, e_in)
    to_out = (d, jnp.where(zz == 2, e - 2 + 4 * hi, e_in))

    dqs = block_out
    dmix = dtok_out

    barrier = pltpu.get_barrier_semaphore()
    for target in (to_x, to_y, to_sib, to_in):
        pl.semaphore_signal(barrier, inc=1, device_id=target, device_id_type=MESH)

    @pl.when(mid)
    def _():
        pl.semaphore_signal(barrier, inc=1, device_id=to_out, device_id_type=MESH)

    pl.semaphore_wait(barrier, 7 - zz)

    def order(i):
        v = i if i < 2 else (5 - zz if i == 2 else zz)
        return v * hi + (3 - v) * (1 - hi)

    def across(k, src, t, fx, fy):
        def diag(i):
            return remote(
                src(d_d, i), t.at[i], t_send.at[k, i], t_recv.at[k, i], (to_x, to_y)[i % 2]
            )

        def direct(i):
            if i % 2 == 0:
                return remote(src(d_x, i), fx.at[i], d_send.at[k, i], x_recv.at[k, i], to_x)
            return remote(src(d_y, i), fy.at[i], d_send.at[k, i], y_recv.at[k, i], to_y)

        def summed(i, ref):
            if i % 2 == 0:
                return remote(ref, fy.at[i], s_send.at[k, i], y_recv.at[k, i], to_y)
            return remote(ref, fx.at[i], s_send.at[k, i], x_recv.at[k, i], to_x)

        def wait_t(i):
            remote(t.at[i], t.at[i], t_send.at[k, i], t_recv.at[k, i], to_x).wait_recv()

        def wait_xy(i):
            remote(fx.at[i], fx.at[i], d_send.at[k, i], x_recv.at[k, i], to_x).wait_recv()
            remote(fy.at[i], fy.at[i], d_send.at[k, i], y_recv.at[k, i], to_y).wait_recv()

        def drain(n):
            for i in range(n):
                diag(i).wait_send()
                direct(i).wait_send()
                summed(i, t.at[i]).wait_send()

        return diag, direct, summed, wait_t, wait_xy, drain

    def along(k, slot, ro, ri):
        def send(i, target, dst, recv):
            return remote(slot(i), dst.at[i], hop_send.at[k, i], recv.at[k, i], target)

        def to_ro(i):
            return send(i, to_in, ro, ro_recv)

        def to_ri(i):
            return send(i, to_in if i < 2 else to_out, ri, ri_recv)

        def wait_ro(i):
            remote(ro.at[i], ro.at[i], hop_send.at[k, i], ro_recv.at[k, i], to_in).wait_recv()

        def wait_ri(i):
            remote(ri.at[i], ri.at[i], hop_send.at[k, i], ri_recv.at[k, i], to_in).wait_recv()

        def drain():
            for i in range(3):
                to_ro(i).wait_send()

        return to_ro, to_ri, wait_ro, wait_ri, drain

    def expert_src(dd, p):
        if p < 4:
            return gin_hbm.at[pl.ds(pl.multiple_of(dd * 384 + p * PIECE, 16), PIECE)]
        return gout_hbm.at[pl.ds(pl.multiple_of(dd * 192 + (p - 4) * PIECE, 16), PIECE)]

    e_diag, e_direct, e_summed, e_wait_t, e_wait_xy, e_drain = across(0, expert_src, te, xe, ye)

    def e_load(p, dd, j):
        return pltpu.make_async_copy(expert_src(dd, p), le.at[j], le_sem.at[j])

    def e_middle(p):
        load = e_load(p, d_y if p % 2 == 0 else d_x, 0)
        load.start()
        e_wait_t(p)
        load.wait()
        te[p] = (te[p].astype(f32) + le[0].astype(f32)).astype(bf)
        e_summed(p, te.at[p]).start()

    def e_final(p):
        load = e_load(p, d, 1)
        load.start()
        e_wait_xy(p)
        load.wait()
        total = le[1].astype(f32) + xe[p].astype(f32) + ye[p].astype(f32)
        if p < 4:
            ein_out[p * PIECE : (p + 1) * PIECE] = total.astype(bf)
        else:
            eout_out[(p - 4) * PIECE : (p - 3) * PIECE] = total.astype(bf)

    dense = ((ga, sib_a, ta, xa, ya, roa, ria, ga_out), (gb, sib_b, tb, xb, yb, rob, rib, gb_out))

    def dense_stream(j):
        grad, sib, t, fx, fy, ro, ri, out = dense[j]

        def src(dd, i):
            return grad.at[dd * 4 + order(i), c]

        diag, direct, summed, wait_t, wait_xy, drain = across(1 + j, src, t, fx, fy)

        def own_slot(i):
            return grad.at[d * 4 + order(i), c]

        to_ro, to_ri, wait_ro, wait_ri, drain_z = along(j, own_slot, ro, ri)

        def sib_copy():
            return remote(grad.at[:, other], sib, ds_send.at[j], ds_recv.at[j], to_sib)

        def begin():
            sib_copy().wait_recv()

            @pl.loop(0, 16)
            def _(k):
                grad[k, c] = (grad[k, c].astype(f32) + sib[k].astype(f32)).astype(bf)

            for i in range(4):
                diag(i).start()
            for i in range(4):
                direct(i).start()

        def middle(i):
            dd = d_y if i % 2 == 0 else d_x
            wait_t(i)
            at = dd * 4 + order(i)
            grad[at, c] = (grad[at, c].astype(f32) + t[i].astype(f32)).astype(bf)
            summed(i, src(dd, i)).start()

        def local(i):
            return grad[d * 4 + order(i), c].astype(f32) + fx[i].astype(f32) + fy[i].astype(f32)

        def put(i, total):
            grad[d * 4 + order(i), c] = total.astype(bf)

        def last(i):
            wait_xy(i)
            if i == 3:
                return

            @pl.when(end)
            def _():
                put(i, local(i))
                to_ro(i).start()

        def hop(i):
            @pl.when(mid)
            def _():
                if i < 2:
                    wait_ro(i)
                    put(i, local(i) + ro[i].astype(f32))
                else:
                    wait_ri(0)
                    put(2, local(2) + ri[0].astype(f32))
                to_ri(i).start()

        def finish():
            @pl.when(mid)
            def _():
                wait_ro(2)
                wait_ri(1)
                out[...] = local(3) + ro[2].astype(f32) + ri[1].astype(f32)

            @pl.when(end)
            def _():
                wait_ri(2)
                out[...] = local(3) + ri[2].astype(f32)

        def drain_all():
            sib_copy().wait_send()
            drain(4)
            drain_z()

        return sib_copy, begin, middle, last, hop, finish, drain_all

    a_sib, a_begin, a_middle, a_last, a_hop, a_finish, a_drain = dense_stream(0)
    b_sib, b_begin, b_middle, b_last, b_hop, b_finish, b_drain = dense_stream(1)

    def out_rows(i, lane):
        return outp_hbm.at[pl.ds(pl.multiple_of((2 * order(i) + lane) * CHUNK, CHUNK), CHUNK)]

    def out_sib(i):
        return remote(out_rows(i, other), osib.at[i], os_send.at[i], os_recv.at[i], to_sib)

    o_ro, o_ri, o_wait_ro, o_wait_ri, o_drain = along(2, lambda i: oslot.at[i], oro, ori)

    def out_sum(i, incoming, store):
        out_sib(i).wait_recv()
        for half in range(2):
            rows = pl.ds(half * 128, 128)
            loads = [
                pltpu.make_async_copy(ref.at[rows], old.at[j], old_sem.at[j])
                for j, ref in enumerate([out_rows(i, c), osib.at[i]] + incoming)
            ]
            for load in loads:
                load.start()
            for load in loads:
                load.wait()
            total = old[0].astype(f32)
            for j in range(1, len(loads)):
                total = total + old[j].astype(f32)
            store(slice(half * 128, (half + 1) * 128), total)

    def out_slot(i):
        def store(rows, total):
            oslot[i, rows] = total.astype(bf)

        return store

    def out_end(i):
        @pl.when(end)
        def _():
            out_sum(i, [], out_slot(i))
            o_ro(i).start()

    def out_mid(i):
        @pl.when(mid)
        def _():
            if i < 2:
                o_wait_ro(i)
                out_sum(i, [oro.at[i]], out_slot(i))
            else:
                o_wait_ri(0)
                out_sum(2, [ori.at[0]], out_slot(2))
            o_ri(i).start()

    def out_finish():
        def store(rows, total):
            total = total + mixed_ref[rows]
            block_out[rows] = jnp.where(live_ref[rows, 0:1] > 0, total, 0.0).astype(bf)

        @pl.when(mid)
        def _():
            o_wait_ro(2)
            o_wait_ri(1)
            out_sum(3, [oro.at[2], ori.at[1]], store)

        @pl.when(end)
        def _():
            o_wait_ri(2)
            out_sum(3, [ori.at[2]], store)

    def kv_src(dd, i):
        return dkv.at[dd, pl.ds(i * 128, 128)]

    k_diag, k_direct, k_summed, k_wait_t, k_wait_xy, k_drain = across(3, kv_src, tk, xk, yk)

    def k_middle(i):
        dd = d_y if i % 2 == 0 else d_x
        k_wait_t(i)
        rows = slice(i * 128, (i + 1) * 128)
        dkv[dd, rows] = (dkv[dd, rows].astype(f32) + tk[i].astype(f32)).astype(bf)
        k_summed(i, kv_src(dd, i)).start()

    small_load = pltpu.make_async_copy(wa_hbm.at[:, pl.ds(2048, 128)], small, load_sem.at[0])
    wb_load = pltpu.make_async_copy(wb_hbm, wide.at[:, pl.ds(0, 1536)], load_sem.at[1])
    wa_load = pltpu.make_async_copy(wa_hbm.at[:, pl.ds(0, 2048)], wide, load_sem.at[2])
    small_load.start()
    wb_load.start()
    for p in range(6):
        e_diag(p).start()
    for p in range(6):
        e_direct(p).start()
    for i in range(4):
        out_sib(i).start()

    ones = lax.broadcasted_iota(jnp.int32, (CHUNK, 128), 1)
    eye = (
        lax.broadcasted_iota(jnp.int32, (128, 128), 0)
        == lax.broadcasted_iota(jnp.int32, (128, 128), 1)
    ).astype(f32)
    dgate = jnp.concatenate(
        [
            lax.dot_general(
                eye,
                jnp.concatenate([dgt_ref[s], jnp.zeros((120, 128), f32)], axis=0),
                (((1,), (1,)), ((), ())),
                preferred_element_type=f32,
                precision=highest,
            )
            for s in range(2)
        ],
        axis=0,
    )
    gates = gates_ref[...]
    dlogit = gates * (dgate - jnp.sum(gates * dgate, axis=1, keepdims=True))

    def halves(v):
        high = v.astype(bf)
        return high, (v - high.astype(f32)).astype(bf)

    dl_hi, dl_lo = halves(dlogit)
    small_load.wait()
    small_t = lax.dot_general(
        eye.astype(bf), small[...], (((1,), (1,)), ((), ())), preferred_element_type=f32
    )
    nt = (((1,), (1,)), ((), ()))
    tn = (((0,), (0,)), ((), ()))

    def dot_nt(a, b):
        return lax.dot_general(a, b, nt, preferred_element_type=f32)

    def dot_tn(a, b):
        return lax.dot_general(a, b, tn, preferred_element_type=f32)

    dn2 = dx_ref[...] + dot_nt(dl_hi, small[...]) + dot_nt(dl_lo, small[...])
    mixed = mixed_ref[...]
    inv2 = lax.rsqrt(jnp.mean(mixed * mixed, axis=1, keepdims=True) + epsilon)
    n2 = mixed * inv2
    normed2 = (n2 * small_t[9:10]).astype(bf)
    mid_hi, mid_lo = halves(dn2 * n2)
    col9 = (ones == 9).astype(bf)
    for r in range(4):
        cols = slice(r * 384, (r + 1) * 384)
        part = (
            dot_tn(normed2[:, cols], dl_hi)
            + dot_tn(normed2[:, cols], dl_lo)
            + dot_tn(mid_hi[:, cols], col9)
            + dot_tn(mid_lo[:, cols], col9)
        )
        dsm = part.reshape(4, 2, 48, 128)
        ga[4 * r : 4 * r + 4, :, :, 2048:] = dsm.astype(bf)
    u = dn2 * small_t[9:10]
    dmixed = g_ref[...].astype(f32) + inv2 * (u - n2 * jnp.mean(u * n2, axis=1, keepdims=True))
    dmix[...] = dmixed
    dproj = dmixed.astype(bf)
    for r in range(4):
        part = dot_tn(att_ref[:, r * 384 : (r + 1) * 384], dproj)
        gb[4 * r : 4 * r + 4] = part.astype(bf).reshape(4, 2, 48, 1536)
    b_sib().start()
    wb_load.wait()
    datt = dot_nt(dproj, wide[:, :1536]).astype(bf)
    for head in range(QUERY_HEADS):
        for s in range(2):
            at = (s * QUERY_HEADS + head) * 128
            dat[at : at + 128] = datt[s * 128 : (s + 1) * 128, head * 128 : (head + 1) * 128]
    wa_load.start()
    e_middle(0)
    e_middle(1)
    b_begin()
    for i in range(3):
        out_end(i)

    query_pos = d * 128 + lax.broadcasted_iota(jnp.int32, (128, 512), 0)
    key_pos = lax.broadcasted_iota(jnp.int32, (128, 512), 1)
    cos_rows = cos_ref[...]
    sin_rows = sin_ref[...]
    scale = HEAD_SIZE ** (-0.5)

    def unrotate_rows(v, cos, sin):
        return v * cos - pltpu.roll(v, 64, 1) * sin

    @pl.loop(0, 4)
    def _(n):
        s = lax.div(n, 2)
        h = lax.rem(n, 2)
        srow = pl.ds(pl.multiple_of(s * 128, 128), 128)
        kcol = pl.ds(pl.multiple_of(h * 128, 128), 128)
        vcol = pl.ds(pl.multiple_of(256 + h * 128, 128), 128)
        lens = lens_ref[s][0:1, 0:1]
        allowed = (key_pos <= query_pos) & (key_pos < lens)
        ks = kv_ref[:, srow, kcol].reshape(512, 128)
        vs = kv_ref[:, srow, vcol].reshape(512, 128)
        dk = None
        dv = None
        for half in range(2):
            rows = pl.ds(pl.multiple_of(n * 768 + half * 384, 128), 384)
            qh = q_ref[rows]
            dh = dat[rows]
            scores = dot_nt(qh, ks).reshape(3, 128, 512) * scale
            scores = jnp.where(allowed[None], scores, -1e30)
            probs = jnp.exp(scores - jnp.max(scores, axis=-1, keepdims=True))
            probs = probs * (1.0 / jnp.sum(probs, axis=-1, keepdims=True))
            dprobs = dot_nt(dh, vs).reshape(3, 128, 512)
            delta = jnp.sum(probs * dprobs, axis=-1, keepdims=True)
            dscores = (probs * (dprobs - delta)).astype(bf).reshape(384, 512)
            low = probs.astype(bf).reshape(384, 512)
            dq = jnp.dot(dscores, ks, preferred_element_type=f32) * scale
            for j in range(3):
                dqs[srow, pl.ds(pl.multiple_of(h * 768 + (half * 3 + j) * 128, 128), 128)] = (
                    unrotate_rows(dq[j * 128 : (j + 1) * 128], cos_rows, sin_rows).astype(bf)
                )
            dk_part = dot_tn(dscores, qh)
            dv_part = dot_tn(low, dh)
            dk = dk_part if dk is None else dk + dk_part
            dv = dv_part if dv is None else dv + dv_part
        dkv[:, srow, kcol] = (dk * scale).astype(bf).reshape(4, 128, 128)
        dkv[:, srow, vcol] = dv.astype(bf).reshape(4, 128, 128)

    for i in range(2):
        k_diag(i).start()
    for i in range(2):
        k_direct(i).start()
    e_middle(2)
    e_middle(3)

    tok = tok_ref[...].astype(f32)
    inv1 = lax.rsqrt(jnp.mean(tok * tok, axis=1, keepdims=True) + epsilon)
    n1 = tok * inv1
    normed = (n1 * small_t[8:9]).astype(bf)
    for r in range(4):
        part = dot_tn(normed[:, r * 384 : (r + 1) * 384], dqs[...])
        ga[4 * r : 4 * r + 4, :, :, :1536] = part.astype(bf).reshape(4, 2, 48, 1536)
    wa_load.wait()
    k_middle(0)
    k_middle(1)
    dn1 = dot_nt(dqs[...], wide[:, :1536])
    e_middle(4)
    e_middle(5)
    out_mid(0)
    for i in range(4):
        b_middle(i)

    for i in range(2):
        k_wait_xy(i)
    own = jnp.concatenate(
        [
            dkv[d, i * 128 : (i + 1) * 128].astype(f32) + xk[i].astype(f32) + yk[i].astype(f32)
            for i in range(2)
        ],
        axis=0,
    )
    cos_two = jnp.concatenate([cos_rows] * 2, axis=0)
    sin_two = jnp.concatenate([sin_rows] * 2, axis=0)
    dkv_own = jnp.concatenate(
        [
            unrotate_rows(own[:, h * 128 : (h + 1) * 128], cos_two, sin_two)
            for h in range(2)
        ]
        + [own[:, 256:]],
        axis=1,
    ).astype(bf)
    dn1 = dn1 + dot_nt(dkv_own, wide[:, 1536:])
    pre_hi, pre_lo = halves(dn1 * n1)
    col8 = (ones == 8).astype(bf)
    for r in range(4):
        cols = slice(r * 384, (r + 1) * 384)
        part = dot_tn(normed[:, cols], dkv_own)
        ga[4 * r : 4 * r + 4, :, :, 1536:2048] = part.astype(bf).reshape(4, 2, 48, 512)
        part = dot_tn(pre_hi[:, cols], col8) + dot_tn(pre_lo[:, cols], col8)
        ga[4 * r : 4 * r + 4, :, :, 2048:] = (
            ga[4 * r : 4 * r + 4, :, :, 2048:].astype(f32) + part.reshape(4, 2, 48, 128)
        ).astype(bf)
    a_sib().start()
    u = dn1 * small_t[8:9]
    dtok_out[...] = dmix[...] + inv1 * (u - n1 * jnp.mean(u * n1, axis=1, keepdims=True))

    a_begin()
    for i in range(4):
        b_last(i)
    out_mid(1)
    out_mid(2)
    for i in range(3):
        b_hop(i)
    for p in range(6):
        e_final(p)
    for i in range(4):
        a_middle(i)
    out_finish()
    b_finish()
    for i in range(4):
        a_last(i)
        if i < 3:
            a_hop(i)
    a_finish()

    e_drain(6)
    k_drain(2)
    a_drain()
    b_drain()
    o_drain()
    for i in range(4):
        out_sib(i).wait_send()


def backward_stage(dx, dgt, gates, mixed, g, tok, q, kv, att, cos, sin, lens, live, wa, wb, gin, gout, outp):
    bf, f32 = jnp.bfloat16, jnp.float32
    shape = jax.ShapeDtypeStruct
    width = tok.shape[-1]
    wide = wa.shape[-1]
    hbm = pl.BlockSpec(memory_space=pltpu.HBM)
    vmem = pl.BlockSpec(memory_space=pltpu.VMEM)
    dma = pltpu.SemaphoreType.DMA
    dense = []
    for w in (wide, width):
        dense += [pltpu.VMEM((4, 48, w), bf)] * 3 + [pltpu.VMEM((3, 48, w), bf)] * 2
    return pl.pallas_call(
        backward_kernel,
        out_shape=(
            shape((CHUNK, width), bf),
            shape((CHUNK, width), f32),
            shape((48, wide), f32),
            shape((48, width), f32),
            shape((384, 2 * FF), bf),
            shape((192, width), bf),
            shape((4, CHUNK, width), bf),
            shape((3, CHUNK, width), bf),
            shape((3, CHUNK, width), bf),
        ),
        in_specs=[vmem] * 13 + [hbm] * 5,
        out_specs=[vmem] * 6 + [hbm] * 3,
        scratch_shapes=[
            pltpu.VMEM((width, 2048), bf),
            pltpu.VMEM((width, 128), bf),
            pltpu.VMEM((16, 2, 48, wide), bf),
            pltpu.VMEM((16, 2, 48, width), bf),
            pltpu.VMEM((16, 48, wide), bf),
            pltpu.VMEM((16, 48, width), bf),
            *dense,
            *([pltpu.VMEM((6, PIECE, width), bf)] * 3),
            pltpu.VMEM((2, PIECE, width), bf),
            pltpu.VMEM((4, 128, width), bf),
            pltpu.VMEM((3, CHUNK, width), bf),
            pltpu.VMEM((2 * QUERY_HEADS * 128, 128), bf),
            pltpu.VMEM((4, CHUNK, 512), bf),
            *([pltpu.VMEM((2, 128, 512), bf)] * 3),
            dma((3,)),
            dma((2,)),
            dma((4,)),
            dma((4,)),
            dma((4,)),
            dma((2,)),
            dma((2,)),
            dma((4, 6)),
            dma((4, 6)),
            dma((4, 6)),
            dma((4, 6)),
            dma((4, 6)),
            dma((4, 6)),
            dma((3, 3)),
            dma((3, 3)),
            dma((3, 3)),
        ],
        compiler_params=pltpu.CompilerParams(
            collective_id=3, has_side_effects=True, vmem_limit_bytes=64 * 2**20 - 65536
        ),
        name="backward_stage",
    )(dx, dgt, gates, mixed, g, tok, q, kv, att, cos, sin, lens, live, wa, wb, gin, gout, outp)


def fast_local(
    tokens,
    lengths,
    routes,
    prenorm,
    w_query,
    key_value_weight,
    w_output,
    midnorm,
    w_router,
    expert_in,
    expert_out,
    cotangent,
):
    bf, f32 = jnp.bfloat16, jnp.float32
    seqs, token_rows, width = tokens.shape
    dp_rank = lax.axis_index("dp")
    rows = seqs * token_rows
    small = jnp.concatenate(
        [w_router, prenorm[:, None], midnorm[:, None], jnp.zeros((w_router.shape[0], 118), bf)], axis=1
    )
    shard_a = jnp.concatenate([w_query, key_value_weight, small], axis=1)
    positions = dp_rank * token_rows + jnp.arange(token_rows, dtype=jnp.int32)
    cosine_table, sine_table = rope_tables(positions)
    cos_rows = jnp.concatenate([cosine_table, cosine_table], axis=1)
    sin_rows = jnp.concatenate([-sine_table, sine_table], axis=1)
    live = (positions[None, :] < lengths[:, None]).reshape(rows, 1)
    x = tokens.reshape(rows, width)
    g = jnp.where(live, cotangent.reshape(rows, width), 0)
    lens = jnp.broadcast_to(lengths[:, None, None], (seqs, 8, 128))
    full_a, full_b, gall, q_rot, kv_all, attended, mixed, normed2, gates = attention_stage(
        x, shard_a, w_output, g, cos_rows, sin_rows, lens, routes.reshape(rows, TOP)
    )
    gates_t = jnp.transpose(gates[:, :8].reshape(seqs, token_rows, 8), (0, 2, 1))
    dx, dgate_t, outp, gin, gout = expert_stage(
        normed2, gall, gates_t, expert_in[0], expert_out[0]
    )
    live_f = jnp.broadcast_to(live.astype(f32), (rows, 128))
    block_out, grad_tokens, g_a, g_b, g_in, g_out = backward_stage(
        dx, dgate_t, gates, mixed, g, x, q_rot, kv_all, attended, cos_rows, sin_rows, lens, live_f,
        full_a, full_b, gin, gout, outp,
    )[:6]
    return (
        block_out.reshape(seqs, token_rows, width),
        grad_tokens.reshape(seqs, token_rows, width),
        g_a[:, 2056],
        g_a[:, :1536],
        g_a[:, 1536:2048],
        g_b,
        g_a[:, 2057],
        g_a[:, 2048:2056],
        g_in.astype(f32)[None],
        g_out.astype(f32)[None],
    )


def solution(mesh):
    placed = (
        P("expert", "dp", None),
        P("expert"),
        P("expert", "dp", None),
        P(("dp", "expert")),
        P(("dp", "expert"), None),
        P(("dp", "expert"), None),
        P(("dp", "expert"), None),
        P(("dp", "expert")),
        P(("dp", "expert"), None),
        P("expert", "dp", None),
        P("expert", "dp", None),
        P("expert", "dp", None),
    )
    fits = mesh.shape["dp"] == 4 and mesh.shape["expert"] == 8
    return jax.shard_map(
        fast_local if fits else local,
        mesh=mesh,
        in_specs=placed,
        out_specs=(
            P("expert", "dp", None),
            P("expert", "dp", None),
            P(("dp", "expert")),
            P(("dp", "expert"), None),
            P(("dp", "expert"), None),
            P(("dp", "expert"), None),
            P(("dp", "expert")),
            P(("dp", "expert"), None),
            P("expert", "dp", None),
            P("expert", "dp", None),
        ),
        check_vma=False,
    )
```

```python
import jax
import jax.numpy as jnp
import numpy as np
from jax import lax
from jax.experimental import pallas as pl
from jax.experimental.pallas import tpu as pltpu
from jax.sharding import PartitionSpec as P

QUERY_HEADS = 12
KEY_VALUE_HEADS = 2
HEAD_SIZE = 128
FF = 768
TOP = 4


epsilon = 1e-06
rope_base = 10000.0
highest = lax.Precision.HIGHEST


def rope_tables(positions):
    half_width = HEAD_SIZE // 2
    inv_freq = rope_base ** (-(jnp.arange(half_width, dtype=jnp.float32) * 2.0 / HEAD_SIZE))
    angles = positions.astype(jnp.float32)[:, None] * inv_freq[None, :]
    return (jnp.cos(angles), jnp.sin(angles))


def apply_rotation(values, cosine_table, sine_table):
    half_width = values.shape[-1] // 2
    first_half = values[..., :half_width]
    second = values[..., half_width:]
    cos_rows = cosine_table[:, None, :]
    sin_rows = sine_table[:, None, :]
    return jnp.concatenate(
        [first_half * cos_rows - second * sin_rows, second * cos_rows + first_half * sin_rows],
        axis=-1,
    )


def unrotate(values, cosine_table, sine_table):
    half_width = values.shape[-1] // 2
    first_half = values[..., :half_width]
    second = values[..., half_width:]
    cos_rows = cosine_table[:, None, :]
    sin_rows = sine_table[:, None, :]
    return jnp.concatenate(
        [first_half * cos_rows + second * sin_rows, second * cos_rows - first_half * sin_rows],
        axis=-1,
    )


def rms_parts(values):
    inverse = lax.rsqrt(jnp.mean(values * values, axis=-1, keepdims=True) + epsilon)
    return (values * inverse, inverse)


def norm_back(grad_normed, normalized_input, inverse, gain):
    scaled = grad_normed * gain
    return inverse * (
        scaled - normalized_input * jnp.mean(scaled * normalized_input, axis=-1, keepdims=True)
    )


def slot_index(route_rows, expert_count, capacity):
    flat_routes = route_rows.reshape(-1)
    onehot = (flat_routes[:, None] == jnp.arange(expert_count, dtype=jnp.int32)[None, :]).astype(
        jnp.int32
    )
    before = jnp.cumsum(onehot, axis=0) - onehot
    within = jnp.sum(before * onehot, axis=-1)
    return flat_routes * capacity + within


def masked_scores(query_matrix, key_rows, allowed):
    scores = jnp.einsum(
        "qhgd,khd->hgqk", query_matrix, key_rows, preferred_element_type=jnp.float32
    ) * HEAD_SIZE ** (-0.5)
    return jnp.where(allowed[None, None], scores, -1e30)


def local(
    tokens,
    lengths,
    routes,
    prenorm,
    w_query,
    key_value_weight,
    w_output,
    midnorm,
    w_router,
    expert_in,
    expert_out,
    cotangent,
):
    micro_count, token_rows, hidden_width = tokens.shape
    dp_size = lax.axis_size("dp")
    expert_size = lax.axis_size("expert")
    dp_rank = lax.axis_index("dp")
    local_experts = expert_in.shape[0]
    expert_count = local_experts * expert_size
    capacity = max(2, 3 * token_rows * TOP // (2 * expert_count))
    query_group_width = QUERY_HEADS // KEY_VALUE_HEADS
    expert_slot_total = token_rows * dp_size
    score_scale = HEAD_SIZE ** (-0.5)
    positions = dp_rank * token_rows + jnp.arange(token_rows, dtype=jnp.int32)
    key_pos = jnp.arange(expert_slot_total, dtype=jnp.int32)
    cosine_table, sine_table = rope_tables(positions)
    total_prenorm = jnp.zeros((hidden_width,), jnp.float32)
    total_query = jnp.zeros((hidden_width, QUERY_HEADS * HEAD_SIZE), jnp.float32)
    total_key_value = jnp.zeros((hidden_width, 2 * KEY_VALUE_HEADS * HEAD_SIZE), jnp.float32)
    total_output = jnp.zeros((QUERY_HEADS * HEAD_SIZE, hidden_width), jnp.float32)
    total_midnorm = jnp.zeros((hidden_width,), jnp.float32)
    total_router = jnp.zeros((hidden_width, expert_count), jnp.float32)
    total_upper = jnp.zeros((local_experts, hidden_width, 2 * FF), jnp.float32)
    total_down = jnp.zeros((local_experts, FF, hidden_width), jnp.float32)
    outputs_list = []
    grads_list = []
    for micro_step in range(micro_count):
        dense_all = (
            lax.all_gather(prenorm, ("dp", "expert"), axis=0, tiled=True),
            lax.all_gather(w_query, ("dp", "expert"), axis=0, tiled=True),
            lax.all_gather(key_value_weight, ("dp", "expert"), axis=0, tiled=True),
            lax.all_gather(w_output, ("dp", "expert"), axis=0, tiled=True),
            lax.all_gather(midnorm, ("dp", "expert"), axis=0, tiled=True),
            lax.all_gather(w_router, ("dp", "expert"), axis=0, tiled=True),
        )
        expert_all = (
            lax.all_gather(expert_in, "dp", axis=1, tiled=True),
            lax.all_gather(expert_out, "dp", axis=1, tiled=True),
        )
        gain_one = dense_all[0].astype(jnp.float32)
        query_all = dense_all[1]
        keyval_all = dense_all[2]
        output_all = dense_all[3]
        gain_two = dense_all[4].astype(jnp.float32)
        router_all = dense_all[5]
        gateup_all = expert_all[0]
        down_all = expert_all[1]
        input_rows = tokens[micro_step].astype(jnp.float32)
        length = lengths[micro_step]
        route_rows = routes[micro_step]
        live_rows = (positions < length)[:, None]
        normed_one, inverse_one = rms_parts(input_rows)
        normalized_input = (normed_one * gain_one).astype(jnp.bfloat16)
        query_pre = jnp.dot(
            normalized_input, query_all, preferred_element_type=jnp.float32
        ).reshape(token_rows, QUERY_HEADS, HEAD_SIZE)
        keyval_pre = jnp.dot(
            normalized_input, keyval_all, preferred_element_type=jnp.float32
        ).reshape(token_rows, 2, KEY_VALUE_HEADS, HEAD_SIZE)
        query_matrix = (
            apply_rotation(query_pre, cosine_table, sine_table)
            .astype(jnp.bfloat16)
            .reshape(token_rows, KEY_VALUE_HEADS, query_group_width, HEAD_SIZE)
        )
        local_key_rows = apply_rotation(keyval_pre[:, 0], cosine_table, sine_table).astype(
            jnp.bfloat16
        )
        local_value_rows = keyval_pre[:, 1].astype(jnp.bfloat16)
        packed_tokens = jnp.stack([local_key_rows, local_value_rows], axis=1).reshape(
            token_rows, 2 * KEY_VALUE_HEADS * HEAD_SIZE
        )
        gathered_rows = lax.all_gather(packed_tokens, "dp", axis=0, tiled=True).reshape(
            expert_slot_total, 2, KEY_VALUE_HEADS, HEAD_SIZE
        )
        key_rows = gathered_rows[:, 0]
        value_rows = gathered_rows[:, 1]
        allowed = (key_pos[None, :] <= positions[:, None]) & (key_pos[None, :] < length)
        scores = masked_scores(query_matrix, key_rows, allowed)
        top_score = jnp.max(scores, axis=-1, keepdims=True)
        weights = jnp.exp(scores - top_score)
        weight_total = jnp.sum(weights, axis=-1, keepdims=True)
        log_total = top_score + jnp.log(weight_total)
        probs_low = (weights / weight_total).astype(jnp.bfloat16)
        attended = jnp.einsum(
            "hgqk,khd->qhgd", probs_low, value_rows, preferred_element_type=jnp.float32
        )
        attended = attended.reshape(token_rows, QUERY_HEADS * HEAD_SIZE).astype(jnp.bfloat16)
        mixed_rows = input_rows + jnp.dot(attended, output_all, preferred_element_type=jnp.float32)
        normed_mid, inverse_two = rms_parts(mixed_rows)
        normed_two = (normed_mid * gain_two).astype(jnp.bfloat16)
        logits = jnp.dot(normed_two, router_all, preferred_element_type=jnp.float32)
        onehot = (
            route_rows[:, :, None] == jnp.arange(expert_count, dtype=jnp.int32)[None, None, :]
        ).astype(jnp.float32)
        chosen = jnp.sum(onehot * logits[:, None, :], axis=-1)
        gate_values = jax.nn.softmax(chosen, axis=-1)
        slot_idx = slot_index(route_rows, expert_count, capacity)
        send_rows = jnp.zeros((expert_count * capacity, hidden_width), jnp.bfloat16)
        send_rows = send_rows.at[slot_idx].set(jnp.repeat(normed_two, TOP, axis=0))
        received = lax.all_to_all(
            send_rows.reshape(expert_count, capacity, hidden_width),
            "expert",
            split_axis=0,
            concat_axis=0,
            tiled=True,
        )
        item_count = received.shape[1]
        grouped = received.reshape(expert_size, local_experts, item_count, hidden_width)
        gate_up = jnp.einsum(
            "slcd,ldf->slcf", grouped, gateup_all, preferred_element_type=jnp.float32
        )
        hidden = (jax.nn.silu(gate_up[..., :FF]) * gate_up[..., FF:]).astype(jnp.bfloat16)
        result = jnp.einsum(
            "slcf,lfd->slcd", hidden, down_all, preferred_element_type=jnp.float32
        ).astype(jnp.bfloat16)
        back_rows = lax.all_to_all(
            result.reshape(expert_count, item_count, hidden_width),
            "expert",
            split_axis=0,
            concat_axis=0,
            tiled=True,
        )
        back_rows, kept_rows, kept_gateup = (
            back_rows,
            received,
            gate_up.reshape(expert_count, item_count, 2 * FF),
        )
        returned = back_rows.reshape(expert_count * capacity, hidden_width)[slot_idx].reshape(
            token_rows, TOP, hidden_width
        )
        returned_wide = returned.astype(jnp.float32)
        expert_sum = jnp.sum(gate_values[:, :, None] * returned_wide, axis=1)
        final_rows = jnp.where(live_rows, mixed_rows + expert_sum, 0.0)
        outputs_list.append(final_rows.astype(jnp.bfloat16))
        grad_rows = jnp.where(live_rows, cotangent[micro_step].astype(jnp.float32), 0.0)
        grad_gate = jnp.sum(grad_rows[:, None, :] * returned_wide, axis=-1)
        grad_chosen = gate_values * (
            grad_gate - jnp.sum(gate_values * grad_gate, axis=-1, keepdims=True)
        )
        grad_logits = jnp.sum(onehot * grad_chosen[:, :, None], axis=1)
        router_term = jnp.dot(normed_two.astype(jnp.float32).T, grad_logits, precision=highest)
        grad_normtwo = jnp.dot(grad_logits, router_all.astype(jnp.float32).T, precision=highest)
        grad_result = (
            (gate_values[:, :, None] * grad_rows[:, None, :])
            .astype(jnp.bfloat16)
            .reshape(token_rows * TOP, hidden_width)
        )
        send_grads = (
            jnp.zeros((expert_count * capacity, hidden_width), jnp.bfloat16)
            .at[slot_idx]
            .set(grad_result)
        )
        recv_grads, again_rows = (
            lax.all_to_all(
                send_grads.reshape(expert_count, capacity, hidden_width),
                "expert",
                split_axis=0,
                concat_axis=0,
                tiled=True,
            ),
            lax.all_to_all(
                send_rows.reshape(expert_count, capacity, hidden_width),
                "expert",
                split_axis=0,
                concat_axis=0,
                tiled=True,
            ),
        )
        grouped_rows = again_rows.reshape(expert_size, local_experts, capacity, hidden_width)
        gate_up = jnp.einsum(
            "slcd,ldf->slcf", grouped_rows, gateup_all, preferred_element_type=jnp.float32
        )
        grouped_grads = recv_grads.reshape(expert_size, local_experts, capacity, hidden_width)
        gate_part = gate_up[..., :FF]
        up_part = gate_up[..., FF:]
        sigmoid_gate = jax.nn.sigmoid(gate_part)
        silu_gate = gate_part * sigmoid_gate
        hidden = (silu_gate * up_part).astype(jnp.bfloat16)
        grad_hidden = jnp.einsum(
            "slcd,lfd->slcf", grouped_grads, down_all, preferred_element_type=jnp.float32
        )
        down_term = jnp.einsum(
            "slcf,slcd->lfd", hidden, grouped_grads, preferred_element_type=jnp.float32
        )
        grad_gatepart = (
            grad_hidden * up_part * sigmoid_gate * (1.0 + gate_part * (1.0 - sigmoid_gate))
        )
        grad_gateup = jnp.concatenate([grad_gatepart, grad_hidden * silu_gate], axis=-1).astype(
            jnp.bfloat16
        )
        upper_term = jnp.einsum(
            "slcd,slcf->ldf", grouped_rows, grad_gateup, preferred_element_type=jnp.float32
        )
        grad_copies = jnp.einsum(
            "slcf,ldf->slcd", grad_gateup, gateup_all, preferred_element_type=jnp.float32
        ).astype(jnp.bfloat16)
        back_grads = lax.all_to_all(
            grad_copies.reshape(expert_count, capacity, hidden_width),
            "expert",
            split_axis=0,
            concat_axis=0,
            tiled=True,
        )
        copy_rows = back_grads.reshape(expert_count * capacity, hidden_width)[slot_idx].reshape(
            token_rows, TOP, hidden_width
        )
        grad_normtwo = grad_normtwo + jnp.sum(copy_rows.astype(jnp.float32), axis=1)
        midnorm_term = jnp.sum(grad_normtwo * normed_mid, axis=0)
        grad_mixed = grad_rows + norm_back(grad_normtwo, normed_mid, inverse_two, gain_two)
        grad_proj = grad_mixed.astype(jnp.bfloat16)
        output_term = jnp.dot(attended.T, grad_proj, preferred_element_type=jnp.float32)
        attention_gradient = jnp.dot(
            grad_proj, output_all.T, preferred_element_type=jnp.float32
        ).astype(jnp.bfloat16)
        attention_gradient = attention_gradient.reshape(
            token_rows, KEY_VALUE_HEADS, query_group_width, HEAD_SIZE
        )
        scores = masked_scores(query_matrix, key_rows, allowed)
        prob_rows = jnp.exp(scores - log_total)
        grad_probs = jnp.einsum(
            "qhgd,khd->hgqk", attention_gradient, value_rows, preferred_element_type=jnp.float32
        )
        row_delta = jnp.sum(prob_rows * grad_probs, axis=-1, keepdims=True)
        grad_scores = (prob_rows * (grad_probs - row_delta)).astype(jnp.bfloat16)
        prob_low = prob_rows.astype(jnp.bfloat16)
        grad_qrot = (
            jnp.einsum("hgqk,khd->qhgd", grad_scores, key_rows, preferred_element_type=jnp.float32)
            * score_scale
        )
        grad_keys = (
            jnp.einsum(
                "hgqk,qhgd->khd", grad_scores, query_matrix, preferred_element_type=jnp.float32
            )
            * score_scale
        )
        grad_vals = jnp.einsum(
            "hgqk,qhgd->khd", prob_low, attention_gradient, preferred_element_type=jnp.float32
        )
        own_keys = (
            lax.psum_scatter(
                jnp.stack([grad_keys, grad_vals], axis=1)
                .reshape(lax.axis_size("dp") * token_rows, 2 * KEY_VALUE_HEADS * HEAD_SIZE)
                .astype(jnp.bfloat16),
                "dp",
                scatter_dimension=0,
                tiled=True,
            )
            .astype(jnp.float32)
            .reshape(token_rows, 2, KEY_VALUE_HEADS, HEAD_SIZE)
        )
        grad_query = (
            unrotate(
                grad_qrot.reshape(token_rows, QUERY_HEADS, HEAD_SIZE), cosine_table, sine_table
            )
            .astype(jnp.bfloat16)
            .reshape(token_rows, QUERY_HEADS * HEAD_SIZE)
        )
        key_gradient = unrotate(own_keys[:, 0], cosine_table, sine_table).astype(jnp.bfloat16)
        value_gradient = own_keys[:, 1].astype(jnp.bfloat16)
        key_value_weight_gradient = jnp.stack([key_gradient, value_gradient], axis=1).reshape(
            token_rows, 2 * KEY_VALUE_HEADS * HEAD_SIZE
        )
        query_term = jnp.dot(normalized_input.T, grad_query, preferred_element_type=jnp.float32)
        keyval_term = jnp.dot(
            normalized_input.T, key_value_weight_gradient, preferred_element_type=jnp.float32
        )
        grad_normone = jnp.dot(grad_query, query_all.T, preferred_element_type=jnp.float32)
        grad_normone = grad_normone + jnp.dot(
            key_value_weight_gradient, keyval_all.T, preferred_element_type=jnp.float32
        )
        prenorm_term = jnp.sum(grad_normone * normed_one, axis=0)
        grads_list.append(grad_mixed + norm_back(grad_normone, normed_one, inverse_one, gain_one))
        total_prenorm = total_prenorm + prenorm_term
        total_query = total_query + query_term
        total_key_value = total_key_value + keyval_term
        total_output = total_output + output_term
        total_midnorm = total_midnorm + midnorm_term
        total_router = total_router + router_term
        total_upper = total_upper + upper_term
        total_down = total_down + down_term
    dense_grads = (
        lax.psum_scatter(total_prenorm, ("dp", "expert"), scatter_dimension=0, tiled=True),
        lax.psum_scatter(total_query, ("dp", "expert"), scatter_dimension=0, tiled=True),
        lax.psum_scatter(total_key_value, ("dp", "expert"), scatter_dimension=0, tiled=True),
        lax.psum_scatter(total_output, ("dp", "expert"), scatter_dimension=0, tiled=True),
        lax.psum_scatter(total_midnorm, ("dp", "expert"), scatter_dimension=0, tiled=True),
        lax.psum_scatter(total_router, ("dp", "expert"), scatter_dimension=0, tiled=True),
    )
    expert_grads = (
        lax.psum_scatter(
            total_upper.astype(jnp.bfloat16), "dp", scatter_dimension=1, tiled=True
        ).astype(jnp.float32),
        lax.psum_scatter(
            total_down.astype(jnp.bfloat16), "dp", scatter_dimension=1, tiled=True
        ).astype(jnp.float32),
    )
    return (
        jnp.stack(outputs_list),
        jnp.stack(grads_list),
        dense_grads[0],
        dense_grads[1],
        dense_grads[2],
        dense_grads[3],
        dense_grads[4],
        dense_grads[5],
        expert_grads[0],
        expert_grads[1],
    )


MESH = pl.DeviceIdType.MESH
CHUNK = 256
PIECE = 96


def remote(src, dst, send_sem, recv_sem, target):
    return pltpu.make_async_remote_copy(
        src_ref=src,
        dst_ref=dst,
        send_sem=send_sem,
        recv_sem=recv_sem,
        device_id=target,
        device_id_type=MESH,
    )


def place():
    d = lax.axis_index("dp")
    e = lax.axis_index("expert")
    z = lax.div(e, 2)
    c = lax.rem(e, 2)
    x = lax.rem(d, 2)
    y = lax.div(d, 2)
    return d, e, z, c, x, y


def attention_kernel(
    tok_ref,
    wq_hbm,
    wkv_hbm,
    wr_ref,
    pre_ref,
    mid_ref,
    wb_hbm,
    cot_ref,
    wo_hbm,
    rope_hbm,
    lens_ref,
    routes_ref,
    wa_out,
    wb_out,
    wo_out,
    gall,
    q_out,
    kv_out,
    att_out,
    mixed_out,
    normed_out,
    gates_out,
    wa,
    wb,
    qs,
    kvs,
    att,
    g_own,
    rope,
    own_sem,
    wo_recv,
    wo_send,
    z_recv,
    z_send,
    xy_recv,
    xy_send,
    sib_recv,
    sib_send,
    g_recv,
    g_send,
    gs_recv,
    gs_send,
    kv_recv,
    kv_send,
):
    bf, f32 = jnp.bfloat16, jnp.float32
    d, e, z, c, x, y = place()
    d_x = d + 1 - 2 * x
    d_y = d + 2 - 4 * y
    d_d = 3 - d
    other = 1 - c
    to_x = (d_x, e)
    to_y = (d_y, e)
    to_sib = (d, 2 * z + other)
    to_up = (d, e + jnp.where(z < 3, 2, -2))
    to_down = (d, e + jnp.where(z > 0, -2, 2))

    barrier = pltpu.get_barrier_semaphore()
    for target in (to_x, to_y, to_sib):
        pl.semaphore_signal(barrier, inc=1, device_id=target, device_id_type=MESH)

    @pl.when(z < 3)
    def _():
        pl.semaphore_signal(barrier, inc=1, device_id=to_up, device_id_type=MESH)

    @pl.when(z > 0)
    def _():
        pl.semaphore_signal(barrier, inc=1, device_id=to_down, device_id_type=MESH)

    own_at = pl.multiple_of((d * 8 + e) * 48, 16)
    own_rows = pl.ds(own_at, 48)
    own_a = [
        pltpu.make_async_copy(wq_hbm, wa.at[own_rows, pl.ds(0, 1536)], own_sem.at[0]),
        pltpu.make_async_copy(wkv_hbm, wa.at[own_rows, pl.ds(1536, 512)], own_sem.at[1]),
        pltpu.make_async_copy(rope_hbm.at[:, pl.ds(pl.multiple_of(d * 128, 128), 128)], rope, own_sem.at[2]),
    ]
    for copy in own_a:
        copy.start()
    eye = lax.broadcasted_iota(jnp.int32, (128, 128), 0) == lax.broadcasted_iota(
        jnp.int32, (128, 128), 1
    )
    eye_low = eye.astype(bf)
    turned = (((0,), (0,)), ((), ()))
    sub = lax.broadcasted_iota(jnp.int32, (8, 48), 0)
    gains = jnp.where(
        sub == 0,
        pre_ref[...].astype(f32),
        jnp.where(sub == 1, mid_ref[...].astype(f32), 0.0),
    )
    tile = jnp.concatenate([wr_ref[...].astype(f32), gains], axis=0).astype(bf)
    wa[own_rows, 2048:] = lax.dot_general(
        tile, eye_low[:16], turned, preferred_element_type=f32
    ).astype(bf)
    for s in range(2):
        rows = slice(s * 128, (s + 1) * 128)
        slot = d * 128 + lax.broadcasted_iota(jnp.int32, (128, 1), 0)
        g_own[rows] = jnp.where(slot < lens_ref[s], cot_ref[rows].astype(f32), 0.0).astype(bf)

    full = (wa, wb)
    shard = (None, wb_hbm)

    def block(a, dd, zp, lane):
        at = pl.multiple_of((dd * 8 + 2 * zp + lane) * 48, 16)
        return full[a].at[pl.ds(at, 48)]

    def z_copy(a, zp, way, src=None):
        ref = block(a, d, zp, c)
        return remote(
            ref if src is None else src,
            ref,
            z_send.at[a, way, zp],
            z_recv.at[a, zp],
            to_up if way == 0 else to_down,
        )

    def xy_copy(a, dd, zp, row, target, src=None):
        ref = block(a, dd, zp, c)
        return remote(
            ref if src is None else src,
            ref,
            xy_send.at[a, row, zp],
            xy_recv.at[a, row, zp],
            target,
        )

    def s_copy(a, dd, zp, src=None, lane=None):
        ref = block(a, dd, zp, c if lane is None else lane)
        return remote(
            ref if src is None else src,
            ref,
            sib_send.at[a, dd, zp],
            sib_recv.at[a, dd, zp],
            to_sib,
        )

    def send_xy(a, zp):
        xy_copy(a, d, zp, 0, to_x).start()
        xy_copy(a, d, zp, 1, to_y).start()

    def own_start(a):
        @pl.when(z < 3)
        def _():
            z_copy(a, z, 0, shard[a]).start()

        @pl.when(z > 0)
        def _():
            z_copy(a, z, 1, shard[a]).start()

        s_copy(a, d, z, shard[a]).start()

    def from_z(a, k):
        def arrived(zp, way):
            z_copy(a, zp, way).wait_recv()

            @pl.when((z < 3) if way == 0 else (z > 0))
            def _():
                z_copy(a, zp, way).start()

            if a == 0:
                send_xy(a, zp)
            s_copy(a, d, zp).start()

        @pl.when(z - k >= 0)
        def _():
            arrived(z - k, 0)

        @pl.when(z + k <= 3)
        def _():
            arrived(z + k, 1)

    def from_xy_one(a, zp):
        xy_copy(a, d_x, zp, 0, to_x).wait_recv()

        @pl.when(lax.rem(zp, 2) == 0)
        def _():
            xy_copy(a, d_x, zp, 2, to_y).start()

        s_copy(a, d_x, zp).start()
        xy_copy(a, d_y, zp, 1, to_y).wait_recv()

        @pl.when(lax.rem(zp, 2) == 1)
        def _():
            xy_copy(a, d_y, zp, 2, to_x).start()

        s_copy(a, d_y, zp).start()

    def from_xy(a, k):
        @pl.when(z - k >= 0)
        def _():
            from_xy_one(a, z - k)

        if k > 0:

            @pl.when(z + k <= 3)
            def _():
                from_xy_one(a, z + k)

    def from_diag(a):
        for k in range(4):
            zp = lax.rem(z + k, 4)
            xy_copy(a, d_d, zp, 2, to_x).wait_recv()
            s_copy(a, d_d, zp).start()

    def from_sib(a):
        for dd in range(4):
            for zp in range(4):
                s_copy(a, dd, zp, lane=other).wait_recv()

    def drain(a):
        for zp in range(4):
            for dd in range(4):
                s_copy(a, dd, zp).wait_send()
            for row in range(3):
                xy_copy(a, d, zp, row, to_x).wait_send()

            @pl.when((zp <= z) & (z < 3))
            def _():
                z_copy(a, zp, 0).wait_send()

            @pl.when((zp >= z) & (z > 0))
            def _():
                z_copy(a, zp, 1).wait_send()

    def g_part(zp, lane, s):
        at = pl.multiple_of((2 * zp + lane) * CHUNK + s * 128, 128)
        return gall.at[pl.ds(at, 128)]

    def g_copy(zp, s, way, src=None):
        ref = g_part(zp, c, s)
        return remote(
            ref if src is None else src,
            ref,
            g_send.at[way, zp, s],
            g_recv.at[zp, s],
            to_up if way == 0 else to_down,
        )

    def gs_copy(zp, s, src=None, lane=None):
        ref = g_part(zp, c if lane is None else lane, s)
        return remote(
            ref if src is None else src, ref, gs_send.at[zp, s], gs_recv.at[zp, s], to_sib
        )

    def g_start():
        for s in range(2):
            src = g_own.at[pl.ds(s * 128, 128)]

            @pl.when(z < 3)
            def _():
                g_copy(z, s, 0, src).start()

            @pl.when(z > 0)
            def _():
                g_copy(z, s, 1, src).start()

            gs_copy(z, s, src).start()

    def g_pass(k, s):
        @pl.when(z - k >= 0)
        def _():
            g_copy(z - k, s, 0).wait_recv()

            @pl.when(z < 3)
            def _():
                g_copy(z - k, s, 0).start()

            gs_copy(z - k, s).start()

        @pl.when(z + k <= 3)
        def _():
            g_copy(z + k, s, 1).wait_recv()

            @pl.when(z > 0)
            def _():
                g_copy(z + k, s, 1).start()

            gs_copy(z + k, s).start()

    def wo_copy(dd, p, row, target, src=None):
        ref = wo_out.at[pl.ds(pl.multiple_of(dd * 192 + p * PIECE, 16), PIECE)]
        return remote(
            ref if src is None else src, ref, wo_send.at[row, p], wo_recv.at[row, p], target
        )

    def wo_start():
        for p in range(2):
            src = wo_hbm.at[pl.ds(p * PIECE, PIECE)]
            wo_copy(d, p, 0, to_x, src).start()
            wo_copy(d, p, 1, to_y, src).start()

    def wo_pass():
        wo_copy(d_x, 0, 0, to_x).wait_recv()
        wo_copy(d_x, 0, 2, to_y).start()
        wo_copy(d_y, 1, 1, to_y).wait_recv()
        wo_copy(d_y, 1, 2, to_x).start()

    def wo_rest():
        wo_copy(d_x, 1, 0, to_x).wait_recv()
        wo_copy(d_y, 0, 1, to_y).wait_recv()
        for p in range(2):
            wo_copy(d_d, p, 2, to_x).wait_recv()

    pl.semaphore_wait(barrier, 5 - jnp.where((z == 0) | (z == 3), 1, 0))
    for copy in own_a:
        copy.wait()
    own_start(0)
    own_start(1)
    own = [
        pltpu.make_async_copy(wb_hbm, block(1, d, z, c), own_sem.at[0]),
        pltpu.make_async_copy(
            g_own, gall.at[pl.ds(pl.multiple_of(e * CHUNK, CHUNK), CHUNK)], own_sem.at[1]
        ),
        pltpu.make_async_copy(
            wo_hbm, wo_out.at[pl.ds(pl.multiple_of(d * 192, 16), 192)], own_sem.at[2]
        ),
    ]
    for copy in own:
        copy.start()
    send_xy(0, z)
    tok = tok_ref[...].astype(f32)
    n1 = tok * lax.rsqrt(jnp.mean(tok * tok, axis=1, keepdims=True) + epsilon)
    from_z(0, 1)
    from_z(1, 1)
    from_xy(0, 0)
    from_z(0, 2)
    from_z(1, 2)
    g_start()
    from_xy(0, 1)
    from_z(0, 3)
    from_z(1, 3)
    from_xy(0, 2)
    from_xy(0, 3)

    def turn(j):
        return lax.rem(z + j, 4)

    own[0].wait()
    for j in range(2):
        send_xy(1, turn(j))
    from_diag(0)
    from_sib(0)

    small_t = lax.dot_general(
        eye_low[:16], wa[:, 2048:], (((1,), (1,)), ((), ())), preferred_element_type=f32
    )
    normed = (n1 * small_t[8:9]).astype(bf)
    cos_rows = jnp.concatenate([rope[0]] * 2, axis=0)
    sin_rows = jnp.concatenate([rope[1]] * 2, axis=0)

    def rotate(v):
        return v * cos_rows + pltpu.roll(v, 64, 1) * sin_rows

    kv = jnp.dot(normed, wa[:, 1536:2048], preferred_element_type=f32)
    for h in range(2):
        kvs[d, :, h * 128 : (h + 1) * 128] = rotate(kv[:, h * 128 : (h + 1) * 128]).astype(bf)
    kvs[d, :, 256:] = kv[:, 256:].astype(bf)

    def kv_copy(dd, s, row, target):
        ref = kvs.at[dd, pl.ds(s * 128, 128)]
        return remote(ref, ref, kv_send.at[row, s], kv_recv.at[row, s], target)

    for s in range(2):
        kv_copy(d, s, 0, to_x).start()
        kv_copy(d, s, 1, to_y).start()
    g_pass(1, 0)
    q = jnp.dot(normed, wa[:, :1536], preferred_element_type=f32)
    for head in range(QUERY_HEADS):
        rot = rotate(q[:, head * 128 : (head + 1) * 128]).astype(bf)
        for s in range(2):
            at = (s * QUERY_HEADS + head) * 128
            qs[at : at + 128] = rot[s * 128 : (s + 1) * 128]
    kv_copy(d_x, 0, 0, to_x).wait_recv()
    kv_copy(d_x, 0, 2, to_y).start()
    kv_copy(d_y, 1, 1, to_y).wait_recv()
    kv_copy(d_y, 1, 2, to_x).start()
    for j in range(2, 4):
        send_xy(1, turn(j))
    for j in range(2):
        from_xy_one(1, turn(j))
    g_pass(1, 1)
    kv_copy(d_y, 0, 1, to_y).wait_recv()
    kv_copy(d_x, 1, 0, to_x).wait_recv()
    for s in range(2):
        kv_copy(d_d, s, 2, to_x).wait_recv()
    q_copy = pltpu.make_async_copy(qs, q_out, own_sem.at[3])
    kvo_copy = pltpu.make_async_copy(kvs, kv_out, own_sem.at[4])
    wa_copy = pltpu.make_async_copy(wa, wa_out, own_sem.at[5])
    for copy in (q_copy, kvo_copy, wa_copy):
        copy.start()

    query_pos = d * 128 + lax.broadcasted_iota(jnp.int32, (128, 512), 0)
    key_pos = lax.broadcasted_iota(jnp.int32, (128, 512), 1)

    def attend(n):
        s = lax.div(n, 2)
        h = lax.rem(n, 2)
        lens = lens_ref[s]
        allowed = (key_pos <= query_pos) & (key_pos < lens)
        ks = kvs[:, pl.ds(pl.multiple_of(s * 128, 128), 128), pl.ds(pl.multiple_of(h * 128, 128), 128)]
        vs = kvs[:, pl.ds(pl.multiple_of(s * 128, 128), 128), pl.ds(pl.multiple_of(256 + h * 128, 128), 128)]
        ks = ks.reshape(512, 128)
        vs = vs.reshape(512, 128)
        for half in range(2):
            qh = qs[pl.ds(pl.multiple_of(n * 768 + half * 384, 128), 384)]
            scores = lax.dot_general(qh, ks, (((1,), (1,)), ((), ())), preferred_element_type=f32)
            scores = scores.reshape(3, 128, 512) * HEAD_SIZE ** (-0.5)
            scores = jnp.where(allowed[None], scores, -1e30)
            top = jnp.max(scores, axis=-1, keepdims=True)
            weights = jnp.exp(scores - top)
            weights = weights * (1.0 / jnp.sum(weights, axis=-1, keepdims=True))
            out = jnp.dot(
                weights.astype(bf).reshape(384, 512), vs, preferred_element_type=f32
            ).astype(bf)
            for j in range(3):
                att[
                    pl.ds(pl.multiple_of(s * 128, 128), 128),
                    pl.ds(pl.multiple_of(h * 768 + (half * 3 + j) * 128, 128), 128),
                ] = out[j * 128 : (j + 1) * 128]

    pl.loop(0, 2)(attend)
    g_pass(2, 0)
    from_xy_one(1, turn(2))
    pl.loop(2, 4)(attend)
    from_xy_one(1, turn(3))
    wo_start()
    g_pass(2, 1)
    from_diag(1)
    from_sib(1)
    att_copy = pltpu.make_async_copy(att, att_out, own_sem.at[6])
    wb_copy = pltpu.make_async_copy(wb, wb_out, own_sem.at[7])
    att_copy.start()
    wb_copy.start()
    mixed = tok_ref[...].astype(f32) + jnp.dot(att[...], wb[...], preferred_element_type=f32)
    mixed_out[...] = mixed
    n2 = mixed * lax.rsqrt(jnp.mean(mixed * mixed, axis=1, keepdims=True) + epsilon)
    normed2 = (n2 * small_t[9:10]).astype(bf)
    normed_out[...] = normed2
    logits = lax.dot_general(
        small_t[:8].astype(bf), normed2, (((1,), (1,)), ((), ())), preferred_element_type=f32
    )
    number = lax.broadcasted_iota(jnp.int32, (8, 128), 0)
    for s in range(2):
        chosen = number == routes_ref[s, 0:1]
        for t in range(1, TOP):
            chosen = chosen | (number == routes_ref[s, t : t + 1])
        picked = jnp.where(chosen, logits[:, s * 128 : (s + 1) * 128], -1e30)
        top = jnp.max(picked, axis=0, keepdims=True)
        weights = jnp.where(chosen, jnp.exp(picked - top), 0.0)
        gates_out[s] = weights / jnp.sum(weights, axis=0, keepdims=True)

    g_pass(3, 0)
    wo_pass()
    g_pass(3, 1)
    wo_rest()
    for zp in range(4):
        for s in range(2):
            gs_copy(zp, s, lane=other).wait_recv()
    own[1].wait()
    own[2].wait()
    for copy in (q_copy, kvo_copy, wa_copy, att_copy, wb_copy):
        copy.wait()
    drain(0)
    drain(1)
    for s in range(2):
        for row in range(3):
            kv_copy(d, s, row, to_x).wait_send()
            wo_copy(d, s, row, to_x).wait_send()
        for zp in range(4):
            gs_copy(zp, s).wait_send()

            @pl.when((zp <= z) & (z < 3))
            def _():
                g_copy(zp, s, 0).wait_send()

            @pl.when((zp >= z) & (z > 0))
            def _():
                g_copy(zp, s, 1).wait_send()


def attention_stage(tok, wq, wkv, wr, pre, mid, wb, cot, wo, rope, lens, routes):
    bf, f32 = jnp.bfloat16, jnp.float32
    shape = jax.ShapeDtypeStruct
    width = tok.shape[-1]
    wide = wq.shape[-1] + wkv.shape[-1] + 128
    hbm = pl.BlockSpec(memory_space=pltpu.HBM)
    vmem = pl.BlockSpec(memory_space=pltpu.VMEM)
    smem = pl.BlockSpec(memory_space=pltpu.SMEM)
    dma = pltpu.SemaphoreType.DMA
    return pl.pallas_call(
        attention_kernel,
        out_shape=(
            shape((width, wide), bf),
            shape((width, width), bf),
            shape((FF, width), bf),
            shape((8 * CHUNK, width), bf),
            shape((2 * QUERY_HEADS * 128, 128), bf),
            shape((4, CHUNK, 512), bf),
            shape((CHUNK, width), bf),
            shape((CHUNK, width), f32),
            shape((CHUNK, width), bf),
            shape((2, 8, 128), f32),
        ),
        in_specs=[vmem, hbm, hbm, vmem, vmem, vmem, hbm, vmem, hbm, hbm, smem, vmem],
        out_specs=[hbm] * 7 + [vmem] * 3,
        scratch_shapes=[
            pltpu.VMEM((width, wide), bf),
            pltpu.VMEM((width, width), bf),
            pltpu.VMEM((2 * QUERY_HEADS * 128, 128), bf),
            pltpu.VMEM((4, CHUNK, 512), bf),
            pltpu.VMEM((CHUNK, width), bf),
            pltpu.VMEM((CHUNK, width), bf),
            pltpu.VMEM((2, 128, 128), f32),
            dma((8,)),
            dma((3, 2)),
            dma((3, 2)),
            dma((2, 4)),
            dma((2, 2, 4)),
            dma((2, 3, 4)),
            dma((2, 3, 4)),
            dma((2, 4, 4)),
            dma((2, 4, 4)),
            dma((4, 2)),
            dma((2, 4, 2)),
            dma((4, 2)),
            dma((4, 2)),
            dma((3, 2)),
            dma((3, 2)),
        ],
        compiler_params=pltpu.CompilerParams(
            collective_id=2, has_side_effects=True, vmem_limit_bytes=60 * 2**20
        ),
        name="attention_stage",
    )(tok, wq, wkv, wr, pre, mid, wb, cot, wo, rope, lens, routes)


def expert_kernel(
    x_hbm,
    g_hbm,
    gt_hbm,
    win_hbm,
    wout_hbm,
    dx_out,
    dgt_out,
    outp_hbm,
    gin_hbm,
    gout_out,
    win,
    wout,
    xall,
    gall,
    gtall,
    dgu,
    hg,
    dxb,
    dgb,
    sibr,
    sibg,
    ro,
    rog,
    ri,
    rig,
    stage,
    gout,
    tg,
    xg,
    yg,
    own_sem,
    stage_sem,
    g_recv,
    g_send,
    w_recv,
    w_send,
    ag_recv,
    ag_send,
    sib_recv,
    sib_send,
    red_recv,
    red_send,
):
    bf, f32 = jnp.bfloat16, jnp.float32
    d, e, z, c, x, y = place()
    d_x = d + 1 - 2 * x
    d_y = d + 2 - 4 * y
    d_d = 3 - d
    hi = lax.div(z, 2)
    zz = z * hi + (3 - z) * (1 - hi)
    other = 1 - c
    to_x = (d_x, e)
    to_y = (d_y, e)
    to_sib = (d, 2 * z + other)
    to_up = (d, e + jnp.where(z < 3, 2, -2))
    to_down = (d, e + jnp.where(z > 0, -2, 2))
    e_in = e + 2 - 4 * hi
    to_in = (d, e_in)
    to_out = (d, jnp.where(zz == 2, e - 2 + 4 * hi, e_in))
    mid = zz == 2
    end = zz == 3

    barrier = pltpu.get_barrier_semaphore()
    for target in (to_x, to_y, to_sib, to_in):
        pl.semaphore_signal(barrier, inc=1, device_id=target, device_id_type=MESH)

    @pl.when(mid)
    def _():
        pl.semaphore_signal(barrier, inc=1, device_id=to_out, device_id_type=MESH)

    own_copies = [
        pltpu.make_async_copy(x_hbm.at[s], xall.at[e, s], own_sem.at[s]) for s in range(2)
    ] + [
        pltpu.make_async_copy(gt_hbm, gtall.at[e], own_sem.at[2]),
        pltpu.make_async_copy(
            win_hbm, win.at[pl.ds(pl.multiple_of(d * 384, 16), 384)], own_sem.at[3]
        ),
        pltpu.make_async_copy(wout_hbm, wout, own_sem.at[4]),
        pltpu.make_async_copy(g_hbm, gall, own_sem.at[5]),
    ]
    pl.semaphore_wait(barrier, 7 - zz)

    gathered = ((x_hbm, xall), (gt_hbm, gtall))

    def ag_copy(a, zp, s, way, src=None):
        ref = gathered[a][1].at[2 * zp + c, s]
        return remote(
            ref if src is None else src,
            ref,
            ag_send.at[way, a, zp, s],
            ag_recv.at[a, zp, s],
            to_up if way == 0 else to_down,
        )

    def sib_copy(a, zp, s, src=None, lane=None):
        ref = gathered[a][1].at[2 * zp + (c if lane is None else lane), s]
        return remote(
            ref if src is None else src,
            ref,
            sib_send.at[a, zp, s],
            sib_recv.at[a, zp, s],
            to_sib,
        )

    def own_rows(s):
        for a in range(2):
            src = gathered[a][0].at[s]

            @pl.when(z < 3)
            def _():
                ag_copy(a, z, s, 0, src).start()

            @pl.when(z > 0)
            def _():
                ag_copy(a, z, s, 1, src).start()

            sib_copy(a, z, s, src).start()

    def pass_on(k, s):
        for a in range(2):

            @pl.when(z - k >= 0)
            def _():
                ag_copy(a, z - k, s, 0).wait_recv()

                @pl.when(z < 3)
                def _():
                    ag_copy(a, z - k, s, 0).start()

                sib_copy(a, z - k, s).start()

            @pl.when(z + k <= 3)
            def _():
                ag_copy(a, z + k, s, 1).wait_recv()

                @pl.when(z > 0)
                def _():
                    ag_copy(a, z + k, s, 1).start()

                sib_copy(a, z + k, s).start()

    def from_sib(s):
        for a in range(2):
            for zp in range(4):
                sib_copy(a, zp, s, lane=other).wait_recv()

    def w_copy(p, src_d, target, row, src=None):
        ref = win.at[pl.ds(pl.multiple_of(src_d * 384 + p * PIECE, 16), PIECE)]
        return remote(
            ref if src is None else src, ref, w_send.at[row, p], w_recv.at[row, p], target
        )

    def w_pass(p):
        w_copy(p, d_x, to_x, 0).wait_recv()
        if p % 2 == 0:
            w_copy(p, d_x, to_y, 3).start()
        w_copy(p, d_y, to_y, 1).wait_recv()
        if p % 2 == 1:
            w_copy(p, d_y, to_x, 2).start()

    own_rows(0)
    for p in range(4):
        src = win_hbm.at[pl.ds(p * PIECE, PIECE)]
        w_copy(p, d, to_x, 0, src).start()
        w_copy(p, d, to_y, 1, src).start()
    for copy in own_copies:
        copy.start()
    w_pass(0)
    pass_on(1, 0)
    w_pass(1)
    pass_on(2, 0)
    own_rows(1)
    w_pass(2)
    w_pass(3)
    pass_on(3, 0)
    pass_on(1, 1)
    from_sib(0)
    for p in range(4):
        if p % 2 == 0:
            w_copy(p, d_d, to_y, 3).wait_recv()
        else:
            w_copy(p, d_d, to_x, 2).wait_recv()
    for copy in own_copies:
        copy.wait()

    def order(i):
        v = i if i < 2 else (5 - zz if i == 2 else zz)
        return v * hi + (3 - v) * (1 - hi)

    def sib_sum(zp, s, a):
        src, dst = ((dxb, sibr), (dgb, sibg))[a]
        return remote(
            src.at[2 * zp + other, s], dst.at[zp, s], red_send.at[a, zp, s], red_recv.at[a, zp, s], to_sib
        )

    def hop(i, s, target, inward):
        dst, dstg, row = (ro, rog, 2) if inward else (ri, rig, 4)
        zp = order(i)
        return (
            remote(
                dxb.at[2 * zp + c, s], dst.at[i, s], red_send.at[2, i, s], red_recv.at[row, i, s], target
            ),
            remote(
                dgb.at[2 * zp + c, s], dstg.at[i, s], red_send.at[3, i, s], red_recv.at[row + 1, i, s], target
            ),
        )

    def wait_from(ref, refg, slot, s, row):
        remote(
            ref.at[slot, s], ref.at[slot, s], red_send.at[2, slot, s], red_recv.at[row, slot, s], to_in
        ).wait_recv()
        remote(
            refg.at[slot, s], refg.at[slot, s], red_send.at[3, slot, s], red_recv.at[row + 1, slot, s], to_in
        ).wait_recv()

    def combine(i, s, incoming):
        zp = order(i)
        for a in range(2):
            remote(
                sibr.at[zp, s] if a == 0 else sibg.at[zp, s],
                sibr.at[zp, s] if a == 0 else sibg.at[zp, s],
                red_send.at[a, zp, s],
                red_recv.at[a, zp, s],
                to_sib,
            ).wait_recv()
        for ref, refg, slot, row in incoming:
            wait_from(ref, refg, slot, s, row)
        total = dxb[2 * zp + c, s].astype(f32) + sibr[zp, s].astype(f32)
        totalg = dgb[2 * zp + c, s] + sibg[zp, s]
        for ref, refg, slot, row in incoming:
            total = total + ref[slot, s].astype(f32)
            totalg = totalg + refg[slot, s]
        return total, totalg

    def pass_sum(i, s, incoming, target, inward):
        total, totalg = combine(i, s, incoming)
        zp = order(i)
        dxb[2 * zp + c, s] = total.astype(bf)
        dgb[2 * zp + c, s] = totalg
        for copy in hop(i, s, target, inward):
            copy.start()

    def end_sums(s, which):
        @pl.when(end)
        def _():
            for i in which:
                pass_sum(i, s, (), to_in, True)

    def mid_sum(i, s):
        @pl.when(mid)
        def _():
            if i < 2:
                pass_sum(i, s, ((ro, rog, i, 2),), to_in, False)
            else:
                pass_sum(2, s, ((ri, rig, 0, 4),), to_out, False)

    def last_sum(s):
        @pl.when(mid)
        def _():
            total, totalg = combine(3, s, ((ro, rog, 2, 2), (ri, rig, 1, 4)))
            dx_out[s * 128 : (s + 1) * 128] = total
            dgt_out[s] = totalg

        @pl.when(end)
        def _():
            total, totalg = combine(3, s, ((ri, rig, 2, 4),))
            dx_out[s * 128 : (s + 1) * 128] = total
            dgt_out[s] = totalg

    eye = lax.broadcasted_iota(jnp.int32, (128, 128), 0) == lax.broadcasted_iota(
        jnp.int32, (128, 128), 1
    )
    mine = lax.broadcasted_iota(jnp.int32, (8, 128), 0) == e
    nt = (((1,), (1,)), ((), ()))
    tn = (((0,), (0,)), ((), ()))

    def expert_step(s, pair):
        first = 4 * pair if pair is not None else 0
        block = pl.ds(first, 4)
        xc = xall[block, s].reshape(512, 1536)
        gate = jnp.dot(xc, win[:, :FF], preferred_element_type=f32)
        up = jnp.dot(xc, win[:, FF:], preferred_element_type=f32)
        back = lax.dot_general(
            gall[block, s].reshape(512, 1536), wout[...], nt, preferred_element_type=f32
        )
        columns = []
        for j in range(4):
            row = jnp.sum(jnp.where(mine, gtall[first + j, s], 0.0), axis=0, keepdims=True)
            columns.append(jnp.sum(jnp.where(eye, row, 0.0), axis=1, keepdims=True))
        weight = jnp.concatenate(columns, axis=0)
        sig = jax.nn.sigmoid(gate)
        silu = gate * sig
        hidden = (silu * up).astype(bf).astype(f32)
        dgate = jnp.sum(hidden * back, axis=1, keepdims=True)
        for j in range(4):
            row = jnp.sum(
                jnp.where(eye, dgate[j * 128 : (j + 1) * 128], 0.0), axis=0, keepdims=True
            )
            dgb[first + j, s] = jnp.where(mine, row, 0.0)
        hgv = (hidden * weight).astype(bf)
        hg[block, s] = hgv.reshape(4, 128, FF)
        back = back * weight
        dgu[block, s, :, :FF] = (
            (back * up * (sig * (1.0 + gate * (1.0 - sig)))).astype(bf).reshape(4, 128, FF)
        )
        dgu[block, s, :, FF:] = (back * silu).astype(bf).reshape(4, 128, FF)
        dxb[block, s] = (
            lax.dot_general(
                dgu[block, s].reshape(512, 1536), win[...], nt, preferred_element_type=f32
            )
            .astype(bf)
            .reshape(4, 128, 1536)
        )
        for j in range(2):
            for a in range(2):
                sib_sum(lax.div(first, 2) + j, s, a).start()

    def out_copy(slot, s, first):
        return pltpu.make_async_copy(
            stage.at[slot], outp_hbm.at[pl.ds(first, 4), s], stage_sem.at[slot]
        )

    def out_step(slot, s, pair):
        first = 4 * pair
        stage[slot] = (
            jnp.dot(
                hg[pl.ds(first, 4), s].reshape(512, FF), wout[...], preferred_element_type=f32
            )
            .astype(bf)
            .reshape(4, 128, 1536)
        )
        out_copy(slot, s, first).start()

    far = 1 - hi
    near = hi

    @pl.loop(0, 4)
    def _(t):
        s = lax.div(t, 2)
        pair = far + lax.rem(t, 2) * (1 - 2 * far)
        expert_step(s, pair)

        @pl.when(t == 0)
        def _():
            pass_on(2, 1)
            out_step(0, 0, far)
            end_sums(0, (0, 1))

        @pl.when(t == 1)
        def _():
            pass_on(3, 1)
            from_sib(1)
            out_step(1, 0, near)
            end_sums(0, (2,))
            mid_sum(0, 0)

        @pl.when(t == 2)
        def _():
            out_copy(0, 0, 0).wait()
            out_step(0, 1, far)
            end_sums(1, (0, 1))
            mid_sum(1, 0)
            mid_sum(2, 0)

        @pl.when(t == 3)
        def _():
            out_copy(1, 0, 0).wait()
            out_step(1, 1, near)
            end_sums(1, (2,))
            mid_sum(0, 1)

    def g_piece(dd, p):
        return gout.at[pl.ds(pl.multiple_of(dd * 192 + p * PIECE, 16), PIECE)]

    def g_diag(p):
        return remote(g_piece(d_d, p), tg.at[p], g_send.at[0, p], g_recv.at[0, p], (to_x, to_y)[p])

    def g_direct(p):
        if p == 0:
            return remote(g_piece(d_x, p), xg.at[p], g_send.at[1, p], g_recv.at[1, p], to_x)
        return remote(g_piece(d_y, p), yg.at[p], g_send.at[1, p], g_recv.at[2, p], to_y)

    def g_summed(p):
        if p == 0:
            return remote(g_piece(d_y, p), yg.at[p], g_send.at[2, p], g_recv.at[2, p], to_y)
        return remote(g_piece(d_x, p), xg.at[p], g_send.at[2, p], g_recv.at[1, p], to_x)

    def g_middle(p):
        g_diag(p).wait_recv()
        rows = pl.ds(pl.multiple_of((d_y if p == 0 else d_x) * 192 + p * PIECE, 16), PIECE)
        gout[rows] = (gout[rows].astype(f32) + tg[p].astype(f32)).astype(bf)
        g_summed(p).start()

    for k in range(2):
        at = k * 384
        gout[at : at + 384] = lax.dot_general(
            hg[:, :, :, at : at + 384].reshape(2048, 384),
            gall[...].reshape(2048, 1536),
            tn,
            preferred_element_type=f32,
        ).astype(bf)
    for p in range(2):
        g_diag(p).start()
    for p in range(2):
        g_direct(p).start()

    def grad_copy(k):
        return pltpu.make_async_copy(
            stage.at[k % 2, pl.ds(0, 3)], gin_hbm.at[k], stage_sem.at[k % 2]
        )

    for k in range(4):
        if k < 2:
            out_copy(k, 0, 0).wait()
        else:
            grad_copy(k - 2).wait()
        stage[k % 2, :3] = (
            lax.dot_general(
                xall[:, :, :, k * 384 : (k + 1) * 384].reshape(2048, 384),
                dgu[...].reshape(2048, 1536),
                tn,
                preferred_element_type=f32,
            )
            .astype(bf)
            .reshape(3, 128, 1536)
        )
        grad_copy(k).start()
        if k == 0:
            mid_sum(1, 1)
        if k == 1:
            for p in range(2):
                g_middle(p)
        if k == 2:
            mid_sum(2, 1)
            last_sum(0)

    for p in range(2):
        remote(xg.at[p], xg.at[p], g_send.at[1, p], g_recv.at[1, p], to_x).wait_recv()
        remote(yg.at[p], yg.at[p], g_send.at[1, p], g_recv.at[2, p], to_y).wait_recv()
        rows = pl.ds(pl.multiple_of(d * 192 + p * PIECE, 16), PIECE)
        gout_out[p * PIECE : (p + 1) * PIECE] = (
            gout[rows].astype(f32) + xg[p].astype(f32) + yg[p].astype(f32)
        ).astype(bf)
    for k in (2, 3):
        grad_copy(k).wait()
    last_sum(1)

    for p in range(2):
        for copy in (g_diag(p), g_direct(p), g_summed(p)):
            copy.wait_send()
    for p in range(4):
        w_copy(p, d, to_x, 0).wait_send()
        w_copy(p, d, to_y, 1).wait_send()
        if p % 2 == 0:
            w_copy(p, d_x, to_y, 3).wait_send()
        else:
            w_copy(p, d_y, to_x, 2).wait_send()
    for s in range(2):
        for zp in range(4):
            for a in range(2):
                sib_copy(a, zp, s).wait_send()
                sib_sum(zp, s, a).wait_send()

                @pl.when((zp <= z) & (z < 3))
                def _():
                    ag_copy(a, zp, s, 0).wait_send()

                @pl.when((zp >= z) & (z > 0))
                def _():
                    ag_copy(a, zp, s, 1).wait_send()

        for i in range(3):
            for copy in hop(i, s, to_in, True):
                copy.wait_send()


def expert_stage(rows, grads, gates_t, w_in, w_out):
    bf, f32 = jnp.bfloat16, jnp.float32
    shape = jax.ShapeDtypeStruct
    width = rows.shape[-1]
    hbm = pl.BlockSpec(memory_space=pltpu.HBM)
    vmem = pl.BlockSpec(memory_space=pltpu.VMEM)
    dma = pltpu.SemaphoreType.DMA
    return pl.pallas_call(
        expert_kernel,
        out_shape=(
            shape((CHUNK, width), f32),
            shape((2, 8, 128), f32),
            shape((8, 2, 128, width), bf),
            shape((4, 3, 128, 2 * FF), bf),
            shape((FF // 4, width), bf),
        ),
        in_specs=[hbm] * 5,
        out_specs=(vmem, vmem, hbm, hbm, vmem),
        scratch_shapes=[
            pltpu.VMEM((width, 2 * FF), bf),
            pltpu.VMEM((FF, width), bf),
            pltpu.VMEM((8, 2, 128, width), bf),
            pltpu.VMEM((8, 2, 128, width), bf),
            pltpu.VMEM((8, 2, 8, 128), f32),
            pltpu.VMEM((8, 2, 128, 2 * FF), bf),
            pltpu.VMEM((8, 2, 128, FF), bf),
            pltpu.VMEM((8, 2, 128, width), bf),
            pltpu.VMEM((8, 2, 8, 128), f32),
            pltpu.VMEM((4, 2, 128, width), bf),
            pltpu.VMEM((4, 2, 8, 128), f32),
            pltpu.VMEM((3, 2, 128, width), bf),
            pltpu.VMEM((3, 2, 8, 128), f32),
            pltpu.VMEM((3, 2, 128, width), bf),
            pltpu.VMEM((3, 2, 8, 128), f32),
            pltpu.VMEM((2, 4, 128, width), bf),
            pltpu.VMEM((FF, width), bf),
            *([pltpu.VMEM((2, PIECE, width), bf)] * 3),
            dma((6,)),
            dma((2,)),
            dma((3, 2)),
            dma((3, 2)),
            dma((4, 4)),
            dma((4, 4)),
            dma((2, 4, 2)),
            dma((2, 2, 4, 2)),
            dma((2, 4, 2)),
            dma((2, 4, 2)),
            dma((6, 4, 2)),
            dma((4, 4, 2)),
        ],
        compiler_params=pltpu.CompilerParams(
            collective_id=1, has_side_effects=True, vmem_limit_bytes=63 * 2**20
        ),
        name="expert_stage",
    )(
        rows.reshape(2, 128, width),
        grads.reshape(8, 2, 128, width),
        gates_t,
        w_in,
        w_out,
    )


def backward_kernel(
    dx_ref,
    dgt_ref,
    gates_ref,
    mixed_ref,
    cot_ref,
    tok_ref,
    q_ref,
    kv_ref,
    att_ref,
    lens_ref,
    rope_hbm,
    wa_hbm,
    wb_hbm,
    gin_hbm,
    outp_hbm,
    block_out,
    dtok_out,
    gq_out,
    gb_out,
    gkv_out,
    small_out,
    ein_out,
    osib,
    oro,
    ori,
    wide,
    small,
    gq,
    gb,
    gk,
    sib_q,
    sib_b,
    sib_k,
    tq,
    xq,
    yq,
    roq,
    riq,
    tb,
    xb,
    yb,
    rob,
    rib,
    tw,
    xw,
    yw,
    row_,
    riw,
    te,
    xe,
    ye,
    le,
    old,
    oslot,
    dat,
    dkv,
    tk,
    xk,
    yk,
    rope,
    load_sem,
    le_sem,
    old_sem,
    os_recv,
    os_send,
    ds_recv,
    ds_send,
    t_recv,
    x_recv,
    y_recv,
    t_send,
    d_send,
    s_send,
    ro_recv,
    ri_recv,
    hop_send,
):
    bf, f32 = jnp.bfloat16, jnp.float32
    d, e, z, c, x, y = place()
    d_x = d + 1 - 2 * x
    d_y = d + 2 - 4 * y
    d_d = 3 - d
    hi = lax.div(z, 2)
    zz = z * hi + (3 - z) * (1 - hi)
    other = 1 - c
    mid = zz == 2
    end = zz == 3
    to_x = (d_x, e)
    to_y = (d_y, e)
    to_sib = (d, 2 * z + other)
    e_in = e + 2 - 4 * hi
    to_in = (d, e_in)
    to_out = (d, jnp.where(zz == 2, e - 2 + 4 * hi, e_in))

    dqs = block_out
    dmix = dtok_out

    barrier = pltpu.get_barrier_semaphore()
    for target in (to_x, to_y, to_sib, to_in):
        pl.semaphore_signal(barrier, inc=1, device_id=target, device_id_type=MESH)

    @pl.when(mid)
    def _():
        pl.semaphore_signal(barrier, inc=1, device_id=to_out, device_id_type=MESH)

    pl.semaphore_wait(barrier, 7 - zz)

    def order(i):
        v = i if i < 2 else (5 - zz if i == 2 else zz)
        return v * hi + (3 - v) * (1 - hi)

    def across(k, src, t, fx, fy):
        def diag(i):
            return remote(
                src(d_d, i), t.at[i], t_send.at[k, i], t_recv.at[k, i], (to_x, to_y)[i % 2]
            )

        def direct(i):
            if i % 2 == 0:
                return remote(src(d_x, i), fx.at[i], d_send.at[k, i], x_recv.at[k, i], to_x)
            return remote(src(d_y, i), fy.at[i], d_send.at[k, i], y_recv.at[k, i], to_y)

        def summed(i, ref):
            if i % 2 == 0:
                return remote(ref, fy.at[i], s_send.at[k, i], y_recv.at[k, i], to_y)
            return remote(ref, fx.at[i], s_send.at[k, i], x_recv.at[k, i], to_x)

        def wait_t(i):
            remote(t.at[i], t.at[i], t_send.at[k, i], t_recv.at[k, i], to_x).wait_recv()

        def wait_xy(i):
            remote(fx.at[i], fx.at[i], d_send.at[k, i], x_recv.at[k, i], to_x).wait_recv()
            remote(fy.at[i], fy.at[i], d_send.at[k, i], y_recv.at[k, i], to_y).wait_recv()

        def drain(n):
            for i in range(n):
                diag(i).wait_send()
                direct(i).wait_send()
                summed(i, t.at[i]).wait_send()

        return diag, direct, summed, wait_t, wait_xy, drain

    def along(k, slot, ro, ri):
        def send(i, target, dst, recv):
            return remote(slot(i), dst.at[i], hop_send.at[k, i], recv.at[k, i], target)

        def to_ro(i):
            return send(i, to_in, ro, ro_recv)

        def to_ri(i):
            return send(i, to_in if i < 2 else to_out, ri, ri_recv)

        def wait_ro(i):
            remote(ro.at[i], ro.at[i], hop_send.at[k, i], ro_recv.at[k, i], to_in).wait_recv()

        def wait_ri(i):
            remote(ri.at[i], ri.at[i], hop_send.at[k, i], ri_recv.at[k, i], to_in).wait_recv()

        def drain():
            for i in range(3):
                to_ro(i).wait_send()

        return to_ro, to_ri, wait_ro, wait_ri, drain

    def expert_src(dd, p):
        return gin_hbm.at[pl.ds(pl.multiple_of(dd * 384 + p * PIECE, 16), PIECE)]

    e_diag, e_direct, e_summed, e_wait_t, e_wait_xy, e_drain = across(0, expert_src, te, xe, ye)

    def e_load(p, dd, j):
        return pltpu.make_async_copy(expert_src(dd, p), le.at[j], le_sem.at[j])

    def e_middle(p):
        load = e_load(p, d_y if p % 2 == 0 else d_x, 0)
        load.start()
        e_wait_t(p)
        load.wait()
        te[p] = (te[p].astype(f32) + le[0].astype(f32)).astype(bf)
        e_summed(p, te.at[p]).start()

    def e_final(p):
        load = e_load(p, d, 1)
        load.start()
        e_wait_xy(p)
        load.wait()
        total = le[1].astype(f32) + xe[p].astype(f32) + ye[p].astype(f32)
        ein_out[p * PIECE : (p + 1) * PIECE] = total.astype(bf)

    def store_q(total):
        gq_out[...] = total

    def store_b(total):
        gb_out[...] = total

    def store_k(total):
        gkv_out[...] = total[:, :512]
        small_out[...] = lax.dot_general(
            eye[:16],
            total[:, 512:],
            (((1,), (1,)), ((), ())),
            preferred_element_type=f32,
            precision=highest,
        )

    dense = (
        (gq, sib_q, tq, xq, yq, roq, riq, store_q),
        (gb, sib_b, tb, xb, yb, rob, rib, store_b),
        (gk, sib_k, tw, xw, yw, row_, riw, store_k),
    )

    def dense_stream(j):
        grad, sib, t, fx, fy, ro, ri, out = dense[j]

        def src(dd, i):
            return grad.at[dd * 4 + order(i), c]

        diag, direct, summed, wait_t, wait_xy, drain = across(1 + j, src, t, fx, fy)

        def own_slot(i):
            return grad.at[d * 4 + order(i), c]

        to_ro, to_ri, wait_ro, wait_ri, drain_z = along(j, own_slot, ro, ri)

        def sib_copy():
            return remote(grad.at[:, other], sib, ds_send.at[j], ds_recv.at[j], to_sib)

        def begin():
            sib_copy().wait_recv()

            @pl.loop(0, 16)
            def _(k):
                grad[k, c] = (grad[k, c].astype(f32) + sib[k].astype(f32)).astype(bf)

            for i in range(4):
                diag(i).start()
            for i in range(4):
                direct(i).start()

        def middle(i):
            dd = d_y if i % 2 == 0 else d_x
            wait_t(i)
            at = dd * 4 + order(i)
            grad[at, c] = (grad[at, c].astype(f32) + t[i].astype(f32)).astype(bf)
            summed(i, src(dd, i)).start()

        def local(i):
            return grad[d * 4 + order(i), c].astype(f32) + fx[i].astype(f32) + fy[i].astype(f32)

        def put(i, total):
            grad[d * 4 + order(i), c] = total.astype(bf)

        def last(i):
            wait_xy(i)
            if i == 3:
                return

            @pl.when(end)
            def _():
                put(i, local(i))
                to_ro(i).start()

        def hop(i):
            @pl.when(mid)
            def _():
                if i < 2:
                    wait_ro(i)
                    put(i, local(i) + ro[i].astype(f32))
                else:
                    wait_ri(0)
                    put(2, local(2) + ri[0].astype(f32))
                to_ri(i).start()

        def finish():
            @pl.when(mid)
            def _():
                wait_ro(2)
                wait_ri(1)
                out(local(3) + ro[2].astype(f32) + ri[1].astype(f32))

            @pl.when(end)
            def _():
                wait_ri(2)
                out(local(3) + ri[2].astype(f32))

        def drain_all():
            sib_copy().wait_send()
            drain(4)
            drain_z()

        return sib_copy, begin, middle, last, hop, finish, drain_all

    q_sib, q_begin, q_middle, q_last, q_hop, q_finish, q_drain = dense_stream(0)
    b_sib, b_begin, b_middle, b_last, b_hop, b_finish, b_drain = dense_stream(1)
    w_sib, w_begin, w_middle, w_last, w_hop, w_finish, w_drain = dense_stream(2)

    def out_rows(i, lane):
        return outp_hbm.at[pl.ds(pl.multiple_of((2 * order(i) + lane) * CHUNK, CHUNK), CHUNK)]

    def out_sib(i):
        return remote(out_rows(i, other), osib.at[i], os_send.at[i], os_recv.at[i], to_sib)

    o_ro, o_ri, o_wait_ro, o_wait_ri, o_drain = along(3, lambda i: oslot.at[i], oro, ori)

    def out_sum(i, incoming, store):
        out_sib(i).wait_recv()
        for half in range(2):
            rows = pl.ds(half * 128, 128)
            loads = [
                pltpu.make_async_copy(ref.at[rows], old.at[j], old_sem.at[j])
                for j, ref in enumerate([out_rows(i, c), osib.at[i]] + incoming)
            ]
            for load in loads:
                load.start()
            for load in loads:
                load.wait()
            total = old[0].astype(f32)
            for j in range(1, len(loads)):
                total = total + old[j].astype(f32)
            store(slice(half * 128, (half + 1) * 128), total)

    def out_slot(i):
        def store(rows, total):
            oslot[i, rows] = total.astype(bf)

        return store

    def out_end(i):
        @pl.when(end)
        def _():
            out_sum(i, [], out_slot(i))
            o_ro(i).start()

    def out_mid(i):
        @pl.when(mid)
        def _():
            if i < 2:
                o_wait_ro(i)
                out_sum(i, [oro.at[i]], out_slot(i))
            else:
                o_wait_ri(0)
                out_sum(2, [ori.at[0]], out_slot(2))
            o_ri(i).start()

    def out_finish():
        def store(rows, total):
            total = total + mixed_ref[rows]
            slot = d * 128 + lax.broadcasted_iota(jnp.int32, (128, 1), 0)
            live = slot < lens_ref[rows.start // 128]
            block_out[rows] = jnp.where(live, total, 0.0).astype(bf)

        @pl.when(mid)
        def _():
            o_wait_ro(2)
            o_wait_ri(1)
            out_sum(3, [oro.at[2], ori.at[1]], store)

        @pl.when(end)
        def _():
            o_wait_ri(2)
            out_sum(3, [ori.at[2]], store)

    def kv_src(dd, i):
        return dkv.at[dd, pl.ds(i * 128, 128)]

    k_diag, k_direct, k_summed, k_wait_t, k_wait_xy, k_drain = across(4, kv_src, tk, xk, yk)

    def k_middle(i):
        dd = d_y if i % 2 == 0 else d_x
        k_wait_t(i)
        rows = slice(i * 128, (i + 1) * 128)
        dkv[dd, rows] = (dkv[dd, rows].astype(f32) + tk[i].astype(f32)).astype(bf)
        k_summed(i, kv_src(dd, i)).start()

    small_load = pltpu.make_async_copy(wa_hbm.at[:, pl.ds(2048, 128)], small, load_sem.at[0])
    wb_load = pltpu.make_async_copy(wb_hbm, wide.at[:, pl.ds(0, 1536)], load_sem.at[1])
    wa_load = pltpu.make_async_copy(wa_hbm.at[:, pl.ds(0, 2048)], wide, load_sem.at[2])
    rope_load = pltpu.make_async_copy(
        rope_hbm.at[:, pl.ds(pl.multiple_of(d * 128, 128), 128)], rope, load_sem.at[3]
    )
    small_load.start()
    rope_load.start()
    wb_load.start()
    for p in range(4):
        e_diag(p).start()
    for p in range(4):
        e_direct(p).start()
    for i in range(4):
        out_sib(i).start()

    nt = (((1,), (1,)), ((), ()))
    tn = (((0,), (0,)), ((), ()))

    def dot_nt(a, b):
        return lax.dot_general(a, b, nt, preferred_element_type=f32)

    def dot_tn(a, b):
        return lax.dot_general(a, b, tn, preferred_element_type=f32)

    eye = (
        lax.broadcasted_iota(jnp.int32, (128, 128), 0)
        == lax.broadcasted_iota(jnp.int32, (128, 128), 1)
    ).astype(f32)
    eye_low = eye.astype(bf)
    gates = jnp.concatenate([gates_ref[s] for s in range(2)], axis=1)
    dgate = jnp.concatenate([dgt_ref[s] for s in range(2)], axis=1)
    dlogit = gates * (dgate - jnp.sum(gates * dgate, axis=0, keepdims=True))
    dl_hi = dlogit.astype(bf).astype(f32)
    dl = jnp.concatenate([dl_hi, dlogit - dl_hi], axis=0).astype(bf)
    small_load.wait()
    small_t = dot_nt(eye_low[:16], small[...])
    router = jnp.concatenate([small_t[:8]] * 2, axis=0).astype(bf)
    dn2 = dx_ref[...] + dot_tn(dl, router)
    mixed = mixed_ref[...]
    inv2 = lax.rsqrt(jnp.mean(mixed * mixed, axis=1, keepdims=True) + epsilon)
    n2 = mixed * inv2
    normed2 = (n2 * small_t[9:10]).astype(bf)
    router_sum = jnp.dot(dl, normed2, preferred_element_type=f32)
    router_sum = router_sum[:8] + router_sum[8:]
    mid_sum = jnp.sum(dn2 * n2, axis=0, keepdims=True)
    grads = [
        jnp.where(
            d * 128 + lax.broadcasted_iota(jnp.int32, (128, 1), 0) < lens_ref[s],
            cot_ref[s * 128 : (s + 1) * 128].astype(f32),
            0.0,
        )
        for s in range(2)
    ]
    u = dn2 * small_t[9:10]
    dmixed = jnp.concatenate(grads, axis=0) + inv2 * (u - n2 * jnp.mean(u * n2, axis=1, keepdims=True))
    dmix[...] = dmixed
    dproj = dmixed.astype(bf)
    for r in range(4):
        part = dot_tn(att_ref[:, r * 384 : (r + 1) * 384], dproj)
        gb[4 * r : 4 * r + 4] = part.astype(bf).reshape(4, 2, 48, 1536)
    b_sib().start()
    wb_load.wait()
    datt = dot_nt(dproj, wide[:, :1536]).astype(bf)
    for head in range(QUERY_HEADS):
        for s in range(2):
            at = (s * QUERY_HEADS + head) * 128
            dat[at : at + 128] = datt[s * 128 : (s + 1) * 128, head * 128 : (head + 1) * 128]
    wa_load.start()
    e_middle(0)
    e_middle(1)
    out_end(0)

    query_pos = d * 128 + lax.broadcasted_iota(jnp.int32, (128, 512), 0)
    key_pos = lax.broadcasted_iota(jnp.int32, (128, 512), 1)
    rope_load.wait()
    cos_rows = rope[0]
    sin_rows = rope[1]
    scale = HEAD_SIZE ** (-0.5)

    def unrotate_rows(v, cos, sin):
        return v * cos - pltpu.roll(v, 64, 1) * sin

    @pl.loop(0, 4)
    def _(n):
        s = lax.div(n, 2)
        h = lax.rem(n, 2)
        srow = pl.ds(pl.multiple_of(s * 128, 128), 128)
        kcol = pl.ds(pl.multiple_of(h * 128, 128), 128)
        vcol = pl.ds(pl.multiple_of(256 + h * 128, 128), 128)
        lens = lens_ref[s]
        allowed = (key_pos <= query_pos) & (key_pos < lens)
        ks = kv_ref[:, srow, kcol].reshape(512, 128)
        vs = kv_ref[:, srow, vcol].reshape(512, 128)
        dk = None
        dv = None
        for half in range(2):
            rows = pl.ds(pl.multiple_of(n * 768 + half * 384, 128), 384)
            qh = q_ref[rows]
            dh = dat[rows]
            scores = dot_nt(qh, ks).reshape(3, 128, 512) * scale
            scores = jnp.where(allowed[None], scores, -1e30)
            probs = jnp.exp(scores - jnp.max(scores, axis=-1, keepdims=True))
            probs = probs * (1.0 / jnp.sum(probs, axis=-1, keepdims=True))
            dprobs = dot_nt(dh, vs).reshape(3, 128, 512)
            delta = jnp.sum(probs * dprobs, axis=-1, keepdims=True)
            dscores = (probs * (dprobs - delta)).astype(bf).reshape(384, 512)
            low = probs.astype(bf).reshape(384, 512)
            dq = jnp.dot(dscores, ks, preferred_element_type=f32) * scale
            for j in range(3):
                dqs[srow, pl.ds(pl.multiple_of(h * 768 + (half * 3 + j) * 128, 128), 128)] = (
                    unrotate_rows(dq[j * 128 : (j + 1) * 128], cos_rows, sin_rows).astype(bf)
                )
            dk_part = dot_tn(dscores, qh)
            dv_part = dot_tn(low, dh)
            dk = dk_part if dk is None else dk + dk_part
            dv = dv_part if dv is None else dv + dv_part
        dkv[:, srow, kcol] = (dk * scale).astype(bf).reshape(4, 128, 128)
        dkv[:, srow, vcol] = dv.astype(bf).reshape(4, 128, 128)

    for i in range(2):
        k_diag(i).start()
    for i in range(2):
        k_direct(i).start()

    tok = tok_ref[...].astype(f32)
    inv1 = lax.rsqrt(jnp.mean(tok * tok, axis=1, keepdims=True) + epsilon)
    n1 = tok * inv1
    normed = (n1 * small_t[8:9]).astype(bf)
    for r in range(4):
        part = dot_tn(normed[:, r * 384 : (r + 1) * 384], dqs[...])
        gq[4 * r : 4 * r + 4] = part.astype(bf).reshape(4, 2, 48, 1536)
    q_sib().start()
    k_middle(0)
    k_middle(1)
    b_begin()
    e_middle(2)
    e_middle(3)
    wa_load.wait()
    dn1 = dot_nt(dqs[...], wide[:, :1536])
    out_end(1)
    out_end(2)
    q_begin()

    for i in range(2):
        k_wait_xy(i)
    own = jnp.concatenate(
        [
            dkv[d, i * 128 : (i + 1) * 128].astype(f32) + xk[i].astype(f32) + yk[i].astype(f32)
            for i in range(2)
        ],
        axis=0,
    )
    cos_two = jnp.concatenate([cos_rows] * 2, axis=0)
    sin_two = jnp.concatenate([sin_rows] * 2, axis=0)
    dkv_own = jnp.concatenate(
        [
            unrotate_rows(own[:, h * 128 : (h + 1) * 128], cos_two, sin_two)
            for h in range(2)
        ]
        + [own[:, 256:]],
        axis=1,
    ).astype(bf)
    dn1 = dn1 + dot_nt(dkv_own, wide[:, 1536:])
    pre_sum = jnp.sum(dn1 * n1, axis=0, keepdims=True)
    row8 = lax.broadcasted_iota(jnp.int32, (8, 1536), 0)
    gains = jnp.where(row8 == 0, pre_sum, jnp.where(row8 == 1, mid_sum, 0.0))
    smalls = jnp.concatenate([router_sum, gains], axis=0).astype(bf)
    for r in range(4):
        cols = slice(r * 384, (r + 1) * 384)
        part = dot_tn(normed[:, cols], dkv_own)
        gk[4 * r : 4 * r + 4, :, :, :512] = part.astype(bf).reshape(4, 2, 48, 512)
        part = dot_tn(smalls[:, cols], eye_low[:16])
        gk[4 * r : 4 * r + 4, :, :, 512:] = part.astype(bf).reshape(4, 2, 48, 128)
    w_sib().start()
    u = dn1 * small_t[8:9]
    dtok_out[...] = dmix[...] + inv1 * (u - n1 * jnp.mean(u * n1, axis=1, keepdims=True))

    for i in range(4):
        b_middle(i)
    w_begin()
    out_mid(0)
    for i in range(4):
        q_middle(i)
    for p in range(4):
        e_final(p)
    out_mid(1)
    out_mid(2)
    for i in range(4):
        w_middle(i)
    for i in range(4):
        b_last(i)
        if i < 3:
            b_hop(i)
    for i in range(4):
        q_last(i)
        if i < 3:
            q_hop(i)
    out_finish()
    for i in range(4):
        w_last(i)
        if i < 3:
            w_hop(i)
    b_finish()
    q_finish()
    w_finish()

    e_drain(4)
    k_drain(2)
    q_drain()
    b_drain()
    w_drain()
    o_drain()
    for i in range(4):
        out_sib(i).wait_send()


def backward_stage(dx, dgt, gates, mixed, cot, tok, q, kv, att, lens, rope, wa, wb, gin, outp):
    bf, f32 = jnp.bfloat16, jnp.float32
    shape = jax.ShapeDtypeStruct
    width = tok.shape[-1]
    hbm = pl.BlockSpec(memory_space=pltpu.HBM)
    vmem = pl.BlockSpec(memory_space=pltpu.VMEM)
    smem = pl.BlockSpec(memory_space=pltpu.SMEM)
    dma = pltpu.SemaphoreType.DMA
    widths = (width, width, 640)
    dense = []
    for w in widths:
        dense += [pltpu.VMEM((4, 48, w), bf)] * 3 + [pltpu.VMEM((3, 48, w), bf)] * 2
    return pl.pallas_call(
        backward_kernel,
        out_shape=(
            shape((CHUNK, width), bf),
            shape((CHUNK, width), f32),
            shape((48, width), f32),
            shape((48, width), f32),
            shape((48, 512), f32),
            shape((16, 48), f32),
            shape((384, 2 * FF), bf),
            shape((4, CHUNK, width), bf),
            shape((3, CHUNK, width), bf),
            shape((3, CHUNK, width), bf),
        ),
        in_specs=[vmem] * 9 + [smem] + [hbm] * 5,
        out_specs=[vmem] * 7 + [hbm] * 3,
        scratch_shapes=[
            pltpu.VMEM((width, 2048), bf),
            pltpu.VMEM((width, 128), bf),
            *[pltpu.VMEM((16, 2, 48, w), bf) for w in widths],
            *[pltpu.VMEM((16, 48, w), bf) for w in widths],
            *dense,
            *([pltpu.VMEM((4, PIECE, width), bf)] * 3),
            pltpu.VMEM((2, PIECE, width), bf),
            pltpu.VMEM((4, 128, width), bf),
            pltpu.VMEM((3, CHUNK, width), bf),
            pltpu.VMEM((2 * QUERY_HEADS * 128, 128), bf),
            pltpu.VMEM((4, CHUNK, 512), bf),
            *([pltpu.VMEM((2, 128, 512), bf)] * 3),
            pltpu.VMEM((2, 128, 128), f32),
            dma((4,)),
            dma((2,)),
            dma((4,)),
            dma((4,)),
            dma((4,)),
            dma((3,)),
            dma((3,)),
            dma((5, 4)),
            dma((5, 4)),
            dma((5, 4)),
            dma((5, 4)),
            dma((5, 4)),
            dma((5, 4)),
            dma((4, 3)),
            dma((4, 3)),
            dma((4, 3)),
        ],
        compiler_params=pltpu.CompilerParams(
            collective_id=3, has_side_effects=True, vmem_limit_bytes=64 * 2**20 - 65536
        ),
        name="backward_stage",
    )(dx, dgt, gates, mixed, cot, tok, q, kv, att, lens, rope, wa, wb, gin, outp)


def rope_constant(slots):
    half = HEAD_SIZE // 2
    inv_freq = np.float32(rope_base) ** (-(np.arange(half, dtype=np.float32) * 2.0 / HEAD_SIZE))
    angles = np.arange(slots, dtype=np.float32)[:, None] * inv_freq[None, :].astype(np.float32)
    cos, sin = np.cos(angles), np.sin(angles)
    return np.stack(
        [np.concatenate([cos, cos], axis=1), np.concatenate([-sin, sin], axis=1)]
    ).astype(np.float32)


def fast_local(
    tokens,
    lengths,
    routes,
    prenorm,
    w_query,
    key_value_weight,
    w_output,
    midnorm,
    w_router,
    expert_in,
    expert_out,
    cotangent,
):
    f32 = jnp.float32
    seqs, token_rows, width = tokens.shape
    rows = seqs * token_rows
    tok = tokens.reshape(rows, width)
    cot = cotangent.reshape(rows, width)
    rope = jnp.asarray(rope_constant(token_rows * lax.axis_size("dp")))
    full_a, full_b, full_out, gall, q_rot, kv_all, attended, mixed, normed2, gates = attention_stage(
        tok,
        w_query,
        key_value_weight,
        w_router.T,
        prenorm[None],
        midnorm[None],
        w_output,
        cot,
        expert_out[0],
        rope,
        lengths,
        jnp.transpose(routes, (0, 2, 1)),
    )
    dx, dgate, outp, gin, g_out = expert_stage(normed2, gall, gates, expert_in[0], full_out)
    block_out, grad_tokens, g_query, g_b, g_kv, small, g_in = backward_stage(
        dx, dgate, gates, mixed, cot, tok, q_rot, kv_all, attended, lengths, rope,
        full_a, full_b, gin.reshape(width, 2 * FF), outp.reshape(8 * rows, width),
    )[:7]
    return (
        block_out.reshape(seqs, token_rows, width),
        grad_tokens.reshape(seqs, token_rows, width),
        small[8],
        g_query,
        g_kv,
        g_b,
        small[9],
        small[:8].T,
        g_in.astype(f32)[None],
        g_out.astype(f32)[None],
    )


def solution(mesh):
    placed = (
        P("expert", "dp", None),
        P("expert"),
        P("expert", "dp", None),
        P(("dp", "expert")),
        P(("dp", "expert"), None),
        P(("dp", "expert"), None),
        P(("dp", "expert"), None),
        P(("dp", "expert")),
        P(("dp", "expert"), None),
        P("expert", "dp", None),
        P("expert", "dp", None),
        P("expert", "dp", None),
    )
    fits = mesh.shape["dp"] == 4 and mesh.shape["expert"] == 8
    return jax.shard_map(
        fast_local if fits else local,
        mesh=mesh,
        in_specs=placed,
        out_specs=(
            P("expert", "dp", None),
            P("expert", "dp", None),
            P(("dp", "expert")),
            P(("dp", "expert"), None),
            P(("dp", "expert"), None),
            P(("dp", "expert"), None),
            P(("dp", "expert")),
            P(("dp", "expert"), None),
            P("expert", "dp", None),
            P("expert", "dp", None),
        ),
        check_vma=False,
    )
```

```python
import jax
import jax.numpy as jnp
import numpy as np
from jax import lax
from jax.experimental import pallas as pl
from jax.experimental.pallas import tpu as pltpu
from jax.sharding import PartitionSpec as P

QUERY_HEADS = 12
KEY_VALUE_HEADS = 2
HEAD_SIZE = 128
FF = 768
TOP = 4


epsilon = 1e-06
rope_base = 10000.0
highest = lax.Precision.HIGHEST


def rope_tables(positions):
    half_width = HEAD_SIZE // 2
    inv_freq = rope_base ** (-(jnp.arange(half_width, dtype=jnp.float32) * 2.0 / HEAD_SIZE))
    angles = positions.astype(jnp.float32)[:, None] * inv_freq[None, :]
    return (jnp.cos(angles), jnp.sin(angles))


def apply_rotation(values, cosine_table, sine_table):
    half_width = values.shape[-1] // 2
    first_half = values[..., :half_width]
    second = values[..., half_width:]
    cos_rows = cosine_table[:, None, :]
    sin_rows = sine_table[:, None, :]
    return jnp.concatenate(
        [first_half * cos_rows - second * sin_rows, second * cos_rows + first_half * sin_rows],
        axis=-1,
    )


def unrotate(values, cosine_table, sine_table):
    half_width = values.shape[-1] // 2
    first_half = values[..., :half_width]
    second = values[..., half_width:]
    cos_rows = cosine_table[:, None, :]
    sin_rows = sine_table[:, None, :]
    return jnp.concatenate(
        [first_half * cos_rows + second * sin_rows, second * cos_rows - first_half * sin_rows],
        axis=-1,
    )


def rms_parts(values):
    inverse = lax.rsqrt(jnp.mean(values * values, axis=-1, keepdims=True) + epsilon)
    return (values * inverse, inverse)


def norm_back(grad_normed, normalized_input, inverse, gain):
    scaled = grad_normed * gain
    return inverse * (
        scaled - normalized_input * jnp.mean(scaled * normalized_input, axis=-1, keepdims=True)
    )


def slot_index(route_rows, expert_count, capacity):
    flat_routes = route_rows.reshape(-1)
    onehot = (flat_routes[:, None] == jnp.arange(expert_count, dtype=jnp.int32)[None, :]).astype(
        jnp.int32
    )
    before = jnp.cumsum(onehot, axis=0) - onehot
    within = jnp.sum(before * onehot, axis=-1)
    return flat_routes * capacity + within


def masked_scores(query_matrix, key_rows, allowed):
    scores = jnp.einsum(
        "qhgd,khd->hgqk", query_matrix, key_rows, preferred_element_type=jnp.float32
    ) * HEAD_SIZE ** (-0.5)
    return jnp.where(allowed[None, None], scores, -1e30)


def local(
    tokens,
    lengths,
    routes,
    prenorm,
    w_query,
    key_value_weight,
    w_output,
    midnorm,
    w_router,
    expert_in,
    expert_out,
    cotangent,
):
    micro_count, token_rows, hidden_width = tokens.shape
    dp_size = lax.axis_size("dp")
    expert_size = lax.axis_size("expert")
    dp_rank = lax.axis_index("dp")
    local_experts = expert_in.shape[0]
    expert_count = local_experts * expert_size
    capacity = max(2, 3 * token_rows * TOP // (2 * expert_count))
    query_group_width = QUERY_HEADS // KEY_VALUE_HEADS
    expert_slot_total = token_rows * dp_size
    score_scale = HEAD_SIZE ** (-0.5)
    positions = dp_rank * token_rows + jnp.arange(token_rows, dtype=jnp.int32)
    key_pos = jnp.arange(expert_slot_total, dtype=jnp.int32)
    cosine_table, sine_table = rope_tables(positions)
    total_prenorm = jnp.zeros((hidden_width,), jnp.float32)
    total_query = jnp.zeros((hidden_width, QUERY_HEADS * HEAD_SIZE), jnp.float32)
    total_key_value = jnp.zeros((hidden_width, 2 * KEY_VALUE_HEADS * HEAD_SIZE), jnp.float32)
    total_output = jnp.zeros((QUERY_HEADS * HEAD_SIZE, hidden_width), jnp.float32)
    total_midnorm = jnp.zeros((hidden_width,), jnp.float32)
    total_router = jnp.zeros((hidden_width, expert_count), jnp.float32)
    total_upper = jnp.zeros((local_experts, hidden_width, 2 * FF), jnp.float32)
    total_down = jnp.zeros((local_experts, FF, hidden_width), jnp.float32)
    outputs_list = []
    grads_list = []
    for micro_step in range(micro_count):
        dense_all = (
            lax.all_gather(prenorm, ("dp", "expert"), axis=0, tiled=True),
            lax.all_gather(w_query, ("dp", "expert"), axis=0, tiled=True),
            lax.all_gather(key_value_weight, ("dp", "expert"), axis=0, tiled=True),
            lax.all_gather(w_output, ("dp", "expert"), axis=0, tiled=True),
            lax.all_gather(midnorm, ("dp", "expert"), axis=0, tiled=True),
            lax.all_gather(w_router, ("dp", "expert"), axis=0, tiled=True),
        )
        expert_all = (
            lax.all_gather(expert_in, "dp", axis=1, tiled=True),
            lax.all_gather(expert_out, "dp", axis=1, tiled=True),
        )
        gain_one = dense_all[0].astype(jnp.float32)
        query_all = dense_all[1]
        keyval_all = dense_all[2]
        output_all = dense_all[3]
        gain_two = dense_all[4].astype(jnp.float32)
        router_all = dense_all[5]
        gateup_all = expert_all[0]
        down_all = expert_all[1]
        input_rows = tokens[micro_step].astype(jnp.float32)
        length = lengths[micro_step]
        route_rows = routes[micro_step]
        live_rows = (positions < length)[:, None]
        normed_one, inverse_one = rms_parts(input_rows)
        normalized_input = (normed_one * gain_one).astype(jnp.bfloat16)
        query_pre = jnp.dot(
            normalized_input, query_all, preferred_element_type=jnp.float32
        ).reshape(token_rows, QUERY_HEADS, HEAD_SIZE)
        keyval_pre = jnp.dot(
            normalized_input, keyval_all, preferred_element_type=jnp.float32
        ).reshape(token_rows, 2, KEY_VALUE_HEADS, HEAD_SIZE)
        query_matrix = (
            apply_rotation(query_pre, cosine_table, sine_table)
            .astype(jnp.bfloat16)
            .reshape(token_rows, KEY_VALUE_HEADS, query_group_width, HEAD_SIZE)
        )
        local_key_rows = apply_rotation(keyval_pre[:, 0], cosine_table, sine_table).astype(
            jnp.bfloat16
        )
        local_value_rows = keyval_pre[:, 1].astype(jnp.bfloat16)
        packed_tokens = jnp.stack([local_key_rows, local_value_rows], axis=1).reshape(
            token_rows, 2 * KEY_VALUE_HEADS * HEAD_SIZE
        )
        gathered_rows = lax.all_gather(packed_tokens, "dp", axis=0, tiled=True).reshape(
            expert_slot_total, 2, KEY_VALUE_HEADS, HEAD_SIZE
        )
        key_rows = gathered_rows[:, 0]
        value_rows = gathered_rows[:, 1]
        allowed = (key_pos[None, :] <= positions[:, None]) & (key_pos[None, :] < length)
        scores = masked_scores(query_matrix, key_rows, allowed)
        top_score = jnp.max(scores, axis=-1, keepdims=True)
        weights = jnp.exp(scores - top_score)
        weight_total = jnp.sum(weights, axis=-1, keepdims=True)
        log_total = top_score + jnp.log(weight_total)
        probs_low = (weights / weight_total).astype(jnp.bfloat16)
        attended = jnp.einsum(
            "hgqk,khd->qhgd", probs_low, value_rows, preferred_element_type=jnp.float32
        )
        attended = attended.reshape(token_rows, QUERY_HEADS * HEAD_SIZE).astype(jnp.bfloat16)
        mixed_rows = input_rows + jnp.dot(attended, output_all, preferred_element_type=jnp.float32)
        normed_mid, inverse_two = rms_parts(mixed_rows)
        normed_two = (normed_mid * gain_two).astype(jnp.bfloat16)
        logits = jnp.dot(normed_two, router_all, preferred_element_type=jnp.float32)
        onehot = (
            route_rows[:, :, None] == jnp.arange(expert_count, dtype=jnp.int32)[None, None, :]
        ).astype(jnp.float32)
        chosen = jnp.sum(onehot * logits[:, None, :], axis=-1)
        gate_values = jax.nn.softmax(chosen, axis=-1)
        slot_idx = slot_index(route_rows, expert_count, capacity)
        send_rows = jnp.zeros((expert_count * capacity, hidden_width), jnp.bfloat16)
        send_rows = send_rows.at[slot_idx].set(jnp.repeat(normed_two, TOP, axis=0))
        received = lax.all_to_all(
            send_rows.reshape(expert_count, capacity, hidden_width),
            "expert",
            split_axis=0,
            concat_axis=0,
            tiled=True,
        )
        item_count = received.shape[1]
        grouped = received.reshape(expert_size, local_experts, item_count, hidden_width)
        gate_up = jnp.einsum(
            "slcd,ldf->slcf", grouped, gateup_all, preferred_element_type=jnp.float32
        )
        hidden = (jax.nn.silu(gate_up[..., :FF]) * gate_up[..., FF:]).astype(jnp.bfloat16)
        result = jnp.einsum(
            "slcf,lfd->slcd", hidden, down_all, preferred_element_type=jnp.float32
        ).astype(jnp.bfloat16)
        back_rows = lax.all_to_all(
            result.reshape(expert_count, item_count, hidden_width),
            "expert",
            split_axis=0,
            concat_axis=0,
            tiled=True,
        )
        back_rows, kept_rows, kept_gateup = (
            back_rows,
            received,
            gate_up.reshape(expert_count, item_count, 2 * FF),
        )
        returned = back_rows.reshape(expert_count * capacity, hidden_width)[slot_idx].reshape(
            token_rows, TOP, hidden_width
        )
        returned_wide = returned.astype(jnp.float32)
        expert_sum = jnp.sum(gate_values[:, :, None] * returned_wide, axis=1)
        final_rows = jnp.where(live_rows, mixed_rows + expert_sum, 0.0)
        outputs_list.append(final_rows.astype(jnp.bfloat16))
        grad_rows = jnp.where(live_rows, cotangent[micro_step].astype(jnp.float32), 0.0)
        grad_gate = jnp.sum(grad_rows[:, None, :] * returned_wide, axis=-1)
        grad_chosen = gate_values * (
            grad_gate - jnp.sum(gate_values * grad_gate, axis=-1, keepdims=True)
        )
        grad_logits = jnp.sum(onehot * grad_chosen[:, :, None], axis=1)
        router_term = jnp.dot(normed_two.astype(jnp.float32).T, grad_logits, precision=highest)
        grad_normtwo = jnp.dot(grad_logits, router_all.astype(jnp.float32).T, precision=highest)
        grad_result = (
            (gate_values[:, :, None] * grad_rows[:, None, :])
            .astype(jnp.bfloat16)
            .reshape(token_rows * TOP, hidden_width)
        )
        send_grads = (
            jnp.zeros((expert_count * capacity, hidden_width), jnp.bfloat16)
            .at[slot_idx]
            .set(grad_result)
        )
        recv_grads, again_rows = (
            lax.all_to_all(
                send_grads.reshape(expert_count, capacity, hidden_width),
                "expert",
                split_axis=0,
                concat_axis=0,
                tiled=True,
            ),
            lax.all_to_all(
                send_rows.reshape(expert_count, capacity, hidden_width),
                "expert",
                split_axis=0,
                concat_axis=0,
                tiled=True,
            ),
        )
        grouped_rows = again_rows.reshape(expert_size, local_experts, capacity, hidden_width)
        gate_up = jnp.einsum(
            "slcd,ldf->slcf", grouped_rows, gateup_all, preferred_element_type=jnp.float32
        )
        grouped_grads = recv_grads.reshape(expert_size, local_experts, capacity, hidden_width)
        gate_part = gate_up[..., :FF]
        up_part = gate_up[..., FF:]
        sigmoid_gate = jax.nn.sigmoid(gate_part)
        silu_gate = gate_part * sigmoid_gate
        hidden = (silu_gate * up_part).astype(jnp.bfloat16)
        grad_hidden = jnp.einsum(
            "slcd,lfd->slcf", grouped_grads, down_all, preferred_element_type=jnp.float32
        )
        down_term = jnp.einsum(
            "slcf,slcd->lfd", hidden, grouped_grads, preferred_element_type=jnp.float32
        )
        grad_gatepart = (
            grad_hidden * up_part * sigmoid_gate * (1.0 + gate_part * (1.0 - sigmoid_gate))
        )
        grad_gateup = jnp.concatenate([grad_gatepart, grad_hidden * silu_gate], axis=-1).astype(
            jnp.bfloat16
        )
        upper_term = jnp.einsum(
            "slcd,slcf->ldf", grouped_rows, grad_gateup, preferred_element_type=jnp.float32
        )
        grad_copies = jnp.einsum(
            "slcf,ldf->slcd", grad_gateup, gateup_all, preferred_element_type=jnp.float32
        ).astype(jnp.bfloat16)
        back_grads = lax.all_to_all(
            grad_copies.reshape(expert_count, capacity, hidden_width),
            "expert",
            split_axis=0,
            concat_axis=0,
            tiled=True,
        )
        copy_rows = back_grads.reshape(expert_count * capacity, hidden_width)[slot_idx].reshape(
            token_rows, TOP, hidden_width
        )
        grad_normtwo = grad_normtwo + jnp.sum(copy_rows.astype(jnp.float32), axis=1)
        midnorm_term = jnp.sum(grad_normtwo * normed_mid, axis=0)
        grad_mixed = grad_rows + norm_back(grad_normtwo, normed_mid, inverse_two, gain_two)
        grad_proj = grad_mixed.astype(jnp.bfloat16)
        output_term = jnp.dot(attended.T, grad_proj, preferred_element_type=jnp.float32)
        attention_gradient = jnp.dot(
            grad_proj, output_all.T, preferred_element_type=jnp.float32
        ).astype(jnp.bfloat16)
        attention_gradient = attention_gradient.reshape(
            token_rows, KEY_VALUE_HEADS, query_group_width, HEAD_SIZE
        )
        scores = masked_scores(query_matrix, key_rows, allowed)
        prob_rows = jnp.exp(scores - log_total)
        grad_probs = jnp.einsum(
            "qhgd,khd->hgqk", attention_gradient, value_rows, preferred_element_type=jnp.float32
        )
        row_delta = jnp.sum(prob_rows * grad_probs, axis=-1, keepdims=True)
        grad_scores = (prob_rows * (grad_probs - row_delta)).astype(jnp.bfloat16)
        prob_low = prob_rows.astype(jnp.bfloat16)
        grad_qrot = (
            jnp.einsum("hgqk,khd->qhgd", grad_scores, key_rows, preferred_element_type=jnp.float32)
            * score_scale
        )
        grad_keys = (
            jnp.einsum(
                "hgqk,qhgd->khd", grad_scores, query_matrix, preferred_element_type=jnp.float32
            )
            * score_scale
        )
        grad_vals = jnp.einsum(
            "hgqk,qhgd->khd", prob_low, attention_gradient, preferred_element_type=jnp.float32
        )
        own_keys = (
            lax.psum_scatter(
                jnp.stack([grad_keys, grad_vals], axis=1)
                .reshape(lax.axis_size("dp") * token_rows, 2 * KEY_VALUE_HEADS * HEAD_SIZE)
                .astype(jnp.bfloat16),
                "dp",
                scatter_dimension=0,
                tiled=True,
            )
            .astype(jnp.float32)
            .reshape(token_rows, 2, KEY_VALUE_HEADS, HEAD_SIZE)
        )
        grad_query = (
            unrotate(
                grad_qrot.reshape(token_rows, QUERY_HEADS, HEAD_SIZE), cosine_table, sine_table
            )
            .astype(jnp.bfloat16)
            .reshape(token_rows, QUERY_HEADS * HEAD_SIZE)
        )
        key_gradient = unrotate(own_keys[:, 0], cosine_table, sine_table).astype(jnp.bfloat16)
        value_gradient = own_keys[:, 1].astype(jnp.bfloat16)
        key_value_weight_gradient = jnp.stack([key_gradient, value_gradient], axis=1).reshape(
            token_rows, 2 * KEY_VALUE_HEADS * HEAD_SIZE
        )
        query_term = jnp.dot(normalized_input.T, grad_query, preferred_element_type=jnp.float32)
        keyval_term = jnp.dot(
            normalized_input.T, key_value_weight_gradient, preferred_element_type=jnp.float32
        )
        grad_normone = jnp.dot(grad_query, query_all.T, preferred_element_type=jnp.float32)
        grad_normone = grad_normone + jnp.dot(
            key_value_weight_gradient, keyval_all.T, preferred_element_type=jnp.float32
        )
        prenorm_term = jnp.sum(grad_normone * normed_one, axis=0)
        grads_list.append(grad_mixed + norm_back(grad_normone, normed_one, inverse_one, gain_one))
        total_prenorm = total_prenorm + prenorm_term
        total_query = total_query + query_term
        total_key_value = total_key_value + keyval_term
        total_output = total_output + output_term
        total_midnorm = total_midnorm + midnorm_term
        total_router = total_router + router_term
        total_upper = total_upper + upper_term
        total_down = total_down + down_term
    dense_grads = (
        lax.psum_scatter(total_prenorm, ("dp", "expert"), scatter_dimension=0, tiled=True),
        lax.psum_scatter(total_query, ("dp", "expert"), scatter_dimension=0, tiled=True),
        lax.psum_scatter(total_key_value, ("dp", "expert"), scatter_dimension=0, tiled=True),
        lax.psum_scatter(total_output, ("dp", "expert"), scatter_dimension=0, tiled=True),
        lax.psum_scatter(total_midnorm, ("dp", "expert"), scatter_dimension=0, tiled=True),
        lax.psum_scatter(total_router, ("dp", "expert"), scatter_dimension=0, tiled=True),
    )
    expert_grads = (
        lax.psum_scatter(
            total_upper.astype(jnp.bfloat16), "dp", scatter_dimension=1, tiled=True
        ).astype(jnp.float32),
        lax.psum_scatter(
            total_down.astype(jnp.bfloat16), "dp", scatter_dimension=1, tiled=True
        ).astype(jnp.float32),
    )
    return (
        jnp.stack(outputs_list),
        jnp.stack(grads_list),
        dense_grads[0],
        dense_grads[1],
        dense_grads[2],
        dense_grads[3],
        dense_grads[4],
        dense_grads[5],
        expert_grads[0],
        expert_grads[1],
    )


MESH = pl.DeviceIdType.MESH
CHUNK = 256
PIECE = 96


def remote(src, dst, send_sem, recv_sem, target):
    return pltpu.make_async_remote_copy(
        src_ref=src,
        dst_ref=dst,
        send_sem=send_sem,
        recv_sem=recv_sem,
        device_id=target,
        device_id_type=MESH,
    )


def place():
    d = lax.axis_index("dp")
    e = lax.axis_index("expert")
    z = lax.div(e, 2)
    c = lax.rem(e, 2)
    x = lax.rem(d, 2)
    y = lax.div(d, 2)
    return d, e, z, c, x, y


def attention_kernel(
    tok_ref,
    wq_hbm,
    wkv_hbm,
    wr_ref,
    pre_ref,
    mid_ref,
    wb_hbm,
    cot_ref,
    wo_hbm,
    rope_hbm,
    lens_ref,
    routes_ref,
    wa_out,
    wb_out,
    wo_out,
    gall,
    q_out,
    kv_out,
    att_out,
    mixed_out,
    normed_out,
    gates_out,
    wa,
    wb,
    qs,
    kvs,
    att,
    g_own,
    rope,
    own_sem,
    wo_recv,
    wo_send,
    z_recv,
    z_send,
    xy_recv,
    xy_send,
    sib_recv,
    sib_send,
    g_recv,
    g_send,
    gs_recv,
    gs_send,
    kv_recv,
    kv_send,
):
    bf, f32 = jnp.bfloat16, jnp.float32
    d, e, z, c, x, y = place()
    d_x = d + 1 - 2 * x
    d_y = d + 2 - 4 * y
    d_d = 3 - d
    other = 1 - c
    to_x = (d_x, e)
    to_y = (d_y, e)
    to_sib = (d, 2 * z + other)
    to_up = (d, e + jnp.where(z < 3, 2, -2))
    to_down = (d, e + jnp.where(z > 0, -2, 2))

    barrier = pltpu.get_barrier_semaphore()
    for target in (to_x, to_y, to_sib):
        pl.semaphore_signal(barrier, inc=1, device_id=target, device_id_type=MESH)

    @pl.when(z < 3)
    def _():
        pl.semaphore_signal(barrier, inc=1, device_id=to_up, device_id_type=MESH)

    @pl.when(z > 0)
    def _():
        pl.semaphore_signal(barrier, inc=1, device_id=to_down, device_id_type=MESH)

    own_at = pl.multiple_of((d * 8 + e) * 48, 16)
    own_rows = pl.ds(own_at, 48)
    own_a = [
        pltpu.make_async_copy(wq_hbm, wa.at[own_rows, pl.ds(0, 1536)], own_sem.at[0]),
        pltpu.make_async_copy(wkv_hbm, wa.at[own_rows, pl.ds(1536, 512)], own_sem.at[1]),
        pltpu.make_async_copy(rope_hbm.at[:, pl.ds(pl.multiple_of(d * 128, 128), 128)], rope, own_sem.at[2]),
    ]
    for copy in own_a:
        copy.start()
    eye = lax.broadcasted_iota(jnp.int32, (128, 128), 0) == lax.broadcasted_iota(
        jnp.int32, (128, 128), 1
    )
    eye_low = eye.astype(bf)
    turned = (((0,), (0,)), ((), ()))
    sub = lax.broadcasted_iota(jnp.int32, (8, 48), 0)
    gains = jnp.where(
        sub == 0,
        pre_ref[...].astype(f32),
        jnp.where(sub == 1, mid_ref[...].astype(f32), 0.0),
    )
    tile = jnp.concatenate([wr_ref[...].astype(f32), gains], axis=0).astype(bf)
    wa[own_rows, 2048:] = lax.dot_general(
        tile, eye_low[:16], turned, preferred_element_type=f32
    ).astype(bf)
    for s in range(2):
        rows = slice(s * 128, (s + 1) * 128)
        slot = d * 128 + lax.broadcasted_iota(jnp.int32, (128, 1), 0)
        g_own[rows] = jnp.where(slot < lens_ref[s], cot_ref[rows].astype(f32), 0.0).astype(bf)

    full = (wa, wb)
    shard = (None, wb_hbm)

    def block(a, dd, zp, lane):
        at = pl.multiple_of((dd * 8 + 2 * zp + lane) * 48, 16)
        return full[a].at[pl.ds(at, 48)]

    def z_copy(a, zp, way, src=None):
        ref = block(a, d, zp, c)
        return remote(
            ref if src is None else src,
            ref,
            z_send.at[a, way, zp],
            z_recv.at[a, zp],
            to_up if way == 0 else to_down,
        )

    def xy_copy(a, dd, zp, row, target, src=None):
        ref = block(a, dd, zp, c)
        return remote(
            ref if src is None else src,
            ref,
            xy_send.at[a, row, zp],
            xy_recv.at[a, row, zp],
            target,
        )

    def s_copy(a, dd, zp, src=None, lane=None):
        ref = block(a, dd, zp, c if lane is None else lane)
        return remote(
            ref if src is None else src,
            ref,
            sib_send.at[a, dd, zp],
            sib_recv.at[a, dd, zp],
            to_sib,
        )

    def send_xy(a, zp):
        xy_copy(a, d, zp, 0, to_x).start()
        xy_copy(a, d, zp, 1, to_y).start()

    def own_start(a):
        @pl.when(z < 3)
        def _():
            z_copy(a, z, 0, shard[a]).start()

        @pl.when(z > 0)
        def _():
            z_copy(a, z, 1, shard[a]).start()

        s_copy(a, d, z, shard[a]).start()

    def from_z(a, k):
        def arrived(zp, way):
            z_copy(a, zp, way).wait_recv()

            @pl.when((z < 3) if way == 0 else (z > 0))
            def _():
                z_copy(a, zp, way).start()

            if a == 0:
                send_xy(a, zp)
            s_copy(a, d, zp).start()

        @pl.when(z - k >= 0)
        def _():
            arrived(z - k, 0)

        @pl.when(z + k <= 3)
        def _():
            arrived(z + k, 1)

    def from_xy_one(a, zp):
        xy_copy(a, d_x, zp, 0, to_x).wait_recv()

        @pl.when(lax.rem(zp, 2) == 0)
        def _():
            xy_copy(a, d_x, zp, 2, to_y).start()

        s_copy(a, d_x, zp).start()
        xy_copy(a, d_y, zp, 1, to_y).wait_recv()

        @pl.when(lax.rem(zp, 2) == 1)
        def _():
            xy_copy(a, d_y, zp, 2, to_x).start()

        s_copy(a, d_y, zp).start()

    def from_xy(a, k):
        @pl.when(z - k >= 0)
        def _():
            from_xy_one(a, z - k)

        if k > 0:

            @pl.when(z + k <= 3)
            def _():
                from_xy_one(a, z + k)

    def from_diag(a):
        for k in range(4):
            zp = lax.rem(z + k, 4)
            xy_copy(a, d_d, zp, 2, to_x).wait_recv()
            s_copy(a, d_d, zp).start()

    def from_sib(a):
        for dd in range(4):
            for zp in range(4):
                s_copy(a, dd, zp, lane=other).wait_recv()

    def drain(a):
        for zp in range(4):
            for dd in range(4):
                s_copy(a, dd, zp).wait_send()
            for row in range(3):
                xy_copy(a, d, zp, row, to_x).wait_send()

            @pl.when((zp <= z) & (z < 3))
            def _():
                z_copy(a, zp, 0).wait_send()

            @pl.when((zp >= z) & (z > 0))
            def _():
                z_copy(a, zp, 1).wait_send()

    def g_part(zp, lane, s):
        at = pl.multiple_of((2 * zp + lane) * CHUNK + s * 128, 128)
        return gall.at[pl.ds(at, 128)]

    def g_copy(zp, s, way, src=None):
        ref = g_part(zp, c, s)
        return remote(
            ref if src is None else src,
            ref,
            g_send.at[way, zp, s],
            g_recv.at[zp, s],
            to_up if way == 0 else to_down,
        )

    def gs_copy(zp, s, src=None, lane=None):
        ref = g_part(zp, c if lane is None else lane, s)
        return remote(
            ref if src is None else src, ref, gs_send.at[zp, s], gs_recv.at[zp, s], to_sib
        )

    def g_start():
        for s in range(2):
            src = g_own.at[pl.ds(s * 128, 128)]

            @pl.when(z < 3)
            def _():
                g_copy(z, s, 0, src).start()

            @pl.when(z > 0)
            def _():
                g_copy(z, s, 1, src).start()

            gs_copy(z, s, src).start()

    def g_pass(k, s):
        @pl.when(z - k >= 0)
        def _():
            g_copy(z - k, s, 0).wait_recv()

            @pl.when(z < 3)
            def _():
                g_copy(z - k, s, 0).start()

            gs_copy(z - k, s).start()

        @pl.when(z + k <= 3)
        def _():
            g_copy(z + k, s, 1).wait_recv()

            @pl.when(z > 0)
            def _():
                g_copy(z + k, s, 1).start()

            gs_copy(z + k, s).start()

    def wo_copy(dd, p, row, target, src=None):
        ref = wo_out.at[pl.ds(pl.multiple_of(dd * 192 + p * PIECE, 16), PIECE)]
        return remote(
            ref if src is None else src, ref, wo_send.at[row, p], wo_recv.at[row, p], target
        )

    def wo_start(p):
        wo_copy(d, p, 0, to_x, wo_hbm.at[pl.ds(p * PIECE, PIECE)]).start()
        wo_copy(d, 1 - p, 1, to_y, wo_hbm.at[pl.ds((1 - p) * PIECE, PIECE)]).start()

    def wo_pass():
        wo_copy(d_x, 0, 0, to_x).wait_recv()
        wo_copy(d_x, 0, 2, to_y).start()
        wo_copy(d_y, 1, 1, to_y).wait_recv()
        wo_copy(d_y, 1, 2, to_x).start()

    def wo_rest():
        wo_copy(d_x, 1, 0, to_x).wait_recv()
        wo_copy(d_y, 0, 1, to_y).wait_recv()
        for p in range(2):
            wo_copy(d_d, p, 2, to_x).wait_recv()

    pl.semaphore_wait(barrier, 5 - jnp.where((z == 0) | (z == 3), 1, 0))
    for copy in own_a:
        copy.wait()
    own_start(0)
    own_start(1)
    own = [
        pltpu.make_async_copy(wb_hbm, block(1, d, z, c), own_sem.at[0]),
        pltpu.make_async_copy(
            g_own, gall.at[pl.ds(pl.multiple_of(e * CHUNK, CHUNK), CHUNK)], own_sem.at[1]
        ),
        pltpu.make_async_copy(
            wo_hbm, wo_out.at[pl.ds(pl.multiple_of(d * 192, 16), 192)], own_sem.at[2]
        ),
    ]
    for copy in own:
        copy.start()
    send_xy(0, z)
    tok = tok_ref[...].astype(f32)
    n1 = tok * lax.rsqrt(jnp.mean(tok * tok, axis=1, keepdims=True) + epsilon)
    from_z(0, 1)
    from_z(1, 1)
    from_xy(0, 0)
    from_z(0, 2)
    from_z(1, 2)
    g_start()
    from_xy(0, 1)
    from_z(0, 3)
    from_z(1, 3)
    from_xy(0, 2)
    from_xy(0, 3)

    def turn(j):
        return lax.rem(z + j, 4)

    own[0].wait()
    for j in range(2):
        send_xy(1, turn(j))
    from_diag(0)
    from_sib(0)

    small_t = lax.dot_general(
        eye_low[:16], wa[:, 2048:], (((1,), (1,)), ((), ())), preferred_element_type=f32
    )
    normed = (n1 * small_t[8:9]).astype(bf)
    cos_rows = jnp.concatenate([rope[0]] * 2, axis=0)
    sin_rows = jnp.concatenate([rope[1]] * 2, axis=0)

    def rotate(v):
        return v * cos_rows + pltpu.roll(v, 64, 1) * sin_rows

    kv = jnp.dot(normed, wa[:, 1536:2048], preferred_element_type=f32)
    for h in range(2):
        kvs[d, :, h * 128 : (h + 1) * 128] = rotate(kv[:, h * 128 : (h + 1) * 128]).astype(bf)
    kvs[d, :, 256:] = kv[:, 256:].astype(bf)

    def kv_copy(dd, s, row, target):
        ref = kvs.at[dd, pl.ds(s * 128, 128)]
        return remote(ref, ref, kv_send.at[row, s], kv_recv.at[row, s], target)

    for s in range(2):
        kv_copy(d, s, 0, to_x).start()
        kv_copy(d, 1 - s, 1, to_y).start()
    send_xy(1, turn(2))
    g_pass(1, 0)
    q = jnp.dot(normed, wa[:, :1536], preferred_element_type=f32)
    for head in range(QUERY_HEADS):
        rot = rotate(q[:, head * 128 : (head + 1) * 128]).astype(bf)
        for s in range(2):
            at = (s * QUERY_HEADS + head) * 128
            qs[at : at + 128] = rot[s * 128 : (s + 1) * 128]
    kv_copy(d_x, 0, 0, to_x).wait_recv()
    kv_copy(d_x, 0, 2, to_y).start()
    kv_copy(d_y, 1, 1, to_y).wait_recv()
    kv_copy(d_y, 1, 2, to_x).start()
    send_xy(1, turn(3))
    for j in range(2):
        from_xy_one(1, turn(j))
    g_pass(1, 1)
    kv_copy(d_y, 0, 1, to_y).wait_recv()
    kv_copy(d_x, 1, 0, to_x).wait_recv()
    for s in range(2):
        kv_copy(d_d, s, 2, to_x).wait_recv()
    q_copy = pltpu.make_async_copy(qs, q_out, own_sem.at[3])
    kvo_copy = pltpu.make_async_copy(kvs, kv_out, own_sem.at[4])
    wa_copy = pltpu.make_async_copy(wa, wa_out, own_sem.at[5])
    for copy in (q_copy, kvo_copy, wa_copy):
        copy.start()

    query_pos = d * 128 + lax.broadcasted_iota(jnp.int32, (128, 512), 0)
    key_pos = lax.broadcasted_iota(jnp.int32, (128, 512), 1)

    def attend(n):
        s = lax.div(n, 2)
        h = lax.rem(n, 2)
        lens = lens_ref[s]
        allowed = (key_pos <= query_pos) & (key_pos < lens)
        ks = kvs[:, pl.ds(pl.multiple_of(s * 128, 128), 128), pl.ds(pl.multiple_of(h * 128, 128), 128)]
        vs = kvs[:, pl.ds(pl.multiple_of(s * 128, 128), 128), pl.ds(pl.multiple_of(256 + h * 128, 128), 128)]
        ks = ks.reshape(512, 128)
        vs = vs.reshape(512, 128)
        for half in range(2):
            qh = qs[pl.ds(pl.multiple_of(n * 768 + half * 384, 128), 384)]
            scores = lax.dot_general(qh, ks, (((1,), (1,)), ((), ())), preferred_element_type=f32)
            scores = scores.reshape(3, 128, 512) * HEAD_SIZE ** (-0.5)
            scores = jnp.where(allowed[None], scores, -1e30)
            top = jnp.max(scores, axis=-1, keepdims=True)
            weights = jnp.exp(scores - top)
            weights = weights * (1.0 / jnp.sum(weights, axis=-1, keepdims=True))
            out = jnp.dot(
                weights.astype(bf).reshape(384, 512), vs, preferred_element_type=f32
            ).astype(bf)
            for j in range(3):
                att[
                    pl.ds(pl.multiple_of(s * 128, 128), 128),
                    pl.ds(pl.multiple_of(h * 768 + (half * 3 + j) * 128, 128), 128),
                ] = out[j * 128 : (j + 1) * 128]

    wo_start(0)
    pl.loop(0, 2)(attend)
    from_xy_one(1, turn(2))
    from_xy_one(1, turn(3))
    wo_start(1)
    g_pass(2, 0)

    @pl.loop(2, 4)
    def _(n):
        attend(n)
        pl.when(n == 2)(wo_pass)

    g_pass(2, 1)
    from_diag(1)
    from_sib(1)
    att_copy = pltpu.make_async_copy(att, att_out, own_sem.at[6])
    wb_copy = pltpu.make_async_copy(wb, wb_out, own_sem.at[7])
    att_copy.start()
    wb_copy.start()
    mixed = tok_ref[...].astype(f32) + jnp.dot(att[...], wb[...], preferred_element_type=f32)
    mixed_out[...] = mixed
    n2 = mixed * lax.rsqrt(jnp.mean(mixed * mixed, axis=1, keepdims=True) + epsilon)
    normed2 = (n2 * small_t[9:10]).astype(bf)
    normed_out[...] = normed2
    logits = lax.dot_general(
        small_t[:8].astype(bf), normed2, (((1,), (1,)), ((), ())), preferred_element_type=f32
    )
    number = lax.broadcasted_iota(jnp.int32, (8, 128), 0)
    for s in range(2):
        chosen = number == routes_ref[s, 0:1]
        for t in range(1, TOP):
            chosen = chosen | (number == routes_ref[s, t : t + 1])
        picked = jnp.where(chosen, logits[:, s * 128 : (s + 1) * 128], -1e30)
        top = jnp.max(picked, axis=0, keepdims=True)
        weights = jnp.where(chosen, jnp.exp(picked - top), 0.0)
        gates_out[s] = weights / jnp.sum(weights, axis=0, keepdims=True)

    g_pass(3, 0)
    g_pass(3, 1)
    wo_rest()
    for zp in range(4):
        for s in range(2):
            gs_copy(zp, s, lane=other).wait_recv()
    own[1].wait()
    own[2].wait()
    for copy in (q_copy, kvo_copy, wa_copy, att_copy, wb_copy):
        copy.wait()
    drain(0)
    drain(1)
    for s in range(2):
        for row in range(3):
            kv_copy(d, s, row, to_x).wait_send()
            wo_copy(d, s, row, to_x).wait_send()
        for zp in range(4):
            gs_copy(zp, s).wait_send()

            @pl.when((zp <= z) & (z < 3))
            def _():
                g_copy(zp, s, 0).wait_send()

            @pl.when((zp >= z) & (z > 0))
            def _():
                g_copy(zp, s, 1).wait_send()


def attention_stage(tok, wq, wkv, wr, pre, mid, wb, cot, wo, rope, lens, routes):
    bf, f32 = jnp.bfloat16, jnp.float32
    shape = jax.ShapeDtypeStruct
    width = tok.shape[-1]
    wide = wq.shape[-1] + wkv.shape[-1] + 128
    hbm = pl.BlockSpec(memory_space=pltpu.HBM)
    vmem = pl.BlockSpec(memory_space=pltpu.VMEM)
    smem = pl.BlockSpec(memory_space=pltpu.SMEM)
    dma = pltpu.SemaphoreType.DMA
    return pl.pallas_call(
        attention_kernel,
        out_shape=(
            shape((width, wide), bf),
            shape((width, width), bf),
            shape((FF, width), bf),
            shape((8 * CHUNK, width), bf),
            shape((2 * QUERY_HEADS * 128, 128), bf),
            shape((4, CHUNK, 512), bf),
            shape((CHUNK, width), bf),
            shape((CHUNK, width), f32),
            shape((CHUNK, width), bf),
            shape((2, 8, 128), f32),
        ),
        in_specs=[vmem, hbm, hbm, vmem, vmem, vmem, hbm, vmem, hbm, hbm, smem, vmem],
        out_specs=[hbm] * 7 + [vmem] * 3,
        scratch_shapes=[
            pltpu.VMEM((width, wide), bf),
            pltpu.VMEM((width, width), bf),
            pltpu.VMEM((2 * QUERY_HEADS * 128, 128), bf),
            pltpu.VMEM((4, CHUNK, 512), bf),
            pltpu.VMEM((CHUNK, width), bf),
            pltpu.VMEM((CHUNK, width), bf),
            pltpu.VMEM((2, 128, 128), f32),
            dma((8,)),
            dma((3, 2)),
            dma((3, 2)),
            dma((2, 4)),
            dma((2, 2, 4)),
            dma((2, 3, 4)),
            dma((2, 3, 4)),
            dma((2, 4, 4)),
            dma((2, 4, 4)),
            dma((4, 2)),
            dma((2, 4, 2)),
            dma((4, 2)),
            dma((4, 2)),
            dma((3, 2)),
            dma((3, 2)),
        ],
        compiler_params=pltpu.CompilerParams(
            collective_id=2, has_side_effects=True, vmem_limit_bytes=60 * 2**20
        ),
        name="attention_stage",
    )(tok, wq, wkv, wr, pre, mid, wb, cot, wo, rope, lens, routes)


def expert_kernel(
    x_hbm,
    g_hbm,
    gt_hbm,
    win_hbm,
    wout_hbm,
    dx_out,
    dgt_out,
    outp_hbm,
    gin_hbm,
    gout_hbm,
    gout_out,
    gin_out,
    win,
    wout,
    xall,
    gall,
    gtall,
    dgu,
    hg,
    dxb,
    dgb,
    sibr,
    sibg,
    ro,
    rog,
    ri,
    rig,
    stage,
    gout,
    tg,
    xg,
    yg,
    gin,
    ti,
    xi,
    yi,
    own_sem,
    stage_sem,
    g_recv,
    g_send,
    i_recv,
    i_send,
    w_recv,
    w_send,
    ag_recv,
    ag_send,
    sib_recv,
    sib_send,
    red_recv,
    red_send,
):
    bf, f32 = jnp.bfloat16, jnp.float32
    d, e, z, c, x, y = place()
    d_x = d + 1 - 2 * x
    d_y = d + 2 - 4 * y
    d_d = 3 - d
    hi = lax.div(z, 2)
    zz = z * hi + (3 - z) * (1 - hi)
    other = 1 - c
    to_x = (d_x, e)
    to_y = (d_y, e)
    to_sib = (d, 2 * z + other)
    to_up = (d, e + jnp.where(z < 3, 2, -2))
    to_down = (d, e + jnp.where(z > 0, -2, 2))
    e_in = e + 2 - 4 * hi
    to_in = (d, e_in)
    to_out = (d, jnp.where(zz == 2, e - 2 + 4 * hi, e_in))
    mid = zz == 2
    end = zz == 3

    barrier = pltpu.get_barrier_semaphore()
    for target in (to_x, to_y, to_sib, to_in):
        pl.semaphore_signal(barrier, inc=1, device_id=target, device_id_type=MESH)

    @pl.when(mid)
    def _():
        pl.semaphore_signal(barrier, inc=1, device_id=to_out, device_id_type=MESH)

    own_copies = [
        pltpu.make_async_copy(x_hbm.at[s], xall.at[e, s], own_sem.at[s]) for s in range(2)
    ] + [
        pltpu.make_async_copy(gt_hbm, gtall.at[e], own_sem.at[2]),
        pltpu.make_async_copy(wout_hbm, wout, own_sem.at[3]),
        pltpu.make_async_copy(g_hbm, gall, own_sem.at[4]),
    ]

    def w_columns(h, kind):
        return pl.ds(h * 768 + kind * 384, 384)

    for h in range(2):
        for kind in range(2):
            own_copies.append(
                pltpu.make_async_copy(
                    win_hbm.at[:, pl.ds(kind * 768 + h * 384, 384)],
                    win.at[pl.ds(pl.multiple_of(d * 384, 16), 384), w_columns(h, kind)],
                    own_sem.at[5 + 2 * h + kind],
                )
            )
    pl.semaphore_wait(barrier, 7 - zz)

    gathered = ((x_hbm, xall), (gt_hbm, gtall))

    def ag_copy(a, zp, s, way, src=None):
        ref = gathered[a][1].at[2 * zp + c, s]
        return remote(
            ref if src is None else src,
            ref,
            ag_send.at[way, a, zp, s],
            ag_recv.at[a, zp, s],
            to_up if way == 0 else to_down,
        )

    def sib_copy(a, zp, s, src=None, lane=None):
        ref = gathered[a][1].at[2 * zp + (c if lane is None else lane), s]
        return remote(
            ref if src is None else src,
            ref,
            sib_send.at[a, zp, s],
            sib_recv.at[a, zp, s],
            to_sib,
        )

    def own_rows(s):
        for a in range(2):
            src = gathered[a][0].at[s]

            @pl.when(z < 3)
            def _():
                ag_copy(a, z, s, 0, src).start()

            @pl.when(z > 0)
            def _():
                ag_copy(a, z, s, 1, src).start()

            sib_copy(a, z, s, src).start()

    def pass_on(k, s):
        for a in range(2):

            @pl.when(z - k >= 0)
            def _():
                ag_copy(a, z - k, s, 0).wait_recv()

                @pl.when(z < 3)
                def _():
                    ag_copy(a, z - k, s, 0).start()

                sib_copy(a, z - k, s).start()

            @pl.when(z + k <= 3)
            def _():
                ag_copy(a, z + k, s, 1).wait_recv()

                @pl.when(z > 0)
                def _():
                    ag_copy(a, z + k, s, 1).start()

                sib_copy(a, z + k, s).start()

    def from_sib(s):
        for a in range(2):
            for zp in range(4):
                sib_copy(a, zp, s, lane=other).wait_recv()

    def w_copy(h, kind, p, src_d, target, row, src=None):
        ref = win.at[
            pl.ds(pl.multiple_of(src_d * 384 + p * 192, 16), 192), w_columns(h, kind)
        ]
        return remote(
            ref if src is None else src,
            ref,
            w_send.at[row, h, kind, p],
            w_recv.at[row, h, kind, p],
            target,
        )

    def w_start(h):
        for p in range(2):
            for kind in range(2):

                def src(q):
                    return win_hbm.at[
                        pl.ds(q * 192, 192), pl.ds(kind * 768 + h * 384, 384)
                    ]

                w_copy(h, kind, p, d, to_x, 0, src(p)).start()
                w_copy(h, kind, 1 - p, d, to_y, 1, src(1 - p)).start()

    def w_pass(h):
        for kind in range(2):
            w_copy(h, kind, 0, d_x, to_x, 0).wait_recv()
            w_copy(h, kind, 0, d_x, to_y, 2).start()
            w_copy(h, kind, 1, d_y, to_y, 1).wait_recv()
            w_copy(h, kind, 1, d_y, to_x, 2).start()

    def w_rest(h):
        for kind in range(2):
            w_copy(h, kind, 1, d_x, to_x, 0).wait_recv()
            w_copy(h, kind, 0, d_y, to_y, 1).wait_recv()
            for p in range(2):
                w_copy(h, kind, p, d_d, to_x, 2).wait_recv()

    own_rows(0)
    w_start(0)
    for copy in own_copies:
        copy.start()
    w_pass(0)
    w_start(1)
    pass_on(1, 0)
    pass_on(2, 0)
    own_rows(1)
    w_rest(0)
    w_pass(1)
    pass_on(3, 0)
    from_sib(0)
    for copy in own_copies:
        copy.wait()

    def order(i):
        v = i if i < 2 else (5 - zz if i == 2 else zz)
        return v * hi + (3 - v) * (1 - hi)

    def sib_sum(zp, s, a):
        src, dst = ((dxb, sibr), (dgb, sibg))[a]
        return remote(
            src.at[2 * zp + other, s], dst.at[zp, s], red_send.at[a, zp, s], red_recv.at[a, zp, s], to_sib
        )

    def hop(i, s, target, inward):
        dst, dstg, row = (ro, rog, 2) if inward else (ri, rig, 4)
        zp = order(i)
        return (
            remote(
                dxb.at[2 * zp + c, s], dst.at[i, s], red_send.at[2, i, s], red_recv.at[row, i, s], target
            ),
            remote(
                dgb.at[2 * zp + c, s], dstg.at[i, s], red_send.at[3, i, s], red_recv.at[row + 1, i, s], target
            ),
        )

    def wait_from(ref, refg, slot, s, row):
        remote(
            ref.at[slot, s], ref.at[slot, s], red_send.at[2, slot, s], red_recv.at[row, slot, s], to_in
        ).wait_recv()
        remote(
            refg.at[slot, s], refg.at[slot, s], red_send.at[3, slot, s], red_recv.at[row + 1, slot, s], to_in
        ).wait_recv()

    def combine(i, s, incoming):
        zp = order(i)
        for a in range(2):
            remote(
                sibr.at[zp, s] if a == 0 else sibg.at[zp, s],
                sibr.at[zp, s] if a == 0 else sibg.at[zp, s],
                red_send.at[a, zp, s],
                red_recv.at[a, zp, s],
                to_sib,
            ).wait_recv()
        for ref, refg, slot, row in incoming:
            wait_from(ref, refg, slot, s, row)
        total = dxb[2 * zp + c, s].astype(f32) + sibr[zp, s].astype(f32)
        totalg = dgb[2 * zp + c, s] + sibg[zp, s]
        for ref, refg, slot, row in incoming:
            total = total + ref[slot, s].astype(f32)
            totalg = totalg + refg[slot, s]
        return total, totalg

    def pass_sum(i, s, incoming, target, inward):
        total, totalg = combine(i, s, incoming)
        zp = order(i)
        dxb[2 * zp + c, s] = total.astype(bf)
        dgb[2 * zp + c, s] = totalg
        for copy in hop(i, s, target, inward):
            copy.start()

    def end_sums(s, which):
        @pl.when(end)
        def _():
            for i in which:
                pass_sum(i, s, (), to_in, True)

    def mid_sum(i, s):
        @pl.when(mid)
        def _():
            if i < 2:
                pass_sum(i, s, ((ro, rog, i, 2),), to_in, False)
            else:
                pass_sum(2, s, ((ri, rig, 0, 4),), to_out, False)

    def last_sum(s):
        @pl.when(mid)
        def _():
            total, totalg = combine(3, s, ((ro, rog, 2, 2), (ri, rig, 1, 4)))
            dx_out[s * 128 : (s + 1) * 128] = total
            dgt_out[s] = totalg

        @pl.when(end)
        def _():
            total, totalg = combine(3, s, ((ri, rig, 2, 4),))
            dx_out[s * 128 : (s + 1) * 128] = total
            dgt_out[s] = totalg

    eye = lax.broadcasted_iota(jnp.int32, (128, 128), 0) == lax.broadcasted_iota(
        jnp.int32, (128, 128), 1
    )
    mine = lax.broadcasted_iota(jnp.int32, (8, 128), 0) == e
    nt = (((1,), (1,)), ((), ()))
    tn = (((0,), (0,)), ((), ()))

    def half_step(s, pair, h):
        first = 4 * pair
        block = pl.ds(first, 4)
        both = jnp.dot(
            xall[block, s].reshape(512, 1536),
            win[:, h * 768 : (h + 1) * 768],
            preferred_element_type=f32,
        )
        gate = both[:, :384]
        up = both[:, 384:]
        back = lax.dot_general(
            gall[block, s].reshape(512, 1536),
            wout[h * 384 : (h + 1) * 384],
            nt,
            preferred_element_type=f32,
        )
        columns = []
        for j in range(4):
            row = jnp.sum(jnp.where(mine, gtall[first + j, s], 0.0), axis=0, keepdims=True)
            columns.append(jnp.sum(jnp.where(eye, row, 0.0), axis=1, keepdims=True))
        weight = jnp.concatenate(columns, axis=0)
        sig = jax.nn.sigmoid(gate)
        silu = gate * sig
        hidden = (silu * up).astype(bf).astype(f32)
        dgate = jnp.sum(hidden * back, axis=1, keepdims=True)
        for j in range(4):
            row = jnp.sum(
                jnp.where(eye, dgate[j * 128 : (j + 1) * 128], 0.0), axis=0, keepdims=True
            )
            part = jnp.where(mine, row, 0.0)
            dgb[first + j, s] = part if h == 0 else dgb[first + j, s] + part
        hg[block, s, :, h * 384 : (h + 1) * 384] = (
            (hidden * weight).astype(bf).reshape(4, 128, 384)
        )
        back = back * weight
        dgu[block, s, :, h * 768 : h * 768 + 384] = (
            (back * up * (sig * (1.0 + gate * (1.0 - sig)))).astype(bf).reshape(4, 128, 384)
        )
        dgu[block, s, :, h * 768 + 384 : (h + 1) * 768] = (
            (back * silu).astype(bf).reshape(4, 128, 384)
        )

    def dx_step(s, pair):
        first = 4 * pair
        block = pl.ds(first, 4)
        dxb[block, s] = (
            lax.dot_general(
                dgu[block, s].reshape(512, 1536), win[...], nt, preferred_element_type=f32
            )
            .astype(bf)
            .reshape(4, 128, 1536)
        )
        for j in range(2):
            for a in range(2):
                sib_sum(2 * pair + j, s, a).start()

    def out_copy(slot, s, first):
        return pltpu.make_async_copy(
            stage.at[slot], outp_hbm.at[pl.ds(first, 4), s], stage_sem.at[slot]
        )

    def out_step(slot, s, pair):
        first = 4 * pair
        stage[slot] = (
            jnp.dot(
                hg[pl.ds(first, 4), s].reshape(512, FF), wout[...], preferred_element_type=f32
            )
            .astype(bf)
            .reshape(4, 128, 1536)
        )
        out_copy(slot, s, first).start()

    far = 1 - hi
    near = hi

    def pair_of(t):
        return far + t * (1 - 2 * far)

    def i_piece(dd, p):
        return gin.at[pl.ds(pl.multiple_of(dd * 384 + p * PIECE, 16), PIECE)]

    def i_diag(p):
        return remote(
            i_piece(d_d, p), ti.at[p], i_send.at[0, p], i_recv.at[0, p], (to_x, to_y)[p % 2]
        )

    def i_direct(p):
        if p % 2 == 0:
            return remote(i_piece(d_x, p), xi.at[p], i_send.at[1, p], i_recv.at[1, p], to_x)
        return remote(i_piece(d_y, p), yi.at[p], i_send.at[1, p], i_recv.at[2, p], to_y)

    def i_summed(p):
        if p % 2 == 0:
            return remote(i_piece(d_y, p), yi.at[p], i_send.at[2, p], i_recv.at[2, p], to_y)
        return remote(i_piece(d_x, p), xi.at[p], i_send.at[2, p], i_recv.at[1, p], to_x)

    def i_middle(p):
        i_diag(p).wait_recv()
        dd = d_y if p % 2 == 0 else d_x
        rows = pl.ds(pl.multiple_of(dd * 384 + p * PIECE, 16), PIECE)
        gin[rows] = (gin[rows].astype(f32) + ti[p].astype(f32)).astype(bf)
        i_summed(p).start()

    def i_final(p):
        remote(xi.at[p], xi.at[p], i_send.at[1, p], i_recv.at[1, p], to_x).wait_recv()
        remote(yi.at[p], yi.at[p], i_send.at[1, p], i_recv.at[2, p], to_y).wait_recv()
        rows = pl.ds(pl.multiple_of(d * 384 + p * PIECE, 16), PIECE)
        gin_out[p * PIECE : (p + 1) * PIECE] = (
            gin[rows].astype(f32) + xi[p].astype(f32) + yi[p].astype(f32)
        ).astype(bf)

    def in_grad(dd, h):
        return lax.dot_general(
            xall[:, :, :, pl.ds(pl.multiple_of(dd * 384, 128), 384)].reshape(2048, 384),
            dgu[:, :, :, h * 768 : (h + 1) * 768].reshape(2048, 768),
            tn,
            preferred_element_type=f32,
        ).astype(bf)

    def in_first(dd):
        gin[pl.ds(pl.multiple_of(dd * 384, 16), 384)] = in_grad(dd, 0)

    @pl.loop(0, 2)
    def _(t):
        half_step(0, pair_of(t), 0)

    @pl.when(mid)
    def _():
        pass_on(1, 1)

    w_rest(1)

    @pl.when(end)
    def _():
        pass_on(1, 1)


    @pl.loop(0, 2)
    def _(t):
        pair = pair_of(t)
        half_step(0, pair, 1)
        dx_step(0, pair)

        @pl.when(t == 0)
        def _():
            out_step(0, 0, far)
            end_sums(0, (0, 1))
            pass_on(2, 1)

        @pl.when(t == 1)
        def _():
            out_step(1, 0, near)
            end_sums(0, (2,))
            pass_on(3, 1)
            from_sib(1)

    @pl.loop(0, 2)
    def _(t):
        half_step(1, pair_of(t), 0)

    mid_sum(0, 0)
    in_first(d_d)
    for p in range(4):
        i_diag(p).start()
    in_first(d_x)
    for p in (0, 2):
        i_direct(p).start()
    in_first(d_y)
    for p in (1, 3):
        i_direct(p).start()
    in_first(d)
    mid_sum(1, 0)

    @pl.loop(0, 2)
    def _(t):
        pair = pair_of(t)
        half_step(1, pair, 1)
        dx_step(1, pair)

        @pl.when(t == 0)
        def _():
            for p in range(4):
                i_middle(p)
            out_copy(0, 0, 0).wait()
            out_step(0, 1, far)
            end_sums(1, (0, 1))
            mid_sum(2, 0)

        @pl.when(t == 1)
        def _():
            out_copy(1, 0, 0).wait()
            out_step(1, 1, near)
            end_sums(1, (2,))
            mid_sum(0, 1)

    def g_piece(dd):
        return gout.at[pl.ds(pl.multiple_of(dd * 192, 16), PIECE)]

    def g_diag():
        return remote(g_piece(d_d), tg, g_send.at[0], g_recv.at[0], to_x)

    def g_direct():
        return remote(g_piece(d_x), xg, g_send.at[1], g_recv.at[1], to_x)

    def g_summed():
        return remote(g_piece(d_y), yg, g_send.at[2], g_recv.at[2], to_y)

    def g_middle():
        g_diag().wait_recv()
        rows = pl.ds(pl.multiple_of(d_y * 192, 16), PIECE)
        gout[rows] = (gout[rows].astype(f32) + tg[...].astype(f32)).astype(bf)
        g_summed().start()

    def out_grad(half):
        at = pl.multiple_of(half * 384, 128)
        gout[pl.ds(at, 384)] = lax.dot_general(
            hg[:, :, :, pl.ds(at, 384)].reshape(2048, 384),
            gall[...].reshape(2048, 1536),
            tn,
            preferred_element_type=f32,
        ).astype(bf)

    out_grad(1 - y)
    g_diag().start()
    out_grad(y)
    g_direct().start()
    rest = [
        pltpu.make_async_copy(
            gout.at[pl.ds(k * 192 + PIECE, PIECE)], gout_hbm.at[k], own_sem.at[k]
        )
        for k in range(4)
    ]
    for copy in rest:
        copy.start()

    def grad_copy(k):
        return pltpu.make_async_copy(
            stage.at[k % 2, pl.ds(0, 3), :, pl.ds(0, 768)], gin_hbm.at[k], stage_sem.at[k % 2]
        )

    for k in range(4):
        if k < 2:
            out_copy(k, 0, 0).wait()
        else:
            grad_copy(k - 2).wait()
        stage[k % 2, :3, :, :768] = in_grad(k, 1).reshape(3, 128, 768)
        grad_copy(k).start()
        if k == 0:
            mid_sum(1, 1)
        if k == 1:
            mid_sum(2, 1)
            g_middle()
        if k == 2:
            last_sum(0)

    for p in range(4):
        i_final(p)
    remote(xg, xg, g_send.at[1], g_recv.at[1], to_x).wait_recv()
    remote(yg, yg, g_send.at[1], g_recv.at[2], to_y).wait_recv()
    gout_out[...] = (
        gout[pl.ds(pl.multiple_of(d * 192, 16), PIECE)].astype(f32)
        + xg[...].astype(f32)
        + yg[...].astype(f32)
    ).astype(bf)
    for copy in rest:
        copy.wait()
    for k in (2, 3):
        grad_copy(k).wait()
    last_sum(1)

    for copy in (g_diag(), g_direct(), g_summed()):
        copy.wait_send()
    for p in range(4):
        for copy in (i_diag(p), i_direct(p), i_summed(p)):
            copy.wait_send()
    for h in range(2):
        for kind in range(2):
            for p in range(2):
                for row in range(3):
                    w_copy(h, kind, p, d, to_x, row).wait_send()
    for s in range(2):
        for zp in range(4):
            for a in range(2):
                sib_copy(a, zp, s).wait_send()
                sib_sum(zp, s, a).wait_send()

                @pl.when((zp <= z) & (z < 3))
                def _():
                    ag_copy(a, zp, s, 0).wait_send()

                @pl.when((zp >= z) & (z > 0))
                def _():
                    ag_copy(a, zp, s, 1).wait_send()

        for i in range(3):
            for copy in hop(i, s, to_in, True):
                copy.wait_send()


def expert_stage(rows, grads, gates_t, w_in, w_out):
    bf, f32 = jnp.bfloat16, jnp.float32
    shape = jax.ShapeDtypeStruct
    width = rows.shape[-1]
    hbm = pl.BlockSpec(memory_space=pltpu.HBM)
    vmem = pl.BlockSpec(memory_space=pltpu.VMEM)
    dma = pltpu.SemaphoreType.DMA
    return pl.pallas_call(
        expert_kernel,
        out_shape=(
            shape((CHUNK, width), f32),
            shape((2, 8, 128), f32),
            shape((8, 2, 128, width), bf),
            shape((4, 3, 128, FF), bf),
            shape((4, PIECE, width), bf),
            shape((PIECE, width), bf),
            shape((width // 4, FF), bf),
        ),
        in_specs=[hbm] * 5,
        out_specs=(vmem, vmem, hbm, hbm, hbm, vmem, vmem),
        scratch_shapes=[
            pltpu.VMEM((width, 2 * FF), bf),
            pltpu.VMEM((FF, width), bf),
            pltpu.VMEM((8, 2, 128, width), bf),
            pltpu.VMEM((8, 2, 128, width), bf),
            pltpu.VMEM((8, 2, 8, 128), f32),
            pltpu.VMEM((8, 2, 128, 2 * FF), bf),
            pltpu.VMEM((8, 2, 128, FF), bf),
            pltpu.VMEM((8, 2, 128, width), bf),
            pltpu.VMEM((8, 2, 8, 128), f32),
            pltpu.VMEM((4, 2, 128, width), bf),
            pltpu.VMEM((4, 2, 8, 128), f32),
            pltpu.VMEM((3, 2, 128, width), bf),
            pltpu.VMEM((3, 2, 8, 128), f32),
            pltpu.VMEM((3, 2, 128, width), bf),
            pltpu.VMEM((3, 2, 8, 128), f32),
            pltpu.VMEM((2, 4, 128, width), bf),
            pltpu.VMEM((FF, width), bf),
            *([pltpu.VMEM((PIECE, width), bf)] * 3),
            pltpu.VMEM((width, FF), bf),
            *([pltpu.VMEM((4, PIECE, FF), bf)] * 3),
            dma((9,)),
            dma((2,)),
            dma((3,)),
            dma((3,)),
            dma((3, 4)),
            dma((3, 4)),
            dma((3, 2, 2, 2)),
            dma((3, 2, 2, 2)),
            dma((2, 4, 2)),
            dma((2, 2, 4, 2)),
            dma((2, 4, 2)),
            dma((2, 4, 2)),
            dma((6, 4, 2)),
            dma((4, 4, 2)),
        ],
        compiler_params=pltpu.CompilerParams(
            collective_id=1, has_side_effects=True, vmem_limit_bytes=63 * 2**20
        ),
        name="expert_stage",
    )(
        rows.reshape(2, 128, width),
        grads.reshape(8, 2, 128, width),
        gates_t,
        w_in,
        w_out,
    )


def backward_kernel(
    dx_ref,
    dgt_ref,
    gates_ref,
    mixed_ref,
    cot_hbm,
    tok_hbm,
    q_hbm,
    kv_hbm,
    att_hbm,
    lens_ref,
    rope_hbm,
    wa_hbm,
    wb_hbm,
    gin_hbm,
    gout_hbm,
    outp_hbm,
    block_out,
    dtok_out,
    gq_out,
    gb_out,
    gkv_out,
    small_out,
    ein_out,
    eout_out,
    osib,
    oro,
    ori,
    wide,
    small,
    gq,
    gb,
    gk,
    sib_q,
    sib_b,
    sib_k,
    tq,
    xq,
    yq,
    roq,
    riq,
    tb,
    xb,
    yb,
    rob,
    rib,
    tw,
    xw,
    yw,
    row_,
    riw,
    te,
    xe,
    ye,
    le,
    td,
    xd,
    yd,
    ld,
    old,
    oslot,
    dat,
    dkv,
    tk,
    xk,
    yk,
    rope,
    cot_ref,
    tok_ref,
    q_ref,
    kv_ref,
    att_ref,
    load_sem,
    le_sem,
    old_sem,
    os_recv,
    os_send,
    ds_recv,
    ds_send,
    t_recv,
    x_recv,
    y_recv,
    t_send,
    d_send,
    s_send,
    ro_recv,
    ri_recv,
    hop_send,
):
    bf, f32 = jnp.bfloat16, jnp.float32
    d, e, z, c, x, y = place()
    d_x = d + 1 - 2 * x
    d_y = d + 2 - 4 * y
    d_d = 3 - d
    hi = lax.div(z, 2)
    zz = z * hi + (3 - z) * (1 - hi)
    other = 1 - c
    mid = zz == 2
    end = zz == 3
    to_x = (d_x, e)
    to_y = (d_y, e)
    to_sib = (d, 2 * z + other)
    e_in = e + 2 - 4 * hi
    to_in = (d, e_in)
    to_out = (d, jnp.where(zz == 2, e - 2 + 4 * hi, e_in))

    dqs = block_out
    dmix = dtok_out

    barrier = pltpu.get_barrier_semaphore()
    for target in (to_x, to_y, to_sib, to_in):
        pl.semaphore_signal(barrier, inc=1, device_id=target, device_id_type=MESH)

    @pl.when(mid)
    def _():
        pl.semaphore_signal(barrier, inc=1, device_id=to_out, device_id_type=MESH)

    pl.semaphore_wait(barrier, 7 - zz)

    def order(i):
        v = i if i < 2 else (5 - zz if i == 2 else zz)
        return v * hi + (3 - v) * (1 - hi)

    def across(k, src, t, fx, fy):
        def diag(i):
            return remote(
                src(d_d, i), t.at[i], t_send.at[k, i], t_recv.at[k, i], (to_x, to_y)[i % 2]
            )

        def direct(i):
            if i % 2 == 0:
                return remote(src(d_x, i), fx.at[i], d_send.at[k, i], x_recv.at[k, i], to_x)
            return remote(src(d_y, i), fy.at[i], d_send.at[k, i], y_recv.at[k, i], to_y)

        def summed(i, ref):
            if i % 2 == 0:
                return remote(ref, fy.at[i], s_send.at[k, i], y_recv.at[k, i], to_y)
            return remote(ref, fx.at[i], s_send.at[k, i], x_recv.at[k, i], to_x)

        def wait_t(i):
            remote(t.at[i], t.at[i], t_send.at[k, i], t_recv.at[k, i], to_x).wait_recv()

        def wait_xy(i):
            remote(fx.at[i], fx.at[i], d_send.at[k, i], x_recv.at[k, i], to_x).wait_recv()
            remote(fy.at[i], fy.at[i], d_send.at[k, i], y_recv.at[k, i], to_y).wait_recv()

        def drain(n):
            for i in range(n):
                diag(i).wait_send()
                direct(i).wait_send()
                summed(i, t.at[i]).wait_send()

        return diag, direct, summed, wait_t, wait_xy, drain

    def along(k, slot, ro, ri):
        def send(i, target, dst, recv):
            return remote(slot(i), dst.at[i], hop_send.at[k, i], recv.at[k, i], target)

        def to_ro(i):
            return send(i, to_in, ro, ro_recv)

        def to_ri(i):
            return send(i, to_in if i < 2 else to_out, ri, ri_recv)

        def wait_ro(i):
            remote(ro.at[i], ro.at[i], hop_send.at[k, i], ro_recv.at[k, i], to_in).wait_recv()

        def wait_ri(i):
            remote(ri.at[i], ri.at[i], hop_send.at[k, i], ri_recv.at[k, i], to_in).wait_recv()

        def drain():
            for i in range(3):
                to_ro(i).wait_send()

        return to_ro, to_ri, wait_ro, wait_ri, drain

    def expert_src(dd, p):
        return gin_hbm.at[pl.ds(pl.multiple_of(dd * 384 + p * PIECE, 16), PIECE)]

    e_diag, e_direct, e_summed, e_wait_t, e_wait_xy, e_drain = across(0, expert_src, te, xe, ye)

    def e_load(p, dd, j):
        return pltpu.make_async_copy(expert_src(dd, p), le.at[j], le_sem.at[j])

    def e_middle(p):
        load = e_load(p, d_y if p % 2 == 0 else d_x, 0)
        load.start()
        e_wait_t(p)
        load.wait()
        te[p] = (te[p].astype(f32) + le[0].astype(f32)).astype(bf)
        e_summed(p, te.at[p]).start()

    def e_final(p):
        load = e_load(p, d, 1)
        load.start()
        e_wait_xy(p)
        load.wait()
        total = le[1].astype(f32) + xe[p].astype(f32) + ye[p].astype(f32)
        ein_out[p * PIECE : (p + 1) * PIECE] = total.astype(bf)

    def d_src(dd):
        return gout_hbm.at[dd]

    def d_diag():
        return remote(d_src(d_d), td, t_send.at[5, 0], t_recv.at[5, 0], to_y)

    def d_direct():
        return remote(d_src(d_y), yd, d_send.at[5, 0], y_recv.at[5, 0], to_y)

    def d_summed():
        return remote(td, xd, s_send.at[5, 0], x_recv.at[5, 0], to_x)

    def d_load(dd, j):
        return pltpu.make_async_copy(d_src(dd), ld, le_sem.at[j])

    def d_middle():
        load = d_load(d_x, 2)
        load.start()
        d_diag().wait_recv()
        load.wait()
        td[...] = (td[...].astype(f32) + ld[...].astype(f32)).astype(bf)
        d_summed().start()

    def d_final():
        load = d_load(d, 3)
        load.start()
        d_summed().wait_recv()
        d_direct().wait_recv()
        load.wait()
        eout_out[...] = (
            ld[...].astype(f32) + xd[...].astype(f32) + yd[...].astype(f32)
        ).astype(bf)

    def store_q(total):
        gq_out[...] = total

    def store_b(total):
        gb_out[...] = total

    def store_k(total):
        gkv_out[...] = total[:, :512]
        small_out[...] = lax.dot_general(
            eye[:16],
            total[:, 512:],
            (((1,), (1,)), ((), ())),
            preferred_element_type=f32,
            precision=highest,
        )

    dense = (
        (gq, sib_q, tq, xq, yq, roq, riq, store_q),
        (gb, sib_b, tb, xb, yb, rob, rib, store_b),
        (gk, sib_k, tw, xw, yw, row_, riw, store_k),
    )

    def dense_stream(j):
        grad, sib, t, fx, fy, ro, ri, out = dense[j]

        def src(dd, i):
            return grad.at[dd * 4 + order(i), c]

        diag, direct, summed, wait_t, wait_xy, drain = across(1 + j, src, t, fx, fy)

        def own_slot(i):
            return grad.at[d * 4 + order(i), c]

        to_ro, to_ri, wait_ro, wait_ri, drain_z = along(j, own_slot, ro, ri)

        def sib_copy():
            return remote(grad.at[:, other], sib, ds_send.at[j], ds_recv.at[j], to_sib)

        def begin():
            sib_copy().wait_recv()

            @pl.loop(0, 16)
            def _(k):
                grad[k, c] = (grad[k, c].astype(f32) + sib[k].astype(f32)).astype(bf)

            for i in range(4):
                diag(i).start()
            for i in range(4):
                direct(i).start()

        def middle(i):
            dd = d_y if i % 2 == 0 else d_x
            wait_t(i)
            at = dd * 4 + order(i)
            grad[at, c] = (grad[at, c].astype(f32) + t[i].astype(f32)).astype(bf)
            summed(i, src(dd, i)).start()

        def local(i):
            return grad[d * 4 + order(i), c].astype(f32) + fx[i].astype(f32) + fy[i].astype(f32)

        def put(i, total):
            grad[d * 4 + order(i), c] = total.astype(bf)

        def last(i):
            wait_xy(i)
            if i == 3:
                return

            @pl.when(end)
            def _():
                put(i, local(i))
                to_ro(i).start()

        def hop(i):
            @pl.when(mid)
            def _():
                if i < 2:
                    wait_ro(i)
                    put(i, local(i) + ro[i].astype(f32))
                else:
                    wait_ri(0)
                    put(2, local(2) + ri[0].astype(f32))
                to_ri(i).start()

        def finish():
            @pl.when(mid)
            def _():
                wait_ro(2)
                wait_ri(1)
                out(local(3) + ro[2].astype(f32) + ri[1].astype(f32))

            @pl.when(end)
            def _():
                wait_ri(2)
                out(local(3) + ri[2].astype(f32))

        def drain_all():
            sib_copy().wait_send()
            drain(4)
            drain_z()

        return sib_copy, begin, middle, last, hop, finish, drain_all

    q_sib, q_begin, q_middle, q_last, q_hop, q_finish, q_drain = dense_stream(0)
    b_sib, b_begin, b_middle, b_last, b_hop, b_finish, b_drain = dense_stream(1)
    w_sib, w_begin, w_middle, w_last, w_hop, w_finish, w_drain = dense_stream(2)

    def out_rows(i, lane):
        return outp_hbm.at[pl.ds(pl.multiple_of((2 * order(i) + lane) * CHUNK, CHUNK), CHUNK)]

    def out_sib(i):
        return remote(out_rows(i, other), osib.at[i], os_send.at[i], os_recv.at[i], to_sib)

    o_ro, o_ri, o_wait_ro, o_wait_ri, o_drain = along(3, lambda i: oslot.at[i], oro, ori)

    def out_sum(i, incoming, store):
        out_sib(i).wait_recv()
        for half in range(2):
            rows = pl.ds(half * 128, 128)
            loads = [
                pltpu.make_async_copy(ref.at[rows], old.at[j], old_sem.at[j])
                for j, ref in enumerate([out_rows(i, c), osib.at[i]] + incoming)
            ]
            for load in loads:
                load.start()
            for load in loads:
                load.wait()
            total = old[0].astype(f32)
            for j in range(1, len(loads)):
                total = total + old[j].astype(f32)
            store(slice(half * 128, (half + 1) * 128), total)

    def out_slot(i):
        def store(rows, total):
            oslot[i, rows] = total.astype(bf)

        return store

    def out_end(i):
        @pl.when(end)
        def _():
            out_sum(i, [], out_slot(i))
            o_ro(i).start()

    def out_mid(i):
        @pl.when(mid)
        def _():
            if i < 2:
                o_wait_ro(i)
                out_sum(i, [oro.at[i]], out_slot(i))
            else:
                o_wait_ri(0)
                out_sum(2, [ori.at[0]], out_slot(2))
            o_ri(i).start()

    def out_finish():
        def store(rows, total):
            total = total + mixed_ref[rows]
            slot = d * 128 + lax.broadcasted_iota(jnp.int32, (128, 1), 0)
            live = slot < lens_ref[rows.start // 128]
            block_out[rows] = jnp.where(live, total, 0.0).astype(bf)

        @pl.when(mid)
        def _():
            o_wait_ro(2)
            o_wait_ri(1)
            out_sum(3, [oro.at[2], ori.at[1]], store)

        @pl.when(end)
        def _():
            o_wait_ri(2)
            out_sum(3, [ori.at[2]], store)

    def kv_src(dd, i):
        return dkv.at[dd, pl.ds(i * 128, 128)]

    k_diag, k_direct, k_summed, k_wait_t, k_wait_xy, k_drain = across(4, kv_src, tk, xk, yk)

    def k_middle(i):
        dd = d_y if i % 2 == 0 else d_x
        k_wait_t(i)
        rows = slice(i * 128, (i + 1) * 128)
        dkv[dd, rows] = (dkv[dd, rows].astype(f32) + tk[i].astype(f32)).astype(bf)
        k_summed(i, kv_src(dd, i)).start()

    small_load = pltpu.make_async_copy(wa_hbm.at[:, pl.ds(2048, 128)], small, load_sem.at[0])
    wb_load = pltpu.make_async_copy(wb_hbm, wide.at[:, pl.ds(0, 1536)], load_sem.at[1])
    wa_load = pltpu.make_async_copy(wa_hbm.at[:, pl.ds(0, 2048)], wide, load_sem.at[2])
    rope_load = pltpu.make_async_copy(
        rope_hbm.at[:, pl.ds(pl.multiple_of(d * 128, 128), 128)], rope, load_sem.at[3]
    )
    small_load.start()
    loads = [
        pltpu.make_async_copy(src, dst, load_sem.at[4 + j])
        for j, (src, dst) in enumerate(
            (
                (cot_hbm, cot_ref),
                (att_hbm, att_ref),
                (q_hbm, q_ref),
                (kv_hbm, kv_ref),
                (tok_hbm, tok_ref),
            )
        )
    ]
    for load in loads[:2]:
        load.start()
    wb_load.start()
    rope_load.start()
    for load in loads[2:]:
        load.start()
    for p in range(4):
        e_diag(p).start()
    for p in (0, 2):
        e_direct(p).start()
    d_diag().start()
    for i in range(4):
        out_sib(i).start()
    out_end(0)

    nt = (((1,), (1,)), ((), ()))
    tn = (((0,), (0,)), ((), ()))

    def dot_nt(a, b):
        return lax.dot_general(a, b, nt, preferred_element_type=f32)

    def dot_tn(a, b):
        return lax.dot_general(a, b, tn, preferred_element_type=f32)

    eye = (
        lax.broadcasted_iota(jnp.int32, (128, 128), 0)
        == lax.broadcasted_iota(jnp.int32, (128, 128), 1)
    ).astype(f32)
    eye_low = eye.astype(bf)
    gates = jnp.concatenate([gates_ref[s] for s in range(2)], axis=1)
    dgate = jnp.concatenate([dgt_ref[s] for s in range(2)], axis=1)
    dlogit = gates * (dgate - jnp.sum(gates * dgate, axis=0, keepdims=True))
    dl_hi = dlogit.astype(bf).astype(f32)
    dl = jnp.concatenate([dl_hi, dlogit - dl_hi], axis=0).astype(bf)
    small_load.wait()
    small_t = dot_nt(eye_low[:16], small[...])
    router = jnp.concatenate([small_t[:8]] * 2, axis=0).astype(bf)
    dn2 = dx_ref[...] + dot_tn(dl, router)
    mixed = mixed_ref[...]
    inv2 = lax.rsqrt(jnp.mean(mixed * mixed, axis=1, keepdims=True) + epsilon)
    n2 = mixed * inv2
    normed2 = (n2 * small_t[9:10]).astype(bf)
    router_sum = jnp.dot(dl, normed2, preferred_element_type=f32)
    router_sum = router_sum[:8] + router_sum[8:]
    mid_sum = jnp.sum(dn2 * n2, axis=0, keepdims=True)
    loads[0].wait()
    loads[1].wait()
    grads = [
        jnp.where(
            d * 128 + lax.broadcasted_iota(jnp.int32, (128, 1), 0) < lens_ref[s],
            cot_ref[s * 128 : (s + 1) * 128].astype(f32),
            0.0,
        )
        for s in range(2)
    ]
    u = dn2 * small_t[9:10]
    dmixed = jnp.concatenate(grads, axis=0) + inv2 * (u - n2 * jnp.mean(u * n2, axis=1, keepdims=True))
    dmix[...] = dmixed
    dproj = dmixed.astype(bf)
    for r in range(4):
        part = dot_tn(att_ref[:, r * 384 : (r + 1) * 384], dproj)
        gb[4 * r : 4 * r + 4] = part.astype(bf).reshape(4, 2, 48, 1536)
    b_sib().start()
    wb_load.wait()
    datt = dot_nt(dproj, wide[:, :1536]).astype(bf)
    for head in range(QUERY_HEADS):
        for s in range(2):
            at = (s * QUERY_HEADS + head) * 128
            dat[at : at + 128] = datt[s * 128 : (s + 1) * 128, head * 128 : (head + 1) * 128]
    wa_load.start()
    b_begin()
    out_end(1)

    query_pos = d * 128 + lax.broadcasted_iota(jnp.int32, (128, 512), 0)
    key_pos = lax.broadcasted_iota(jnp.int32, (128, 512), 1)
    rope_load.wait()
    for load in loads[2:]:
        load.wait()
    cos_rows = rope[0]
    sin_rows = rope[1]
    scale = HEAD_SIZE ** (-0.5)

    def unrotate_rows(v, cos, sin):
        return v * cos - pltpu.roll(v, 64, 1) * sin

    def attend(n):
        s = lax.div(n, 2)
        h = lax.rem(n, 2)
        srow = pl.ds(pl.multiple_of(s * 128, 128), 128)
        kcol = pl.ds(pl.multiple_of(h * 128, 128), 128)
        vcol = pl.ds(pl.multiple_of(256 + h * 128, 128), 128)
        lens = lens_ref[s]
        allowed = (key_pos <= query_pos) & (key_pos < lens)
        ks = kv_ref[:, srow, kcol].reshape(512, 128)
        vs = kv_ref[:, srow, vcol].reshape(512, 128)
        dk = None
        dv = None
        for half in range(2):
            rows = pl.ds(pl.multiple_of(n * 768 + half * 384, 128), 384)
            qh = q_ref[rows]
            dh = dat[rows]
            scores = dot_nt(qh, ks).reshape(3, 128, 512) * scale
            scores = jnp.where(allowed[None], scores, -1e30)
            probs = jnp.exp(scores - jnp.max(scores, axis=-1, keepdims=True))
            probs = probs * (1.0 / jnp.sum(probs, axis=-1, keepdims=True))
            dprobs = dot_nt(dh, vs).reshape(3, 128, 512)
            delta = jnp.sum(probs * dprobs, axis=-1, keepdims=True)
            dscores = (probs * (dprobs - delta)).astype(bf).reshape(384, 512)
            low = probs.astype(bf).reshape(384, 512)
            dq = jnp.dot(dscores, ks, preferred_element_type=f32) * scale
            for j in range(3):
                dqs[srow, pl.ds(pl.multiple_of(h * 768 + (half * 3 + j) * 128, 128), 128)] = (
                    unrotate_rows(dq[j * 128 : (j + 1) * 128], cos_rows, sin_rows).astype(bf)
                )
            dk_part = dot_tn(dscores, qh)
            dv_part = dot_tn(low, dh)
            dk = dk_part if dk is None else dk + dk_part
            dv = dv_part if dv is None else dv + dv_part
        dkv[:, srow, kcol] = (dk * scale).astype(bf).reshape(4, 128, 128)
        dkv[:, srow, vcol] = dv.astype(bf).reshape(4, 128, 128)

    pl.loop(0, 2)(attend)
    for i in range(4):
        b_middle(i)
    e_direct(1).start()
    e_middle(1)
    out_mid(0)
    pl.loop(2, 4)(attend)
    for i in range(2):
        k_diag(i).start()
    for i in range(2):
        k_direct(i).start()
    for i in range(4):
        b_last(i)
    out_end(2)

    tok = tok_ref[...].astype(f32)
    inv1 = lax.rsqrt(jnp.mean(tok * tok, axis=1, keepdims=True) + epsilon)
    n1 = tok * inv1
    normed = (n1 * small_t[8:9]).astype(bf)
    for r in range(4):
        part = dot_tn(normed[:, r * 384 : (r + 1) * 384], dqs[...])
        gq[4 * r : 4 * r + 4] = part.astype(bf).reshape(4, 2, 48, 1536)
    q_sib().start()
    k_middle(0)
    k_middle(1)
    q_begin()
    wa_load.wait()
    dn1 = dot_nt(dqs[...], wide[:, :1536])

    for i in range(2):
        k_wait_xy(i)
    own = jnp.concatenate(
        [
            dkv[d, i * 128 : (i + 1) * 128].astype(f32) + xk[i].astype(f32) + yk[i].astype(f32)
            for i in range(2)
        ],
        axis=0,
    )
    cos_two = jnp.concatenate([cos_rows] * 2, axis=0)
    sin_two = jnp.concatenate([sin_rows] * 2, axis=0)
    dkv_own = jnp.concatenate(
        [
            unrotate_rows(own[:, h * 128 : (h + 1) * 128], cos_two, sin_two)
            for h in range(2)
        ]
        + [own[:, 256:]],
        axis=1,
    ).astype(bf)
    dn1 = dn1 + dot_nt(dkv_own, wide[:, 1536:])
    pre_sum = jnp.sum(dn1 * n1, axis=0, keepdims=True)
    row8 = lax.broadcasted_iota(jnp.int32, (8, 1536), 0)
    gains = jnp.where(row8 == 0, pre_sum, jnp.where(row8 == 1, mid_sum, 0.0))
    smalls = jnp.concatenate([router_sum, gains], axis=0).astype(bf)
    for r in range(4):
        cols = slice(r * 384, (r + 1) * 384)
        part = dot_tn(normed[:, cols], dkv_own)
        gk[4 * r : 4 * r + 4, :, :, :512] = part.astype(bf).reshape(4, 2, 48, 512)
        part = dot_tn(smalls[:, cols], eye_low[:16])
        gk[4 * r : 4 * r + 4, :, :, 512:] = part.astype(bf).reshape(4, 2, 48, 128)
    w_sib().start()
    u = dn1 * small_t[8:9]
    dtok_out[...] = dmix[...] + inv1 * (u - n1 * jnp.mean(u * n1, axis=1, keepdims=True))

    for i in range(4):
        q_middle(i)
    w_begin()
    e_direct(3).start()
    b_hop(0)
    b_hop(1)
    out_mid(1)
    out_mid(2)
    for i in range(4):
        q_last(i)
    for i in range(4):
        w_middle(i)
    d_direct().start()
    d_middle()
    for p in (3, 0, 2):
        e_middle(p)
    b_hop(2)
    for i in range(3):
        q_hop(i)
    out_finish()
    b_finish()
    for i in range(4):
        w_last(i)
    for i in range(3):
        w_hop(i)
    q_finish()
    for p in range(4):
        e_final(p)
    d_final()
    w_finish()

    e_drain(4)
    for copy in (d_diag(), d_direct(), d_summed()):
        copy.wait_send()
    k_drain(2)
    q_drain()
    b_drain()
    w_drain()
    o_drain()
    for i in range(4):
        out_sib(i).wait_send()


def backward_stage(dx, dgt, gates, mixed, cot, tok, q, kv, att, lens, rope, wa, wb, gin, gout, outp):
    bf, f32 = jnp.bfloat16, jnp.float32
    shape = jax.ShapeDtypeStruct
    width = tok.shape[-1]
    hbm = pl.BlockSpec(memory_space=pltpu.HBM)
    vmem = pl.BlockSpec(memory_space=pltpu.VMEM)
    smem = pl.BlockSpec(memory_space=pltpu.SMEM)
    dma = pltpu.SemaphoreType.DMA
    widths = (width, width, 640)
    dense = []
    for w in widths:
        dense += [pltpu.VMEM((4, 48, w), bf)] * 3 + [pltpu.VMEM((3, 48, w), bf)] * 2
    return pl.pallas_call(
        backward_kernel,
        out_shape=(
            shape((CHUNK, width), bf),
            shape((CHUNK, width), f32),
            shape((48, width), f32),
            shape((48, width), f32),
            shape((48, 512), f32),
            shape((16, 48), f32),
            shape((384, FF), bf),
            shape((PIECE, width), bf),
            shape((4, CHUNK, width), bf),
            shape((3, CHUNK, width), bf),
            shape((3, CHUNK, width), bf),
        ),
        in_specs=[vmem] * 4 + [hbm] * 5 + [smem] + [hbm] * 6,
        out_specs=[vmem] * 8 + [hbm] * 3,
        scratch_shapes=[
            pltpu.VMEM((width, 2048), bf),
            pltpu.VMEM((width, 128), bf),
            *[pltpu.VMEM((16, 2, 48, w), bf) for w in widths],
            *[pltpu.VMEM((16, 48, w), bf) for w in widths],
            *dense,
            *([pltpu.VMEM((4, PIECE, FF), bf)] * 3),
            pltpu.VMEM((2, PIECE, FF), bf),
            *([pltpu.VMEM((PIECE, width), bf)] * 4),
            pltpu.VMEM((4, 128, width), bf),
            pltpu.VMEM((3, CHUNK, width), bf),
            pltpu.VMEM((2 * QUERY_HEADS * 128, 128), bf),
            pltpu.VMEM((4, CHUNK, 512), bf),
            *([pltpu.VMEM((2, 128, 512), bf)] * 3),
            pltpu.VMEM((2, 128, 128), f32),
            *[pltpu.VMEM(ref.shape, bf) for ref in (cot, tok, q, kv, att)],
            dma((9,)),
            dma((4,)),
            dma((4,)),
            dma((4,)),
            dma((4,)),
            dma((3,)),
            dma((3,)),
            dma((6, 4)),
            dma((6, 4)),
            dma((6, 4)),
            dma((6, 4)),
            dma((6, 4)),
            dma((6, 4)),
            dma((4, 3)),
            dma((4, 3)),
            dma((4, 3)),
        ],
        compiler_params=pltpu.CompilerParams(
            collective_id=3, has_side_effects=True, vmem_limit_bytes=64 * 2**20 - 65536
        ),
        name="backward_stage",
    )(dx, dgt, gates, mixed, cot, tok, q, kv, att, lens, rope, wa, wb, gin, gout, outp)


def rope_constant(slots):
    half = HEAD_SIZE // 2
    inv_freq = np.float32(rope_base) ** (-(np.arange(half, dtype=np.float32) * 2.0 / HEAD_SIZE))
    angles = np.arange(slots, dtype=np.float32)[:, None] * inv_freq[None, :].astype(np.float32)
    cos, sin = np.cos(angles), np.sin(angles)
    return np.stack(
        [np.concatenate([cos, cos], axis=1), np.concatenate([-sin, sin], axis=1)]
    ).astype(np.float32)


def fast_local(
    tokens,
    lengths,
    routes,
    prenorm,
    w_query,
    key_value_weight,
    w_output,
    midnorm,
    w_router,
    expert_in,
    expert_out,
    cotangent,
):
    f32 = jnp.float32
    seqs, token_rows, width = tokens.shape
    rows = seqs * token_rows
    tok = tokens.reshape(rows, width)
    cot = cotangent.reshape(rows, width)
    rope = jnp.asarray(rope_constant(token_rows * lax.axis_size("dp")))
    full_a, full_b, full_out, gall, q_rot, kv_all, attended, mixed, normed2, gates = attention_stage(
        tok,
        w_query,
        key_value_weight,
        w_router.T,
        prenorm[None],
        midnorm[None],
        w_output,
        cot,
        expert_out[0],
        rope,
        lengths,
        jnp.transpose(routes, (0, 2, 1)),
    )
    dx, dgate, outp, gin, gout, out_first, g_first = expert_stage(normed2, gall, gates, expert_in[0], full_out)
    block_out, grad_tokens, g_query, g_b, g_kv, small, g_second, out_second = backward_stage(
        dx, dgate, gates, mixed, cot, tok, q_rot, kv_all, attended, lengths, rope,
        full_a, full_b, gin.reshape(width, FF), gout, outp.reshape(8 * rows, width),
    )[:8]
    half = FF // 2
    g_in = jnp.concatenate(
        [g_first[:, :half], g_second[:, :half], g_first[:, half:], g_second[:, half:]], axis=1
    )
    return (
        block_out.reshape(seqs, token_rows, width),
        grad_tokens.reshape(seqs, token_rows, width),
        small[8],
        g_query,
        g_kv,
        g_b,
        small[9],
        small[:8].T,
        g_in.astype(f32)[None],
        jnp.concatenate([out_first, out_second], axis=0).astype(f32)[None],
    )


def solution(mesh):
    placed = (
        P("expert", "dp", None),
        P("expert"),
        P("expert", "dp", None),
        P(("dp", "expert")),
        P(("dp", "expert"), None),
        P(("dp", "expert"), None),
        P(("dp", "expert"), None),
        P(("dp", "expert")),
        P(("dp", "expert"), None),
        P("expert", "dp", None),
        P("expert", "dp", None),
        P("expert", "dp", None),
    )
    fits = mesh.shape["dp"] == 4 and mesh.shape["expert"] == 8
    return jax.shard_map(
        fast_local if fits else local,
        mesh=mesh,
        in_specs=placed,
        out_specs=(
            P("expert", "dp", None),
            P("expert", "dp", None),
            P(("dp", "expert")),
            P(("dp", "expert"), None),
            P(("dp", "expert"), None),
            P(("dp", "expert"), None),
            P(("dp", "expert")),
            P(("dp", "expert"), None),
            P("expert", "dp", None),
            P("expert", "dp", None),
        ),
        check_vma=False,
    )
```

```python
import jax
import jax.numpy as jnp
import numpy as np
from jax import lax
from jax.experimental import pallas as pl
from jax.experimental.pallas import tpu as pltpu
from jax.sharding import PartitionSpec as P

QUERY_HEADS = 12
KEY_VALUE_HEADS = 2
HEAD_SIZE = 128
FF = 768
TOP = 4


epsilon = 1e-06
rope_base = 10000.0
highest = lax.Precision.HIGHEST


def rope_tables(positions):
    half_width = HEAD_SIZE // 2
    inv_freq = rope_base ** (-(jnp.arange(half_width, dtype=jnp.float32) * 2.0 / HEAD_SIZE))
    angles = positions.astype(jnp.float32)[:, None] * inv_freq[None, :]
    return (jnp.cos(angles), jnp.sin(angles))


def apply_rotation(values, cosine_table, sine_table):
    half_width = values.shape[-1] // 2
    first_half = values[..., :half_width]
    second = values[..., half_width:]
    cos_rows = cosine_table[:, None, :]
    sin_rows = sine_table[:, None, :]
    return jnp.concatenate(
        [first_half * cos_rows - second * sin_rows, second * cos_rows + first_half * sin_rows],
        axis=-1,
    )


def unrotate(values, cosine_table, sine_table):
    half_width = values.shape[-1] // 2
    first_half = values[..., :half_width]
    second = values[..., half_width:]
    cos_rows = cosine_table[:, None, :]
    sin_rows = sine_table[:, None, :]
    return jnp.concatenate(
        [first_half * cos_rows + second * sin_rows, second * cos_rows - first_half * sin_rows],
        axis=-1,
    )


def rms_parts(values):
    inverse = lax.rsqrt(jnp.mean(values * values, axis=-1, keepdims=True) + epsilon)
    return (values * inverse, inverse)


def norm_back(grad_normed, normalized_input, inverse, gain):
    scaled = grad_normed * gain
    return inverse * (
        scaled - normalized_input * jnp.mean(scaled * normalized_input, axis=-1, keepdims=True)
    )


def slot_index(route_rows, expert_count, capacity):
    flat_routes = route_rows.reshape(-1)
    onehot = (flat_routes[:, None] == jnp.arange(expert_count, dtype=jnp.int32)[None, :]).astype(
        jnp.int32
    )
    before = jnp.cumsum(onehot, axis=0) - onehot
    within = jnp.sum(before * onehot, axis=-1)
    return flat_routes * capacity + within


def masked_scores(query_matrix, key_rows, allowed):
    scores = jnp.einsum(
        "qhgd,khd->hgqk", query_matrix, key_rows, preferred_element_type=jnp.float32
    ) * HEAD_SIZE ** (-0.5)
    return jnp.where(allowed[None, None], scores, -1e30)


def local(
    tokens,
    lengths,
    routes,
    prenorm,
    w_query,
    key_value_weight,
    w_output,
    midnorm,
    w_router,
    expert_in,
    expert_out,
    cotangent,
):
    micro_count, token_rows, hidden_width = tokens.shape
    dp_size = lax.axis_size("dp")
    expert_size = lax.axis_size("expert")
    dp_rank = lax.axis_index("dp")
    local_experts = expert_in.shape[0]
    expert_count = local_experts * expert_size
    capacity = max(2, 3 * token_rows * TOP // (2 * expert_count))
    query_group_width = QUERY_HEADS // KEY_VALUE_HEADS
    expert_slot_total = token_rows * dp_size
    score_scale = HEAD_SIZE ** (-0.5)
    positions = dp_rank * token_rows + jnp.arange(token_rows, dtype=jnp.int32)
    key_pos = jnp.arange(expert_slot_total, dtype=jnp.int32)
    cosine_table, sine_table = rope_tables(positions)
    total_prenorm = jnp.zeros((hidden_width,), jnp.float32)
    total_query = jnp.zeros((hidden_width, QUERY_HEADS * HEAD_SIZE), jnp.float32)
    total_key_value = jnp.zeros((hidden_width, 2 * KEY_VALUE_HEADS * HEAD_SIZE), jnp.float32)
    total_output = jnp.zeros((QUERY_HEADS * HEAD_SIZE, hidden_width), jnp.float32)
    total_midnorm = jnp.zeros((hidden_width,), jnp.float32)
    total_router = jnp.zeros((hidden_width, expert_count), jnp.float32)
    total_upper = jnp.zeros((local_experts, hidden_width, 2 * FF), jnp.float32)
    total_down = jnp.zeros((local_experts, FF, hidden_width), jnp.float32)
    outputs_list = []
    grads_list = []
    for micro_step in range(micro_count):
        dense_all = (
            lax.all_gather(prenorm, ("dp", "expert"), axis=0, tiled=True),
            lax.all_gather(w_query, ("dp", "expert"), axis=0, tiled=True),
            lax.all_gather(key_value_weight, ("dp", "expert"), axis=0, tiled=True),
            lax.all_gather(w_output, ("dp", "expert"), axis=0, tiled=True),
            lax.all_gather(midnorm, ("dp", "expert"), axis=0, tiled=True),
            lax.all_gather(w_router, ("dp", "expert"), axis=0, tiled=True),
        )
        expert_all = (
            lax.all_gather(expert_in, "dp", axis=1, tiled=True),
            lax.all_gather(expert_out, "dp", axis=1, tiled=True),
        )
        gain_one = dense_all[0].astype(jnp.float32)
        query_all = dense_all[1]
        keyval_all = dense_all[2]
        output_all = dense_all[3]
        gain_two = dense_all[4].astype(jnp.float32)
        router_all = dense_all[5]
        gateup_all = expert_all[0]
        down_all = expert_all[1]
        input_rows = tokens[micro_step].astype(jnp.float32)
        length = lengths[micro_step]
        route_rows = routes[micro_step]
        live_rows = (positions < length)[:, None]
        normed_one, inverse_one = rms_parts(input_rows)
        normalized_input = (normed_one * gain_one).astype(jnp.bfloat16)
        query_pre = jnp.dot(
            normalized_input, query_all, preferred_element_type=jnp.float32
        ).reshape(token_rows, QUERY_HEADS, HEAD_SIZE)
        keyval_pre = jnp.dot(
            normalized_input, keyval_all, preferred_element_type=jnp.float32
        ).reshape(token_rows, 2, KEY_VALUE_HEADS, HEAD_SIZE)
        query_matrix = (
            apply_rotation(query_pre, cosine_table, sine_table)
            .astype(jnp.bfloat16)
            .reshape(token_rows, KEY_VALUE_HEADS, query_group_width, HEAD_SIZE)
        )
        local_key_rows = apply_rotation(keyval_pre[:, 0], cosine_table, sine_table).astype(
            jnp.bfloat16
        )
        local_value_rows = keyval_pre[:, 1].astype(jnp.bfloat16)
        packed_tokens = jnp.stack([local_key_rows, local_value_rows], axis=1).reshape(
            token_rows, 2 * KEY_VALUE_HEADS * HEAD_SIZE
        )
        gathered_rows = lax.all_gather(packed_tokens, "dp", axis=0, tiled=True).reshape(
            expert_slot_total, 2, KEY_VALUE_HEADS, HEAD_SIZE
        )
        key_rows = gathered_rows[:, 0]
        value_rows = gathered_rows[:, 1]
        allowed = (key_pos[None, :] <= positions[:, None]) & (key_pos[None, :] < length)
        scores = masked_scores(query_matrix, key_rows, allowed)
        top_score = jnp.max(scores, axis=-1, keepdims=True)
        weights = jnp.exp(scores - top_score)
        weight_total = jnp.sum(weights, axis=-1, keepdims=True)
        log_total = top_score + jnp.log(weight_total)
        probs_low = (weights / weight_total).astype(jnp.bfloat16)
        attended = jnp.einsum(
            "hgqk,khd->qhgd", probs_low, value_rows, preferred_element_type=jnp.float32
        )
        attended = attended.reshape(token_rows, QUERY_HEADS * HEAD_SIZE).astype(jnp.bfloat16)
        mixed_rows = input_rows + jnp.dot(attended, output_all, preferred_element_type=jnp.float32)
        normed_mid, inverse_two = rms_parts(mixed_rows)
        normed_two = (normed_mid * gain_two).astype(jnp.bfloat16)
        logits = jnp.dot(normed_two, router_all, preferred_element_type=jnp.float32)
        onehot = (
            route_rows[:, :, None] == jnp.arange(expert_count, dtype=jnp.int32)[None, None, :]
        ).astype(jnp.float32)
        chosen = jnp.sum(onehot * logits[:, None, :], axis=-1)
        gate_values = jax.nn.softmax(chosen, axis=-1)
        slot_idx = slot_index(route_rows, expert_count, capacity)
        send_rows = jnp.zeros((expert_count * capacity, hidden_width), jnp.bfloat16)
        send_rows = send_rows.at[slot_idx].set(jnp.repeat(normed_two, TOP, axis=0))
        received = lax.all_to_all(
            send_rows.reshape(expert_count, capacity, hidden_width),
            "expert",
            split_axis=0,
            concat_axis=0,
            tiled=True,
        )
        item_count = received.shape[1]
        grouped = received.reshape(expert_size, local_experts, item_count, hidden_width)
        gate_up = jnp.einsum(
            "slcd,ldf->slcf", grouped, gateup_all, preferred_element_type=jnp.float32
        )
        hidden = (jax.nn.silu(gate_up[..., :FF]) * gate_up[..., FF:]).astype(jnp.bfloat16)
        result = jnp.einsum(
            "slcf,lfd->slcd", hidden, down_all, preferred_element_type=jnp.float32
        ).astype(jnp.bfloat16)
        back_rows = lax.all_to_all(
            result.reshape(expert_count, item_count, hidden_width),
            "expert",
            split_axis=0,
            concat_axis=0,
            tiled=True,
        )
        back_rows, kept_rows, kept_gateup = (
            back_rows,
            received,
            gate_up.reshape(expert_count, item_count, 2 * FF),
        )
        returned = back_rows.reshape(expert_count * capacity, hidden_width)[slot_idx].reshape(
            token_rows, TOP, hidden_width
        )
        returned_wide = returned.astype(jnp.float32)
        expert_sum = jnp.sum(gate_values[:, :, None] * returned_wide, axis=1)
        final_rows = jnp.where(live_rows, mixed_rows + expert_sum, 0.0)
        outputs_list.append(final_rows.astype(jnp.bfloat16))
        grad_rows = jnp.where(live_rows, cotangent[micro_step].astype(jnp.float32), 0.0)
        grad_gate = jnp.sum(grad_rows[:, None, :] * returned_wide, axis=-1)
        grad_chosen = gate_values * (
            grad_gate - jnp.sum(gate_values * grad_gate, axis=-1, keepdims=True)
        )
        grad_logits = jnp.sum(onehot * grad_chosen[:, :, None], axis=1)
        router_term = jnp.dot(normed_two.astype(jnp.float32).T, grad_logits, precision=highest)
        grad_normtwo = jnp.dot(grad_logits, router_all.astype(jnp.float32).T, precision=highest)
        grad_result = (
            (gate_values[:, :, None] * grad_rows[:, None, :])
            .astype(jnp.bfloat16)
            .reshape(token_rows * TOP, hidden_width)
        )
        send_grads = (
            jnp.zeros((expert_count * capacity, hidden_width), jnp.bfloat16)
            .at[slot_idx]
            .set(grad_result)
        )
        recv_grads, again_rows = (
            lax.all_to_all(
                send_grads.reshape(expert_count, capacity, hidden_width),
                "expert",
                split_axis=0,
                concat_axis=0,
                tiled=True,
            ),
            lax.all_to_all(
                send_rows.reshape(expert_count, capacity, hidden_width),
                "expert",
                split_axis=0,
                concat_axis=0,
                tiled=True,
            ),
        )
        grouped_rows = again_rows.reshape(expert_size, local_experts, capacity, hidden_width)
        gate_up = jnp.einsum(
            "slcd,ldf->slcf", grouped_rows, gateup_all, preferred_element_type=jnp.float32
        )
        grouped_grads = recv_grads.reshape(expert_size, local_experts, capacity, hidden_width)
        gate_part = gate_up[..., :FF]
        up_part = gate_up[..., FF:]
        sigmoid_gate = jax.nn.sigmoid(gate_part)
        silu_gate = gate_part * sigmoid_gate
        hidden = (silu_gate * up_part).astype(jnp.bfloat16)
        grad_hidden = jnp.einsum(
            "slcd,lfd->slcf", grouped_grads, down_all, preferred_element_type=jnp.float32
        )
        down_term = jnp.einsum(
            "slcf,slcd->lfd", hidden, grouped_grads, preferred_element_type=jnp.float32
        )
        grad_gatepart = (
            grad_hidden * up_part * sigmoid_gate * (1.0 + gate_part * (1.0 - sigmoid_gate))
        )
        grad_gateup = jnp.concatenate([grad_gatepart, grad_hidden * silu_gate], axis=-1).astype(
            jnp.bfloat16
        )
        upper_term = jnp.einsum(
            "slcd,slcf->ldf", grouped_rows, grad_gateup, preferred_element_type=jnp.float32
        )
        grad_copies = jnp.einsum(
            "slcf,ldf->slcd", grad_gateup, gateup_all, preferred_element_type=jnp.float32
        ).astype(jnp.bfloat16)
        back_grads = lax.all_to_all(
            grad_copies.reshape(expert_count, capacity, hidden_width),
            "expert",
            split_axis=0,
            concat_axis=0,
            tiled=True,
        )
        copy_rows = back_grads.reshape(expert_count * capacity, hidden_width)[slot_idx].reshape(
            token_rows, TOP, hidden_width
        )
        grad_normtwo = grad_normtwo + jnp.sum(copy_rows.astype(jnp.float32), axis=1)
        midnorm_term = jnp.sum(grad_normtwo * normed_mid, axis=0)
        grad_mixed = grad_rows + norm_back(grad_normtwo, normed_mid, inverse_two, gain_two)
        grad_proj = grad_mixed.astype(jnp.bfloat16)
        output_term = jnp.dot(attended.T, grad_proj, preferred_element_type=jnp.float32)
        attention_gradient = jnp.dot(
            grad_proj, output_all.T, preferred_element_type=jnp.float32
        ).astype(jnp.bfloat16)
        attention_gradient = attention_gradient.reshape(
            token_rows, KEY_VALUE_HEADS, query_group_width, HEAD_SIZE
        )
        scores = masked_scores(query_matrix, key_rows, allowed)
        prob_rows = jnp.exp(scores - log_total)
        grad_probs = jnp.einsum(
            "qhgd,khd->hgqk", attention_gradient, value_rows, preferred_element_type=jnp.float32
        )
        row_delta = jnp.sum(prob_rows * grad_probs, axis=-1, keepdims=True)
        grad_scores = (prob_rows * (grad_probs - row_delta)).astype(jnp.bfloat16)
        prob_low = prob_rows.astype(jnp.bfloat16)
        grad_qrot = (
            jnp.einsum("hgqk,khd->qhgd", grad_scores, key_rows, preferred_element_type=jnp.float32)
            * score_scale
        )
        grad_keys = (
            jnp.einsum(
                "hgqk,qhgd->khd", grad_scores, query_matrix, preferred_element_type=jnp.float32
            )
            * score_scale
        )
        grad_vals = jnp.einsum(
            "hgqk,qhgd->khd", prob_low, attention_gradient, preferred_element_type=jnp.float32
        )
        own_keys = (
            lax.psum_scatter(
                jnp.stack([grad_keys, grad_vals], axis=1)
                .reshape(lax.axis_size("dp") * token_rows, 2 * KEY_VALUE_HEADS * HEAD_SIZE)
                .astype(jnp.bfloat16),
                "dp",
                scatter_dimension=0,
                tiled=True,
            )
            .astype(jnp.float32)
            .reshape(token_rows, 2, KEY_VALUE_HEADS, HEAD_SIZE)
        )
        grad_query = (
            unrotate(
                grad_qrot.reshape(token_rows, QUERY_HEADS, HEAD_SIZE), cosine_table, sine_table
            )
            .astype(jnp.bfloat16)
            .reshape(token_rows, QUERY_HEADS * HEAD_SIZE)
        )
        key_gradient = unrotate(own_keys[:, 0], cosine_table, sine_table).astype(jnp.bfloat16)
        value_gradient = own_keys[:, 1].astype(jnp.bfloat16)
        key_value_weight_gradient = jnp.stack([key_gradient, value_gradient], axis=1).reshape(
            token_rows, 2 * KEY_VALUE_HEADS * HEAD_SIZE
        )
        query_term = jnp.dot(normalized_input.T, grad_query, preferred_element_type=jnp.float32)
        keyval_term = jnp.dot(
            normalized_input.T, key_value_weight_gradient, preferred_element_type=jnp.float32
        )
        grad_normone = jnp.dot(grad_query, query_all.T, preferred_element_type=jnp.float32)
        grad_normone = grad_normone + jnp.dot(
            key_value_weight_gradient, keyval_all.T, preferred_element_type=jnp.float32
        )
        prenorm_term = jnp.sum(grad_normone * normed_one, axis=0)
        grads_list.append(grad_mixed + norm_back(grad_normone, normed_one, inverse_one, gain_one))
        total_prenorm = total_prenorm + prenorm_term
        total_query = total_query + query_term
        total_key_value = total_key_value + keyval_term
        total_output = total_output + output_term
        total_midnorm = total_midnorm + midnorm_term
        total_router = total_router + router_term
        total_upper = total_upper + upper_term
        total_down = total_down + down_term
    dense_grads = (
        lax.psum_scatter(total_prenorm, ("dp", "expert"), scatter_dimension=0, tiled=True),
        lax.psum_scatter(total_query, ("dp", "expert"), scatter_dimension=0, tiled=True),
        lax.psum_scatter(total_key_value, ("dp", "expert"), scatter_dimension=0, tiled=True),
        lax.psum_scatter(total_output, ("dp", "expert"), scatter_dimension=0, tiled=True),
        lax.psum_scatter(total_midnorm, ("dp", "expert"), scatter_dimension=0, tiled=True),
        lax.psum_scatter(total_router, ("dp", "expert"), scatter_dimension=0, tiled=True),
    )
    expert_grads = (
        lax.psum_scatter(
            total_upper.astype(jnp.bfloat16), "dp", scatter_dimension=1, tiled=True
        ).astype(jnp.float32),
        lax.psum_scatter(
            total_down.astype(jnp.bfloat16), "dp", scatter_dimension=1, tiled=True
        ).astype(jnp.float32),
    )
    return (
        jnp.stack(outputs_list),
        jnp.stack(grads_list),
        dense_grads[0],
        dense_grads[1],
        dense_grads[2],
        dense_grads[3],
        dense_grads[4],
        dense_grads[5],
        expert_grads[0],
        expert_grads[1],
    )


MESH = pl.DeviceIdType.MESH
CHUNK = 256
PIECE = 96


def remote(src, dst, send_sem, recv_sem, target):
    return pltpu.make_async_remote_copy(
        src_ref=src,
        dst_ref=dst,
        send_sem=send_sem,
        recv_sem=recv_sem,
        device_id=target,
        device_id_type=MESH,
    )


def place():
    d = lax.axis_index("dp")
    e = lax.axis_index("expert")
    z = lax.div(e, 2)
    c = lax.rem(e, 2)
    x = lax.rem(d, 2)
    y = lax.div(d, 2)
    return d, e, z, c, x, y


def attention_kernel(
    tok_hbm,
    wq_hbm,
    wkv_hbm,
    wr_ref,
    pre_ref,
    mid_ref,
    wb_hbm,
    cot_hbm,
    wo_hbm,
    rope_hbm,
    lens_ref,
    routes_ref,
    wa_out,
    wb_out,
    wo_out,
    gall,
    q_out,
    kv_out,
    att_out,
    mixed_hbm,
    normed_hbm,
    gates_out,
    wa,
    wb,
    qs,
    kvs,
    att,
    g_own,
    rope,
    tok_ref,
    cot_ref,
    mixed_out,
    normed_out,
    own_sem,
    wo_recv,
    wo_send,
    z_recv,
    z_send,
    xy_recv,
    xy_send,
    sib_recv,
    sib_send,
    g_recv,
    g_send,
    gs_recv,
    gs_send,
    kv_recv,
    kv_send,
):
    bf, f32 = jnp.bfloat16, jnp.float32
    d, e, z, c, x, y = place()
    d_x = d + 1 - 2 * x
    d_y = d + 2 - 4 * y
    d_d = 3 - d
    other = 1 - c
    to_x = (d_x, e)
    to_y = (d_y, e)
    to_sib = (d, 2 * z + other)
    to_up = (d, e + jnp.where(z < 3, 2, -2))
    to_down = (d, e + jnp.where(z > 0, -2, 2))

    barrier = pltpu.get_barrier_semaphore()
    for target in (to_x, to_y, to_sib):
        pl.semaphore_signal(barrier, inc=1, device_id=target, device_id_type=MESH)

    @pl.when(z < 3)
    def _():
        pl.semaphore_signal(barrier, inc=1, device_id=to_up, device_id_type=MESH)

    @pl.when(z > 0)
    def _():
        pl.semaphore_signal(barrier, inc=1, device_id=to_down, device_id_type=MESH)

    own_at = pl.multiple_of((d * 8 + e) * 48, 16)
    own_rows = pl.ds(own_at, 48)
    own_a = [
        pltpu.make_async_copy(wq_hbm, wa.at[own_rows, pl.ds(0, 1536)], own_sem.at[0]),
        pltpu.make_async_copy(wkv_hbm, wa.at[own_rows, pl.ds(1536, 512)], own_sem.at[1]),
        pltpu.make_async_copy(rope_hbm.at[:, pl.ds(pl.multiple_of(d * 128, 128), 128)], rope, own_sem.at[2]),
    ]
    loads = [
        pltpu.make_async_copy(cot_hbm, cot_ref, own_sem.at[8]),
        pltpu.make_async_copy(tok_hbm, tok_ref, own_sem.at[9]),
    ]
    for copy in own_a + loads:
        copy.start()
    eye = lax.broadcasted_iota(jnp.int32, (128, 128), 0) == lax.broadcasted_iota(
        jnp.int32, (128, 128), 1
    )
    eye_low = eye.astype(bf)
    turned = (((0,), (0,)), ((), ()))
    sub = lax.broadcasted_iota(jnp.int32, (8, 48), 0)
    gains = jnp.where(
        sub == 0,
        pre_ref[...].astype(f32),
        jnp.where(sub == 1, mid_ref[...].astype(f32), 0.0),
    )
    tile = jnp.concatenate([wr_ref[...].astype(f32), gains], axis=0).astype(bf)
    wa[own_rows, 2048:] = lax.dot_general(
        tile, eye_low[:16], turned, preferred_element_type=f32
    ).astype(bf)
    full = (wa, wb)
    shard = (None, wb_hbm)

    def block(a, dd, zp, lane):
        at = pl.multiple_of((dd * 8 + 2 * zp + lane) * 48, 16)
        return full[a].at[pl.ds(at, 48)]

    def z_copy(a, zp, way, src=None):
        ref = block(a, d, zp, c)
        return remote(
            ref if src is None else src,
            ref,
            z_send.at[a, way, zp],
            z_recv.at[a, zp],
            to_up if way == 0 else to_down,
        )

    def xy_copy(a, dd, zp, row, target, src=None):
        ref = block(a, dd, zp, c)
        return remote(
            ref if src is None else src,
            ref,
            xy_send.at[a, row, zp],
            xy_recv.at[a, row, zp],
            target,
        )

    def s_copy(a, dd, zp, src=None, lane=None):
        ref = block(a, dd, zp, c if lane is None else lane)
        return remote(
            ref if src is None else src,
            ref,
            sib_send.at[a, dd, zp],
            sib_recv.at[a, dd, zp],
            to_sib,
        )

    def send_xy(a, zp):
        xy_copy(a, d, zp, 0, to_x).start()
        xy_copy(a, d, zp, 1, to_y).start()

    def own_start(a):
        @pl.when(z < 3)
        def _():
            z_copy(a, z, 0, shard[a]).start()

        @pl.when(z > 0)
        def _():
            z_copy(a, z, 1, shard[a]).start()

        s_copy(a, d, z, shard[a]).start()

    def from_z(a, k):
        def arrived(zp, way):
            z_copy(a, zp, way).wait_recv()

            @pl.when((z < 3) if way == 0 else (z > 0))
            def _():
                z_copy(a, zp, way).start()

            if a == 0:
                send_xy(a, zp)
            s_copy(a, d, zp).start()

        @pl.when(z - k >= 0)
        def _():
            arrived(z - k, 0)

        @pl.when(z + k <= 3)
        def _():
            arrived(z + k, 1)

    def from_xy_one(a, zp):
        xy_copy(a, d_x, zp, 0, to_x).wait_recv()

        @pl.when(lax.rem(zp, 2) == 0)
        def _():
            xy_copy(a, d_x, zp, 2, to_y).start()

        s_copy(a, d_x, zp).start()
        xy_copy(a, d_y, zp, 1, to_y).wait_recv()

        @pl.when(lax.rem(zp, 2) == 1)
        def _():
            xy_copy(a, d_y, zp, 2, to_x).start()

        s_copy(a, d_y, zp).start()

    def from_xy(a, k):
        @pl.when(z - k >= 0)
        def _():
            from_xy_one(a, z - k)

        if k > 0:

            @pl.when(z + k <= 3)
            def _():
                from_xy_one(a, z + k)

    def from_diag(a):
        for k in range(4):
            zp = lax.rem(z + k, 4)
            xy_copy(a, d_d, zp, 2, to_x).wait_recv()
            s_copy(a, d_d, zp).start()

    def from_sib(a):
        for dd in range(4):
            for zp in range(4):
                s_copy(a, dd, zp, lane=other).wait_recv()

    def drain(a):
        for zp in range(4):
            for dd in range(4):
                s_copy(a, dd, zp).wait_send()
            for row in range(3):
                xy_copy(a, d, zp, row, to_x).wait_send()

            @pl.when((zp <= z) & (z < 3))
            def _():
                z_copy(a, zp, 0).wait_send()

            @pl.when((zp >= z) & (z > 0))
            def _():
                z_copy(a, zp, 1).wait_send()

    def g_part(zp, lane, s):
        at = pl.multiple_of((2 * zp + lane) * CHUNK + s * 128, 128)
        return gall.at[pl.ds(at, 128)]

    def g_copy(zp, s, way, src=None):
        ref = g_part(zp, c, s)
        return remote(
            ref if src is None else src,
            ref,
            g_send.at[way, zp, s],
            g_recv.at[zp, s],
            to_up if way == 0 else to_down,
        )

    def gs_copy(zp, s, src=None, lane=None):
        ref = g_part(zp, c if lane is None else lane, s)
        return remote(
            ref if src is None else src, ref, gs_send.at[zp, s], gs_recv.at[zp, s], to_sib
        )

    def g_start():
        for s in range(2):
            src = g_own.at[pl.ds(s * 128, 128)]

            @pl.when(z < 3)
            def _():
                g_copy(z, s, 0, src).start()

            @pl.when(z > 0)
            def _():
                g_copy(z, s, 1, src).start()

            gs_copy(z, s, src).start()

    def g_pass(k, s):
        @pl.when(z - k >= 0)
        def _():
            g_copy(z - k, s, 0).wait_recv()

            @pl.when(z < 3)
            def _():
                g_copy(z - k, s, 0).start()

            gs_copy(z - k, s).start()

        @pl.when(z + k <= 3)
        def _():
            g_copy(z + k, s, 1).wait_recv()

            @pl.when(z > 0)
            def _():
                g_copy(z + k, s, 1).start()

            gs_copy(z + k, s).start()

    def wo_copy(dd, p, row, target, src=None):
        ref = wo_out.at[pl.ds(pl.multiple_of(dd * 192 + p * PIECE, 16), PIECE)]
        return remote(
            ref if src is None else src, ref, wo_send.at[row, p], wo_recv.at[row, p], target
        )

    def wo_start(p):
        wo_copy(d, p, 0, to_x, wo_hbm.at[pl.ds(p * PIECE, PIECE)]).start()
        wo_copy(d, 1 - p, 1, to_y, wo_hbm.at[pl.ds((1 - p) * PIECE, PIECE)]).start()

    def wo_pass():
        wo_copy(d_x, 0, 0, to_x).wait_recv()
        wo_copy(d_x, 0, 2, to_y).start()
        wo_copy(d_y, 1, 1, to_y).wait_recv()
        wo_copy(d_y, 1, 2, to_x).start()

    def wo_rest():
        wo_copy(d_x, 1, 0, to_x).wait_recv()
        wo_copy(d_y, 0, 1, to_y).wait_recv()
        for p in range(2):
            wo_copy(d_d, p, 2, to_x).wait_recv()

    pl.semaphore_wait(barrier, 5 - jnp.where((z == 0) | (z == 3), 1, 0))
    for copy in own_a:
        copy.wait()
    own_start(0)
    own_start(1)
    own = [
        pltpu.make_async_copy(wb_hbm, block(1, d, z, c), own_sem.at[0]),
        pltpu.make_async_copy(
            g_own, gall.at[pl.ds(pl.multiple_of(e * CHUNK, CHUNK), CHUNK)], own_sem.at[1]
        ),
        pltpu.make_async_copy(
            wo_hbm, wo_out.at[pl.ds(pl.multiple_of(d * 192, 16), 192)], own_sem.at[2]
        ),
    ]
    own[0].start()
    own[2].start()
    send_xy(0, z)
    loads[0].wait()
    for s in range(2):
        rows = slice(s * 128, (s + 1) * 128)
        slot = d * 128 + lax.broadcasted_iota(jnp.int32, (128, 1), 0)
        g_own[rows] = jnp.where(slot < lens_ref[s], cot_ref[rows].astype(f32), 0.0).astype(bf)

    own[1].start()
    loads[1].wait()
    tok = tok_ref[...].astype(f32)
    n1 = tok * lax.rsqrt(jnp.mean(tok * tok, axis=1, keepdims=True) + epsilon)
    from_z(0, 1)
    from_z(1, 1)
    from_xy(0, 0)
    from_z(0, 2)
    from_z(1, 2)
    g_start()
    from_xy(0, 1)
    from_z(0, 3)
    from_z(1, 3)
    from_xy(0, 2)
    from_xy(0, 3)

    def turn(j):
        return lax.rem(z + j, 4)

    own[0].wait()
    for j in range(2):
        send_xy(1, turn(j))
    from_diag(0)
    from_sib(0)

    small_t = lax.dot_general(
        eye_low[:16], wa[:, 2048:], (((1,), (1,)), ((), ())), preferred_element_type=f32
    )
    normed = (n1 * small_t[8:9]).astype(bf)
    cos_rows = jnp.concatenate([rope[0]] * 2, axis=0)
    sin_rows = jnp.concatenate([rope[1]] * 2, axis=0)

    def rotate(v):
        return v * cos_rows + pltpu.roll(v, 64, 1) * sin_rows

    kv = jnp.dot(normed, wa[:, 1536:2048], preferred_element_type=f32)
    for h in range(2):
        kvs[d, :, h * 128 : (h + 1) * 128] = rotate(kv[:, h * 128 : (h + 1) * 128]).astype(bf)
    kvs[d, :, 256:] = kv[:, 256:].astype(bf)

    def kv_copy(dd, s, row, target):
        ref = kvs.at[dd, pl.ds(s * 128, 128)]
        return remote(ref, ref, kv_send.at[row, s], kv_recv.at[row, s], target)

    for s in range(2):
        kv_copy(d, s, 0, to_x).start()
        kv_copy(d, 1 - s, 1, to_y).start()
    send_xy(1, turn(2))
    g_pass(1, 0)
    q = jnp.dot(normed, wa[:, :1536], preferred_element_type=f32)
    for head in range(QUERY_HEADS):
        rot = rotate(q[:, head * 128 : (head + 1) * 128]).astype(bf)
        for s in range(2):
            at = (s * QUERY_HEADS + head) * 128
            qs[at : at + 128] = rot[s * 128 : (s + 1) * 128]
    kv_copy(d_x, 0, 0, to_x).wait_recv()
    kv_copy(d_x, 0, 2, to_y).start()
    kv_copy(d_y, 1, 1, to_y).wait_recv()
    kv_copy(d_y, 1, 2, to_x).start()
    send_xy(1, turn(3))
    for j in range(2):
        from_xy_one(1, turn(j))
    g_pass(1, 1)
    kv_copy(d_y, 0, 1, to_y).wait_recv()
    kv_copy(d_x, 1, 0, to_x).wait_recv()
    for s in range(2):
        kv_copy(d_d, s, 2, to_x).wait_recv()
    q_copy = pltpu.make_async_copy(qs, q_out, own_sem.at[3])
    kvo_copy = pltpu.make_async_copy(kvs, kv_out, own_sem.at[4])
    wa_copy = pltpu.make_async_copy(wa, wa_out, own_sem.at[5])
    for copy in (q_copy, kvo_copy, wa_copy):
        copy.start()

    query_pos = d * 128 + lax.broadcasted_iota(jnp.int32, (128, 512), 0)
    key_pos = lax.broadcasted_iota(jnp.int32, (128, 512), 1)

    def attend(n):
        s = lax.div(n, 2)
        h = lax.rem(n, 2)
        lens = lens_ref[s]
        allowed = (key_pos <= query_pos) & (key_pos < lens)
        ks = kvs[:, pl.ds(pl.multiple_of(s * 128, 128), 128), pl.ds(pl.multiple_of(h * 128, 128), 128)]
        vs = kvs[:, pl.ds(pl.multiple_of(s * 128, 128), 128), pl.ds(pl.multiple_of(256 + h * 128, 128), 128)]
        ks = ks.reshape(512, 128)
        vs = vs.reshape(512, 128)
        for half in range(2):
            qh = qs[pl.ds(pl.multiple_of(n * 768 + half * 384, 128), 384)]
            scores = lax.dot_general(qh, ks, (((1,), (1,)), ((), ())), preferred_element_type=f32)
            scores = scores.reshape(3, 128, 512) * HEAD_SIZE ** (-0.5)
            scores = jnp.where(allowed[None], scores, -1e30)
            top = jnp.max(scores, axis=-1, keepdims=True)
            weights = jnp.exp(scores - top)
            weights = weights * (1.0 / jnp.sum(weights, axis=-1, keepdims=True))
            out = jnp.dot(
                weights.astype(bf).reshape(384, 512), vs, preferred_element_type=f32
            ).astype(bf)
            for j in range(3):
                att[
                    pl.ds(pl.multiple_of(s * 128, 128), 128),
                    pl.ds(pl.multiple_of(h * 768 + (half * 3 + j) * 128, 128), 128),
                ] = out[j * 128 : (j + 1) * 128]

    wo_start(0)
    pl.loop(0, 2)(attend)
    from_xy_one(1, turn(2))
    from_xy_one(1, turn(3))
    wo_start(1)
    g_pass(2, 0)

    @pl.loop(2, 4)
    def _(n):
        attend(n)
        pl.when(n == 2)(wo_pass)

    g_pass(2, 1)
    from_diag(1)
    from_sib(1)
    att_copy = pltpu.make_async_copy(att, att_out, own_sem.at[6])
    wb_copy = pltpu.make_async_copy(wb, wb_out, own_sem.at[7])
    att_copy.start()
    wb_copy.start()
    mixed = tok_ref[...].astype(f32) + jnp.dot(att[...], wb[...], preferred_element_type=f32)
    mixed_out[...] = mixed
    mixed_copy = pltpu.make_async_copy(mixed_out, mixed_hbm, own_sem.at[10])
    mixed_copy.start()
    n2 = mixed * lax.rsqrt(jnp.mean(mixed * mixed, axis=1, keepdims=True) + epsilon)
    normed2 = (n2 * small_t[9:10]).astype(bf)
    normed_out[...] = normed2
    normed_copy = pltpu.make_async_copy(normed_out, normed_hbm, own_sem.at[11])
    normed_copy.start()
    logits = lax.dot_general(
        small_t[:8].astype(bf), normed2, (((1,), (1,)), ((), ())), preferred_element_type=f32
    )
    number = lax.broadcasted_iota(jnp.int32, (8, 128), 0)
    for s in range(2):
        chosen = number == routes_ref[s, 0:1]
        for t in range(1, TOP):
            chosen = chosen | (number == routes_ref[s, t : t + 1])
        picked = jnp.where(chosen, logits[:, s * 128 : (s + 1) * 128], -1e30)
        top = jnp.max(picked, axis=0, keepdims=True)
        weights = jnp.where(chosen, jnp.exp(picked - top), 0.0)
        gates_out[s] = weights / jnp.sum(weights, axis=0, keepdims=True)

    g_pass(3, 0)
    g_pass(3, 1)
    wo_rest()
    for zp in range(4):
        for s in range(2):
            gs_copy(zp, s, lane=other).wait_recv()
    own[1].wait()
    own[2].wait()
    for copy in (q_copy, kvo_copy, wa_copy, att_copy, wb_copy, mixed_copy, normed_copy):
        copy.wait()
    drain(0)
    drain(1)
    for s in range(2):
        for row in range(3):
            kv_copy(d, s, row, to_x).wait_send()
            wo_copy(d, s, row, to_x).wait_send()
        for zp in range(4):
            gs_copy(zp, s).wait_send()

            @pl.when((zp <= z) & (z < 3))
            def _():
                g_copy(zp, s, 0).wait_send()

            @pl.when((zp >= z) & (z > 0))
            def _():
                g_copy(zp, s, 1).wait_send()


def attention_stage(tok, wq, wkv, wr, pre, mid, wb, cot, wo, rope, lens, routes):
    bf, f32 = jnp.bfloat16, jnp.float32
    shape = jax.ShapeDtypeStruct
    width = tok.shape[-1]
    wide = wq.shape[-1] + wkv.shape[-1] + 128
    hbm = pl.BlockSpec(memory_space=pltpu.HBM)
    vmem = pl.BlockSpec(memory_space=pltpu.VMEM)
    smem = pl.BlockSpec(memory_space=pltpu.SMEM)
    dma = pltpu.SemaphoreType.DMA
    return pl.pallas_call(
        attention_kernel,
        out_shape=(
            shape((width, wide), bf),
            shape((width, width), bf),
            shape((FF, width), bf),
            shape((8 * CHUNK, width), bf),
            shape((2 * QUERY_HEADS * 128, 128), bf),
            shape((4, CHUNK, 512), bf),
            shape((CHUNK, width), bf),
            shape((CHUNK, width), f32),
            shape((CHUNK, width), bf),
            shape((2, 8, 128), f32),
        ),
        in_specs=[hbm, hbm, hbm, vmem, vmem, vmem, hbm, hbm, hbm, hbm, smem, vmem],
        out_specs=[hbm] * 9 + [vmem],
        scratch_shapes=[
            pltpu.VMEM((width, wide), bf),
            pltpu.VMEM((width, width), bf),
            pltpu.VMEM((2 * QUERY_HEADS * 128, 128), bf),
            pltpu.VMEM((4, CHUNK, 512), bf),
            pltpu.VMEM((CHUNK, width), bf),
            pltpu.VMEM((CHUNK, width), bf),
            pltpu.VMEM((2, 128, 128), f32),
            pltpu.VMEM((CHUNK, width), bf),
            pltpu.VMEM((CHUNK, width), bf),
            pltpu.VMEM((CHUNK, width), f32),
            pltpu.VMEM((CHUNK, width), bf),
            dma((12,)),
            dma((3, 2)),
            dma((3, 2)),
            dma((2, 4)),
            dma((2, 2, 4)),
            dma((2, 3, 4)),
            dma((2, 3, 4)),
            dma((2, 4, 4)),
            dma((2, 4, 4)),
            dma((4, 2)),
            dma((2, 4, 2)),
            dma((4, 2)),
            dma((4, 2)),
            dma((3, 2)),
            dma((3, 2)),
        ],
        compiler_params=pltpu.CompilerParams(
            collective_id=2, has_side_effects=True, vmem_limit_bytes=60 * 2**20
        ),
        name="attention_stage",
    )(tok, wq, wkv, wr, pre, mid, wb, cot, wo, rope, lens, routes)


def expert_kernel(
    x_hbm,
    g_hbm,
    gt_hbm,
    win_hbm,
    wout_hbm,
    dx_hbm,
    dgt_out,
    outp_hbm,
    gin_hbm,
    gout_hbm,
    gout_out,
    gin_first_hbm,
    win,
    wout,
    xall,
    gall,
    gtall,
    dgu,
    hg,
    dxb,
    dgb,
    sibr,
    sibg,
    ro,
    rog,
    ri,
    rig,
    gout,
    tg,
    xg,
    yg,
    gin,
    ti,
    xi,
    yi,
    dx_out,
    gin_out,
    own_sem,
    stage_sem,
    grad_sem,
    g_recv,
    g_send,
    i_recv,
    i_send,
    w_recv,
    w_send,
    ag_recv,
    ag_send,
    sib_recv,
    sib_send,
    red_recv,
    red_send,
):
    bf, f32 = jnp.bfloat16, jnp.float32
    d, e, z, c, x, y = place()
    d_x = d + 1 - 2 * x
    d_y = d + 2 - 4 * y
    d_d = 3 - d
    hi = lax.div(z, 2)
    zz = z * hi + (3 - z) * (1 - hi)
    other = 1 - c
    to_x = (d_x, e)
    to_y = (d_y, e)
    to_sib = (d, 2 * z + other)
    to_up = (d, e + jnp.where(z < 3, 2, -2))
    to_down = (d, e + jnp.where(z > 0, -2, 2))
    e_in = e + 2 - 4 * hi
    to_in = (d, e_in)
    to_out = (d, jnp.where(zz == 2, e - 2 + 4 * hi, e_in))
    mid = zz == 2
    end = zz == 3

    barrier = pltpu.get_barrier_semaphore()
    for target in (to_x, to_y, to_sib, to_in):
        pl.semaphore_signal(barrier, inc=1, device_id=target, device_id_type=MESH)

    @pl.when(mid)
    def _():
        pl.semaphore_signal(barrier, inc=1, device_id=to_out, device_id_type=MESH)

    own_copies = [
        pltpu.make_async_copy(x_hbm.at[s], xall.at[e, s], own_sem.at[s]) for s in range(2)
    ] + [
        pltpu.make_async_copy(gt_hbm, gtall.at[e], own_sem.at[2]),
        pltpu.make_async_copy(wout_hbm, wout, own_sem.at[3]),
        pltpu.make_async_copy(g_hbm, gall, own_sem.at[4]),
    ]

    def w_columns(h, kind):
        return pl.ds(h * 768 + kind * 384, 384)

    for h in range(2):
        for kind in range(2):
            own_copies.append(
                pltpu.make_async_copy(
                    win_hbm.at[:, pl.ds(kind * 768 + h * 384, 384)],
                    win.at[d, :, w_columns(h, kind)],
                    own_sem.at[5 + 2 * h + kind],
                )
            )
    pl.semaphore_wait(barrier, 7 - zz)

    gathered = ((x_hbm, xall), (gt_hbm, gtall))

    def ag_copy(a, zp, s, way, src=None):
        ref = gathered[a][1].at[2 * zp + c, s]
        return remote(
            ref if src is None else src,
            ref,
            ag_send.at[way, a, zp, s],
            ag_recv.at[a, zp, s],
            to_up if way == 0 else to_down,
        )

    def sib_copy(a, zp, s, src=None, lane=None):
        ref = gathered[a][1].at[2 * zp + (c if lane is None else lane), s]
        return remote(
            ref if src is None else src,
            ref,
            sib_send.at[a, zp, s],
            sib_recv.at[a, zp, s],
            to_sib,
        )

    def own_rows(s):
        for a in range(2):
            src = gathered[a][0].at[s]

            @pl.when(z < 3)
            def _():
                ag_copy(a, z, s, 0, src).start()

            @pl.when(z > 0)
            def _():
                ag_copy(a, z, s, 1, src).start()

            sib_copy(a, z, s, src).start()

    def pass_on(k, s):
        for a in range(2):

            @pl.when(z - k >= 0)
            def _():
                ag_copy(a, z - k, s, 0).wait_recv()

                @pl.when(z < 3)
                def _():
                    ag_copy(a, z - k, s, 0).start()

                sib_copy(a, z - k, s).start()

            @pl.when(z + k <= 3)
            def _():
                ag_copy(a, z + k, s, 1).wait_recv()

                @pl.when(z > 0)
                def _():
                    ag_copy(a, z + k, s, 1).start()

                sib_copy(a, z + k, s).start()

    def from_sib(s):
        for a in range(2):
            for zp in range(4):
                sib_copy(a, zp, s, lane=other).wait_recv()

    def w_copy(h, kind, p, src_d, target, row, src=None):
        ref = win.at[src_d, pl.ds(p * 192, 192), w_columns(h, kind)]
        return remote(
            ref if src is None else src,
            ref,
            w_send.at[row, h, kind, p],
            w_recv.at[row, h, kind, p],
            target,
        )

    def w_start(h):
        for p in range(2):
            for kind in range(2):

                def src(q):
                    return win_hbm.at[
                        pl.ds(q * 192, 192), pl.ds(kind * 768 + h * 384, 384)
                    ]

                w_copy(h, kind, p, d, to_x, 0, src(p)).start()
                w_copy(h, kind, 1 - p, d, to_y, 1, src(1 - p)).start()

    def w_pass(h):
        for kind in range(2):
            w_copy(h, kind, 0, d_x, to_x, 0).wait_recv()
            w_copy(h, kind, 0, d_x, to_y, 2).start()
            w_copy(h, kind, 1, d_y, to_y, 1).wait_recv()
            w_copy(h, kind, 1, d_y, to_x, 2).start()

    def w_rest(h):
        for kind in range(2):
            w_copy(h, kind, 1, d_x, to_x, 0).wait_recv()
            w_copy(h, kind, 0, d_y, to_y, 1).wait_recv()
            for p in range(2):
                w_copy(h, kind, p, d_d, to_x, 2).wait_recv()

    own_rows(0)
    w_start(0)
    for copy in own_copies:
        copy.start()
    w_pass(0)
    w_start(1)
    pass_on(1, 0)
    pass_on(2, 0)
    own_rows(1)
    w_rest(0)
    w_pass(1)
    pass_on(3, 0)
    from_sib(0)
    for copy in own_copies:
        copy.wait()

    def order(i):
        v = i if i < 2 else (5 - zz if i == 2 else zz)
        return v * hi + (3 - v) * (1 - hi)

    def sib_sum(zp, s, a):
        src, dst = ((dxb, sibr), (dgb, sibg))[a]
        return remote(
            src.at[2 * zp + other, s], dst.at[zp, s], red_send.at[a, zp, s], red_recv.at[a, zp, s], to_sib
        )

    def hop(i, s, target, inward):
        dst, dstg, row = (ro, rog, 2) if inward else (ri, rig, 4)
        zp = order(i)
        return (
            remote(
                dxb.at[2 * zp + c, s], dst.at[i, s], red_send.at[2, i, s], red_recv.at[row, i, s], target
            ),
            remote(
                dgb.at[2 * zp + c, s], dstg.at[i, s], red_send.at[3, i, s], red_recv.at[row + 1, i, s], target
            ),
        )

    def wait_from(ref, refg, slot, s, row):
        remote(
            ref.at[slot, s], ref.at[slot, s], red_send.at[2, slot, s], red_recv.at[row, slot, s], to_in
        ).wait_recv()
        remote(
            refg.at[slot, s], refg.at[slot, s], red_send.at[3, slot, s], red_recv.at[row + 1, slot, s], to_in
        ).wait_recv()

    def combine(i, s, incoming):
        zp = order(i)
        for a in range(2):
            remote(
                sibr.at[zp, s] if a == 0 else sibg.at[zp, s],
                sibr.at[zp, s] if a == 0 else sibg.at[zp, s],
                red_send.at[a, zp, s],
                red_recv.at[a, zp, s],
                to_sib,
            ).wait_recv()
        for ref, refg, slot, row in incoming:
            wait_from(ref, refg, slot, s, row)
        total = dxb[2 * zp + c, s].astype(f32) + sibr[zp, s].astype(f32)
        totalg = dgb[2 * zp + c, s] + sibg[zp, s]
        for ref, refg, slot, row in incoming:
            total = total + ref[slot, s].astype(f32)
            totalg = totalg + refg[slot, s]
        return total, totalg

    def pass_sum(i, s, incoming, target, inward):
        total, totalg = combine(i, s, incoming)
        zp = order(i)
        dxb[2 * zp + c, s] = total.astype(bf)
        dgb[2 * zp + c, s] = totalg
        for copy in hop(i, s, target, inward):
            copy.start()

    def end_sums(s, which):
        @pl.when(end)
        def _():
            for i in which:
                pass_sum(i, s, (), to_in, True)

    def mid_sum(i, s):
        @pl.when(mid)
        def _():
            if i < 2:
                pass_sum(i, s, ((ro, rog, i, 2),), to_in, False)
            else:
                pass_sum(2, s, ((ri, rig, 0, 4),), to_out, False)

    def dx_copy(s):
        rows = pl.ds(s * 128, 128)
        return pltpu.make_async_copy(dx_out.at[rows], dx_hbm.at[rows], own_sem.at[4 + s])

    def last_sum(s):
        @pl.when(mid)
        def _():
            total, totalg = combine(3, s, ((ro, rog, 2, 2), (ri, rig, 1, 4)))
            dx_out[s * 128 : (s + 1) * 128] = total
            dgt_out[s] = totalg

        @pl.when(end)
        def _():
            total, totalg = combine(3, s, ((ri, rig, 2, 4),))
            dx_out[s * 128 : (s + 1) * 128] = total
            dgt_out[s] = totalg

        dx_copy(s).start()

    eye = lax.broadcasted_iota(jnp.int32, (128, 128), 0) == lax.broadcasted_iota(
        jnp.int32, (128, 128), 1
    )
    mine = lax.broadcasted_iota(jnp.int32, (8, 128), 0) == e
    nt = (((1,), (1,)), ((), ()))
    tn = (((0,), (0,)), ((), ()))

    def half_step(s, pair, h):
        first = 4 * pair
        block = pl.ds(first, 4)
        both = jnp.dot(
            xall[block, s].reshape(512, 1536),
            win[:, :, h * 768 : (h + 1) * 768].reshape(1536, 768),
            preferred_element_type=f32,
        )
        gate = both[:, :384]
        up = both[:, 384:]
        back = lax.dot_general(
            gall[block, s].reshape(512, 1536),
            wout[h * 384 : (h + 1) * 384],
            nt,
            preferred_element_type=f32,
        )
        columns = []
        for j in range(4):
            row = jnp.sum(jnp.where(mine, gtall[first + j, s], 0.0), axis=0, keepdims=True)
            columns.append(jnp.sum(jnp.where(eye, row, 0.0), axis=1, keepdims=True))
        weight = jnp.concatenate(columns, axis=0)
        sig = jax.nn.sigmoid(gate)
        silu = gate * sig
        hidden = (silu * up).astype(bf).astype(f32)
        dgate = jnp.sum(hidden * back, axis=1, keepdims=True)
        for j in range(4):
            row = jnp.sum(
                jnp.where(eye, dgate[j * 128 : (j + 1) * 128], 0.0), axis=0, keepdims=True
            )
            part = jnp.where(mine, row, 0.0)
            dgb[first + j, s] = part if h == 0 else dgb[first + j, s] + part
        hg[block, s, :, h * 384 : (h + 1) * 384] = (
            (hidden * weight).astype(bf).reshape(4, 128, 384)
        )
        back = back * weight
        dgu[block, s, :, h * 768 : h * 768 + 384] = (
            (back * up * (sig * (1.0 + gate * (1.0 - sig)))).astype(bf).reshape(4, 128, 384)
        )
        dgu[block, s, :, h * 768 + 384 : (h + 1) * 768] = (
            (back * silu).astype(bf).reshape(4, 128, 384)
        )

    def dx_step(s, pair):
        first = 4 * pair
        block = pl.ds(first, 4)
        dxb[block, s] = (
            lax.dot_general(
                dgu[block, s].reshape(512, 1536),
                win[...].reshape(1536, 1536),
                nt,
                preferred_element_type=f32,
            )
            .astype(bf)
            .reshape(4, 128, 1536)
        )
        for j in range(2):
            for a in range(2):
                sib_sum(2 * pair + j, s, a).start()

    def out_slot(slot):
        return win.at[:, pl.ds(slot * 128, 128)]

    def out_copy(slot, s, first):
        return pltpu.make_async_copy(
            out_slot(slot), outp_hbm.at[pl.ds(first, 4), s], stage_sem.at[slot]
        )

    def out_step(slot, s, pair):
        first = 4 * pair
        win[:, slot * 128 : (slot + 1) * 128] = (
            jnp.dot(
                hg[pl.ds(first, 4), s].reshape(512, FF), wout[...], preferred_element_type=f32
            )
            .astype(bf)
            .reshape(4, 128, 1536)
        )
        out_copy(slot, s, first).start()

    far = 1 - hi
    near = hi

    def pair_of(t):
        return far + t * (1 - 2 * far)

    def i_piece(dd, p):
        return gin.at[pl.ds(pl.multiple_of(dd * 384 + p * PIECE, 16), PIECE)]

    def i_diag(p):
        return remote(
            i_piece(d_d, p), ti.at[p], i_send.at[0, p], i_recv.at[0, p], (to_x, to_y)[p % 2]
        )

    def i_direct(p):
        if p % 2 == 0:
            return remote(i_piece(d_x, p), xi.at[p], i_send.at[1, p], i_recv.at[1, p], to_x)
        return remote(i_piece(d_y, p), yi.at[p], i_send.at[1, p], i_recv.at[2, p], to_y)

    def i_summed(p):
        if p % 2 == 0:
            return remote(i_piece(d_y, p), yi.at[p], i_send.at[2, p], i_recv.at[2, p], to_y)
        return remote(i_piece(d_x, p), xi.at[p], i_send.at[2, p], i_recv.at[1, p], to_x)

    def i_middle(p):
        i_diag(p).wait_recv()
        dd = d_y if p % 2 == 0 else d_x
        rows = pl.ds(pl.multiple_of(dd * 384 + p * PIECE, 16), PIECE)
        gin[rows] = (gin[rows].astype(f32) + ti[p].astype(f32)).astype(bf)
        i_summed(p).start()

    def i_final(p):
        remote(xi.at[p], xi.at[p], i_send.at[1, p], i_recv.at[1, p], to_x).wait_recv()
        remote(yi.at[p], yi.at[p], i_send.at[1, p], i_recv.at[2, p], to_y).wait_recv()
        rows = pl.ds(pl.multiple_of(d * 384 + p * PIECE, 16), PIECE)
        gin_out[p * PIECE : (p + 1) * PIECE] = (
            gin[rows].astype(f32) + xi[p].astype(f32) + yi[p].astype(f32)
        ).astype(bf)

    def in_grad(dd, h):
        return lax.dot_general(
            xall[:, :, :, pl.ds(pl.multiple_of(dd * 384, 128), 384)].reshape(2048, 384),
            dgu[:, :, :, h * 768 : (h + 1) * 768].reshape(2048, 768),
            tn,
            preferred_element_type=f32,
        ).astype(bf)

    def in_first(dd):
        gin[pl.ds(pl.multiple_of(dd * 384, 16), 384)] = in_grad(dd, 0)

    @pl.loop(0, 2)
    def _(t):
        half_step(0, pair_of(t), 0)

    @pl.when(mid)
    def _():
        pass_on(1, 1)

    w_rest(1)

    @pl.when(end)
    def _():
        pass_on(1, 1)


    @pl.loop(0, 2)
    def _(t):
        pair = pair_of(t)
        half_step(0, pair, 1)
        dx_step(0, pair)

        @pl.when(t == 0)
        def _():
            end_sums(0, (0, 1))
            pass_on(2, 1)

        @pl.when(t == 1)
        def _():
            end_sums(0, (2,))
            pass_on(3, 1)
            from_sib(1)

    @pl.loop(0, 2)
    def _(t):
        half_step(1, pair_of(t), 0)

    mid_sum(0, 0)

    @pl.loop(0, 2)
    def _(t):
        pair = pair_of(t)
        half_step(1, pair, 1)
        dx_step(1, pair)

        @pl.when(t == 0)
        def _():
            in_first(d_d)
            for p in range(4):
                i_diag(p).start()
            end_sums(1, (0, 1))
            in_first(d_x)
            for p in (0, 2):
                i_direct(p).start()
            in_first(d_y)
            for p in (1, 3):
                i_direct(p).start()
            in_first(d)
            mid_sum(1, 0)
            mid_sum(2, 0)

    def g_piece(dd):
        return gout.at[pl.ds(pl.multiple_of(dd * 192, 16), PIECE)]

    def g_diag():
        return remote(g_piece(d_d), tg, g_send.at[0], g_recv.at[0], to_x)

    def g_direct():
        return remote(g_piece(d_x), xg, g_send.at[1], g_recv.at[1], to_x)

    def g_summed():
        return remote(g_piece(d_y), yg, g_send.at[2], g_recv.at[2], to_y)

    def g_middle():
        g_diag().wait_recv()
        rows = pl.ds(pl.multiple_of(d_y * 192, 16), PIECE)
        gout[rows] = (gout[rows].astype(f32) + tg[...].astype(f32)).astype(bf)
        g_summed().start()

    def out_grad(half):
        at = pl.multiple_of(half * 384, 128)
        gout[pl.ds(at, 384)] = lax.dot_general(
            hg[:, :, :, pl.ds(at, 384)].reshape(2048, 384),
            gall[...].reshape(2048, 1536),
            tn,
            preferred_element_type=f32,
        ).astype(bf)

    for p in range(4):
        i_middle(p)
    out_grad(1 - y)
    g_diag().start()
    end_sums(1, (2,))
    out_grad(y)
    g_direct().start()
    mid_sum(0, 1)
    rest = [
        pltpu.make_async_copy(
            gout.at[pl.ds(k * 192 + PIECE, PIECE)], gout_hbm.at[k], own_sem.at[k]
        )
        for k in range(4)
    ]
    for copy in rest:
        copy.start()

    def grad_copy(k):
        return pltpu.make_async_copy(
            win.at[k, :, pl.ds(0, 768)], gin_hbm.at[k], grad_sem.at[k]
        )

    for h in range(2):
        for kind in range(2):
            for p in range(2):
                w_copy(h, kind, p, d, to_x, 2).wait_send()
    for k in range(4):
        win[k, :, :768] = in_grad(k, 1)
        grad_copy(k).start()
    for p in range(4):
        i_final(p)
    in_copy = pltpu.make_async_copy(gin_out, gin_first_hbm, own_sem.at[6])
    in_copy.start()
    for k in range(4):
        grad_copy(k).wait()
    out_step(0, 0, far)
    mid_sum(1, 1)
    g_middle()
    mid_sum(2, 1)
    out_step(1, 0, near)
    out_step(2, 1, far)
    out_copy(0, 0, 0).wait()
    out_step(0, 1, near)
    last_sum(0)
    remote(xg, xg, g_send.at[1], g_recv.at[1], to_x).wait_recv()
    remote(yg, yg, g_send.at[1], g_recv.at[2], to_y).wait_recv()
    gout_out[...] = (
        gout[pl.ds(pl.multiple_of(d * 192, 16), PIECE)].astype(f32)
        + xg[...].astype(f32)
        + yg[...].astype(f32)
    ).astype(bf)
    for copy in rest:
        copy.wait()
    for k in range(3):
        out_copy(k, 1, 0).wait()
    last_sum(1)
    in_copy.wait()
    for s in range(2):
        dx_copy(s).wait()

    for copy in (g_diag(), g_direct(), g_summed()):
        copy.wait_send()
    for p in range(4):
        for copy in (i_diag(p), i_direct(p), i_summed(p)):
            copy.wait_send()
    for h in range(2):
        for kind in range(2):
            for p in range(2):
                for row in range(2):
                    w_copy(h, kind, p, d, to_x, row).wait_send()
    for s in range(2):
        for zp in range(4):
            for a in range(2):
                sib_copy(a, zp, s).wait_send()
                sib_sum(zp, s, a).wait_send()

                @pl.when((zp <= z) & (z < 3))
                def _():
                    ag_copy(a, zp, s, 0).wait_send()

                @pl.when((zp >= z) & (z > 0))
                def _():
                    ag_copy(a, zp, s, 1).wait_send()

        for i in range(3):
            for copy in hop(i, s, to_in, True):
                copy.wait_send()


def expert_stage(rows, grads, gates_t, w_in, w_out):
    bf, f32 = jnp.bfloat16, jnp.float32
    shape = jax.ShapeDtypeStruct
    width = rows.shape[-1]
    hbm = pl.BlockSpec(memory_space=pltpu.HBM)
    vmem = pl.BlockSpec(memory_space=pltpu.VMEM)
    dma = pltpu.SemaphoreType.DMA
    return pl.pallas_call(
        expert_kernel,
        out_shape=(
            shape((CHUNK, width), f32),
            shape((2, 8, 128), f32),
            shape((8, 2, 128, width), bf),
            shape((4, 384, FF), bf),
            shape((4, PIECE, width), bf),
            shape((PIECE, width), bf),
            shape((width // 4, FF), bf),
        ),
        in_specs=[hbm] * 5,
        out_specs=(hbm, vmem, hbm, hbm, hbm, vmem, hbm),
        scratch_shapes=[
            pltpu.VMEM((4, width // 4, 2 * FF), bf),
            pltpu.VMEM((FF, width), bf),
            pltpu.VMEM((8, 2, 128, width), bf),
            pltpu.VMEM((8, 2, 128, width), bf),
            pltpu.VMEM((8, 2, 8, 128), f32),
            pltpu.VMEM((8, 2, 128, 2 * FF), bf),
            pltpu.VMEM((8, 2, 128, FF), bf),
            pltpu.VMEM((8, 2, 128, width), bf),
            pltpu.VMEM((8, 2, 8, 128), f32),
            pltpu.VMEM((4, 2, 128, width), bf),
            pltpu.VMEM((4, 2, 8, 128), f32),
            pltpu.VMEM((3, 2, 128, width), bf),
            pltpu.VMEM((3, 2, 8, 128), f32),
            pltpu.VMEM((3, 2, 128, width), bf),
            pltpu.VMEM((3, 2, 8, 128), f32),
            pltpu.VMEM((FF, width), bf),
            *([pltpu.VMEM((PIECE, width), bf)] * 3),
            pltpu.VMEM((width, FF), bf),
            *([pltpu.VMEM((4, PIECE, FF), bf)] * 3),
            pltpu.VMEM((CHUNK, width), f32),
            pltpu.VMEM((width // 4, FF), bf),
            dma((9,)),
            dma((3,)),
            dma((4,)),
            dma((3,)),
            dma((3,)),
            dma((3, 4)),
            dma((3, 4)),
            dma((3, 2, 2, 2)),
            dma((3, 2, 2, 2)),
            dma((2, 4, 2)),
            dma((2, 2, 4, 2)),
            dma((2, 4, 2)),
            dma((2, 4, 2)),
            dma((6, 4, 2)),
            dma((4, 4, 2)),
        ],
        compiler_params=pltpu.CompilerParams(
            collective_id=1, has_side_effects=True, vmem_limit_bytes=63 * 2**20
        ),
        name="expert_stage",
    )(
        rows.reshape(2, 128, width),
        grads.reshape(8, 2, 128, width),
        gates_t,
        w_in,
        w_out,
    )


def backward_kernel(
    dx_hbm,
    dgt_ref,
    gates_ref,
    mixed_hbm,
    cot_hbm,
    tok_hbm,
    q_hbm,
    kv_hbm,
    att_hbm,
    lens_ref,
    rope_hbm,
    wa_hbm,
    wb_hbm,
    gin_hbm,
    gout_hbm,
    outp_hbm,
    block_hbm,
    dtok_hbm,
    gq_out,
    gb_out,
    gkv_out,
    small_out,
    ein_out,
    eout_out,
    osib,
    oro,
    ori,
    wide,
    small,
    gq,
    gb,
    gk,
    sib_q,
    sib_b,
    sib_k,
    tq,
    xq,
    yq,
    roq,
    riq,
    tb,
    xb,
    yb,
    rob,
    rib,
    tw,
    xw,
    yw,
    row_,
    riw,
    te,
    xe,
    ye,
    le,
    td,
    xd,
    yd,
    ld,
    old,
    oslot,
    dat,
    dkv,
    tk,
    xk,
    yk,
    rope,
    cot_ref,
    tok_ref,
    q_ref,
    kv_ref,
    att_ref,
    mixed_ref,
    block_out,
    dtok_out,
    load_sem,
    le_sem,
    old_sem,
    os_recv,
    os_send,
    ds_recv,
    ds_send,
    t_recv,
    x_recv,
    y_recv,
    t_send,
    d_send,
    s_send,
    ro_recv,
    ri_recv,
    hop_send,
):
    bf, f32 = jnp.bfloat16, jnp.float32
    d, e, z, c, x, y = place()
    d_x = d + 1 - 2 * x
    d_y = d + 2 - 4 * y
    d_d = 3 - d
    hi = lax.div(z, 2)
    zz = z * hi + (3 - z) * (1 - hi)
    other = 1 - c
    mid = zz == 2
    end = zz == 3
    to_x = (d_x, e)
    to_y = (d_y, e)
    to_sib = (d, 2 * z + other)
    e_in = e + 2 - 4 * hi
    to_in = (d, e_in)
    to_out = (d, jnp.where(zz == 2, e - 2 + 4 * hi, e_in))

    dqs = block_out
    dmix = dtok_out
    dx_ref = dtok_out

    first_loads = [
        pltpu.make_async_copy(dx_hbm, dx_ref, load_sem.at[9]),
        pltpu.make_async_copy(mixed_hbm, mixed_ref, load_sem.at[10]),
    ]
    for load in first_loads:
        load.start()

    barrier = pltpu.get_barrier_semaphore()
    for target in (to_x, to_y, to_sib, to_in):
        pl.semaphore_signal(barrier, inc=1, device_id=target, device_id_type=MESH)

    @pl.when(mid)
    def _():
        pl.semaphore_signal(barrier, inc=1, device_id=to_out, device_id_type=MESH)

    pl.semaphore_wait(barrier, 7 - zz)

    def order(i):
        v = i if i < 2 else (5 - zz if i == 2 else zz)
        return v * hi + (3 - v) * (1 - hi)

    def across(k, src, t, fx, fy):
        def diag(i):
            return remote(
                src(d_d, i), t.at[i], t_send.at[k, i], t_recv.at[k, i], (to_x, to_y)[i % 2]
            )

        def direct(i):
            if i % 2 == 0:
                return remote(src(d_x, i), fx.at[i], d_send.at[k, i], x_recv.at[k, i], to_x)
            return remote(src(d_y, i), fy.at[i], d_send.at[k, i], y_recv.at[k, i], to_y)

        def summed(i, ref):
            if i % 2 == 0:
                return remote(ref, fy.at[i], s_send.at[k, i], y_recv.at[k, i], to_y)
            return remote(ref, fx.at[i], s_send.at[k, i], x_recv.at[k, i], to_x)

        def wait_t(i):
            remote(t.at[i], t.at[i], t_send.at[k, i], t_recv.at[k, i], to_x).wait_recv()

        def wait_xy(i):
            remote(fx.at[i], fx.at[i], d_send.at[k, i], x_recv.at[k, i], to_x).wait_recv()
            remote(fy.at[i], fy.at[i], d_send.at[k, i], y_recv.at[k, i], to_y).wait_recv()

        def drain(n):
            for i in range(n):
                diag(i).wait_send()
                direct(i).wait_send()
                summed(i, t.at[i]).wait_send()

        return diag, direct, summed, wait_t, wait_xy, drain

    def along(k, slot, ro, ri):
        def send(i, target, dst, recv):
            return remote(slot(i), dst.at[i], hop_send.at[k, i], recv.at[k, i], target)

        def to_ro(i):
            return send(i, to_in, ro, ro_recv)

        def to_ri(i):
            return send(i, to_in if i < 2 else to_out, ri, ri_recv)

        def wait_ro(i):
            remote(ro.at[i], ro.at[i], hop_send.at[k, i], ro_recv.at[k, i], to_in).wait_recv()

        def wait_ri(i):
            remote(ri.at[i], ri.at[i], hop_send.at[k, i], ri_recv.at[k, i], to_in).wait_recv()

        def drain():
            for i in range(3):
                to_ro(i).wait_send()

        return to_ro, to_ri, wait_ro, wait_ri, drain

    def expert_src(dd, p):
        return gin_hbm.at[pl.ds(pl.multiple_of(dd * 384 + p * PIECE, 16), PIECE)]

    e_diag, e_direct, e_summed, e_wait_t, e_wait_xy, e_drain = across(0, expert_src, te, xe, ye)

    def e_load(p, dd, j):
        return pltpu.make_async_copy(expert_src(dd, p), le.at[j], le_sem.at[j])

    def e_middle(p):
        load = e_load(p, d_y if p % 2 == 0 else d_x, 0)
        load.start()
        e_wait_t(p)
        load.wait()
        te[p] = (te[p].astype(f32) + le[0].astype(f32)).astype(bf)
        e_summed(p, te.at[p]).start()

    def e_final(p):
        load = e_load(p, d, 1)
        load.start()
        e_wait_xy(p)
        load.wait()
        total = le[1].astype(f32) + xe[p].astype(f32) + ye[p].astype(f32)
        ein_out[p * PIECE : (p + 1) * PIECE] = total.astype(bf)

    def d_src(dd):
        return gout_hbm.at[dd]

    def d_diag():
        return remote(d_src(d_d), td, t_send.at[5, 0], t_recv.at[5, 0], to_y)

    def d_direct():
        return remote(d_src(d_y), yd, d_send.at[5, 0], y_recv.at[5, 0], to_y)

    def d_summed():
        return remote(td, xd, s_send.at[5, 0], x_recv.at[5, 0], to_x)

    def d_load(dd, j):
        return pltpu.make_async_copy(d_src(dd), ld, le_sem.at[j])

    def d_middle():
        load = d_load(d_x, 2)
        load.start()
        d_diag().wait_recv()
        load.wait()
        td[...] = (td[...].astype(f32) + ld[...].astype(f32)).astype(bf)
        d_summed().start()

    def d_final():
        load = d_load(d, 3)
        load.start()
        d_summed().wait_recv()
        d_direct().wait_recv()
        load.wait()
        eout_out[...] = (
            ld[...].astype(f32) + xd[...].astype(f32) + yd[...].astype(f32)
        ).astype(bf)

    def store_q(total):
        gq_out[...] = total

    def store_b(total):
        gb_out[...] = total

    def store_k(total):
        gkv_out[...] = total[:, :512]
        small_out[...] = lax.dot_general(
            eye[:16],
            total[:, 512:],
            (((1,), (1,)), ((), ())),
            preferred_element_type=f32,
            precision=highest,
        )

    dense = (
        (gq, sib_q, tq, xq, yq, roq, riq, store_q),
        (gb, sib_b, tb, xb, yb, rob, rib, store_b),
        (gk, sib_k, tw, xw, yw, row_, riw, store_k),
    )

    def dense_stream(j):
        grad, sib, t, fx, fy, ro, ri, out = dense[j]

        def src(dd, i):
            return grad.at[dd * 4 + order(i), c]

        diag, direct, summed, wait_t, wait_xy, drain = across(1 + j, src, t, fx, fy)

        def own_slot(i):
            return grad.at[d * 4 + order(i), c]

        to_ro, to_ri, wait_ro, wait_ri, drain_z = along(j, own_slot, ro, ri)

        def sib_copy():
            return remote(grad.at[:, other], sib, ds_send.at[j], ds_recv.at[j], to_sib)

        def begin():
            sib_copy().wait_recv()

            @pl.loop(0, 16)
            def _(k):
                grad[k, c] = (grad[k, c].astype(f32) + sib[k].astype(f32)).astype(bf)

            for i in range(4):
                diag(i).start()
            for i in range(4):
                direct(i).start()

        def middle(i):
            dd = d_y if i % 2 == 0 else d_x
            wait_t(i)
            at = dd * 4 + order(i)
            grad[at, c] = (grad[at, c].astype(f32) + t[i].astype(f32)).astype(bf)
            summed(i, src(dd, i)).start()

        def local(i):
            return grad[d * 4 + order(i), c].astype(f32) + fx[i].astype(f32) + fy[i].astype(f32)

        def put(i, total):
            grad[d * 4 + order(i), c] = total.astype(bf)

        def last(i):
            wait_xy(i)
            if i == 3:
                return

            @pl.when(end)
            def _():
                put(i, local(i))
                to_ro(i).start()

        def hop(i):
            @pl.when(mid)
            def _():
                if i < 2:
                    wait_ro(i)
                    put(i, local(i) + ro[i].astype(f32))
                else:
                    wait_ri(0)
                    put(2, local(2) + ri[0].astype(f32))
                to_ri(i).start()

        def finish():
            @pl.when(mid)
            def _():
                wait_ro(2)
                wait_ri(1)
                out(local(3) + ro[2].astype(f32) + ri[1].astype(f32))

            @pl.when(end)
            def _():
                wait_ri(2)
                out(local(3) + ri[2].astype(f32))

        def drain_all():
            sib_copy().wait_send()
            drain(4)
            drain_z()

        return sib_copy, begin, middle, last, hop, finish, drain_all

    q_sib, q_begin, q_middle, q_last, q_hop, q_finish, q_drain = dense_stream(0)
    b_sib, b_begin, b_middle, b_last, b_hop, b_finish, b_drain = dense_stream(1)
    w_sib, w_begin, w_middle, w_last, w_hop, w_finish, w_drain = dense_stream(2)

    def out_rows(i, lane):
        return outp_hbm.at[pl.ds(pl.multiple_of((2 * order(i) + lane) * CHUNK, CHUNK), CHUNK)]

    def out_sib(i):
        return remote(out_rows(i, other), osib.at[i], os_send.at[i], os_recv.at[i], to_sib)

    o_ro, o_ri, o_wait_ro, o_wait_ri, _ = along(3, lambda i: oslot.at[i % 2], oro, ori)

    def out_sum(i, incoming, store):
        out_sib(i).wait_recv()
        for half in range(2):
            rows = pl.ds(half * 128, 128)
            loads = [
                pltpu.make_async_copy(ref.at[rows], old.at[j], old_sem.at[j])
                for j, ref in enumerate([out_rows(i, c), osib.at[i]] + incoming)
            ]
            for load in loads:
                load.start()
            for load in loads:
                load.wait()
            total = old[0].astype(f32)
            for j in range(1, len(loads)):
                total = total + old[j].astype(f32)
            store(slice(half * 128, (half + 1) * 128), total)

    def out_slot(i):
        def store(rows, total):
            oslot[i % 2, rows] = total.astype(bf)

        return store

    def out_end(i):
        @pl.when(end)
        def _():
            if i == 2:
                o_ro(0).wait_send()
            out_sum(i, [], out_slot(i))
            o_ro(i).start()

    def out_mid(i):
        @pl.when(mid)
        def _():
            if i < 2:
                o_wait_ro(i)
                out_sum(i, [oro.at[i]], out_slot(i))
            else:
                o_ri(0).wait_send()
                o_wait_ri(0)
                out_sum(2, [ori.at[0]], out_slot(2))
            o_ri(i).start()

    def out_finish():
        def store(rows, total):
            total = total + mixed_ref[rows]
            slot = d * 128 + lax.broadcasted_iota(jnp.int32, (128, 1), 0)
            live = slot < lens_ref[rows.start // 128]
            block_out[rows] = jnp.where(live, total, 0.0).astype(bf)

        @pl.when(mid)
        def _():
            o_wait_ro(2)
            o_wait_ri(1)
            out_sum(3, [oro.at[2], ori.at[1]], store)

        @pl.when(end)
        def _():
            o_wait_ri(2)
            out_sum(3, [ori.at[2]], store)

    def kv_src(dd, i):
        return dkv.at[dd, pl.ds(i * 128, 128)]

    k_diag, k_direct, k_summed, k_wait_t, k_wait_xy, k_drain = across(4, kv_src, tk, xk, yk)

    def k_middle(i):
        dd = d_y if i % 2 == 0 else d_x
        k_wait_t(i)
        rows = slice(i * 128, (i + 1) * 128)
        dkv[dd, rows] = (dkv[dd, rows].astype(f32) + tk[i].astype(f32)).astype(bf)
        k_summed(i, kv_src(dd, i)).start()

    small_load = pltpu.make_async_copy(wa_hbm.at[:, pl.ds(2048, 128)], small, load_sem.at[0])
    wb_load = pltpu.make_async_copy(wb_hbm, wide.at[:, pl.ds(0, 1536)], load_sem.at[1])
    wa_load = pltpu.make_async_copy(wa_hbm.at[:, pl.ds(0, 2048)], wide, load_sem.at[2])
    rope_load = pltpu.make_async_copy(
        rope_hbm.at[:, pl.ds(pl.multiple_of(d * 128, 128), 128)], rope, load_sem.at[3]
    )
    small_load.start()
    loads = [
        pltpu.make_async_copy(src, dst, load_sem.at[4 + j])
        for j, (src, dst) in enumerate(
            (
                (cot_hbm, cot_ref),
                (att_hbm, att_ref),
                (q_hbm, q_ref),
                (kv_hbm, kv_ref),
                (tok_hbm, tok_ref),
            )
        )
    ]
    for load in loads[:2]:
        load.start()
    wb_load.start()
    rope_load.start()
    for load in loads[2:]:
        load.start()
    for p in range(4):
        e_diag(p).start()
    for p in (0, 2):
        e_direct(p).start()
    d_diag().start()
    for i in range(4):
        out_sib(i).start()
    out_end(0)

    nt = (((1,), (1,)), ((), ()))
    tn = (((0,), (0,)), ((), ()))

    def dot_nt(a, b):
        return lax.dot_general(a, b, nt, preferred_element_type=f32)

    def dot_tn(a, b):
        return lax.dot_general(a, b, tn, preferred_element_type=f32)

    eye = (
        lax.broadcasted_iota(jnp.int32, (128, 128), 0)
        == lax.broadcasted_iota(jnp.int32, (128, 128), 1)
    ).astype(f32)
    eye_low = eye.astype(bf)
    gates = jnp.concatenate([gates_ref[s] for s in range(2)], axis=1)
    dgate = jnp.concatenate([dgt_ref[s] for s in range(2)], axis=1)
    dlogit = gates * (dgate - jnp.sum(gates * dgate, axis=0, keepdims=True))
    dl_hi = dlogit.astype(bf).astype(f32)
    dl = jnp.concatenate([dl_hi, dlogit - dl_hi], axis=0).astype(bf)
    small_load.wait()
    small_t = dot_nt(eye_low[:16], small[...])
    router = jnp.concatenate([small_t[:8]] * 2, axis=0).astype(bf)
    for load in first_loads:
        load.wait()
    dn2 = dx_ref[...] + dot_tn(dl, router)
    mixed = mixed_ref[...]
    inv2 = lax.rsqrt(jnp.mean(mixed * mixed, axis=1, keepdims=True) + epsilon)
    n2 = mixed * inv2
    normed2 = (n2 * small_t[9:10]).astype(bf)
    router_sum = jnp.dot(dl, normed2, preferred_element_type=f32)
    router_sum = router_sum[:8] + router_sum[8:]
    mid_sum = jnp.sum(dn2 * n2, axis=0, keepdims=True)
    loads[0].wait()
    loads[1].wait()
    grads = [
        jnp.where(
            d * 128 + lax.broadcasted_iota(jnp.int32, (128, 1), 0) < lens_ref[s],
            cot_ref[s * 128 : (s + 1) * 128].astype(f32),
            0.0,
        )
        for s in range(2)
    ]
    u = dn2 * small_t[9:10]
    dmixed = jnp.concatenate(grads, axis=0) + inv2 * (u - n2 * jnp.mean(u * n2, axis=1, keepdims=True))
    dmix[...] = dmixed
    dproj = dmixed.astype(bf)
    for r in range(4):
        part = dot_tn(att_ref[:, r * 384 : (r + 1) * 384], dproj)
        gb[4 * r : 4 * r + 4] = part.astype(bf).reshape(4, 2, 48, 1536)
    b_sib().start()
    wb_load.wait()
    datt = dot_nt(dproj, wide[:, :1536]).astype(bf)
    for head in range(QUERY_HEADS):
        for s in range(2):
            at = (s * QUERY_HEADS + head) * 128
            dat[at : at + 128] = datt[s * 128 : (s + 1) * 128, head * 128 : (head + 1) * 128]
    wa_load.start()
    b_begin()
    out_end(1)

    query_pos = d * 128 + lax.broadcasted_iota(jnp.int32, (128, 512), 0)
    key_pos = lax.broadcasted_iota(jnp.int32, (128, 512), 1)
    rope_load.wait()
    for load in loads[2:]:
        load.wait()
    cos_rows = rope[0]
    sin_rows = rope[1]
    scale = HEAD_SIZE ** (-0.5)

    def unrotate_rows(v, cos, sin):
        return v * cos - pltpu.roll(v, 64, 1) * sin

    def attend(n):
        s = lax.div(n, 2)
        h = lax.rem(n, 2)
        srow = pl.ds(pl.multiple_of(s * 128, 128), 128)
        kcol = pl.ds(pl.multiple_of(h * 128, 128), 128)
        vcol = pl.ds(pl.multiple_of(256 + h * 128, 128), 128)
        lens = lens_ref[s]
        allowed = (key_pos <= query_pos) & (key_pos < lens)
        ks = kv_ref[:, srow, kcol].reshape(512, 128)
        vs = kv_ref[:, srow, vcol].reshape(512, 128)
        dk = None
        dv = None
        for half in range(2):
            rows = pl.ds(pl.multiple_of(n * 768 + half * 384, 128), 384)
            qh = q_ref[rows]
            dh = dat[rows]
            scores = dot_nt(qh, ks).reshape(3, 128, 512) * scale
            scores = jnp.where(allowed[None], scores, -1e30)
            probs = jnp.exp(scores - jnp.max(scores, axis=-1, keepdims=True))
            probs = probs * (1.0 / jnp.sum(probs, axis=-1, keepdims=True))
            dprobs = dot_nt(dh, vs).reshape(3, 128, 512)
            delta = jnp.sum(probs * dprobs, axis=-1, keepdims=True)
            dscores = (probs * (dprobs - delta)).astype(bf).reshape(384, 512)
            low = probs.astype(bf).reshape(384, 512)
            dq = jnp.dot(dscores, ks, preferred_element_type=f32) * scale
            for j in range(3):
                dqs[srow, pl.ds(pl.multiple_of(h * 768 + (half * 3 + j) * 128, 128), 128)] = (
                    unrotate_rows(dq[j * 128 : (j + 1) * 128], cos_rows, sin_rows).astype(bf)
                )
            dk_part = dot_tn(dscores, qh)
            dv_part = dot_tn(low, dh)
            dk = dk_part if dk is None else dk + dk_part
            dv = dv_part if dv is None else dv + dv_part
        dkv[:, srow, kcol] = (dk * scale).astype(bf).reshape(4, 128, 128)
        dkv[:, srow, vcol] = dv.astype(bf).reshape(4, 128, 128)

    pl.loop(0, 2)(attend)
    for i in range(4):
        b_middle(i)
    e_direct(1).start()
    e_middle(1)
    out_mid(0)
    pl.loop(2, 4)(attend)
    for i in range(2):
        k_diag(i).start()
    for i in range(2):
        k_direct(i).start()
    for i in range(4):
        b_last(i)
    out_end(2)

    tok = tok_ref[...].astype(f32)
    inv1 = lax.rsqrt(jnp.mean(tok * tok, axis=1, keepdims=True) + epsilon)
    n1 = tok * inv1
    normed = (n1 * small_t[8:9]).astype(bf)
    for r in range(4):
        part = dot_tn(normed[:, r * 384 : (r + 1) * 384], dqs[...])
        gq[4 * r : 4 * r + 4] = part.astype(bf).reshape(4, 2, 48, 1536)
    q_sib().start()
    k_middle(0)
    k_middle(1)
    q_begin()
    wa_load.wait()
    dn1 = dot_nt(dqs[...], wide[:, :1536])

    for i in range(2):
        k_wait_xy(i)
    own = jnp.concatenate(
        [
            dkv[d, i * 128 : (i + 1) * 128].astype(f32) + xk[i].astype(f32) + yk[i].astype(f32)
            for i in range(2)
        ],
        axis=0,
    )
    cos_two = jnp.concatenate([cos_rows] * 2, axis=0)
    sin_two = jnp.concatenate([sin_rows] * 2, axis=0)
    dkv_own = jnp.concatenate(
        [
            unrotate_rows(own[:, h * 128 : (h + 1) * 128], cos_two, sin_two)
            for h in range(2)
        ]
        + [own[:, 256:]],
        axis=1,
    ).astype(bf)
    dn1 = dn1 + dot_nt(dkv_own, wide[:, 1536:])
    pre_sum = jnp.sum(dn1 * n1, axis=0, keepdims=True)
    row8 = lax.broadcasted_iota(jnp.int32, (8, 1536), 0)
    gains = jnp.where(row8 == 0, pre_sum, jnp.where(row8 == 1, mid_sum, 0.0))
    smalls = jnp.concatenate([router_sum, gains], axis=0).astype(bf)
    for r in range(4):
        cols = slice(r * 384, (r + 1) * 384)
        part = dot_tn(normed[:, cols], dkv_own)
        gk[4 * r : 4 * r + 4, :, :, :512] = part.astype(bf).reshape(4, 2, 48, 512)
        part = dot_tn(smalls[:, cols], eye_low[:16])
        gk[4 * r : 4 * r + 4, :, :, 512:] = part.astype(bf).reshape(4, 2, 48, 128)
    w_sib().start()
    u = dn1 * small_t[8:9]
    dtok_copy = pltpu.make_async_copy(dtok_out, dtok_hbm, load_sem.at[11])
    dtok_out[...] = dmix[...] + inv1 * (u - n1 * jnp.mean(u * n1, axis=1, keepdims=True))

    dtok_copy.start()

    for i in range(4):
        q_middle(i)
    w_begin()
    e_direct(3).start()
    b_hop(0)
    b_hop(1)
    out_mid(1)
    out_mid(2)
    for i in range(4):
        q_last(i)
    for i in range(4):
        w_middle(i)
    d_direct().start()
    d_middle()
    for p in (3, 0, 2):
        e_middle(p)
    b_hop(2)
    for i in range(3):
        q_hop(i)
    out_finish()
    block_copy = pltpu.make_async_copy(block_out, block_hbm, load_sem.at[12])
    block_copy.start()
    b_finish()
    for i in range(4):
        w_last(i)
    for i in range(3):
        w_hop(i)
    q_finish()
    for p in range(4):
        e_final(p)
    d_final()
    w_finish()
    dtok_copy.wait()
    block_copy.wait()

    e_drain(4)
    for copy in (d_diag(), d_direct(), d_summed()):
        copy.wait_send()
    k_drain(2)
    q_drain()
    b_drain()
    w_drain()
    for i in range(1, 3):
        o_ro(i).wait_send()
    for i in range(4):
        out_sib(i).wait_send()


def backward_stage(dx, dgt, gates, mixed, cot, tok, q, kv, att, lens, rope, wa, wb, gin, gout, outp):
    bf, f32 = jnp.bfloat16, jnp.float32
    shape = jax.ShapeDtypeStruct
    width = tok.shape[-1]
    hbm = pl.BlockSpec(memory_space=pltpu.HBM)
    vmem = pl.BlockSpec(memory_space=pltpu.VMEM)
    smem = pl.BlockSpec(memory_space=pltpu.SMEM)
    dma = pltpu.SemaphoreType.DMA
    widths = (width, width, 640)
    dense = []
    for w in widths:
        dense += [pltpu.VMEM((4, 48, w), bf)] * 3 + [pltpu.VMEM((3, 48, w), bf)] * 2
    return pl.pallas_call(
        backward_kernel,
        out_shape=(
            shape((CHUNK, width), bf),
            shape((CHUNK, width), f32),
            shape((48, width), f32),
            shape((48, width), f32),
            shape((48, 512), f32),
            shape((16, 48), f32),
            shape((384, FF), bf),
            shape((PIECE, width), bf),
            shape((4, CHUNK, width), bf),
            shape((3, CHUNK, width), bf),
            shape((3, CHUNK, width), bf),
        ),
        in_specs=[hbm, vmem, vmem] + [hbm] * 6 + [smem] + [hbm] * 6,
        out_specs=[hbm] * 2 + [vmem] * 6 + [hbm] * 3,
        scratch_shapes=[
            pltpu.VMEM((width, 2048), bf),
            pltpu.VMEM((width, 128), bf),
            *[pltpu.VMEM((16, 2, 48, w), bf) for w in widths],
            *[pltpu.VMEM((16, 48, w), bf) for w in widths],
            *dense,
            *([pltpu.VMEM((4, PIECE, FF), bf)] * 3),
            pltpu.VMEM((2, PIECE, FF), bf),
            *([pltpu.VMEM((PIECE, width), bf)] * 4),
            pltpu.VMEM((4, 128, width), bf),
            pltpu.VMEM((2, CHUNK, width), bf),
            pltpu.VMEM((2 * QUERY_HEADS * 128, 128), bf),
            pltpu.VMEM((4, CHUNK, 512), bf),
            *([pltpu.VMEM((2, 128, 512), bf)] * 3),
            pltpu.VMEM((2, 128, 128), f32),
            *[pltpu.VMEM(ref.shape, ref.dtype) for ref in (cot, tok, q, kv, att, mixed)],
            pltpu.VMEM((CHUNK, width), bf),
            pltpu.VMEM((CHUNK, width), f32),
            dma((13,)),
            dma((4,)),
            dma((4,)),
            dma((4,)),
            dma((4,)),
            dma((3,)),
            dma((3,)),
            dma((6, 4)),
            dma((6, 4)),
            dma((6, 4)),
            dma((6, 4)),
            dma((6, 4)),
            dma((6, 4)),
            dma((4, 3)),
            dma((4, 3)),
            dma((4, 3)),
        ],
        compiler_params=pltpu.CompilerParams(
            collective_id=3, has_side_effects=True, vmem_limit_bytes=64 * 2**20 - 65536
        ),
        name="backward_stage",
    )(dx, dgt, gates, mixed, cot, tok, q, kv, att, lens, rope, wa, wb, gin, gout, outp)


def finish_kernel(
    block_in,
    dtok_in,
    gq_in,
    gb_in,
    gkv_in,
    small_ref,
    first_ref,
    second_ref,
    down_first_ref,
    down_second_ref,
    block_out,
    dtok_out,
    gq_out,
    gb_out,
    gkv_out,
    pre_out,
    mid_out,
    router_out,
    in_out,
    down_out,
):
    f32 = jnp.float32
    i = pl.program_id(0)
    block_out[...] = block_in[...]
    dtok_out[...] = dtok_in[...]
    gq_out[...] = gq_in[...]
    gb_out[...] = gb_in[...]
    gkv_out[...] = gkv_in[...]
    half = FF // 2
    first = first_ref[...].astype(f32)
    second = second_ref[...].astype(f32)
    in_out[:, :half] = first[:, :half]
    in_out[:, half:FF] = second[:, :half]
    in_out[:, FF : FF + half] = first[:, half:]
    in_out[:, FF + half :] = second[:, half:]
    down_out[...] = jnp.where(i < 2, down_first_ref[...], down_second_ref[...]).astype(f32)
    router_out[...] = small_ref[:8]
    pre_out[...] = small_ref[8:9]
    mid_out[...] = small_ref[9:10]


def finish_stage(block, dtok, gq, gb, gkv, small, first, second, down_first, down_second):
    f32 = jnp.float32
    shape = jax.ShapeDtypeStruct
    width = block.shape[-1]

    def rows(count, columns, index):
        return pl.BlockSpec((count, columns), index)

    def whole(count, columns):
        return pl.BlockSpec((count, columns), lambda i: (0, 0))

    return pl.pallas_call(
        finish_kernel,
        grid=(4,),
        out_shape=(
            shape(block.shape, block.dtype),
            shape(dtok.shape, f32),
            shape(gq.shape, f32),
            shape(gb.shape, f32),
            shape(gkv.shape, f32),
            shape((1, 48), f32),
            shape((1, 48), f32),
            shape((8, 48), f32),
            shape((384, 2 * FF), f32),
            shape((192, width), f32),
        ),
        in_specs=[
            rows(64, width, lambda i: (i, 0)),
            rows(64, width, lambda i: (i, 0)),
            whole(48, width),
            whole(48, width),
            whole(48, 512),
            whole(16, 48),
            rows(96, FF, lambda i: (i, 0)),
            rows(96, FF, lambda i: (i, 0)),
            rows(48, width, lambda i: (jnp.minimum(i, 1), 0)),
            rows(48, width, lambda i: (jnp.maximum(i - 2, 0), 0)),
        ],
        out_specs=[
            rows(64, width, lambda i: (i, 0)),
            rows(64, width, lambda i: (i, 0)),
            whole(48, width),
            whole(48, width),
            whole(48, 512),
            whole(1, 48),
            whole(1, 48),
            whole(8, 48),
            rows(96, 2 * FF, lambda i: (i, 0)),
            rows(48, width, lambda i: (i, 0)),
        ],
        name="finish_stage",
    )(block, dtok, gq, gb, gkv, small, first, second, down_first, down_second)


def rope_constant(slots):
    half = HEAD_SIZE // 2
    inv_freq = np.float32(rope_base) ** (-(np.arange(half, dtype=np.float32) * 2.0 / HEAD_SIZE))
    angles = np.arange(slots, dtype=np.float32)[:, None] * inv_freq[None, :].astype(np.float32)
    cos, sin = np.cos(angles), np.sin(angles)
    return np.stack(
        [np.concatenate([cos, cos], axis=1), np.concatenate([-sin, sin], axis=1)]
    ).astype(np.float32)


def fast_local(
    tokens,
    lengths,
    routes,
    prenorm,
    w_query,
    key_value_weight,
    w_output,
    midnorm,
    w_router,
    expert_in,
    expert_out,
    cotangent,
):
    seqs, token_rows, width = tokens.shape
    rows = seqs * token_rows
    tok = tokens.reshape(rows, width)
    cot = cotangent.reshape(rows, width)
    rope = jnp.asarray(rope_constant(token_rows * lax.axis_size("dp")))
    full_a, full_b, full_out, gall, q_rot, kv_all, attended, mixed, normed2, gates = attention_stage(
        tok,
        w_query,
        key_value_weight,
        w_router.T,
        prenorm[None],
        midnorm[None],
        w_output,
        cot,
        expert_out[0],
        rope,
        lengths,
        jnp.transpose(routes, (0, 2, 1)),
    )
    dx, dgate, outp, gin, gout, out_first, g_first = expert_stage(normed2, gall, gates, expert_in[0], full_out)
    block_out, grad_tokens, g_query, g_b, g_kv, small, g_second, out_second = backward_stage(
        dx, dgate, gates, mixed, cot, tok, q_rot, kv_all, attended, lengths, rope,
        full_a, full_b, gin.reshape(width, FF), gout, outp.reshape(8 * rows, width),
    )[:8]
    block_out, grad_tokens, g_query, g_b, g_kv, g_pre, g_mid, g_router, g_in, g_out = finish_stage(
        block_out, grad_tokens, g_query, g_b, g_kv, small, g_first, g_second, out_first, out_second
    )
    return (
        block_out.reshape(seqs, token_rows, width),
        grad_tokens.reshape(seqs, token_rows, width),
        g_pre.reshape(-1),
        g_query,
        g_kv,
        g_b,
        g_mid.reshape(-1),
        g_router.T,
        g_in[None],
        g_out[None],
    )


def solution(mesh):
    placed = (
        P("expert", "dp", None),
        P("expert"),
        P("expert", "dp", None),
        P(("dp", "expert")),
        P(("dp", "expert"), None),
        P(("dp", "expert"), None),
        P(("dp", "expert"), None),
        P(("dp", "expert")),
        P(("dp", "expert"), None),
        P("expert", "dp", None),
        P("expert", "dp", None),
        P("expert", "dp", None),
    )
    fits = mesh.shape["dp"] == 4 and mesh.shape["expert"] == 8
    return jax.shard_map(
        fast_local if fits else local,
        mesh=mesh,
        in_specs=placed,
        out_specs=(
            P("expert", "dp", None),
            P("expert", "dp", None),
            P(("dp", "expert")),
            P(("dp", "expert"), None),
            P(("dp", "expert"), None),
            P(("dp", "expert"), None),
            P(("dp", "expert")),
            P(("dp", "expert"), None),
            P("expert", "dp", None),
            P("expert", "dp", None),
        ),
        check_vma=False,
    )
```

```python
import jax
import jax.numpy as jnp
import numpy as np
from jax import lax
from jax.experimental import pallas as pl
from jax.experimental.pallas import tpu as pltpu
from jax.sharding import PartitionSpec as P

QUERY_HEADS = 12
KEY_VALUE_HEADS = 2
HEAD_SIZE = 128
FF = 768
TOP = 4


epsilon = 1e-06
rope_base = 10000.0
highest = lax.Precision.HIGHEST


def rope_tables(positions):
    half_width = HEAD_SIZE // 2
    inv_freq = rope_base ** (-(jnp.arange(half_width, dtype=jnp.float32) * 2.0 / HEAD_SIZE))
    angles = positions.astype(jnp.float32)[:, None] * inv_freq[None, :]
    return (jnp.cos(angles), jnp.sin(angles))


def apply_rotation(values, cosine_table, sine_table):
    half_width = values.shape[-1] // 2
    first_half = values[..., :half_width]
    second = values[..., half_width:]
    cos_rows = cosine_table[:, None, :]
    sin_rows = sine_table[:, None, :]
    return jnp.concatenate(
        [first_half * cos_rows - second * sin_rows, second * cos_rows + first_half * sin_rows],
        axis=-1,
    )


def unrotate(values, cosine_table, sine_table):
    half_width = values.shape[-1] // 2
    first_half = values[..., :half_width]
    second = values[..., half_width:]
    cos_rows = cosine_table[:, None, :]
    sin_rows = sine_table[:, None, :]
    return jnp.concatenate(
        [first_half * cos_rows + second * sin_rows, second * cos_rows - first_half * sin_rows],
        axis=-1,
    )


def rms_parts(values):
    inverse = lax.rsqrt(jnp.mean(values * values, axis=-1, keepdims=True) + epsilon)
    return (values * inverse, inverse)


def norm_back(grad_normed, normalized_input, inverse, gain):
    scaled = grad_normed * gain
    return inverse * (
        scaled - normalized_input * jnp.mean(scaled * normalized_input, axis=-1, keepdims=True)
    )


def slot_index(route_rows, expert_count, capacity):
    flat_routes = route_rows.reshape(-1)
    onehot = (flat_routes[:, None] == jnp.arange(expert_count, dtype=jnp.int32)[None, :]).astype(
        jnp.int32
    )
    before = jnp.cumsum(onehot, axis=0) - onehot
    within = jnp.sum(before * onehot, axis=-1)
    return flat_routes * capacity + within


def masked_scores(query_matrix, key_rows, allowed):
    scores = jnp.einsum(
        "qhgd,khd->hgqk", query_matrix, key_rows, preferred_element_type=jnp.float32
    ) * HEAD_SIZE ** (-0.5)
    return jnp.where(allowed[None, None], scores, -1e30)


def local(
    tokens,
    lengths,
    routes,
    prenorm,
    w_query,
    key_value_weight,
    w_output,
    midnorm,
    w_router,
    expert_in,
    expert_out,
    cotangent,
):
    micro_count, token_rows, hidden_width = tokens.shape
    dp_size = lax.axis_size("dp")
    expert_size = lax.axis_size("expert")
    dp_rank = lax.axis_index("dp")
    local_experts = expert_in.shape[0]
    expert_count = local_experts * expert_size
    capacity = max(2, 3 * token_rows * TOP // (2 * expert_count))
    query_group_width = QUERY_HEADS // KEY_VALUE_HEADS
    expert_slot_total = token_rows * dp_size
    score_scale = HEAD_SIZE ** (-0.5)
    positions = dp_rank * token_rows + jnp.arange(token_rows, dtype=jnp.int32)
    key_pos = jnp.arange(expert_slot_total, dtype=jnp.int32)
    cosine_table, sine_table = rope_tables(positions)
    total_prenorm = jnp.zeros((hidden_width,), jnp.float32)
    total_query = jnp.zeros((hidden_width, QUERY_HEADS * HEAD_SIZE), jnp.float32)
    total_key_value = jnp.zeros((hidden_width, 2 * KEY_VALUE_HEADS * HEAD_SIZE), jnp.float32)
    total_output = jnp.zeros((QUERY_HEADS * HEAD_SIZE, hidden_width), jnp.float32)
    total_midnorm = jnp.zeros((hidden_width,), jnp.float32)
    total_router = jnp.zeros((hidden_width, expert_count), jnp.float32)
    total_upper = jnp.zeros((local_experts, hidden_width, 2 * FF), jnp.float32)
    total_down = jnp.zeros((local_experts, FF, hidden_width), jnp.float32)
    outputs_list = []
    grads_list = []
    for micro_step in range(micro_count):
        dense_all = (
            lax.all_gather(prenorm, ("dp", "expert"), axis=0, tiled=True),
            lax.all_gather(w_query, ("dp", "expert"), axis=0, tiled=True),
            lax.all_gather(key_value_weight, ("dp", "expert"), axis=0, tiled=True),
            lax.all_gather(w_output, ("dp", "expert"), axis=0, tiled=True),
            lax.all_gather(midnorm, ("dp", "expert"), axis=0, tiled=True),
            lax.all_gather(w_router, ("dp", "expert"), axis=0, tiled=True),
        )
        expert_all = (
            lax.all_gather(expert_in, "dp", axis=1, tiled=True),
            lax.all_gather(expert_out, "dp", axis=1, tiled=True),
        )
        gain_one = dense_all[0].astype(jnp.float32)
        query_all = dense_all[1]
        keyval_all = dense_all[2]
        output_all = dense_all[3]
        gain_two = dense_all[4].astype(jnp.float32)
        router_all = dense_all[5]
        gateup_all = expert_all[0]
        down_all = expert_all[1]
        input_rows = tokens[micro_step].astype(jnp.float32)
        length = lengths[micro_step]
        route_rows = routes[micro_step]
        live_rows = (positions < length)[:, None]
        normed_one, inverse_one = rms_parts(input_rows)
        normalized_input = (normed_one * gain_one).astype(jnp.bfloat16)
        query_pre = jnp.dot(
            normalized_input, query_all, preferred_element_type=jnp.float32
        ).reshape(token_rows, QUERY_HEADS, HEAD_SIZE)
        keyval_pre = jnp.dot(
            normalized_input, keyval_all, preferred_element_type=jnp.float32
        ).reshape(token_rows, 2, KEY_VALUE_HEADS, HEAD_SIZE)
        query_matrix = (
            apply_rotation(query_pre, cosine_table, sine_table)
            .astype(jnp.bfloat16)
            .reshape(token_rows, KEY_VALUE_HEADS, query_group_width, HEAD_SIZE)
        )
        local_key_rows = apply_rotation(keyval_pre[:, 0], cosine_table, sine_table).astype(
            jnp.bfloat16
        )
        local_value_rows = keyval_pre[:, 1].astype(jnp.bfloat16)
        packed_tokens = jnp.stack([local_key_rows, local_value_rows], axis=1).reshape(
            token_rows, 2 * KEY_VALUE_HEADS * HEAD_SIZE
        )
        gathered_rows = lax.all_gather(packed_tokens, "dp", axis=0, tiled=True).reshape(
            expert_slot_total, 2, KEY_VALUE_HEADS, HEAD_SIZE
        )
        key_rows = gathered_rows[:, 0]
        value_rows = gathered_rows[:, 1]
        allowed = (key_pos[None, :] <= positions[:, None]) & (key_pos[None, :] < length)
        scores = masked_scores(query_matrix, key_rows, allowed)
        top_score = jnp.max(scores, axis=-1, keepdims=True)
        weights = jnp.exp(scores - top_score)
        weight_total = jnp.sum(weights, axis=-1, keepdims=True)
        log_total = top_score + jnp.log(weight_total)
        probs_low = (weights / weight_total).astype(jnp.bfloat16)
        attended = jnp.einsum(
            "hgqk,khd->qhgd", probs_low, value_rows, preferred_element_type=jnp.float32
        )
        attended = attended.reshape(token_rows, QUERY_HEADS * HEAD_SIZE).astype(jnp.bfloat16)
        mixed_rows = input_rows + jnp.dot(attended, output_all, preferred_element_type=jnp.float32)
        normed_mid, inverse_two = rms_parts(mixed_rows)
        normed_two = (normed_mid * gain_two).astype(jnp.bfloat16)
        logits = jnp.dot(normed_two, router_all, preferred_element_type=jnp.float32)
        onehot = (
            route_rows[:, :, None] == jnp.arange(expert_count, dtype=jnp.int32)[None, None, :]
        ).astype(jnp.float32)
        chosen = jnp.sum(onehot * logits[:, None, :], axis=-1)
        gate_values = jax.nn.softmax(chosen, axis=-1)
        slot_idx = slot_index(route_rows, expert_count, capacity)
        send_rows = jnp.zeros((expert_count * capacity, hidden_width), jnp.bfloat16)
        send_rows = send_rows.at[slot_idx].set(jnp.repeat(normed_two, TOP, axis=0))
        received = lax.all_to_all(
            send_rows.reshape(expert_count, capacity, hidden_width),
            "expert",
            split_axis=0,
            concat_axis=0,
            tiled=True,
        )
        item_count = received.shape[1]
        grouped = received.reshape(expert_size, local_experts, item_count, hidden_width)
        gate_up = jnp.einsum(
            "slcd,ldf->slcf", grouped, gateup_all, preferred_element_type=jnp.float32
        )
        hidden = (jax.nn.silu(gate_up[..., :FF]) * gate_up[..., FF:]).astype(jnp.bfloat16)
        result = jnp.einsum(
            "slcf,lfd->slcd", hidden, down_all, preferred_element_type=jnp.float32
        ).astype(jnp.bfloat16)
        back_rows = lax.all_to_all(
            result.reshape(expert_count, item_count, hidden_width),
            "expert",
            split_axis=0,
            concat_axis=0,
            tiled=True,
        )
        back_rows, kept_rows, kept_gateup = (
            back_rows,
            received,
            gate_up.reshape(expert_count, item_count, 2 * FF),
        )
        returned = back_rows.reshape(expert_count * capacity, hidden_width)[slot_idx].reshape(
            token_rows, TOP, hidden_width
        )
        returned_wide = returned.astype(jnp.float32)
        expert_sum = jnp.sum(gate_values[:, :, None] * returned_wide, axis=1)
        final_rows = jnp.where(live_rows, mixed_rows + expert_sum, 0.0)
        outputs_list.append(final_rows.astype(jnp.bfloat16))
        grad_rows = jnp.where(live_rows, cotangent[micro_step].astype(jnp.float32), 0.0)
        grad_gate = jnp.sum(grad_rows[:, None, :] * returned_wide, axis=-1)
        grad_chosen = gate_values * (
            grad_gate - jnp.sum(gate_values * grad_gate, axis=-1, keepdims=True)
        )
        grad_logits = jnp.sum(onehot * grad_chosen[:, :, None], axis=1)
        router_term = jnp.dot(normed_two.astype(jnp.float32).T, grad_logits, precision=highest)
        grad_normtwo = jnp.dot(grad_logits, router_all.astype(jnp.float32).T, precision=highest)
        grad_result = (
            (gate_values[:, :, None] * grad_rows[:, None, :])
            .astype(jnp.bfloat16)
            .reshape(token_rows * TOP, hidden_width)
        )
        send_grads = (
            jnp.zeros((expert_count * capacity, hidden_width), jnp.bfloat16)
            .at[slot_idx]
            .set(grad_result)
        )
        recv_grads, again_rows = (
            lax.all_to_all(
                send_grads.reshape(expert_count, capacity, hidden_width),
                "expert",
                split_axis=0,
                concat_axis=0,
                tiled=True,
            ),
            lax.all_to_all(
                send_rows.reshape(expert_count, capacity, hidden_width),
                "expert",
                split_axis=0,
                concat_axis=0,
                tiled=True,
            ),
        )
        grouped_rows = again_rows.reshape(expert_size, local_experts, capacity, hidden_width)
        gate_up = jnp.einsum(
            "slcd,ldf->slcf", grouped_rows, gateup_all, preferred_element_type=jnp.float32
        )
        grouped_grads = recv_grads.reshape(expert_size, local_experts, capacity, hidden_width)
        gate_part = gate_up[..., :FF]
        up_part = gate_up[..., FF:]
        sigmoid_gate = jax.nn.sigmoid(gate_part)
        silu_gate = gate_part * sigmoid_gate
        hidden = (silu_gate * up_part).astype(jnp.bfloat16)
        grad_hidden = jnp.einsum(
            "slcd,lfd->slcf", grouped_grads, down_all, preferred_element_type=jnp.float32
        )
        down_term = jnp.einsum(
            "slcf,slcd->lfd", hidden, grouped_grads, preferred_element_type=jnp.float32
        )
        grad_gatepart = (
            grad_hidden * up_part * sigmoid_gate * (1.0 + gate_part * (1.0 - sigmoid_gate))
        )
        grad_gateup = jnp.concatenate([grad_gatepart, grad_hidden * silu_gate], axis=-1).astype(
            jnp.bfloat16
        )
        upper_term = jnp.einsum(
            "slcd,slcf->ldf", grouped_rows, grad_gateup, preferred_element_type=jnp.float32
        )
        grad_copies = jnp.einsum(
            "slcf,ldf->slcd", grad_gateup, gateup_all, preferred_element_type=jnp.float32
        ).astype(jnp.bfloat16)
        back_grads = lax.all_to_all(
            grad_copies.reshape(expert_count, capacity, hidden_width),
            "expert",
            split_axis=0,
            concat_axis=0,
            tiled=True,
        )
        copy_rows = back_grads.reshape(expert_count * capacity, hidden_width)[slot_idx].reshape(
            token_rows, TOP, hidden_width
        )
        grad_normtwo = grad_normtwo + jnp.sum(copy_rows.astype(jnp.float32), axis=1)
        midnorm_term = jnp.sum(grad_normtwo * normed_mid, axis=0)
        grad_mixed = grad_rows + norm_back(grad_normtwo, normed_mid, inverse_two, gain_two)
        grad_proj = grad_mixed.astype(jnp.bfloat16)
        output_term = jnp.dot(attended.T, grad_proj, preferred_element_type=jnp.float32)
        attention_gradient = jnp.dot(
            grad_proj, output_all.T, preferred_element_type=jnp.float32
        ).astype(jnp.bfloat16)
        attention_gradient = attention_gradient.reshape(
            token_rows, KEY_VALUE_HEADS, query_group_width, HEAD_SIZE
        )
        scores = masked_scores(query_matrix, key_rows, allowed)
        prob_rows = jnp.exp(scores - log_total)
        grad_probs = jnp.einsum(
            "qhgd,khd->hgqk", attention_gradient, value_rows, preferred_element_type=jnp.float32
        )
        row_delta = jnp.sum(prob_rows * grad_probs, axis=-1, keepdims=True)
        grad_scores = (prob_rows * (grad_probs - row_delta)).astype(jnp.bfloat16)
        prob_low = prob_rows.astype(jnp.bfloat16)
        grad_qrot = (
            jnp.einsum("hgqk,khd->qhgd", grad_scores, key_rows, preferred_element_type=jnp.float32)
            * score_scale
        )
        grad_keys = (
            jnp.einsum(
                "hgqk,qhgd->khd", grad_scores, query_matrix, preferred_element_type=jnp.float32
            )
            * score_scale
        )
        grad_vals = jnp.einsum(
            "hgqk,qhgd->khd", prob_low, attention_gradient, preferred_element_type=jnp.float32
        )
        own_keys = (
            lax.psum_scatter(
                jnp.stack([grad_keys, grad_vals], axis=1)
                .reshape(lax.axis_size("dp") * token_rows, 2 * KEY_VALUE_HEADS * HEAD_SIZE)
                .astype(jnp.bfloat16),
                "dp",
                scatter_dimension=0,
                tiled=True,
            )
            .astype(jnp.float32)
            .reshape(token_rows, 2, KEY_VALUE_HEADS, HEAD_SIZE)
        )
        grad_query = (
            unrotate(
                grad_qrot.reshape(token_rows, QUERY_HEADS, HEAD_SIZE), cosine_table, sine_table
            )
            .astype(jnp.bfloat16)
            .reshape(token_rows, QUERY_HEADS * HEAD_SIZE)
        )
        key_gradient = unrotate(own_keys[:, 0], cosine_table, sine_table).astype(jnp.bfloat16)
        value_gradient = own_keys[:, 1].astype(jnp.bfloat16)
        key_value_weight_gradient = jnp.stack([key_gradient, value_gradient], axis=1).reshape(
            token_rows, 2 * KEY_VALUE_HEADS * HEAD_SIZE
        )
        query_term = jnp.dot(normalized_input.T, grad_query, preferred_element_type=jnp.float32)
        keyval_term = jnp.dot(
            normalized_input.T, key_value_weight_gradient, preferred_element_type=jnp.float32
        )
        grad_normone = jnp.dot(grad_query, query_all.T, preferred_element_type=jnp.float32)
        grad_normone = grad_normone + jnp.dot(
            key_value_weight_gradient, keyval_all.T, preferred_element_type=jnp.float32
        )
        prenorm_term = jnp.sum(grad_normone * normed_one, axis=0)
        grads_list.append(grad_mixed + norm_back(grad_normone, normed_one, inverse_one, gain_one))
        total_prenorm = total_prenorm + prenorm_term
        total_query = total_query + query_term
        total_key_value = total_key_value + keyval_term
        total_output = total_output + output_term
        total_midnorm = total_midnorm + midnorm_term
        total_router = total_router + router_term
        total_upper = total_upper + upper_term
        total_down = total_down + down_term
    dense_grads = (
        lax.psum_scatter(total_prenorm, ("dp", "expert"), scatter_dimension=0, tiled=True),
        lax.psum_scatter(total_query, ("dp", "expert"), scatter_dimension=0, tiled=True),
        lax.psum_scatter(total_key_value, ("dp", "expert"), scatter_dimension=0, tiled=True),
        lax.psum_scatter(total_output, ("dp", "expert"), scatter_dimension=0, tiled=True),
        lax.psum_scatter(total_midnorm, ("dp", "expert"), scatter_dimension=0, tiled=True),
        lax.psum_scatter(total_router, ("dp", "expert"), scatter_dimension=0, tiled=True),
    )
    expert_grads = (
        lax.psum_scatter(
            total_upper.astype(jnp.bfloat16), "dp", scatter_dimension=1, tiled=True
        ).astype(jnp.float32),
        lax.psum_scatter(
            total_down.astype(jnp.bfloat16), "dp", scatter_dimension=1, tiled=True
        ).astype(jnp.float32),
    )
    return (
        jnp.stack(outputs_list),
        jnp.stack(grads_list),
        dense_grads[0],
        dense_grads[1],
        dense_grads[2],
        dense_grads[3],
        dense_grads[4],
        dense_grads[5],
        expert_grads[0],
        expert_grads[1],
    )


MESH = pl.DeviceIdType.MESH
CHUNK = 256
PIECE = 96


def remote(src, dst, send_sem, recv_sem, target):
    return pltpu.make_async_remote_copy(
        src_ref=src,
        dst_ref=dst,
        send_sem=send_sem,
        recv_sem=recv_sem,
        device_id=target,
        device_id_type=MESH,
    )


def place():
    d = lax.axis_index("dp")
    e = lax.axis_index("expert")
    z = lax.div(e, 2)
    c = lax.rem(e, 2)
    x = lax.rem(d, 2)
    y = lax.div(d, 2)
    return d, e, z, c, x, y


def attention_kernel(
    tok_hbm,
    wq_hbm,
    wkv_hbm,
    wr_ref,
    pre_ref,
    mid_ref,
    wb_hbm,
    cot_hbm,
    wo_hbm,
    rope_hbm,
    lens_ref,
    routes_ref,
    wa_out,
    wb_out,
    wo_out,
    gall,
    q_out,
    kv_out,
    att_out,
    mixed_hbm,
    normed_hbm,
    gates_out,
    wa,
    wb,
    qs,
    kvs,
    att,
    g_own,
    rope,
    tok_ref,
    cot_ref,
    mixed_out,
    normed_out,
    own_sem,
    wo_recv,
    wo_send,
    z_recv,
    z_send,
    xy_recv,
    xy_send,
    sib_recv,
    sib_send,
    g_recv,
    g_send,
    gs_recv,
    gs_send,
    kv_recv,
    kv_send,
):
    bf, f32 = jnp.bfloat16, jnp.float32
    d, e, z, c, x, y = place()
    d_x = d + 1 - 2 * x
    d_y = d + 2 - 4 * y
    d_d = 3 - d
    other = 1 - c
    to_x = (d_x, e)
    to_y = (d_y, e)
    to_sib = (d, 2 * z + other)
    to_up = (d, e + jnp.where(z < 3, 2, -2))
    to_down = (d, e + jnp.where(z > 0, -2, 2))

    barrier = pltpu.get_barrier_semaphore()
    for target in (to_x, to_y, to_sib):
        pl.semaphore_signal(barrier, inc=1, device_id=target, device_id_type=MESH)

    @pl.when(z < 3)
    def _():
        pl.semaphore_signal(barrier, inc=1, device_id=to_up, device_id_type=MESH)

    @pl.when(z > 0)
    def _():
        pl.semaphore_signal(barrier, inc=1, device_id=to_down, device_id_type=MESH)

    own_at = pl.multiple_of((d * 8 + e) * 48, 16)
    own_rows = pl.ds(own_at, 48)
    own_a = [
        pltpu.make_async_copy(wq_hbm, wa.at[own_rows, pl.ds(0, 1536)], own_sem.at[0]),
        pltpu.make_async_copy(wkv_hbm, wa.at[own_rows, pl.ds(1536, 512)], own_sem.at[1]),
        pltpu.make_async_copy(rope_hbm.at[:, pl.ds(pl.multiple_of(d * 128, 128), 128)], rope, own_sem.at[2]),
    ]
    loads = [
        pltpu.make_async_copy(cot_hbm, cot_ref, own_sem.at[8]),
        pltpu.make_async_copy(tok_hbm, tok_ref, own_sem.at[9]),
    ]
    for copy in own_a + loads:
        copy.start()
    eye = lax.broadcasted_iota(jnp.int32, (128, 128), 0) == lax.broadcasted_iota(
        jnp.int32, (128, 128), 1
    )
    eye_low = eye.astype(bf)
    turned = (((0,), (0,)), ((), ()))
    sub = lax.broadcasted_iota(jnp.int32, (8, 48), 0)
    gains = jnp.where(
        sub == 0,
        pre_ref[...].astype(f32),
        jnp.where(sub == 1, mid_ref[...].astype(f32), 0.0),
    )
    tile = jnp.concatenate([wr_ref[...].astype(f32), gains], axis=0).astype(bf)
    wa[own_rows, 2048:] = lax.dot_general(
        tile, eye_low[:16], turned, preferred_element_type=f32
    ).astype(bf)
    full = (wa, wb)
    shard = (None, wb_hbm)

    def block(a, dd, zp, lane):
        at = pl.multiple_of((dd * 8 + 2 * zp + lane) * 48, 16)
        return full[a].at[pl.ds(at, 48)]

    def z_copy(a, zp, way, src=None):
        ref = block(a, d, zp, c)
        return remote(
            ref if src is None else src,
            ref,
            z_send.at[a, way, zp],
            z_recv.at[a, zp],
            to_up if way == 0 else to_down,
        )

    def xy_copy(a, dd, zp, row, target, src=None):
        ref = block(a, dd, zp, c)
        return remote(
            ref if src is None else src,
            ref,
            xy_send.at[a, row, zp],
            xy_recv.at[a, row, zp],
            target,
        )

    def s_copy(a, dd, zp, src=None, lane=None):
        ref = block(a, dd, zp, c if lane is None else lane)
        return remote(
            ref if src is None else src,
            ref,
            sib_send.at[a, dd, zp],
            sib_recv.at[a, dd, zp],
            to_sib,
        )

    def send_xy(a, zp):
        xy_copy(a, d, zp, 0, to_x).start()
        xy_copy(a, d, zp, 1, to_y).start()

    def own_start(a):
        @pl.when(z < 3)
        def _():
            z_copy(a, z, 0, shard[a]).start()

        @pl.when(z > 0)
        def _():
            z_copy(a, z, 1, shard[a]).start()

        s_copy(a, d, z, shard[a]).start()

    def from_z(a, k):
        def arrived(zp, way):
            z_copy(a, zp, way).wait_recv()

            @pl.when((z < 3) if way == 0 else (z > 0))
            def _():
                z_copy(a, zp, way).start()

            if a == 0:
                send_xy(a, zp)
            s_copy(a, d, zp).start()

        @pl.when(z - k >= 0)
        def _():
            arrived(z - k, 0)

        @pl.when(z + k <= 3)
        def _():
            arrived(z + k, 1)

    def from_xy_one(a, zp):
        xy_copy(a, d_x, zp, 0, to_x).wait_recv()

        @pl.when(lax.rem(zp, 2) == 0)
        def _():
            xy_copy(a, d_x, zp, 2, to_y).start()

        s_copy(a, d_x, zp).start()
        xy_copy(a, d_y, zp, 1, to_y).wait_recv()

        @pl.when(lax.rem(zp, 2) == 1)
        def _():
            xy_copy(a, d_y, zp, 2, to_x).start()

        s_copy(a, d_y, zp).start()

    def from_xy(a, k):
        @pl.when(z - k >= 0)
        def _():
            from_xy_one(a, z - k)

        if k > 0:

            @pl.when(z + k <= 3)
            def _():
                from_xy_one(a, z + k)

    def from_diag(a):
        for k in range(4):
            zp = lax.rem(z + k, 4)
            xy_copy(a, d_d, zp, 2, to_x).wait_recv()
            s_copy(a, d_d, zp).start()

    def from_sib(a):
        for dd in range(4):
            for zp in range(4):
                s_copy(a, dd, zp, lane=other).wait_recv()

    def drain(a):
        for zp in range(4):
            for dd in range(4):
                s_copy(a, dd, zp).wait_send()
            for row in range(3):
                xy_copy(a, d, zp, row, to_x).wait_send()

            @pl.when((zp <= z) & (z < 3))
            def _():
                z_copy(a, zp, 0).wait_send()

            @pl.when((zp >= z) & (z > 0))
            def _():
                z_copy(a, zp, 1).wait_send()

    def g_part(zp, lane, s):
        at = pl.multiple_of((2 * zp + lane) * CHUNK + s * 128, 128)
        return gall.at[pl.ds(at, 128)]

    def g_copy(zp, s, way, src=None):
        ref = g_part(zp, c, s)
        return remote(
            ref if src is None else src,
            ref,
            g_send.at[way, zp, s],
            g_recv.at[zp, s],
            to_up if way == 0 else to_down,
        )

    def gs_copy(zp, s, src=None, lane=None):
        ref = g_part(zp, c if lane is None else lane, s)
        return remote(
            ref if src is None else src, ref, gs_send.at[zp, s], gs_recv.at[zp, s], to_sib
        )

    def g_start():
        for s in range(2):
            src = g_own.at[pl.ds(s * 128, 128)]

            @pl.when(z < 3)
            def _():
                g_copy(z, s, 0, src).start()

            @pl.when(z > 0)
            def _():
                g_copy(z, s, 1, src).start()

            gs_copy(z, s, src).start()

    def g_pass(k, s):
        @pl.when(z - k >= 0)
        def _():
            g_copy(z - k, s, 0).wait_recv()

            @pl.when(z < 3)
            def _():
                g_copy(z - k, s, 0).start()

            gs_copy(z - k, s).start()

        @pl.when(z + k <= 3)
        def _():
            g_copy(z + k, s, 1).wait_recv()

            @pl.when(z > 0)
            def _():
                g_copy(z + k, s, 1).start()

            gs_copy(z + k, s).start()

    def wo_copy(dd, p, row, target, src=None):
        ref = wo_out.at[pl.ds(pl.multiple_of(dd * 192 + p * PIECE, 16), PIECE)]
        return remote(
            ref if src is None else src, ref, wo_send.at[row, p], wo_recv.at[row, p], target
        )

    def wo_start(p):
        wo_copy(d, p, 0, to_x, wo_hbm.at[pl.ds(p * PIECE, PIECE)]).start()
        wo_copy(d, 1 - p, 1, to_y, wo_hbm.at[pl.ds((1 - p) * PIECE, PIECE)]).start()

    def wo_pass():
        wo_copy(d_x, 0, 0, to_x).wait_recv()
        wo_copy(d_x, 0, 2, to_y).start()
        wo_copy(d_y, 1, 1, to_y).wait_recv()
        wo_copy(d_y, 1, 2, to_x).start()

    def wo_rest():
        wo_copy(d_x, 1, 0, to_x).wait_recv()
        wo_copy(d_y, 0, 1, to_y).wait_recv()
        for p in range(2):
            wo_copy(d_d, p, 2, to_x).wait_recv()

    pl.semaphore_wait(barrier, 5 - jnp.where((z == 0) | (z == 3), 1, 0))
    for copy in own_a:
        copy.wait()
    own_start(0)
    own_start(1)
    own = [
        pltpu.make_async_copy(wb_hbm, block(1, d, z, c), own_sem.at[0]),
        pltpu.make_async_copy(
            g_own, gall.at[pl.ds(pl.multiple_of(e * CHUNK, CHUNK), CHUNK)], own_sem.at[1]
        ),
        pltpu.make_async_copy(
            wo_hbm, wo_out.at[pl.ds(pl.multiple_of(d * 192, 16), 192)], own_sem.at[2]
        ),
    ]
    own[0].start()
    own[2].start()
    send_xy(0, z)
    own[0].wait()
    at_end = (z == 0) | (z == 3)

    @pl.when(at_end)
    def _():
        send_xy(1, z)

    loads[0].wait()
    for s in range(2):
        rows = slice(s * 128, (s + 1) * 128)
        slot = d * 128 + lax.broadcasted_iota(jnp.int32, (128, 1), 0)
        g_own[rows] = jnp.where(slot < lens_ref[s], cot_ref[rows].astype(f32), 0.0).astype(bf)

    own[1].start()
    loads[1].wait()
    tok = tok_ref[...].astype(f32)
    n1 = tok * lax.rsqrt(jnp.mean(tok * tok, axis=1, keepdims=True) + epsilon)
    from_z(0, 1)
    from_z(1, 1)
    from_xy(0, 0)
    from_z(0, 2)
    from_z(1, 2)
    g_start()
    from_xy(0, 1)
    from_z(0, 3)
    from_z(1, 3)
    from_xy(0, 2)
    from_xy(0, 3)

    def turn(j):
        return lax.rem(z + j, 4)

    @pl.when(jnp.logical_not(at_end))
    def _():
        send_xy(1, z)

    send_xy(1, turn(1))
    from_diag(0)
    from_sib(0)

    small_t = lax.dot_general(
        eye_low[:16], wa[:, 2048:], (((1,), (1,)), ((), ())), preferred_element_type=f32
    )
    normed = (n1 * small_t[8:9]).astype(bf)
    cos_rows = jnp.concatenate([rope[0]] * 2, axis=0)
    sin_rows = jnp.concatenate([rope[1]] * 2, axis=0)

    def rotate(v):
        return v * cos_rows + pltpu.roll(v, 64, 1) * sin_rows

    kv = jnp.dot(normed, wa[:, 1536:2048], preferred_element_type=f32)
    for h in range(2):
        kvs[d, :, h * 128 : (h + 1) * 128] = rotate(kv[:, h * 128 : (h + 1) * 128]).astype(bf)
    kvs[d, :, 256:] = kv[:, 256:].astype(bf)

    def kv_copy(dd, s, row, target):
        ref = kvs.at[dd, pl.ds(s * 128, 128)]
        return remote(ref, ref, kv_send.at[row, s], kv_recv.at[row, s], target)

    for s in range(2):
        kv_copy(d, s, 0, to_x).start()
        kv_copy(d, 1 - s, 1, to_y).start()
    send_xy(1, turn(2))
    g_pass(1, 0)
    q = jnp.dot(normed, wa[:, :1536], preferred_element_type=f32)
    for head in range(QUERY_HEADS):
        rot = rotate(q[:, head * 128 : (head + 1) * 128]).astype(bf)
        for s in range(2):
            at = (s * QUERY_HEADS + head) * 128
            qs[at : at + 128] = rot[s * 128 : (s + 1) * 128]
    kv_copy(d_x, 0, 0, to_x).wait_recv()
    kv_copy(d_x, 0, 2, to_y).start()
    kv_copy(d_y, 1, 1, to_y).wait_recv()
    kv_copy(d_y, 1, 2, to_x).start()
    send_xy(1, turn(3))
    for j in range(2):
        from_xy_one(1, turn(j))
    g_pass(1, 1)
    kv_copy(d_y, 0, 1, to_y).wait_recv()
    kv_copy(d_x, 1, 0, to_x).wait_recv()
    for s in range(2):
        kv_copy(d_d, s, 2, to_x).wait_recv()
    q_copy = pltpu.make_async_copy(qs, q_out, own_sem.at[3])
    kvo_copy = pltpu.make_async_copy(kvs, kv_out, own_sem.at[4])
    wa_copy = pltpu.make_async_copy(wa, wa_out, own_sem.at[5])
    for copy in (q_copy, kvo_copy, wa_copy):
        copy.start()

    query_pos = d * 128 + lax.broadcasted_iota(jnp.int32, (128, 512), 0)
    key_pos = lax.broadcasted_iota(jnp.int32, (128, 512), 1)

    def attend(n):
        s = lax.div(n, 2)
        h = lax.rem(n, 2)
        lens = lens_ref[s]
        allowed = (key_pos <= query_pos) & (key_pos < lens)
        ks = kvs[:, pl.ds(pl.multiple_of(s * 128, 128), 128), pl.ds(pl.multiple_of(h * 128, 128), 128)]
        vs = kvs[:, pl.ds(pl.multiple_of(s * 128, 128), 128), pl.ds(pl.multiple_of(256 + h * 128, 128), 128)]
        ks = ks.reshape(512, 128)
        vs = vs.reshape(512, 128)
        for half in range(2):
            qh = qs[pl.ds(pl.multiple_of(n * 768 + half * 384, 128), 384)]
            scores = lax.dot_general(qh, ks, (((1,), (1,)), ((), ())), preferred_element_type=f32)
            scores = scores.reshape(3, 128, 512) * HEAD_SIZE ** (-0.5)
            scores = jnp.where(allowed[None], scores, -1e30)
            top = jnp.max(scores, axis=-1, keepdims=True)
            weights = jnp.exp(scores - top)
            weights = weights * (1.0 / jnp.sum(weights, axis=-1, keepdims=True))
            out = jnp.dot(
                weights.astype(bf).reshape(384, 512), vs, preferred_element_type=f32
            ).astype(bf)
            for j in range(3):
                att[
                    pl.ds(pl.multiple_of(s * 128, 128), 128),
                    pl.ds(pl.multiple_of(h * 768 + (half * 3 + j) * 128, 128), 128),
                ] = out[j * 128 : (j + 1) * 128]

    wo_start(0)
    g_pass(2, 0)
    pl.loop(0, 2)(attend)
    from_xy_one(1, turn(2))
    from_xy_one(1, turn(3))
    wo_start(1)
    g_pass(2, 1)

    @pl.loop(2, 4)
    def _(n):
        attend(n)
        pl.when(n == 2)(wo_pass)

    from_diag(1)
    from_sib(1)
    att_copy = pltpu.make_async_copy(att, att_out, own_sem.at[6])
    wb_copy = pltpu.make_async_copy(wb, wb_out, own_sem.at[7])
    att_copy.start()
    wb_copy.start()
    mixed = tok_ref[...].astype(f32) + jnp.dot(att[...], wb[...], preferred_element_type=f32)
    mixed_out[...] = mixed
    mixed_copy = pltpu.make_async_copy(mixed_out, mixed_hbm, own_sem.at[10])
    mixed_copy.start()
    n2 = mixed * lax.rsqrt(jnp.mean(mixed * mixed, axis=1, keepdims=True) + epsilon)
    normed2 = (n2 * small_t[9:10]).astype(bf)
    normed_out[...] = normed2
    normed_copy = pltpu.make_async_copy(normed_out, normed_hbm, own_sem.at[11])
    normed_copy.start()
    logits = lax.dot_general(
        small_t[:8].astype(bf), normed2, (((1,), (1,)), ((), ())), preferred_element_type=f32
    )
    number = lax.broadcasted_iota(jnp.int32, (8, 128), 0)
    for s in range(2):
        chosen = number == routes_ref[s, 0:1]
        for t in range(1, TOP):
            chosen = chosen | (number == routes_ref[s, t : t + 1])
        picked = jnp.where(chosen, logits[:, s * 128 : (s + 1) * 128], -1e30)
        top = jnp.max(picked, axis=0, keepdims=True)
        weights = jnp.where(chosen, jnp.exp(picked - top), 0.0)
        gates_out[s] = weights / jnp.sum(weights, axis=0, keepdims=True)

    g_pass(3, 0)
    g_pass(3, 1)
    wo_rest()
    for zp in range(4):
        for s in range(2):
            gs_copy(zp, s, lane=other).wait_recv()
    own[1].wait()
    own[2].wait()
    for copy in (q_copy, kvo_copy, wa_copy, att_copy, wb_copy, mixed_copy, normed_copy):
        copy.wait()
    drain(0)
    drain(1)
    for s in range(2):
        for row in range(3):
            kv_copy(d, s, row, to_x).wait_send()
            wo_copy(d, s, row, to_x).wait_send()
        for zp in range(4):
            gs_copy(zp, s).wait_send()

            @pl.when((zp <= z) & (z < 3))
            def _():
                g_copy(zp, s, 0).wait_send()

            @pl.when((zp >= z) & (z > 0))
            def _():
                g_copy(zp, s, 1).wait_send()


def attention_stage(tok, wq, wkv, wr, pre, mid, wb, cot, wo, rope, lens, routes):
    bf, f32 = jnp.bfloat16, jnp.float32
    shape = jax.ShapeDtypeStruct
    width = tok.shape[-1]
    wide = wq.shape[-1] + wkv.shape[-1] + 128
    hbm = pl.BlockSpec(memory_space=pltpu.HBM)
    vmem = pl.BlockSpec(memory_space=pltpu.VMEM)
    smem = pl.BlockSpec(memory_space=pltpu.SMEM)
    dma = pltpu.SemaphoreType.DMA
    return pl.pallas_call(
        attention_kernel,
        out_shape=(
            shape((width, wide), bf),
            shape((width, width), bf),
            shape((FF, width), bf),
            shape((8 * CHUNK, width), bf),
            shape((2 * QUERY_HEADS * 128, 128), bf),
            shape((4, CHUNK, 512), bf),
            shape((CHUNK, width), bf),
            shape((CHUNK, width), f32),
            shape((CHUNK, width), bf),
            shape((2, 8, 128), f32),
        ),
        in_specs=[hbm, hbm, hbm, vmem, vmem, vmem, hbm, hbm, hbm, hbm, smem, vmem],
        out_specs=[hbm] * 9 + [vmem],
        scratch_shapes=[
            pltpu.VMEM((width, wide), bf),
            pltpu.VMEM((width, width), bf),
            pltpu.VMEM((2 * QUERY_HEADS * 128, 128), bf),
            pltpu.VMEM((4, CHUNK, 512), bf),
            pltpu.VMEM((CHUNK, width), bf),
            pltpu.VMEM((CHUNK, width), bf),
            pltpu.VMEM((2, 128, 128), f32),
            pltpu.VMEM((CHUNK, width), bf),
            pltpu.VMEM((CHUNK, width), bf),
            pltpu.VMEM((CHUNK, width), f32),
            pltpu.VMEM((CHUNK, width), bf),
            dma((12,)),
            dma((3, 2)),
            dma((3, 2)),
            dma((2, 4)),
            dma((2, 2, 4)),
            dma((2, 3, 4)),
            dma((2, 3, 4)),
            dma((2, 4, 4)),
            dma((2, 4, 4)),
            dma((4, 2)),
            dma((2, 4, 2)),
            dma((4, 2)),
            dma((4, 2)),
            dma((3, 2)),
            dma((3, 2)),
        ],
        compiler_params=pltpu.CompilerParams(
            collective_id=2, has_side_effects=True, vmem_limit_bytes=60 * 2**20
        ),
        name="attention_stage",
    )(tok, wq, wkv, wr, pre, mid, wb, cot, wo, rope, lens, routes)


def expert_kernel(
    x_hbm,
    g_hbm,
    gt_hbm,
    win_hbm,
    wout_hbm,
    dx_hbm,
    dgt_out,
    outp_hbm,
    gin_hbm,
    gout_hbm,
    gout_first_hbm,
    gin_first_hbm,
    win,
    wout,
    xall,
    gall,
    gtall,
    dgu,
    hg,
    dxb,
    dgb,
    sibr,
    sibg,
    ro,
    rog,
    ri,
    rig,
    gout,
    tg,
    xg,
    yg,
    gin,
    ti,
    xi,
    yi,
    kept,
    own_sem,
    stage_sem,
    grad_sem,
    g_recv,
    g_send,
    i_recv,
    i_send,
    w_recv,
    w_send,
    ag_recv,
    ag_send,
    sib_recv,
    sib_send,
    red_recv,
    red_send,
):
    bf, f32 = jnp.bfloat16, jnp.float32
    d, e, z, c, x, y = place()
    d_x = d + 1 - 2 * x
    d_y = d + 2 - 4 * y
    d_d = 3 - d
    hi = lax.div(z, 2)
    zz = z * hi + (3 - z) * (1 - hi)
    other = 1 - c
    to_x = (d_x, e)
    to_y = (d_y, e)
    to_sib = (d, 2 * z + other)
    to_up = (d, e + jnp.where(z < 3, 2, -2))
    to_down = (d, e + jnp.where(z > 0, -2, 2))
    e_in = e + 2 - 4 * hi
    to_in = (d, e_in)
    to_out = (d, jnp.where(zz == 2, e - 2 + 4 * hi, e_in))
    mid = zz == 2
    end = zz == 3

    barrier = pltpu.get_barrier_semaphore()
    for target in (to_x, to_y, to_sib, to_in):
        pl.semaphore_signal(barrier, inc=1, device_id=target, device_id_type=MESH)

    @pl.when(mid)
    def _():
        pl.semaphore_signal(barrier, inc=1, device_id=to_out, device_id_type=MESH)

    own_copies = [
        pltpu.make_async_copy(x_hbm.at[s], xall.at[e, s], own_sem.at[s]) for s in range(2)
    ] + [
        pltpu.make_async_copy(gt_hbm, gtall.at[e], own_sem.at[2]),
        pltpu.make_async_copy(wout_hbm, wout, own_sem.at[3]),
        pltpu.make_async_copy(g_hbm, gall, own_sem.at[4]),
    ]

    def w_columns(h, kind):
        return pl.ds(h * 768 + kind * 384, 384)

    for h in range(2):
        for kind in range(2):
            own_copies.append(
                pltpu.make_async_copy(
                    win_hbm.at[:, pl.ds(kind * 768 + h * 384, 384)],
                    win.at[d, :, w_columns(h, kind)],
                    own_sem.at[5 + 2 * h + kind],
                )
            )
    pl.semaphore_wait(barrier, 7 - zz)

    gathered = ((x_hbm, xall), (gt_hbm, gtall))

    def ag_copy(a, zp, s, way, src=None):
        ref = gathered[a][1].at[2 * zp + c, s]
        return remote(
            ref if src is None else src,
            ref,
            ag_send.at[way, a, zp, s],
            ag_recv.at[a, zp, s],
            to_up if way == 0 else to_down,
        )

    def sib_copy(a, zp, s, src=None, lane=None):
        ref = gathered[a][1].at[2 * zp + (c if lane is None else lane), s]
        return remote(
            ref if src is None else src,
            ref,
            sib_send.at[a, zp, s],
            sib_recv.at[a, zp, s],
            to_sib,
        )

    def own_rows(s):
        for a in range(2):
            src = gathered[a][0].at[s]

            @pl.when(z < 3)
            def _():
                ag_copy(a, z, s, 0, src).start()

            @pl.when(z > 0)
            def _():
                ag_copy(a, z, s, 1, src).start()

            sib_copy(a, z, s, src).start()

    def pass_on(k, s):
        for a in range(2):

            @pl.when(z - k >= 0)
            def _():
                ag_copy(a, z - k, s, 0).wait_recv()

                @pl.when(z < 3)
                def _():
                    ag_copy(a, z - k, s, 0).start()

                sib_copy(a, z - k, s).start()

            @pl.when(z + k <= 3)
            def _():
                ag_copy(a, z + k, s, 1).wait_recv()

                @pl.when(z > 0)
                def _():
                    ag_copy(a, z + k, s, 1).start()

                sib_copy(a, z + k, s).start()

    def from_sib(s):
        for a in range(2):
            for zp in range(4):
                sib_copy(a, zp, s, lane=other).wait_recv()

    def w_copy(h, kind, p, src_d, target, row, src=None):
        ref = win.at[src_d, pl.ds(p * 192, 192), w_columns(h, kind)]
        return remote(
            ref if src is None else src,
            ref,
            w_send.at[row, h, kind, p],
            w_recv.at[row, h, kind, p],
            target,
        )

    def w_start(h):
        for p in range(2):
            for kind in range(2):

                def src(q):
                    return win_hbm.at[
                        pl.ds(q * 192, 192), pl.ds(kind * 768 + h * 384, 384)
                    ]

                w_copy(h, kind, p, d, to_x, 0, src(p)).start()
                w_copy(h, kind, 1 - p, d, to_y, 1, src(1 - p)).start()

    def w_pass(h):
        for kind in range(2):
            w_copy(h, kind, 0, d_x, to_x, 0).wait_recv()
            w_copy(h, kind, 0, d_x, to_y, 2).start()
            w_copy(h, kind, 1, d_y, to_y, 1).wait_recv()
            w_copy(h, kind, 1, d_y, to_x, 2).start()

    def w_rest(h):
        for kind in range(2):
            w_copy(h, kind, 1, d_x, to_x, 0).wait_recv()
            w_copy(h, kind, 0, d_y, to_y, 1).wait_recv()
            for p in range(2):
                w_copy(h, kind, p, d_d, to_x, 2).wait_recv()

    own_rows(0)
    w_start(0)
    for copy in own_copies:
        copy.start()
    w_pass(0)
    w_start(1)
    pass_on(1, 0)
    pass_on(2, 0)
    own_rows(1)
    w_rest(0)
    w_pass(1)
    pass_on(3, 0)
    from_sib(0)
    for copy in own_copies:
        copy.wait()

    def order(i):
        v = i if i < 2 else (5 - zz if i == 2 else zz)
        return v * hi + (3 - v) * (1 - hi)

    def sib_sum(zp, s, a):
        src, dst = ((dxb, sibr), (dgb, sibg))[a]
        return remote(
            src.at[2 * zp + other, s], dst.at[zp, s], red_send.at[a, zp, s], red_recv.at[a, zp, s], to_sib
        )

    def hop(i, s, target, inward):
        dst, dstg, row = (ro, rog, 2) if inward else (ri, rig, 4)
        zp = order(i)
        return (
            remote(
                dxb.at[2 * zp + c, s], dst.at[i, s], red_send.at[2, i, s], red_recv.at[row, i, s], target
            ),
            remote(
                dgb.at[2 * zp + c, s], dstg.at[i, s], red_send.at[3, i, s], red_recv.at[row + 1, i, s], target
            ),
        )

    def wait_from(ref, refg, slot, s, row):
        remote(
            ref.at[slot, s], ref.at[slot, s], red_send.at[2, slot, s], red_recv.at[row, slot, s], to_in
        ).wait_recv()
        remote(
            refg.at[slot, s], refg.at[slot, s], red_send.at[3, slot, s], red_recv.at[row + 1, slot, s], to_in
        ).wait_recv()

    def combine(i, s, incoming):
        zp = order(i)
        for a in range(2):
            remote(
                sibr.at[zp, s] if a == 0 else sibg.at[zp, s],
                sibr.at[zp, s] if a == 0 else sibg.at[zp, s],
                red_send.at[a, zp, s],
                red_recv.at[a, zp, s],
                to_sib,
            ).wait_recv()
        for ref, refg, slot, row in incoming:
            wait_from(ref, refg, slot, s, row)
        total = dxb[2 * zp + c, s].astype(f32) + sibr[zp, s].astype(f32)
        totalg = dgb[2 * zp + c, s] + sibg[zp, s]
        for ref, refg, slot, row in incoming:
            total = total + ref[slot, s].astype(f32)
            totalg = totalg + refg[slot, s]
        return total, totalg

    def pass_sum(i, s, incoming, target, inward):
        total, totalg = combine(i, s, incoming)
        zp = order(i)
        dxb[2 * zp + c, s] = total.astype(bf)
        dgb[2 * zp + c, s] = totalg
        for copy in hop(i, s, target, inward):
            copy.start()

    def end_sums(s, which):
        @pl.when(end)
        def _():
            for i in which:
                pass_sum(i, s, (), to_in, True)

    def mid_sum(i, s):
        @pl.when(mid)
        def _():
            if i < 2:
                pass_sum(i, s, ((ro, rog, i, 2),), to_in, False)
            else:
                pass_sum(2, s, ((ri, rig, 0, 4),), to_out, False)

    def dx_copy(s):
        part = pl.ds(4 * s, 4)
        return pltpu.make_async_copy(kept.at[part], dx_hbm.at[part], own_sem.at[4 + s])

    def dx_store(s, total, totalg):
        for j in range(4):
            kept[4 * s + j] = total[:, j * 384 : (j + 1) * 384]
        dgt_out[s] = totalg

    def last_sum(s):
        @pl.when(mid)
        def _():
            dx_store(s, *combine(3, s, ((ro, rog, 2, 2), (ri, rig, 1, 4))))

        @pl.when(end)
        def _():
            dx_store(s, *combine(3, s, ((ri, rig, 2, 4),)))

        dx_copy(s).start()

    eye = lax.broadcasted_iota(jnp.int32, (128, 128), 0) == lax.broadcasted_iota(
        jnp.int32, (128, 128), 1
    )
    mine = lax.broadcasted_iota(jnp.int32, (8, 128), 0) == e
    nt = (((1,), (1,)), ((), ()))
    tn = (((0,), (0,)), ((), ()))

    def half_step(s, pair, h):
        first = 4 * pair
        block = pl.ds(first, 4)
        both = jnp.dot(
            xall[block, s].reshape(512, 1536),
            win[:, :, h * 768 : (h + 1) * 768].reshape(1536, 768),
            preferred_element_type=f32,
        )
        gate = both[:, :384]
        up = both[:, 384:]
        if h == 0:
            full = lax.dot_general(
                gall[block, s].reshape(512, 1536), wout[...], nt, preferred_element_type=f32
            )
            kept[block] = full[:, 384:].reshape(4, 128, 384)
            back = full[:, :384]
        else:
            back = kept[block].reshape(512, 384)
        columns = []
        for j in range(4):
            row = jnp.sum(jnp.where(mine, gtall[first + j, s], 0.0), axis=0, keepdims=True)
            columns.append(jnp.sum(jnp.where(eye, row, 0.0), axis=1, keepdims=True))
        weight = jnp.concatenate(columns, axis=0)
        sig = jax.nn.sigmoid(gate)
        silu = gate * sig
        hidden = (silu * up).astype(bf).astype(f32)
        dgate = jnp.sum(hidden * back, axis=1, keepdims=True)
        for j in range(4):
            row = jnp.sum(
                jnp.where(eye, dgate[j * 128 : (j + 1) * 128], 0.0), axis=0, keepdims=True
            )
            part = jnp.where(mine, row, 0.0)
            dgb[first + j, s] = part if h == 0 else dgb[first + j, s] + part
        hg[block, s, :, h * 384 : (h + 1) * 384] = (
            (hidden * weight).astype(bf).reshape(4, 128, 384)
        )
        back = back * weight
        dgu[block, s, :, h * 768 : h * 768 + 384] = (
            (back * up * (sig * (1.0 + gate * (1.0 - sig)))).astype(bf).reshape(4, 128, 384)
        )
        dgu[block, s, :, h * 768 + 384 : (h + 1) * 768] = (
            (back * silu).astype(bf).reshape(4, 128, 384)
        )

    def dx_step(s, pair):
        first = 4 * pair
        block = pl.ds(first, 4)
        dxb[block, s] = (
            lax.dot_general(
                dgu[block, s].reshape(512, 1536),
                win[...].reshape(1536, 1536),
                nt,
                preferred_element_type=f32,
            )
            .astype(bf)
            .reshape(4, 128, 1536)
        )
        for j in range(2):
            for a in range(2):
                sib_sum(2 * pair + j, s, a).start()

    def out_slot(slot):
        return win.at[:, pl.ds(slot * 128, 128)]

    def out_copy(slot, s, first):
        return pltpu.make_async_copy(
            out_slot(slot), outp_hbm.at[pl.ds(first, 4), s], stage_sem.at[slot]
        )

    def out_step(slot, s, pair):
        first = 4 * pair
        win[:, slot * 128 : (slot + 1) * 128] = (
            jnp.dot(
                hg[pl.ds(first, 4), s].reshape(512, FF), wout[...], preferred_element_type=f32
            )
            .astype(bf)
            .reshape(4, 128, 1536)
        )
        out_copy(slot, s, first).start()

    def early_copies(first):
        return [
            pltpu.make_async_copy(
                gout.at[pl.ds(j * 128, 128)], outp_hbm.at[first + j, 0], grad_sem.at[j]
            )
            for j in range(4)
        ]

    def early_step(pair):
        first = 4 * pair
        gout[:512] = jnp.dot(
            hg[pl.ds(first, 4), 0].reshape(512, FF), wout[...], preferred_element_type=f32
        ).astype(bf)
        for copy in early_copies(first):
            copy.start()

    def early_wait():
        for copy in early_copies(0):
            copy.wait()

    far = 1 - hi
    near = hi

    def pair_of(t):
        return far + t * (1 - 2 * far)

    def i_piece(dd, p):
        return gin.at[pl.ds(pl.multiple_of(dd * 384 + p * PIECE, 16), PIECE)]

    def i_diag(p):
        return remote(
            i_piece(d_d, p), ti.at[p], i_send.at[0, p], i_recv.at[0, p], (to_x, to_y)[p % 2]
        )

    def i_direct(p):
        if p % 2 == 0:
            return remote(i_piece(d_x, p), xi.at[p], i_send.at[1, p], i_recv.at[1, p], to_x)
        return remote(i_piece(d_y, p), yi.at[p], i_send.at[1, p], i_recv.at[2, p], to_y)

    def i_summed(p):
        if p % 2 == 0:
            return remote(i_piece(d_y, p), yi.at[p], i_send.at[2, p], i_recv.at[2, p], to_y)
        return remote(i_piece(d_x, p), xi.at[p], i_send.at[2, p], i_recv.at[1, p], to_x)

    def i_middle(p):
        i_diag(p).wait_recv()
        dd = d_y if p % 2 == 0 else d_x
        rows = pl.ds(pl.multiple_of(dd * 384 + p * PIECE, 16), PIECE)
        gin[rows] = (gin[rows].astype(f32) + ti[p].astype(f32)).astype(bf)
        i_summed(p).start()

    def i_final(p):
        remote(xi.at[p], xi.at[p], i_send.at[1, p], i_recv.at[1, p], to_x).wait_recv()
        remote(yi.at[p], yi.at[p], i_send.at[1, p], i_recv.at[2, p], to_y).wait_recv()
        rows = pl.ds(pl.multiple_of(d * 384 + p * PIECE, 16), PIECE)
        xi[p] = (gin[rows].astype(f32) + xi[p].astype(f32) + yi[p].astype(f32)).astype(bf)

    def in_grad(yy, h):
        return lax.dot_general(
            xall[:, :, :, pl.ds(pl.multiple_of(yy * 768, 128), 768)].reshape(2048, 768),
            dgu[:, :, :, h * 768 : (h + 1) * 768].reshape(2048, 768),
            tn,
            preferred_element_type=f32,
        ).astype(bf)

    def in_first(yy):
        gin[pl.ds(pl.multiple_of(yy * 768, 16), 768)] = in_grad(yy, 0)

    @pl.loop(0, 2)
    def _(t):
        half_step(0, pair_of(t), 0)

    @pl.when(mid)
    def _():
        pass_on(1, 1)

    w_rest(1)

    @pl.when(end)
    def _():
        pass_on(1, 1)


    @pl.loop(0, 2)
    def _(t):
        pair = pair_of(t)
        half_step(0, pair, 1)
        dx_step(0, pair)

        @pl.when(t == 0)
        def _():
            end_sums(0, (0, 1))
            pass_on(2, 1)

        @pl.when(t == 1)
        def _():
            end_sums(0, (2,))

    early_step(far)
    pass_on(3, 1)
    from_sib(1)

    @pl.loop(0, 2)
    def _(t):
        half_step(1, pair_of(t), 0)

    mid_sum(0, 0)

    @pl.loop(0, 2)
    def _(t):
        pair = pair_of(t)
        half_step(1, pair, 1)
        dx_step(1, pair)

        @pl.when(t == 0)
        def _():
            in_first(1 - y)
            for p in range(4):
                i_diag(p).start()
            for p in (1, 3):
                i_direct(p).start()
            end_sums(1, (0, 1))
            in_first(y)
            for p in (0, 2):
                i_direct(p).start()
            mid_sum(1, 0)
            mid_sum(2, 0)

    def g_rows(dd, i):
        return pl.ds(pl.multiple_of(dd * 192 + i * 48, 16), 48)

    def g_piece(dd, i):
        return gout.at[g_rows(dd, i)]

    def g_diag(i):
        return remote(
            g_piece(d_d, i), tg.at[i], g_send.at[0, i], g_recv.at[0, i], (to_x, to_y)[i]
        )

    def g_direct(i):
        if i == 0:
            return remote(g_piece(d_x, i), xg.at[i], g_send.at[1, i], g_recv.at[1, i], to_x)
        return remote(g_piece(d_y, i), yg.at[i], g_send.at[1, i], g_recv.at[2, i], to_y)

    def g_summed(i):
        if i == 0:
            return remote(g_piece(d_y, i), yg.at[i], g_send.at[2, i], g_recv.at[2, i], to_y)
        return remote(g_piece(d_x, i), xg.at[i], g_send.at[2, i], g_recv.at[1, i], to_x)

    def g_middle(i):
        g_diag(i).wait_recv()
        rows = g_rows(d_y if i == 0 else d_x, i)
        gout[rows] = (gout[rows].astype(f32) + tg[i].astype(f32)).astype(bf)
        g_summed(i).start()

    def out_grad(half):
        at = pl.multiple_of(half * 384, 128)
        gout[pl.ds(at, 384)] = lax.dot_general(
            hg[:, :, :, pl.ds(at, 384)].reshape(2048, 384),
            gall[...].reshape(2048, 1536),
            tn,
            preferred_element_type=f32,
        ).astype(bf)

    for p in range(4):
        i_middle(p)
    early_wait()
    out_grad(1 - y)
    g_diag(0).start()
    g_diag(1).start()
    g_direct(1).start()
    end_sums(1, (2,))
    out_grad(y)
    g_direct(0).start()
    mid_sum(0, 1)
    rest = [
        pltpu.make_async_copy(
            gout.at[pl.ds(k * 192 + PIECE, PIECE)], gout_hbm.at[k], own_sem.at[k]
        )
        for k in range(4)
    ]
    for copy in rest:
        copy.start()

    def grad_copy(k):
        return pltpu.make_async_copy(
            win.at[k, :, pl.ds(0, 768)], gin_hbm.at[k], grad_sem.at[k]
        )

    for h in range(2):
        for kind in range(2):
            for p in range(2):
                w_copy(h, kind, p, d, to_x, 2).wait_send()
    for k in range(2):
        win[2 * k : 2 * k + 2, :, :768] = in_grad(k, 1).reshape(2, 384, 768)
        grad_copy(2 * k).start()
        grad_copy(2 * k + 1).start()
    for p in range(4):
        i_final(p)
    in_copy = pltpu.make_async_copy(xi, gin_first_hbm, own_sem.at[6])
    in_copy.start()
    for k in range(4):
        grad_copy(k).wait()
    for i in range(2):
        g_middle(i)
    mid_sum(1, 1)
    out_step(0, 0, near)
    mid_sum(2, 1)
    out_step(1, 1, far)
    out_step(2, 1, near)
    last_sum(0)
    for i in range(2):
        remote(xg.at[i], xg.at[i], g_send.at[1, i], g_recv.at[1, i], to_x).wait_recv()
        remote(yg.at[i], yg.at[i], g_send.at[1, i], g_recv.at[2, i], to_y).wait_recv()
        xg[i] = (
            gout[g_rows(d, i)].astype(f32) + xg[i].astype(f32) + yg[i].astype(f32)
        ).astype(bf)
    out_first_copy = pltpu.make_async_copy(xg, gout_first_hbm, own_sem.at[7])
    out_first_copy.start()
    for copy in rest:
        copy.wait()
    for k in range(3):
        out_copy(k, 1, 0).wait()
    last_sum(1)
    in_copy.wait()
    out_first_copy.wait()
    for s in range(2):
        dx_copy(s).wait()

    for i in range(2):
        for copy in (g_diag(i), g_direct(i), g_summed(i)):
            copy.wait_send()
    for p in range(4):
        for copy in (i_diag(p), i_direct(p), i_summed(p)):
            copy.wait_send()
    for h in range(2):
        for kind in range(2):
            for p in range(2):
                for row in range(2):
                    w_copy(h, kind, p, d, to_x, row).wait_send()
    for s in range(2):
        for zp in range(4):
            for a in range(2):
                sib_copy(a, zp, s).wait_send()
                sib_sum(zp, s, a).wait_send()

                @pl.when((zp <= z) & (z < 3))
                def _():
                    ag_copy(a, zp, s, 0).wait_send()

                @pl.when((zp >= z) & (z > 0))
                def _():
                    ag_copy(a, zp, s, 1).wait_send()

        for i in range(3):
            for copy in hop(i, s, to_in, True):
                copy.wait_send()


def expert_stage(rows, grads, gates_t, w_in, w_out):
    bf, f32 = jnp.bfloat16, jnp.float32
    shape = jax.ShapeDtypeStruct
    width = rows.shape[-1]
    hbm = pl.BlockSpec(memory_space=pltpu.HBM)
    vmem = pl.BlockSpec(memory_space=pltpu.VMEM)
    dma = pltpu.SemaphoreType.DMA
    return pl.pallas_call(
        expert_kernel,
        out_shape=(
            shape((8, 128, width // 4), f32),
            shape((2, 8, 128), f32),
            shape((8, 2, 128, width), bf),
            shape((4, 384, FF), bf),
            shape((4, PIECE, width), bf),
            shape((2, 48, width), bf),
            shape((4, PIECE, FF), bf),
        ),
        in_specs=[hbm] * 5,
        out_specs=(hbm, vmem, hbm, hbm, hbm, hbm, hbm),
        scratch_shapes=[
            pltpu.VMEM((4, width // 4, 2 * FF), bf),
            pltpu.VMEM((FF, width), bf),
            pltpu.VMEM((8, 2, 128, width), bf),
            pltpu.VMEM((8, 2, 128, width), bf),
            pltpu.VMEM((8, 2, 8, 128), f32),
            pltpu.VMEM((8, 2, 128, 2 * FF), bf),
            pltpu.VMEM((8, 2, 128, FF), bf),
            pltpu.VMEM((8, 2, 128, width), bf),
            pltpu.VMEM((8, 2, 8, 128), f32),
            pltpu.VMEM((4, 2, 128, width), bf),
            pltpu.VMEM((4, 2, 8, 128), f32),
            pltpu.VMEM((3, 2, 128, width), bf),
            pltpu.VMEM((3, 2, 8, 128), f32),
            pltpu.VMEM((3, 2, 128, width), bf),
            pltpu.VMEM((3, 2, 8, 128), f32),
            pltpu.VMEM((FF, width), bf),
            *([pltpu.VMEM((2, 48, width), bf)] * 3),
            pltpu.VMEM((width, FF), bf),
            *([pltpu.VMEM((4, PIECE, FF), bf)] * 3),
            pltpu.VMEM((8, 128, width // 4), f32),
            dma((9,)),
            dma((3,)),
            dma((4,)),
            dma((3, 2)),
            dma((3, 2)),
            dma((3, 4)),
            dma((3, 4)),
            dma((3, 2, 2, 2)),
            dma((3, 2, 2, 2)),
            dma((2, 4, 2)),
            dma((2, 2, 4, 2)),
            dma((2, 4, 2)),
            dma((2, 4, 2)),
            dma((6, 4, 2)),
            dma((4, 4, 2)),
        ],
        compiler_params=pltpu.CompilerParams(
            collective_id=1, has_side_effects=True, vmem_limit_bytes=63 * 2**20
        ),
        name="expert_stage",
    )(
        rows.reshape(2, 128, width),
        grads.reshape(8, 2, 128, width),
        gates_t,
        w_in,
        w_out,
    )


def backward_kernel(
    dx_hbm,
    dgt_ref,
    gates_ref,
    mixed_hbm,
    cot_hbm,
    tok_hbm,
    q_hbm,
    kv_hbm,
    att_hbm,
    lens_ref,
    rope_hbm,
    wa_hbm,
    wb_hbm,
    gin_hbm,
    gout_hbm,
    outp_hbm,
    block_hbm,
    dtok_hbm,
    gq_out,
    gb_out,
    gkv_out,
    small_out,
    ein_out,
    eout_out,
    osib,
    oro,
    ori,
    wide,
    small,
    gq,
    gb,
    gk,
    sib_q,
    sib_b,
    sib_k,
    tq,
    xq,
    yq,
    roq,
    riq,
    tb,
    xb,
    yb,
    rob,
    rib,
    tw,
    xw,
    yw,
    row_,
    riw,
    te,
    xe,
    ye,
    le,
    lf,
    td,
    xd,
    yd,
    ld,
    old,
    oslot,
    dat,
    dkv,
    tk,
    xk,
    yk,
    rope,
    cot_ref,
    tok_ref,
    q_ref,
    kv_ref,
    att_ref,
    mixed_ref,
    block_out,
    dtok_out,
    load_sem,
    le_sem,
    old_sem,
    os_recv,
    os_send,
    ds_recv,
    ds_send,
    t_recv,
    x_recv,
    y_recv,
    t_send,
    d_send,
    s_send,
    ro_recv,
    ri_recv,
    hop_send,
):
    bf, f32 = jnp.bfloat16, jnp.float32
    d, e, z, c, x, y = place()
    d_x = d + 1 - 2 * x
    d_y = d + 2 - 4 * y
    d_d = 3 - d
    hi = lax.div(z, 2)
    zz = z * hi + (3 - z) * (1 - hi)
    other = 1 - c
    mid = zz == 2
    end = zz == 3
    to_x = (d_x, e)
    to_y = (d_y, e)
    to_sib = (d, 2 * z + other)
    e_in = e + 2 - 4 * hi
    to_in = (d, e_in)
    to_out = (d, jnp.where(zz == 2, e - 2 + 4 * hi, e_in))

    dqs = block_out
    dmix = dtok_out
    dx_ref = dtok_out

    first_loads = [
        pltpu.make_async_copy(
            dx_hbm.at[4 * s + j],
            dx_ref.at[pl.ds(s * 128, 128), pl.ds(j * 384, 384)],
            load_sem.at[13 + 4 * s + j],
        )
        for s in range(2)
        for j in range(4)
    ] + [
        pltpu.make_async_copy(mixed_hbm, mixed_ref, load_sem.at[10]),
    ]
    for load in first_loads:
        load.start()

    barrier = pltpu.get_barrier_semaphore()
    for target in (to_x, to_y, to_sib, to_in):
        pl.semaphore_signal(barrier, inc=1, device_id=target, device_id_type=MESH)

    @pl.when(mid)
    def _():
        pl.semaphore_signal(barrier, inc=1, device_id=to_out, device_id_type=MESH)

    pl.semaphore_wait(barrier, 7 - zz)

    def order(i):
        v = i if i < 2 else (5 - zz if i == 2 else zz)
        return v * hi + (3 - v) * (1 - hi)

    def across(k, src, t, fx, fy, ways=(0, 1, 0, 1)):
        def diag(i):
            return remote(
                src(d_d, i), t.at[i], t_send.at[k, i], t_recv.at[k, i], (to_x, to_y)[ways[i]]
            )

        def direct(i):
            if ways[i] == 0:
                return remote(src(d_x, i), fx.at[i], d_send.at[k, i], x_recv.at[k, i], to_x)
            return remote(src(d_y, i), fy.at[i], d_send.at[k, i], y_recv.at[k, i], to_y)

        def summed(i, ref):
            if ways[i] == 0:
                return remote(ref, fy.at[i], s_send.at[k, i], y_recv.at[k, i], to_y)
            return remote(ref, fx.at[i], s_send.at[k, i], x_recv.at[k, i], to_x)

        def wait_t(i):
            remote(t.at[i], t.at[i], t_send.at[k, i], t_recv.at[k, i], to_x).wait_recv()

        def wait_xy(i):
            remote(fx.at[i], fx.at[i], d_send.at[k, i], x_recv.at[k, i], to_x).wait_recv()
            remote(fy.at[i], fy.at[i], d_send.at[k, i], y_recv.at[k, i], to_y).wait_recv()

        def drain(n):
            for i in range(n):
                diag(i).wait_send()
                direct(i).wait_send()
                summed(i, t.at[i]).wait_send()

        return diag, direct, summed, wait_t, wait_xy, drain

    def along(k, slot, ro, ri):
        def send(i, target, dst, recv):
            return remote(slot(i), dst.at[i], hop_send.at[k, i], recv.at[k, i], target)

        def to_ro(i):
            return send(i, to_in, ro, ro_recv)

        def to_ri(i):
            return send(i, to_in if i < 2 else to_out, ri, ri_recv)

        def wait_ro(i):
            remote(ro.at[i], ro.at[i], hop_send.at[k, i], ro_recv.at[k, i], to_in).wait_recv()

        def wait_ri(i):
            remote(ri.at[i], ri.at[i], hop_send.at[k, i], ri_recv.at[k, i], to_in).wait_recv()

        def drain():
            for i in range(3):
                to_ro(i).wait_send()

        return to_ro, to_ri, wait_ro, wait_ri, drain

    expert_ways = (0, 1, 0, 0)

    def expert_src(dd, p):
        return gin_hbm.at[pl.ds(pl.multiple_of(dd * 384 + p * PIECE, 16), PIECE)]

    e_diag, e_direct, e_summed, e_wait_t, e_wait_xy, e_drain = across(
        0, expert_src, te, xe, ye, expert_ways
    )

    def e_sent_to(p):
        return d_y if expert_ways[p] == 0 else d_x

    e_loads = [
        pltpu.make_async_copy(expert_src(e_sent_to(p), p), le.at[p], le_sem.at[p])
        for p in range(4)
    ]
    e_own = pltpu.make_async_copy(
        gin_hbm.at[pl.ds(pl.multiple_of(d * 384, 16), 384)], lf, le_sem.at[4]
    )

    def e_middle(p):
        e_wait_t(p)
        e_loads[p].wait()
        te[p] = (te[p].astype(f32) + le[p].astype(f32)).astype(bf)
        e_summed(p, te.at[p]).start()

    def e_final(p):
        e_wait_xy(p)
        rows = slice(p * PIECE, (p + 1) * PIECE)
        total = lf[rows].astype(f32) + xe[p].astype(f32) + ye[p].astype(f32)
        ein_out[rows] = total.astype(bf)

    def d_src(dd):
        return gout_hbm.at[dd]

    def d_diag():
        return remote(d_src(d_d), td, t_send.at[5, 0], t_recv.at[5, 0], to_y)

    def d_direct():
        return remote(d_src(d_y), yd, d_send.at[5, 0], y_recv.at[5, 0], to_y)

    def d_summed():
        return remote(td, xd, s_send.at[5, 0], x_recv.at[5, 0], to_x)

    d_loads = [
        pltpu.make_async_copy(d_src(dd), ld.at[j], le_sem.at[5 + j])
        for j, dd in enumerate((d_x, d))
    ]

    def d_middle():
        d_diag().wait_recv()
        d_loads[0].wait()
        td[...] = (td[...].astype(f32) + ld[0].astype(f32)).astype(bf)
        d_summed().start()

    def d_final():
        d_summed().wait_recv()
        d_direct().wait_recv()
        eout_out[...] = (
            ld[1].astype(f32) + xd[...].astype(f32) + yd[...].astype(f32)
        ).astype(bf)

    def store_q(total):
        gq_out[...] = total

    def store_b(total):
        gb_out[...] = total

    def store_k(total):
        gkv_out[...] = total[:, :512]
        small_out[...] = lax.dot_general(
            eye[:16],
            total[:, 512:],
            (((1,), (1,)), ((), ())),
            preferred_element_type=f32,
            precision=highest,
        )

    dense = (
        (gq, sib_q, tq, xq, yq, roq, riq, store_q),
        (gb, sib_b, tb, xb, yb, rob, rib, store_b),
        (gk, sib_k, tw, xw, yw, row_, riw, store_k),
    )

    def dense_stream(j):
        grad, sib, t, fx, fy, ro, ri, out = dense[j]

        def src(dd, i):
            return grad.at[dd * 4 + order(i), c]

        diag, direct, summed, wait_t, wait_xy, drain = across(1 + j, src, t, fx, fy)

        def own_slot(i):
            return grad.at[d * 4 + order(i), c]

        to_ro, to_ri, wait_ro, wait_ri, drain_z = along(j, own_slot, ro, ri)

        def sib_copy():
            return remote(grad.at[:, other], sib, ds_send.at[j], ds_recv.at[j], to_sib)

        def begin():
            sib_copy().wait_recv()

            @pl.loop(0, 16)
            def _(k):
                grad[k, c] = (grad[k, c].astype(f32) + sib[k].astype(f32)).astype(bf)

            for i in range(4):
                diag(i).start()
            for i in range(4):
                direct(i).start()

        def middle(i):
            dd = d_y if i % 2 == 0 else d_x
            wait_t(i)
            at = dd * 4 + order(i)
            grad[at, c] = (grad[at, c].astype(f32) + t[i].astype(f32)).astype(bf)
            summed(i, src(dd, i)).start()

        def local(i):
            return grad[d * 4 + order(i), c].astype(f32) + fx[i].astype(f32) + fy[i].astype(f32)

        def put(i, total):
            grad[d * 4 + order(i), c] = total.astype(bf)

        def last(i):
            wait_xy(i)
            if i == 3:
                return

            @pl.when(end)
            def _():
                put(i, local(i))
                to_ro(i).start()

        def hop(i):
            @pl.when(mid)
            def _():
                if i < 2:
                    wait_ro(i)
                    put(i, local(i) + ro[i].astype(f32))
                else:
                    wait_ri(0)
                    put(2, local(2) + ri[0].astype(f32))
                to_ri(i).start()

        def finish():
            @pl.when(mid)
            def _():
                wait_ro(2)
                wait_ri(1)
                out(local(3) + ro[2].astype(f32) + ri[1].astype(f32))

            @pl.when(end)
            def _():
                wait_ri(2)
                out(local(3) + ri[2].astype(f32))

        def drain_all():
            sib_copy().wait_send()
            drain(4)
            drain_z()

        return sib_copy, begin, middle, last, hop, finish, drain_all

    q_sib, q_begin, q_middle, q_last, q_hop, q_finish, q_drain = dense_stream(0)
    b_sib, b_begin, b_middle, b_last, b_hop, b_finish, b_drain = dense_stream(1)
    w_sib, w_begin, w_middle, w_last, w_hop, w_finish, w_drain = dense_stream(2)

    def out_rows(i, lane):
        return outp_hbm.at[pl.ds(pl.multiple_of((2 * order(i) + lane) * CHUNK, CHUNK), CHUNK)]

    def out_sib(i):
        return remote(out_rows(i, other), osib.at[i], os_send.at[i], os_recv.at[i], to_sib)

    o_ro, o_ri, o_wait_ro, o_wait_ri, _ = along(3, lambda i: oslot.at[i % 2], oro, ori)

    def out_sum(i, incoming, store):
        out_sib(i).wait_recv()
        for half in range(2):
            rows = pl.ds(half * 128, 128)
            loads = [
                pltpu.make_async_copy(ref.at[rows], old.at[j], old_sem.at[j])
                for j, ref in enumerate([out_rows(i, c), osib.at[i]] + incoming)
            ]
            for load in loads:
                load.start()
            for load in loads:
                load.wait()
            total = old[0].astype(f32)
            for j in range(1, len(loads)):
                total = total + old[j].astype(f32)
            store(slice(half * 128, (half + 1) * 128), total)

    def out_slot(i):
        def store(rows, total):
            oslot[i % 2, rows] = total.astype(bf)

        return store

    def out_end(i):
        @pl.when(end)
        def _():
            if i == 2:
                o_ro(0).wait_send()
            out_sum(i, [], out_slot(i))
            o_ro(i).start()

    def out_mid(i):
        @pl.when(mid)
        def _():
            if i < 2:
                o_wait_ro(i)
                out_sum(i, [oro.at[i]], out_slot(i))
            else:
                o_ri(0).wait_send()
                o_wait_ri(0)
                out_sum(2, [ori.at[0]], out_slot(2))
            o_ri(i).start()

    def out_finish():
        def store(rows, total):
            total = total + mixed_ref[rows]
            slot = d * 128 + lax.broadcasted_iota(jnp.int32, (128, 1), 0)
            live = slot < lens_ref[rows.start // 128]
            block_out[rows] = jnp.where(live, total, 0.0).astype(bf)

        @pl.when(mid)
        def _():
            o_wait_ro(2)
            o_wait_ri(1)
            out_sum(3, [oro.at[2], ori.at[1]], store)

        @pl.when(end)
        def _():
            o_wait_ri(2)
            out_sum(3, [ori.at[2]], store)

    def kv_src(dd, i):
        return dkv.at[dd, pl.ds(i * 128, 128)]

    k_diag, k_direct, k_summed, k_wait_t, k_wait_xy, k_drain = across(4, kv_src, tk, xk, yk)

    def k_middle(i):
        dd = d_y if i % 2 == 0 else d_x
        k_wait_t(i)
        rows = slice(i * 128, (i + 1) * 128)
        dkv[dd, rows] = (dkv[dd, rows].astype(f32) + tk[i].astype(f32)).astype(bf)
        k_summed(i, kv_src(dd, i)).start()

    small_load = pltpu.make_async_copy(wa_hbm.at[:, pl.ds(2048, 128)], small, load_sem.at[0])
    wb_load = pltpu.make_async_copy(wb_hbm, wide.at[:, pl.ds(0, 1536)], load_sem.at[1])
    wa_load = pltpu.make_async_copy(wa_hbm.at[:, pl.ds(0, 2048)], wide, load_sem.at[2])
    rope_load = pltpu.make_async_copy(
        rope_hbm.at[:, pl.ds(pl.multiple_of(d * 128, 128), 128)], rope, load_sem.at[3]
    )
    small_load.start()
    loads = [
        pltpu.make_async_copy(src, dst, load_sem.at[4 + j])
        for j, (src, dst) in enumerate(
            (
                (cot_hbm, cot_ref),
                (att_hbm, att_ref),
                (q_hbm, q_ref),
                (kv_hbm, kv_ref),
                (tok_hbm, tok_ref),
            )
        )
    ]
    for load in loads[:2]:
        load.start()
    wb_load.start()
    rope_load.start()
    for load in loads[2:] + e_loads + [e_own] + d_loads:
        load.start()
    for p in range(4):
        e_diag(p).start()
    for p in (0, 1):
        e_direct(p).start()
    d_diag().start()
    for i in range(4):
        out_sib(i).start()
    out_end(0)

    nt = (((1,), (1,)), ((), ()))
    tn = (((0,), (0,)), ((), ()))

    def dot_nt(a, b):
        return lax.dot_general(a, b, nt, preferred_element_type=f32)

    def dot_tn(a, b):
        return lax.dot_general(a, b, tn, preferred_element_type=f32)

    eye = (
        lax.broadcasted_iota(jnp.int32, (128, 128), 0)
        == lax.broadcasted_iota(jnp.int32, (128, 128), 1)
    ).astype(f32)
    eye_low = eye.astype(bf)
    gates = jnp.concatenate([gates_ref[s] for s in range(2)], axis=1)
    dgate = jnp.concatenate([dgt_ref[s] for s in range(2)], axis=1)
    dlogit = gates * (dgate - jnp.sum(gates * dgate, axis=0, keepdims=True))
    dl_hi = dlogit.astype(bf).astype(f32)
    dl = jnp.concatenate([dl_hi, dlogit - dl_hi], axis=0).astype(bf)
    small_load.wait()
    small_t = dot_nt(eye_low[:16], small[...])
    router = jnp.concatenate([small_t[:8]] * 2, axis=0).astype(bf)
    for load in first_loads:
        load.wait()
    dn2 = dx_ref[...] + dot_tn(dl, router)
    mixed = mixed_ref[...]
    inv2 = lax.rsqrt(jnp.mean(mixed * mixed, axis=1, keepdims=True) + epsilon)
    n2 = mixed * inv2
    normed2 = (n2 * small_t[9:10]).astype(bf)
    router_sum = jnp.dot(dl, normed2, preferred_element_type=f32)
    router_sum = router_sum[:8] + router_sum[8:]
    mid_sum = jnp.sum(dn2 * n2, axis=0, keepdims=True)
    loads[0].wait()
    loads[1].wait()
    grads = [
        jnp.where(
            d * 128 + lax.broadcasted_iota(jnp.int32, (128, 1), 0) < lens_ref[s],
            cot_ref[s * 128 : (s + 1) * 128].astype(f32),
            0.0,
        )
        for s in range(2)
    ]
    u = dn2 * small_t[9:10]
    dmixed = jnp.concatenate(grads, axis=0) + inv2 * (u - n2 * jnp.mean(u * n2, axis=1, keepdims=True))
    dmix[...] = dmixed
    dproj = dmixed.astype(bf)
    for r in range(4):
        part = dot_tn(att_ref[:, r * 384 : (r + 1) * 384], dproj)
        gb[4 * r : 4 * r + 4] = part.astype(bf).reshape(4, 2, 48, 1536)
    b_sib().start()
    wb_load.wait()
    datt = dot_nt(dproj, wide[:, :1536]).astype(bf)
    for head in range(QUERY_HEADS):
        for s in range(2):
            at = (s * QUERY_HEADS + head) * 128
            dat[at : at + 128] = datt[s * 128 : (s + 1) * 128, head * 128 : (head + 1) * 128]
    wa_load.start()
    b_begin()
    out_end(1)

    query_pos = d * 128 + lax.broadcasted_iota(jnp.int32, (128, 512), 0)
    key_pos = lax.broadcasted_iota(jnp.int32, (128, 512), 1)
    rope_load.wait()
    for load in loads[2:]:
        load.wait()
    cos_rows = rope[0]
    sin_rows = rope[1]
    scale = HEAD_SIZE ** (-0.5)

    def unrotate_rows(v, cos, sin):
        return v * cos - pltpu.roll(v, 64, 1) * sin

    def attend(n):
        s = lax.div(n, 2)
        h = lax.rem(n, 2)
        srow = pl.ds(pl.multiple_of(s * 128, 128), 128)
        kcol = pl.ds(pl.multiple_of(h * 128, 128), 128)
        vcol = pl.ds(pl.multiple_of(256 + h * 128, 128), 128)
        lens = lens_ref[s]
        allowed = (key_pos <= query_pos) & (key_pos < lens)
        ks = kv_ref[:, srow, kcol].reshape(512, 128)
        vs = kv_ref[:, srow, vcol].reshape(512, 128)
        dk = None
        dv = None
        for half in range(2):
            rows = pl.ds(pl.multiple_of(n * 768 + half * 384, 128), 384)
            qh = q_ref[rows]
            dh = dat[rows]
            scores = dot_nt(qh, ks).reshape(3, 128, 512) * scale
            scores = jnp.where(allowed[None], scores, -1e30)
            probs = jnp.exp(scores - jnp.max(scores, axis=-1, keepdims=True))
            probs = probs * (1.0 / jnp.sum(probs, axis=-1, keepdims=True))
            dprobs = dot_nt(dh, vs).reshape(3, 128, 512)
            delta = jnp.sum(probs * dprobs, axis=-1, keepdims=True)
            dscores = (probs * (dprobs - delta)).astype(bf).reshape(384, 512)
            low = probs.astype(bf).reshape(384, 512)
            dq = jnp.dot(dscores, ks, preferred_element_type=f32) * scale
            for j in range(3):
                dqs[srow, pl.ds(pl.multiple_of(h * 768 + (half * 3 + j) * 128, 128), 128)] = (
                    unrotate_rows(dq[j * 128 : (j + 1) * 128], cos_rows, sin_rows).astype(bf)
                )
            dk_part = dot_tn(dscores, qh)
            dv_part = dot_tn(low, dh)
            dk = dk_part if dk is None else dk + dk_part
            dv = dv_part if dv is None else dv + dv_part
        dkv[:, srow, kcol] = (dk * scale).astype(bf).reshape(4, 128, 128)
        dkv[:, srow, vcol] = dv.astype(bf).reshape(4, 128, 128)

    pl.loop(0, 2)(attend)
    for i in range(4):
        b_middle(i)
    e_middle(1)
    e_middle(0)
    out_mid(0)
    pl.loop(2, 4)(attend)
    for i in range(2):
        k_diag(i).start()
    for i in range(2):
        k_direct(i).start()
    for i in range(4):
        b_last(i)
    out_end(2)

    tok = tok_ref[...].astype(f32)
    inv1 = lax.rsqrt(jnp.mean(tok * tok, axis=1, keepdims=True) + epsilon)
    n1 = tok * inv1
    normed = (n1 * small_t[8:9]).astype(bf)
    for r in range(4):
        part = dot_tn(normed[:, r * 384 : (r + 1) * 384], dqs[...])
        gq[4 * r : 4 * r + 4] = part.astype(bf).reshape(4, 2, 48, 1536)
    q_sib().start()
    k_middle(0)
    k_middle(1)
    q_begin()
    wa_load.wait()
    dn1 = dot_nt(dqs[...], wide[:, :1536])

    for i in range(2):
        k_wait_xy(i)
    own = jnp.concatenate(
        [
            dkv[d, i * 128 : (i + 1) * 128].astype(f32) + xk[i].astype(f32) + yk[i].astype(f32)
            for i in range(2)
        ],
        axis=0,
    )
    cos_two = jnp.concatenate([cos_rows] * 2, axis=0)
    sin_two = jnp.concatenate([sin_rows] * 2, axis=0)
    dkv_own = jnp.concatenate(
        [
            unrotate_rows(own[:, h * 128 : (h + 1) * 128], cos_two, sin_two)
            for h in range(2)
        ]
        + [own[:, 256:]],
        axis=1,
    ).astype(bf)
    dn1 = dn1 + dot_nt(dkv_own, wide[:, 1536:])
    pre_sum = jnp.sum(dn1 * n1, axis=0, keepdims=True)
    row8 = lax.broadcasted_iota(jnp.int32, (8, 1536), 0)
    gains = jnp.where(row8 == 0, pre_sum, jnp.where(row8 == 1, mid_sum, 0.0))
    smalls = jnp.concatenate([router_sum, gains], axis=0).astype(bf)
    for r in range(4):
        cols = slice(r * 384, (r + 1) * 384)
        part = dot_tn(normed[:, cols], dkv_own)
        gk[4 * r : 4 * r + 4, :, :, :512] = part.astype(bf).reshape(4, 2, 48, 512)
        part = dot_tn(smalls[:, cols], eye_low[:16])
        gk[4 * r : 4 * r + 4, :, :, 512:] = part.astype(bf).reshape(4, 2, 48, 128)
    w_sib().start()
    u = dn1 * small_t[8:9]
    dtok_copy = pltpu.make_async_copy(dtok_out, dtok_hbm, load_sem.at[11])
    dtok_out[...] = dmix[...] + inv1 * (u - n1 * jnp.mean(u * n1, axis=1, keepdims=True))

    dtok_copy.start()

    for i in range(4):
        q_middle(i)
    w_begin()
    e_direct(2).start()
    b_hop(0)
    b_hop(1)
    out_mid(1)
    out_mid(2)
    for i in range(4):
        q_last(i)
    for i in range(4):
        w_middle(i)
    d_direct().start()
    d_middle()
    e_direct(3).start()
    for p in (2, 3):
        e_middle(p)
    b_hop(2)
    q_hop(0)
    q_hop(1)
    out_finish()
    block_copy = pltpu.make_async_copy(block_out, block_hbm, load_sem.at[12])
    block_copy.start()
    for i in range(4):
        w_last(i)
    w_hop(0)
    q_hop(2)
    w_hop(1)
    w_hop(2)
    b_finish()
    q_finish()
    e_own.wait()
    d_loads[1].wait()
    for p in range(4):
        e_final(p)
    d_final()
    w_finish()
    dtok_copy.wait()
    block_copy.wait()

    e_drain(4)
    for copy in (d_diag(), d_direct(), d_summed()):
        copy.wait_send()
    k_drain(2)
    q_drain()
    b_drain()
    w_drain()
    for i in range(1, 3):
        o_ro(i).wait_send()
    for i in range(4):
        out_sib(i).wait_send()


def backward_stage(dx, dgt, gates, mixed, cot, tok, q, kv, att, lens, rope, wa, wb, gin, gout, outp):
    bf, f32 = jnp.bfloat16, jnp.float32
    shape = jax.ShapeDtypeStruct
    width = tok.shape[-1]
    hbm = pl.BlockSpec(memory_space=pltpu.HBM)
    vmem = pl.BlockSpec(memory_space=pltpu.VMEM)
    smem = pl.BlockSpec(memory_space=pltpu.SMEM)
    dma = pltpu.SemaphoreType.DMA
    widths = (width, width, 640)
    dense = []
    for w in widths:
        dense += [pltpu.VMEM((4, 48, w), bf)] * 3 + [pltpu.VMEM((3, 48, w), bf)] * 2
    return pl.pallas_call(
        backward_kernel,
        out_shape=(
            shape((CHUNK, width), bf),
            shape((CHUNK, width), f32),
            shape((48, width), f32),
            shape((48, width), f32),
            shape((48, 512), f32),
            shape((16, 48), f32),
            shape((384, FF), bf),
            shape((PIECE, width), bf),
            shape((4, CHUNK, width), bf),
            shape((3, CHUNK, width), bf),
            shape((3, CHUNK, width), bf),
        ),
        in_specs=[hbm, vmem, vmem] + [hbm] * 6 + [smem] + [hbm] * 6,
        out_specs=[hbm] * 2 + [vmem] * 6 + [hbm] * 3,
        scratch_shapes=[
            pltpu.VMEM((width, 2048), bf),
            pltpu.VMEM((width, 128), bf),
            *[pltpu.VMEM((16, 2, 48, w), bf) for w in widths],
            *[pltpu.VMEM((16, 48, w), bf) for w in widths],
            *dense,
            *([pltpu.VMEM((4, PIECE, FF), bf)] * 3),
            pltpu.VMEM((4, PIECE, FF), bf),
            pltpu.VMEM((4 * PIECE, FF), bf),
            *([pltpu.VMEM((PIECE, width), bf)] * 3),
            pltpu.VMEM((2, PIECE, width), bf),
            pltpu.VMEM((4, 128, width), bf),
            pltpu.VMEM((2, CHUNK, width), bf),
            pltpu.VMEM((2 * QUERY_HEADS * 128, 128), bf),
            pltpu.VMEM((4, CHUNK, 512), bf),
            *([pltpu.VMEM((2, 128, 512), bf)] * 3),
            pltpu.VMEM((2, 128, 128), f32),
            *[pltpu.VMEM(ref.shape, ref.dtype) for ref in (cot, tok, q, kv, att, mixed)],
            pltpu.VMEM((CHUNK, width), bf),
            pltpu.VMEM((CHUNK, width), f32),
            dma((21,)),
            dma((7,)),
            dma((4,)),
            dma((4,)),
            dma((4,)),
            dma((3,)),
            dma((3,)),
            dma((6, 4)),
            dma((6, 4)),
            dma((6, 4)),
            dma((6, 4)),
            dma((6, 4)),
            dma((6, 4)),
            dma((4, 3)),
            dma((4, 3)),
            dma((4, 3)),
        ],
        compiler_params=pltpu.CompilerParams(
            collective_id=3, has_side_effects=True, vmem_limit_bytes=64 * 2**20 - 65536
        ),
        name="backward_stage",
    )(dx, dgt, gates, mixed, cot, tok, q, kv, att, lens, rope, wa, wb, gin, gout, outp)


def finish_kernel(
    block_in,
    dtok_in,
    gq_in,
    gb_in,
    gkv_in,
    small_ref,
    first_ref,
    second_ref,
    down_first_ref,
    down_second_ref,
    block_out,
    dtok_out,
    gq_out,
    gb_out,
    gkv_out,
    pre_out,
    mid_out,
    router_out,
    in_out,
    down_out,
):
    f32 = jnp.float32
    i = pl.program_id(0)
    block_out[...] = block_in[...]
    dtok_out[...] = dtok_in[...]
    gq_out[...] = gq_in[...]
    gb_out[...] = gb_in[...]
    gkv_out[...] = gkv_in[...]
    half = FF // 2
    first = first_ref[...].astype(f32)
    second = second_ref[...].astype(f32)
    in_out[:, :half] = first[:, :half]
    in_out[:, half:FF] = second[:, :half]
    in_out[:, FF : FF + half] = first[:, half:]
    in_out[:, FF + half :] = second[:, half:]
    down_out[...] = jnp.where(i < 2, down_first_ref[...], down_second_ref[...]).astype(f32)
    router_out[...] = small_ref[:8]
    pre_out[...] = small_ref[8:9]
    mid_out[...] = small_ref[9:10]


def finish_stage(block, dtok, gq, gb, gkv, small, first, second, down_first, down_second):
    f32 = jnp.float32
    shape = jax.ShapeDtypeStruct
    width = block.shape[-1]

    def rows(count, columns, index):
        return pl.BlockSpec((count, columns), index)

    def whole(count, columns):
        return pl.BlockSpec((count, columns), lambda i: (0, 0))

    return pl.pallas_call(
        finish_kernel,
        grid=(4,),
        out_shape=(
            shape(block.shape, block.dtype),
            shape(dtok.shape, f32),
            shape(gq.shape, f32),
            shape(gb.shape, f32),
            shape(gkv.shape, f32),
            shape((1, 48), f32),
            shape((1, 48), f32),
            shape((8, 48), f32),
            shape((384, 2 * FF), f32),
            shape((192, width), f32),
        ),
        in_specs=[
            rows(64, width, lambda i: (i, 0)),
            rows(64, width, lambda i: (i, 0)),
            whole(48, width),
            whole(48, width),
            whole(48, 512),
            whole(16, 48),
            rows(96, FF, lambda i: (i, 0)),
            rows(96, FF, lambda i: (i, 0)),
            rows(48, width, lambda i: (jnp.minimum(i, 1), 0)),
            rows(48, width, lambda i: (jnp.maximum(i - 2, 0), 0)),
        ],
        out_specs=[
            rows(64, width, lambda i: (i, 0)),
            rows(64, width, lambda i: (i, 0)),
            whole(48, width),
            whole(48, width),
            whole(48, 512),
            whole(1, 48),
            whole(1, 48),
            whole(8, 48),
            rows(96, 2 * FF, lambda i: (i, 0)),
            rows(48, width, lambda i: (i, 0)),
        ],
        name="finish_stage",
    )(block, dtok, gq, gb, gkv, small, first, second, down_first, down_second)


def rope_constant(slots):
    half = HEAD_SIZE // 2
    inv_freq = np.float32(rope_base) ** (-(np.arange(half, dtype=np.float32) * 2.0 / HEAD_SIZE))
    angles = np.arange(slots, dtype=np.float32)[:, None] * inv_freq[None, :].astype(np.float32)
    cos, sin = np.cos(angles), np.sin(angles)
    return np.stack(
        [np.concatenate([cos, cos], axis=1), np.concatenate([-sin, sin], axis=1)]
    ).astype(np.float32)


def fast_local(
    tokens,
    lengths,
    routes,
    prenorm,
    w_query,
    key_value_weight,
    w_output,
    midnorm,
    w_router,
    expert_in,
    expert_out,
    cotangent,
):
    seqs, token_rows, width = tokens.shape
    rows = seqs * token_rows
    tok = tokens.reshape(rows, width)
    cot = cotangent.reshape(rows, width)
    rope = jnp.asarray(rope_constant(token_rows * lax.axis_size("dp")))
    full_a, full_b, full_out, gall, q_rot, kv_all, attended, mixed, normed2, gates = attention_stage(
        tok,
        w_query,
        key_value_weight,
        w_router.T,
        prenorm[None],
        midnorm[None],
        w_output,
        cot,
        expert_out[0],
        rope,
        lengths,
        jnp.transpose(routes, (0, 2, 1)),
    )
    dx, dgate, outp, gin, gout, out_first, g_first = expert_stage(normed2, gall, gates, expert_in[0], full_out)
    block_out, grad_tokens, g_query, g_b, g_kv, small, g_second, out_second = backward_stage(
        dx, dgate, gates, mixed, cot, tok, q_rot, kv_all, attended, lengths, rope,
        full_a, full_b, gin.reshape(width, FF), gout, outp.reshape(8 * rows, width),
    )[:8]
    block_out, grad_tokens, g_query, g_b, g_kv, g_pre, g_mid, g_router, g_in, g_out = finish_stage(
        block_out,
        grad_tokens,
        g_query,
        g_b,
        g_kv,
        small,
        g_first.reshape(width // 4, FF),
        g_second,
        out_first.reshape(FF // 8, width),
        out_second,
    )
    return (
        block_out.reshape(seqs, token_rows, width),
        grad_tokens.reshape(seqs, token_rows, width),
        g_pre.reshape(-1),
        g_query,
        g_kv,
        g_b,
        g_mid.reshape(-1),
        g_router.T,
        g_in[None],
        g_out[None],
    )


def solution(mesh):
    placed = (
        P("expert", "dp", None),
        P("expert"),
        P("expert", "dp", None),
        P(("dp", "expert")),
        P(("dp", "expert"), None),
        P(("dp", "expert"), None),
        P(("dp", "expert"), None),
        P(("dp", "expert")),
        P(("dp", "expert"), None),
        P("expert", "dp", None),
        P("expert", "dp", None),
        P("expert", "dp", None),
    )
    fits = mesh.shape["dp"] == 4 and mesh.shape["expert"] == 8
    return jax.shard_map(
        fast_local if fits else local,
        mesh=mesh,
        in_specs=placed,
        out_specs=(
            P("expert", "dp", None),
            P("expert", "dp", None),
            P(("dp", "expert")),
            P(("dp", "expert"), None),
            P(("dp", "expert"), None),
            P(("dp", "expert"), None),
            P(("dp", "expert")),
            P(("dp", "expert"), None),
            P("expert", "dp", None),
            P("expert", "dp", None),
        ),
        check_vma=False,
    )
```

```python
import jax
import jax.numpy as jnp
import numpy as np
from jax import lax
from jax.experimental import pallas as pl
from jax.experimental.pallas import tpu as pltpu
from jax.sharding import PartitionSpec as P

QUERY_HEADS = 12
KEY_VALUE_HEADS = 2
HEAD_SIZE = 128
FF = 768
TOP = 4


epsilon = 1e-06
rope_base = 10000.0
highest = lax.Precision.HIGHEST


def rope_tables(positions):
    half_width = HEAD_SIZE // 2
    inv_freq = rope_base ** (-(jnp.arange(half_width, dtype=jnp.float32) * 2.0 / HEAD_SIZE))
    angles = positions.astype(jnp.float32)[:, None] * inv_freq[None, :]
    return (jnp.cos(angles), jnp.sin(angles))


def apply_rotation(values, cosine_table, sine_table):
    half_width = values.shape[-1] // 2
    first_half = values[..., :half_width]
    second = values[..., half_width:]
    cos_rows = cosine_table[:, None, :]
    sin_rows = sine_table[:, None, :]
    return jnp.concatenate(
        [first_half * cos_rows - second * sin_rows, second * cos_rows + first_half * sin_rows],
        axis=-1,
    )


def unrotate(values, cosine_table, sine_table):
    half_width = values.shape[-1] // 2
    first_half = values[..., :half_width]
    second = values[..., half_width:]
    cos_rows = cosine_table[:, None, :]
    sin_rows = sine_table[:, None, :]
    return jnp.concatenate(
        [first_half * cos_rows + second * sin_rows, second * cos_rows - first_half * sin_rows],
        axis=-1,
    )


def rms_parts(values):
    inverse = lax.rsqrt(jnp.mean(values * values, axis=-1, keepdims=True) + epsilon)
    return (values * inverse, inverse)


def norm_back(grad_normed, normalized_input, inverse, gain):
    scaled = grad_normed * gain
    return inverse * (
        scaled - normalized_input * jnp.mean(scaled * normalized_input, axis=-1, keepdims=True)
    )


def slot_index(route_rows, expert_count, capacity):
    flat_routes = route_rows.reshape(-1)
    onehot = (flat_routes[:, None] == jnp.arange(expert_count, dtype=jnp.int32)[None, :]).astype(
        jnp.int32
    )
    before = jnp.cumsum(onehot, axis=0) - onehot
    within = jnp.sum(before * onehot, axis=-1)
    return flat_routes * capacity + within


def masked_scores(query_matrix, key_rows, allowed):
    scores = jnp.einsum(
        "qhgd,khd->hgqk", query_matrix, key_rows, preferred_element_type=jnp.float32
    ) * HEAD_SIZE ** (-0.5)
    return jnp.where(allowed[None, None], scores, -1e30)


def local(
    tokens,
    lengths,
    routes,
    prenorm,
    w_query,
    key_value_weight,
    w_output,
    midnorm,
    w_router,
    expert_in,
    expert_out,
    cotangent,
):
    micro_count, token_rows, hidden_width = tokens.shape
    dp_size = lax.axis_size("dp")
    expert_size = lax.axis_size("expert")
    dp_rank = lax.axis_index("dp")
    local_experts = expert_in.shape[0]
    expert_count = local_experts * expert_size
    capacity = max(2, 3 * token_rows * TOP // (2 * expert_count))
    query_group_width = QUERY_HEADS // KEY_VALUE_HEADS
    expert_slot_total = token_rows * dp_size
    score_scale = HEAD_SIZE ** (-0.5)
    positions = dp_rank * token_rows + jnp.arange(token_rows, dtype=jnp.int32)
    key_pos = jnp.arange(expert_slot_total, dtype=jnp.int32)
    cosine_table, sine_table = rope_tables(positions)
    total_prenorm = jnp.zeros((hidden_width,), jnp.float32)
    total_query = jnp.zeros((hidden_width, QUERY_HEADS * HEAD_SIZE), jnp.float32)
    total_key_value = jnp.zeros((hidden_width, 2 * KEY_VALUE_HEADS * HEAD_SIZE), jnp.float32)
    total_output = jnp.zeros((QUERY_HEADS * HEAD_SIZE, hidden_width), jnp.float32)
    total_midnorm = jnp.zeros((hidden_width,), jnp.float32)
    total_router = jnp.zeros((hidden_width, expert_count), jnp.float32)
    total_upper = jnp.zeros((local_experts, hidden_width, 2 * FF), jnp.float32)
    total_down = jnp.zeros((local_experts, FF, hidden_width), jnp.float32)
    outputs_list = []
    grads_list = []
    for micro_step in range(micro_count):
        dense_all = (
            lax.all_gather(prenorm, ("dp", "expert"), axis=0, tiled=True),
            lax.all_gather(w_query, ("dp", "expert"), axis=0, tiled=True),
            lax.all_gather(key_value_weight, ("dp", "expert"), axis=0, tiled=True),
            lax.all_gather(w_output, ("dp", "expert"), axis=0, tiled=True),
            lax.all_gather(midnorm, ("dp", "expert"), axis=0, tiled=True),
            lax.all_gather(w_router, ("dp", "expert"), axis=0, tiled=True),
        )
        expert_all = (
            lax.all_gather(expert_in, "dp", axis=1, tiled=True),
            lax.all_gather(expert_out, "dp", axis=1, tiled=True),
        )
        gain_one = dense_all[0].astype(jnp.float32)
        query_all = dense_all[1]
        keyval_all = dense_all[2]
        output_all = dense_all[3]
        gain_two = dense_all[4].astype(jnp.float32)
        router_all = dense_all[5]
        gateup_all = expert_all[0]
        down_all = expert_all[1]
        input_rows = tokens[micro_step].astype(jnp.float32)
        length = lengths[micro_step]
        route_rows = routes[micro_step]
        live_rows = (positions < length)[:, None]
        normed_one, inverse_one = rms_parts(input_rows)
        normalized_input = (normed_one * gain_one).astype(jnp.bfloat16)
        query_pre = jnp.dot(
            normalized_input, query_all, preferred_element_type=jnp.float32
        ).reshape(token_rows, QUERY_HEADS, HEAD_SIZE)
        keyval_pre = jnp.dot(
            normalized_input, keyval_all, preferred_element_type=jnp.float32
        ).reshape(token_rows, 2, KEY_VALUE_HEADS, HEAD_SIZE)
        query_matrix = (
            apply_rotation(query_pre, cosine_table, sine_table)
            .astype(jnp.bfloat16)
            .reshape(token_rows, KEY_VALUE_HEADS, query_group_width, HEAD_SIZE)
        )
        local_key_rows = apply_rotation(keyval_pre[:, 0], cosine_table, sine_table).astype(
            jnp.bfloat16
        )
        local_value_rows = keyval_pre[:, 1].astype(jnp.bfloat16)
        packed_tokens = jnp.stack([local_key_rows, local_value_rows], axis=1).reshape(
            token_rows, 2 * KEY_VALUE_HEADS * HEAD_SIZE
        )
        gathered_rows = lax.all_gather(packed_tokens, "dp", axis=0, tiled=True).reshape(
            expert_slot_total, 2, KEY_VALUE_HEADS, HEAD_SIZE
        )
        key_rows = gathered_rows[:, 0]
        value_rows = gathered_rows[:, 1]
        allowed = (key_pos[None, :] <= positions[:, None]) & (key_pos[None, :] < length)
        scores = masked_scores(query_matrix, key_rows, allowed)
        top_score = jnp.max(scores, axis=-1, keepdims=True)
        weights = jnp.exp(scores - top_score)
        weight_total = jnp.sum(weights, axis=-1, keepdims=True)
        log_total = top_score + jnp.log(weight_total)
        probs_low = (weights / weight_total).astype(jnp.bfloat16)
        attended = jnp.einsum(
            "hgqk,khd->qhgd", probs_low, value_rows, preferred_element_type=jnp.float32
        )
        attended = attended.reshape(token_rows, QUERY_HEADS * HEAD_SIZE).astype(jnp.bfloat16)
        mixed_rows = input_rows + jnp.dot(attended, output_all, preferred_element_type=jnp.float32)
        normed_mid, inverse_two = rms_parts(mixed_rows)
        normed_two = (normed_mid * gain_two).astype(jnp.bfloat16)
        logits = jnp.dot(normed_two, router_all, preferred_element_type=jnp.float32)
        onehot = (
            route_rows[:, :, None] == jnp.arange(expert_count, dtype=jnp.int32)[None, None, :]
        ).astype(jnp.float32)
        chosen = jnp.sum(onehot * logits[:, None, :], axis=-1)
        gate_values = jax.nn.softmax(chosen, axis=-1)
        slot_idx = slot_index(route_rows, expert_count, capacity)
        send_rows = jnp.zeros((expert_count * capacity, hidden_width), jnp.bfloat16)
        send_rows = send_rows.at[slot_idx].set(jnp.repeat(normed_two, TOP, axis=0))
        received = lax.all_to_all(
            send_rows.reshape(expert_count, capacity, hidden_width),
            "expert",
            split_axis=0,
            concat_axis=0,
            tiled=True,
        )
        item_count = received.shape[1]
        grouped = received.reshape(expert_size, local_experts, item_count, hidden_width)
        gate_up = jnp.einsum(
            "slcd,ldf->slcf", grouped, gateup_all, preferred_element_type=jnp.float32
        )
        hidden = (jax.nn.silu(gate_up[..., :FF]) * gate_up[..., FF:]).astype(jnp.bfloat16)
        result = jnp.einsum(
            "slcf,lfd->slcd", hidden, down_all, preferred_element_type=jnp.float32
        ).astype(jnp.bfloat16)
        back_rows = lax.all_to_all(
            result.reshape(expert_count, item_count, hidden_width),
            "expert",
            split_axis=0,
            concat_axis=0,
            tiled=True,
        )
        back_rows, kept_rows, kept_gateup = (
            back_rows,
            received,
            gate_up.reshape(expert_count, item_count, 2 * FF),
        )
        returned = back_rows.reshape(expert_count * capacity, hidden_width)[slot_idx].reshape(
            token_rows, TOP, hidden_width
        )
        returned_wide = returned.astype(jnp.float32)
        expert_sum = jnp.sum(gate_values[:, :, None] * returned_wide, axis=1)
        final_rows = jnp.where(live_rows, mixed_rows + expert_sum, 0.0)
        outputs_list.append(final_rows.astype(jnp.bfloat16))
        grad_rows = jnp.where(live_rows, cotangent[micro_step].astype(jnp.float32), 0.0)
        grad_gate = jnp.sum(grad_rows[:, None, :] * returned_wide, axis=-1)
        grad_chosen = gate_values * (
            grad_gate - jnp.sum(gate_values * grad_gate, axis=-1, keepdims=True)
        )
        grad_logits = jnp.sum(onehot * grad_chosen[:, :, None], axis=1)
        router_term = jnp.dot(normed_two.astype(jnp.float32).T, grad_logits, precision=highest)
        grad_normtwo = jnp.dot(grad_logits, router_all.astype(jnp.float32).T, precision=highest)
        grad_result = (
            (gate_values[:, :, None] * grad_rows[:, None, :])
            .astype(jnp.bfloat16)
            .reshape(token_rows * TOP, hidden_width)
        )
        send_grads = (
            jnp.zeros((expert_count * capacity, hidden_width), jnp.bfloat16)
            .at[slot_idx]
            .set(grad_result)
        )
        recv_grads, again_rows = (
            lax.all_to_all(
                send_grads.reshape(expert_count, capacity, hidden_width),
                "expert",
                split_axis=0,
                concat_axis=0,
                tiled=True,
            ),
            lax.all_to_all(
                send_rows.reshape(expert_count, capacity, hidden_width),
                "expert",
                split_axis=0,
                concat_axis=0,
                tiled=True,
            ),
        )
        grouped_rows = again_rows.reshape(expert_size, local_experts, capacity, hidden_width)
        gate_up = jnp.einsum(
            "slcd,ldf->slcf", grouped_rows, gateup_all, preferred_element_type=jnp.float32
        )
        grouped_grads = recv_grads.reshape(expert_size, local_experts, capacity, hidden_width)
        gate_part = gate_up[..., :FF]
        up_part = gate_up[..., FF:]
        sigmoid_gate = jax.nn.sigmoid(gate_part)
        silu_gate = gate_part * sigmoid_gate
        hidden = (silu_gate * up_part).astype(jnp.bfloat16)
        grad_hidden = jnp.einsum(
            "slcd,lfd->slcf", grouped_grads, down_all, preferred_element_type=jnp.float32
        )
        down_term = jnp.einsum(
            "slcf,slcd->lfd", hidden, grouped_grads, preferred_element_type=jnp.float32
        )
        grad_gatepart = (
            grad_hidden * up_part * sigmoid_gate * (1.0 + gate_part * (1.0 - sigmoid_gate))
        )
        grad_gateup = jnp.concatenate([grad_gatepart, grad_hidden * silu_gate], axis=-1).astype(
            jnp.bfloat16
        )
        upper_term = jnp.einsum(
            "slcd,slcf->ldf", grouped_rows, grad_gateup, preferred_element_type=jnp.float32
        )
        grad_copies = jnp.einsum(
            "slcf,ldf->slcd", grad_gateup, gateup_all, preferred_element_type=jnp.float32
        ).astype(jnp.bfloat16)
        back_grads = lax.all_to_all(
            grad_copies.reshape(expert_count, capacity, hidden_width),
            "expert",
            split_axis=0,
            concat_axis=0,
            tiled=True,
        )
        copy_rows = back_grads.reshape(expert_count * capacity, hidden_width)[slot_idx].reshape(
            token_rows, TOP, hidden_width
        )
        grad_normtwo = grad_normtwo + jnp.sum(copy_rows.astype(jnp.float32), axis=1)
        midnorm_term = jnp.sum(grad_normtwo * normed_mid, axis=0)
        grad_mixed = grad_rows + norm_back(grad_normtwo, normed_mid, inverse_two, gain_two)
        grad_proj = grad_mixed.astype(jnp.bfloat16)
        output_term = jnp.dot(attended.T, grad_proj, preferred_element_type=jnp.float32)
        attention_gradient = jnp.dot(
            grad_proj, output_all.T, preferred_element_type=jnp.float32
        ).astype(jnp.bfloat16)
        attention_gradient = attention_gradient.reshape(
            token_rows, KEY_VALUE_HEADS, query_group_width, HEAD_SIZE
        )
        scores = masked_scores(query_matrix, key_rows, allowed)
        prob_rows = jnp.exp(scores - log_total)
        grad_probs = jnp.einsum(
            "qhgd,khd->hgqk", attention_gradient, value_rows, preferred_element_type=jnp.float32
        )
        row_delta = jnp.sum(prob_rows * grad_probs, axis=-1, keepdims=True)
        grad_scores = (prob_rows * (grad_probs - row_delta)).astype(jnp.bfloat16)
        prob_low = prob_rows.astype(jnp.bfloat16)
        grad_qrot = (
            jnp.einsum("hgqk,khd->qhgd", grad_scores, key_rows, preferred_element_type=jnp.float32)
            * score_scale
        )
        grad_keys = (
            jnp.einsum(
                "hgqk,qhgd->khd", grad_scores, query_matrix, preferred_element_type=jnp.float32
            )
            * score_scale
        )
        grad_vals = jnp.einsum(
            "hgqk,qhgd->khd", prob_low, attention_gradient, preferred_element_type=jnp.float32
        )
        own_keys = (
            lax.psum_scatter(
                jnp.stack([grad_keys, grad_vals], axis=1)
                .reshape(lax.axis_size("dp") * token_rows, 2 * KEY_VALUE_HEADS * HEAD_SIZE)
                .astype(jnp.bfloat16),
                "dp",
                scatter_dimension=0,
                tiled=True,
            )
            .astype(jnp.float32)
            .reshape(token_rows, 2, KEY_VALUE_HEADS, HEAD_SIZE)
        )
        grad_query = (
            unrotate(
                grad_qrot.reshape(token_rows, QUERY_HEADS, HEAD_SIZE), cosine_table, sine_table
            )
            .astype(jnp.bfloat16)
            .reshape(token_rows, QUERY_HEADS * HEAD_SIZE)
        )
        key_gradient = unrotate(own_keys[:, 0], cosine_table, sine_table).astype(jnp.bfloat16)
        value_gradient = own_keys[:, 1].astype(jnp.bfloat16)
        key_value_weight_gradient = jnp.stack([key_gradient, value_gradient], axis=1).reshape(
            token_rows, 2 * KEY_VALUE_HEADS * HEAD_SIZE
        )
        query_term = jnp.dot(normalized_input.T, grad_query, preferred_element_type=jnp.float32)
        keyval_term = jnp.dot(
            normalized_input.T, key_value_weight_gradient, preferred_element_type=jnp.float32
        )
        grad_normone = jnp.dot(grad_query, query_all.T, preferred_element_type=jnp.float32)
        grad_normone = grad_normone + jnp.dot(
            key_value_weight_gradient, keyval_all.T, preferred_element_type=jnp.float32
        )
        prenorm_term = jnp.sum(grad_normone * normed_one, axis=0)
        grads_list.append(grad_mixed + norm_back(grad_normone, normed_one, inverse_one, gain_one))
        total_prenorm = total_prenorm + prenorm_term
        total_query = total_query + query_term
        total_key_value = total_key_value + keyval_term
        total_output = total_output + output_term
        total_midnorm = total_midnorm + midnorm_term
        total_router = total_router + router_term
        total_upper = total_upper + upper_term
        total_down = total_down + down_term
    dense_grads = (
        lax.psum_scatter(total_prenorm, ("dp", "expert"), scatter_dimension=0, tiled=True),
        lax.psum_scatter(total_query, ("dp", "expert"), scatter_dimension=0, tiled=True),
        lax.psum_scatter(total_key_value, ("dp", "expert"), scatter_dimension=0, tiled=True),
        lax.psum_scatter(total_output, ("dp", "expert"), scatter_dimension=0, tiled=True),
        lax.psum_scatter(total_midnorm, ("dp", "expert"), scatter_dimension=0, tiled=True),
        lax.psum_scatter(total_router, ("dp", "expert"), scatter_dimension=0, tiled=True),
    )
    expert_grads = (
        lax.psum_scatter(
            total_upper.astype(jnp.bfloat16), "dp", scatter_dimension=1, tiled=True
        ).astype(jnp.float32),
        lax.psum_scatter(
            total_down.astype(jnp.bfloat16), "dp", scatter_dimension=1, tiled=True
        ).astype(jnp.float32),
    )
    return (
        jnp.stack(outputs_list),
        jnp.stack(grads_list),
        dense_grads[0],
        dense_grads[1],
        dense_grads[2],
        dense_grads[3],
        dense_grads[4],
        dense_grads[5],
        expert_grads[0],
        expert_grads[1],
    )


MESH = pl.DeviceIdType.MESH
CHUNK = 256
PIECE = 96


def remote(src, dst, send_sem, recv_sem, target):
    return pltpu.make_async_remote_copy(
        src_ref=src,
        dst_ref=dst,
        send_sem=send_sem,
        recv_sem=recv_sem,
        device_id=target,
        device_id_type=MESH,
    )


def place():
    d = lax.axis_index("dp")
    e = lax.axis_index("expert")
    z = lax.div(e, 2)
    c = lax.rem(e, 2)
    x = lax.rem(d, 2)
    y = lax.div(d, 2)
    return d, e, z, c, x, y


def attention_kernel(
    tok_hbm,
    wq_hbm,
    wkv_hbm,
    wr_ref,
    pre_ref,
    mid_ref,
    wb_hbm,
    cot_hbm,
    wo_hbm,
    rope_hbm,
    lens_ref,
    routes_ref,
    wa_out,
    wb_out,
    wo_out,
    gall,
    q_out,
    kv_out,
    att_out,
    mixed_hbm,
    normed_hbm,
    gates_out,
    small_out,
    wa,
    wb,
    qs,
    kvs,
    att,
    g_own,
    rope,
    tok_ref,
    cot_ref,
    mixed_out,
    normed_out,
    own_sem,
    wo_recv,
    wo_send,
    z_recv,
    z_send,
    xy_recv,
    xy_send,
    sib_recv,
    sib_send,
    g_recv,
    g_send,
    gs_recv,
    gs_send,
    kv_recv,
    kv_send,
):
    bf, f32 = jnp.bfloat16, jnp.float32
    d, e, z, c, x, y = place()
    d_x = d + 1 - 2 * x
    d_y = d + 2 - 4 * y
    d_d = 3 - d
    other = 1 - c
    to_x = (d_x, e)
    to_y = (d_y, e)
    to_sib = (d, 2 * z + other)
    to_up = (d, e + jnp.where(z < 3, 2, -2))
    to_down = (d, e + jnp.where(z > 0, -2, 2))

    barrier = pltpu.get_barrier_semaphore()
    for target in (to_x, to_y, to_sib):
        pl.semaphore_signal(barrier, inc=1, device_id=target, device_id_type=MESH)

    @pl.when(z < 3)
    def _():
        pl.semaphore_signal(barrier, inc=1, device_id=to_up, device_id_type=MESH)

    @pl.when(z > 0)
    def _():
        pl.semaphore_signal(barrier, inc=1, device_id=to_down, device_id_type=MESH)

    own_at = pl.multiple_of((d * 8 + e) * 48, 16)
    own_rows = pl.ds(own_at, 48)
    own_a = [
        pltpu.make_async_copy(wq_hbm, wa.at[own_rows, pl.ds(0, 1536)], own_sem.at[0]),
        pltpu.make_async_copy(wkv_hbm, wa.at[own_rows, pl.ds(1536, 512)], own_sem.at[1]),
        pltpu.make_async_copy(rope_hbm.at[:, pl.ds(pl.multiple_of(d * 128, 128), 128)], rope, own_sem.at[2]),
    ]
    loads = [
        pltpu.make_async_copy(cot_hbm, cot_ref, own_sem.at[8]),
        pltpu.make_async_copy(tok_hbm, tok_ref, own_sem.at[9]),
    ]
    for copy in own_a + loads:
        copy.start()
    eye = lax.broadcasted_iota(jnp.int32, (128, 128), 0) == lax.broadcasted_iota(
        jnp.int32, (128, 128), 1
    )
    eye_low = eye.astype(bf)
    turned = (((0,), (0,)), ((), ()))
    sub = lax.broadcasted_iota(jnp.int32, (8, 48), 0)
    gains = jnp.where(
        sub == 0,
        pre_ref[...].astype(f32),
        jnp.where(sub == 1, mid_ref[...].astype(f32), 0.0),
    )
    tile = jnp.concatenate([wr_ref[...].astype(f32), gains], axis=0).astype(bf)
    wa[own_rows, 2048:] = lax.dot_general(
        tile, eye_low[:16], turned, preferred_element_type=f32
    ).astype(bf)
    full = (wa, wb)
    shard = (None, wb_hbm)

    def block(a, dd, zp, lane):
        at = pl.multiple_of((dd * 8 + 2 * zp + lane) * 48, 16)
        return full[a].at[pl.ds(at, 48)]

    def z_copy(a, zp, way, src=None):
        ref = block(a, d, zp, c)
        return remote(
            ref if src is None else src,
            ref,
            z_send.at[a, way, zp],
            z_recv.at[a, zp],
            to_up if way == 0 else to_down,
        )

    def xy_copy(a, dd, zp, row, target, src=None):
        ref = block(a, dd, zp, c)
        return remote(
            ref if src is None else src,
            ref,
            xy_send.at[a, row, zp],
            xy_recv.at[a, row, zp],
            target,
        )

    def s_copy(a, dd, zp, src=None, lane=None):
        ref = block(a, dd, zp, c if lane is None else lane)
        return remote(
            ref if src is None else src,
            ref,
            sib_send.at[a, dd, zp],
            sib_recv.at[a, dd, zp],
            to_sib,
        )

    def send_xy(a, zp):
        xy_copy(a, d, zp, 0, to_x).start()
        xy_copy(a, d, zp, 1, to_y).start()

    def own_start(a):
        @pl.when(z < 3)
        def _():
            z_copy(a, z, 0, shard[a]).start()

        @pl.when(z > 0)
        def _():
            z_copy(a, z, 1, shard[a]).start()

        s_copy(a, d, z, shard[a]).start()

    def from_z(a, k):
        def arrived(zp, way):
            z_copy(a, zp, way).wait_recv()

            @pl.when((z < 3) if way == 0 else (z > 0))
            def _():
                z_copy(a, zp, way).start()

            if a == 0:
                send_xy(a, zp)
            s_copy(a, d, zp).start()

        @pl.when(z - k >= 0)
        def _():
            arrived(z - k, 0)

        @pl.when(z + k <= 3)
        def _():
            arrived(z + k, 1)

    def from_xy_one(a, zp):
        xy_copy(a, d_x, zp, 0, to_x).wait_recv()

        @pl.when(lax.rem(zp, 2) == 0)
        def _():
            xy_copy(a, d_x, zp, 2, to_y).start()

        s_copy(a, d_x, zp).start()
        xy_copy(a, d_y, zp, 1, to_y).wait_recv()

        @pl.when(lax.rem(zp, 2) == 1)
        def _():
            xy_copy(a, d_y, zp, 2, to_x).start()

        s_copy(a, d_y, zp).start()

    def from_xy(a, k):
        @pl.when(z - k >= 0)
        def _():
            from_xy_one(a, z - k)

        if k > 0:

            @pl.when(z + k <= 3)
            def _():
                from_xy_one(a, z + k)

    def from_diag(a):
        for k in range(4):
            zp = lax.rem(z + k, 4)
            xy_copy(a, d_d, zp, 2, to_x).wait_recv()
            s_copy(a, d_d, zp).start()

    def from_sib(a):
        for dd in range(4):
            for zp in range(4):
                s_copy(a, dd, zp, lane=other).wait_recv()

    def drain(a):
        for zp in range(4):
            for dd in range(4):
                s_copy(a, dd, zp).wait_send()
            for row in range(3):
                xy_copy(a, d, zp, row, to_x).wait_send()

            @pl.when((zp <= z) & (z < 3))
            def _():
                z_copy(a, zp, 0).wait_send()

            @pl.when((zp >= z) & (z > 0))
            def _():
                z_copy(a, zp, 1).wait_send()

    def g_part(zp, lane, s):
        at = pl.multiple_of((2 * zp + lane) * CHUNK + s * 128, 128)
        return gall.at[pl.ds(at, 128)]

    def g_copy(zp, s, way, src=None):
        ref = g_part(zp, c, s)
        return remote(
            ref if src is None else src,
            ref,
            g_send.at[way, zp, s],
            g_recv.at[zp, s],
            to_up if way == 0 else to_down,
        )

    def gs_copy(zp, s, src=None, lane=None):
        ref = g_part(zp, c if lane is None else lane, s)
        return remote(
            ref if src is None else src, ref, gs_send.at[zp, s], gs_recv.at[zp, s], to_sib
        )

    def g_start():
        for s in range(2):
            src = g_own.at[pl.ds(s * 128, 128)]

            @pl.when(z < 3)
            def _():
                g_copy(z, s, 0, src).start()

            @pl.when(z > 0)
            def _():
                g_copy(z, s, 1, src).start()

            gs_copy(z, s, src).start()

    def g_pass(k, s):
        @pl.when(z - k >= 0)
        def _():
            g_copy(z - k, s, 0).wait_recv()

            @pl.when(z < 3)
            def _():
                g_copy(z - k, s, 0).start()

            gs_copy(z - k, s).start()

        @pl.when(z + k <= 3)
        def _():
            g_copy(z + k, s, 1).wait_recv()

            @pl.when(z > 0)
            def _():
                g_copy(z + k, s, 1).start()

            gs_copy(z + k, s).start()

    def wo_copy(dd, p, row, target, src=None):
        ref = wo_out.at[pl.ds(pl.multiple_of(dd * 192 + p * PIECE, 16), PIECE)]
        return remote(
            ref if src is None else src, ref, wo_send.at[row, p], wo_recv.at[row, p], target
        )

    def wo_start(p):
        wo_copy(d, p, 0, to_x, wo_hbm.at[pl.ds(p * PIECE, PIECE)]).start()
        wo_copy(d, 1 - p, 1, to_y, wo_hbm.at[pl.ds((1 - p) * PIECE, PIECE)]).start()

    def wo_pass():
        wo_copy(d_x, 0, 0, to_x).wait_recv()
        wo_copy(d_x, 0, 2, to_y).start()
        wo_copy(d_y, 1, 1, to_y).wait_recv()
        wo_copy(d_y, 1, 2, to_x).start()

    def wo_rest():
        wo_copy(d_x, 1, 0, to_x).wait_recv()
        wo_copy(d_y, 0, 1, to_y).wait_recv()
        for p in range(2):
            wo_copy(d_d, p, 2, to_x).wait_recv()

    pl.semaphore_wait(barrier, 5 - jnp.where((z == 0) | (z == 3), 1, 0))
    for copy in own_a:
        copy.wait()
    own_start(0)
    own_start(1)
    own = [
        pltpu.make_async_copy(wb_hbm, block(1, d, z, c), own_sem.at[0]),
        pltpu.make_async_copy(
            g_own, gall.at[pl.ds(pl.multiple_of(e * CHUNK, CHUNK), CHUNK)], own_sem.at[1]
        ),
        pltpu.make_async_copy(
            wo_hbm, wo_out.at[pl.ds(pl.multiple_of(d * 192, 16), 192)], own_sem.at[2]
        ),
    ]
    own[0].start()
    own[2].start()
    send_xy(0, z)
    own[0].wait()
    at_end = (z == 0) | (z == 3)

    @pl.when(at_end)
    def _():
        send_xy(1, z)

    loads[0].wait()
    for s in range(2):
        rows = slice(s * 128, (s + 1) * 128)
        slot = d * 128 + lax.broadcasted_iota(jnp.int32, (128, 1), 0)
        g_own[rows] = jnp.where(slot < lens_ref[s], cot_ref[rows].astype(f32), 0.0).astype(bf)

    own[1].start()
    loads[1].wait()
    tok = tok_ref[...].astype(f32)
    n1 = tok * lax.rsqrt(jnp.mean(tok * tok, axis=1, keepdims=True) + epsilon)
    from_z(0, 1)
    from_z(1, 1)
    from_xy(0, 0)
    from_z(0, 2)
    from_z(1, 2)
    g_start()
    from_xy(0, 1)
    from_z(0, 3)
    from_z(1, 3)
    from_xy(0, 2)
    from_xy(0, 3)

    def turn(j):
        return lax.rem(z + j, 4)

    @pl.when(jnp.logical_not(at_end))
    def _():
        send_xy(1, z)

    send_xy(1, turn(1))
    from_diag(0)
    from_sib(0)

    small_t = lax.dot_general(
        eye_low[:16], wa[:, 2048:], (((1,), (1,)), ((), ())), preferred_element_type=f32
    )
    small_out[...] = small_t
    normed = (n1 * small_t[8:9]).astype(bf)
    cos_rows = jnp.concatenate([rope[0]] * 2, axis=0)
    sin_rows = jnp.concatenate([rope[1]] * 2, axis=0)

    def rotate(v):
        return v * cos_rows + pltpu.roll(v, 64, 1) * sin_rows

    kv = jnp.dot(normed, wa[:, 1536:2048], preferred_element_type=f32)
    for h in range(2):
        kvs[d, :, h * 128 : (h + 1) * 128] = rotate(kv[:, h * 128 : (h + 1) * 128]).astype(bf)
    kvs[d, :, 256:] = kv[:, 256:].astype(bf)

    def kv_copy(dd, s, row, target):
        ref = kvs.at[dd, pl.ds(s * 128, 128)]
        return remote(ref, ref, kv_send.at[row, s], kv_recv.at[row, s], target)

    for s in range(2):
        kv_copy(d, s, 0, to_x).start()
        kv_copy(d, 1 - s, 1, to_y).start()
    send_xy(1, turn(2))
    g_pass(1, 0)
    q = jnp.dot(normed, wa[:, :1536], preferred_element_type=f32)
    for head in range(QUERY_HEADS):
        rot = rotate(q[:, head * 128 : (head + 1) * 128]).astype(bf)
        for s in range(2):
            at = (s * QUERY_HEADS + head) * 128
            qs[at : at + 128] = rot[s * 128 : (s + 1) * 128]
    kv_copy(d_x, 0, 0, to_x).wait_recv()
    kv_copy(d_x, 0, 2, to_y).start()
    kv_copy(d_y, 1, 1, to_y).wait_recv()
    kv_copy(d_y, 1, 2, to_x).start()
    send_xy(1, turn(3))
    for j in range(2):
        from_xy_one(1, turn(j))
    g_pass(1, 1)
    kv_copy(d_y, 0, 1, to_y).wait_recv()
    kv_copy(d_x, 1, 0, to_x).wait_recv()
    for s in range(2):
        kv_copy(d_d, s, 2, to_x).wait_recv()
    q_copy = pltpu.make_async_copy(qs, q_out, own_sem.at[3])
    kvo_copy = pltpu.make_async_copy(kvs, kv_out, own_sem.at[4])
    wa_copy = pltpu.make_async_copy(wa, wa_out, own_sem.at[5])
    for copy in (q_copy, kvo_copy, wa_copy):
        copy.start()

    query_pos = d * 128 + lax.broadcasted_iota(jnp.int32, (128, 512), 0)
    key_pos = lax.broadcasted_iota(jnp.int32, (128, 512), 1)

    def attend(n):
        s = lax.div(n, 2)
        h = lax.rem(n, 2)
        lens = lens_ref[s]
        allowed = (key_pos <= query_pos) & (key_pos < lens)
        ks = kvs[:, pl.ds(pl.multiple_of(s * 128, 128), 128), pl.ds(pl.multiple_of(h * 128, 128), 128)]
        vs = kvs[:, pl.ds(pl.multiple_of(s * 128, 128), 128), pl.ds(pl.multiple_of(256 + h * 128, 128), 128)]
        ks = ks.reshape(512, 128)
        vs = vs.reshape(512, 128)
        for half in range(2):
            qh = qs[pl.ds(pl.multiple_of(n * 768 + half * 384, 128), 384)]
            scores = lax.dot_general(qh, ks, (((1,), (1,)), ((), ())), preferred_element_type=f32)
            scores = scores.reshape(3, 128, 512) * HEAD_SIZE ** (-0.5)
            scores = jnp.where(allowed[None], scores, -1e30)
            top = jnp.max(scores, axis=-1, keepdims=True)
            weights = jnp.exp(scores - top)
            weights = weights * (1.0 / jnp.sum(weights, axis=-1, keepdims=True))
            out = jnp.dot(
                weights.astype(bf).reshape(384, 512), vs, preferred_element_type=f32
            ).astype(bf)
            for j in range(3):
                att[
                    pl.ds(pl.multiple_of(s * 128, 128), 128),
                    pl.ds(pl.multiple_of(h * 768 + (half * 3 + j) * 128, 128), 128),
                ] = out[j * 128 : (j + 1) * 128]

    wo_start(0)
    g_pass(2, 0)
    pl.loop(0, 2)(attend)
    from_xy_one(1, turn(2))
    from_xy_one(1, turn(3))
    wo_start(1)
    g_pass(2, 1)

    @pl.loop(2, 4)
    def _(n):
        attend(n)
        pl.when(n == 2)(wo_pass)

    from_diag(1)
    from_sib(1)
    att_copy = pltpu.make_async_copy(att, att_out, own_sem.at[6])
    wb_copy = pltpu.make_async_copy(wb, wb_out, own_sem.at[7])
    att_copy.start()
    wb_copy.start()
    mixed = tok_ref[...].astype(f32) + jnp.dot(att[...], wb[...], preferred_element_type=f32)
    mixed_out[...] = mixed
    mixed_copy = pltpu.make_async_copy(mixed_out, mixed_hbm, own_sem.at[10])
    mixed_copy.start()
    n2 = mixed * lax.rsqrt(jnp.mean(mixed * mixed, axis=1, keepdims=True) + epsilon)
    normed2 = (n2 * small_t[9:10]).astype(bf)
    normed_out[...] = normed2
    normed_copy = pltpu.make_async_copy(normed_out, normed_hbm, own_sem.at[11])
    normed_copy.start()
    logits = lax.dot_general(
        small_t[:8].astype(bf), normed2, (((1,), (1,)), ((), ())), preferred_element_type=f32
    )
    number = lax.broadcasted_iota(jnp.int32, (8, 128), 0)
    for s in range(2):
        chosen = number == routes_ref[s, 0:1]
        for t in range(1, TOP):
            chosen = chosen | (number == routes_ref[s, t : t + 1])
        picked = jnp.where(chosen, logits[:, s * 128 : (s + 1) * 128], -1e30)
        top = jnp.max(picked, axis=0, keepdims=True)
        weights = jnp.where(chosen, jnp.exp(picked - top), 0.0)
        gates_out[s] = weights / jnp.sum(weights, axis=0, keepdims=True)

    g_pass(3, 0)
    g_pass(3, 1)
    wo_rest()
    for zp in range(4):
        for s in range(2):
            gs_copy(zp, s, lane=other).wait_recv()
    own[1].wait()
    own[2].wait()
    for copy in (q_copy, kvo_copy, wa_copy, att_copy, wb_copy, mixed_copy, normed_copy):
        copy.wait()
    drain(0)
    drain(1)
    for s in range(2):
        for row in range(3):
            kv_copy(d, s, row, to_x).wait_send()
            wo_copy(d, s, row, to_x).wait_send()
        for zp in range(4):
            gs_copy(zp, s).wait_send()

            @pl.when((zp <= z) & (z < 3))
            def _():
                g_copy(zp, s, 0).wait_send()

            @pl.when((zp >= z) & (z > 0))
            def _():
                g_copy(zp, s, 1).wait_send()


def attention_stage(tok, wq, wkv, wr, pre, mid, wb, cot, wo, rope, lens, routes):
    bf, f32 = jnp.bfloat16, jnp.float32
    shape = jax.ShapeDtypeStruct
    width = tok.shape[-1]
    wide = wq.shape[-1] + wkv.shape[-1] + 128
    hbm = pl.BlockSpec(memory_space=pltpu.HBM)
    vmem = pl.BlockSpec(memory_space=pltpu.VMEM)
    smem = pl.BlockSpec(memory_space=pltpu.SMEM)
    dma = pltpu.SemaphoreType.DMA
    return pl.pallas_call(
        attention_kernel,
        out_shape=(
            shape((width, wide), bf),
            shape((width, width), bf),
            shape((FF, width), bf),
            shape((8 * CHUNK, width), bf),
            shape((2 * QUERY_HEADS * 128, 128), bf),
            shape((4, CHUNK, 512), bf),
            shape((CHUNK, width), bf),
            shape((CHUNK, width), f32),
            shape((CHUNK, width), bf),
            shape((2, 8, 128), f32),
            shape((16, width), f32),
        ),
        in_specs=[hbm, hbm, hbm, vmem, vmem, vmem, hbm, hbm, hbm, hbm, smem, vmem],
        out_specs=[hbm] * 9 + [vmem] * 2,
        scratch_shapes=[
            pltpu.VMEM((width, wide), bf),
            pltpu.VMEM((width, width), bf),
            pltpu.VMEM((2 * QUERY_HEADS * 128, 128), bf),
            pltpu.VMEM((4, CHUNK, 512), bf),
            pltpu.VMEM((CHUNK, width), bf),
            pltpu.VMEM((CHUNK, width), bf),
            pltpu.VMEM((2, 128, 128), f32),
            pltpu.VMEM((CHUNK, width), bf),
            pltpu.VMEM((CHUNK, width), bf),
            pltpu.VMEM((CHUNK, width), f32),
            pltpu.VMEM((CHUNK, width), bf),
            dma((12,)),
            dma((3, 2)),
            dma((3, 2)),
            dma((2, 4)),
            dma((2, 2, 4)),
            dma((2, 3, 4)),
            dma((2, 3, 4)),
            dma((2, 4, 4)),
            dma((2, 4, 4)),
            dma((4, 2)),
            dma((2, 4, 2)),
            dma((4, 2)),
            dma((4, 2)),
            dma((3, 2)),
            dma((3, 2)),
        ],
        compiler_params=pltpu.CompilerParams(
            collective_id=2, has_side_effects=True, vmem_limit_bytes=60 * 2**20
        ),
        name="attention_stage",
    )(tok, wq, wkv, wr, pre, mid, wb, cot, wo, rope, lens, routes)


def expert_kernel(
    x_hbm,
    g_hbm,
    gt_hbm,
    win_hbm,
    wout_hbm,
    dx_hbm,
    dgt_out,
    outp_hbm,
    gin_hbm,
    gout_hbm,
    gout_first_hbm,
    gin_first_hbm,
    win,
    wout,
    xall,
    gall,
    gtall,
    dgu,
    hg,
    dxb,
    dgb,
    sibr,
    sibg,
    ro,
    rog,
    ri,
    rig,
    gout,
    tg,
    xg,
    yg,
    gin,
    ti,
    xi,
    yi,
    kept,
    own_sem,
    stage_sem,
    grad_sem,
    g_recv,
    g_send,
    i_recv,
    i_send,
    w_recv,
    w_send,
    ag_recv,
    ag_send,
    sib_recv,
    sib_send,
    red_recv,
    red_send,
    hop_recv,
    hop_send,
):
    bf, f32 = jnp.bfloat16, jnp.float32
    d, e, z, c, x, y = place()
    d_x = d + 1 - 2 * x
    d_y = d + 2 - 4 * y
    d_d = 3 - d
    hi = lax.div(z, 2)
    zz = z * hi + (3 - z) * (1 - hi)
    other = 1 - c
    to_x = (d_x, e)
    to_y = (d_y, e)
    to_sib = (d, 2 * z + other)
    to_up = (d, e + jnp.where(z < 3, 2, -2))
    to_down = (d, e + jnp.where(z > 0, -2, 2))
    e_in = e + 2 - 4 * hi
    to_in = (d, e_in)
    to_out = (d, jnp.where(zz == 2, e - 2 + 4 * hi, e_in))
    mid = zz == 2
    end = zz == 3

    barrier = pltpu.get_barrier_semaphore()
    for target in (to_x, to_y, to_sib, to_in):
        pl.semaphore_signal(barrier, inc=1, device_id=target, device_id_type=MESH)

    @pl.when(mid)
    def _():
        pl.semaphore_signal(barrier, inc=1, device_id=to_out, device_id_type=MESH)

    own_copies = [
        pltpu.make_async_copy(x_hbm.at[s], xall.at[e, s], own_sem.at[s]) for s in range(2)
    ] + [
        pltpu.make_async_copy(gt_hbm, gtall.at[e], own_sem.at[2]),
        pltpu.make_async_copy(wout_hbm, wout, own_sem.at[3]),
        pltpu.make_async_copy(g_hbm, gall, own_sem.at[4]),
    ]

    def w_columns(h, kind):
        return pl.ds(h * 768 + kind * 384, 384)

    for h in range(2):
        for kind in range(2):
            own_copies.append(
                pltpu.make_async_copy(
                    win_hbm.at[:, pl.ds(kind * 768 + h * 384, 384)],
                    win.at[d, :, w_columns(h, kind)],
                    own_sem.at[5 + 2 * h + kind],
                )
            )
    pl.semaphore_wait(barrier, 7 - zz)

    gathered = ((x_hbm, xall), (gt_hbm, gtall))

    def ag_copy(a, zp, s, way, src=None):
        ref = gathered[a][1].at[2 * zp + c, s]
        return remote(
            ref if src is None else src,
            ref,
            ag_send.at[way, a, zp, s],
            ag_recv.at[a, zp, s],
            to_up if way == 0 else to_down,
        )

    def sib_copy(a, zp, s, src=None, lane=None):
        ref = gathered[a][1].at[2 * zp + (c if lane is None else lane), s]
        return remote(
            ref if src is None else src,
            ref,
            sib_send.at[a, zp, s],
            sib_recv.at[a, zp, s],
            to_sib,
        )

    def own_rows(s):
        for a in range(2):
            src = gathered[a][0].at[s]

            @pl.when(z < 3)
            def _():
                ag_copy(a, z, s, 0, src).start()

            @pl.when(z > 0)
            def _():
                ag_copy(a, z, s, 1, src).start()

            sib_copy(a, z, s, src).start()

    def pass_on(k, s):
        for a in range(2):

            @pl.when(z - k >= 0)
            def _():
                ag_copy(a, z - k, s, 0).wait_recv()

                @pl.when(z < 3)
                def _():
                    ag_copy(a, z - k, s, 0).start()

                sib_copy(a, z - k, s).start()

            @pl.when(z + k <= 3)
            def _():
                ag_copy(a, z + k, s, 1).wait_recv()

                @pl.when(z > 0)
                def _():
                    ag_copy(a, z + k, s, 1).start()

                sib_copy(a, z + k, s).start()

    def from_sib(s, pairs):
        for a in range(2):
            for pair in pairs:
                for j in range(2):
                    sib_copy(a, 2 * pair + j, s, lane=other).wait_recv()

    def w_copy(h, kind, p, src_d, target, row, src=None):
        ref = win.at[src_d, pl.ds(p * 192, 192), w_columns(h, kind)]
        return remote(
            ref if src is None else src,
            ref,
            w_send.at[row, h, kind, p],
            w_recv.at[row, h, kind, p],
            target,
        )

    def w_start(h):
        for p in range(2):
            for kind in range(2):

                def src(q):
                    return win_hbm.at[
                        pl.ds(q * 192, 192), pl.ds(kind * 768 + h * 384, 384)
                    ]

                w_copy(h, kind, p, d, to_x, 0, src(p)).start()
                w_copy(h, kind, 1 - p, d, to_y, 1, src(1 - p)).start()

    def w_pass(h):
        for kind in range(2):
            w_copy(h, kind, 0, d_x, to_x, 0).wait_recv()
            w_copy(h, kind, 0, d_x, to_y, 2).start()
            w_copy(h, kind, 1, d_y, to_y, 1).wait_recv()
            w_copy(h, kind, 1, d_y, to_x, 2).start()

    def w_rest(h):
        for kind in range(2):
            w_copy(h, kind, 1, d_x, to_x, 0).wait_recv()
            w_copy(h, kind, 0, d_y, to_y, 1).wait_recv()
            for p in range(2):
                w_copy(h, kind, p, d_d, to_x, 2).wait_recv()

    own_rows(0)
    w_start(0)
    for copy in own_copies:
        copy.start()
    w_pass(0)
    w_start(1)
    pass_on(1, 0)
    pass_on(2, 0)
    own_rows(1)
    w_rest(0)
    w_pass(1)
    pass_on(3, 0)
    from_sib(0, (0, 1))
    for copy in own_copies:
        copy.wait()

    def order(i):
        v = i if i < 2 else (5 - zz if i == 2 else zz)
        return v * hi + (3 - v) * (1 - hi)

    def sib_sum(zp, s, a):
        src, dst = ((dxb, sibr), (dgb, sibg))[a]
        return remote(
            src.at[2 * zp + other, s], dst.at[zp, s], red_send.at[a, zp, s], red_recv.at[a, zp, s], to_sib
        )

    def hop(i, s, target, inward):
        dst, dstg, row = (ro, rog, 2) if inward else (ri, rig, 4)
        zp = order(i)
        halves = [
            remote(
                dxb.at[2 * zp + c, s, pl.ds(h * 64, 64)],
                dst.at[i, s, pl.ds(h * 64, 64)],
                hop_send.at[h, i, s],
                hop_recv.at[row // 2 - 1, h, i, s],
                target,
            )
            for h in range(2)
        ]
        last = remote(
            dgb.at[2 * zp + c, s],
            dstg.at[i, s],
            red_send.at[3, i, s],
            red_recv.at[row + 1, i, s],
            target,
        )
        return halves, last

    def wait_half(ref, slot, s, row, h):
        part = ref.at[slot, s, pl.ds(h * 64, 64)]
        remote(
            part, part, hop_send.at[h, slot, s], hop_recv.at[row // 2 - 1, h, slot, s], to_in
        ).wait_recv()

    def wait_last(refg, slot, s, row):
        remote(
            refg.at[slot, s],
            refg.at[slot, s],
            red_send.at[3, slot, s],
            red_recv.at[row + 1, slot, s],
            to_in,
        ).wait_recv()

    def wait_sib(zp, s):
        for a, ref in enumerate((sibr, sibg)):
            remote(
                ref.at[zp, s], ref.at[zp, s], red_send.at[a, zp, s], red_recv.at[a, zp, s], to_sib
            ).wait_recv()

    def half_sum(zp, s, incoming, h):
        rows = slice(h * 64, (h + 1) * 64)
        total = dxb[2 * zp + c, s, rows].astype(f32) + sibr[zp, s, rows].astype(f32)
        for ref, refg, slot, row in incoming:
            wait_half(ref, slot, s, row, h)
            total = total + ref[slot, s, rows].astype(f32)
        return total

    def gate_sum(zp, s, incoming):
        total = dgb[2 * zp + c, s] + sibg[zp, s]
        for ref, refg, slot, row in incoming:
            wait_last(refg, slot, s, row)
            total = total + refg[slot, s]
        return total

    def pass_sum(i, s, incoming, target, inward):
        zp = order(i)
        wait_sib(zp, s)
        halves, last = hop(i, s, target, inward)
        for h in range(2):
            dxb[2 * zp + c, s, h * 64 : (h + 1) * 64] = half_sum(zp, s, incoming, h).astype(bf)
            halves[h].start()
        dgb[2 * zp + c, s] = gate_sum(zp, s, incoming)
        last.start()

    def end_sums(s, which):
        @pl.when(end)
        def _():
            for i in which:
                pass_sum(i, s, (), to_in, True)

    def mid_sum(i, s):
        @pl.when(mid)
        def _():
            if i < 2:
                pass_sum(i, s, ((ro, rog, i, 2),), to_in, False)
            else:
                pass_sum(2, s, ((ri, rig, 0, 4),), to_out, False)

    def dx_copy(s):
        part = pl.ds(4 * s, 4)
        return pltpu.make_async_copy(kept.at[part], dx_hbm.at[part], own_sem.at[4 + s])

    def dx_store(s, incoming):
        zp = order(3)
        wait_sib(zp, s)
        for h in range(2):
            total = half_sum(zp, s, incoming, h)
            for j in range(4):
                kept[4 * s + j, h * 64 : (h + 1) * 64] = total[:, j * 384 : (j + 1) * 384]
        dgt_out[s] = gate_sum(zp, s, incoming)

    def last_sum(s):
        @pl.when(mid)
        def _():
            dx_store(s, ((ro, rog, 2, 2), (ri, rig, 1, 4)))

        @pl.when(end)
        def _():
            dx_store(s, ((ri, rig, 2, 4),))

        dx_copy(s).start()

    eye = lax.broadcasted_iota(jnp.int32, (128, 128), 0) == lax.broadcasted_iota(
        jnp.int32, (128, 128), 1
    )
    mine = lax.broadcasted_iota(jnp.int32, (8, 128), 0) == e
    nt = (((1,), (1,)), ((), ()))
    tn = (((0,), (0,)), ((), ()))

    def half_step(s, pair, h):
        first = 4 * pair
        block = pl.ds(first, 4)
        both = jnp.dot(
            xall[block, s].reshape(512, 1536),
            win[:, :, h * 768 : (h + 1) * 768].reshape(1536, 768),
            preferred_element_type=f32,
        )
        gate = both[:, :384]
        up = both[:, 384:]
        if h == 0:
            full = lax.dot_general(
                gall[block, s].reshape(512, 1536), wout[...], nt, preferred_element_type=f32
            )
            kept[block] = full[:, 384:].reshape(4, 128, 384)
            back = full[:, :384]
        else:
            back = kept[block].reshape(512, 384)
        columns = []
        for j in range(4):
            row = jnp.sum(jnp.where(mine, gtall[first + j, s], 0.0), axis=0, keepdims=True)
            columns.append(jnp.sum(jnp.where(eye, row, 0.0), axis=1, keepdims=True))
        weight = jnp.concatenate(columns, axis=0)
        sig = jax.nn.sigmoid(gate)
        silu = gate * sig
        hidden = (silu * up).astype(bf).astype(f32)
        dgate = jnp.sum(hidden * back, axis=1, keepdims=True)
        for j in range(4):
            row = jnp.sum(
                jnp.where(eye, dgate[j * 128 : (j + 1) * 128], 0.0), axis=0, keepdims=True
            )
            part = jnp.where(mine, row, 0.0)
            dgb[first + j, s] = part if h == 0 else dgb[first + j, s] + part
        hg[block, s, :, h * 384 : (h + 1) * 384] = (
            (hidden * weight).astype(bf).reshape(4, 128, 384)
        )
        back = back * weight
        dgu[block, s, :, h * 768 : h * 768 + 384] = (
            (back * up * (sig * (1.0 + gate * (1.0 - sig)))).astype(bf).reshape(4, 128, 384)
        )
        dgu[block, s, :, h * 768 + 384 : (h + 1) * 768] = (
            (back * silu).astype(bf).reshape(4, 128, 384)
        )

    def dx_step(s, pair):
        first = 4 * pair
        block = pl.ds(first, 4)
        dxb[block, s] = (
            lax.dot_general(
                dgu[block, s].reshape(512, 1536),
                win[...].reshape(1536, 1536),
                nt,
                preferred_element_type=f32,
            )
            .astype(bf)
            .reshape(4, 128, 1536)
        )
        for j in range(2):
            for a in range(2):
                sib_sum(2 * pair + j, s, a).start()

    def out_slot(slot):
        return win.at[:, pl.ds(slot * 128, 128)]

    def out_copy(slot, s, first):
        return pltpu.make_async_copy(
            out_slot(slot), outp_hbm.at[pl.ds(first, 4), s], stage_sem.at[slot]
        )

    def out_step(slot, s, pair):
        first = 4 * pair
        win[:, slot * 128 : (slot + 1) * 128] = (
            jnp.dot(
                hg[pl.ds(first, 4), s].reshape(512, FF), wout[...], preferred_element_type=f32
            )
            .astype(bf)
            .reshape(4, 128, 1536)
        )
        out_copy(slot, s, first).start()

    def early_copies(first):
        return [
            pltpu.make_async_copy(
                gout.at[pl.ds(j * 128, 128)], outp_hbm.at[first + j, 0], grad_sem.at[j]
            )
            for j in range(4)
        ]

    def early_step(pair):
        first = 4 * pair
        gout[:512] = jnp.dot(
            hg[pl.ds(first, 4), 0].reshape(512, FF), wout[...], preferred_element_type=f32
        ).astype(bf)
        for copy in early_copies(first):
            copy.start()

    def early_wait():
        for copy in early_copies(0):
            copy.wait()

    far = 1 - hi
    near = hi

    def pair_of(t):
        return far + t * (1 - 2 * far)

    def i_piece(dd, p):
        return gin.at[pl.ds(pl.multiple_of(dd * 384 + p * PIECE, 16), PIECE)]

    def i_diag(p):
        return remote(
            i_piece(d_d, p), ti.at[p], i_send.at[0, p], i_recv.at[0, p], (to_x, to_y)[p % 2]
        )

    def i_direct(p):
        if p % 2 == 0:
            return remote(i_piece(d_x, p), xi.at[p], i_send.at[1, p], i_recv.at[1, p], to_x)
        return remote(i_piece(d_y, p), yi.at[p], i_send.at[1, p], i_recv.at[2, p], to_y)

    def i_summed(p):
        if p % 2 == 0:
            return remote(i_piece(d_y, p), yi.at[p], i_send.at[2, p], i_recv.at[2, p], to_y)
        return remote(i_piece(d_x, p), xi.at[p], i_send.at[2, p], i_recv.at[1, p], to_x)

    def i_middle(p):
        i_diag(p).wait_recv()
        dd = d_y if p % 2 == 0 else d_x
        rows = pl.ds(pl.multiple_of(dd * 384 + p * PIECE, 16), PIECE)
        gin[rows] = (gin[rows].astype(f32) + ti[p].astype(f32)).astype(bf)
        i_summed(p).start()

    def i_final(p):
        remote(xi.at[p], xi.at[p], i_send.at[1, p], i_recv.at[1, p], to_x).wait_recv()
        remote(yi.at[p], yi.at[p], i_send.at[1, p], i_recv.at[2, p], to_y).wait_recv()
        rows = pl.ds(pl.multiple_of(d * 384 + p * PIECE, 16), PIECE)
        xi[p] = (gin[rows].astype(f32) + xi[p].astype(f32) + yi[p].astype(f32)).astype(bf)

    def in_grad(yy, h):
        return lax.dot_general(
            xall[:, :, :, pl.ds(pl.multiple_of(yy * 768, 128), 768)].reshape(2048, 768),
            dgu[:, :, :, h * 768 : (h + 1) * 768].reshape(2048, 768),
            tn,
            preferred_element_type=f32,
        ).astype(bf)

    def in_first(yy):
        gin[pl.ds(pl.multiple_of(yy * 768, 16), 768)] = in_grad(yy, 0)

    @pl.loop(0, 2)
    def _(t):
        half_step(0, pair_of(t), 0)

    @pl.when(mid)
    def _():
        pass_on(1, 1)

    w_rest(1)

    @pl.when(end)
    def _():
        pass_on(1, 1)


    @pl.loop(0, 2)
    def _(t):
        pair = pair_of(t)
        half_step(0, pair, 1)
        dx_step(0, pair)

        @pl.when(t == 0)
        def _():
            end_sums(0, (0, 1))
            pass_on(2, 1)

        @pl.when(t == 1)
        def _():
            end_sums(0, (2,))

    from_sib(1, (near,))

    @pl.loop(0, 2)
    def _(t):
        half_step(1, pair_of(1 - t), 0)

        @pl.when(t == 0)
        def _():
            pass_on(3, 1)
            early_step(far)
            from_sib(1, (far,))

    mid_sum(0, 0)

    @pl.loop(0, 2)
    def _(t):
        pair = pair_of(t)
        half_step(1, pair, 1)
        dx_step(1, pair)

        @pl.when(t == 0)
        def _():
            in_first(1 - y)
            for p in range(4):
                i_diag(p).start()
            for p in (1, 3):
                i_direct(p).start()
            end_sums(1, (0, 1))
            in_first(y)
            for p in (0, 2):
                i_direct(p).start()
            mid_sum(1, 0)
            mid_sum(2, 0)

    def g_rows(dd, i):
        return pl.ds(pl.multiple_of(dd * 192 + i * 48, 16), 48)

    def g_piece(dd, i):
        return gout.at[g_rows(dd, i)]

    def g_diag(i):
        return remote(
            g_piece(d_d, i), tg.at[i], g_send.at[0, i], g_recv.at[0, i], (to_x, to_y)[i]
        )

    def g_direct(i):
        if i == 0:
            return remote(g_piece(d_x, i), xg.at[i], g_send.at[1, i], g_recv.at[1, i], to_x)
        return remote(g_piece(d_y, i), yg.at[i], g_send.at[1, i], g_recv.at[2, i], to_y)

    def g_summed(i):
        if i == 0:
            return remote(g_piece(d_y, i), yg.at[i], g_send.at[2, i], g_recv.at[2, i], to_y)
        return remote(g_piece(d_x, i), xg.at[i], g_send.at[2, i], g_recv.at[1, i], to_x)

    def g_middle(i):
        g_diag(i).wait_recv()
        rows = g_rows(d_y if i == 0 else d_x, i)
        gout[rows] = (gout[rows].astype(f32) + tg[i].astype(f32)).astype(bf)
        g_summed(i).start()

    def out_grad(half):
        at = pl.multiple_of(half * 384, 128)
        gout[pl.ds(at, 384)] = lax.dot_general(
            hg[:, :, :, pl.ds(at, 384)].reshape(2048, 384),
            gall[...].reshape(2048, 1536),
            tn,
            preferred_element_type=f32,
        ).astype(bf)

    for p in range(4):
        i_middle(p)
    early_wait()
    out_grad(1 - y)
    g_diag(0).start()
    g_diag(1).start()
    g_direct(1).start()
    end_sums(1, (2,))
    out_grad(y)
    g_direct(0).start()
    mid_sum(0, 1)
    rest = [
        pltpu.make_async_copy(
            gout.at[pl.ds(k * 192 + PIECE, PIECE)], gout_hbm.at[k], own_sem.at[k]
        )
        for k in range(4)
    ]
    for copy in rest:
        copy.start()

    def grad_copy(k):
        return pltpu.make_async_copy(
            win.at[k, :, pl.ds(0, 768)], gin_hbm.at[k], grad_sem.at[k]
        )

    for h in range(2):
        for kind in range(2):
            for p in range(2):
                w_copy(h, kind, p, d, to_x, 2).wait_send()
    for k in range(2):
        win[2 * k : 2 * k + 2, :, :768] = in_grad(k, 1).reshape(2, 384, 768)
        grad_copy(2 * k).start()
        grad_copy(2 * k + 1).start()
    for p in range(4):
        i_final(p)
    in_copy = pltpu.make_async_copy(xi, gin_first_hbm, own_sem.at[6])
    in_copy.start()
    for k in range(4):
        grad_copy(k).wait()
    for i in range(2):
        g_middle(i)
    mid_sum(1, 1)
    mid_sum(2, 1)
    out_step(0, 0, near)
    out_step(1, 1, far)
    out_step(2, 1, near)
    last_sum(0)
    for i in range(2):
        remote(xg.at[i], xg.at[i], g_send.at[1, i], g_recv.at[1, i], to_x).wait_recv()
        remote(yg.at[i], yg.at[i], g_send.at[1, i], g_recv.at[2, i], to_y).wait_recv()
        xg[i] = (
            gout[g_rows(d, i)].astype(f32) + xg[i].astype(f32) + yg[i].astype(f32)
        ).astype(bf)
    out_first_copy = pltpu.make_async_copy(xg, gout_first_hbm, own_sem.at[7])
    out_first_copy.start()
    for copy in rest:
        copy.wait()
    for k in range(3):
        out_copy(k, 1, 0).wait()
    last_sum(1)
    in_copy.wait()
    out_first_copy.wait()
    for s in range(2):
        dx_copy(s).wait()

    for i in range(2):
        for copy in (g_diag(i), g_direct(i), g_summed(i)):
            copy.wait_send()
    for p in range(4):
        for copy in (i_diag(p), i_direct(p), i_summed(p)):
            copy.wait_send()
    for h in range(2):
        for kind in range(2):
            for p in range(2):
                for row in range(2):
                    w_copy(h, kind, p, d, to_x, row).wait_send()
    for s in range(2):
        for zp in range(4):
            for a in range(2):
                sib_copy(a, zp, s).wait_send()
                sib_sum(zp, s, a).wait_send()

                @pl.when((zp <= z) & (z < 3))
                def _():
                    ag_copy(a, zp, s, 0).wait_send()

                @pl.when((zp >= z) & (z > 0))
                def _():
                    ag_copy(a, zp, s, 1).wait_send()

        for i in range(3):
            halves, last = hop(i, s, to_in, True)
            for copy in halves + [last]:
                copy.wait_send()


def expert_stage(rows, grads, gates_t, w_in, w_out):
    bf, f32 = jnp.bfloat16, jnp.float32
    shape = jax.ShapeDtypeStruct
    width = rows.shape[-1]
    hbm = pl.BlockSpec(memory_space=pltpu.HBM)
    vmem = pl.BlockSpec(memory_space=pltpu.VMEM)
    dma = pltpu.SemaphoreType.DMA
    return pl.pallas_call(
        expert_kernel,
        out_shape=(
            shape((8, 128, width // 4), f32),
            shape((2, 8, 128), f32),
            shape((8, 2, 128, width), bf),
            shape((4, 384, FF), bf),
            shape((4, PIECE, width), bf),
            shape((2, 48, width), bf),
            shape((4, PIECE, FF), bf),
        ),
        in_specs=[hbm] * 5,
        out_specs=(hbm, vmem, hbm, hbm, hbm, hbm, hbm),
        scratch_shapes=[
            pltpu.VMEM((4, width // 4, 2 * FF), bf),
            pltpu.VMEM((FF, width), bf),
            pltpu.VMEM((8, 2, 128, width), bf),
            pltpu.VMEM((8, 2, 128, width), bf),
            pltpu.VMEM((8, 2, 8, 128), f32),
            pltpu.VMEM((8, 2, 128, 2 * FF), bf),
            pltpu.VMEM((8, 2, 128, FF), bf),
            pltpu.VMEM((8, 2, 128, width), bf),
            pltpu.VMEM((8, 2, 8, 128), f32),
            pltpu.VMEM((4, 2, 128, width), bf),
            pltpu.VMEM((4, 2, 8, 128), f32),
            pltpu.VMEM((3, 2, 128, width), bf),
            pltpu.VMEM((3, 2, 8, 128), f32),
            pltpu.VMEM((3, 2, 128, width), bf),
            pltpu.VMEM((3, 2, 8, 128), f32),
            pltpu.VMEM((FF, width), bf),
            *([pltpu.VMEM((2, 48, width), bf)] * 3),
            pltpu.VMEM((width, FF), bf),
            *([pltpu.VMEM((4, PIECE, FF), bf)] * 3),
            pltpu.VMEM((8, 128, width // 4), f32),
            dma((9,)),
            dma((3,)),
            dma((4,)),
            dma((3, 2)),
            dma((3, 2)),
            dma((3, 4)),
            dma((3, 4)),
            dma((3, 2, 2, 2)),
            dma((3, 2, 2, 2)),
            dma((2, 4, 2)),
            dma((2, 2, 4, 2)),
            dma((2, 4, 2)),
            dma((2, 4, 2)),
            dma((6, 4, 2)),
            dma((4, 4, 2)),
            dma((2, 2, 3, 2)),
            dma((2, 3, 2)),
        ],
        compiler_params=pltpu.CompilerParams(
            collective_id=1, has_side_effects=True, vmem_limit_bytes=63 * 2**20
        ),
        name="expert_stage",
    )(
        rows.reshape(2, 128, width),
        grads.reshape(8, 2, 128, width),
        gates_t,
        w_in,
        w_out,
    )


def backward_kernel(
    dx_hbm,
    dgt_hbm,
    gates_hbm,
    mixed_hbm,
    cot_hbm,
    tok_hbm,
    q_hbm,
    kv_hbm,
    att_hbm,
    lens_ref,
    small_hbm,
    rope_hbm,
    wa_hbm,
    wb_hbm,
    gin_hbm,
    gout_hbm,
    outp_hbm,
    block_hbm,
    dtok_hbm,
    gq_hbm,
    gb_hbm,
    gkv_out,
    small_out,
    ein_hbm,
    eout_hbm,
    osib,
    oro,
    ori,
    wide,
    gq,
    gb,
    gk,
    sib_q,
    sib_b,
    sib_k,
    tq,
    xq,
    yq,
    roq,
    riq,
    tb,
    xb,
    yb,
    rob,
    rib,
    tw,
    xw,
    yw,
    row_,
    riw,
    te,
    xe,
    ye,
    le,
    lf,
    td,
    xd,
    yd,
    ld,
    old,
    oslot,
    dat,
    dkv,
    tk,
    xk,
    yk,
    rope,
    cot_ref,
    tok_ref,
    q_ref,
    kv_ref,
    att_ref,
    mixed_ref,
    block_out,
    dtok_out,
    dgt_ref,
    gates_ref,
    small_ref,
    gq_out,
    gb_out,
    load_sem,
    out_sem,
    le_sem,
    old_sem,
    os_recv,
    os_send,
    ds_recv,
    ds_send,
    t_recv,
    x_recv,
    y_recv,
    t_send,
    d_send,
    s_send,
    ro_recv,
    ri_recv,
    hop_send,
):
    bf, f32 = jnp.bfloat16, jnp.float32
    d, e, z, c, x, y = place()
    d_x = d + 1 - 2 * x
    d_y = d + 2 - 4 * y
    d_d = 3 - d
    hi = lax.div(z, 2)
    zz = z * hi + (3 - z) * (1 - hi)
    other = 1 - c
    mid = zz == 2
    end = zz == 3
    to_x = (d_x, e)
    to_y = (d_y, e)
    to_sib = (d, 2 * z + other)
    e_in = e + 2 - 4 * hi
    to_in = (d, e_in)
    to_out = (d, jnp.where(zz == 2, e - 2 + 4 * hi, e_in))

    dqs = block_out
    dmix = dtok_out
    dx_ref = dtok_out

    first_loads = [
        pltpu.make_async_copy(
            dx_hbm.at[4 * s + j],
            dx_ref.at[pl.ds(s * 128, 128), pl.ds(j * 384, 384)],
            load_sem.at[13 + 4 * s + j],
        )
        for s in range(2)
        for j in range(4)
    ] + [
        pltpu.make_async_copy(mixed_hbm, mixed_ref, load_sem.at[10]),
    ]
    tiny_loads = [
        pltpu.make_async_copy(src, dst, load_sem.at[21 + j])
        for j, (src, dst) in enumerate(
            ((dgt_hbm, dgt_ref), (gates_hbm, gates_ref), (small_hbm, small_ref))
        )
    ]
    results = [
        pltpu.make_async_copy(src, dst, out_sem.at[j])
        for j, (src, dst) in enumerate(
            ((gq_out, gq_hbm), (gb_out, gb_hbm), (xe, ein_hbm), (xd, eout_hbm))
        )
    ]
    for load in tiny_loads:
        load.start()
    for load in first_loads:
        load.start()

    barrier = pltpu.get_barrier_semaphore()
    for target in (to_x, to_y, to_sib, to_in):
        pl.semaphore_signal(barrier, inc=1, device_id=target, device_id_type=MESH)

    @pl.when(mid)
    def _():
        pl.semaphore_signal(barrier, inc=1, device_id=to_out, device_id_type=MESH)

    pl.semaphore_wait(barrier, 7 - zz)

    def order(i):
        v = i if i < 2 else (5 - zz if i == 2 else zz)
        return v * hi + (3 - v) * (1 - hi)

    def across(k, src, t, fx, fy, ways=(0, 1, 0, 1)):
        def diag(i):
            return remote(
                src(d_d, i), t.at[i], t_send.at[k, i], t_recv.at[k, i], (to_x, to_y)[ways[i]]
            )

        def direct(i):
            if ways[i] == 0:
                return remote(src(d_x, i), fx.at[i], d_send.at[k, i], x_recv.at[k, i], to_x)
            return remote(src(d_y, i), fy.at[i], d_send.at[k, i], y_recv.at[k, i], to_y)

        def summed(i, ref):
            if ways[i] == 0:
                return remote(ref, fy.at[i], s_send.at[k, i], y_recv.at[k, i], to_y)
            return remote(ref, fx.at[i], s_send.at[k, i], x_recv.at[k, i], to_x)

        def wait_t(i):
            remote(t.at[i], t.at[i], t_send.at[k, i], t_recv.at[k, i], to_x).wait_recv()

        def wait_xy(i):
            remote(fx.at[i], fx.at[i], d_send.at[k, i], x_recv.at[k, i], to_x).wait_recv()
            remote(fy.at[i], fy.at[i], d_send.at[k, i], y_recv.at[k, i], to_y).wait_recv()

        def drain(n):
            for i in range(n):
                diag(i).wait_send()
                direct(i).wait_send()
                summed(i, t.at[i]).wait_send()

        return diag, direct, summed, wait_t, wait_xy, drain

    def along(k, slot, ro, ri):
        def send(i, target, dst, recv):
            return remote(slot(i), dst.at[i], hop_send.at[k, i], recv.at[k, i], target)

        def to_ro(i):
            return send(i, to_in, ro, ro_recv)

        def to_ri(i):
            return send(i, to_in if i < 2 else to_out, ri, ri_recv)

        def wait_ro(i):
            remote(ro.at[i], ro.at[i], hop_send.at[k, i], ro_recv.at[k, i], to_in).wait_recv()

        def wait_ri(i):
            remote(ri.at[i], ri.at[i], hop_send.at[k, i], ri_recv.at[k, i], to_in).wait_recv()

        def drain():
            for i in range(3):
                to_ro(i).wait_send()

        return to_ro, to_ri, wait_ro, wait_ri, drain

    expert_ways = (0, 1, 0, 0)

    def expert_src(dd, p):
        return gin_hbm.at[pl.ds(pl.multiple_of(dd * 384 + p * PIECE, 16), PIECE)]

    e_diag, e_direct, e_summed, e_wait_t, e_wait_xy, e_drain = across(
        0, expert_src, te, xe, ye, expert_ways
    )

    def e_sent_to(p):
        return d_y if expert_ways[p] == 0 else d_x

    e_loads = [
        pltpu.make_async_copy(expert_src(e_sent_to(p), p), le.at[p], le_sem.at[p])
        for p in range(4)
    ]
    e_own = pltpu.make_async_copy(
        gin_hbm.at[pl.ds(pl.multiple_of(d * 384, 16), 384)], lf, le_sem.at[4]
    )

    def e_middle(p):
        e_wait_t(p)
        e_loads[p].wait()
        te[p] = (te[p].astype(f32) + le[p].astype(f32)).astype(bf)
        e_summed(p, te.at[p]).start()

    def e_final(p):
        e_wait_xy(p)
        rows = slice(p * PIECE, (p + 1) * PIECE)
        total = lf[rows].astype(f32) + xe[p].astype(f32) + ye[p].astype(f32)
        xe[p] = total.astype(bf)

    def d_src(dd):
        return gout_hbm.at[dd]

    def d_diag():
        return remote(d_src(d_d), td, t_send.at[5, 0], t_recv.at[5, 0], to_y)

    def d_direct():
        return remote(d_src(d_y), yd, d_send.at[5, 0], y_recv.at[5, 0], to_y)

    def d_summed():
        return remote(td, xd, s_send.at[5, 0], x_recv.at[5, 0], to_x)

    d_loads = [
        pltpu.make_async_copy(d_src(dd), ld.at[j], le_sem.at[5 + j])
        for j, dd in enumerate((d_x, d))
    ]

    def d_middle():
        d_diag().wait_recv()
        d_loads[0].wait()
        td[...] = (td[...].astype(f32) + ld[0].astype(f32)).astype(bf)
        d_summed().start()

    def d_final():
        d_summed().wait_recv()
        d_direct().wait_recv()
        xd[...] = (ld[1].astype(f32) + xd[...].astype(f32) + yd[...].astype(f32)).astype(bf)

    def store_q(total):
        gq_out[...] = total

    def store_b(total):
        gb_out[...] = total

    def store_k(total):
        gkv_out[...] = total[:, :512]
        small_out[...] = lax.dot_general(
            eye[:16],
            total[:, 512:],
            (((1,), (1,)), ((), ())),
            preferred_element_type=f32,
            precision=highest,
        )

    dense = (
        (gq, sib_q, tq, xq, yq, roq, riq, store_q),
        (gb, sib_b, tb, xb, yb, rob, rib, store_b),
        (gk, sib_k, tw, xw, yw, row_, riw, store_k),
    )

    def dense_stream(j):
        grad, sib, t, fx, fy, ro, ri, out = dense[j]

        def src(dd, i):
            return grad.at[dd * 4 + order(i), c]

        diag, direct, summed, wait_t, wait_xy, drain = across(1 + j, src, t, fx, fy)

        def own_slot(i):
            return grad.at[d * 4 + order(i), c]

        to_ro, to_ri, wait_ro, wait_ri, drain_z = along(j, own_slot, ro, ri)

        def sib_copy():
            return remote(grad.at[:, other], sib, ds_send.at[j], ds_recv.at[j], to_sib)

        def begin():
            sib_copy().wait_recv()

            @pl.loop(0, 16)
            def _(k):
                grad[k, c] = (grad[k, c].astype(f32) + sib[k].astype(f32)).astype(bf)

            for i in range(4):
                diag(i).start()
            for i in range(4):
                direct(i).start()

        def middle(i):
            dd = d_y if i % 2 == 0 else d_x
            wait_t(i)
            at = dd * 4 + order(i)
            grad[at, c] = (grad[at, c].astype(f32) + t[i].astype(f32)).astype(bf)
            summed(i, src(dd, i)).start()

        def local(i):
            return grad[d * 4 + order(i), c].astype(f32) + fx[i].astype(f32) + fy[i].astype(f32)

        def put(i, total):
            grad[d * 4 + order(i), c] = total.astype(bf)

        def last(i):
            wait_xy(i)
            if i == 3:
                return

            @pl.when(end)
            def _():
                put(i, local(i))
                to_ro(i).start()

        def hop(i):
            @pl.when(mid)
            def _():
                if i < 2:
                    wait_ro(i)
                    put(i, local(i) + ro[i].astype(f32))
                else:
                    wait_ri(0)
                    put(2, local(2) + ri[0].astype(f32))
                to_ri(i).start()

        def finish():
            @pl.when(mid)
            def _():
                wait_ro(2)
                wait_ri(1)
                out(local(3) + ro[2].astype(f32) + ri[1].astype(f32))

            @pl.when(end)
            def _():
                wait_ri(2)
                out(local(3) + ri[2].astype(f32))

        def drain_all():
            sib_copy().wait_send()
            drain(4)
            drain_z()

        return sib_copy, begin, middle, last, hop, finish, drain_all

    q_sib, q_begin, q_middle, q_last, q_hop, q_finish, q_drain = dense_stream(0)
    b_sib, b_begin, b_middle, b_last, b_hop, b_finish, b_drain = dense_stream(1)
    w_sib, w_begin, w_middle, w_last, w_hop, w_finish, w_drain = dense_stream(2)

    def out_rows(i, lane):
        return outp_hbm.at[pl.ds(pl.multiple_of((2 * order(i) + lane) * CHUNK, CHUNK), CHUNK)]

    def out_sib(i):
        return remote(out_rows(i, other), osib.at[i], os_send.at[i], os_recv.at[i], to_sib)

    o_ro, o_ri, o_wait_ro, o_wait_ri, _ = along(3, lambda i: oslot.at[i % 2], oro, ori)

    def out_sum(i, incoming, store):
        out_sib(i).wait_recv()
        for half in range(2):
            rows = pl.ds(half * 128, 128)
            loads = [
                pltpu.make_async_copy(ref.at[rows], old.at[j], old_sem.at[j])
                for j, ref in enumerate([out_rows(i, c), osib.at[i]] + incoming)
            ]
            for load in loads:
                load.start()
            for load in loads:
                load.wait()
            total = old[0].astype(f32)
            for j in range(1, len(loads)):
                total = total + old[j].astype(f32)
            store(slice(half * 128, (half + 1) * 128), total)

    def out_slot(i):
        def store(rows, total):
            oslot[i % 2, rows] = total.astype(bf)

        return store

    def out_end(i):
        @pl.when(end)
        def _():
            if i == 2:
                o_ro(0).wait_send()
            out_sum(i, [], out_slot(i))
            o_ro(i).start()

    def out_mid(i):
        @pl.when(mid)
        def _():
            if i < 2:
                o_wait_ro(i)
                out_sum(i, [oro.at[i]], out_slot(i))
            else:
                o_ri(0).wait_send()
                o_wait_ri(0)
                out_sum(2, [ori.at[0]], out_slot(2))
            o_ri(i).start()

    def out_finish():
        def store(rows, total):
            total = total + mixed_ref[rows]
            slot = d * 128 + lax.broadcasted_iota(jnp.int32, (128, 1), 0)
            live = slot < lens_ref[rows.start // 128]
            block_out[rows] = jnp.where(live, total, 0.0).astype(bf)

        @pl.when(mid)
        def _():
            o_wait_ro(2)
            o_wait_ri(1)
            out_sum(3, [oro.at[2], ori.at[1]], store)

        @pl.when(end)
        def _():
            o_wait_ri(2)
            out_sum(3, [ori.at[2]], store)

    def kv_src(dd, i):
        return dkv.at[dd, pl.ds(i * 128, 128)]

    k_diag, k_direct, k_summed, k_wait_t, k_wait_xy, k_drain = across(4, kv_src, tk, xk, yk)

    def k_middle(i):
        dd = d_y if i % 2 == 0 else d_x
        k_wait_t(i)
        rows = slice(i * 128, (i + 1) * 128)
        dkv[dd, rows] = (dkv[dd, rows].astype(f32) + tk[i].astype(f32)).astype(bf)
        k_summed(i, kv_src(dd, i)).start()

    wb_load = pltpu.make_async_copy(wb_hbm, wide.at[:, pl.ds(0, 1536)], load_sem.at[1])
    wa_load = pltpu.make_async_copy(wa_hbm.at[:, pl.ds(0, 2048)], wide, load_sem.at[2])
    rope_load = pltpu.make_async_copy(
        rope_hbm.at[:, pl.ds(pl.multiple_of(d * 128, 128), 128)], rope, load_sem.at[3]
    )
    loads = [
        pltpu.make_async_copy(src, dst, load_sem.at[4 + j])
        for j, (src, dst) in enumerate(
            (
                (cot_hbm, cot_ref),
                (att_hbm, att_ref),
                (q_hbm, q_ref),
                (kv_hbm, kv_ref),
                (tok_hbm, tok_ref),
            )
        )
    ]
    for load in loads[:2]:
        load.start()
    wb_load.start()
    rope_load.start()
    for load in loads[2:] + e_loads + [e_own] + d_loads:
        load.start()
    for p in range(4):
        e_diag(p).start()
    for p in (0, 1):
        e_direct(p).start()
    d_diag().start()
    for i in range(4):
        out_sib(i).start()
    out_end(0)

    nt = (((1,), (1,)), ((), ()))
    tn = (((0,), (0,)), ((), ()))

    def dot_nt(a, b):
        return lax.dot_general(a, b, nt, preferred_element_type=f32)

    def dot_tn(a, b):
        return lax.dot_general(a, b, tn, preferred_element_type=f32)

    eye = (
        lax.broadcasted_iota(jnp.int32, (128, 128), 0)
        == lax.broadcasted_iota(jnp.int32, (128, 128), 1)
    ).astype(f32)
    eye_low = eye.astype(bf)
    for load in tiny_loads:
        load.wait()
    gates = jnp.concatenate([gates_ref[s] for s in range(2)], axis=1)
    dgate = jnp.concatenate([dgt_ref[s] for s in range(2)], axis=1)
    dlogit = gates * (dgate - jnp.sum(gates * dgate, axis=0, keepdims=True))
    dl_hi = dlogit.astype(bf).astype(f32)
    dl = jnp.concatenate([dl_hi, dlogit - dl_hi], axis=0).astype(bf)
    small_t = small_ref[...]
    router = jnp.concatenate([small_t[:8]] * 2, axis=0).astype(bf)
    for load in first_loads:
        load.wait()
    dn2 = dx_ref[...] + dot_tn(dl, router)
    mixed = mixed_ref[...]
    inv2 = lax.rsqrt(jnp.mean(mixed * mixed, axis=1, keepdims=True) + epsilon)
    n2 = mixed * inv2
    normed2 = (n2 * small_t[9:10]).astype(bf)
    router_sum = jnp.dot(dl, normed2, preferred_element_type=f32)
    router_sum = router_sum[:8] + router_sum[8:]
    mid_sum = jnp.sum(dn2 * n2, axis=0, keepdims=True)
    loads[0].wait()
    loads[1].wait()
    grads = [
        jnp.where(
            d * 128 + lax.broadcasted_iota(jnp.int32, (128, 1), 0) < lens_ref[s],
            cot_ref[s * 128 : (s + 1) * 128].astype(f32),
            0.0,
        )
        for s in range(2)
    ]
    u = dn2 * small_t[9:10]
    dmixed = jnp.concatenate(grads, axis=0) + inv2 * (u - n2 * jnp.mean(u * n2, axis=1, keepdims=True))
    dmix[...] = dmixed
    dproj = dmixed.astype(bf)
    for r in range(4):
        part = dot_tn(att_ref[:, r * 384 : (r + 1) * 384], dproj)
        gb[4 * r : 4 * r + 4] = part.astype(bf).reshape(4, 2, 48, 1536)
    b_sib().start()
    wb_load.wait()
    datt = dot_nt(dproj, wide[:, :1536]).astype(bf)
    for head in range(QUERY_HEADS):
        for s in range(2):
            at = (s * QUERY_HEADS + head) * 128
            dat[at : at + 128] = datt[s * 128 : (s + 1) * 128, head * 128 : (head + 1) * 128]
    wa_load.start()
    b_begin()
    out_end(1)

    query_pos = d * 128 + lax.broadcasted_iota(jnp.int32, (128, 512), 0)
    key_pos = lax.broadcasted_iota(jnp.int32, (128, 512), 1)
    rope_load.wait()
    for load in loads[2:]:
        load.wait()
    cos_rows = rope[0]
    sin_rows = rope[1]
    scale = HEAD_SIZE ** (-0.5)

    def unrotate_rows(v, cos, sin):
        return v * cos - pltpu.roll(v, 64, 1) * sin

    def attend(n):
        s = lax.div(n, 2)
        h = lax.rem(n, 2)
        srow = pl.ds(pl.multiple_of(s * 128, 128), 128)
        kcol = pl.ds(pl.multiple_of(h * 128, 128), 128)
        vcol = pl.ds(pl.multiple_of(256 + h * 128, 128), 128)
        lens = lens_ref[s]
        allowed = (key_pos <= query_pos) & (key_pos < lens)
        ks = kv_ref[:, srow, kcol].reshape(512, 128)
        vs = kv_ref[:, srow, vcol].reshape(512, 128)
        dk = None
        dv = None
        for half in range(2):
            rows = pl.ds(pl.multiple_of(n * 768 + half * 384, 128), 384)
            qh = q_ref[rows]
            dh = dat[rows]
            scores = dot_nt(qh, ks).reshape(3, 128, 512) * scale
            scores = jnp.where(allowed[None], scores, -1e30)
            probs = jnp.exp(scores - jnp.max(scores, axis=-1, keepdims=True))
            probs = probs * (1.0 / jnp.sum(probs, axis=-1, keepdims=True))
            dprobs = dot_nt(dh, vs).reshape(3, 128, 512)
            delta = jnp.sum(probs * dprobs, axis=-1, keepdims=True)
            dscores = (probs * (dprobs - delta)).astype(bf).reshape(384, 512)
            low = probs.astype(bf).reshape(384, 512)
            dq = jnp.dot(dscores, ks, preferred_element_type=f32) * scale
            for j in range(3):
                dqs[srow, pl.ds(pl.multiple_of(h * 768 + (half * 3 + j) * 128, 128), 128)] = (
                    unrotate_rows(dq[j * 128 : (j + 1) * 128], cos_rows, sin_rows).astype(bf)
                )
            dk_part = dot_tn(dscores, qh)
            dv_part = dot_tn(low, dh)
            dk = dk_part if dk is None else dk + dk_part
            dv = dv_part if dv is None else dv + dv_part
        dkv[:, srow, kcol] = (dk * scale).astype(bf).reshape(4, 128, 128)
        dkv[:, srow, vcol] = dv.astype(bf).reshape(4, 128, 128)

    pl.loop(0, 2)(attend)
    for i in range(4):
        b_middle(i)
    e_middle(1)
    e_middle(0)
    out_mid(0)
    pl.loop(2, 4)(attend)
    for i in range(2):
        k_diag(i).start()
    for i in range(2):
        k_direct(i).start()
    for i in range(4):
        b_last(i)
    out_end(2)

    tok = tok_ref[...].astype(f32)
    inv1 = lax.rsqrt(jnp.mean(tok * tok, axis=1, keepdims=True) + epsilon)
    n1 = tok * inv1
    normed = (n1 * small_t[8:9]).astype(bf)
    for r in range(4):
        part = dot_tn(normed[:, r * 384 : (r + 1) * 384], dqs[...])
        gq[4 * r : 4 * r + 4] = part.astype(bf).reshape(4, 2, 48, 1536)
    q_sib().start()
    k_middle(0)
    k_middle(1)
    q_begin()
    wa_load.wait()
    dn1 = dot_nt(dqs[...], wide[:, :1536])

    for i in range(2):
        k_wait_xy(i)
    own = jnp.concatenate(
        [
            dkv[d, i * 128 : (i + 1) * 128].astype(f32) + xk[i].astype(f32) + yk[i].astype(f32)
            for i in range(2)
        ],
        axis=0,
    )
    cos_two = jnp.concatenate([cos_rows] * 2, axis=0)
    sin_two = jnp.concatenate([sin_rows] * 2, axis=0)
    dkv_own = jnp.concatenate(
        [
            unrotate_rows(own[:, h * 128 : (h + 1) * 128], cos_two, sin_two)
            for h in range(2)
        ]
        + [own[:, 256:]],
        axis=1,
    ).astype(bf)
    dn1 = dn1 + dot_nt(dkv_own, wide[:, 1536:])
    pre_sum = jnp.sum(dn1 * n1, axis=0, keepdims=True)
    row8 = lax.broadcasted_iota(jnp.int32, (8, 1536), 0)
    gains = jnp.where(row8 == 0, pre_sum, jnp.where(row8 == 1, mid_sum, 0.0))
    smalls = jnp.concatenate([router_sum, gains], axis=0).astype(bf)
    for r in range(4):
        cols = slice(r * 384, (r + 1) * 384)
        part = dot_tn(normed[:, cols], dkv_own)
        gk[4 * r : 4 * r + 4, :, :, :512] = part.astype(bf).reshape(4, 2, 48, 512)
        part = dot_tn(smalls[:, cols], eye_low[:16])
        gk[4 * r : 4 * r + 4, :, :, 512:] = part.astype(bf).reshape(4, 2, 48, 128)
    w_sib().start()
    u = dn1 * small_t[8:9]
    dtok_copy = pltpu.make_async_copy(dtok_out, dtok_hbm, load_sem.at[11])
    dtok_out[...] = dmix[...] + inv1 * (u - n1 * jnp.mean(u * n1, axis=1, keepdims=True))

    dtok_copy.start()

    for i in range(4):
        q_middle(i)
    w_begin()
    e_direct(2).start()
    b_hop(0)
    b_hop(1)
    out_mid(1)
    out_mid(2)
    for i in range(4):
        q_last(i)
    for i in range(4):
        w_middle(i)
    d_direct().start()
    d_middle()
    e_direct(3).start()
    for p in (2, 3):
        e_middle(p)
    b_hop(2)
    q_hop(0)
    q_hop(1)
    out_finish()
    block_copy = pltpu.make_async_copy(block_out, block_hbm, load_sem.at[12])
    block_copy.start()
    for i in range(4):
        w_last(i)
    w_hop(0)
    q_hop(2)
    w_hop(1)
    w_hop(2)
    b_finish()
    results[1].start()
    q_finish()
    results[0].start()
    e_own.wait()
    d_loads[1].wait()
    d_final()
    results[3].start()
    for p in range(4):
        e_final(p)
    results[2].start()
    w_finish()
    dtok_copy.wait()
    block_copy.wait()
    for copy in results:
        copy.wait()

    e_drain(4)
    for copy in (d_diag(), d_direct(), d_summed()):
        copy.wait_send()
    k_drain(2)
    q_drain()
    b_drain()
    w_drain()
    for i in range(1, 3):
        o_ro(i).wait_send()
    for i in range(4):
        out_sib(i).wait_send()


def backward_stage(dx, dgt, gates, mixed, cot, tok, q, kv, att, lens, small, rope, wa, wb, gin, gout, outp):
    bf, f32 = jnp.bfloat16, jnp.float32
    shape = jax.ShapeDtypeStruct
    width = tok.shape[-1]
    hbm = pl.BlockSpec(memory_space=pltpu.HBM)
    vmem = pl.BlockSpec(memory_space=pltpu.VMEM)
    smem = pl.BlockSpec(memory_space=pltpu.SMEM)
    dma = pltpu.SemaphoreType.DMA
    widths = (width, width, 640)
    dense = []
    for w in widths:
        dense += [pltpu.VMEM((4, 48, w), bf)] * 3 + [pltpu.VMEM((3, 48, w), bf)] * 2
    return pl.pallas_call(
        backward_kernel,
        out_shape=(
            shape((CHUNK, width), bf),
            shape((CHUNK, width), f32),
            shape((48, width), f32),
            shape((48, width), f32),
            shape((48, 512), f32),
            shape((16, 48), f32),
            shape((4, PIECE, FF), bf),
            shape((PIECE, width), bf),
            shape((4, CHUNK, width), bf),
            shape((3, CHUNK, width), bf),
            shape((3, CHUNK, width), bf),
        ),
        in_specs=[hbm] * 9 + [smem] + [hbm] * 7,
        out_specs=[hbm] * 4 + [vmem] * 2 + [hbm] * 5,
        scratch_shapes=[
            pltpu.VMEM((width, 2048), bf),
            *[pltpu.VMEM((16, 2, 48, w), bf) for w in widths],
            *[pltpu.VMEM((16, 48, w), bf) for w in widths],
            *dense,
            *([pltpu.VMEM((4, PIECE, FF), bf)] * 3),
            pltpu.VMEM((4, PIECE, FF), bf),
            pltpu.VMEM((4 * PIECE, FF), bf),
            *([pltpu.VMEM((PIECE, width), bf)] * 3),
            pltpu.VMEM((2, PIECE, width), bf),
            pltpu.VMEM((4, 128, width), bf),
            pltpu.VMEM((2, CHUNK, width), bf),
            pltpu.VMEM((2 * QUERY_HEADS * 128, 128), bf),
            pltpu.VMEM((4, CHUNK, 512), bf),
            *([pltpu.VMEM((2, 128, 512), bf)] * 3),
            pltpu.VMEM((2, 128, 128), f32),
            *[pltpu.VMEM(ref.shape, ref.dtype) for ref in (cot, tok, q, kv, att, mixed)],
            pltpu.VMEM((CHUNK, width), bf),
            pltpu.VMEM((CHUNK, width), f32),
            pltpu.VMEM((2, 8, 128), f32),
            pltpu.VMEM((2, 8, 128), f32),
            pltpu.VMEM((16, width), f32),
            *([pltpu.VMEM((48, width), f32)] * 2),
            dma((24,)),
            dma((4,)),
            dma((7,)),
            dma((4,)),
            dma((4,)),
            dma((4,)),
            dma((3,)),
            dma((3,)),
            dma((6, 4)),
            dma((6, 4)),
            dma((6, 4)),
            dma((6, 4)),
            dma((6, 4)),
            dma((6, 4)),
            dma((4, 3)),
            dma((4, 3)),
            dma((4, 3)),
        ],
        compiler_params=pltpu.CompilerParams(
            collective_id=3, has_side_effects=True, vmem_limit_bytes=64 * 2**20 - 65536
        ),
        name="backward_stage",
    )(dx, dgt, gates, mixed, cot, tok, q, kv, att, lens, small, rope, wa, wb, gin, gout, outp)


def finish_kernel(
    block_in,
    dtok_in,
    gq_in,
    gb_in,
    gkv_in,
    small_ref,
    first_ref,
    second_ref,
    down_first_ref,
    down_second_ref,
    block_out,
    dtok_out,
    gq_out,
    gb_out,
    gkv_out,
    pre_out,
    mid_out,
    router_out,
    in_out,
    down_out,
):
    f32 = jnp.float32
    i = pl.program_id(0)
    block_out[...] = block_in[...]
    dtok_out[...] = dtok_in[...]
    gq_out[...] = gq_in[...]
    gb_out[...] = gb_in[...]
    gkv_out[...] = gkv_in[...]
    half = FF // 2
    first = first_ref[...].astype(f32)
    second = second_ref[...].astype(f32)
    in_out[:, :half] = first[:, :half]
    in_out[:, half:FF] = second[:, :half]
    in_out[:, FF : FF + half] = first[:, half:]
    in_out[:, FF + half :] = second[:, half:]
    down_out[...] = jnp.where(i < 2, down_first_ref[...], down_second_ref[...]).astype(f32)
    router_out[...] = small_ref[:8]
    pre_out[...] = small_ref[8:9]
    mid_out[...] = small_ref[9:10]


def finish_stage(block, dtok, gq, gb, gkv, small, first, second, down_first, down_second):
    f32 = jnp.float32
    shape = jax.ShapeDtypeStruct
    width = block.shape[-1]

    def rows(count, columns, index):
        return pl.BlockSpec((count, columns), index)

    def whole(count, columns):
        return pl.BlockSpec((count, columns), lambda i: (0, 0))

    return pl.pallas_call(
        finish_kernel,
        grid=(4,),
        out_shape=(
            shape(block.shape, block.dtype),
            shape(dtok.shape, f32),
            shape(gq.shape, f32),
            shape(gb.shape, f32),
            shape(gkv.shape, f32),
            shape((1, 48), f32),
            shape((1, 48), f32),
            shape((8, 48), f32),
            shape((384, 2 * FF), f32),
            shape((192, width), f32),
        ),
        in_specs=[
            rows(64, width, lambda i: (i, 0)),
            rows(64, width, lambda i: (i, 0)),
            whole(48, width),
            whole(48, width),
            whole(48, 512),
            whole(16, 48),
            rows(96, FF, lambda i: (i, 0)),
            rows(96, FF, lambda i: (i, 0)),
            rows(48, width, lambda i: (jnp.minimum(i, 1), 0)),
            rows(48, width, lambda i: (jnp.maximum(i - 2, 0), 0)),
        ],
        out_specs=[
            rows(64, width, lambda i: (i, 0)),
            rows(64, width, lambda i: (i, 0)),
            whole(48, width),
            whole(48, width),
            whole(48, 512),
            whole(1, 48),
            whole(1, 48),
            whole(8, 48),
            rows(96, 2 * FF, lambda i: (i, 0)),
            rows(48, width, lambda i: (i, 0)),
        ],
        name="finish_stage",
    )(block, dtok, gq, gb, gkv, small, first, second, down_first, down_second)


def rope_constant(slots):
    half = HEAD_SIZE // 2
    inv_freq = np.float32(rope_base) ** (-(np.arange(half, dtype=np.float32) * 2.0 / HEAD_SIZE))
    angles = np.arange(slots, dtype=np.float32)[:, None] * inv_freq[None, :].astype(np.float32)
    cos, sin = np.cos(angles), np.sin(angles)
    return np.stack(
        [np.concatenate([cos, cos], axis=1), np.concatenate([-sin, sin], axis=1)]
    ).astype(np.float32)


def fast_local(
    tokens,
    lengths,
    routes,
    prenorm,
    w_query,
    key_value_weight,
    w_output,
    midnorm,
    w_router,
    expert_in,
    expert_out,
    cotangent,
):
    seqs, token_rows, width = tokens.shape
    rows = seqs * token_rows
    tok = tokens.reshape(rows, width)
    cot = cotangent.reshape(rows, width)
    rope = jnp.asarray(rope_constant(token_rows * lax.axis_size("dp")))
    full_a, full_b, full_out, gall, q_rot, kv_all, attended, mixed, normed2, gates, small_t = attention_stage(
        tok,
        w_query,
        key_value_weight,
        w_router.T,
        prenorm[None],
        midnorm[None],
        w_output,
        cot,
        expert_out[0],
        rope,
        lengths,
        jnp.transpose(routes, (0, 2, 1)),
    )
    dx, dgate, outp, gin, gout, out_first, g_first = expert_stage(normed2, gall, gates, expert_in[0], full_out)
    block_out, grad_tokens, g_query, g_b, g_kv, small, g_second, out_second = backward_stage(
        dx, dgate, gates, mixed, cot, tok, q_rot, kv_all, attended, lengths, small_t, rope,
        full_a, full_b, gin.reshape(width, FF), gout, outp.reshape(8 * rows, width),
    )[:8]
    block_out, grad_tokens, g_query, g_b, g_kv, g_pre, g_mid, g_router, g_in, g_out = finish_stage(
        block_out,
        grad_tokens,
        g_query,
        g_b,
        g_kv,
        small,
        g_first.reshape(width // 4, FF),
        g_second.reshape(width // 4, FF),
        out_first.reshape(FF // 8, width),
        out_second,
    )
    return (
        block_out.reshape(seqs, token_rows, width),
        grad_tokens.reshape(seqs, token_rows, width),
        g_pre.reshape(-1),
        g_query,
        g_kv,
        g_b,
        g_mid.reshape(-1),
        g_router.T,
        g_in[None],
        g_out[None],
    )


def solution(mesh):
    placed = (
        P("expert", "dp", None),
        P("expert"),
        P("expert", "dp", None),
        P(("dp", "expert")),
        P(("dp", "expert"), None),
        P(("dp", "expert"), None),
        P(("dp", "expert"), None),
        P(("dp", "expert")),
        P(("dp", "expert"), None),
        P("expert", "dp", None),
        P("expert", "dp", None),
        P("expert", "dp", None),
    )
    fits = mesh.shape["dp"] == 4 and mesh.shape["expert"] == 8
    return jax.shard_map(
        fast_local if fits else local,
        mesh=mesh,
        in_specs=placed,
        out_specs=(
            P("expert", "dp", None),
            P("expert", "dp", None),
            P(("dp", "expert")),
            P(("dp", "expert"), None),
            P(("dp", "expert"), None),
            P(("dp", "expert"), None),
            P(("dp", "expert")),
            P(("dp", "expert"), None),
            P("expert", "dp", None),
            P("expert", "dp", None),
        ),
        check_vma=False,
    )
```

```python
import jax
import jax.numpy as jnp
import numpy as np
from jax import lax
from jax.experimental import pallas as pl
from jax.experimental.pallas import tpu as pltpu
from jax.sharding import PartitionSpec as P

QUERY_HEADS = 12
KEY_VALUE_HEADS = 2
HEAD_SIZE = 128
FF = 768
TOP = 4


epsilon = 1e-06
rope_base = 10000.0
highest = lax.Precision.HIGHEST


def rope_tables(positions):
    half_width = HEAD_SIZE // 2
    inv_freq = rope_base ** (-(jnp.arange(half_width, dtype=jnp.float32) * 2.0 / HEAD_SIZE))
    angles = positions.astype(jnp.float32)[:, None] * inv_freq[None, :]
    return (jnp.cos(angles), jnp.sin(angles))


def apply_rotation(values, cosine_table, sine_table):
    half_width = values.shape[-1] // 2
    first_half = values[..., :half_width]
    second = values[..., half_width:]
    cos_rows = cosine_table[:, None, :]
    sin_rows = sine_table[:, None, :]
    return jnp.concatenate(
        [first_half * cos_rows - second * sin_rows, second * cos_rows + first_half * sin_rows],
        axis=-1,
    )


def unrotate(values, cosine_table, sine_table):
    half_width = values.shape[-1] // 2
    first_half = values[..., :half_width]
    second = values[..., half_width:]
    cos_rows = cosine_table[:, None, :]
    sin_rows = sine_table[:, None, :]
    return jnp.concatenate(
        [first_half * cos_rows + second * sin_rows, second * cos_rows - first_half * sin_rows],
        axis=-1,
    )


def rms_parts(values):
    inverse = lax.rsqrt(jnp.mean(values * values, axis=-1, keepdims=True) + epsilon)
    return (values * inverse, inverse)


def norm_back(grad_normed, normalized_input, inverse, gain):
    scaled = grad_normed * gain
    return inverse * (
        scaled - normalized_input * jnp.mean(scaled * normalized_input, axis=-1, keepdims=True)
    )


def slot_index(route_rows, expert_count, capacity):
    flat_routes = route_rows.reshape(-1)
    onehot = (flat_routes[:, None] == jnp.arange(expert_count, dtype=jnp.int32)[None, :]).astype(
        jnp.int32
    )
    before = jnp.cumsum(onehot, axis=0) - onehot
    within = jnp.sum(before * onehot, axis=-1)
    return flat_routes * capacity + within


def masked_scores(query_matrix, key_rows, allowed):
    scores = jnp.einsum(
        "qhgd,khd->hgqk", query_matrix, key_rows, preferred_element_type=jnp.float32
    ) * HEAD_SIZE ** (-0.5)
    return jnp.where(allowed[None, None], scores, -1e30)


def local(
    tokens,
    lengths,
    routes,
    prenorm,
    w_query,
    key_value_weight,
    w_output,
    midnorm,
    w_router,
    expert_in,
    expert_out,
    cotangent,
):
    micro_count, token_rows, hidden_width = tokens.shape
    dp_size = lax.axis_size("dp")
    expert_size = lax.axis_size("expert")
    dp_rank = lax.axis_index("dp")
    local_experts = expert_in.shape[0]
    expert_count = local_experts * expert_size
    capacity = max(2, 3 * token_rows * TOP // (2 * expert_count))
    query_group_width = QUERY_HEADS // KEY_VALUE_HEADS
    expert_slot_total = token_rows * dp_size
    score_scale = HEAD_SIZE ** (-0.5)
    positions = dp_rank * token_rows + jnp.arange(token_rows, dtype=jnp.int32)
    key_pos = jnp.arange(expert_slot_total, dtype=jnp.int32)
    cosine_table, sine_table = rope_tables(positions)
    total_prenorm = jnp.zeros((hidden_width,), jnp.float32)
    total_query = jnp.zeros((hidden_width, QUERY_HEADS * HEAD_SIZE), jnp.float32)
    total_key_value = jnp.zeros((hidden_width, 2 * KEY_VALUE_HEADS * HEAD_SIZE), jnp.float32)
    total_output = jnp.zeros((QUERY_HEADS * HEAD_SIZE, hidden_width), jnp.float32)
    total_midnorm = jnp.zeros((hidden_width,), jnp.float32)
    total_router = jnp.zeros((hidden_width, expert_count), jnp.float32)
    total_upper = jnp.zeros((local_experts, hidden_width, 2 * FF), jnp.float32)
    total_down = jnp.zeros((local_experts, FF, hidden_width), jnp.float32)
    outputs_list = []
    grads_list = []
    for micro_step in range(micro_count):
        dense_all = (
            lax.all_gather(prenorm, ("dp", "expert"), axis=0, tiled=True),
            lax.all_gather(w_query, ("dp", "expert"), axis=0, tiled=True),
            lax.all_gather(key_value_weight, ("dp", "expert"), axis=0, tiled=True),
            lax.all_gather(w_output, ("dp", "expert"), axis=0, tiled=True),
            lax.all_gather(midnorm, ("dp", "expert"), axis=0, tiled=True),
            lax.all_gather(w_router, ("dp", "expert"), axis=0, tiled=True),
        )
        expert_all = (
            lax.all_gather(expert_in, "dp", axis=1, tiled=True),
            lax.all_gather(expert_out, "dp", axis=1, tiled=True),
        )
        gain_one = dense_all[0].astype(jnp.float32)
        query_all = dense_all[1]
        keyval_all = dense_all[2]
        output_all = dense_all[3]
        gain_two = dense_all[4].astype(jnp.float32)
        router_all = dense_all[5]
        gateup_all = expert_all[0]
        down_all = expert_all[1]
        input_rows = tokens[micro_step].astype(jnp.float32)
        length = lengths[micro_step]
        route_rows = routes[micro_step]
        live_rows = (positions < length)[:, None]
        normed_one, inverse_one = rms_parts(input_rows)
        normalized_input = (normed_one * gain_one).astype(jnp.bfloat16)
        query_pre = jnp.dot(
            normalized_input, query_all, preferred_element_type=jnp.float32
        ).reshape(token_rows, QUERY_HEADS, HEAD_SIZE)
        keyval_pre = jnp.dot(
            normalized_input, keyval_all, preferred_element_type=jnp.float32
        ).reshape(token_rows, 2, KEY_VALUE_HEADS, HEAD_SIZE)
        query_matrix = (
            apply_rotation(query_pre, cosine_table, sine_table)
            .astype(jnp.bfloat16)
            .reshape(token_rows, KEY_VALUE_HEADS, query_group_width, HEAD_SIZE)
        )
        local_key_rows = apply_rotation(keyval_pre[:, 0], cosine_table, sine_table).astype(
            jnp.bfloat16
        )
        local_value_rows = keyval_pre[:, 1].astype(jnp.bfloat16)
        packed_tokens = jnp.stack([local_key_rows, local_value_rows], axis=1).reshape(
            token_rows, 2 * KEY_VALUE_HEADS * HEAD_SIZE
        )
        gathered_rows = lax.all_gather(packed_tokens, "dp", axis=0, tiled=True).reshape(
            expert_slot_total, 2, KEY_VALUE_HEADS, HEAD_SIZE
        )
        key_rows = gathered_rows[:, 0]
        value_rows = gathered_rows[:, 1]
        allowed = (key_pos[None, :] <= positions[:, None]) & (key_pos[None, :] < length)
        scores = masked_scores(query_matrix, key_rows, allowed)
        top_score = jnp.max(scores, axis=-1, keepdims=True)
        weights = jnp.exp(scores - top_score)
        weight_total = jnp.sum(weights, axis=-1, keepdims=True)
        log_total = top_score + jnp.log(weight_total)
        probs_low = (weights / weight_total).astype(jnp.bfloat16)
        attended = jnp.einsum(
            "hgqk,khd->qhgd", probs_low, value_rows, preferred_element_type=jnp.float32
        )
        attended = attended.reshape(token_rows, QUERY_HEADS * HEAD_SIZE).astype(jnp.bfloat16)
        mixed_rows = input_rows + jnp.dot(attended, output_all, preferred_element_type=jnp.float32)
        normed_mid, inverse_two = rms_parts(mixed_rows)
        normed_two = (normed_mid * gain_two).astype(jnp.bfloat16)
        logits = jnp.dot(normed_two, router_all, preferred_element_type=jnp.float32)
        onehot = (
            route_rows[:, :, None] == jnp.arange(expert_count, dtype=jnp.int32)[None, None, :]
        ).astype(jnp.float32)
        chosen = jnp.sum(onehot * logits[:, None, :], axis=-1)
        gate_values = jax.nn.softmax(chosen, axis=-1)
        slot_idx = slot_index(route_rows, expert_count, capacity)
        send_rows = jnp.zeros((expert_count * capacity, hidden_width), jnp.bfloat16)
        send_rows = send_rows.at[slot_idx].set(jnp.repeat(normed_two, TOP, axis=0))
        received = lax.all_to_all(
            send_rows.reshape(expert_count, capacity, hidden_width),
            "expert",
            split_axis=0,
            concat_axis=0,
            tiled=True,
        )
        item_count = received.shape[1]
        grouped = received.reshape(expert_size, local_experts, item_count, hidden_width)
        gate_up = jnp.einsum(
            "slcd,ldf->slcf", grouped, gateup_all, preferred_element_type=jnp.float32
        )
        hidden = (jax.nn.silu(gate_up[..., :FF]) * gate_up[..., FF:]).astype(jnp.bfloat16)
        result = jnp.einsum(
            "slcf,lfd->slcd", hidden, down_all, preferred_element_type=jnp.float32
        ).astype(jnp.bfloat16)
        back_rows = lax.all_to_all(
            result.reshape(expert_count, item_count, hidden_width),
            "expert",
            split_axis=0,
            concat_axis=0,
            tiled=True,
        )
        back_rows, kept_rows, kept_gateup = (
            back_rows,
            received,
            gate_up.reshape(expert_count, item_count, 2 * FF),
        )
        returned = back_rows.reshape(expert_count * capacity, hidden_width)[slot_idx].reshape(
            token_rows, TOP, hidden_width
        )
        returned_wide = returned.astype(jnp.float32)
        expert_sum = jnp.sum(gate_values[:, :, None] * returned_wide, axis=1)
        final_rows = jnp.where(live_rows, mixed_rows + expert_sum, 0.0)
        outputs_list.append(final_rows.astype(jnp.bfloat16))
        grad_rows = jnp.where(live_rows, cotangent[micro_step].astype(jnp.float32), 0.0)
        grad_gate = jnp.sum(grad_rows[:, None, :] * returned_wide, axis=-1)
        grad_chosen = gate_values * (
            grad_gate - jnp.sum(gate_values * grad_gate, axis=-1, keepdims=True)
        )
        grad_logits = jnp.sum(onehot * grad_chosen[:, :, None], axis=1)
        router_term = jnp.dot(normed_two.astype(jnp.float32).T, grad_logits, precision=highest)
        grad_normtwo = jnp.dot(grad_logits, router_all.astype(jnp.float32).T, precision=highest)
        grad_result = (
            (gate_values[:, :, None] * grad_rows[:, None, :])
            .astype(jnp.bfloat16)
            .reshape(token_rows * TOP, hidden_width)
        )
        send_grads = (
            jnp.zeros((expert_count * capacity, hidden_width), jnp.bfloat16)
            .at[slot_idx]
            .set(grad_result)
        )
        recv_grads, again_rows = (
            lax.all_to_all(
                send_grads.reshape(expert_count, capacity, hidden_width),
                "expert",
                split_axis=0,
                concat_axis=0,
                tiled=True,
            ),
            lax.all_to_all(
                send_rows.reshape(expert_count, capacity, hidden_width),
                "expert",
                split_axis=0,
                concat_axis=0,
                tiled=True,
            ),
        )
        grouped_rows = again_rows.reshape(expert_size, local_experts, capacity, hidden_width)
        gate_up = jnp.einsum(
            "slcd,ldf->slcf", grouped_rows, gateup_all, preferred_element_type=jnp.float32
        )
        grouped_grads = recv_grads.reshape(expert_size, local_experts, capacity, hidden_width)
        gate_part = gate_up[..., :FF]
        up_part = gate_up[..., FF:]
        sigmoid_gate = jax.nn.sigmoid(gate_part)
        silu_gate = gate_part * sigmoid_gate
        hidden = (silu_gate * up_part).astype(jnp.bfloat16)
        grad_hidden = jnp.einsum(
            "slcd,lfd->slcf", grouped_grads, down_all, preferred_element_type=jnp.float32
        )
        down_term = jnp.einsum(
            "slcf,slcd->lfd", hidden, grouped_grads, preferred_element_type=jnp.float32
        )
        grad_gatepart = (
            grad_hidden * up_part * sigmoid_gate * (1.0 + gate_part * (1.0 - sigmoid_gate))
        )
        grad_gateup = jnp.concatenate([grad_gatepart, grad_hidden * silu_gate], axis=-1).astype(
            jnp.bfloat16
        )
        upper_term = jnp.einsum(
            "slcd,slcf->ldf", grouped_rows, grad_gateup, preferred_element_type=jnp.float32
        )
        grad_copies = jnp.einsum(
            "slcf,ldf->slcd", grad_gateup, gateup_all, preferred_element_type=jnp.float32
        ).astype(jnp.bfloat16)
        back_grads = lax.all_to_all(
            grad_copies.reshape(expert_count, capacity, hidden_width),
            "expert",
            split_axis=0,
            concat_axis=0,
            tiled=True,
        )
        copy_rows = back_grads.reshape(expert_count * capacity, hidden_width)[slot_idx].reshape(
            token_rows, TOP, hidden_width
        )
        grad_normtwo = grad_normtwo + jnp.sum(copy_rows.astype(jnp.float32), axis=1)
        midnorm_term = jnp.sum(grad_normtwo * normed_mid, axis=0)
        grad_mixed = grad_rows + norm_back(grad_normtwo, normed_mid, inverse_two, gain_two)
        grad_proj = grad_mixed.astype(jnp.bfloat16)
        output_term = jnp.dot(attended.T, grad_proj, preferred_element_type=jnp.float32)
        attention_gradient = jnp.dot(
            grad_proj, output_all.T, preferred_element_type=jnp.float32
        ).astype(jnp.bfloat16)
        attention_gradient = attention_gradient.reshape(
            token_rows, KEY_VALUE_HEADS, query_group_width, HEAD_SIZE
        )
        scores = masked_scores(query_matrix, key_rows, allowed)
        prob_rows = jnp.exp(scores - log_total)
        grad_probs = jnp.einsum(
            "qhgd,khd->hgqk", attention_gradient, value_rows, preferred_element_type=jnp.float32
        )
        row_delta = jnp.sum(prob_rows * grad_probs, axis=-1, keepdims=True)
        grad_scores = (prob_rows * (grad_probs - row_delta)).astype(jnp.bfloat16)
        prob_low = prob_rows.astype(jnp.bfloat16)
        grad_qrot = (
            jnp.einsum("hgqk,khd->qhgd", grad_scores, key_rows, preferred_element_type=jnp.float32)
            * score_scale
        )
        grad_keys = (
            jnp.einsum(
                "hgqk,qhgd->khd", grad_scores, query_matrix, preferred_element_type=jnp.float32
            )
            * score_scale
        )
        grad_vals = jnp.einsum(
            "hgqk,qhgd->khd", prob_low, attention_gradient, preferred_element_type=jnp.float32
        )
        own_keys = (
            lax.psum_scatter(
                jnp.stack([grad_keys, grad_vals], axis=1)
                .reshape(lax.axis_size("dp") * token_rows, 2 * KEY_VALUE_HEADS * HEAD_SIZE)
                .astype(jnp.bfloat16),
                "dp",
                scatter_dimension=0,
                tiled=True,
            )
            .astype(jnp.float32)
            .reshape(token_rows, 2, KEY_VALUE_HEADS, HEAD_SIZE)
        )
        grad_query = (
            unrotate(
                grad_qrot.reshape(token_rows, QUERY_HEADS, HEAD_SIZE), cosine_table, sine_table
            )
            .astype(jnp.bfloat16)
            .reshape(token_rows, QUERY_HEADS * HEAD_SIZE)
        )
        key_gradient = unrotate(own_keys[:, 0], cosine_table, sine_table).astype(jnp.bfloat16)
        value_gradient = own_keys[:, 1].astype(jnp.bfloat16)
        key_value_weight_gradient = jnp.stack([key_gradient, value_gradient], axis=1).reshape(
            token_rows, 2 * KEY_VALUE_HEADS * HEAD_SIZE
        )
        query_term = jnp.dot(normalized_input.T, grad_query, preferred_element_type=jnp.float32)
        keyval_term = jnp.dot(
            normalized_input.T, key_value_weight_gradient, preferred_element_type=jnp.float32
        )
        grad_normone = jnp.dot(grad_query, query_all.T, preferred_element_type=jnp.float32)
        grad_normone = grad_normone + jnp.dot(
            key_value_weight_gradient, keyval_all.T, preferred_element_type=jnp.float32
        )
        prenorm_term = jnp.sum(grad_normone * normed_one, axis=0)
        grads_list.append(grad_mixed + norm_back(grad_normone, normed_one, inverse_one, gain_one))
        total_prenorm = total_prenorm + prenorm_term
        total_query = total_query + query_term
        total_key_value = total_key_value + keyval_term
        total_output = total_output + output_term
        total_midnorm = total_midnorm + midnorm_term
        total_router = total_router + router_term
        total_upper = total_upper + upper_term
        total_down = total_down + down_term
    dense_grads = (
        lax.psum_scatter(total_prenorm, ("dp", "expert"), scatter_dimension=0, tiled=True),
        lax.psum_scatter(total_query, ("dp", "expert"), scatter_dimension=0, tiled=True),
        lax.psum_scatter(total_key_value, ("dp", "expert"), scatter_dimension=0, tiled=True),
        lax.psum_scatter(total_output, ("dp", "expert"), scatter_dimension=0, tiled=True),
        lax.psum_scatter(total_midnorm, ("dp", "expert"), scatter_dimension=0, tiled=True),
        lax.psum_scatter(total_router, ("dp", "expert"), scatter_dimension=0, tiled=True),
    )
    expert_grads = (
        lax.psum_scatter(
            total_upper.astype(jnp.bfloat16), "dp", scatter_dimension=1, tiled=True
        ).astype(jnp.float32),
        lax.psum_scatter(
            total_down.astype(jnp.bfloat16), "dp", scatter_dimension=1, tiled=True
        ).astype(jnp.float32),
    )
    return (
        jnp.stack(outputs_list),
        jnp.stack(grads_list),
        dense_grads[0],
        dense_grads[1],
        dense_grads[2],
        dense_grads[3],
        dense_grads[4],
        dense_grads[5],
        expert_grads[0],
        expert_grads[1],
    )


MESH = pl.DeviceIdType.MESH
CHUNK = 256
PIECE = 96


def remote(src, dst, send_sem, recv_sem, target):
    return pltpu.make_async_remote_copy(
        src_ref=src,
        dst_ref=dst,
        send_sem=send_sem,
        recv_sem=recv_sem,
        device_id=target,
        device_id_type=MESH,
    )


def place():
    d = lax.axis_index("dp")
    e = lax.axis_index("expert")
    z = lax.div(e, 2)
    c = lax.rem(e, 2)
    x = lax.rem(d, 2)
    y = lax.div(d, 2)
    return d, e, z, c, x, y


def attention_kernel(
    tok_hbm,
    wq_hbm,
    wkv_hbm,
    wr_ref,
    pre_ref,
    mid_ref,
    wb_hbm,
    cot_hbm,
    wo_hbm,
    rope_hbm,
    lens_ref,
    routes_ref,
    wa_out,
    wb_out,
    wo_out,
    gall,
    q_out,
    kv_out,
    att_out,
    mixed_hbm,
    normed_hbm,
    gates_out,
    small_out,
    wa,
    wb,
    qs,
    kvs,
    att,
    g_own,
    rope,
    tok_ref,
    cot_ref,
    mixed_out,
    normed_out,
    own_sem,
    wo_recv,
    wo_send,
    z_recv,
    z_send,
    xy_recv,
    xy_send,
    sib_recv,
    sib_send,
    g_recv,
    g_send,
    gs_recv,
    gs_send,
    kv_recv,
    kv_send,
):
    bf, f32 = jnp.bfloat16, jnp.float32
    d, e, z, c, x, y = place()
    d_x = d + 1 - 2 * x
    d_y = d + 2 - 4 * y
    d_d = 3 - d
    other = 1 - c
    to_x = (d_x, e)
    to_y = (d_y, e)
    to_sib = (d, 2 * z + other)
    to_up = (d, e + jnp.where(z < 3, 2, -2))
    to_down = (d, e + jnp.where(z > 0, -2, 2))

    barrier = pltpu.get_barrier_semaphore()
    for target in (to_x, to_y, to_sib):
        pl.semaphore_signal(barrier, inc=1, device_id=target, device_id_type=MESH)

    @pl.when(z < 3)
    def _():
        pl.semaphore_signal(barrier, inc=1, device_id=to_up, device_id_type=MESH)

    @pl.when(z > 0)
    def _():
        pl.semaphore_signal(barrier, inc=1, device_id=to_down, device_id_type=MESH)

    own_at = pl.multiple_of((d * 8 + e) * 48, 16)
    own_rows = pl.ds(own_at, 48)
    own_a = [
        pltpu.make_async_copy(wq_hbm, wa.at[own_rows, pl.ds(0, 1536)], own_sem.at[0]),
        pltpu.make_async_copy(wkv_hbm, wa.at[own_rows, pl.ds(1536, 512)], own_sem.at[1]),
        pltpu.make_async_copy(rope_hbm.at[:, pl.ds(pl.multiple_of(d * 128, 128), 128)], rope, own_sem.at[2]),
    ]
    loads = [
        pltpu.make_async_copy(cot_hbm, cot_ref, own_sem.at[8]),
        pltpu.make_async_copy(tok_hbm, tok_ref, own_sem.at[9]),
    ]
    for copy in own_a + loads:
        copy.start()
    eye = lax.broadcasted_iota(jnp.int32, (128, 128), 0) == lax.broadcasted_iota(
        jnp.int32, (128, 128), 1
    )
    eye_low = eye.astype(bf)
    turned = (((0,), (0,)), ((), ()))
    sub = lax.broadcasted_iota(jnp.int32, (8, 48), 0)
    gains = jnp.where(
        sub == 0,
        pre_ref[...].astype(f32),
        jnp.where(sub == 1, mid_ref[...].astype(f32), 0.0),
    )
    tile = jnp.concatenate([wr_ref[...].astype(f32), gains], axis=0).astype(bf)
    wa[own_rows, 2048:] = lax.dot_general(
        tile, eye_low[:16], turned, preferred_element_type=f32
    ).astype(bf)
    full = (wa, wb)
    shard = (None, wb_hbm)

    def block(a, dd, zp, lane):
        at = pl.multiple_of((dd * 8 + 2 * zp + lane) * 48, 16)
        return full[a].at[pl.ds(at, 48)]

    def z_copy(a, zp, way, src=None):
        ref = block(a, d, zp, c)
        return remote(
            ref if src is None else src,
            ref,
            z_send.at[a, way, zp],
            z_recv.at[a, zp],
            to_up if way == 0 else to_down,
        )

    def xy_copy(a, dd, zp, row, target, src=None):
        ref = block(a, dd, zp, c)
        return remote(
            ref if src is None else src,
            ref,
            xy_send.at[a, row, zp],
            xy_recv.at[a, row, zp],
            target,
        )

    def s_copy(a, dd, zp, src=None, lane=None):
        ref = block(a, dd, zp, c if lane is None else lane)
        return remote(
            ref if src is None else src,
            ref,
            sib_send.at[a, dd, zp],
            sib_recv.at[a, dd, zp],
            to_sib,
        )

    def send_xy(a, zp):
        xy_copy(a, d, zp, 0, to_x).start()
        xy_copy(a, d, zp, 1, to_y).start()

    def own_start(a):
        @pl.when(z < 3)
        def _():
            z_copy(a, z, 0, shard[a]).start()

        @pl.when(z > 0)
        def _():
            z_copy(a, z, 1, shard[a]).start()

        s_copy(a, d, z, shard[a]).start()

    def from_z(a, k):
        def arrived(zp, way):
            z_copy(a, zp, way).wait_recv()

            @pl.when((z < 3) if way == 0 else (z > 0))
            def _():
                z_copy(a, zp, way).start()

            if a == 0:
                send_xy(a, zp)
            s_copy(a, d, zp).start()

        @pl.when(z - k >= 0)
        def _():
            arrived(z - k, 0)

        @pl.when(z + k <= 3)
        def _():
            arrived(z + k, 1)

    def from_xy_one(a, zp):
        xy_copy(a, d_x, zp, 0, to_x).wait_recv()

        @pl.when(lax.rem(zp, 2) == 0)
        def _():
            xy_copy(a, d_x, zp, 2, to_y).start()

        s_copy(a, d_x, zp).start()
        xy_copy(a, d_y, zp, 1, to_y).wait_recv()

        @pl.when(lax.rem(zp, 2) == 1)
        def _():
            xy_copy(a, d_y, zp, 2, to_x).start()

        s_copy(a, d_y, zp).start()

    def from_xy(a, k):
        @pl.when(z - k >= 0)
        def _():
            from_xy_one(a, z - k)

        if k > 0:

            @pl.when(z + k <= 3)
            def _():
                from_xy_one(a, z + k)

    def from_diag(a):
        for k in range(4):
            zp = lax.rem(z + k, 4)
            xy_copy(a, d_d, zp, 2, to_x).wait_recv()
            s_copy(a, d_d, zp).start()

    def from_sib(a):
        for dd in range(4):
            for zp in range(4):
                s_copy(a, dd, zp, lane=other).wait_recv()

    def drain(a):
        for zp in range(4):
            for dd in range(4):
                s_copy(a, dd, zp).wait_send()
            for row in range(3):
                xy_copy(a, d, zp, row, to_x).wait_send()

            @pl.when((zp <= z) & (z < 3))
            def _():
                z_copy(a, zp, 0).wait_send()

            @pl.when((zp >= z) & (z > 0))
            def _():
                z_copy(a, zp, 1).wait_send()

    def g_part(zp, lane, s):
        at = pl.multiple_of((2 * zp + lane) * CHUNK + s * 128, 128)
        return gall.at[pl.ds(at, 128)]

    def g_copy(zp, s, way, src=None):
        ref = g_part(zp, c, s)
        return remote(
            ref if src is None else src,
            ref,
            g_send.at[way, zp, s],
            g_recv.at[zp, s],
            to_up if way == 0 else to_down,
        )

    def gs_copy(zp, s, src=None, lane=None):
        ref = g_part(zp, c if lane is None else lane, s)
        return remote(
            ref if src is None else src, ref, gs_send.at[zp, s], gs_recv.at[zp, s], to_sib
        )

    def g_start():
        for s in range(2):
            src = g_own.at[pl.ds(s * 128, 128)]

            @pl.when(z < 3)
            def _():
                g_copy(z, s, 0, src).start()

            @pl.when(z > 0)
            def _():
                g_copy(z, s, 1, src).start()

            gs_copy(z, s, src).start()

    def g_pass(k, s):
        @pl.when(z - k >= 0)
        def _():
            g_copy(z - k, s, 0).wait_recv()

            @pl.when(z < 3)
            def _():
                g_copy(z - k, s, 0).start()

            gs_copy(z - k, s).start()

        @pl.when(z + k <= 3)
        def _():
            g_copy(z + k, s, 1).wait_recv()

            @pl.when(z > 0)
            def _():
                g_copy(z + k, s, 1).start()

            gs_copy(z + k, s).start()

    def wo_copy(dd, p, row, target, src=None):
        ref = wo_out.at[pl.ds(pl.multiple_of(dd * 192 + p * PIECE, 16), PIECE)]
        return remote(
            ref if src is None else src, ref, wo_send.at[row, p], wo_recv.at[row, p], target
        )

    def wo_start(p):
        wo_copy(d, p, 0, to_x, wo_hbm.at[pl.ds(p * PIECE, PIECE)]).start()
        wo_copy(d, 1 - p, 1, to_y, wo_hbm.at[pl.ds((1 - p) * PIECE, PIECE)]).start()

    def wo_pass():
        wo_copy(d_x, 0, 0, to_x).wait_recv()
        wo_copy(d_x, 0, 2, to_y).start()
        wo_copy(d_y, 1, 1, to_y).wait_recv()
        wo_copy(d_y, 1, 2, to_x).start()

    def wo_rest():
        wo_copy(d_x, 1, 0, to_x).wait_recv()
        wo_copy(d_y, 0, 1, to_y).wait_recv()
        for p in range(2):
            wo_copy(d_d, p, 2, to_x).wait_recv()

    pl.semaphore_wait(barrier, 5 - jnp.where((z == 0) | (z == 3), 1, 0))
    for copy in own_a:
        copy.wait()
    own_start(0)
    own_start(1)
    own = [
        pltpu.make_async_copy(wb_hbm, block(1, d, z, c), own_sem.at[0]),
        pltpu.make_async_copy(
            g_own, gall.at[pl.ds(pl.multiple_of(e * CHUNK, CHUNK), CHUNK)], own_sem.at[1]
        ),
        pltpu.make_async_copy(
            wo_hbm, wo_out.at[pl.ds(pl.multiple_of(d * 192, 16), 192)], own_sem.at[2]
        ),
    ]
    own[0].start()
    own[2].start()
    send_xy(0, z)
    own[0].wait()
    at_end = (z == 0) | (z == 3)

    @pl.when(at_end)
    def _():
        send_xy(1, z)

    loads[0].wait()
    for s in range(2):
        rows = slice(s * 128, (s + 1) * 128)
        slot = d * 128 + lax.broadcasted_iota(jnp.int32, (128, 1), 0)
        g_own[rows] = jnp.where(slot < lens_ref[s], cot_ref[rows].astype(f32), 0.0).astype(bf)

    own[1].start()
    loads[1].wait()
    tok = tok_ref[...].astype(f32)
    n1 = tok * lax.rsqrt(jnp.mean(tok * tok, axis=1, keepdims=True) + epsilon)
    from_z(0, 1)
    from_z(1, 1)
    from_xy(0, 0)
    from_z(0, 2)
    from_z(1, 2)
    g_start()
    from_xy(0, 1)
    from_z(0, 3)
    from_z(1, 3)
    from_xy(0, 2)
    from_xy(0, 3)

    def turn(j):
        return lax.rem(z + j, 4)

    @pl.when(jnp.logical_not(at_end))
    def _():
        send_xy(1, z)

    send_xy(1, turn(1))
    from_diag(0)
    from_sib(0)

    small_t = lax.dot_general(
        eye_low[:16], wa[:, 2048:], (((1,), (1,)), ((), ())), preferred_element_type=f32
    )
    small_out[...] = small_t
    normed = (n1 * small_t[8:9]).astype(bf)
    cos_rows = jnp.concatenate([rope[0]] * 2, axis=0)
    sin_rows = jnp.concatenate([rope[1]] * 2, axis=0)

    def rotate(v):
        return v * cos_rows + pltpu.roll(v, 64, 1) * sin_rows

    kv = jnp.dot(normed, wa[:, 1536:2048], preferred_element_type=f32)
    for h in range(2):
        kvs[d, :, h * 128 : (h + 1) * 128] = rotate(kv[:, h * 128 : (h + 1) * 128]).astype(bf)
    kvs[d, :, 256:] = kv[:, 256:].astype(bf)

    def kv_copy(dd, s, row, target):
        ref = kvs.at[dd, pl.ds(s * 128, 128)]
        return remote(ref, ref, kv_send.at[row, s], kv_recv.at[row, s], target)

    for s in range(2):
        kv_copy(d, s, 0, to_x).start()
        kv_copy(d, 1 - s, 1, to_y).start()
    send_xy(1, turn(2))
    g_pass(1, 0)
    q = jnp.dot(normed, wa[:, :1536], preferred_element_type=f32)
    for head in range(QUERY_HEADS):
        rot = rotate(q[:, head * 128 : (head + 1) * 128]).astype(bf)
        for s in range(2):
            at = (s * QUERY_HEADS + head) * 128
            qs[at : at + 128] = rot[s * 128 : (s + 1) * 128]
    kv_copy(d_x, 0, 0, to_x).wait_recv()
    kv_copy(d_x, 0, 2, to_y).start()
    kv_copy(d_y, 1, 1, to_y).wait_recv()
    kv_copy(d_y, 1, 2, to_x).start()
    send_xy(1, turn(3))
    for j in range(2):
        from_xy_one(1, turn(j))
    g_pass(1, 1)
    kv_copy(d_y, 0, 1, to_y).wait_recv()
    kv_copy(d_x, 1, 0, to_x).wait_recv()
    for s in range(2):
        kv_copy(d_d, s, 2, to_x).wait_recv()
    q_copy = pltpu.make_async_copy(qs, q_out, own_sem.at[3])
    kvo_copy = pltpu.make_async_copy(kvs, kv_out, own_sem.at[4])
    wa_copy = pltpu.make_async_copy(wa, wa_out, own_sem.at[5])
    for copy in (q_copy, kvo_copy, wa_copy):
        copy.start()

    query_pos = d * 128 + lax.broadcasted_iota(jnp.int32, (128, 512), 0)
    key_pos = lax.broadcasted_iota(jnp.int32, (128, 512), 1)

    def attend(n):
        s = lax.div(n, 2)
        h = lax.rem(n, 2)
        lens = lens_ref[s]
        allowed = (key_pos <= query_pos) & (key_pos < lens)
        ks = kvs[:, pl.ds(pl.multiple_of(s * 128, 128), 128), pl.ds(pl.multiple_of(h * 128, 128), 128)]
        vs = kvs[:, pl.ds(pl.multiple_of(s * 128, 128), 128), pl.ds(pl.multiple_of(256 + h * 128, 128), 128)]
        ks = ks.reshape(512, 128)
        vs = vs.reshape(512, 128)
        for half in range(2):
            qh = qs[pl.ds(pl.multiple_of(n * 768 + half * 384, 128), 384)]
            scores = lax.dot_general(qh, ks, (((1,), (1,)), ((), ())), preferred_element_type=f32)
            scores = scores.reshape(3, 128, 512) * HEAD_SIZE ** (-0.5)
            scores = jnp.where(allowed[None], scores, -1e30)
            top = jnp.max(scores, axis=-1, keepdims=True)
            weights = jnp.exp(scores - top)
            weights = weights * (1.0 / jnp.sum(weights, axis=-1, keepdims=True))
            out = jnp.dot(
                weights.astype(bf).reshape(384, 512), vs, preferred_element_type=f32
            ).astype(bf)
            for j in range(3):
                att[
                    pl.ds(pl.multiple_of(s * 128, 128), 128),
                    pl.ds(pl.multiple_of(h * 768 + (half * 3 + j) * 128, 128), 128),
                ] = out[j * 128 : (j + 1) * 128]

    wo_start(0)
    g_pass(2, 0)
    pl.loop(0, 2)(attend)
    from_xy_one(1, turn(2))
    from_xy_one(1, turn(3))
    wo_start(1)
    g_pass(2, 1)

    @pl.loop(2, 4)
    def _(n):
        attend(n)
        pl.when(n == 2)(wo_pass)

    from_diag(1)
    from_sib(1)
    att_copy = pltpu.make_async_copy(att, att_out, own_sem.at[6])
    wb_copy = pltpu.make_async_copy(wb, wb_out, own_sem.at[7])
    att_copy.start()
    wb_copy.start()
    mixed = tok_ref[...].astype(f32) + jnp.dot(att[...], wb[...], preferred_element_type=f32)
    mixed_out[...] = mixed
    mixed_copy = pltpu.make_async_copy(mixed_out, mixed_hbm, own_sem.at[10])
    mixed_copy.start()
    n2 = mixed * lax.rsqrt(jnp.mean(mixed * mixed, axis=1, keepdims=True) + epsilon)
    normed2 = (n2 * small_t[9:10]).astype(bf)
    normed_out[...] = normed2
    normed_copy = pltpu.make_async_copy(normed_out, normed_hbm, own_sem.at[11])
    normed_copy.start()
    logits = lax.dot_general(
        small_t[:8].astype(bf), normed2, (((1,), (1,)), ((), ())), preferred_element_type=f32
    )
    number = lax.broadcasted_iota(jnp.int32, (8, 128), 0)
    for s in range(2):
        chosen = number == routes_ref[s, 0:1]
        for t in range(1, TOP):
            chosen = chosen | (number == routes_ref[s, t : t + 1])
        picked = jnp.where(chosen, logits[:, s * 128 : (s + 1) * 128], -1e30)
        top = jnp.max(picked, axis=0, keepdims=True)
        weights = jnp.where(chosen, jnp.exp(picked - top), 0.0)
        gates_out[s] = weights / jnp.sum(weights, axis=0, keepdims=True)

    g_pass(3, 0)
    g_pass(3, 1)
    wo_rest()
    for zp in range(4):
        for s in range(2):
            gs_copy(zp, s, lane=other).wait_recv()
    own[1].wait()
    own[2].wait()
    for copy in (q_copy, kvo_copy, wa_copy, att_copy, wb_copy, mixed_copy, normed_copy):
        copy.wait()
    drain(0)
    drain(1)
    for s in range(2):
        for row in range(3):
            kv_copy(d, s, row, to_x).wait_send()
            wo_copy(d, s, row, to_x).wait_send()
        for zp in range(4):
            gs_copy(zp, s).wait_send()

            @pl.when((zp <= z) & (z < 3))
            def _():
                g_copy(zp, s, 0).wait_send()

            @pl.when((zp >= z) & (z > 0))
            def _():
                g_copy(zp, s, 1).wait_send()


def attention_stage(tok, wq, wkv, wr, pre, mid, wb, cot, wo, rope, lens, routes):
    bf, f32 = jnp.bfloat16, jnp.float32
    shape = jax.ShapeDtypeStruct
    width = tok.shape[-1]
    wide = wq.shape[-1] + wkv.shape[-1] + 128
    hbm = pl.BlockSpec(memory_space=pltpu.HBM)
    vmem = pl.BlockSpec(memory_space=pltpu.VMEM)
    smem = pl.BlockSpec(memory_space=pltpu.SMEM)
    dma = pltpu.SemaphoreType.DMA
    return pl.pallas_call(
        attention_kernel,
        out_shape=(
            shape((width, wide), bf),
            shape((width, width), bf),
            shape((FF, width), bf),
            shape((8 * CHUNK, width), bf),
            shape((2 * QUERY_HEADS * 128, 128), bf),
            shape((4, CHUNK, 512), bf),
            shape((CHUNK, width), bf),
            shape((CHUNK, width), f32),
            shape((CHUNK, width), bf),
            shape((2, 8, 128), f32),
            shape((16, width), f32),
        ),
        in_specs=[hbm, hbm, hbm, vmem, vmem, vmem, hbm, hbm, hbm, hbm, smem, vmem],
        out_specs=[hbm] * 9 + [vmem] * 2,
        scratch_shapes=[
            pltpu.VMEM((width, wide), bf),
            pltpu.VMEM((width, width), bf),
            pltpu.VMEM((2 * QUERY_HEADS * 128, 128), bf),
            pltpu.VMEM((4, CHUNK, 512), bf),
            pltpu.VMEM((CHUNK, width), bf),
            pltpu.VMEM((CHUNK, width), bf),
            pltpu.VMEM((2, 128, 128), f32),
            pltpu.VMEM((CHUNK, width), bf),
            pltpu.VMEM((CHUNK, width), bf),
            pltpu.VMEM((CHUNK, width), f32),
            pltpu.VMEM((CHUNK, width), bf),
            dma((12,)),
            dma((3, 2)),
            dma((3, 2)),
            dma((2, 4)),
            dma((2, 2, 4)),
            dma((2, 3, 4)),
            dma((2, 3, 4)),
            dma((2, 4, 4)),
            dma((2, 4, 4)),
            dma((4, 2)),
            dma((2, 4, 2)),
            dma((4, 2)),
            dma((4, 2)),
            dma((3, 2)),
            dma((3, 2)),
        ],
        compiler_params=pltpu.CompilerParams(
            collective_id=2, has_side_effects=True, vmem_limit_bytes=60 * 2**20
        ),
        name="attention_stage",
    )(tok, wq, wkv, wr, pre, mid, wb, cot, wo, rope, lens, routes)


def expert_kernel(
    x_hbm,
    g_hbm,
    gt_hbm,
    win_hbm,
    wout_hbm,
    dx_hbm,
    dgt_out,
    outp_hbm,
    gin_hbm,
    gout_hbm,
    gout_first_hbm,
    gin_first_hbm,
    win,
    wout,
    xall,
    gall,
    gtall,
    dgu,
    hg,
    dxb,
    dgb,
    sibr,
    sibg,
    ro,
    rog,
    ri,
    rig,
    gout,
    tg,
    xg,
    yg,
    gin,
    ti,
    xi,
    yi,
    kept,
    own_sem,
    stage_sem,
    grad_sem,
    g_recv,
    g_send,
    i_recv,
    i_send,
    w_recv,
    w_send,
    ag_recv,
    ag_send,
    sib_recv,
    sib_send,
    red_recv,
    red_send,
    hop_recv,
    hop_send,
):
    bf, f32 = jnp.bfloat16, jnp.float32
    d, e, z, c, x, y = place()
    d_x = d + 1 - 2 * x
    d_y = d + 2 - 4 * y
    d_d = 3 - d
    hi = lax.div(z, 2)
    zz = z * hi + (3 - z) * (1 - hi)
    other = 1 - c
    to_x = (d_x, e)
    to_y = (d_y, e)
    to_sib = (d, 2 * z + other)
    to_up = (d, e + jnp.where(z < 3, 2, -2))
    to_down = (d, e + jnp.where(z > 0, -2, 2))
    e_in = e + 2 - 4 * hi
    to_in = (d, e_in)
    to_out = (d, jnp.where(zz == 2, e - 2 + 4 * hi, e_in))
    mid = zz == 2
    end = zz == 3

    barrier = pltpu.get_barrier_semaphore()
    for target in (to_x, to_y, to_sib, to_in):
        pl.semaphore_signal(barrier, inc=1, device_id=target, device_id_type=MESH)

    @pl.when(mid)
    def _():
        pl.semaphore_signal(barrier, inc=1, device_id=to_out, device_id_type=MESH)

    own_copies = [
        pltpu.make_async_copy(x_hbm.at[s], xall.at[e, s], own_sem.at[s]) for s in range(2)
    ] + [
        pltpu.make_async_copy(gt_hbm, gtall.at[e], own_sem.at[2]),
        pltpu.make_async_copy(wout_hbm, wout, own_sem.at[3]),
        pltpu.make_async_copy(g_hbm, gall, own_sem.at[4]),
    ]

    def w_columns(h, kind):
        return pl.ds(h * 768 + kind * 384, 384)

    for h in range(2):
        for kind in range(2):
            own_copies.append(
                pltpu.make_async_copy(
                    win_hbm.at[:, pl.ds(kind * 768 + h * 384, 384)],
                    win.at[d, :, w_columns(h, kind)],
                    own_sem.at[5 + 2 * h + kind],
                )
            )
    pl.semaphore_wait(barrier, 7 - zz)

    gathered = ((x_hbm, xall), (gt_hbm, gtall))

    def ag_copy(a, zp, s, way, src=None):
        ref = gathered[a][1].at[2 * zp + c, s]
        return remote(
            ref if src is None else src,
            ref,
            ag_send.at[way, a, zp, s],
            ag_recv.at[a, zp, s],
            to_up if way == 0 else to_down,
        )

    def sib_copy(a, zp, s, src=None, lane=None):
        ref = gathered[a][1].at[2 * zp + (c if lane is None else lane), s]
        return remote(
            ref if src is None else src,
            ref,
            sib_send.at[a, zp, s],
            sib_recv.at[a, zp, s],
            to_sib,
        )

    def own_rows(s):
        for a in range(2):
            src = gathered[a][0].at[s]

            @pl.when(z < 3)
            def _():
                ag_copy(a, z, s, 0, src).start()

            @pl.when(z > 0)
            def _():
                ag_copy(a, z, s, 1, src).start()

            sib_copy(a, z, s, src).start()

    def pass_on(k, s):
        for a in range(2):

            @pl.when(z - k >= 0)
            def _():
                ag_copy(a, z - k, s, 0).wait_recv()

                @pl.when(z < 3)
                def _():
                    ag_copy(a, z - k, s, 0).start()

                sib_copy(a, z - k, s).start()

            @pl.when(z + k <= 3)
            def _():
                ag_copy(a, z + k, s, 1).wait_recv()

                @pl.when(z > 0)
                def _():
                    ag_copy(a, z + k, s, 1).start()

                sib_copy(a, z + k, s).start()

    def from_sib(s, pairs):
        for a in range(2):
            for pair in pairs:
                for j in range(2):
                    sib_copy(a, 2 * pair + j, s, lane=other).wait_recv()

    def w_copy(h, kind, p, src_d, target, row, src=None):
        ref = win.at[src_d, pl.ds(p * 192, 192), w_columns(h, kind)]
        return remote(
            ref if src is None else src,
            ref,
            w_send.at[row, h, kind, p],
            w_recv.at[row, h, kind, p],
            target,
        )

    def w_start(h):
        for p in range(2):
            for kind in range(2):

                def src(q):
                    return win_hbm.at[
                        pl.ds(q * 192, 192), pl.ds(kind * 768 + h * 384, 384)
                    ]

                w_copy(h, kind, p, d, to_x, 0, src(p)).start()
                w_copy(h, kind, 1 - p, d, to_y, 1, src(1 - p)).start()

    def w_pass(h):
        for kind in range(2):
            w_copy(h, kind, 0, d_x, to_x, 0).wait_recv()
            w_copy(h, kind, 0, d_x, to_y, 2).start()
            w_copy(h, kind, 1, d_y, to_y, 1).wait_recv()
            w_copy(h, kind, 1, d_y, to_x, 2).start()

    def w_rest(h):
        for kind in range(2):
            w_copy(h, kind, 1, d_x, to_x, 0).wait_recv()
            w_copy(h, kind, 0, d_y, to_y, 1).wait_recv()
            for p in range(2):
                w_copy(h, kind, p, d_d, to_x, 2).wait_recv()

    own_rows(0)
    w_start(0)
    for copy in own_copies:
        copy.start()
    w_pass(0)
    w_start(1)
    pass_on(1, 0)
    pass_on(2, 0)
    own_rows(1)
    w_rest(0)
    w_pass(1)
    pass_on(3, 0)
    from_sib(0, (0, 1))
    for copy in own_copies:
        copy.wait()

    def order(i):
        v = i if i < 2 else (5 - zz if i == 2 else zz)
        return v * hi + (3 - v) * (1 - hi)

    def sib_sum(zp, s, a):
        src, dst = ((dxb, sibr), (dgb, sibg))[a]
        return remote(
            src.at[2 * zp + other, s], dst.at[zp, s], red_send.at[a, zp, s], red_recv.at[a, zp, s], to_sib
        )

    def hop(i, s, target, inward):
        dst, dstg, row = (ro, rog, 2) if inward else (ri, rig, 4)
        zp = order(i)
        halves = [
            remote(
                dxb.at[2 * zp + c, s, pl.ds(h * 64, 64)],
                dst.at[i, s, pl.ds(h * 64, 64)],
                hop_send.at[h, i, s],
                hop_recv.at[row // 2 - 1, h, i, s],
                target,
            )
            for h in range(2)
        ]
        last = remote(
            dgb.at[2 * zp + c, s],
            dstg.at[i, s],
            red_send.at[3, i, s],
            red_recv.at[row + 1, i, s],
            target,
        )
        return halves, last

    def wait_half(ref, slot, s, row, h):
        part = ref.at[slot, s, pl.ds(h * 64, 64)]
        remote(
            part, part, hop_send.at[h, slot, s], hop_recv.at[row // 2 - 1, h, slot, s], to_in
        ).wait_recv()

    def wait_last(refg, slot, s, row):
        remote(
            refg.at[slot, s],
            refg.at[slot, s],
            red_send.at[3, slot, s],
            red_recv.at[row + 1, slot, s],
            to_in,
        ).wait_recv()

    def wait_sib(zp, s):
        for a, ref in enumerate((sibr, sibg)):
            remote(
                ref.at[zp, s], ref.at[zp, s], red_send.at[a, zp, s], red_recv.at[a, zp, s], to_sib
            ).wait_recv()

    def half_sum(zp, s, incoming, h):
        rows = slice(h * 64, (h + 1) * 64)
        total = dxb[2 * zp + c, s, rows].astype(f32) + sibr[zp, s, rows].astype(f32)
        for ref, refg, slot, row in incoming:
            wait_half(ref, slot, s, row, h)
            total = total + ref[slot, s, rows].astype(f32)
        return total

    def gate_sum(zp, s, incoming):
        total = dgb[2 * zp + c, s] + sibg[zp, s]
        for ref, refg, slot, row in incoming:
            wait_last(refg, slot, s, row)
            total = total + refg[slot, s]
        return total

    def pass_sum(i, s, incoming, target, inward):
        zp = order(i)
        wait_sib(zp, s)
        halves, last = hop(i, s, target, inward)
        for h in range(2):
            dxb[2 * zp + c, s, h * 64 : (h + 1) * 64] = half_sum(zp, s, incoming, h).astype(bf)
            halves[h].start()
        dgb[2 * zp + c, s] = gate_sum(zp, s, incoming)
        last.start()

    def end_sums(s, which):
        @pl.when(end)
        def _():
            for i in which:
                pass_sum(i, s, (), to_in, True)

    def mid_sum(i, s):
        @pl.when(mid)
        def _():
            if i < 2:
                pass_sum(i, s, ((ro, rog, i, 2),), to_in, False)
            else:
                pass_sum(2, s, ((ri, rig, 0, 4),), to_out, False)

    def dx_copy(s):
        part = pl.ds(4 * s, 4)
        return pltpu.make_async_copy(kept.at[part], dx_hbm.at[part], own_sem.at[4 + s])

    def dx_store(s, incoming):
        zp = order(3)
        wait_sib(zp, s)
        for h in range(2):
            total = half_sum(zp, s, incoming, h)
            for j in range(4):
                kept[4 * s + j, h * 64 : (h + 1) * 64] = total[:, j * 384 : (j + 1) * 384]
        dgt_out[s] = gate_sum(zp, s, incoming)

    def last_sum(s):
        @pl.when(mid)
        def _():
            dx_store(s, ((ro, rog, 2, 2), (ri, rig, 1, 4)))

        @pl.when(end)
        def _():
            dx_store(s, ((ri, rig, 2, 4),))

        dx_copy(s).start()

    eye = lax.broadcasted_iota(jnp.int32, (128, 128), 0) == lax.broadcasted_iota(
        jnp.int32, (128, 128), 1
    )
    mine = lax.broadcasted_iota(jnp.int32, (8, 128), 0) == e
    nt = (((1,), (1,)), ((), ()))
    tn = (((0,), (0,)), ((), ()))

    def half_step(s, pair, h):
        first = 4 * pair
        block = pl.ds(first, 4)
        both = jnp.dot(
            xall[block, s].reshape(512, 1536),
            win[:, :, h * 768 : (h + 1) * 768].reshape(1536, 768),
            preferred_element_type=f32,
        )
        gate = both[:, :384]
        up = both[:, 384:]
        if h == 0:
            full = lax.dot_general(
                gall[block, s].reshape(512, 1536), wout[...], nt, preferred_element_type=f32
            )
            kept[block] = full[:, 384:].reshape(4, 128, 384)
            back = full[:, :384]
        else:
            back = kept[block].reshape(512, 384)
        columns = []
        for j in range(4):
            row = jnp.sum(jnp.where(mine, gtall[first + j, s], 0.0), axis=0, keepdims=True)
            columns.append(jnp.sum(jnp.where(eye, row, 0.0), axis=1, keepdims=True))
        weight = jnp.concatenate(columns, axis=0)
        sig = jax.nn.sigmoid(gate)
        silu = gate * sig
        hidden = (silu * up).astype(bf).astype(f32)
        dgate = jnp.sum(hidden * back, axis=1, keepdims=True)
        for j in range(4):
            row = jnp.sum(
                jnp.where(eye, dgate[j * 128 : (j + 1) * 128], 0.0), axis=0, keepdims=True
            )
            part = jnp.where(mine, row, 0.0)
            dgb[first + j, s] = part if h == 0 else dgb[first + j, s] + part
        hg[block, s, :, h * 384 : (h + 1) * 384] = (
            (hidden * weight).astype(bf).reshape(4, 128, 384)
        )
        back = back * weight
        dgu[block, s, :, h * 768 : h * 768 + 384] = (
            (back * up * (sig * (1.0 + gate * (1.0 - sig)))).astype(bf).reshape(4, 128, 384)
        )
        dgu[block, s, :, h * 768 + 384 : (h + 1) * 768] = (
            (back * silu).astype(bf).reshape(4, 128, 384)
        )

    def dx_step(s, pair):
        first = 4 * pair
        block = pl.ds(first, 4)
        dxb[block, s] = (
            lax.dot_general(
                dgu[block, s].reshape(512, 1536),
                win[...].reshape(1536, 1536),
                nt,
                preferred_element_type=f32,
            )
            .astype(bf)
            .reshape(4, 128, 1536)
        )
        for j in range(2):
            for a in range(2):
                sib_sum(2 * pair + j, s, a).start()

    def out_slot(slot):
        return win.at[:, pl.ds(slot * 128, 128)]

    def out_copy(slot, s, first):
        return pltpu.make_async_copy(
            out_slot(slot), outp_hbm.at[pl.ds(first, 4), s], stage_sem.at[slot]
        )

    def out_step(slot, s, pair):
        first = 4 * pair
        win[:, slot * 128 : (slot + 1) * 128] = (
            jnp.dot(
                hg[pl.ds(first, 4), s].reshape(512, FF), wout[...], preferred_element_type=f32
            )
            .astype(bf)
            .reshape(4, 128, 1536)
        )
        out_copy(slot, s, first).start()

    def early_copies(first):
        return [
            pltpu.make_async_copy(
                gout.at[pl.ds(j * 128, 128)], outp_hbm.at[first + j, 0], grad_sem.at[j]
            )
            for j in range(4)
        ]

    def early_step(pair):
        first = 4 * pair
        gout[:512] = jnp.dot(
            hg[pl.ds(first, 4), 0].reshape(512, FF), wout[...], preferred_element_type=f32
        ).astype(bf)
        for copy in early_copies(first):
            copy.start()

    def early_wait():
        for copy in early_copies(0):
            copy.wait()

    far = 1 - hi
    near = hi

    def pair_of(t):
        return far + t * (1 - 2 * far)

    def i_piece(dd, p):
        return gin.at[pl.ds(pl.multiple_of(dd * 384 + p * PIECE, 16), PIECE)]

    def i_diag(p):
        return remote(
            i_piece(d_d, p), ti.at[p], i_send.at[0, p], i_recv.at[0, p], (to_x, to_y)[p % 2]
        )

    def i_direct(p):
        if p % 2 == 0:
            return remote(i_piece(d_x, p), xi.at[p], i_send.at[1, p], i_recv.at[1, p], to_x)
        return remote(i_piece(d_y, p), yi.at[p], i_send.at[1, p], i_recv.at[2, p], to_y)

    def i_summed(p):
        if p % 2 == 0:
            return remote(i_piece(d_y, p), yi.at[p], i_send.at[2, p], i_recv.at[2, p], to_y)
        return remote(i_piece(d_x, p), xi.at[p], i_send.at[2, p], i_recv.at[1, p], to_x)

    def i_middle(p):
        i_diag(p).wait_recv()
        dd = d_y if p % 2 == 0 else d_x
        rows = pl.ds(pl.multiple_of(dd * 384 + p * PIECE, 16), PIECE)
        gin[rows] = (gin[rows].astype(f32) + ti[p].astype(f32)).astype(bf)
        i_summed(p).start()

    def i_final(p):
        remote(xi.at[p], xi.at[p], i_send.at[1, p], i_recv.at[1, p], to_x).wait_recv()
        remote(yi.at[p], yi.at[p], i_send.at[1, p], i_recv.at[2, p], to_y).wait_recv()
        rows = pl.ds(pl.multiple_of(d * 384 + p * PIECE, 16), PIECE)
        xi[p] = (gin[rows].astype(f32) + xi[p].astype(f32) + yi[p].astype(f32)).astype(bf)

    def in_grad(yy, h):
        return lax.dot_general(
            xall[:, :, :, pl.ds(pl.multiple_of(yy * 768, 128), 768)].reshape(2048, 768),
            dgu[:, :, :, h * 768 : (h + 1) * 768].reshape(2048, 768),
            tn,
            preferred_element_type=f32,
        ).astype(bf)

    def in_first(yy):
        gin[pl.ds(pl.multiple_of(yy * 768, 16), 768)] = in_grad(yy, 0)

    @pl.loop(0, 2)
    def _(t):
        half_step(0, pair_of(t), 0)

    @pl.when(mid)
    def _():
        pass_on(1, 1)

    w_rest(1)

    @pl.when(end)
    def _():
        pass_on(1, 1)


    @pl.loop(0, 2)
    def _(t):
        pair = pair_of(t)
        half_step(0, pair, 1)
        dx_step(0, pair)

        @pl.when(t == 0)
        def _():
            end_sums(0, (0, 1))
            pass_on(2, 1)

        @pl.when(t == 1)
        def _():
            end_sums(0, (2,))

    from_sib(1, (near,))

    @pl.loop(0, 2)
    def _(t):
        half_step(1, pair_of(1 - t), 0)

        @pl.when(t == 0)
        def _():
            pass_on(3, 1)
            early_step(far)
            from_sib(1, (far,))

    mid_sum(0, 0)

    @pl.loop(0, 2)
    def _(t):
        pair = pair_of(t)
        half_step(1, pair, 1)
        dx_step(1, pair)

        @pl.when(t == 0)
        def _():
            in_first(1 - y)
            for p in range(4):
                i_diag(p).start()
            for p in (1, 3):
                i_direct(p).start()
            end_sums(1, (0, 1))
            in_first(y)
            for p in (0, 2):
                i_direct(p).start()
            mid_sum(1, 0)
            mid_sum(2, 0)

    def g_rows(dd, i):
        return pl.ds(pl.multiple_of(dd * 192 + i * 48, 16), 48)

    def g_piece(dd, i):
        return gout.at[g_rows(dd, i)]

    def g_diag(i):
        return remote(
            g_piece(d_d, i), tg.at[i], g_send.at[0, i], g_recv.at[0, i], (to_x, to_y)[i]
        )

    def g_direct(i):
        if i == 0:
            return remote(g_piece(d_x, i), xg.at[i], g_send.at[1, i], g_recv.at[1, i], to_x)
        return remote(g_piece(d_y, i), yg.at[i], g_send.at[1, i], g_recv.at[2, i], to_y)

    def g_summed(i):
        if i == 0:
            return remote(g_piece(d_y, i), yg.at[i], g_send.at[2, i], g_recv.at[2, i], to_y)
        return remote(g_piece(d_x, i), xg.at[i], g_send.at[2, i], g_recv.at[1, i], to_x)

    def g_middle(i):
        g_diag(i).wait_recv()
        rows = g_rows(d_y if i == 0 else d_x, i)
        gout[rows] = (gout[rows].astype(f32) + tg[i].astype(f32)).astype(bf)
        g_summed(i).start()

    def out_grad(half):
        at = pl.multiple_of(half * 384, 128)
        gout[pl.ds(at, 384)] = lax.dot_general(
            hg[:, :, :, pl.ds(at, 384)].reshape(2048, 384),
            gall[...].reshape(2048, 1536),
            tn,
            preferred_element_type=f32,
        ).astype(bf)

    for p in range(4):
        i_middle(p)
    early_wait()
    out_grad(1 - y)
    g_diag(0).start()
    g_diag(1).start()
    g_direct(1).start()
    end_sums(1, (2,))
    out_grad(y)
    g_direct(0).start()
    mid_sum(0, 1)
    rest = [
        pltpu.make_async_copy(
            gout.at[pl.ds(k * 192 + PIECE, PIECE)], gout_hbm.at[k], own_sem.at[k]
        )
        for k in range(4)
    ]
    for copy in rest:
        copy.start()

    def grad_copy(k):
        return pltpu.make_async_copy(
            win.at[k, :, pl.ds(0, 768)], gin_hbm.at[k], grad_sem.at[k]
        )

    for h in range(2):
        for kind in range(2):
            for p in range(2):
                w_copy(h, kind, p, d, to_x, 2).wait_send()
    for k in range(2):
        win[2 * k : 2 * k + 2, :, :768] = in_grad(k, 1).reshape(2, 384, 768)
        grad_copy(2 * k).start()
        grad_copy(2 * k + 1).start()
    for p in range(4):
        i_final(p)
    in_copy = pltpu.make_async_copy(xi, gin_first_hbm, own_sem.at[6])
    in_copy.start()
    for k in range(4):
        grad_copy(k).wait()
    for i in range(2):
        g_middle(i)
    mid_sum(1, 1)
    mid_sum(2, 1)
    out_step(0, 0, near)
    out_step(1, 1, far)
    out_step(2, 1, near)
    last_sum(0)
    for i in range(2):
        remote(xg.at[i], xg.at[i], g_send.at[1, i], g_recv.at[1, i], to_x).wait_recv()
        remote(yg.at[i], yg.at[i], g_send.at[1, i], g_recv.at[2, i], to_y).wait_recv()
        xg[i] = (
            gout[g_rows(d, i)].astype(f32) + xg[i].astype(f32) + yg[i].astype(f32)
        ).astype(bf)
    out_first_copy = pltpu.make_async_copy(xg, gout_first_hbm, own_sem.at[7])
    out_first_copy.start()
    for copy in rest:
        copy.wait()
    for k in range(3):
        out_copy(k, 1, 0).wait()
    last_sum(1)
    in_copy.wait()
    out_first_copy.wait()
    for s in range(2):
        dx_copy(s).wait()

    for i in range(2):
        for copy in (g_diag(i), g_direct(i), g_summed(i)):
            copy.wait_send()
    for p in range(4):
        for copy in (i_diag(p), i_direct(p), i_summed(p)):
            copy.wait_send()
    for h in range(2):
        for kind in range(2):
            for p in range(2):
                for row in range(2):
                    w_copy(h, kind, p, d, to_x, row).wait_send()
    for s in range(2):
        for zp in range(4):
            for a in range(2):
                sib_copy(a, zp, s).wait_send()
                sib_sum(zp, s, a).wait_send()

                @pl.when((zp <= z) & (z < 3))
                def _():
                    ag_copy(a, zp, s, 0).wait_send()

                @pl.when((zp >= z) & (z > 0))
                def _():
                    ag_copy(a, zp, s, 1).wait_send()

        for i in range(3):
            halves, last = hop(i, s, to_in, True)
            for copy in halves + [last]:
                copy.wait_send()


def expert_stage(rows, grads, gates_t, w_in, w_out):
    bf, f32 = jnp.bfloat16, jnp.float32
    shape = jax.ShapeDtypeStruct
    width = rows.shape[-1]
    hbm = pl.BlockSpec(memory_space=pltpu.HBM)
    vmem = pl.BlockSpec(memory_space=pltpu.VMEM)
    dma = pltpu.SemaphoreType.DMA
    return pl.pallas_call(
        expert_kernel,
        out_shape=(
            shape((8, 128, width // 4), f32),
            shape((2, 8, 128), f32),
            shape((8, 2, 128, width), bf),
            shape((4, 384, FF), bf),
            shape((4, PIECE, width), bf),
            shape((2, 48, width), bf),
            shape((4, PIECE, FF), bf),
        ),
        in_specs=[hbm] * 5,
        out_specs=(hbm, vmem, hbm, hbm, hbm, hbm, hbm),
        scratch_shapes=[
            pltpu.VMEM((4, width // 4, 2 * FF), bf),
            pltpu.VMEM((FF, width), bf),
            pltpu.VMEM((8, 2, 128, width), bf),
            pltpu.VMEM((8, 2, 128, width), bf),
            pltpu.VMEM((8, 2, 8, 128), f32),
            pltpu.VMEM((8, 2, 128, 2 * FF), bf),
            pltpu.VMEM((8, 2, 128, FF), bf),
            pltpu.VMEM((8, 2, 128, width), bf),
            pltpu.VMEM((8, 2, 8, 128), f32),
            pltpu.VMEM((4, 2, 128, width), bf),
            pltpu.VMEM((4, 2, 8, 128), f32),
            pltpu.VMEM((3, 2, 128, width), bf),
            pltpu.VMEM((3, 2, 8, 128), f32),
            pltpu.VMEM((3, 2, 128, width), bf),
            pltpu.VMEM((3, 2, 8, 128), f32),
            pltpu.VMEM((FF, width), bf),
            *([pltpu.VMEM((2, 48, width), bf)] * 3),
            pltpu.VMEM((width, FF), bf),
            *([pltpu.VMEM((4, PIECE, FF), bf)] * 3),
            pltpu.VMEM((8, 128, width // 4), f32),
            dma((9,)),
            dma((3,)),
            dma((4,)),
            dma((3, 2)),
            dma((3, 2)),
            dma((3, 4)),
            dma((3, 4)),
            dma((3, 2, 2, 2)),
            dma((3, 2, 2, 2)),
            dma((2, 4, 2)),
            dma((2, 2, 4, 2)),
            dma((2, 4, 2)),
            dma((2, 4, 2)),
            dma((6, 4, 2)),
            dma((4, 4, 2)),
            dma((2, 2, 3, 2)),
            dma((2, 3, 2)),
        ],
        compiler_params=pltpu.CompilerParams(
            collective_id=1, has_side_effects=True, vmem_limit_bytes=63 * 2**20
        ),
        name="expert_stage",
    )(
        rows.reshape(2, 128, width),
        grads.reshape(8, 2, 128, width),
        gates_t,
        w_in,
        w_out,
    )


def backward_kernel(
    dx_hbm,
    dgt_hbm,
    gates_hbm,
    mixed_hbm,
    cot_hbm,
    tok_hbm,
    q_hbm,
    kv_hbm,
    att_hbm,
    lens_ref,
    small_hbm,
    rope_hbm,
    wa_hbm,
    wb_hbm,
    gin_hbm,
    gout_hbm,
    outp_hbm,
    block_hbm,
    dtok_hbm,
    gq_hbm,
    gb_hbm,
    gkv_out,
    small_out,
    ein_hbm,
    eout_hbm,
    osib,
    oro,
    ori,
    wide,
    gq,
    gb,
    gk,
    sib_q,
    sib_b,
    sib_k,
    tq,
    xq,
    yq,
    roq,
    riq,
    tb,
    xb,
    yb,
    rob,
    rib,
    tw,
    xw,
    yw,
    row_,
    riw,
    te,
    xe,
    ye,
    le,
    lf,
    td,
    xd,
    yd,
    ld,
    old,
    oslot,
    dat,
    dkv,
    tk,
    xk,
    yk,
    rope,
    cot_ref,
    tok_ref,
    q_ref,
    kv_ref,
    att_ref,
    mixed_ref,
    block_out,
    dtok_out,
    dgt_ref,
    gates_ref,
    small_ref,
    gq_out,
    gb_out,
    load_sem,
    out_sem,
    le_sem,
    old_sem,
    os_recv,
    os_send,
    ds_recv,
    ds_send,
    t_recv,
    x_recv,
    y_recv,
    t_send,
    d_send,
    s_send,
    ro_recv,
    ri_recv,
    hop_send,
):
    bf, f32 = jnp.bfloat16, jnp.float32
    d, e, z, c, x, y = place()
    d_x = d + 1 - 2 * x
    d_y = d + 2 - 4 * y
    d_d = 3 - d
    hi = lax.div(z, 2)
    zz = z * hi + (3 - z) * (1 - hi)
    other = 1 - c
    mid = zz == 2
    end = zz == 3
    to_x = (d_x, e)
    to_y = (d_y, e)
    to_sib = (d, 2 * z + other)
    e_in = e + 2 - 4 * hi
    to_in = (d, e_in)
    to_out = (d, jnp.where(zz == 2, e - 2 + 4 * hi, e_in))

    dqs = block_out
    dmix = dtok_out
    dx_ref = dtok_out

    first_loads = [
        pltpu.make_async_copy(
            dx_hbm.at[4 * s + j],
            dx_ref.at[pl.ds(s * 128, 128), pl.ds(j * 384, 384)],
            load_sem.at[13 + 4 * s + j],
        )
        for s in range(2)
        for j in range(4)
    ] + [
        pltpu.make_async_copy(mixed_hbm, mixed_ref, load_sem.at[10]),
    ]
    tiny_loads = [
        pltpu.make_async_copy(src, dst, load_sem.at[21 + j])
        for j, (src, dst) in enumerate(
            ((dgt_hbm, dgt_ref), (gates_hbm, gates_ref), (small_hbm, small_ref))
        )
    ]
    results = [
        pltpu.make_async_copy(src, dst, out_sem.at[j])
        for j, (src, dst) in enumerate(
            ((gq_out, gq_hbm), (gb_out, gb_hbm), (xe, ein_hbm), (xd, eout_hbm))
        )
    ]
    for load in tiny_loads:
        load.start()
    for load in first_loads:
        load.start()

    barrier = pltpu.get_barrier_semaphore()
    for target in (to_x, to_y, to_sib, to_in):
        pl.semaphore_signal(barrier, inc=1, device_id=target, device_id_type=MESH)

    @pl.when(mid)
    def _():
        pl.semaphore_signal(barrier, inc=1, device_id=to_out, device_id_type=MESH)

    pl.semaphore_wait(barrier, 7 - zz)

    def order(i):
        v = i if i < 2 else (5 - zz if i == 2 else zz)
        return v * hi + (3 - v) * (1 - hi)

    def across(k, src, t, fx, fy, ways=(0, 1, 0, 1)):
        def diag(i):
            return remote(
                src(d_d, i), t.at[i], t_send.at[k, i], t_recv.at[k, i], (to_x, to_y)[ways[i]]
            )

        def direct(i):
            if ways[i] == 0:
                return remote(src(d_x, i), fx.at[i], d_send.at[k, i], x_recv.at[k, i], to_x)
            return remote(src(d_y, i), fy.at[i], d_send.at[k, i], y_recv.at[k, i], to_y)

        def summed(i, ref):
            if ways[i] == 0:
                return remote(ref, fy.at[i], s_send.at[k, i], y_recv.at[k, i], to_y)
            return remote(ref, fx.at[i], s_send.at[k, i], x_recv.at[k, i], to_x)

        def wait_t(i):
            remote(t.at[i], t.at[i], t_send.at[k, i], t_recv.at[k, i], to_x).wait_recv()

        def wait_xy(i):
            remote(fx.at[i], fx.at[i], d_send.at[k, i], x_recv.at[k, i], to_x).wait_recv()
            remote(fy.at[i], fy.at[i], d_send.at[k, i], y_recv.at[k, i], to_y).wait_recv()

        def drain(n):
            for i in range(n):
                diag(i).wait_send()
                direct(i).wait_send()
                summed(i, t.at[i]).wait_send()

        return diag, direct, summed, wait_t, wait_xy, drain

    def along(k, slot, ro, ri):
        def send(i, target, dst, recv):
            return remote(slot(i), dst.at[i], hop_send.at[k, i], recv.at[k, i], target)

        def to_ro(i):
            return send(i, to_in, ro, ro_recv)

        def to_ri(i):
            return send(i, to_in if i < 2 else to_out, ri, ri_recv)

        def wait_ro(i):
            remote(ro.at[i], ro.at[i], hop_send.at[k, i], ro_recv.at[k, i], to_in).wait_recv()

        def wait_ri(i):
            remote(ri.at[i], ri.at[i], hop_send.at[k, i], ri_recv.at[k, i], to_in).wait_recv()

        def drain():
            for i in range(3):
                to_ro(i).wait_send()

        return to_ro, to_ri, wait_ro, wait_ri, drain

    expert_ways = (0, 1, 0, 0)

    def expert_src(dd, p):
        return gin_hbm.at[pl.ds(pl.multiple_of(dd * 384 + p * PIECE, 16), PIECE)]

    e_diag, e_direct, e_summed, e_wait_t, e_wait_xy, e_drain = across(
        0, expert_src, te, xe, ye, expert_ways
    )

    def e_sent_to(p):
        return d_y if expert_ways[p] == 0 else d_x

    e_loads = [
        pltpu.make_async_copy(expert_src(e_sent_to(p), p), le.at[p], le_sem.at[p])
        for p in range(4)
    ]
    e_own = pltpu.make_async_copy(
        gin_hbm.at[pl.ds(pl.multiple_of(d * 384, 16), 384)], lf, le_sem.at[4]
    )

    def e_middle(p):
        e_wait_t(p)
        e_loads[p].wait()
        te[p] = (te[p].astype(f32) + le[p].astype(f32)).astype(bf)
        e_summed(p, te.at[p]).start()

    def e_final(p):
        e_wait_xy(p)
        rows = slice(p * PIECE, (p + 1) * PIECE)
        total = lf[rows].astype(f32) + xe[p].astype(f32) + ye[p].astype(f32)
        xe[p] = total.astype(bf)

    def d_src(dd):
        return gout_hbm.at[dd]

    def d_diag():
        return remote(d_src(d_d), td, t_send.at[5, 0], t_recv.at[5, 0], to_y)

    def d_direct():
        return remote(d_src(d_y), yd, d_send.at[5, 0], y_recv.at[5, 0], to_y)

    def d_summed():
        return remote(td, xd, s_send.at[5, 0], x_recv.at[5, 0], to_x)

    d_loads = [
        pltpu.make_async_copy(d_src(dd), ld.at[j], le_sem.at[5 + j])
        for j, dd in enumerate((d_x, d))
    ]

    def d_middle():
        d_diag().wait_recv()
        d_loads[0].wait()
        td[...] = (td[...].astype(f32) + ld[0].astype(f32)).astype(bf)
        d_summed().start()

    def d_final():
        d_summed().wait_recv()
        d_direct().wait_recv()
        xd[...] = (ld[1].astype(f32) + xd[...].astype(f32) + yd[...].astype(f32)).astype(bf)

    def store_q(total):
        gq_out[...] = total

    def store_b(total):
        gb_out[...] = total

    def store_k(total):
        gkv_out[...] = total[:, :512]
        small_out[...] = lax.dot_general(
            eye[:16],
            total[:, 512:],
            (((1,), (1,)), ((), ())),
            preferred_element_type=f32,
            precision=highest,
        )

    dense = (
        (gq, sib_q, tq, xq, yq, roq, riq, store_q),
        (gb, sib_b, tb, xb, yb, rob, rib, store_b),
        (gk, sib_k, tw, xw, yw, row_, riw, store_k),
    )

    def dense_stream(j):
        grad, sib, t, fx, fy, ro, ri, out = dense[j]

        def src(dd, i):
            return grad.at[dd * 4 + order(i), c]

        diag, direct, summed, wait_t, wait_xy, drain = across(1 + j, src, t, fx, fy)

        def own_slot(i):
            return grad.at[d * 4 + order(i), c]

        to_ro, to_ri, wait_ro, wait_ri, drain_z = along(j, own_slot, ro, ri)

        def sib_copy():
            return remote(grad.at[:, other], sib, ds_send.at[j], ds_recv.at[j], to_sib)

        def begin():
            sib_copy().wait_recv()

            @pl.loop(0, 16)
            def _(k):
                grad[k, c] = (grad[k, c].astype(f32) + sib[k].astype(f32)).astype(bf)

            for i in range(4):
                diag(i).start()
            for i in range(4):
                direct(i).start()

        def middle(i):
            dd = d_y if i % 2 == 0 else d_x
            wait_t(i)
            at = dd * 4 + order(i)
            grad[at, c] = (grad[at, c].astype(f32) + t[i].astype(f32)).astype(bf)
            summed(i, src(dd, i)).start()

        def local(i):
            return grad[d * 4 + order(i), c].astype(f32) + fx[i].astype(f32) + fy[i].astype(f32)

        def put(i, total):
            grad[d * 4 + order(i), c] = total.astype(bf)

        def last(i):
            wait_xy(i)
            if i == 3:
                return

            @pl.when(end)
            def _():
                put(i, local(i))
                to_ro(i).start()

        def hop(i):
            @pl.when(mid)
            def _():
                if i < 2:
                    wait_ro(i)
                    put(i, local(i) + ro[i].astype(f32))
                else:
                    wait_ri(0)
                    put(2, local(2) + ri[0].astype(f32))
                to_ri(i).start()

        def finish():
            @pl.when(mid)
            def _():
                wait_ro(2)
                wait_ri(1)
                out(local(3) + ro[2].astype(f32) + ri[1].astype(f32))

            @pl.when(end)
            def _():
                wait_ri(2)
                out(local(3) + ri[2].astype(f32))

        def drain_all():
            sib_copy().wait_send()
            drain(4)
            drain_z()

        return sib_copy, begin, middle, last, hop, finish, drain_all

    q_sib, q_begin, q_middle, q_last, q_hop, q_finish, q_drain = dense_stream(0)
    b_sib, b_begin, b_middle, b_last, b_hop, b_finish, b_drain = dense_stream(1)
    w_sib, w_begin, w_middle, w_last, w_hop, w_finish, w_drain = dense_stream(2)

    def out_rows(i, lane):
        return outp_hbm.at[pl.ds(pl.multiple_of((2 * order(i) + lane) * CHUNK, CHUNK), CHUNK)]

    def out_sib(i):
        return remote(out_rows(i, other), osib.at[i], os_send.at[i], os_recv.at[i], to_sib)

    o_ro, o_ri, o_wait_ro, o_wait_ri, _ = along(3, lambda i: oslot.at[i % 2], oro, ori)

    def out_sum(i, incoming, store):
        out_sib(i).wait_recv()
        for half in range(2):
            rows = pl.ds(half * 128, 128)
            loads = [
                pltpu.make_async_copy(ref.at[rows], old.at[j], old_sem.at[j])
                for j, ref in enumerate([out_rows(i, c), osib.at[i]] + incoming)
            ]
            for load in loads:
                load.start()
            for load in loads:
                load.wait()
            total = old[0].astype(f32)
            for j in range(1, len(loads)):
                total = total + old[j].astype(f32)
            store(slice(half * 128, (half + 1) * 128), total)

    def out_slot(i):
        def store(rows, total):
            oslot[i % 2, rows] = total.astype(bf)

        return store

    def out_end(i):
        @pl.when(end)
        def _():
            if i == 2:
                o_ro(0).wait_send()
            out_sum(i, [], out_slot(i))
            o_ro(i).start()

    def out_mid(i):
        @pl.when(mid)
        def _():
            if i < 2:
                o_wait_ro(i)
                out_sum(i, [oro.at[i]], out_slot(i))
            else:
                o_ri(0).wait_send()
                o_wait_ri(0)
                out_sum(2, [ori.at[0]], out_slot(2))
            o_ri(i).start()

    def out_finish():
        def store(rows, total):
            total = total + mixed_ref[rows]
            slot = d * 128 + lax.broadcasted_iota(jnp.int32, (128, 1), 0)
            live = slot < lens_ref[rows.start // 128]
            block_out[rows] = jnp.where(live, total, 0.0).astype(bf)

        @pl.when(mid)
        def _():
            o_wait_ro(2)
            o_wait_ri(1)
            out_sum(3, [oro.at[2], ori.at[1]], store)

        @pl.when(end)
        def _():
            o_wait_ri(2)
            out_sum(3, [ori.at[2]], store)

    def kv_src(dd, i):
        return dkv.at[dd, pl.ds(i * 128, 128)]

    k_diag, k_direct, k_summed, k_wait_t, k_wait_xy, k_drain = across(4, kv_src, tk, xk, yk)

    def k_middle(i):
        dd = d_y if i % 2 == 0 else d_x
        k_wait_t(i)
        rows = slice(i * 128, (i + 1) * 128)
        dkv[dd, rows] = (dkv[dd, rows].astype(f32) + tk[i].astype(f32)).astype(bf)
        k_summed(i, kv_src(dd, i)).start()

    wb_load = pltpu.make_async_copy(wb_hbm, wide.at[:, pl.ds(0, 1536)], load_sem.at[1])
    wa_load = pltpu.make_async_copy(wa_hbm.at[:, pl.ds(0, 2048)], wide, load_sem.at[2])
    rope_load = pltpu.make_async_copy(
        rope_hbm.at[:, pl.ds(pl.multiple_of(d * 128, 128), 128)], rope, load_sem.at[3]
    )
    loads = [
        pltpu.make_async_copy(src, dst, load_sem.at[4 + j])
        for j, (src, dst) in enumerate(
            (
                (cot_hbm, cot_ref),
                (att_hbm, att_ref),
                (q_hbm, q_ref),
                (kv_hbm, kv_ref),
                (tok_hbm, tok_ref),
            )
        )
    ]
    for load in loads[:2]:
        load.start()
    wb_load.start()
    rope_load.start()
    for load in loads[2:] + e_loads + [e_own] + d_loads:
        load.start()
    for p in range(4):
        e_diag(p).start()
    for p in (0, 1):
        e_direct(p).start()
    d_diag().start()
    for i in range(4):
        out_sib(i).start()
    out_end(0)

    nt = (((1,), (1,)), ((), ()))
    tn = (((0,), (0,)), ((), ()))

    def dot_nt(a, b):
        return lax.dot_general(a, b, nt, preferred_element_type=f32)

    def dot_tn(a, b):
        return lax.dot_general(a, b, tn, preferred_element_type=f32)

    eye = (
        lax.broadcasted_iota(jnp.int32, (128, 128), 0)
        == lax.broadcasted_iota(jnp.int32, (128, 128), 1)
    ).astype(f32)
    eye_low = eye.astype(bf)
    for load in tiny_loads:
        load.wait()
    gates = jnp.concatenate([gates_ref[s] for s in range(2)], axis=1)
    dgate = jnp.concatenate([dgt_ref[s] for s in range(2)], axis=1)
    dlogit = gates * (dgate - jnp.sum(gates * dgate, axis=0, keepdims=True))
    dl_hi = dlogit.astype(bf).astype(f32)
    dl = jnp.concatenate([dl_hi, dlogit - dl_hi], axis=0).astype(bf)
    small_t = small_ref[...]
    router = jnp.concatenate([small_t[:8]] * 2, axis=0).astype(bf)
    for load in first_loads:
        load.wait()
    dn2 = dx_ref[...] + dot_tn(dl, router)
    mixed = mixed_ref[...]
    inv2 = lax.rsqrt(jnp.mean(mixed * mixed, axis=1, keepdims=True) + epsilon)
    n2 = mixed * inv2
    normed2 = (n2 * small_t[9:10]).astype(bf)
    router_sum = jnp.dot(dl, normed2, preferred_element_type=f32)
    router_sum = router_sum[:8] + router_sum[8:]
    mid_sum = jnp.sum(dn2 * n2, axis=0, keepdims=True)
    loads[0].wait()
    loads[1].wait()
    grads = [
        jnp.where(
            d * 128 + lax.broadcasted_iota(jnp.int32, (128, 1), 0) < lens_ref[s],
            cot_ref[s * 128 : (s + 1) * 128].astype(f32),
            0.0,
        )
        for s in range(2)
    ]
    u = dn2 * small_t[9:10]
    dmixed = jnp.concatenate(grads, axis=0) + inv2 * (u - n2 * jnp.mean(u * n2, axis=1, keepdims=True))
    dmix[...] = dmixed
    dproj = dmixed.astype(bf)
    for r in range(4):
        part = dot_tn(att_ref[:, r * 384 : (r + 1) * 384], dproj)
        gb[4 * r : 4 * r + 4] = part.astype(bf).reshape(4, 2, 48, 1536)
    b_sib().start()
    wb_load.wait()
    datt = dot_nt(dproj, wide[:, :1536]).astype(bf)
    for head in range(QUERY_HEADS):
        for s in range(2):
            at = (s * QUERY_HEADS + head) * 128
            dat[at : at + 128] = datt[s * 128 : (s + 1) * 128, head * 128 : (head + 1) * 128]
    wa_load.start()
    b_begin()
    out_end(1)

    query_pos = d * 128 + lax.broadcasted_iota(jnp.int32, (128, 512), 0)
    key_pos = lax.broadcasted_iota(jnp.int32, (128, 512), 1)
    rope_load.wait()
    for load in loads[2:]:
        load.wait()
    cos_rows = rope[0]
    sin_rows = rope[1]
    scale = HEAD_SIZE ** (-0.5)

    def unrotate_rows(v, cos, sin):
        return v * cos - pltpu.roll(v, 64, 1) * sin

    def attend(n):
        s = lax.div(n, 2)
        h = lax.rem(n, 2)
        srow = pl.ds(pl.multiple_of(s * 128, 128), 128)
        kcol = pl.ds(pl.multiple_of(h * 128, 128), 128)
        vcol = pl.ds(pl.multiple_of(256 + h * 128, 128), 128)
        lens = lens_ref[s]
        allowed = (key_pos <= query_pos) & (key_pos < lens)
        ks = kv_ref[:, srow, kcol].reshape(512, 128)
        vs = kv_ref[:, srow, vcol].reshape(512, 128)
        dk = None
        dv = None
        for half in range(2):
            rows = pl.ds(pl.multiple_of(n * 768 + half * 384, 128), 384)
            qh = q_ref[rows]
            dh = dat[rows]
            scores = dot_nt(qh, ks).reshape(3, 128, 512) * scale
            scores = jnp.where(allowed[None], scores, -1e30)
            probs = jnp.exp(scores - jnp.max(scores, axis=-1, keepdims=True))
            probs = probs * (1.0 / jnp.sum(probs, axis=-1, keepdims=True))
            dprobs = dot_nt(dh, vs).reshape(3, 128, 512)
            delta = jnp.sum(probs * dprobs, axis=-1, keepdims=True)
            dscores = (probs * (dprobs - delta)).astype(bf).reshape(384, 512)
            low = probs.astype(bf).reshape(384, 512)
            dq = jnp.dot(dscores, ks, preferred_element_type=f32) * scale
            for j in range(3):
                dqs[srow, pl.ds(pl.multiple_of(h * 768 + (half * 3 + j) * 128, 128), 128)] = (
                    unrotate_rows(dq[j * 128 : (j + 1) * 128], cos_rows, sin_rows).astype(bf)
                )
            dk_part = dot_tn(dscores, qh)
            dv_part = dot_tn(low, dh)
            dk = dk_part if dk is None else dk + dk_part
            dv = dv_part if dv is None else dv + dv_part
        dkv[:, srow, kcol] = (dk * scale).astype(bf).reshape(4, 128, 128)
        dkv[:, srow, vcol] = dv.astype(bf).reshape(4, 128, 128)

    pl.loop(0, 2)(attend)
    for i in range(4):
        b_middle(i)
    e_middle(1)
    e_middle(0)
    out_mid(0)
    pl.loop(2, 4)(attend)
    for i in range(2):
        k_diag(i).start()
    for i in range(2):
        k_direct(i).start()
    for i in range(4):
        b_last(i)
    out_end(2)

    tok = tok_ref[...].astype(f32)
    inv1 = lax.rsqrt(jnp.mean(tok * tok, axis=1, keepdims=True) + epsilon)
    n1 = tok * inv1
    normed = (n1 * small_t[8:9]).astype(bf)
    for r in range(4):
        part = dot_tn(normed[:, r * 384 : (r + 1) * 384], dqs[...])
        gq[4 * r : 4 * r + 4] = part.astype(bf).reshape(4, 2, 48, 1536)
    q_sib().start()
    k_middle(0)
    k_middle(1)
    q_begin()
    wa_load.wait()
    dn1 = dot_nt(dqs[...], wide[:, :1536])

    for i in range(2):
        k_wait_xy(i)
    own = jnp.concatenate(
        [
            dkv[d, i * 128 : (i + 1) * 128].astype(f32) + xk[i].astype(f32) + yk[i].astype(f32)
            for i in range(2)
        ],
        axis=0,
    )
    cos_two = jnp.concatenate([cos_rows] * 2, axis=0)
    sin_two = jnp.concatenate([sin_rows] * 2, axis=0)
    dkv_own = jnp.concatenate(
        [
            unrotate_rows(own[:, h * 128 : (h + 1) * 128], cos_two, sin_two)
            for h in range(2)
        ]
        + [own[:, 256:]],
        axis=1,
    ).astype(bf)
    dn1 = dn1 + dot_nt(dkv_own, wide[:, 1536:])
    pre_sum = jnp.sum(dn1 * n1, axis=0, keepdims=True)
    row8 = lax.broadcasted_iota(jnp.int32, (8, 1536), 0)
    gains = jnp.where(row8 == 0, pre_sum, jnp.where(row8 == 1, mid_sum, 0.0))
    smalls = jnp.concatenate([router_sum, gains], axis=0).astype(bf)
    for r in range(4):
        cols = slice(r * 384, (r + 1) * 384)
        part = dot_tn(normed[:, cols], dkv_own)
        gk[4 * r : 4 * r + 4, :, :, :512] = part.astype(bf).reshape(4, 2, 48, 512)
        part = dot_tn(smalls[:, cols], eye_low[:16])
        gk[4 * r : 4 * r + 4, :, :, 512:] = part.astype(bf).reshape(4, 2, 48, 128)
    w_sib().start()
    u = dn1 * small_t[8:9]
    dtok_copy = pltpu.make_async_copy(dtok_out, dtok_hbm, load_sem.at[11])
    dtok_out[...] = dmix[...] + inv1 * (u - n1 * jnp.mean(u * n1, axis=1, keepdims=True))

    dtok_copy.start()

    for i in range(4):
        q_middle(i)
    w_begin()
    e_direct(2).start()
    b_hop(0)
    b_hop(1)
    out_mid(1)
    out_mid(2)
    for i in range(4):
        q_last(i)
    for i in range(4):
        w_middle(i)
    d_direct().start()
    d_middle()
    e_direct(3).start()
    for p in (2, 3):
        e_middle(p)
    b_hop(2)
    q_hop(0)
    q_hop(1)
    out_finish()
    block_copy = pltpu.make_async_copy(block_out, block_hbm, load_sem.at[12])
    block_copy.start()
    for i in range(4):
        w_last(i)
    w_hop(0)
    q_hop(2)
    w_hop(1)
    w_hop(2)
    b_finish()
    results[1].start()
    q_finish()
    results[0].start()
    e_own.wait()
    d_loads[1].wait()
    d_final()
    results[3].start()
    for p in range(4):
        e_final(p)
    results[2].start()
    w_finish()
    dtok_copy.wait()
    block_copy.wait()
    for copy in results:
        copy.wait()

    e_drain(4)
    for copy in (d_diag(), d_direct(), d_summed()):
        copy.wait_send()
    k_drain(2)
    q_drain()
    b_drain()
    w_drain()
    for i in range(1, 3):
        o_ro(i).wait_send()
    for i in range(4):
        out_sib(i).wait_send()


def backward_stage(dx, dgt, gates, mixed, cot, tok, q, kv, att, lens, small, rope, wa, wb, gin, gout, outp):
    bf, f32 = jnp.bfloat16, jnp.float32
    shape = jax.ShapeDtypeStruct
    width = tok.shape[-1]
    hbm = pl.BlockSpec(memory_space=pltpu.HBM)
    vmem = pl.BlockSpec(memory_space=pltpu.VMEM)
    smem = pl.BlockSpec(memory_space=pltpu.SMEM)
    dma = pltpu.SemaphoreType.DMA
    widths = (width, width, 640)
    dense = []
    for w in widths:
        dense += [pltpu.VMEM((4, 48, w), bf)] * 3 + [pltpu.VMEM((3, 48, w), bf)] * 2
    return pl.pallas_call(
        backward_kernel,
        out_shape=(
            shape((CHUNK, width), bf),
            shape((CHUNK, width), f32),
            shape((48, width), f32),
            shape((48, width), f32),
            shape((48, 512), f32),
            shape((16, 48), f32),
            shape((4, PIECE, FF), bf),
            shape((PIECE, width), bf),
            shape((4, CHUNK, width), bf),
            shape((3, CHUNK, width), bf),
            shape((3, CHUNK, width), bf),
        ),
        in_specs=[hbm] * 9 + [smem] + [hbm] * 7,
        out_specs=[hbm] * 4 + [vmem] * 2 + [hbm] * 5,
        scratch_shapes=[
            pltpu.VMEM((width, 2048), bf),
            *[pltpu.VMEM((16, 2, 48, w), bf) for w in widths],
            *[pltpu.VMEM((16, 48, w), bf) for w in widths],
            *dense,
            *([pltpu.VMEM((4, PIECE, FF), bf)] * 3),
            pltpu.VMEM((4, PIECE, FF), bf),
            pltpu.VMEM((4 * PIECE, FF), bf),
            *([pltpu.VMEM((PIECE, width), bf)] * 3),
            pltpu.VMEM((2, PIECE, width), bf),
            pltpu.VMEM((4, 128, width), bf),
            pltpu.VMEM((2, CHUNK, width), bf),
            pltpu.VMEM((2 * QUERY_HEADS * 128, 128), bf),
            pltpu.VMEM((4, CHUNK, 512), bf),
            *([pltpu.VMEM((2, 128, 512), bf)] * 3),
            pltpu.VMEM((2, 128, 128), f32),
            *[pltpu.VMEM(ref.shape, ref.dtype) for ref in (cot, tok, q, kv, att, mixed)],
            pltpu.VMEM((CHUNK, width), bf),
            pltpu.VMEM((CHUNK, width), f32),
            pltpu.VMEM((2, 8, 128), f32),
            pltpu.VMEM((2, 8, 128), f32),
            pltpu.VMEM((16, width), f32),
            *([pltpu.VMEM((48, width), f32)] * 2),
            dma((24,)),
            dma((4,)),
            dma((7,)),
            dma((4,)),
            dma((4,)),
            dma((4,)),
            dma((3,)),
            dma((3,)),
            dma((6, 4)),
            dma((6, 4)),
            dma((6, 4)),
            dma((6, 4)),
            dma((6, 4)),
            dma((6, 4)),
            dma((4, 3)),
            dma((4, 3)),
            dma((4, 3)),
        ],
        compiler_params=pltpu.CompilerParams(
            collective_id=3, has_side_effects=True, vmem_limit_bytes=64 * 2**20 - 65536
        ),
        name="backward_stage",
    )(dx, dgt, gates, mixed, cot, tok, q, kv, att, lens, small, rope, wa, wb, gin, gout, outp)


def finish_kernel(
    block_in,
    dtok_in,
    gq_in,
    gb_in,
    gkv_in,
    small_ref,
    first_ref,
    second_ref,
    down_first_ref,
    down_second_ref,
    block_out,
    dtok_out,
    gq_out,
    gb_out,
    gkv_out,
    pre_out,
    mid_out,
    router_out,
    in_out,
    down_out,
):
    f32 = jnp.float32
    i = pl.program_id(0)
    block_out[...] = block_in[...]
    dtok_out[...] = dtok_in[...]
    gq_out[...] = gq_in[...]
    gb_out[...] = gb_in[...]
    gkv_out[...] = gkv_in[...]
    half = FF // 2
    first = first_ref[...].astype(f32)
    second = second_ref[...].astype(f32)
    in_out[:, :half] = first[:, :half]
    in_out[:, half:FF] = second[:, :half]
    in_out[:, FF : FF + half] = first[:, half:]
    in_out[:, FF + half :] = second[:, half:]
    down_out[...] = jnp.where(i < 1, down_first_ref[...], down_second_ref[...]).astype(f32)
    router_out[...] = small_ref[:8]
    pre_out[...] = small_ref[8:9]
    mid_out[...] = small_ref[9:10]


def finish_stage(block, dtok, gq, gb, gkv, small, first, second, down_first, down_second):
    f32 = jnp.float32
    shape = jax.ShapeDtypeStruct
    width = block.shape[-1]

    def rows(count, columns, index):
        return pl.BlockSpec((count, columns), index)

    def whole(count, columns):
        return pl.BlockSpec((count, columns), lambda i: (0, 0))

    return pl.pallas_call(
        finish_kernel,
        grid=(2,),
        out_shape=(
            shape(block.shape, block.dtype),
            shape(dtok.shape, f32),
            shape(gq.shape, f32),
            shape(gb.shape, f32),
            shape(gkv.shape, f32),
            shape((1, 48), f32),
            shape((1, 48), f32),
            shape((8, 48), f32),
            shape((384, 2 * FF), f32),
            shape((192, width), f32),
        ),
        in_specs=[
            rows(128, width, lambda i: (i, 0)),
            rows(128, width, lambda i: (i, 0)),
            whole(48, width),
            whole(48, width),
            whole(48, 512),
            whole(16, 48),
            rows(192, FF, lambda i: (i, 0)),
            rows(192, FF, lambda i: (i, 0)),
            whole(96, width),
            whole(96, width),
        ],
        out_specs=[
            rows(128, width, lambda i: (i, 0)),
            rows(128, width, lambda i: (i, 0)),
            whole(48, width),
            whole(48, width),
            whole(48, 512),
            whole(1, 48),
            whole(1, 48),
            whole(8, 48),
            rows(192, 2 * FF, lambda i: (i, 0)),
            rows(96, width, lambda i: (i, 0)),
        ],
        compiler_params=pltpu.CompilerParams(vmem_limit_bytes=32 * 2**20),
        name="finish_stage",
    )(block, dtok, gq, gb, gkv, small, first, second, down_first, down_second)


def rope_constant(slots):
    half = HEAD_SIZE // 2
    inv_freq = np.float32(rope_base) ** (-(np.arange(half, dtype=np.float32) * 2.0 / HEAD_SIZE))
    angles = np.arange(slots, dtype=np.float32)[:, None] * inv_freq[None, :].astype(np.float32)
    cos, sin = np.cos(angles), np.sin(angles)
    return np.stack(
        [np.concatenate([cos, cos], axis=1), np.concatenate([-sin, sin], axis=1)]
    ).astype(np.float32)


def fast_local(
    tokens,
    lengths,
    routes,
    prenorm,
    w_query,
    key_value_weight,
    w_output,
    midnorm,
    w_router,
    expert_in,
    expert_out,
    cotangent,
):
    seqs, token_rows, width = tokens.shape
    rows = seqs * token_rows
    tok = tokens.reshape(rows, width)
    cot = cotangent.reshape(rows, width)
    rope = jnp.asarray(rope_constant(token_rows * lax.axis_size("dp")))
    full_a, full_b, full_out, gall, q_rot, kv_all, attended, mixed, normed2, gates, small_t = attention_stage(
        tok,
        w_query,
        key_value_weight,
        w_router.T,
        prenorm[None],
        midnorm[None],
        w_output,
        cot,
        expert_out[0],
        rope,
        lengths,
        jnp.transpose(routes, (0, 2, 1)),
    )
    dx, dgate, outp, gin, gout, out_first, g_first = expert_stage(normed2, gall, gates, expert_in[0], full_out)
    block_out, grad_tokens, g_query, g_b, g_kv, small, g_second, out_second = backward_stage(
        dx, dgate, gates, mixed, cot, tok, q_rot, kv_all, attended, lengths, small_t, rope,
        full_a, full_b, gin.reshape(width, FF), gout, outp.reshape(8 * rows, width),
    )[:8]
    block_out, grad_tokens, g_query, g_b, g_kv, g_pre, g_mid, g_router, g_in, g_out = finish_stage(
        block_out,
        grad_tokens,
        g_query,
        g_b,
        g_kv,
        small,
        g_first.reshape(width // 4, FF),
        g_second.reshape(width // 4, FF),
        out_first.reshape(FF // 8, width),
        out_second,
    )
    return (
        block_out.reshape(seqs, token_rows, width),
        grad_tokens.reshape(seqs, token_rows, width),
        g_pre.reshape(-1),
        g_query,
        g_kv,
        g_b,
        g_mid.reshape(-1),
        g_router.T,
        g_in[None],
        g_out[None],
    )


def solution(mesh):
    placed = (
        P("expert", "dp", None),
        P("expert"),
        P("expert", "dp", None),
        P(("dp", "expert")),
        P(("dp", "expert"), None),
        P(("dp", "expert"), None),
        P(("dp", "expert"), None),
        P(("dp", "expert")),
        P(("dp", "expert"), None),
        P("expert", "dp", None),
        P("expert", "dp", None),
        P("expert", "dp", None),
    )
    fits = mesh.shape["dp"] == 4 and mesh.shape["expert"] == 8
    return jax.shard_map(
        fast_local if fits else local,
        mesh=mesh,
        in_specs=placed,
        out_specs=(
            P("expert", "dp", None),
            P("expert", "dp", None),
            P(("dp", "expert")),
            P(("dp", "expert"), None),
            P(("dp", "expert"), None),
            P(("dp", "expert"), None),
            P(("dp", "expert")),
            P(("dp", "expert"), None),
            P("expert", "dp", None),
            P("expert", "dp", None),
        ),
        check_vma=False,
    )
```

```python
import jax
import jax.numpy as jnp
import numpy as np
from jax import lax
from jax.experimental import pallas as pl
from jax.experimental.pallas import tpu as pltpu
from jax.sharding import PartitionSpec as P

QUERY_HEADS = 12
KEY_VALUE_HEADS = 2
HEAD_SIZE = 128
FF = 768
TOP = 4


epsilon = 1e-06
rope_base = 10000.0
highest = lax.Precision.HIGHEST


def rope_tables(positions):
    half_width = HEAD_SIZE // 2
    inv_freq = rope_base ** (-(jnp.arange(half_width, dtype=jnp.float32) * 2.0 / HEAD_SIZE))
    angles = positions.astype(jnp.float32)[:, None] * inv_freq[None, :]
    return (jnp.cos(angles), jnp.sin(angles))


def apply_rotation(values, cosine_table, sine_table):
    half_width = values.shape[-1] // 2
    first_half = values[..., :half_width]
    second = values[..., half_width:]
    cos_rows = cosine_table[:, None, :]
    sin_rows = sine_table[:, None, :]
    return jnp.concatenate(
        [first_half * cos_rows - second * sin_rows, second * cos_rows + first_half * sin_rows],
        axis=-1,
    )


def unrotate(values, cosine_table, sine_table):
    half_width = values.shape[-1] // 2
    first_half = values[..., :half_width]
    second = values[..., half_width:]
    cos_rows = cosine_table[:, None, :]
    sin_rows = sine_table[:, None, :]
    return jnp.concatenate(
        [first_half * cos_rows + second * sin_rows, second * cos_rows - first_half * sin_rows],
        axis=-1,
    )


def rms_parts(values):
    inverse = lax.rsqrt(jnp.mean(values * values, axis=-1, keepdims=True) + epsilon)
    return (values * inverse, inverse)


def norm_back(grad_normed, normalized_input, inverse, gain):
    scaled = grad_normed * gain
    return inverse * (
        scaled - normalized_input * jnp.mean(scaled * normalized_input, axis=-1, keepdims=True)
    )


def slot_index(route_rows, expert_count, capacity):
    flat_routes = route_rows.reshape(-1)
    onehot = (flat_routes[:, None] == jnp.arange(expert_count, dtype=jnp.int32)[None, :]).astype(
        jnp.int32
    )
    before = jnp.cumsum(onehot, axis=0) - onehot
    within = jnp.sum(before * onehot, axis=-1)
    return flat_routes * capacity + within


def masked_scores(query_matrix, key_rows, allowed):
    scores = jnp.einsum(
        "qhgd,khd->hgqk", query_matrix, key_rows, preferred_element_type=jnp.float32
    ) * HEAD_SIZE ** (-0.5)
    return jnp.where(allowed[None, None], scores, -1e30)


def local(
    tokens,
    lengths,
    routes,
    prenorm,
    w_query,
    key_value_weight,
    w_output,
    midnorm,
    w_router,
    expert_in,
    expert_out,
    cotangent,
):
    micro_count, token_rows, hidden_width = tokens.shape
    dp_size = lax.axis_size("dp")
    expert_size = lax.axis_size("expert")
    dp_rank = lax.axis_index("dp")
    local_experts = expert_in.shape[0]
    expert_count = local_experts * expert_size
    capacity = max(2, 3 * token_rows * TOP // (2 * expert_count))
    query_group_width = QUERY_HEADS // KEY_VALUE_HEADS
    expert_slot_total = token_rows * dp_size
    score_scale = HEAD_SIZE ** (-0.5)
    positions = dp_rank * token_rows + jnp.arange(token_rows, dtype=jnp.int32)
    key_pos = jnp.arange(expert_slot_total, dtype=jnp.int32)
    cosine_table, sine_table = rope_tables(positions)
    total_prenorm = jnp.zeros((hidden_width,), jnp.float32)
    total_query = jnp.zeros((hidden_width, QUERY_HEADS * HEAD_SIZE), jnp.float32)
    total_key_value = jnp.zeros((hidden_width, 2 * KEY_VALUE_HEADS * HEAD_SIZE), jnp.float32)
    total_output = jnp.zeros((QUERY_HEADS * HEAD_SIZE, hidden_width), jnp.float32)
    total_midnorm = jnp.zeros((hidden_width,), jnp.float32)
    total_router = jnp.zeros((hidden_width, expert_count), jnp.float32)
    total_upper = jnp.zeros((local_experts, hidden_width, 2 * FF), jnp.float32)
    total_down = jnp.zeros((local_experts, FF, hidden_width), jnp.float32)
    outputs_list = []
    grads_list = []
    for micro_step in range(micro_count):
        dense_all = (
            lax.all_gather(prenorm, ("dp", "expert"), axis=0, tiled=True),
            lax.all_gather(w_query, ("dp", "expert"), axis=0, tiled=True),
            lax.all_gather(key_value_weight, ("dp", "expert"), axis=0, tiled=True),
            lax.all_gather(w_output, ("dp", "expert"), axis=0, tiled=True),
            lax.all_gather(midnorm, ("dp", "expert"), axis=0, tiled=True),
            lax.all_gather(w_router, ("dp", "expert"), axis=0, tiled=True),
        )
        expert_all = (
            lax.all_gather(expert_in, "dp", axis=1, tiled=True),
            lax.all_gather(expert_out, "dp", axis=1, tiled=True),
        )
        gain_one = dense_all[0].astype(jnp.float32)
        query_all = dense_all[1]
        keyval_all = dense_all[2]
        output_all = dense_all[3]
        gain_two = dense_all[4].astype(jnp.float32)
        router_all = dense_all[5]
        gateup_all = expert_all[0]
        down_all = expert_all[1]
        input_rows = tokens[micro_step].astype(jnp.float32)
        length = lengths[micro_step]
        route_rows = routes[micro_step]
        live_rows = (positions < length)[:, None]
        normed_one, inverse_one = rms_parts(input_rows)
        normalized_input = (normed_one * gain_one).astype(jnp.bfloat16)
        query_pre = jnp.dot(
            normalized_input, query_all, preferred_element_type=jnp.float32
        ).reshape(token_rows, QUERY_HEADS, HEAD_SIZE)
        keyval_pre = jnp.dot(
            normalized_input, keyval_all, preferred_element_type=jnp.float32
        ).reshape(token_rows, 2, KEY_VALUE_HEADS, HEAD_SIZE)
        query_matrix = (
            apply_rotation(query_pre, cosine_table, sine_table)
            .astype(jnp.bfloat16)
            .reshape(token_rows, KEY_VALUE_HEADS, query_group_width, HEAD_SIZE)
        )
        local_key_rows = apply_rotation(keyval_pre[:, 0], cosine_table, sine_table).astype(
            jnp.bfloat16
        )
        local_value_rows = keyval_pre[:, 1].astype(jnp.bfloat16)
        packed_tokens = jnp.stack([local_key_rows, local_value_rows], axis=1).reshape(
            token_rows, 2 * KEY_VALUE_HEADS * HEAD_SIZE
        )
        gathered_rows = lax.all_gather(packed_tokens, "dp", axis=0, tiled=True).reshape(
            expert_slot_total, 2, KEY_VALUE_HEADS, HEAD_SIZE
        )
        key_rows = gathered_rows[:, 0]
        value_rows = gathered_rows[:, 1]
        allowed = (key_pos[None, :] <= positions[:, None]) & (key_pos[None, :] < length)
        scores = masked_scores(query_matrix, key_rows, allowed)
        top_score = jnp.max(scores, axis=-1, keepdims=True)
        weights = jnp.exp(scores - top_score)
        weight_total = jnp.sum(weights, axis=-1, keepdims=True)
        log_total = top_score + jnp.log(weight_total)
        probs_low = (weights / weight_total).astype(jnp.bfloat16)
        attended = jnp.einsum(
            "hgqk,khd->qhgd", probs_low, value_rows, preferred_element_type=jnp.float32
        )
        attended = attended.reshape(token_rows, QUERY_HEADS * HEAD_SIZE).astype(jnp.bfloat16)
        mixed_rows = input_rows + jnp.dot(attended, output_all, preferred_element_type=jnp.float32)
        normed_mid, inverse_two = rms_parts(mixed_rows)
        normed_two = (normed_mid * gain_two).astype(jnp.bfloat16)
        logits = jnp.dot(normed_two, router_all, preferred_element_type=jnp.float32)
        onehot = (
            route_rows[:, :, None] == jnp.arange(expert_count, dtype=jnp.int32)[None, None, :]
        ).astype(jnp.float32)
        chosen = jnp.sum(onehot * logits[:, None, :], axis=-1)
        gate_values = jax.nn.softmax(chosen, axis=-1)
        slot_idx = slot_index(route_rows, expert_count, capacity)
        send_rows = jnp.zeros((expert_count * capacity, hidden_width), jnp.bfloat16)
        send_rows = send_rows.at[slot_idx].set(jnp.repeat(normed_two, TOP, axis=0))
        received = lax.all_to_all(
            send_rows.reshape(expert_count, capacity, hidden_width),
            "expert",
            split_axis=0,
            concat_axis=0,
            tiled=True,
        )
        item_count = received.shape[1]
        grouped = received.reshape(expert_size, local_experts, item_count, hidden_width)
        gate_up = jnp.einsum(
            "slcd,ldf->slcf", grouped, gateup_all, preferred_element_type=jnp.float32
        )
        hidden = (jax.nn.silu(gate_up[..., :FF]) * gate_up[..., FF:]).astype(jnp.bfloat16)
        result = jnp.einsum(
            "slcf,lfd->slcd", hidden, down_all, preferred_element_type=jnp.float32
        ).astype(jnp.bfloat16)
        back_rows = lax.all_to_all(
            result.reshape(expert_count, item_count, hidden_width),
            "expert",
            split_axis=0,
            concat_axis=0,
            tiled=True,
        )
        back_rows, kept_rows, kept_gateup = (
            back_rows,
            received,
            gate_up.reshape(expert_count, item_count, 2 * FF),
        )
        returned = back_rows.reshape(expert_count * capacity, hidden_width)[slot_idx].reshape(
            token_rows, TOP, hidden_width
        )
        returned_wide = returned.astype(jnp.float32)
        expert_sum = jnp.sum(gate_values[:, :, None] * returned_wide, axis=1)
        final_rows = jnp.where(live_rows, mixed_rows + expert_sum, 0.0)
        outputs_list.append(final_rows.astype(jnp.bfloat16))
        grad_rows = jnp.where(live_rows, cotangent[micro_step].astype(jnp.float32), 0.0)
        grad_gate = jnp.sum(grad_rows[:, None, :] * returned_wide, axis=-1)
        grad_chosen = gate_values * (
            grad_gate - jnp.sum(gate_values * grad_gate, axis=-1, keepdims=True)
        )
        grad_logits = jnp.sum(onehot * grad_chosen[:, :, None], axis=1)
        router_term = jnp.dot(normed_two.astype(jnp.float32).T, grad_logits, precision=highest)
        grad_normtwo = jnp.dot(grad_logits, router_all.astype(jnp.float32).T, precision=highest)
        grad_result = (
            (gate_values[:, :, None] * grad_rows[:, None, :])
            .astype(jnp.bfloat16)
            .reshape(token_rows * TOP, hidden_width)
        )
        send_grads = (
            jnp.zeros((expert_count * capacity, hidden_width), jnp.bfloat16)
            .at[slot_idx]
            .set(grad_result)
        )
        recv_grads, again_rows = (
            lax.all_to_all(
                send_grads.reshape(expert_count, capacity, hidden_width),
                "expert",
                split_axis=0,
                concat_axis=0,
                tiled=True,
            ),
            lax.all_to_all(
                send_rows.reshape(expert_count, capacity, hidden_width),
                "expert",
                split_axis=0,
                concat_axis=0,
                tiled=True,
            ),
        )
        grouped_rows = again_rows.reshape(expert_size, local_experts, capacity, hidden_width)
        gate_up = jnp.einsum(
            "slcd,ldf->slcf", grouped_rows, gateup_all, preferred_element_type=jnp.float32
        )
        grouped_grads = recv_grads.reshape(expert_size, local_experts, capacity, hidden_width)
        gate_part = gate_up[..., :FF]
        up_part = gate_up[..., FF:]
        sigmoid_gate = jax.nn.sigmoid(gate_part)
        silu_gate = gate_part * sigmoid_gate
        hidden = (silu_gate * up_part).astype(jnp.bfloat16)
        grad_hidden = jnp.einsum(
            "slcd,lfd->slcf", grouped_grads, down_all, preferred_element_type=jnp.float32
        )
        down_term = jnp.einsum(
            "slcf,slcd->lfd", hidden, grouped_grads, preferred_element_type=jnp.float32
        )
        grad_gatepart = (
            grad_hidden * up_part * sigmoid_gate * (1.0 + gate_part * (1.0 - sigmoid_gate))
        )
        grad_gateup = jnp.concatenate([grad_gatepart, grad_hidden * silu_gate], axis=-1).astype(
            jnp.bfloat16
        )
        upper_term = jnp.einsum(
            "slcd,slcf->ldf", grouped_rows, grad_gateup, preferred_element_type=jnp.float32
        )
        grad_copies = jnp.einsum(
            "slcf,ldf->slcd", grad_gateup, gateup_all, preferred_element_type=jnp.float32
        ).astype(jnp.bfloat16)
        back_grads = lax.all_to_all(
            grad_copies.reshape(expert_count, capacity, hidden_width),
            "expert",
            split_axis=0,
            concat_axis=0,
            tiled=True,
        )
        copy_rows = back_grads.reshape(expert_count * capacity, hidden_width)[slot_idx].reshape(
            token_rows, TOP, hidden_width
        )
        grad_normtwo = grad_normtwo + jnp.sum(copy_rows.astype(jnp.float32), axis=1)
        midnorm_term = jnp.sum(grad_normtwo * normed_mid, axis=0)
        grad_mixed = grad_rows + norm_back(grad_normtwo, normed_mid, inverse_two, gain_two)
        grad_proj = grad_mixed.astype(jnp.bfloat16)
        output_term = jnp.dot(attended.T, grad_proj, preferred_element_type=jnp.float32)
        attention_gradient = jnp.dot(
            grad_proj, output_all.T, preferred_element_type=jnp.float32
        ).astype(jnp.bfloat16)
        attention_gradient = attention_gradient.reshape(
            token_rows, KEY_VALUE_HEADS, query_group_width, HEAD_SIZE
        )
        scores = masked_scores(query_matrix, key_rows, allowed)
        prob_rows = jnp.exp(scores - log_total)
        grad_probs = jnp.einsum(
            "qhgd,khd->hgqk", attention_gradient, value_rows, preferred_element_type=jnp.float32
        )
        row_delta = jnp.sum(prob_rows * grad_probs, axis=-1, keepdims=True)
        grad_scores = (prob_rows * (grad_probs - row_delta)).astype(jnp.bfloat16)
        prob_low = prob_rows.astype(jnp.bfloat16)
        grad_qrot = (
            jnp.einsum("hgqk,khd->qhgd", grad_scores, key_rows, preferred_element_type=jnp.float32)
            * score_scale
        )
        grad_keys = (
            jnp.einsum(
                "hgqk,qhgd->khd", grad_scores, query_matrix, preferred_element_type=jnp.float32
            )
            * score_scale
        )
        grad_vals = jnp.einsum(
            "hgqk,qhgd->khd", prob_low, attention_gradient, preferred_element_type=jnp.float32
        )
        own_keys = (
            lax.psum_scatter(
                jnp.stack([grad_keys, grad_vals], axis=1)
                .reshape(lax.axis_size("dp") * token_rows, 2 * KEY_VALUE_HEADS * HEAD_SIZE)
                .astype(jnp.bfloat16),
                "dp",
                scatter_dimension=0,
                tiled=True,
            )
            .astype(jnp.float32)
            .reshape(token_rows, 2, KEY_VALUE_HEADS, HEAD_SIZE)
        )
        grad_query = (
            unrotate(
                grad_qrot.reshape(token_rows, QUERY_HEADS, HEAD_SIZE), cosine_table, sine_table
            )
            .astype(jnp.bfloat16)
            .reshape(token_rows, QUERY_HEADS * HEAD_SIZE)
        )
        key_gradient = unrotate(own_keys[:, 0], cosine_table, sine_table).astype(jnp.bfloat16)
        value_gradient = own_keys[:, 1].astype(jnp.bfloat16)
        key_value_weight_gradient = jnp.stack([key_gradient, value_gradient], axis=1).reshape(
            token_rows, 2 * KEY_VALUE_HEADS * HEAD_SIZE
        )
        query_term = jnp.dot(normalized_input.T, grad_query, preferred_element_type=jnp.float32)
        keyval_term = jnp.dot(
            normalized_input.T, key_value_weight_gradient, preferred_element_type=jnp.float32
        )
        grad_normone = jnp.dot(grad_query, query_all.T, preferred_element_type=jnp.float32)
        grad_normone = grad_normone + jnp.dot(
            key_value_weight_gradient, keyval_all.T, preferred_element_type=jnp.float32
        )
        prenorm_term = jnp.sum(grad_normone * normed_one, axis=0)
        grads_list.append(grad_mixed + norm_back(grad_normone, normed_one, inverse_one, gain_one))
        total_prenorm = total_prenorm + prenorm_term
        total_query = total_query + query_term
        total_key_value = total_key_value + keyval_term
        total_output = total_output + output_term
        total_midnorm = total_midnorm + midnorm_term
        total_router = total_router + router_term
        total_upper = total_upper + upper_term
        total_down = total_down + down_term
    dense_grads = (
        lax.psum_scatter(total_prenorm, ("dp", "expert"), scatter_dimension=0, tiled=True),
        lax.psum_scatter(total_query, ("dp", "expert"), scatter_dimension=0, tiled=True),
        lax.psum_scatter(total_key_value, ("dp", "expert"), scatter_dimension=0, tiled=True),
        lax.psum_scatter(total_output, ("dp", "expert"), scatter_dimension=0, tiled=True),
        lax.psum_scatter(total_midnorm, ("dp", "expert"), scatter_dimension=0, tiled=True),
        lax.psum_scatter(total_router, ("dp", "expert"), scatter_dimension=0, tiled=True),
    )
    expert_grads = (
        lax.psum_scatter(
            total_upper.astype(jnp.bfloat16), "dp", scatter_dimension=1, tiled=True
        ).astype(jnp.float32),
        lax.psum_scatter(
            total_down.astype(jnp.bfloat16), "dp", scatter_dimension=1, tiled=True
        ).astype(jnp.float32),
    )
    return (
        jnp.stack(outputs_list),
        jnp.stack(grads_list),
        dense_grads[0],
        dense_grads[1],
        dense_grads[2],
        dense_grads[3],
        dense_grads[4],
        dense_grads[5],
        expert_grads[0],
        expert_grads[1],
    )


MESH = pl.DeviceIdType.MESH
CHUNK = 256
PIECE = 96


def remote(src, dst, send_sem, recv_sem, target):
    return pltpu.make_async_remote_copy(
        src_ref=src,
        dst_ref=dst,
        send_sem=send_sem,
        recv_sem=recv_sem,
        device_id=target,
        device_id_type=MESH,
    )


def place():
    d = lax.axis_index("dp")
    e = lax.axis_index("expert")
    z = lax.div(e, 2)
    c = lax.rem(e, 2)
    x = lax.rem(d, 2)
    y = lax.div(d, 2)
    return d, e, z, c, x, y


def attention_kernel(
    tok_hbm,
    wq_hbm,
    wkv_hbm,
    wr_ref,
    pre_ref,
    mid_ref,
    wb_hbm,
    cot_hbm,
    wo_hbm,
    rope_hbm,
    lens_ref,
    routes_ref,
    wa_out,
    wb_out,
    wo_out,
    gall,
    q_out,
    kv_out,
    att_out,
    mixed_hbm,
    normed_hbm,
    gates_out,
    small_out,
    wa,
    wb,
    qs,
    kvs,
    att,
    g_own,
    rope,
    tok_ref,
    cot_ref,
    mixed_out,
    normed_out,
    own_sem,
    wo_recv,
    wo_send,
    z_recv,
    z_send,
    xy_recv,
    xy_send,
    sib_recv,
    sib_send,
    g_recv,
    g_send,
    gs_recv,
    gs_send,
    kv_recv,
    kv_send,
):
    bf, f32 = jnp.bfloat16, jnp.float32
    d, e, z, c, x, y = place()
    d_x = d + 1 - 2 * x
    d_y = d + 2 - 4 * y
    d_d = 3 - d
    other = 1 - c
    to_x = (d_x, e)
    to_y = (d_y, e)
    to_sib = (d, 2 * z + other)
    to_up = (d, e + jnp.where(z < 3, 2, -2))
    to_down = (d, e + jnp.where(z > 0, -2, 2))

    barrier = pltpu.get_barrier_semaphore()
    for target in (to_x, to_y, to_sib):
        pl.semaphore_signal(barrier, inc=1, device_id=target, device_id_type=MESH)

    @pl.when(z < 3)
    def _():
        pl.semaphore_signal(barrier, inc=1, device_id=to_up, device_id_type=MESH)

    @pl.when(z > 0)
    def _():
        pl.semaphore_signal(barrier, inc=1, device_id=to_down, device_id_type=MESH)

    own_at = pl.multiple_of((d * 8 + e) * 48, 16)
    own_rows = pl.ds(own_at, 48)
    own_a = [
        pltpu.make_async_copy(wq_hbm, wa.at[own_rows, pl.ds(0, 1536)], own_sem.at[0]),
        pltpu.make_async_copy(wkv_hbm, wa.at[own_rows, pl.ds(1536, 512)], own_sem.at[1]),
        pltpu.make_async_copy(rope_hbm.at[:, pl.ds(pl.multiple_of(d * 128, 128), 128)], rope, own_sem.at[2]),
    ]
    loads = [
        pltpu.make_async_copy(cot_hbm, cot_ref, own_sem.at[8]),
        pltpu.make_async_copy(tok_hbm, tok_ref, own_sem.at[9]),
    ]
    for copy in own_a + loads:
        copy.start()
    eye = lax.broadcasted_iota(jnp.int32, (128, 128), 0) == lax.broadcasted_iota(
        jnp.int32, (128, 128), 1
    )
    eye_low = eye.astype(bf)
    turned = (((0,), (0,)), ((), ()))
    sub = lax.broadcasted_iota(jnp.int32, (8, 48), 0)
    gains = jnp.where(
        sub == 0,
        pre_ref[...].astype(f32),
        jnp.where(sub == 1, mid_ref[...].astype(f32), 0.0),
    )
    tile = jnp.concatenate([wr_ref[...].astype(f32), gains], axis=0).astype(bf)
    wa[own_rows, 2048:] = lax.dot_general(
        tile, eye_low[:16], turned, preferred_element_type=f32
    ).astype(bf)
    full = (wa, wb)
    shard = (None, wb_hbm)

    def block(a, dd, zp, lane):
        at = pl.multiple_of((dd * 8 + 2 * zp + lane) * 48, 16)
        return full[a].at[pl.ds(at, 48)]

    def z_copy(a, zp, way, src=None):
        ref = block(a, d, zp, c)
        return remote(
            ref if src is None else src,
            ref,
            z_send.at[a, way, zp],
            z_recv.at[a, zp],
            to_up if way == 0 else to_down,
        )

    def xy_copy(a, dd, zp, row, target, src=None):
        ref = block(a, dd, zp, c)
        return remote(
            ref if src is None else src,
            ref,
            xy_send.at[a, row, zp],
            xy_recv.at[a, row, zp],
            target,
        )

    def s_copy(a, dd, zp, src=None, lane=None):
        ref = block(a, dd, zp, c if lane is None else lane)
        return remote(
            ref if src is None else src,
            ref,
            sib_send.at[a, dd, zp],
            sib_recv.at[a, dd, zp],
            to_sib,
        )

    def send_xy(a, zp):
        xy_copy(a, d, zp, 0, to_x).start()
        xy_copy(a, d, zp, 1, to_y).start()

    def own_start(a):
        @pl.when(z < 3)
        def _():
            z_copy(a, z, 0, shard[a]).start()

        @pl.when(z > 0)
        def _():
            z_copy(a, z, 1, shard[a]).start()

        s_copy(a, d, z, shard[a]).start()

    def from_z(a, k):
        def arrived(zp, way):
            z_copy(a, zp, way).wait_recv()

            @pl.when((z < 3) if way == 0 else (z > 0))
            def _():
                z_copy(a, zp, way).start()

            if a == 0:
                send_xy(a, zp)
            s_copy(a, d, zp).start()

        @pl.when(z - k >= 0)
        def _():
            arrived(z - k, 0)

        @pl.when(z + k <= 3)
        def _():
            arrived(z + k, 1)

    def from_xy_one(a, zp):
        xy_copy(a, d_x, zp, 0, to_x).wait_recv()

        @pl.when(lax.rem(zp, 2) == 0)
        def _():
            xy_copy(a, d_x, zp, 2, to_y).start()

        s_copy(a, d_x, zp).start()
        xy_copy(a, d_y, zp, 1, to_y).wait_recv()

        @pl.when(lax.rem(zp, 2) == 1)
        def _():
            xy_copy(a, d_y, zp, 2, to_x).start()

        s_copy(a, d_y, zp).start()

    def from_xy(a, k):
        @pl.when(z - k >= 0)
        def _():
            from_xy_one(a, z - k)

        if k > 0:

            @pl.when(z + k <= 3)
            def _():
                from_xy_one(a, z + k)

    def from_diag(a):
        for k in range(4):
            zp = lax.rem(z + k, 4)
            xy_copy(a, d_d, zp, 2, to_x).wait_recv()
            s_copy(a, d_d, zp).start()

    def from_sib(a):
        for dd in range(4):
            for zp in range(4):
                s_copy(a, dd, zp, lane=other).wait_recv()

    def drain(a):
        for zp in range(4):
            for dd in range(4):
                s_copy(a, dd, zp).wait_send()
            for row in range(3):
                xy_copy(a, d, zp, row, to_x).wait_send()

            @pl.when((zp <= z) & (z < 3))
            def _():
                z_copy(a, zp, 0).wait_send()

            @pl.when((zp >= z) & (z > 0))
            def _():
                z_copy(a, zp, 1).wait_send()

    def g_part(zp, lane, s):
        at = pl.multiple_of((2 * zp + lane) * CHUNK + s * 128, 128)
        return gall.at[pl.ds(at, 128)]

    def g_copy(zp, s, way, src=None):
        ref = g_part(zp, c, s)
        return remote(
            ref if src is None else src,
            ref,
            g_send.at[way, zp, s],
            g_recv.at[zp, s],
            to_up if way == 0 else to_down,
        )

    def gs_copy(zp, s, src=None, lane=None):
        ref = g_part(zp, c if lane is None else lane, s)
        return remote(
            ref if src is None else src, ref, gs_send.at[zp, s], gs_recv.at[zp, s], to_sib
        )

    def g_start():
        for s in range(2):
            src = g_own.at[pl.ds(s * 128, 128)]

            @pl.when(z < 3)
            def _():
                g_copy(z, s, 0, src).start()

            @pl.when(z > 0)
            def _():
                g_copy(z, s, 1, src).start()

            gs_copy(z, s, src).start()

    def g_pass(k, s):
        @pl.when(z - k >= 0)
        def _():
            g_copy(z - k, s, 0).wait_recv()

            @pl.when(z < 3)
            def _():
                g_copy(z - k, s, 0).start()

            gs_copy(z - k, s).start()

        @pl.when(z + k <= 3)
        def _():
            g_copy(z + k, s, 1).wait_recv()

            @pl.when(z > 0)
            def _():
                g_copy(z + k, s, 1).start()

            gs_copy(z + k, s).start()

    def wo_copy(dd, p, row, target, src=None):
        ref = wo_out.at[pl.ds(pl.multiple_of(dd * 192 + p * PIECE, 16), PIECE)]
        return remote(
            ref if src is None else src, ref, wo_send.at[row, p], wo_recv.at[row, p], target
        )

    def wo_start(p):
        wo_copy(d, p, 0, to_x, wo_hbm.at[pl.ds(p * PIECE, PIECE)]).start()
        wo_copy(d, 1 - p, 1, to_y, wo_hbm.at[pl.ds((1 - p) * PIECE, PIECE)]).start()

    def wo_pass():
        wo_copy(d_x, 0, 0, to_x).wait_recv()
        wo_copy(d_x, 0, 2, to_y).start()
        wo_copy(d_y, 1, 1, to_y).wait_recv()
        wo_copy(d_y, 1, 2, to_x).start()

    def wo_rest():
        wo_copy(d_x, 1, 0, to_x).wait_recv()
        wo_copy(d_y, 0, 1, to_y).wait_recv()
        for p in range(2):
            wo_copy(d_d, p, 2, to_x).wait_recv()

    pl.semaphore_wait(barrier, 5 - jnp.where((z == 0) | (z == 3), 1, 0))
    for copy in own_a:
        copy.wait()
    own_start(0)
    own_start(1)
    own = [
        pltpu.make_async_copy(wb_hbm, block(1, d, z, c), own_sem.at[0]),
        pltpu.make_async_copy(
            g_own, gall.at[pl.ds(pl.multiple_of(e * CHUNK, CHUNK), CHUNK)], own_sem.at[1]
        ),
        pltpu.make_async_copy(
            wo_hbm, wo_out.at[pl.ds(pl.multiple_of(d * 192, 16), 192)], own_sem.at[2]
        ),
    ]
    own[0].start()
    own[2].start()
    send_xy(0, z)
    own[0].wait()
    at_end = (z == 0) | (z == 3)

    @pl.when(at_end)
    def _():
        send_xy(1, z)

    loads[0].wait()
    for s in range(2):
        rows = slice(s * 128, (s + 1) * 128)
        slot = d * 128 + lax.broadcasted_iota(jnp.int32, (128, 1), 0)
        g_own[rows] = jnp.where(slot < lens_ref[s], cot_ref[rows].astype(f32), 0.0).astype(bf)

    own[1].start()
    loads[1].wait()
    tok = tok_ref[...].astype(f32)
    n1 = tok * lax.rsqrt(jnp.mean(tok * tok, axis=1, keepdims=True) + epsilon)
    from_z(0, 1)
    from_z(1, 1)
    from_xy(0, 0)
    from_z(0, 2)
    from_z(1, 2)
    g_start()
    from_xy(0, 1)
    from_z(0, 3)
    from_z(1, 3)
    from_xy(0, 2)
    from_xy(0, 3)

    def turn(j):
        return lax.rem(z + j, 4)

    @pl.when(jnp.logical_not(at_end))
    def _():
        send_xy(1, z)

    send_xy(1, turn(1))
    from_diag(0)
    from_sib(0)

    small_t = lax.dot_general(
        eye_low[:16], wa[:, 2048:], (((1,), (1,)), ((), ())), preferred_element_type=f32
    )
    small_out[...] = small_t
    normed = (n1 * small_t[8:9]).astype(bf)
    cos_rows = jnp.concatenate([rope[0]] * 2, axis=0)
    sin_rows = jnp.concatenate([rope[1]] * 2, axis=0)

    def rotate(v):
        return v * cos_rows + pltpu.roll(v, 64, 1) * sin_rows

    kv = jnp.dot(normed, wa[:, 1536:2048], preferred_element_type=f32)
    for h in range(2):
        kvs[d, :, h * 128 : (h + 1) * 128] = rotate(kv[:, h * 128 : (h + 1) * 128]).astype(bf)
    kvs[d, :, 256:] = kv[:, 256:].astype(bf)

    def kv_copy(dd, s, row, target):
        ref = kvs.at[dd, pl.ds(s * 128, 128)]
        return remote(ref, ref, kv_send.at[row, s], kv_recv.at[row, s], target)

    for s in range(2):
        kv_copy(d, s, 0, to_x).start()
        kv_copy(d, 1 - s, 1, to_y).start()
    send_xy(1, turn(2))
    g_pass(1, 0)
    q = jnp.dot(normed, wa[:, :1536], preferred_element_type=f32)
    for head in range(QUERY_HEADS):
        rot = rotate(q[:, head * 128 : (head + 1) * 128]).astype(bf)
        for s in range(2):
            at = (s * QUERY_HEADS + head) * 128
            qs[at : at + 128] = rot[s * 128 : (s + 1) * 128]
    kv_copy(d_x, 0, 0, to_x).wait_recv()
    kv_copy(d_x, 0, 2, to_y).start()
    kv_copy(d_y, 1, 1, to_y).wait_recv()
    kv_copy(d_y, 1, 2, to_x).start()
    send_xy(1, turn(3))
    for j in range(2):
        from_xy_one(1, turn(j))
    g_pass(1, 1)
    kv_copy(d_y, 0, 1, to_y).wait_recv()
    kv_copy(d_x, 1, 0, to_x).wait_recv()
    for s in range(2):
        kv_copy(d_d, s, 2, to_x).wait_recv()
    q_copy = pltpu.make_async_copy(qs, q_out, own_sem.at[3])
    kvo_copy = pltpu.make_async_copy(kvs, kv_out, own_sem.at[4])
    wa_copy = pltpu.make_async_copy(wa, wa_out, own_sem.at[5])
    for copy in (q_copy, kvo_copy, wa_copy):
        copy.start()

    query_pos = d * 128 + lax.broadcasted_iota(jnp.int32, (128, 512), 0)
    key_pos = lax.broadcasted_iota(jnp.int32, (128, 512), 1)

    def attend(n):
        s = lax.div(n, 2)
        h = lax.rem(n, 2)
        lens = lens_ref[s]
        allowed = (key_pos <= query_pos) & (key_pos < lens)
        ks = kvs[:, pl.ds(pl.multiple_of(s * 128, 128), 128), pl.ds(pl.multiple_of(h * 128, 128), 128)]
        vs = kvs[:, pl.ds(pl.multiple_of(s * 128, 128), 128), pl.ds(pl.multiple_of(256 + h * 128, 128), 128)]
        ks = ks.reshape(512, 128)
        vs = vs.reshape(512, 128)
        for half in range(2):
            qh = qs[pl.ds(pl.multiple_of(n * 768 + half * 384, 128), 384)]
            scores = lax.dot_general(qh, ks, (((1,), (1,)), ((), ())), preferred_element_type=f32)
            scores = scores.reshape(3, 128, 512) * HEAD_SIZE ** (-0.5)
            scores = jnp.where(allowed[None], scores, -1e30)
            top = jnp.max(scores, axis=-1, keepdims=True)
            weights = jnp.exp(scores - top)
            weights = weights * (1.0 / jnp.sum(weights, axis=-1, keepdims=True))
            out = jnp.dot(
                weights.astype(bf).reshape(384, 512), vs, preferred_element_type=f32
            ).astype(bf)
            for j in range(3):
                att[
                    pl.ds(pl.multiple_of(s * 128, 128), 128),
                    pl.ds(pl.multiple_of(h * 768 + (half * 3 + j) * 128, 128), 128),
                ] = out[j * 128 : (j + 1) * 128]

    wo_start(0)
    g_pass(2, 0)
    pl.loop(0, 2)(attend)
    from_xy_one(1, turn(2))
    from_xy_one(1, turn(3))
    wo_start(1)
    g_pass(2, 1)

    @pl.loop(2, 4)
    def _(n):
        attend(n)
        pl.when(n == 2)(wo_pass)

    from_diag(1)
    from_sib(1)
    att_copy = pltpu.make_async_copy(att, att_out, own_sem.at[6])
    wb_copy = pltpu.make_async_copy(wb, wb_out, own_sem.at[7])
    att_copy.start()
    wb_copy.start()
    mixed = tok_ref[...].astype(f32) + jnp.dot(att[...], wb[...], preferred_element_type=f32)
    mixed_out[...] = mixed
    mixed_copy = pltpu.make_async_copy(mixed_out, mixed_hbm, own_sem.at[10])
    mixed_copy.start()
    n2 = mixed * lax.rsqrt(jnp.mean(mixed * mixed, axis=1, keepdims=True) + epsilon)
    normed2 = (n2 * small_t[9:10]).astype(bf)
    normed_out[...] = normed2
    normed_copy = pltpu.make_async_copy(normed_out, normed_hbm, own_sem.at[11])
    normed_copy.start()
    logits = lax.dot_general(
        small_t[:8].astype(bf), normed2, (((1,), (1,)), ((), ())), preferred_element_type=f32
    )
    number = lax.broadcasted_iota(jnp.int32, (8, 128), 0)
    for s in range(2):
        chosen = number == routes_ref[s, 0:1]
        for t in range(1, TOP):
            chosen = chosen | (number == routes_ref[s, t : t + 1])
        picked = jnp.where(chosen, logits[:, s * 128 : (s + 1) * 128], -1e30)
        top = jnp.max(picked, axis=0, keepdims=True)
        weights = jnp.where(chosen, jnp.exp(picked - top), 0.0)
        gates_out[s] = weights / jnp.sum(weights, axis=0, keepdims=True)

    g_pass(3, 0)
    g_pass(3, 1)
    wo_rest()
    for zp in range(4):
        for s in range(2):
            gs_copy(zp, s, lane=other).wait_recv()
    own[1].wait()
    own[2].wait()
    for copy in (q_copy, kvo_copy, wa_copy, att_copy, wb_copy, mixed_copy, normed_copy):
        copy.wait()
    drain(0)
    drain(1)
    for s in range(2):
        for row in range(3):
            kv_copy(d, s, row, to_x).wait_send()
            wo_copy(d, s, row, to_x).wait_send()
        for zp in range(4):
            gs_copy(zp, s).wait_send()

            @pl.when((zp <= z) & (z < 3))
            def _():
                g_copy(zp, s, 0).wait_send()

            @pl.when((zp >= z) & (z > 0))
            def _():
                g_copy(zp, s, 1).wait_send()


def attention_stage(tok, wq, wkv, wr, pre, mid, wb, cot, wo, rope, lens, routes):
    bf, f32 = jnp.bfloat16, jnp.float32
    shape = jax.ShapeDtypeStruct
    width = tok.shape[-1]
    wide = wq.shape[-1] + wkv.shape[-1] + 128
    hbm = pl.BlockSpec(memory_space=pltpu.HBM)
    vmem = pl.BlockSpec(memory_space=pltpu.VMEM)
    smem = pl.BlockSpec(memory_space=pltpu.SMEM)
    dma = pltpu.SemaphoreType.DMA
    return pl.pallas_call(
        attention_kernel,
        out_shape=(
            shape((width, wide), bf),
            shape((width, width), bf),
            shape((FF, width), bf),
            shape((8 * CHUNK, width), bf),
            shape((2 * QUERY_HEADS * 128, 128), bf),
            shape((4, CHUNK, 512), bf),
            shape((CHUNK, width), bf),
            shape((CHUNK, width), f32),
            shape((CHUNK, width), bf),
            shape((2, 8, 128), f32),
            shape((16, width), f32),
        ),
        in_specs=[hbm, hbm, hbm, vmem, vmem, vmem, hbm, hbm, hbm, hbm, smem, vmem],
        out_specs=[hbm] * 9 + [vmem] * 2,
        scratch_shapes=[
            pltpu.VMEM((width, wide), bf),
            pltpu.VMEM((width, width), bf),
            pltpu.VMEM((2 * QUERY_HEADS * 128, 128), bf),
            pltpu.VMEM((4, CHUNK, 512), bf),
            pltpu.VMEM((CHUNK, width), bf),
            pltpu.VMEM((CHUNK, width), bf),
            pltpu.VMEM((2, 128, 128), f32),
            pltpu.VMEM((CHUNK, width), bf),
            pltpu.VMEM((CHUNK, width), bf),
            pltpu.VMEM((CHUNK, width), f32),
            pltpu.VMEM((CHUNK, width), bf),
            dma((12,)),
            dma((3, 2)),
            dma((3, 2)),
            dma((2, 4)),
            dma((2, 2, 4)),
            dma((2, 3, 4)),
            dma((2, 3, 4)),
            dma((2, 4, 4)),
            dma((2, 4, 4)),
            dma((4, 2)),
            dma((2, 4, 2)),
            dma((4, 2)),
            dma((4, 2)),
            dma((3, 2)),
            dma((3, 2)),
        ],
        compiler_params=pltpu.CompilerParams(
            collective_id=2, has_side_effects=True, vmem_limit_bytes=60 * 2**20
        ),
        name="attention_stage",
    )(tok, wq, wkv, wr, pre, mid, wb, cot, wo, rope, lens, routes)


def expert_kernel(
    x_hbm,
    g_hbm,
    gt_hbm,
    win_hbm,
    wout_hbm,
    dx_hbm,
    dgt_out,
    outp_hbm,
    gin_hbm,
    gout_hbm,
    gout_first_hbm,
    gin_first_hbm,
    win,
    wout,
    xall,
    gall,
    gtall,
    dgu,
    hg,
    dxb,
    dgb,
    sibr,
    sibg,
    ro,
    rog,
    ri,
    rig,
    gout,
    tg,
    xg,
    yg,
    gin,
    ti,
    xi,
    yi,
    kept,
    own_sem,
    stage_sem,
    grad_sem,
    g_recv,
    g_send,
    i_recv,
    i_send,
    w_recv,
    w_send,
    ag_recv,
    ag_send,
    sib_recv,
    sib_send,
    red_recv,
    red_send,
    hop_recv,
    hop_send,
):
    bf, f32 = jnp.bfloat16, jnp.float32
    d, e, z, c, x, y = place()
    d_x = d + 1 - 2 * x
    d_y = d + 2 - 4 * y
    d_d = 3 - d
    hi = lax.div(z, 2)
    zz = z * hi + (3 - z) * (1 - hi)
    other = 1 - c
    to_x = (d_x, e)
    to_y = (d_y, e)
    to_sib = (d, 2 * z + other)
    to_up = (d, e + jnp.where(z < 3, 2, -2))
    to_down = (d, e + jnp.where(z > 0, -2, 2))
    e_in = e + 2 - 4 * hi
    to_in = (d, e_in)
    to_out = (d, jnp.where(zz == 2, e - 2 + 4 * hi, e_in))
    mid = zz == 2
    end = zz == 3

    barrier = pltpu.get_barrier_semaphore()
    for target in (to_x, to_y, to_sib, to_in):
        pl.semaphore_signal(barrier, inc=1, device_id=target, device_id_type=MESH)

    @pl.when(mid)
    def _():
        pl.semaphore_signal(barrier, inc=1, device_id=to_out, device_id_type=MESH)

    own_copies = [
        pltpu.make_async_copy(x_hbm.at[s], xall.at[e, s], own_sem.at[s]) for s in range(2)
    ] + [
        pltpu.make_async_copy(gt_hbm, gtall.at[e], own_sem.at[2]),
        pltpu.make_async_copy(wout_hbm, wout, own_sem.at[3]),
        pltpu.make_async_copy(g_hbm, gall, own_sem.at[4]),
    ]

    def w_columns(h, kind):
        return pl.ds(h * 768 + kind * 384, 384)

    for h in range(2):
        for kind in range(2):
            own_copies.append(
                pltpu.make_async_copy(
                    win_hbm.at[:, pl.ds(kind * 768 + h * 384, 384)],
                    win.at[d, :, w_columns(h, kind)],
                    own_sem.at[5 + 2 * h + kind],
                )
            )
    pl.semaphore_wait(barrier, 7 - zz)

    gathered = ((x_hbm, xall), (gt_hbm, gtall))

    def ag_copy(a, zp, s, way, src=None):
        ref = gathered[a][1].at[2 * zp + c, s]
        return remote(
            ref if src is None else src,
            ref,
            ag_send.at[way, a, zp, s],
            ag_recv.at[a, zp, s],
            to_up if way == 0 else to_down,
        )

    def sib_copy(a, zp, s, src=None, lane=None):
        ref = gathered[a][1].at[2 * zp + (c if lane is None else lane), s]
        return remote(
            ref if src is None else src,
            ref,
            sib_send.at[a, zp, s],
            sib_recv.at[a, zp, s],
            to_sib,
        )

    def own_rows(s):
        for a in range(2):
            src = gathered[a][0].at[s]

            @pl.when(z < 3)
            def _():
                ag_copy(a, z, s, 0, src).start()

            @pl.when(z > 0)
            def _():
                ag_copy(a, z, s, 1, src).start()

            sib_copy(a, z, s, src).start()

    def pass_on(k, s):
        for a in range(2):

            @pl.when(z - k >= 0)
            def _():
                ag_copy(a, z - k, s, 0).wait_recv()

                @pl.when(z < 3)
                def _():
                    ag_copy(a, z - k, s, 0).start()

                sib_copy(a, z - k, s).start()

            @pl.when(z + k <= 3)
            def _():
                ag_copy(a, z + k, s, 1).wait_recv()

                @pl.when(z > 0)
                def _():
                    ag_copy(a, z + k, s, 1).start()

                sib_copy(a, z + k, s).start()

    def from_sib(s, pairs):
        for a in range(2):
            for pair in pairs:
                for j in range(2):
                    sib_copy(a, 2 * pair + j, s, lane=other).wait_recv()

    def w_copy(h, kind, p, src_d, target, row, src=None):
        ref = win.at[src_d, pl.ds(p * 192, 192), w_columns(h, kind)]
        return remote(
            ref if src is None else src,
            ref,
            w_send.at[row, h, kind, p],
            w_recv.at[row, h, kind, p],
            target,
        )

    def w_start(h):
        for p in range(2):
            for kind in range(2):

                def src(q):
                    return win_hbm.at[
                        pl.ds(q * 192, 192), pl.ds(kind * 768 + h * 384, 384)
                    ]

                w_copy(h, kind, p, d, to_x, 0, src(p)).start()
                w_copy(h, kind, 1 - p, d, to_y, 1, src(1 - p)).start()

    def w_pass(h):
        for kind in range(2):
            w_copy(h, kind, 0, d_x, to_x, 0).wait_recv()
            w_copy(h, kind, 0, d_x, to_y, 2).start()
            w_copy(h, kind, 1, d_y, to_y, 1).wait_recv()
            w_copy(h, kind, 1, d_y, to_x, 2).start()

    def w_rest(h):
        for kind in range(2):
            w_copy(h, kind, 1, d_x, to_x, 0).wait_recv()
            w_copy(h, kind, 0, d_y, to_y, 1).wait_recv()
            for p in range(2):
                w_copy(h, kind, p, d_d, to_x, 2).wait_recv()

    own_rows(0)
    w_start(0)
    for copy in own_copies:
        copy.start()
    w_pass(0)
    w_start(1)
    pass_on(1, 0)
    pass_on(2, 0)
    own_rows(1)
    w_rest(0)
    w_pass(1)
    pass_on(3, 0)
    from_sib(0, (0, 1))
    for copy in own_copies:
        copy.wait()

    def order(i):
        v = i if i < 2 else (5 - zz if i == 2 else zz)
        return v * hi + (3 - v) * (1 - hi)

    def sib_sum(zp, s, a):
        src, dst = ((dxb, sibr), (dgb, sibg))[a]
        return remote(
            src.at[2 * zp + other, s], dst.at[zp, s], red_send.at[a, zp, s], red_recv.at[a, zp, s], to_sib
        )

    def hop(i, s, target, inward):
        dst, dstg, row = (ro, rog, 2) if inward else (ri, rig, 4)
        zp = order(i)
        halves = [
            remote(
                dxb.at[2 * zp + c, s, pl.ds(h * 64, 64)],
                dst.at[i, s, pl.ds(h * 64, 64)],
                hop_send.at[h, i, s],
                hop_recv.at[row // 2 - 1, h, i, s],
                target,
            )
            for h in range(2)
        ]
        last = remote(
            dgb.at[2 * zp + c, s],
            dstg.at[i, s],
            red_send.at[3, i, s],
            red_recv.at[row + 1, i, s],
            target,
        )
        return halves, last

    def wait_half(ref, slot, s, row, h):
        part = ref.at[slot, s, pl.ds(h * 64, 64)]
        remote(
            part, part, hop_send.at[h, slot, s], hop_recv.at[row // 2 - 1, h, slot, s], to_in
        ).wait_recv()

    def wait_last(refg, slot, s, row):
        remote(
            refg.at[slot, s],
            refg.at[slot, s],
            red_send.at[3, slot, s],
            red_recv.at[row + 1, slot, s],
            to_in,
        ).wait_recv()

    def wait_sib(zp, s):
        for a, ref in enumerate((sibr, sibg)):
            remote(
                ref.at[zp, s], ref.at[zp, s], red_send.at[a, zp, s], red_recv.at[a, zp, s], to_sib
            ).wait_recv()

    def half_sum(zp, s, incoming, h):
        rows = slice(h * 64, (h + 1) * 64)
        total = dxb[2 * zp + c, s, rows].astype(f32) + sibr[zp, s, rows].astype(f32)
        for ref, refg, slot, row in incoming:
            wait_half(ref, slot, s, row, h)
            total = total + ref[slot, s, rows].astype(f32)
        return total

    def gate_sum(zp, s, incoming):
        total = dgb[2 * zp + c, s] + sibg[zp, s]
        for ref, refg, slot, row in incoming:
            wait_last(refg, slot, s, row)
            total = total + refg[slot, s]
        return total

    def pass_sum(i, s, incoming, target, inward):
        zp = order(i)
        wait_sib(zp, s)
        halves, last = hop(i, s, target, inward)
        for h in range(2):
            dxb[2 * zp + c, s, h * 64 : (h + 1) * 64] = half_sum(zp, s, incoming, h).astype(bf)
            halves[h].start()
        dgb[2 * zp + c, s] = gate_sum(zp, s, incoming)
        last.start()

    def end_sums(s, which):
        @pl.when(end)
        def _():
            for i in which:
                pass_sum(i, s, (), to_in, True)

    def mid_sum(i, s):
        @pl.when(mid)
        def _():
            if i < 2:
                pass_sum(i, s, ((ro, rog, i, 2),), to_in, False)
            else:
                pass_sum(2, s, ((ri, rig, 0, 4),), to_out, False)

    def dx_copy(s):
        part = pl.ds(4 * s, 4)
        return pltpu.make_async_copy(kept.at[part], dx_hbm.at[part], own_sem.at[4 + s])

    def dx_store(s, incoming):
        zp = order(3)
        wait_sib(zp, s)
        for h in range(2):
            total = half_sum(zp, s, incoming, h)
            for j in range(4):
                kept[4 * s + j, h * 64 : (h + 1) * 64] = total[:, j * 384 : (j + 1) * 384]
        dgt_out[s] = gate_sum(zp, s, incoming)

    def last_sum(s):
        @pl.when(mid)
        def _():
            dx_store(s, ((ro, rog, 2, 2), (ri, rig, 1, 4)))

        @pl.when(end)
        def _():
            dx_store(s, ((ri, rig, 2, 4),))

        dx_copy(s).start()

    eye = lax.broadcasted_iota(jnp.int32, (128, 128), 0) == lax.broadcasted_iota(
        jnp.int32, (128, 128), 1
    )
    mine = lax.broadcasted_iota(jnp.int32, (8, 128), 0) == e
    nt = (((1,), (1,)), ((), ()))
    tn = (((0,), (0,)), ((), ()))

    def half_step(s, pair, h):
        first = 4 * pair
        block = pl.ds(first, 4)
        both = jnp.dot(
            xall[block, s].reshape(512, 1536),
            win[:, :, h * 768 : (h + 1) * 768].reshape(1536, 768),
            preferred_element_type=f32,
        )
        gate = both[:, :384]
        up = both[:, 384:]
        if h == 0:
            full = lax.dot_general(
                gall[block, s].reshape(512, 1536), wout[...], nt, preferred_element_type=f32
            )
            kept[block] = full[:, 384:].reshape(4, 128, 384)
            back = full[:, :384]
        else:
            back = kept[block].reshape(512, 384)
        columns = []
        for j in range(4):
            row = jnp.sum(jnp.where(mine, gtall[first + j, s], 0.0), axis=0, keepdims=True)
            columns.append(jnp.sum(jnp.where(eye, row, 0.0), axis=1, keepdims=True))
        weight = jnp.concatenate(columns, axis=0)
        sig = jax.nn.sigmoid(gate)
        silu = gate * sig
        hidden = (silu * up).astype(bf).astype(f32)
        dgate = jnp.sum(hidden * back, axis=1, keepdims=True)
        for j in range(4):
            row = jnp.sum(
                jnp.where(eye, dgate[j * 128 : (j + 1) * 128], 0.0), axis=0, keepdims=True
            )
            part = jnp.where(mine, row, 0.0)
            dgb[first + j, s] = part if h == 0 else dgb[first + j, s] + part
        hg[block, s, :, h * 384 : (h + 1) * 384] = (
            (hidden * weight).astype(bf).reshape(4, 128, 384)
        )
        back = back * weight
        dgu[block, s, :, h * 768 : h * 768 + 384] = (
            (back * up * (sig * (1.0 + gate * (1.0 - sig)))).astype(bf).reshape(4, 128, 384)
        )
        dgu[block, s, :, h * 768 + 384 : (h + 1) * 768] = (
            (back * silu).astype(bf).reshape(4, 128, 384)
        )

    def dx_step(s, pair):
        first = 4 * pair
        block = pl.ds(first, 4)
        dxb[block, s] = (
            lax.dot_general(
                dgu[block, s].reshape(512, 1536),
                win[...].reshape(1536, 1536),
                nt,
                preferred_element_type=f32,
            )
            .astype(bf)
            .reshape(4, 128, 1536)
        )
        for j in range(2):
            for a in range(2):
                sib_sum(2 * pair + j, s, a).start()

    def out_slot(slot):
        return win.at[:, pl.ds(slot * 128, 128)]

    def out_copy(slot, s, first):
        return pltpu.make_async_copy(
            out_slot(slot), outp_hbm.at[pl.ds(first, 4), s], stage_sem.at[slot]
        )

    def out_step(slot, s, pair):
        first = 4 * pair
        win[:, slot * 128 : (slot + 1) * 128] = (
            jnp.dot(
                hg[pl.ds(first, 4), s].reshape(512, FF), wout[...], preferred_element_type=f32
            )
            .astype(bf)
            .reshape(4, 128, 1536)
        )
        out_copy(slot, s, first).start()

    def early_copies(first):
        return [
            pltpu.make_async_copy(
                gout.at[pl.ds(j * 128, 128)], outp_hbm.at[first + j, 0], grad_sem.at[j]
            )
            for j in range(4)
        ]

    def early_step(pair):
        first = 4 * pair
        gout[:512] = jnp.dot(
            hg[pl.ds(first, 4), 0].reshape(512, FF), wout[...], preferred_element_type=f32
        ).astype(bf)
        for copy in early_copies(first):
            copy.start()

    def early_wait():
        for copy in early_copies(0):
            copy.wait()

    far = 1 - hi
    near = hi

    def pair_of(t):
        return far + t * (1 - 2 * far)

    def i_piece(dd, p):
        return gin.at[pl.ds(pl.multiple_of(dd * 384 + p * PIECE, 16), PIECE)]

    def i_diag(p):
        return remote(
            i_piece(d_d, p), ti.at[p], i_send.at[0, p], i_recv.at[0, p], (to_x, to_y)[p % 2]
        )

    def i_direct(p):
        if p % 2 == 0:
            return remote(i_piece(d_x, p), xi.at[p], i_send.at[1, p], i_recv.at[1, p], to_x)
        return remote(i_piece(d_y, p), yi.at[p], i_send.at[1, p], i_recv.at[2, p], to_y)

    def i_summed(p):
        if p % 2 == 0:
            return remote(i_piece(d_y, p), yi.at[p], i_send.at[2, p], i_recv.at[2, p], to_y)
        return remote(i_piece(d_x, p), xi.at[p], i_send.at[2, p], i_recv.at[1, p], to_x)

    def i_middle(p):
        i_diag(p).wait_recv()
        dd = d_y if p % 2 == 0 else d_x
        rows = pl.ds(pl.multiple_of(dd * 384 + p * PIECE, 16), PIECE)
        gin[rows] = (gin[rows].astype(f32) + ti[p].astype(f32)).astype(bf)
        i_summed(p).start()

    def i_final(p):
        remote(xi.at[p], xi.at[p], i_send.at[1, p], i_recv.at[1, p], to_x).wait_recv()
        remote(yi.at[p], yi.at[p], i_send.at[1, p], i_recv.at[2, p], to_y).wait_recv()
        rows = pl.ds(pl.multiple_of(d * 384 + p * PIECE, 16), PIECE)
        xi[p] = (gin[rows].astype(f32) + xi[p].astype(f32) + yi[p].astype(f32)).astype(bf)

    def in_grad(yy, h):
        return lax.dot_general(
            xall[:, :, :, pl.ds(pl.multiple_of(yy * 768, 128), 768)].reshape(2048, 768),
            dgu[:, :, :, h * 768 : (h + 1) * 768].reshape(2048, 768),
            tn,
            preferred_element_type=f32,
        ).astype(bf)

    def in_first(yy):
        gin[pl.ds(pl.multiple_of(yy * 768, 16), 768)] = in_grad(yy, 0)

    @pl.loop(0, 2)
    def _(t):
        half_step(0, pair_of(t), 0)

    @pl.when(mid)
    def _():
        pass_on(1, 1)

    w_rest(1)

    @pl.when(end)
    def _():
        pass_on(1, 1)


    @pl.loop(0, 2)
    def _(t):
        pair = pair_of(t)
        half_step(0, pair, 1)
        dx_step(0, pair)

        @pl.when(t == 0)
        def _():
            end_sums(0, (0, 1))
            pass_on(2, 1)

        @pl.when(t == 1)
        def _():
            end_sums(0, (2,))

    from_sib(1, (near,))

    @pl.loop(0, 2)
    def _(t):
        half_step(1, pair_of(1 - t), 0)

        @pl.when(t == 0)
        def _():
            pass_on(3, 1)
            early_step(far)
            from_sib(1, (far,))

    mid_sum(0, 0)

    @pl.loop(0, 2)
    def _(t):
        pair = pair_of(t)
        half_step(1, pair, 1)
        dx_step(1, pair)

        @pl.when(t == 0)
        def _():
            in_first(1 - y)
            for p in range(4):
                i_diag(p).start()
            for p in (1, 3):
                i_direct(p).start()
            end_sums(1, (0, 1))
            in_first(y)
            for p in (0, 2):
                i_direct(p).start()
            mid_sum(1, 0)
            mid_sum(2, 0)

    def g_rows(dd, i):
        return pl.ds(pl.multiple_of(dd * 192 + i * 48, 16), 48)

    def g_piece(dd, i):
        return gout.at[g_rows(dd, i)]

    def g_diag(i):
        return remote(
            g_piece(d_d, i), tg.at[i], g_send.at[0, i], g_recv.at[0, i], (to_x, to_y)[i]
        )

    def g_direct(i):
        if i == 0:
            return remote(g_piece(d_x, i), xg.at[i], g_send.at[1, i], g_recv.at[1, i], to_x)
        return remote(g_piece(d_y, i), yg.at[i], g_send.at[1, i], g_recv.at[2, i], to_y)

    def g_summed(i):
        if i == 0:
            return remote(g_piece(d_y, i), yg.at[i], g_send.at[2, i], g_recv.at[2, i], to_y)
        return remote(g_piece(d_x, i), xg.at[i], g_send.at[2, i], g_recv.at[1, i], to_x)

    def g_middle(i):
        g_diag(i).wait_recv()
        rows = g_rows(d_y if i == 0 else d_x, i)
        gout[rows] = (gout[rows].astype(f32) + tg[i].astype(f32)).astype(bf)
        g_summed(i).start()

    def out_grad(half):
        at = pl.multiple_of(half * 384, 128)
        gout[pl.ds(at, 384)] = lax.dot_general(
            hg[:, :, :, pl.ds(at, 384)].reshape(2048, 384),
            gall[...].reshape(2048, 1536),
            tn,
            preferred_element_type=f32,
        ).astype(bf)

    for p in range(4):
        i_middle(p)
    early_wait()
    out_grad(1 - y)
    g_diag(0).start()
    g_diag(1).start()
    g_direct(1).start()
    end_sums(1, (2,))
    out_grad(y)
    g_direct(0).start()
    mid_sum(0, 1)
    rest = [
        pltpu.make_async_copy(
            gout.at[pl.ds(k * 192 + PIECE, PIECE)], gout_hbm.at[k], own_sem.at[k]
        )
        for k in range(4)
    ]
    for copy in rest:
        copy.start()

    def grad_copy(k):
        return pltpu.make_async_copy(
            win.at[k, :, pl.ds(0, 768)], gin_hbm.at[k], grad_sem.at[k]
        )

    for h in range(2):
        for kind in range(2):
            for p in range(2):
                w_copy(h, kind, p, d, to_x, 2).wait_send()
    for k in range(2):
        win[2 * k : 2 * k + 2, :, :768] = in_grad(k, 1).reshape(2, 384, 768)
        grad_copy(2 * k).start()
        grad_copy(2 * k + 1).start()
    for p in range(4):
        i_final(p)
    in_copy = pltpu.make_async_copy(xi, gin_first_hbm, own_sem.at[6])
    in_copy.start()
    for k in range(4):
        grad_copy(k).wait()
    for i in range(2):
        g_middle(i)
    mid_sum(1, 1)
    mid_sum(2, 1)
    out_step(0, 0, near)
    out_step(1, 1, far)
    out_step(2, 1, near)
    last_sum(0)
    for i in range(2):
        remote(xg.at[i], xg.at[i], g_send.at[1, i], g_recv.at[1, i], to_x).wait_recv()
        remote(yg.at[i], yg.at[i], g_send.at[1, i], g_recv.at[2, i], to_y).wait_recv()
        xg[i] = (
            gout[g_rows(d, i)].astype(f32) + xg[i].astype(f32) + yg[i].astype(f32)
        ).astype(bf)
    out_first_copy = pltpu.make_async_copy(xg, gout_first_hbm, own_sem.at[7])
    out_first_copy.start()
    for copy in rest:
        copy.wait()
    for k in range(3):
        out_copy(k, 1, 0).wait()
    last_sum(1)
    in_copy.wait()
    out_first_copy.wait()
    for s in range(2):
        dx_copy(s).wait()

    for i in range(2):
        for copy in (g_diag(i), g_direct(i), g_summed(i)):
            copy.wait_send()
    for p in range(4):
        for copy in (i_diag(p), i_direct(p), i_summed(p)):
            copy.wait_send()
    for h in range(2):
        for kind in range(2):
            for p in range(2):
                for row in range(2):
                    w_copy(h, kind, p, d, to_x, row).wait_send()
    for s in range(2):
        for zp in range(4):
            for a in range(2):
                sib_copy(a, zp, s).wait_send()
                sib_sum(zp, s, a).wait_send()

                @pl.when((zp <= z) & (z < 3))
                def _():
                    ag_copy(a, zp, s, 0).wait_send()

                @pl.when((zp >= z) & (z > 0))
                def _():
                    ag_copy(a, zp, s, 1).wait_send()

        for i in range(3):
            halves, last = hop(i, s, to_in, True)
            for copy in halves + [last]:
                copy.wait_send()


def expert_stage(rows, grads, gates_t, w_in, w_out):
    bf, f32 = jnp.bfloat16, jnp.float32
    shape = jax.ShapeDtypeStruct
    width = rows.shape[-1]
    hbm = pl.BlockSpec(memory_space=pltpu.HBM)
    vmem = pl.BlockSpec(memory_space=pltpu.VMEM)
    dma = pltpu.SemaphoreType.DMA
    return pl.pallas_call(
        expert_kernel,
        out_shape=(
            shape((8, 128, width // 4), f32),
            shape((2, 8, 128), f32),
            shape((8, 2, 128, width), bf),
            shape((4, 384, FF), bf),
            shape((4, PIECE, width), bf),
            shape((2, 48, width), bf),
            shape((4, PIECE, FF), bf),
        ),
        in_specs=[hbm] * 5,
        out_specs=(hbm, vmem, hbm, hbm, hbm, hbm, hbm),
        scratch_shapes=[
            pltpu.VMEM((4, width // 4, 2 * FF), bf),
            pltpu.VMEM((FF, width), bf),
            pltpu.VMEM((8, 2, 128, width), bf),
            pltpu.VMEM((8, 2, 128, width), bf),
            pltpu.VMEM((8, 2, 8, 128), f32),
            pltpu.VMEM((8, 2, 128, 2 * FF), bf),
            pltpu.VMEM((8, 2, 128, FF), bf),
            pltpu.VMEM((8, 2, 128, width), bf),
            pltpu.VMEM((8, 2, 8, 128), f32),
            pltpu.VMEM((4, 2, 128, width), bf),
            pltpu.VMEM((4, 2, 8, 128), f32),
            pltpu.VMEM((3, 2, 128, width), bf),
            pltpu.VMEM((3, 2, 8, 128), f32),
            pltpu.VMEM((3, 2, 128, width), bf),
            pltpu.VMEM((3, 2, 8, 128), f32),
            pltpu.VMEM((FF, width), bf),
            *([pltpu.VMEM((2, 48, width), bf)] * 3),
            pltpu.VMEM((width, FF), bf),
            *([pltpu.VMEM((4, PIECE, FF), bf)] * 3),
            pltpu.VMEM((8, 128, width // 4), f32),
            dma((9,)),
            dma((3,)),
            dma((4,)),
            dma((3, 2)),
            dma((3, 2)),
            dma((3, 4)),
            dma((3, 4)),
            dma((3, 2, 2, 2)),
            dma((3, 2, 2, 2)),
            dma((2, 4, 2)),
            dma((2, 2, 4, 2)),
            dma((2, 4, 2)),
            dma((2, 4, 2)),
            dma((6, 4, 2)),
            dma((4, 4, 2)),
            dma((2, 2, 3, 2)),
            dma((2, 3, 2)),
        ],
        compiler_params=pltpu.CompilerParams(
            collective_id=1, has_side_effects=True, vmem_limit_bytes=63 * 2**20
        ),
        name="expert_stage",
    )(
        rows.reshape(2, 128, width),
        grads.reshape(8, 2, 128, width),
        gates_t,
        w_in,
        w_out,
    )


def backward_kernel(
    dx_hbm,
    dgt_hbm,
    gates_hbm,
    mixed_hbm,
    cot_hbm,
    tok_hbm,
    q_hbm,
    kv_hbm,
    att_hbm,
    lens_ref,
    small_hbm,
    rope_hbm,
    wa_hbm,
    wb_hbm,
    gin_hbm,
    gout_hbm,
    outp_hbm,
    block_hbm,
    dtok_hbm,
    gq_hbm,
    gb_hbm,
    gkv_out,
    small_out,
    ein_hbm,
    eout_hbm,
    osib,
    oro,
    ori,
    wide,
    gq,
    gb,
    gk,
    sib_q,
    sib_b,
    sib_k,
    tq,
    xq,
    yq,
    roq,
    riq,
    tb,
    xb,
    yb,
    rob,
    rib,
    tw,
    xw,
    yw,
    row_,
    riw,
    te,
    xe,
    ye,
    le,
    lf,
    td,
    xd,
    yd,
    ld,
    old,
    oslot,
    dat,
    dkv,
    tk,
    xk,
    yk,
    rope,
    cot_ref,
    tok_ref,
    q_ref,
    kv_ref,
    att_ref,
    mixed_ref,
    block_out,
    dtok_out,
    dgt_ref,
    gates_ref,
    small_ref,
    gq_out,
    gb_out,
    load_sem,
    out_sem,
    le_sem,
    old_sem,
    os_recv,
    os_send,
    ds_recv,
    ds_send,
    t_recv,
    x_recv,
    y_recv,
    t_send,
    d_send,
    s_send,
    ro_recv,
    ri_recv,
    hop_send,
):
    bf, f32 = jnp.bfloat16, jnp.float32
    d, e, z, c, x, y = place()
    d_x = d + 1 - 2 * x
    d_y = d + 2 - 4 * y
    d_d = 3 - d
    hi = lax.div(z, 2)
    zz = z * hi + (3 - z) * (1 - hi)
    other = 1 - c
    mid = zz == 2
    end = zz == 3
    to_x = (d_x, e)
    to_y = (d_y, e)
    to_sib = (d, 2 * z + other)
    e_in = e + 2 - 4 * hi
    to_in = (d, e_in)
    to_out = (d, jnp.where(zz == 2, e - 2 + 4 * hi, e_in))

    dqs = block_out
    dmix = dtok_out
    dx_ref = dtok_out

    first_loads = [
        pltpu.make_async_copy(
            dx_hbm.at[4 * s + j],
            dx_ref.at[pl.ds(s * 128, 128), pl.ds(j * 384, 384)],
            load_sem.at[13 + 4 * s + j],
        )
        for s in range(2)
        for j in range(4)
    ] + [
        pltpu.make_async_copy(mixed_hbm, mixed_ref, load_sem.at[10]),
    ]
    tiny_loads = [
        pltpu.make_async_copy(src, dst, load_sem.at[21 + j])
        for j, (src, dst) in enumerate(
            ((dgt_hbm, dgt_ref), (gates_hbm, gates_ref), (small_hbm, small_ref))
        )
    ]
    results = [
        pltpu.make_async_copy(src, dst, out_sem.at[j])
        for j, (src, dst) in enumerate(
            ((gq_out, gq_hbm), (gb_out, gb_hbm), (xe, ein_hbm), (xd, eout_hbm))
        )
    ]
    for load in tiny_loads:
        load.start()
    for load in first_loads:
        load.start()

    barrier = pltpu.get_barrier_semaphore()
    for target in (to_x, to_y, to_sib, to_in):
        pl.semaphore_signal(barrier, inc=1, device_id=target, device_id_type=MESH)

    @pl.when(mid)
    def _():
        pl.semaphore_signal(barrier, inc=1, device_id=to_out, device_id_type=MESH)

    pl.semaphore_wait(barrier, 7 - zz)

    def order(i):
        v = i if i < 2 else (5 - zz if i == 2 else zz)
        return v * hi + (3 - v) * (1 - hi)

    def across(k, src, t, fx, fy, ways=(0, 1, 0, 1)):
        def diag(i):
            return remote(
                src(d_d, i), t.at[i], t_send.at[k, i], t_recv.at[k, i], (to_x, to_y)[ways[i]]
            )

        def direct(i):
            if ways[i] == 0:
                return remote(src(d_x, i), fx.at[i], d_send.at[k, i], x_recv.at[k, i], to_x)
            return remote(src(d_y, i), fy.at[i], d_send.at[k, i], y_recv.at[k, i], to_y)

        def summed(i, ref):
            if ways[i] == 0:
                return remote(ref, fy.at[i], s_send.at[k, i], y_recv.at[k, i], to_y)
            return remote(ref, fx.at[i], s_send.at[k, i], x_recv.at[k, i], to_x)

        def wait_t(i):
            remote(t.at[i], t.at[i], t_send.at[k, i], t_recv.at[k, i], to_x).wait_recv()

        def wait_xy(i):
            remote(fx.at[i], fx.at[i], d_send.at[k, i], x_recv.at[k, i], to_x).wait_recv()
            remote(fy.at[i], fy.at[i], d_send.at[k, i], y_recv.at[k, i], to_y).wait_recv()

        def drain(n):
            for i in range(n):
                diag(i).wait_send()
                direct(i).wait_send()
                summed(i, t.at[i]).wait_send()

        return diag, direct, summed, wait_t, wait_xy, drain

    def along(k, slot, ro, ri):
        def send(i, target, dst, recv):
            return remote(slot(i), dst.at[i], hop_send.at[k, i], recv.at[k, i], target)

        def to_ro(i):
            return send(i, to_in, ro, ro_recv)

        def to_ri(i):
            return send(i, to_in if i < 2 else to_out, ri, ri_recv)

        def wait_ro(i):
            remote(ro.at[i], ro.at[i], hop_send.at[k, i], ro_recv.at[k, i], to_in).wait_recv()

        def wait_ri(i):
            remote(ri.at[i], ri.at[i], hop_send.at[k, i], ri_recv.at[k, i], to_in).wait_recv()

        def drain():
            for i in range(3):
                to_ro(i).wait_send()

        return to_ro, to_ri, wait_ro, wait_ri, drain

    expert_ways = (0, 1, 0, 0)

    def expert_src(dd, p):
        return gin_hbm.at[pl.ds(pl.multiple_of(dd * 384 + p * PIECE, 16), PIECE)]

    e_diag, e_direct, e_summed, e_wait_t, e_wait_xy, e_drain = across(
        0, expert_src, te, xe, ye, expert_ways
    )

    def e_sent_to(p):
        return d_y if expert_ways[p] == 0 else d_x

    e_loads = [
        pltpu.make_async_copy(expert_src(e_sent_to(p), p), le.at[p], le_sem.at[p])
        for p in range(4)
    ]
    e_own = pltpu.make_async_copy(
        gin_hbm.at[pl.ds(pl.multiple_of(d * 384, 16), 384)], lf, le_sem.at[4]
    )

    def e_middle(p):
        e_wait_t(p)
        e_loads[p].wait()
        te[p] = (te[p].astype(f32) + le[p].astype(f32)).astype(bf)
        e_summed(p, te.at[p]).start()

    def e_final(p):
        e_wait_xy(p)
        rows = slice(p * PIECE, (p + 1) * PIECE)
        total = lf[rows].astype(f32) + xe[p].astype(f32) + ye[p].astype(f32)
        xe[p] = total.astype(bf)

    def d_src(dd):
        return gout_hbm.at[dd]

    def d_diag():
        return remote(d_src(d_d), td, t_send.at[5, 0], t_recv.at[5, 0], to_y)

    def d_direct():
        return remote(d_src(d_y), yd, d_send.at[5, 0], y_recv.at[5, 0], to_y)

    def d_summed():
        return remote(td, xd, s_send.at[5, 0], x_recv.at[5, 0], to_x)

    d_loads = [
        pltpu.make_async_copy(d_src(dd), ld.at[j], le_sem.at[5 + j])
        for j, dd in enumerate((d_x, d))
    ]

    def d_middle():
        d_diag().wait_recv()
        d_loads[0].wait()
        td[...] = (td[...].astype(f32) + ld[0].astype(f32)).astype(bf)
        d_summed().start()

    def d_final():
        d_summed().wait_recv()
        d_direct().wait_recv()
        xd[...] = (ld[1].astype(f32) + xd[...].astype(f32) + yd[...].astype(f32)).astype(bf)

    def store_q(total):
        gq_out[...] = total

    def store_b(total):
        gb_out[...] = total

    def store_k(total):
        gkv_out[...] = total[:, :512]
        small_out[...] = lax.dot_general(
            eye[:16],
            total[:, 512:],
            (((1,), (1,)), ((), ())),
            preferred_element_type=f32,
            precision=highest,
        )

    dense = (
        (gq, sib_q, tq, xq, yq, roq, riq, store_q),
        (gb, sib_b, tb, xb, yb, rob, rib, store_b),
        (gk, sib_k, tw, xw, yw, row_, riw, store_k),
    )

    def dense_stream(j):
        grad, sib, t, fx, fy, ro, ri, out = dense[j]

        def src(dd, i):
            return grad.at[dd * 4 + order(i), c]

        diag, direct, summed, wait_t, wait_xy, drain = across(1 + j, src, t, fx, fy)

        def own_slot(i):
            return grad.at[d * 4 + order(i), c]

        to_ro, to_ri, wait_ro, wait_ri, drain_z = along(j, own_slot, ro, ri)

        def sib_copy():
            return remote(grad.at[:, other], sib, ds_send.at[j], ds_recv.at[j], to_sib)

        def begin():
            sib_copy().wait_recv()

            @pl.loop(0, 16)
            def _(k):
                grad[k, c] = (grad[k, c].astype(f32) + sib[k].astype(f32)).astype(bf)

            for i in range(4):
                diag(i).start()
            for i in range(4):
                direct(i).start()

        def middle(i):
            dd = d_y if i % 2 == 0 else d_x
            wait_t(i)
            at = dd * 4 + order(i)
            grad[at, c] = (grad[at, c].astype(f32) + t[i].astype(f32)).astype(bf)
            summed(i, src(dd, i)).start()

        def local(i):
            return grad[d * 4 + order(i), c].astype(f32) + fx[i].astype(f32) + fy[i].astype(f32)

        def put(i, total):
            grad[d * 4 + order(i), c] = total.astype(bf)

        def last(i):
            wait_xy(i)
            if i == 3:
                return

            @pl.when(end)
            def _():
                put(i, local(i))
                to_ro(i).start()

        def hop(i):
            @pl.when(mid)
            def _():
                if i < 2:
                    wait_ro(i)
                    put(i, local(i) + ro[i].astype(f32))
                else:
                    wait_ri(0)
                    put(2, local(2) + ri[0].astype(f32))
                to_ri(i).start()

        def finish():
            @pl.when(mid)
            def _():
                wait_ro(2)
                wait_ri(1)
                out(local(3) + ro[2].astype(f32) + ri[1].astype(f32))

            @pl.when(end)
            def _():
                wait_ri(2)
                out(local(3) + ri[2].astype(f32))

        def drain_all():
            sib_copy().wait_send()
            drain(4)
            drain_z()

        return sib_copy, begin, middle, last, hop, finish, drain_all

    q_sib, q_begin, q_middle, q_last, q_hop, q_finish, q_drain = dense_stream(0)
    b_sib, b_begin, b_middle, b_last, b_hop, b_finish, b_drain = dense_stream(1)
    w_sib, w_begin, w_middle, w_last, w_hop, w_finish, w_drain = dense_stream(2)

    def out_rows(i, lane):
        return outp_hbm.at[pl.ds(pl.multiple_of((2 * order(i) + lane) * CHUNK, CHUNK), CHUNK)]

    def out_sib(i):
        return remote(out_rows(i, other), osib.at[i], os_send.at[i], os_recv.at[i], to_sib)

    o_ro, o_ri, o_wait_ro, o_wait_ri, _ = along(3, lambda i: oslot.at[i % 2], oro, ori)

    def out_sum(i, incoming, store):
        out_sib(i).wait_recv()
        for half in range(2):
            rows = pl.ds(half * 128, 128)
            loads = [
                pltpu.make_async_copy(ref.at[rows], old.at[j], old_sem.at[j])
                for j, ref in enumerate([out_rows(i, c), osib.at[i]] + incoming)
            ]
            for load in loads:
                load.start()
            for load in loads:
                load.wait()
            total = old[0].astype(f32)
            for j in range(1, len(loads)):
                total = total + old[j].astype(f32)
            store(slice(half * 128, (half + 1) * 128), total)

    def out_slot(i):
        def store(rows, total):
            oslot[i % 2, rows] = total.astype(bf)

        return store

    def out_end(i):
        @pl.when(end)
        def _():
            if i == 2:
                o_ro(0).wait_send()
            out_sum(i, [], out_slot(i))
            o_ro(i).start()

    def out_mid(i):
        @pl.when(mid)
        def _():
            if i < 2:
                o_wait_ro(i)
                out_sum(i, [oro.at[i]], out_slot(i))
            else:
                o_ri(0).wait_send()
                o_wait_ri(0)
                out_sum(2, [ori.at[0]], out_slot(2))
            o_ri(i).start()

    def out_finish():
        def store(rows, total):
            total = total + mixed_ref[rows]
            slot = d * 128 + lax.broadcasted_iota(jnp.int32, (128, 1), 0)
            live = slot < lens_ref[rows.start // 128]
            block_out[rows] = jnp.where(live, total, 0.0).astype(bf)

        @pl.when(mid)
        def _():
            o_wait_ro(2)
            o_wait_ri(1)
            out_sum(3, [oro.at[2], ori.at[1]], store)

        @pl.when(end)
        def _():
            o_wait_ri(2)
            out_sum(3, [ori.at[2]], store)

    def kv_src(dd, i):
        return dkv.at[dd, pl.ds(i * 128, 128)]

    k_diag, k_direct, k_summed, k_wait_t, k_wait_xy, k_drain = across(4, kv_src, tk, xk, yk)

    def k_middle(i):
        dd = d_y if i % 2 == 0 else d_x
        k_wait_t(i)
        rows = slice(i * 128, (i + 1) * 128)
        dkv[dd, rows] = (dkv[dd, rows].astype(f32) + tk[i].astype(f32)).astype(bf)
        k_summed(i, kv_src(dd, i)).start()

    wb_load = pltpu.make_async_copy(wb_hbm, wide.at[:, pl.ds(0, 1536)], load_sem.at[1])
    wa_load = pltpu.make_async_copy(wa_hbm.at[:, pl.ds(0, 2048)], wide, load_sem.at[2])
    rope_load = pltpu.make_async_copy(
        rope_hbm.at[:, pl.ds(pl.multiple_of(d * 128, 128), 128)], rope, load_sem.at[3]
    )
    loads = [
        pltpu.make_async_copy(src, dst, load_sem.at[4 + j])
        for j, (src, dst) in enumerate(
            (
                (cot_hbm, cot_ref),
                (att_hbm, att_ref),
                (q_hbm, q_ref),
                (kv_hbm, kv_ref),
                (tok_hbm, tok_ref),
            )
        )
    ]
    for load in loads[:2]:
        load.start()
    wb_load.start()
    rope_load.start()
    for load in loads[2:] + e_loads + [e_own] + d_loads:
        load.start()
    for p in range(4):
        e_diag(p).start()
    for p in (0, 1):
        e_direct(p).start()
    d_diag().start()
    for i in range(4):
        out_sib(i).start()
    out_end(0)

    nt = (((1,), (1,)), ((), ()))
    tn = (((0,), (0,)), ((), ()))

    def dot_nt(a, b):
        return lax.dot_general(a, b, nt, preferred_element_type=f32)

    def dot_tn(a, b):
        return lax.dot_general(a, b, tn, preferred_element_type=f32)

    eye = (
        lax.broadcasted_iota(jnp.int32, (128, 128), 0)
        == lax.broadcasted_iota(jnp.int32, (128, 128), 1)
    ).astype(f32)
    eye_low = eye.astype(bf)
    for load in tiny_loads:
        load.wait()
    gates = jnp.concatenate([gates_ref[s] for s in range(2)], axis=1)
    dgate = jnp.concatenate([dgt_ref[s] for s in range(2)], axis=1)
    dlogit = gates * (dgate - jnp.sum(gates * dgate, axis=0, keepdims=True))
    dl_hi = dlogit.astype(bf).astype(f32)
    dl = jnp.concatenate([dl_hi, dlogit - dl_hi], axis=0).astype(bf)
    small_t = small_ref[...]
    router = jnp.concatenate([small_t[:8]] * 2, axis=0).astype(bf)
    for load in first_loads:
        load.wait()
    dn2 = dx_ref[...] + dot_tn(dl, router)
    mixed = mixed_ref[...]
    inv2 = lax.rsqrt(jnp.mean(mixed * mixed, axis=1, keepdims=True) + epsilon)
    n2 = mixed * inv2
    normed2 = (n2 * small_t[9:10]).astype(bf)
    router_sum = jnp.dot(dl, normed2, preferred_element_type=f32)
    router_sum = router_sum[:8] + router_sum[8:]
    mid_sum = jnp.sum(dn2 * n2, axis=0, keepdims=True)
    loads[0].wait()
    loads[1].wait()
    grads = [
        jnp.where(
            d * 128 + lax.broadcasted_iota(jnp.int32, (128, 1), 0) < lens_ref[s],
            cot_ref[s * 128 : (s + 1) * 128].astype(f32),
            0.0,
        )
        for s in range(2)
    ]
    u = dn2 * small_t[9:10]
    dmixed = jnp.concatenate(grads, axis=0) + inv2 * (u - n2 * jnp.mean(u * n2, axis=1, keepdims=True))
    dmix[...] = dmixed
    dproj = dmixed.astype(bf)
    for r in range(4):
        part = dot_tn(att_ref[:, r * 384 : (r + 1) * 384], dproj)
        gb[4 * r : 4 * r + 4] = part.astype(bf).reshape(4, 2, 48, 1536)
    b_sib().start()
    wb_load.wait()
    datt = dot_nt(dproj, wide[:, :1536]).astype(bf)
    for head in range(QUERY_HEADS):
        for s in range(2):
            at = (s * QUERY_HEADS + head) * 128
            dat[at : at + 128] = datt[s * 128 : (s + 1) * 128, head * 128 : (head + 1) * 128]
    wa_load.start()
    b_begin()
    out_end(1)

    query_pos = d * 128 + lax.broadcasted_iota(jnp.int32, (128, 512), 0)
    key_pos = lax.broadcasted_iota(jnp.int32, (128, 512), 1)
    rope_load.wait()
    for load in loads[2:]:
        load.wait()
    cos_rows = rope[0]
    sin_rows = rope[1]
    scale = HEAD_SIZE ** (-0.5)

    def unrotate_rows(v, cos, sin):
        return v * cos - pltpu.roll(v, 64, 1) * sin

    def attend(n):
        s = lax.div(n, 2)
        h = lax.rem(n, 2)
        srow = pl.ds(pl.multiple_of(s * 128, 128), 128)
        kcol = pl.ds(pl.multiple_of(h * 128, 128), 128)
        vcol = pl.ds(pl.multiple_of(256 + h * 128, 128), 128)
        lens = lens_ref[s]
        allowed = (key_pos <= query_pos) & (key_pos < lens)
        ks = kv_ref[:, srow, kcol].reshape(512, 128)
        vs = kv_ref[:, srow, vcol].reshape(512, 128)
        dk = None
        dv = None
        for half in range(2):
            rows = pl.ds(pl.multiple_of(n * 768 + half * 384, 128), 384)
            qh = q_ref[rows]
            dh = dat[rows]
            scores = dot_nt(qh, ks).reshape(3, 128, 512) * scale
            scores = jnp.where(allowed[None], scores, -1e30)
            probs = jnp.exp(scores - jnp.max(scores, axis=-1, keepdims=True))
            probs = probs * (1.0 / jnp.sum(probs, axis=-1, keepdims=True))
            dprobs = dot_nt(dh, vs).reshape(3, 128, 512)
            delta = jnp.sum(probs * dprobs, axis=-1, keepdims=True)
            dscores = (probs * (dprobs - delta)).astype(bf).reshape(384, 512)
            low = probs.astype(bf).reshape(384, 512)
            dq = jnp.dot(dscores, ks, preferred_element_type=f32) * scale
            for j in range(3):
                dqs[srow, pl.ds(pl.multiple_of(h * 768 + (half * 3 + j) * 128, 128), 128)] = (
                    unrotate_rows(dq[j * 128 : (j + 1) * 128], cos_rows, sin_rows).astype(bf)
                )
            dk_part = dot_tn(dscores, qh)
            dv_part = dot_tn(low, dh)
            dk = dk_part if dk is None else dk + dk_part
            dv = dv_part if dv is None else dv + dv_part
        dkv[:, srow, kcol] = (dk * scale).astype(bf).reshape(4, 128, 128)
        dkv[:, srow, vcol] = dv.astype(bf).reshape(4, 128, 128)

    pl.loop(0, 2)(attend)
    for i in range(4):
        b_middle(i)
    e_middle(1)
    e_middle(0)
    out_mid(0)
    pl.loop(2, 4)(attend)
    for i in range(2):
        k_diag(i).start()
    for i in range(2):
        k_direct(i).start()
    for i in range(4):
        b_last(i)
    out_end(2)

    tok = tok_ref[...].astype(f32)
    inv1 = lax.rsqrt(jnp.mean(tok * tok, axis=1, keepdims=True) + epsilon)
    n1 = tok * inv1
    normed = (n1 * small_t[8:9]).astype(bf)
    for r in range(4):
        part = dot_tn(normed[:, r * 384 : (r + 1) * 384], dqs[...])
        gq[4 * r : 4 * r + 4] = part.astype(bf).reshape(4, 2, 48, 1536)
    q_sib().start()
    k_middle(0)
    k_middle(1)
    q_begin()
    wa_load.wait()
    dn1 = dot_nt(dqs[...], wide[:, :1536])

    for i in range(2):
        k_wait_xy(i)
    own = jnp.concatenate(
        [
            dkv[d, i * 128 : (i + 1) * 128].astype(f32) + xk[i].astype(f32) + yk[i].astype(f32)
            for i in range(2)
        ],
        axis=0,
    )
    cos_two = jnp.concatenate([cos_rows] * 2, axis=0)
    sin_two = jnp.concatenate([sin_rows] * 2, axis=0)
    dkv_own = jnp.concatenate(
        [
            unrotate_rows(own[:, h * 128 : (h + 1) * 128], cos_two, sin_two)
            for h in range(2)
        ]
        + [own[:, 256:]],
        axis=1,
    ).astype(bf)
    dn1 = dn1 + dot_nt(dkv_own, wide[:, 1536:])
    pre_sum = jnp.sum(dn1 * n1, axis=0, keepdims=True)
    row8 = lax.broadcasted_iota(jnp.int32, (8, 1536), 0)
    gains = jnp.where(row8 == 0, pre_sum, jnp.where(row8 == 1, mid_sum, 0.0))
    smalls = jnp.concatenate([router_sum, gains], axis=0).astype(bf)
    for r in range(4):
        cols = slice(r * 384, (r + 1) * 384)
        part = dot_tn(normed[:, cols], dkv_own)
        gk[4 * r : 4 * r + 4, :, :, :512] = part.astype(bf).reshape(4, 2, 48, 512)
        part = dot_tn(smalls[:, cols], eye_low[:16])
        gk[4 * r : 4 * r + 4, :, :, 512:] = part.astype(bf).reshape(4, 2, 48, 128)
    w_sib().start()
    u = dn1 * small_t[8:9]
    dtok_copy = pltpu.make_async_copy(dtok_out, dtok_hbm, load_sem.at[11])
    dtok_out[...] = dmix[...] + inv1 * (u - n1 * jnp.mean(u * n1, axis=1, keepdims=True))

    dtok_copy.start()

    for i in range(4):
        q_middle(i)
    w_begin()
    e_direct(2).start()
    b_hop(0)
    b_hop(1)
    out_mid(1)
    out_mid(2)
    for i in range(4):
        q_last(i)
    for i in range(4):
        w_middle(i)
    d_direct().start()
    d_middle()
    e_direct(3).start()
    for p in (2, 3):
        e_middle(p)
    b_hop(2)
    q_hop(0)
    q_hop(1)
    out_finish()
    block_copy = pltpu.make_async_copy(block_out, block_hbm, load_sem.at[12])
    block_copy.start()
    for i in range(4):
        w_last(i)
    w_hop(0)
    q_hop(2)
    w_hop(1)
    w_hop(2)
    b_finish()
    results[1].start()
    q_finish()
    results[0].start()
    e_own.wait()
    d_loads[1].wait()
    d_final()
    results[3].start()
    for p in range(4):
        e_final(p)
    results[2].start()
    w_finish()
    dtok_copy.wait()
    block_copy.wait()
    for copy in results:
        copy.wait()

    e_drain(4)
    for copy in (d_diag(), d_direct(), d_summed()):
        copy.wait_send()
    k_drain(2)
    q_drain()
    b_drain()
    w_drain()
    for i in range(1, 3):
        o_ro(i).wait_send()
    for i in range(4):
        out_sib(i).wait_send()


def backward_stage(dx, dgt, gates, mixed, cot, tok, q, kv, att, lens, small, rope, wa, wb, gin, gout, outp):
    bf, f32 = jnp.bfloat16, jnp.float32
    shape = jax.ShapeDtypeStruct
    width = tok.shape[-1]
    hbm = pl.BlockSpec(memory_space=pltpu.HBM)
    vmem = pl.BlockSpec(memory_space=pltpu.VMEM)
    smem = pl.BlockSpec(memory_space=pltpu.SMEM)
    dma = pltpu.SemaphoreType.DMA
    widths = (width, width, 640)
    dense = []
    for w in widths:
        dense += [pltpu.VMEM((4, 48, w), bf)] * 3 + [pltpu.VMEM((3, 48, w), bf)] * 2
    return pl.pallas_call(
        backward_kernel,
        out_shape=(
            shape((CHUNK, width), bf),
            shape((CHUNK, width), f32),
            shape((48, width), f32),
            shape((48, width), f32),
            shape((48, 512), f32),
            shape((16, 48), f32),
            shape((4, PIECE, FF), bf),
            shape((PIECE, width), bf),
            shape((4, CHUNK, width), bf),
            shape((3, CHUNK, width), bf),
            shape((3, CHUNK, width), bf),
        ),
        in_specs=[hbm] * 9 + [smem] + [hbm] * 7,
        out_specs=[hbm] * 4 + [vmem] * 2 + [hbm] * 5,
        scratch_shapes=[
            pltpu.VMEM((width, 2048), bf),
            *[pltpu.VMEM((16, 2, 48, w), bf) for w in widths],
            *[pltpu.VMEM((16, 48, w), bf) for w in widths],
            *dense,
            *([pltpu.VMEM((4, PIECE, FF), bf)] * 3),
            pltpu.VMEM((4, PIECE, FF), bf),
            pltpu.VMEM((4 * PIECE, FF), bf),
            *([pltpu.VMEM((PIECE, width), bf)] * 3),
            pltpu.VMEM((2, PIECE, width), bf),
            pltpu.VMEM((4, 128, width), bf),
            pltpu.VMEM((2, CHUNK, width), bf),
            pltpu.VMEM((2 * QUERY_HEADS * 128, 128), bf),
            pltpu.VMEM((4, CHUNK, 512), bf),
            *([pltpu.VMEM((2, 128, 512), bf)] * 3),
            pltpu.VMEM((2, 128, 128), f32),
            *[pltpu.VMEM(ref.shape, ref.dtype) for ref in (cot, tok, q, kv, att, mixed)],
            pltpu.VMEM((CHUNK, width), bf),
            pltpu.VMEM((CHUNK, width), f32),
            pltpu.VMEM((2, 8, 128), f32),
            pltpu.VMEM((2, 8, 128), f32),
            pltpu.VMEM((16, width), f32),
            *([pltpu.VMEM((48, width), f32)] * 2),
            dma((24,)),
            dma((4,)),
            dma((7,)),
            dma((4,)),
            dma((4,)),
            dma((4,)),
            dma((3,)),
            dma((3,)),
            dma((6, 4)),
            dma((6, 4)),
            dma((6, 4)),
            dma((6, 4)),
            dma((6, 4)),
            dma((6, 4)),
            dma((4, 3)),
            dma((4, 3)),
            dma((4, 3)),
        ],
        compiler_params=pltpu.CompilerParams(
            collective_id=3, has_side_effects=True, vmem_limit_bytes=64 * 2**20 - 65536
        ),
        name="backward_stage",
    )(dx, dgt, gates, mixed, cot, tok, q, kv, att, lens, small, rope, wa, wb, gin, gout, outp)


def finish_kernel(
    block_in,
    dtok_in,
    gq_in,
    gb_in,
    gkv_in,
    small_ref,
    first_ref,
    second_ref,
    down_first_ref,
    down_second_ref,
    block_out,
    dtok_out,
    gq_out,
    gb_out,
    gkv_out,
    pre_out,
    mid_out,
    router_out,
    in_out,
    down_out,
):
    f32 = jnp.float32
    i = pl.program_id(0)
    block_out[...] = block_in[...]
    dtok_out[...] = dtok_in[...]
    gq_out[...] = gq_in[...]
    gb_out[...] = gb_in[...]
    gkv_out[...] = gkv_in[...]
    half = FF // 2
    first = first_ref[...].astype(f32)
    second = second_ref[...].astype(f32)
    in_out[:, :half] = first[:, :half]
    in_out[:, half:FF] = second[:, :half]
    in_out[:, FF : FF + half] = first[:, half:]
    in_out[:, FF + half :] = second[:, half:]
    down_out[...] = jnp.where(i < 1, down_first_ref[...], down_second_ref[...]).astype(f32)
    router_out[...] = small_ref[:8]
    pre_out[...] = small_ref[8:9]
    mid_out[...] = small_ref[9:10]


def finish_stage(block, dtok, gq, gb, gkv, small, first, second, down_first, down_second):
    f32 = jnp.float32
    shape = jax.ShapeDtypeStruct
    width = block.shape[-1]

    def rows(count, columns, index):
        return pl.BlockSpec((count, columns), index)

    def whole(count, columns):
        return pl.BlockSpec((count, columns), lambda i: (0, 0))

    return pl.pallas_call(
        finish_kernel,
        grid=(2,),
        out_shape=(
            shape(block.shape, block.dtype),
            shape(dtok.shape, f32),
            shape(gq.shape, f32),
            shape(gb.shape, f32),
            shape(gkv.shape, f32),
            shape((1, 48), f32),
            shape((1, 48), f32),
            shape((8, 48), f32),
            shape((384, 2 * FF), f32),
            shape((192, width), f32),
        ),
        in_specs=[
            rows(128, width, lambda i: (i, 0)),
            rows(128, width, lambda i: (i, 0)),
            whole(48, width),
            whole(48, width),
            whole(48, 512),
            whole(16, 48),
            rows(192, FF, lambda i: (i, 0)),
            rows(192, FF, lambda i: (i, 0)),
            whole(96, width),
            whole(96, width),
        ],
        out_specs=[
            rows(128, width, lambda i: (i, 0)),
            rows(128, width, lambda i: (i, 0)),
            whole(48, width),
            whole(48, width),
            whole(48, 512),
            whole(1, 48),
            whole(1, 48),
            whole(8, 48),
            rows(192, 2 * FF, lambda i: (i, 0)),
            rows(96, width, lambda i: (i, 0)),
        ],
        compiler_params=pltpu.CompilerParams(vmem_limit_bytes=63 * 2**20),
        name="finish_stage",
    )(block, dtok, gq, gb, gkv, small, first, second, down_first, down_second)


def rope_constant(slots):
    half = HEAD_SIZE // 2
    inv_freq = np.float32(rope_base) ** (-(np.arange(half, dtype=np.float32) * 2.0 / HEAD_SIZE))
    angles = np.arange(slots, dtype=np.float32)[:, None] * inv_freq[None, :].astype(np.float32)
    cos, sin = np.cos(angles), np.sin(angles)
    return np.stack(
        [np.concatenate([cos, cos], axis=1), np.concatenate([-sin, sin], axis=1)]
    ).astype(np.float32)


def fast_local(
    tokens,
    lengths,
    routes,
    prenorm,
    w_query,
    key_value_weight,
    w_output,
    midnorm,
    w_router,
    expert_in,
    expert_out,
    cotangent,
):
    seqs, token_rows, width = tokens.shape
    rows = seqs * token_rows
    tok = tokens.reshape(rows, width)
    cot = cotangent.reshape(rows, width)
    rope = jnp.asarray(rope_constant(token_rows * lax.axis_size("dp")))
    full_a, full_b, full_out, gall, q_rot, kv_all, attended, mixed, normed2, gates, small_t = attention_stage(
        tok,
        w_query,
        key_value_weight,
        w_router.T,
        prenorm[None],
        midnorm[None],
        w_output,
        cot,
        expert_out[0],
        rope,
        lengths,
        jnp.transpose(routes, (0, 2, 1)),
    )
    dx, dgate, outp, gin, gout, out_first, g_first = expert_stage(normed2, gall, gates, expert_in[0], full_out)
    block_out, grad_tokens, g_query, g_b, g_kv, small, g_second, out_second = backward_stage(
        dx, dgate, gates, mixed, cot, tok, q_rot, kv_all, attended, lengths, small_t, rope,
        full_a, full_b, gin.reshape(width, FF), gout, outp.reshape(8 * rows, width),
    )[:8]
    block_out, grad_tokens, g_query, g_b, g_kv, g_pre, g_mid, g_router, g_in, g_out = finish_stage(
        block_out,
        grad_tokens,
        g_query,
        g_b,
        g_kv,
        small,
        g_first.reshape(width // 4, FF),
        g_second.reshape(width // 4, FF),
        out_first.reshape(FF // 8, width),
        out_second,
    )
    return (
        block_out.reshape(seqs, token_rows, width),
        grad_tokens.reshape(seqs, token_rows, width),
        g_pre.reshape(-1),
        g_query,
        g_kv,
        g_b,
        g_mid.reshape(-1),
        g_router.T,
        g_in[None],
        g_out[None],
    )


def solution(mesh):
    placed = (
        P("expert", "dp", None),
        P("expert"),
        P("expert", "dp", None),
        P(("dp", "expert")),
        P(("dp", "expert"), None),
        P(("dp", "expert"), None),
        P(("dp", "expert"), None),
        P(("dp", "expert")),
        P(("dp", "expert"), None),
        P("expert", "dp", None),
        P("expert", "dp", None),
        P("expert", "dp", None),
    )
    fits = mesh.shape["dp"] == 4 and mesh.shape["expert"] == 8
    return jax.shard_map(
        fast_local if fits else local,
        mesh=mesh,
        in_specs=placed,
        out_specs=(
            P("expert", "dp", None),
            P("expert", "dp", None),
            P(("dp", "expert")),
            P(("dp", "expert"), None),
            P(("dp", "expert"), None),
            P(("dp", "expert"), None),
            P(("dp", "expert")),
            P(("dp", "expert"), None),
            P("expert", "dp", None),
            P("expert", "dp", None),
        ),
        check_vma=False,
    )
```
